32 devices in a mesh: lat: 8 (over z, core), lon: 4 (over y, x).
Axes of the slice: x: 2, y: 2, z: 4, core: 2. Of those that a mesh axis runs over, the one named last changes fastest.
Arguments:
- winds: float32 [2, 72, 11520], P(None, 'lat', 'lon'), as said below
- thickness: float32 [72, 11520], P('lat', 'lon'), may hold values from 0.5 to 1.5
- tracers: bfloat16 [3, 72, 11520], P(None, 'lat', 'lon'), may hold values from 0 to 1
- cutoff: int32 [72], replicated, may hold values from 1 to 360, as said below
Outputs:
- new_winds: float32 [2, 72, 11520], P(None, 'lat', 'lon')
- new_thickness: float32 [72, 11520], P('lat', 'lon')
- tracer_mass: bfloat16 [3, 72, 11520], P(None, 'lat', 'lon')
The draws below stay inside these ranges and needn't reach their ends.
Inputs may be any that keep to these rules, and one draw needn't show every extreme that they name: `cutoff`: the 12 rows nearest each pole have cutoffs that grow from 1 at the pole row to at most a quarter of 720; every other row has exactly 360, so that the filter leaves it unchanged. `winds`: each wind is the cosine of its row's latitude times a value of order one.
All inputs are finite; a program needn't handle non-finite values.
Results may differ from the reference program's by a relative error of at most 0.001.
Values sent between devices are 32-bit elements; how exact they have to be, the bound alone decides.
No kernel may reach another device: no remote copies, remote signals or barrier semaphores. Data moves between devices by JAX's collectives and lax.ppermute only.
A program may use at most 64 MiB of HBM per device.

```python
import math
import jax
import jax.numpy as jnp
from jax import lax

LEVELS = 16
NLAT = 72
NLON = 720
POLAR = 12


def draw_winds(key, part):
    rows = jnp.arange(NLAT, dtype=jnp.float32)
    centre = (rows + 0.5) * (math.pi / NLAT) - math.pi / 2
    scale = jnp.cos(centre)[None, :, None]
    shape = (2, NLAT, NLON * LEVELS)
    values = jax.random.normal(key, shape, jnp.float32)
    return (values * scale).astype(jnp.float32)


def draw_cutoff(key, part):
    index = jnp.arange(NLAT, dtype=jnp.int32)
    distance = jnp.minimum(index, NLAT - 1 - index)
    jitter = jax.random.randint(key, (NLAT,), 0, 3, dtype=jnp.int32)
    polar_value = 1 + distance * (NLON // 4 - 3) // POLAR + jnp.where(distance > 0, jitter, 0)
    return jnp.where(distance < POLAR, polar_value, NLON // 2).astype(jnp.int32)


def levels(key, dims, shards, low, top_value):
    def one(axis_at, shards_of):
        steps = jax.random.uniform(jax.random.fold_in(jax.random.fold_in(key, 6), axis_at), (shards_of,), jnp.float32, low / len(shards), top_value / len(shards))
        return jnp.repeat(jnp.exp(steps), dims[axis_at] // shards_of).reshape((-1,) + (1,) * (len(dims) - axis_at - 1))

    gain = one(*shards[0])
    for cut in shards[1:]:
        gain = gain * one(*cut)
    return gain


def setup_inputs(seed: int = 0) -> dict:
    seeds = jax.random.split(jax.random.key(seed), 5)
    winds = draw_winds(jax.random.fold_in(seeds[4], 71), 0)
    thickness = jnp.clip(0.5 + 1.0 * jax.random.uniform(seeds[1], (NLAT, NLON * LEVELS), jnp.float32) ** levels(seeds[1], (NLAT, NLON * LEVELS), ((0, 8), (1, 4)), -0.2, 0.2), 0.5, 1.5)
    tracers = jnp.clip(1.0 * jax.random.uniform(seeds[2], (3, NLAT, NLON * LEVELS), jnp.float32) ** levels(seeds[2], (3, NLAT, NLON * LEVELS), ((1, 8), (2, 4)), -0.2, 0.2), 0.0, 1.0).astype(jnp.bfloat16)
    cutoff = draw_cutoff(jax.random.fold_in(seeds[4], 71), 0)
    return {"winds": winds, "thickness": thickness, "tracers": tracers, "cutoff": cutoff}


TIME_STEP = 0.05
DIFFUSION = 0.5


def grid_rows(first_row, count, nlat):
    index = first_row + jnp.arange(count, dtype=jnp.int32)
    centre = (index.astype(jnp.float32) + 0.5) * (math.pi / nlat) - math.pi / 2

    def face(row_index):
        inside = (row_index >= 0) & (row_index < nlat - 1)
        return jnp.where(inside, jnp.sin((row_index + 1).astype(jnp.float32) * (math.pi / nlat)), 0.0)

    return (jnp.cos(centre)[:, None], jnp.sin(centre)[:, None], face(index)[:, None], face(index - 1)[:, None])


def tendencies(thick, wind_u, wind_v, tracer, thick_e, thick_w, wind_ue, wind_uw, tracer_e, tracer_w,
               thick_n, thick_s, wind_vn, wind_vs, tracer_n, tracer_s, cos_centre, sin_centre, cos_north,
               cos_south, ratio):
    flux_east = 0.5 * (wind_u + wind_ue) * (0.5 * (thick + thick_e))
    flux_west = 0.5 * (wind_uw + wind_u) * (0.5 * (thick_w + thick))
    flux_north = 0.5 * (wind_v + wind_vn) * (0.5 * (thick + thick_n)) * cos_north
    flux_south = 0.5 * (wind_vs + wind_v) * (0.5 * (thick_s + thick)) * cos_south
    thick_tend = -((flux_east - flux_west) + ratio * (flux_north - flux_south)) / cos_centre
    wind_u_tend = sin_centre * wind_v - (thick_e - thick_w) / (2.0 * cos_centre)
    wind_v_tend = -sin_centre * wind_u - ratio * (thick_n - thick_s) * 0.5
    zonal_part = flux_east * (0.5 * (tracer + tracer_e)) - flux_west * (0.5 * (tracer_w + tracer))
    merid_part = flux_north * (0.5 * (tracer + tracer_n)) - flux_south * (0.5 * (tracer_s + tracer))
    tracer_flux = (zonal_part + ratio * merid_part) / cos_centre
    laplace = (tracer_e + tracer_w) + (tracer_n + tracer_s) - 4.0 * tracer
    tracer_mass = thick * tracer + TIME_STEP * (DIFFUSION * laplace - tracer_flux)
    return thick_tend, wind_u_tend, wind_v_tend, tracer_mass


def zonal_filter(field, cutoff, nlon):
    spectrum = jnp.fft.rfft(field, axis=-1)
    wave = jnp.arange(nlon // 2 + 1, dtype=jnp.int32)
    keep = wave[None, :] <= cutoff[:, None]
    return jnp.fft.irfft(jnp.where(keep, spectrum, 0.0), n=nlon, axis=-1).astype(jnp.float32)


def reference(winds, thickness, tracers, cutoff):
    nlat = thickness.shape[0]
    nlon = thickness.shape[1] // LEVELS
    half = nlon // 2
    ratio = 2.0 * nlat / nlon
    cos_centre, sin_centre, cos_north, cos_south = grid_rows(0, nlat, nlat)

    def unpack(field):
        shaped = field.reshape(field.shape[:-2] + (nlat, nlon, LEVELS))
        return jnp.moveaxis(shaped, -1, -3)

    def pack(field):
        moved = jnp.moveaxis(field, -3, -1)
        return moved.reshape(moved.shape[:-3] + (nlat, nlon * LEVELS))

    def east(field):
        return jnp.roll(field, -1, axis=-1)

    def west(field):
        return jnp.roll(field, 1, axis=-1)

    def north(field, sign):
        return jnp.concatenate([field[..., 1:, :], sign * jnp.roll(field[..., -1:, :], half, axis=-1)], axis=-2)

    def south(field, sign):
        return jnp.concatenate([sign * jnp.roll(field[..., :1, :], half, axis=-1), field[..., :-1, :]], axis=-2)

    def one_level(inputs):
        thick, wind_u, wind_v, tracer = inputs
        thick_tend, wind_u_tend, wind_v_tend, tracer_mass = tendencies(
            thick, wind_u, wind_v, tracer, east(thick), west(thick), east(wind_u), west(wind_u),
            east(tracer), west(tracer), north(thick, 1.0), south(thick, 1.0), north(wind_v, -1.0),
            south(wind_v, -1.0), north(tracer, 1.0), south(tracer, 1.0), cos_centre, sin_centre,
            cos_north, cos_south, ratio)
        new_thick = thick + TIME_STEP * zonal_filter(thick_tend, cutoff, nlon)
        new_u = wind_u + TIME_STEP * zonal_filter(wind_u_tend, cutoff, nlon)
        new_v = wind_v + TIME_STEP * zonal_filter(wind_v_tend, cutoff, nlon)
        return new_thick, new_u, new_v, tracer_mass

    level_winds = unpack(winds)
    level_tracers = unpack(tracers.astype(jnp.float32))
    new_thick, new_u, new_v, masses = lax.map(
        one_level, (unpack(thickness), level_winds[0], level_winds[1], jnp.moveaxis(level_tracers, 1, 0)))
    mass_out = pack(jnp.moveaxis(masses, 0, 1)).astype(jnp.bfloat16)
    return pack(jnp.stack([new_u, new_v])), pack(new_thick), mass_out
```

```python
import functools
import math

import jax
import jax.numpy as jnp
import numpy as np
from jax import lax
from jax.experimental import pallas as pl
from jax.experimental.pallas import tpu as pltpu
from jax.sharding import PartitionSpec as P

LEVELS = 16
TIME_STEP = 0.05
DIFFUSION = 0.5
LANES = 128
PER_TILE = LANES // LEVELS
EXT_ROWS = 16
LIMIT = 48 * 1024 * 1024


class Sizes:
    def __init__(self, rows, merged, n_lat, n_lon):
        self.rows = rows
        self.merged = merged
        self.columns = merged // LEVELS
        self.n_lat = n_lat
        self.n_lon = n_lon
        self.nlat = rows * n_lat
        self.nlon = self.columns * n_lon
        self.ratio = 2.0 * self.nlat / self.nlon
        self.tiles = -(-merged // LANES)
        self.tail = merged - (self.tiles - 1) * LANES
        self.stack = -(-(self.tiles + 1) // 8) * 8
        self.units = 3 * rows
        self.share = -(-self.units // n_lon)
        assert self.tail <= LANES - 2 * LEVELS and rows + 2 <= EXT_ROWS

    def span(self, tile):
        return self.tail if tile == self.tiles - 1 else LANES


def geometry(sz):
    table = np.zeros((sz.n_lat, 3, EXT_ROWS, LANES), np.float64)

    def face(j):
        return math.sin((j + 1) * math.pi / sz.nlat) if 0 <= j < sz.nlat - 1 else 0.0

    for band in range(sz.n_lat):
        for row in range(sz.rows):
            j = band * sz.rows + row
            centre = (j + 0.5) * math.pi / sz.nlat - math.pi / 2
            table[band, 0, row] = 1.0 / math.cos(centre)
            table[band, 1, row] = math.sin(centre)
            table[band, 2, row] = face(j)
        table[band, 2, EXT_ROWS - 1] = face(band * sz.rows - 1)
    return table.astype(np.float32)


def offsets(sz):
    shift, out_tile = np.divmod(np.arange(PER_TILE * sz.stack), sz.stack)
    sector, in_tile = np.divmod(np.arange(sz.n_lon * sz.stack), sz.stack)
    n = (PER_TILE * (out_tile - 1) + shift)[:, None] - (PER_TILE * in_tile + sz.columns * sector)[None, :]
    n = (n + sz.nlon // 2) % sz.nlon - sz.nlon // 2
    with np.errstate(divide="ignore"):
        inverse = np.where(n == 0, 0.0, 1.0 / (sz.nlon * np.sin(np.pi * n / sz.nlon)))
    return n.astype(np.float32), inverse.astype(np.float32)


def pack_kernel(sz, h_ref, w_ref, q_ref, east_ref, west_ref, north_ref, south_ref, across_ref):
    top = lax.axis_index("lat") == sz.n_lat - 1
    last = sz.rows - 1
    for f in range(5):
        to = slice(LEVELS * f, LEVELS * (f + 1))

        def load(lanes, other):
            if f < 2:
                source = (h_ref[:, lanes], w_ref[other, :, lanes])[f]
            else:
                source = q_ref[f - 2, :, lanes].astype(jnp.float32)
            return source

        east_ref[:, to] = load(slice(sz.merged - LEVELS, sz.merged), 0)
        west_ref[:, to] = load(slice(0, LEVELS), 0)
        for t in range(sz.tiles):
            wide = sz.span(t)
            block = load(slice(LANES * t, LANES * t + wide), 1)
            at = sz.stack * f + t
            north_ref[at : at + 1, :wide] = block[last : last + 1]
            south_ref[at : at + 1, :wide] = block[0:1]
            across_ref[at : at + 1, :wide] = jnp.where(top, block[last : last + 1], block[0:1])


def step_kernel(
    sz, h_ref, w_ref, q_ref, from_w, from_e, from_s, from_n, from_a, geo_ref, mass_ref, tend_ref, ext
):
    band = lax.axis_index("lat")
    bottom, top = band == 0, band == sz.n_lat - 1
    lane = lax.broadcasted_iota(jnp.int32, (EXT_ROWS, LANES), 1)
    wide = sz.tiles * LANES
    for f in range(6):
        if f == 0:
            ext[f, : sz.rows, : sz.merged] = h_ref[...]
        elif f == 1:
            ext[f, : sz.rows, : sz.merged] = w_ref[1]
        elif f == 5:
            ext[f, : sz.rows, : sz.merged] = w_ref[0]
        else:
            ext[f, : sz.rows, : sz.merged] = q_ref[f - 2].astype(jnp.float32)
    for f in range(5):
        flip = -1.0 if f == 1 else 1.0
        for t in range(sz.tiles):
            at = slice(sz.stack * f + t, sz.stack * f + t + 1)
            over = from_a[at] * flip
            lanes = slice(LANES * t, LANES * (t + 1))
            ext[f, sz.rows : sz.rows + 1, lanes] = jnp.where(top, over, from_n[at])
            ext[f, EXT_ROWS - 1 : EXT_ROWS, lanes] = jnp.where(bottom, over, from_s[at])
    lane9 = lane[: sz.rows]
    end = (sz.tiles - 1) * LANES
    for place, f in enumerate((0, 5, 2, 3, 4)):
        after = pltpu.roll(from_e[...], (sz.tail - LEVELS * place) % LANES, 1)
        before = pltpu.roll(from_w[...], (LANES - LEVELS - LEVELS * place) % LANES, 1)
        own = ext[f, : sz.rows, end:wide]
        edge = jnp.where(lane9 < LANES - LEVELS, after, before)
        ext[f, : sz.rows, end:wide] = jnp.where(lane9 < sz.tail, own, edge)

    inv_cos = geo_ref[band, 0]
    sin_centre = geo_ref[band, 1]
    cos_face = geo_ref[band, 2]
    ratio = sz.ratio
    tiles = sz.tiles
    rolled = {}

    def tile(f, t):
        t = t % tiles
        return ext[f, :, LANES * t : LANES * (t + 1)]

    def turned(name, t, value, step):
        if (name, t, step) not in rolled:
            rolled[name, t, step] = pltpu.roll(value(t), step % LANES, 1)
        return rolled[name, t, step]

    def east(name, t, value):
        here = turned(name, t, value, -LEVELS)
        return jnp.where(lane < LANES - LEVELS, here, turned(name, (t + 1) % tiles, value, -LEVELS))

    def west(name, t, value):
        here = turned(name, t, value, LEVELS)
        return jnp.where(lane >= LEVELS, here, turned(name, (t - 1) % tiles, value, LEVELS))

    def north(value):
        return pltpu.roll(value, EXT_ROWS - 1, 0)

    def south(value):
        return pltpu.roll(value, 1, 0)

    kept = {}

    def zonal(t):
        t = t % tiles
        if t not in kept:
            thick, wind_u = tile(0, t), tile(5, t)
            thick_e = east("h", t, functools.partial(tile, 0))
            wind_e = east("u", t, functools.partial(tile, 5))
            flux = 0.25 * (wind_u + wind_e) * (thick + thick_e) * inv_cos
            parts = []
            for k in range(3):
                q = tile(2 + k, t)
                q_e = east(k, t, functools.partial(tile, 2 + k))
                parts.append(DIFFUSION * (q_e - q) - flux * (0.5 * (q + q_e)))
            kept[t] = (flux, thick_e, parts)
        return kept[t]

    for t in range(tiles):
        span = sz.span(t)
        lanes = slice(LANES * t, LANES * t + span)
        flux, thick_e, parts = zonal(t)
        thick, wind_u, wind_v = tile(0, t), tile(5, t), tile(1, t)
        flux_w = west("f", t, lambda s: zonal(s)[0])
        thick_w = west("hw", t, functools.partial(tile, 0))
        thick_n = north(thick)
        flux_n = (0.25 * ratio) * (wind_v + north(wind_v)) * (thick + thick_n) * cos_face
        flux_s = south(flux_n)
        thick_tend = -((flux - flux_w) + (flux_n - flux_s) * inv_cos)
        wind_u_tend = sin_centre * wind_v - (thick_e - thick_w) * (0.5 * inv_cos)
        wind_v_tend = -sin_centre * wind_u - (0.5 * ratio) * (thick_n - south(thick))
        for k in range(3):
            q = tile(2 + k, t)
            q_n = north(q)
            zonal_part = parts[k] - west(("p", k), t, lambda s: zonal(s)[2][k])
            lap = q_n + south(q) - 2.0 * q
            over = flux_n * (0.5 * (q + q_n))
            merid_part = DIFFUSION * lap - (over - south(over)) * inv_cos
            mass = thick * q + TIME_STEP * (zonal_part + merid_part)
            mass_ref[k, :, lanes] = mass[: sz.rows, :span].astype(jnp.bfloat16)
        for f, tend in enumerate((thick_tend, wind_u_tend, wind_v_tend)):
            if span < LANES:
                tend = jnp.where(lane < span, tend, 0.0)
            first = sz.stack * sz.rows * f + t
            tend_ref[pl.ds(first, sz.rows, stride=sz.stack), :] = tend[: sz.rows]
    for f in range(3):
        for t in range(tiles, sz.stack):
            first = sz.stack * sz.rows * f + t
            tend_ref[pl.ds(first, sz.rows, stride=sz.stack), :] = jnp.zeros((sz.rows, LANES), jnp.float32)
    spare = sz.stack * sz.units
    if spare < tend_ref.shape[0]:
        tend_ref[spare:, :] = jnp.zeros((tend_ref.shape[0] - spare, LANES), jnp.float32)


def sin_pi(y):
    y = jnp.where(y > 0.5, 1.0 - y, jnp.where(y < -0.5, -1.0 - y, y))
    s = y * y
    series = [(-1) ** i * math.pi ** (2 * i + 1) / math.factorial(2 * i + 1) for i in range(7)]
    total = series[-1]
    for factor in reversed(series[:-1]):
        total = total * s + factor
    return total * y


def filter_kernel(sz, cut_ref, n_ref, inverse_ref, in_ref, out_ref):
    band, sector = lax.axis_index("lat"), lax.axis_index("lon")
    stack, nlon = sz.stack, sz.nlon
    lane = lax.broadcasted_iota(jnp.int32, (stack, LANES), 1)
    n = n_ref[...]
    inverse = inverse_ref[...]
    for i in range(sz.share):
        unit = sector * sz.share + i
        row = lax.rem(unit, sz.rows)
        width = 2 * cut_ref[band * sz.rows + row] + 1
        width = width.astype(jnp.float32)
        turns = n * width
        turns = turns - jnp.round(turns * (0.5 / nlon)) * (2.0 * nlon)
        weights = sin_pi(turns * (1.0 / nlon)) * inverse
        weights = jnp.where(n == 0.0, width * (1.0 / nlon), weights).astype(jnp.bfloat16)
        pieces = [in_ref[s, stack * i : stack * (i + 1)].astype(jnp.bfloat16) for s in range(sz.n_lon)]
        circle = jnp.concatenate(
            [jnp.concatenate(pieces[s:] + pieces[:s], axis=0) for s in range(sz.n_lon)], axis=1
        )
        spread = jnp.dot(weights, circle, preferred_element_type=jnp.float32)
        for s in range(sz.n_lon):
            same = spread[:stack, LANES * s : LANES * (s + 1)]
            carried = None
            for e in range(1, PER_TILE):
                part = spread[stack * e : stack * (e + 1), LANES * s : LANES * (s + 1)]
                part = pltpu.roll(part, LEVELS * e, 1)
                inside = lane >= LEVELS * e
                same = same + jnp.where(inside, part, 0.0)
                over = jnp.where(inside, 0.0, part)
                carried = over if carried is None else carried + over
            out_ref[s, stack * i : stack * (i + 1)] = pltpu.roll(same, stack - 1, 0) + carried


def finish_kernel(sz, cut_ref, h_ref, w_ref, tend_ref, back_ref, new_w_ref, new_h_ref):
    band = lax.axis_index("lat")
    row = lax.broadcasted_iota(jnp.int32, (sz.rows, LANES), 0)
    cuts = jnp.zeros((sz.rows, LANES), jnp.int32)
    for j in range(sz.rows):
        cuts = jnp.where(row == j, cut_ref[band * sz.rows + j], cuts)
    active = cuts < sz.nlon // 2
    for f in range(3):
        for t in range(sz.tiles):
            span = sz.span(t)
            lanes = slice(LANES * t, LANES * t + span)
            at = pl.ds(sz.stack * sz.rows * f + t, sz.rows, stride=sz.stack)
            tend = jnp.where(active, back_ref[at, :], tend_ref[at, :])[:, :span]
            if f == 0:
                new_h_ref[:, lanes] = h_ref[:, lanes] + TIME_STEP * tend
            else:
                new_w_ref[f - 1, :, lanes] = w_ref[f - 1, :, lanes] + TIME_STEP * tend


def local(winds, thickness, tracers, cutoff):
    n_lat = lax.axis_size("lat")
    n_lon = lax.axis_size("lon")
    rows, merged = thickness.shape
    sz = Sizes(rows, merged, n_lat, n_lon)
    f32 = jnp.float32
    vmem = pl.BlockSpec(memory_space=pltpu.VMEM)
    smem = pl.BlockSpec(memory_space=pltpu.SMEM)
    params = pltpu.CompilerParams(vmem_limit_bytes=LIMIT)
    band_rows = jax.ShapeDtypeStruct((5 * sz.stack, LANES), f32)
    edge = jax.ShapeDtypeStruct((rows, LANES), f32)

    to_e, to_w, to_n, to_s, to_a = pl.pallas_call(
        functools.partial(pack_kernel, sz),
        out_shape=(edge, edge, band_rows, band_rows, band_rows),
        in_specs=[vmem] * 3,
        out_specs=(vmem,) * 5,
        compiler_params=params,
        name="pack",
    )(thickness, winds, tracers)

    up = [(i, i + 1) for i in range(n_lat - 1)]
    down = [(i + 1, i) for i in range(n_lat - 1)]
    from_s = lax.ppermute(to_n, "lat", up)
    from_n = lax.ppermute(to_s, "lat", down)
    poles = [
        (band * n_lon + i, band * n_lon + (i + n_lon // 2) % n_lon) for band in (0, n_lat - 1) for i in range(n_lon)
    ]
    from_a = lax.ppermute(to_a, ("lat", "lon"), poles)
    from_w = lax.ppermute(to_e, "lon", [(i, (i + 1) % n_lon) for i in range(n_lon)])
    from_e = lax.ppermute(to_w, "lon", [((i + 1) % n_lon, i) for i in range(n_lon)])

    total = sz.share * n_lon * sz.stack
    mass, tend = pl.pallas_call(
        functools.partial(step_kernel, sz),
        out_shape=(
            jax.ShapeDtypeStruct(tracers.shape, jnp.bfloat16),
            jax.ShapeDtypeStruct((total, LANES), f32),
        ),
        in_specs=[vmem] * 9,
        out_specs=(vmem,) * 2,
        scratch_shapes=[pltpu.VMEM((6, EXT_ROWS, sz.tiles * LANES), f32)],
        compiler_params=params,
        name="step",
    )(thickness, winds, tracers, from_w, from_e, from_s, from_n, from_a, jnp.asarray(geometry(sz)))

    split = (n_lon, sz.share * sz.stack, LANES)
    sent = lax.all_to_all(tend.reshape(split), "lon", 0, 0)
    n, inverse = offsets(sz)
    worked = pl.pallas_call(
        functools.partial(filter_kernel, sz),
        out_shape=jax.ShapeDtypeStruct(split, f32),
        in_specs=[smem] + [vmem] * 3,
        out_specs=vmem,
        compiler_params=params,
        name="filter",
    )(cutoff, jnp.asarray(n), jnp.asarray(inverse), sent)
    back = lax.all_to_all(worked, "lon", 0, 0).reshape(total, LANES)

    new_w, new_h = pl.pallas_call(
        functools.partial(finish_kernel, sz),
        out_shape=(jax.ShapeDtypeStruct(winds.shape, f32), jax.ShapeDtypeStruct(thickness.shape, f32)),
        in_specs=[smem] + [vmem] * 4,
        out_specs=(vmem,) * 2,
        compiler_params=params,
        name="finish",
    )(cutoff, thickness, winds, tend, back)
    return new_w, new_h, mass


def solution(mesh):
    in_specs = (P(None, "lat", "lon"), P("lat", "lon"), P(None, "lat", "lon"), P())
    out_specs = (P(None, "lat", "lon"), P("lat", "lon"), P(None, "lat", "lon"))
    return jax.shard_map(local, mesh=mesh, in_specs=in_specs, out_specs=out_specs, check_vma=False)
```

```python
import functools
import math

import jax
import jax.numpy as jnp
import numpy as np
from jax import lax
from jax.experimental import pallas as pl
from jax.experimental.pallas import tpu as pltpu
from jax.sharding import PartitionSpec as P

LEVELS = 16
TIME_STEP = 0.05
DIFFUSION = 0.5
LANES = 128
PER_TILE = LANES // LEVELS
EXT_ROWS = 16
LIMIT = 48 * 1024 * 1024


class Sizes:
    def __init__(self, rows, merged, n_lat, n_lon):
        self.rows = rows
        self.merged = merged
        self.columns = merged // LEVELS
        self.n_lat = n_lat
        self.n_lon = n_lon
        self.nlat = rows * n_lat
        self.nlon = self.columns * n_lon
        self.ratio = 2.0 * self.nlat / self.nlon
        self.tiles = -(-merged // LANES)
        self.tail = merged - (self.tiles - 1) * LANES
        self.stack = -(-(self.tiles + 1) // 8) * 8
        self.units = 3 * rows
        self.share = -(-self.units // n_lon)
        assert self.tail <= LANES - 2 * LEVELS and rows + 2 <= EXT_ROWS

    def span(self, tile):
        return self.tail if tile == self.tiles - 1 else LANES


def geometry(sz):
    table = np.zeros((sz.n_lat, 3, EXT_ROWS, LANES), np.float64)

    def face(j):
        return math.sin((j + 1) * math.pi / sz.nlat) if 0 <= j < sz.nlat - 1 else 0.0

    for band in range(sz.n_lat):
        for row in range(sz.rows):
            j = band * sz.rows + row
            centre = (j + 0.5) * math.pi / sz.nlat - math.pi / 2
            table[band, 0, row] = 1.0 / math.cos(centre)
            table[band, 1, row] = math.sin(centre)
            table[band, 2, row] = face(j)
        table[band, 2, EXT_ROWS - 1] = face(band * sz.rows - 1)
    return table.astype(np.float32)


def offsets(sz):
    shift, out_tile = np.divmod(np.arange(PER_TILE * sz.stack), sz.stack)
    sector, in_tile = np.divmod(np.arange(sz.n_lon * sz.stack), sz.stack)
    n = (PER_TILE * (out_tile - 1) + shift)[:, None] - (PER_TILE * in_tile + sz.columns * sector)[None, :]
    n = (n + sz.nlon // 2) % sz.nlon - sz.nlon // 2
    with np.errstate(divide="ignore"):
        inverse = np.where(n == 0, 0.0, 1.0 / (sz.nlon * np.sin(np.pi * n / sz.nlon)))
    return n.astype(np.float32), inverse.astype(np.float32)


def pack_kernel(sz, h_ref, w_ref, q_ref, east_ref, west_ref, near_ref, far_ref):
    even = lax.rem(lax.axis_index("lat"), 2) == 0
    last = sz.rows - 1
    for f in range(5):
        to = slice(LEVELS * f, LEVELS * (f + 1))

        def load(lanes, other):
            if f < 2:
                return (h_ref[:, lanes], w_ref[other, :, lanes])[f]
            return q_ref[f - 2, :, lanes].astype(jnp.float32)

        east_ref[:, to] = load(slice(sz.merged - LEVELS, sz.merged), 0)
        west_ref[:, to] = load(slice(0, LEVELS), 0)
        for t in range(sz.tiles):
            wide = sz.span(t)
            block = load(slice(LANES * t, LANES * t + wide), 1)
            at = sz.stack * f + t
            near_ref[at : at + 1, :wide] = jnp.where(even, block[last : last + 1], block[0:1])
            far_ref[at : at + 1, :wide] = jnp.where(even, block[0:1], block[last : last + 1])


def step_kernel(sz, h_ref, w_ref, q_ref, from_w, from_e, near_ref, far_ref, geo_ref, mass_ref, *refs):
    out_refs, (tend_ref, ext) = refs[: sz.n_lon], refs[sz.n_lon :]
    band = lax.axis_index("lat")
    even = lax.rem(band, 2) == 0
    over_pole = (band == 0) | (band == sz.n_lat - 1)
    lane = lax.broadcasted_iota(jnp.int32, (EXT_ROWS, LANES), 1)
    wide = sz.tiles * LANES
    for f in range(6):
        if f == 0:
            ext[f, : sz.rows, : sz.merged] = h_ref[...]
        elif f == 1:
            ext[f, : sz.rows, : sz.merged] = w_ref[1]
        elif f == 5:
            ext[f, : sz.rows, : sz.merged] = w_ref[0]
        else:
            ext[f, : sz.rows, : sz.merged] = q_ref[f - 2].astype(jnp.float32)
    for f in range(5):
        flip = jnp.where(over_pole, -1.0, 1.0) if f == 1 else 1.0
        for t in range(sz.tiles):
            at = slice(sz.stack * f + t, sz.stack * f + t + 1)
            near, far = near_ref[at], far_ref[at] * flip
            lanes = slice(LANES * t, LANES * (t + 1))
            ext[f, sz.rows : sz.rows + 1, lanes] = jnp.where(even, near, far)
            ext[f, EXT_ROWS - 1 : EXT_ROWS, lanes] = jnp.where(even, far, near)
    lane9 = lane[: sz.rows]
    end = (sz.tiles - 1) * LANES
    for place, f in enumerate((0, 5, 2, 3, 4)):
        after = pltpu.roll(from_e[...], (sz.tail - LEVELS * place) % LANES, 1)
        before = pltpu.roll(from_w[...], (LANES - LEVELS - LEVELS * place) % LANES, 1)
        own = ext[f, : sz.rows, end:wide]
        edge = jnp.where(lane9 < LANES - LEVELS, after, before)
        ext[f, : sz.rows, end:wide] = jnp.where(lane9 < sz.tail, own, edge)

    inv_cos = geo_ref[band, 0]
    sin_centre = geo_ref[band, 1]
    cos_face = geo_ref[band, 2]
    ratio = sz.ratio
    tiles = sz.tiles
    rolled = {}

    def tile(f, t):
        t = t % tiles
        return ext[f, :, LANES * t : LANES * (t + 1)]

    def turned(name, t, value, step):
        if (name, t, step) not in rolled:
            rolled[name, t, step] = pltpu.roll(value(t), step % LANES, 1)
        return rolled[name, t, step]

    def east(name, t, value):
        here = turned(name, t, value, -LEVELS)
        return jnp.where(lane < LANES - LEVELS, here, turned(name, (t + 1) % tiles, value, -LEVELS))

    def west(name, t, value):
        here = turned(name, t, value, LEVELS)
        return jnp.where(lane >= LEVELS, here, turned(name, (t - 1) % tiles, value, LEVELS))

    def north(value):
        return pltpu.roll(value, EXT_ROWS - 1, 0)

    def south(value):
        return pltpu.roll(value, 1, 0)

    kept = {}

    def zonal(t):
        t = t % tiles
        if t not in kept:
            thick, wind_u = tile(0, t), tile(5, t)
            thick_e = east("h", t, functools.partial(tile, 0))
            wind_e = east("u", t, functools.partial(tile, 5))
            flux = 0.25 * (wind_u + wind_e) * (thick + thick_e) * inv_cos
            parts = []
            for k in range(3):
                q = tile(2 + k, t)
                q_e = east(k, t, functools.partial(tile, 2 + k))
                parts.append(DIFFUSION * (q_e - q) - flux * (0.5 * (q + q_e)))
            kept[t] = (flux, thick_e, parts)
        return kept[t]

    for t in range(tiles):
        span = sz.span(t)
        lanes = slice(LANES * t, LANES * t + span)
        flux, thick_e, parts = zonal(t)
        thick, wind_u, wind_v = tile(0, t), tile(5, t), tile(1, t)
        flux_w = west("f", t, lambda s: zonal(s)[0])
        thick_w = west("hw", t, functools.partial(tile, 0))
        thick_n = north(thick)
        flux_n = (0.25 * ratio) * (wind_v + north(wind_v)) * (thick + thick_n) * cos_face
        flux_s = south(flux_n)
        thick_tend = -((flux - flux_w) + (flux_n - flux_s) * inv_cos)
        wind_u_tend = sin_centre * wind_v - (thick_e - thick_w) * (0.5 * inv_cos)
        wind_v_tend = -sin_centre * wind_u - (0.5 * ratio) * (thick_n - south(thick))
        for k in range(3):
            q = tile(2 + k, t)
            q_n = north(q)
            zonal_part = parts[k] - west(("p", k), t, lambda s: zonal(s)[2][k])
            lap = q_n + south(q) - 2.0 * q
            over = flux_n * (0.5 * (q + q_n))
            merid_part = DIFFUSION * lap - (over - south(over)) * inv_cos
            mass = thick * q + TIME_STEP * (zonal_part + merid_part)
            mass_ref[k, :, lanes] = mass[: sz.rows, :span].astype(jnp.bfloat16)
        for f, tend in enumerate((thick_tend, wind_u_tend, wind_v_tend)):
            if span < LANES:
                tend = jnp.where(lane < span, tend, 0.0)
            first = sz.stack * sz.rows * f + t
            tend_ref[pl.ds(first, sz.rows, stride=sz.stack), :] = tend[: sz.rows]
    for f in range(3):
        for t in range(tiles, sz.stack):
            first = sz.stack * sz.rows * f + t
            tend_ref[pl.ds(first, sz.rows, stride=sz.stack), :] = jnp.zeros((sz.rows, LANES), jnp.float32)
    spare = sz.stack * sz.units
    if spare < tend_ref.shape[0]:
        tend_ref[spare:, :] = jnp.zeros((tend_ref.shape[0] - spare, LANES), jnp.float32)
    for p, out_ref in enumerate(out_refs):
        out_ref[...] = tend_ref[piece(sz, p), :]


def partner(sz, index, p):
    return jnp.bitwise_xor(index, p) if isinstance(index, jax.Array) else index ^ p


def piece(sz, p):
    size = sz.share * sz.stack
    return pl.ds(pl.multiple_of(partner(sz, lax.axis_index("lon"), p) * size, 8), size)


def sin_pi(y):
    y = jnp.where(y > 0.5, 1.0 - y, jnp.where(y < -0.5, -1.0 - y, y))
    s = y * y
    series = [(-1) ** i * math.pi ** (2 * i + 1) / math.factorial(2 * i + 1) for i in range(7)]
    total = series[-1]
    for factor in reversed(series[:-1]):
        total = total * s + factor
    return total * y


def filter_kernel(sz, cut_ref, n_ref, inverse_ref, *refs):
    in_refs, out_refs, (gathered, results) = refs[: sz.n_lon], refs[sz.n_lon : 2 * sz.n_lon], refs[2 * sz.n_lon :]
    for p, in_ref in enumerate(in_refs):
        gathered[piece(sz, p), :] = in_ref[...]
    size = sz.share * sz.stack
    band, sector = lax.axis_index("lat"), lax.axis_index("lon")
    stack, nlon = sz.stack, sz.nlon
    lane = lax.broadcasted_iota(jnp.int32, (stack, LANES), 1)
    n = n_ref[...]
    inverse = inverse_ref[...]
    for i in range(sz.share):
        unit = sector * sz.share + i
        row = lax.rem(unit, sz.rows)
        width = 2 * cut_ref[band * sz.rows + row] + 1
        width = width.astype(jnp.float32)
        turns = n * width
        turns = turns - jnp.round(turns * (0.5 / nlon)) * (2.0 * nlon)
        weights = sin_pi(turns * (1.0 / nlon)) * inverse
        weights = jnp.where(n == 0.0, width * (1.0 / nlon), weights).astype(jnp.bfloat16)
        starts = [size * s + stack * i for s in range(sz.n_lon)]
        pieces = [gathered[at : at + stack].astype(jnp.bfloat16) for at in starts]
        circle = jnp.concatenate(
            [jnp.concatenate(pieces[s:] + pieces[:s], axis=0) for s in range(sz.n_lon)], axis=1
        )
        spread = jnp.dot(weights, circle, preferred_element_type=jnp.float32)
        for s in range(sz.n_lon):
            same = spread[:stack, LANES * s : LANES * (s + 1)]
            carried = None
            for e in range(1, PER_TILE):
                part = spread[stack * e : stack * (e + 1), LANES * s : LANES * (s + 1)]
                part = pltpu.roll(part, LEVELS * e, 1)
                inside = lane >= LEVELS * e
                same = same + jnp.where(inside, part, 0.0)
                over = jnp.where(inside, 0.0, part)
                carried = over if carried is None else carried + over
            results[starts[s] : starts[s] + stack] = pltpu.roll(same, stack - 1, 0) + carried
    for p, out_ref in enumerate(out_refs):
        out_ref[...] = results[piece(sz, p), :]


def finish_kernel(sz, cut_ref, h_ref, w_ref, *refs):
    tend_refs, back_refs = refs[: sz.n_lon], refs[sz.n_lon : 2 * sz.n_lon]
    new_w_ref, new_h_ref, tend_ref, back_ref = refs[2 * sz.n_lon :]
    for p in range(sz.n_lon):
        tend_ref[piece(sz, p), :] = tend_refs[p][...]
        back_ref[piece(sz, p), :] = back_refs[p][...]
    band = lax.axis_index("lat")
    row = lax.broadcasted_iota(jnp.int32, (sz.rows, LANES), 0)
    cuts = jnp.zeros((sz.rows, LANES), jnp.int32)
    for j in range(sz.rows):
        cuts = jnp.where(row == j, cut_ref[band * sz.rows + j], cuts)
    active = cuts < sz.nlon // 2
    for f in range(3):
        for t in range(sz.tiles):
            span = sz.span(t)
            lanes = slice(LANES * t, LANES * t + span)
            at = pl.ds(sz.stack * sz.rows * f + t, sz.rows, stride=sz.stack)
            tend = jnp.where(active, back_ref[at, :], tend_ref[at, :])[:, :span]
            if f == 0:
                new_h_ref[:, lanes] = h_ref[:, lanes] + TIME_STEP * tend
            else:
                new_w_ref[f - 1, :, lanes] = w_ref[f - 1, :, lanes] + TIME_STEP * tend


def local(winds, thickness, tracers, cutoff):
    n_lat = lax.axis_size("lat")
    n_lon = lax.axis_size("lon")
    rows, merged = thickness.shape
    sz = Sizes(rows, merged, n_lat, n_lon)
    f32 = jnp.float32
    vmem = pl.BlockSpec(memory_space=pltpu.VMEM)
    smem = pl.BlockSpec(memory_space=pltpu.SMEM)
    params = pltpu.CompilerParams(vmem_limit_bytes=LIMIT)
    band_rows = jax.ShapeDtypeStruct((5 * sz.stack, LANES), f32)
    edge = jax.ShapeDtypeStruct((rows, LANES), f32)

    to_e, to_w, to_near, to_far = pl.pallas_call(
        functools.partial(pack_kernel, sz),
        out_shape=(edge, edge, band_rows, band_rows),
        in_specs=[vmem] * 3,
        out_specs=(vmem,) * 4,
        compiler_params=params,
        name="pack",
    )(thickness, winds, tracers)

    near = [(band * n_lon + i, (band ^ 1) * n_lon + i) for band in range(n_lat) for i in range(n_lon)]
    far = []
    for band in range(n_lat):
        other = band - 1 if band % 2 == 0 else band + 1
        for i in range(n_lon):
            if 0 <= other < n_lat:
                far.append((band * n_lon + i, other * n_lon + i))
            else:
                far.append((band * n_lon + i, band * n_lon + (i + n_lon // 2) % n_lon))
    from_near = lax.ppermute(to_near, ("lat", "lon"), near)
    from_far = lax.ppermute(to_far, ("lat", "lon"), far)
    from_w = lax.ppermute(to_e, "lon", [(i, (i + 1) % n_lon) for i in range(n_lon)])
    from_e = lax.ppermute(to_w, "lon", [((i + 1) % n_lon, i) for i in range(n_lon)])

    total = sz.share * n_lon * sz.stack
    share = jax.ShapeDtypeStruct((sz.share * sz.stack, LANES), f32)
    all_units = pltpu.VMEM((total, LANES), f32)
    mass, *tends = pl.pallas_call(
        functools.partial(step_kernel, sz),
        out_shape=(jax.ShapeDtypeStruct(tracers.shape, jnp.bfloat16),) + (share,) * n_lon,
        in_specs=[vmem] * 8,
        out_specs=(vmem,) * (1 + n_lon),
        scratch_shapes=[all_units, pltpu.VMEM((6, EXT_ROWS, sz.tiles * LANES), f32)],
        compiler_params=params,
        name="step",
    )(thickness, winds, tracers, from_w, from_e, from_near, from_far, jnp.asarray(geometry(sz)))

    def exchange(shares):
        pairs = [[(i, partner(sz, i, p)) for i in range(n_lon)] for p in range(n_lon)]
        return [shares[0]] + [lax.ppermute(shares[p], "lon", pairs[p]) for p in range(1, n_lon)]

    n, inverse = offsets(sz)
    worked = pl.pallas_call(
        functools.partial(filter_kernel, sz),
        out_shape=(share,) * n_lon,
        in_specs=[smem] + [vmem] * (2 + n_lon),
        out_specs=(vmem,) * n_lon,
        scratch_shapes=[all_units, all_units],
        compiler_params=params,
        name="filter",
    )(cutoff, jnp.asarray(n), jnp.asarray(inverse), *exchange(tends))

    new_w, new_h = pl.pallas_call(
        functools.partial(finish_kernel, sz),
        out_shape=(jax.ShapeDtypeStruct(winds.shape, f32), jax.ShapeDtypeStruct(thickness.shape, f32)),
        in_specs=[smem] + [vmem] * (2 + 2 * n_lon),
        out_specs=(vmem,) * 2,
        scratch_shapes=[all_units, all_units],
        compiler_params=params,
        name="finish",
    )(cutoff, thickness, winds, *tends, *exchange(worked))
    return new_w, new_h, mass


def solution(mesh):
    in_specs = (P(None, "lat", "lon"), P("lat", "lon"), P(None, "lat", "lon"), P())
    out_specs = (P(None, "lat", "lon"), P("lat", "lon"), P(None, "lat", "lon"))
    return jax.shard_map(local, mesh=mesh, in_specs=in_specs, out_specs=out_specs, check_vma=False)
```

```python
import functools
import math

import jax
import jax.numpy as jnp
import numpy as np
from jax import lax
from jax.experimental import pallas as pl
from jax.experimental.pallas import tpu as pltpu
from jax.sharding import PartitionSpec as P

LEVELS = 16
TIME_STEP = 0.05
DIFFUSION = 0.5
LANES = 128
PER_TILE = LANES // LEVELS
EXT_ROWS = 16
LIMIT = 48 * 1024 * 1024


class Sizes:
    def __init__(self, rows, merged, n_lat, n_lon):
        self.rows = rows
        self.merged = merged
        self.columns = merged // LEVELS
        self.n_lat = n_lat
        self.n_lon = n_lon
        self.nlat = rows * n_lat
        self.nlon = self.columns * n_lon
        self.ratio = 2.0 * self.nlat / self.nlon
        self.tiles = -(-merged // LANES)
        self.end = (self.tiles - 1) * LANES
        self.tail = merged - self.end
        self.stack = -(-(self.tiles + 1) // 8) * 8
        polar = self.nlat // 6
        self.full = polar // rows
        self.part = polar % rows
        assert self.tail <= LANES - 4 * LEVELS and rows + 2 <= EXT_ROWS and n_lat % 2 == 0

    def span(self, tile):
        return self.tail if tile == self.tiles - 1 else LANES

    def full_bands(self):
        return [b for b in range(self.n_lat) if min(b, self.n_lat - 1 - b) < self.full]

    def part_bands(self):
        return [b for b in range(self.n_lat) if min(b, self.n_lat - 1 - b) == self.full and self.part]

    def part_first(self, band):
        return jnp.where(band < self.n_lat // 2, 0, self.rows - self.part)


def geometry(sz):
    table = np.zeros((sz.n_lat, 3, EXT_ROWS, LANES), np.float64)

    def face(j):
        return math.sin((j + 1) * math.pi / sz.nlat) if 0 <= j < sz.nlat - 1 else 0.0

    for band in range(sz.n_lat):
        for row in range(sz.rows):
            j = band * sz.rows + row
            centre = (j + 0.5) * math.pi / sz.nlat - math.pi / 2
            table[band, 0, row] = 1.0 / math.cos(centre)
            table[band, 1, row] = math.sin(centre)
            table[band, 2, row] = face(j)
        table[band, 2, EXT_ROWS - 1] = face(band * sz.rows - 1)
    return table.astype(np.float32)


def offsets(sz):
    shift, out_tile = np.divmod(np.arange(PER_TILE * sz.stack), sz.stack)
    sector, in_tile = np.divmod(np.arange(sz.n_lon * sz.stack), sz.stack)
    n = (PER_TILE * (out_tile - 1) + shift)[:, None] - (PER_TILE * in_tile + sz.columns * sector)[None, :]
    n = (n + sz.nlon // 2) % sz.nlon - sz.nlon // 2
    with np.errstate(divide="ignore"):
        inverse = np.where(n == 0, 0.0, 1.0 / (sz.nlon * np.sin(np.pi * n / sz.nlon)))
    return n.astype(np.float32), inverse.astype(np.float32)


def rows_kernel(sz, h_hbm, w_hbm, q_hbm, near_ref, far_ref, h_rows, w_rows, q_rows, sems):
    last = sz.rows - 1
    copies = []
    for k, row in enumerate((0, last)):
        copies.append(pltpu.make_async_copy(h_hbm.at[pl.ds(row, 1)], h_rows.at[k], sems.at[k, 0]))
        copies.append(pltpu.make_async_copy(w_hbm.at[row], w_rows.at[k], sems.at[k, 1]))
        copies.append(pltpu.make_async_copy(q_hbm.at[row], q_rows.at[k], sems.at[k, 2]))
    for copy in copies:
        copy.start()
    for copy in copies:
        copy.wait()
    even = lax.rem(lax.axis_index("lat"), 2) == 0
    for t in range(sz.tiles):
        wide = sz.span(t)
        lanes = slice(LANES * t, LANES * t + wide)
        q = [q_rows[k, :, lanes].astype(jnp.float32) for k in range(2)]
        for f in range(5):
            if f == 0:
                first, final = h_rows[0, :, lanes], h_rows[1, :, lanes]
            elif f == 1:
                first, final = w_rows[0, 1:2, lanes], w_rows[1, 1:2, lanes]
            else:
                first, final = q[0][f - 2 : f - 1], q[1][f - 2 : f - 1]
            at = sz.stack * f + t
            near_ref[at : at + 1, :wide] = jnp.where(even, final, first)
            far_ref[at : at + 1, :wide] = jnp.where(even, first, final)


def columns_kernel(sz, h_ref, w_ref, q_ref, after_ref, east_ref, west_ref):
    for f in range(5):
        to = slice(LEVELS * f, LEVELS * (f + 1))

        def load(lanes):
            if f < 2:
                return (h_ref[:, lanes], w_ref[0, :, lanes])[f]
            return q_ref[f - 2, :, lanes].astype(jnp.float32)

        east_ref[:, to] = load(slice(sz.merged - LEVELS, sz.merged))
        west_ref[:, to] = load(slice(0, LEVELS))


def add_rows(sz, ext, fields, near_ref, far_ref):
    band = lax.axis_index("lat")
    even = lax.rem(band, 2) == 0
    over_pole = (band == 0) | (band == sz.n_lat - 1)
    for f in range(fields):
        flip = jnp.where(over_pole, -1.0, 1.0) if f == 1 else 1.0
        for t in range(sz.tiles):
            at = slice(sz.stack * f + t, sz.stack * f + t + 1)
            near, far = near_ref[at], far_ref[at] * flip
            lanes = slice(LANES * t, LANES * (t + 1))
            ext[f, sz.rows : sz.rows + 1, lanes] = jnp.where(even, near, far)
            ext[f, EXT_ROWS - 1 : EXT_ROWS, lanes] = jnp.where(even, far, near)


class Tiles:
    def __init__(self, sz):
        self.sz = sz
        self.lane = lax.broadcasted_iota(jnp.int32, (EXT_ROWS, LANES), 1)
        self.turned = {}

    def turn(self, name, t, value, step):
        key = (name, t % self.sz.tiles, step)
        if key not in self.turned:
            self.turned[key] = pltpu.roll(value(t % self.sz.tiles), step % LANES, 1)
        return self.turned[key]

    def east(self, name, t, value):
        here = self.turn(name, t, value, -LEVELS)
        return jnp.where(self.lane < LANES - LEVELS, here, self.turn(name, t + 1, value, -LEVELS))

    def west(self, name, t, value):
        here = self.turn(name, t, value, LEVELS)
        return jnp.where(self.lane >= LEVELS, here, self.turn(name, t - 1, value, LEVELS))


def north(value):
    return pltpu.roll(value, EXT_ROWS - 1, 0)


def south(value):
    return pltpu.roll(value, 1, 0)


def polar_kernel(sz, h_ref, w_ref, near_ref, far_ref, geo_ref, *refs):
    tend_ref, ext = refs[0], refs[-1]
    band = lax.axis_index("lat")
    ring = Tiles(sz)
    lane = ring.lane
    tiles, stack, rows = sz.tiles, sz.stack, sz.rows
    for f, value in enumerate((h_ref[...], w_ref[1], w_ref[0])):
        ext[f, :rows, sz.end :] = jnp.zeros((rows, LANES), jnp.float32)
        ext[f, :rows, : sz.merged] = value
    add_rows(sz, ext, 2, near_ref, far_ref)
    inv_cos, sin_centre, cos_face = geo_ref[band, 0], geo_ref[band, 1], geo_ref[band, 2]
    ratio = sz.ratio

    def tile(f, t):
        return ext[f, :, LANES * t : LANES * (t + 1)]

    kept = {}

    def zonal(t):
        if t not in kept:
            thick_e = ring.east("h", t, functools.partial(tile, 0))
            wind_e = ring.east("u", t, functools.partial(tile, 2))
            flux = 0.25 * (tile(2, t) + wind_e) * (tile(0, t) + thick_e) * inv_cos
            if t == tiles - 1:
                flux = jnp.where(lane < sz.tail - LEVELS, flux, 0.0)
            kept[t] = (flux, thick_e)
        return kept[t]

    for t in range(tiles):
        flux, thick_e = zonal(t)
        thick, wind_v, wind_u = tile(0, t), tile(1, t), tile(2, t)
        flux_w = ring.west("f", t, lambda s: zonal(s)[0])
        thick_w = ring.west("hw", t, functools.partial(tile, 0))
        thick_n = north(thick)
        flux_n = (0.25 * ratio) * (wind_v + north(wind_v)) * (thick + thick_n) * cos_face
        thick_tend = -((flux - flux_w) + (flux_n - south(flux_n)) * inv_cos)
        wind_u_tend = sin_centre * wind_v - (thick_e - thick_w) * (0.5 * inv_cos)
        wind_v_tend = -sin_centre * wind_u - (0.5 * ratio) * (thick_n - south(thick))
        for f, tend in enumerate((thick_tend, wind_u_tend, wind_v_tend)):
            if t == tiles - 1:
                spare = 0.0
                if f == 0:
                    last = sz.tail - LEVELS
                    columns = [(tile(0, 0), 0), (thick, last), (tile(2, 0), 0), (wind_u, last)]
                    for k, (source, at) in reversed(list(enumerate(columns))):
                        to = sz.tail + LEVELS * k
                        spare = jnp.where(lane < to + LEVELS, pltpu.roll(source, (to - at) % LANES, 1), spare)
                tend = jnp.where(lane < sz.tail, tend, spare)
            tend_ref[pl.ds(stack * rows * f + t, rows, stride=stack), :] = tend[:rows]
    for f in range(3):
        for t in range(tiles, stack):
            tend_ref[pl.ds(stack * rows * f + t, rows, stride=stack), :] = jnp.zeros((rows, LANES), jnp.float32)
    if sz.part:
        size = sz.part * stack
        first = sz.part_first(band)
        for f in range(3):
            start = pl.multiple_of((rows * f + first) * stack, 8)
            refs[1][size * f : size * (f + 1)] = tend_ref[pl.ds(start, size), :]


def rest_kernel(
    sz, h_ref, w_ref, q_ref, from_w, from_e, near_ref, far_ref, geo_ref, new_w_ref, new_h_ref, mass_ref, ext
):
    band = lax.axis_index("lat")
    ring = Tiles(sz)
    lane = ring.lane
    tiles, rows = sz.tiles, sz.rows
    for f in range(6):
        if f < 2 or f == 5:
            value = (h_ref[...], w_ref[1], w_ref[0])[min(f, 2)]
        else:
            value = q_ref[f - 2].astype(jnp.float32)
        ext[f, :rows, : sz.merged] = value
    add_rows(sz, ext, 5, near_ref, far_ref)
    lane9 = lane[:rows]
    for place, f in enumerate((0, 5, 2, 3, 4)):
        after = pltpu.roll(from_e[...], (sz.tail - LEVELS * place) % LANES, 1)
        before = pltpu.roll(from_w[...], (LANES - LEVELS - LEVELS * place) % LANES, 1)
        own = ext[f, :rows, sz.end :]
        edge = jnp.where(lane9 < LANES - LEVELS, after, before)
        ext[f, :rows, sz.end :] = jnp.where(lane9 < sz.tail, own, edge)
    inv_cos, sin_centre, cos_face = geo_ref[band, 0], geo_ref[band, 1], geo_ref[band, 2]
    ratio = sz.ratio

    def tile(f, t):
        return ext[f, :, LANES * t : LANES * (t + 1)]

    kept = {}

    def zonal(t):
        if t not in kept:
            thick_e = ring.east("h", t, functools.partial(tile, 0))
            wind_e = ring.east("u", t, functools.partial(tile, 5))
            flux = 0.25 * (tile(5, t) + wind_e) * (tile(0, t) + thick_e) * inv_cos
            parts = []
            for k in range(3):
                q = tile(2 + k, t)
                q_e = ring.east(k, t, functools.partial(tile, 2 + k))
                parts.append(DIFFUSION * (q_e - q) - flux * (0.5 * (q + q_e)))
            kept[t] = (flux, thick_e, parts)
        return kept[t]

    for t in range(tiles):
        span = sz.span(t)
        lanes = slice(LANES * t, LANES * t + span)
        flux, thick_e, parts = zonal(t)
        thick, wind_u, wind_v = tile(0, t), tile(5, t), tile(1, t)
        flux_w = ring.west("f", t, lambda s: zonal(s)[0])
        thick_w = ring.west("hw", t, functools.partial(tile, 0))
        thick_n = north(thick)
        flux_n = (0.25 * ratio) * (wind_v + north(wind_v)) * (thick + thick_n) * cos_face
        thick_tend = -((flux - flux_w) + (flux_n - south(flux_n)) * inv_cos)
        wind_u_tend = sin_centre * wind_v - (thick_e - thick_w) * (0.5 * inv_cos)
        wind_v_tend = -sin_centre * wind_u - (0.5 * ratio) * (thick_n - south(thick))
        new_h_ref[:, lanes] = (thick + TIME_STEP * thick_tend)[:rows, :span]
        new_w_ref[0, :, lanes] = (wind_u + TIME_STEP * wind_u_tend)[:rows, :span]
        new_w_ref[1, :, lanes] = (wind_v + TIME_STEP * wind_v_tend)[:rows, :span]
        for k in range(3):
            q = tile(2 + k, t)
            q_n = north(q)
            zonal_part = parts[k] - ring.west(("p", k), t, lambda s: zonal(s)[2][k])
            lap = q_n + south(q) - 2.0 * q
            over = flux_n * (0.5 * (q + q_n))
            merid_part = DIFFUSION * lap - (over - south(over)) * inv_cos
            mass = thick * q + TIME_STEP * (zonal_part + merid_part)
            mass_ref[k, :, lanes] = mass[:rows, :span].astype(jnp.bfloat16)


def sin_pi(y):
    y = jnp.where(y > 0.5, 1.0 - y, jnp.where(y < -0.5, -1.0 - y, y))
    s = y * y
    series = [(-1) ** i * math.pi ** (2 * i + 1) / math.factorial(2 * i + 1) for i in range(7)]
    total = series[-1]
    for factor in reversed(series[:-1]):
        total = total * s + factor
    return total * y


def weights_kernel(sz, cut_ref, n_ref, inverse_ref, after_ref, weights_ref):
    band = lax.axis_index("lat")
    size = PER_TILE * sz.stack
    for row in range(sz.rows):
        width = (2 * cut_ref[band * sz.rows + row] + 1).astype(jnp.float32)
        n = n_ref[...]
        turns = n * width
        turns = turns - jnp.round(turns * (0.5 / sz.nlon)) * (2.0 * sz.nlon)
        weights = sin_pi(turns * (1.0 / sz.nlon)) * inverse_ref[...]
        weights = jnp.where(n == 0.0, width * (1.0 / sz.nlon), weights)
        weights_ref[size * row : size * (row + 1)] = weights.astype(jnp.bfloat16)


def filter_rows(sz, pieces, gathered, inv_cos, count, first, weights_ref, results):
    stack, n_lon = sz.stack, sz.n_lon
    lane = lax.broadcasted_iota(jnp.int32, (count, LANES), 1)
    for s, ref in enumerate(pieces):
        gathered[s, : 3 * count * stack] = ref[...]
    sides = [ref[pl.ds(sz.tiles - 1, count, stride=stack), :] for ref in pieces]

    def column(s, k):
        return pltpu.roll(sides[s % n_lon], (-sz.tail - LEVELS * k) % LANES, 1)

    for s in range(n_lon):
        thick_w, thick_e = column(s, 1), column(s + 1, 0)
        flux = 0.25 * (column(s, 3) + column(s + 1, 2)) * (thick_w + thick_e) * inv_cos
        slope = 0.5 * inv_cos
        for f, (west_of, east_of) in enumerate(((flux, flux), (slope * thick_e, slope * thick_w))):
            at = pl.ds(stack * count * f + sz.tiles - 1, count, stride=stack)
            own = gathered[s, at, :]
            own = own - jnp.where(lane >= sz.tail - LEVELS, pltpu.roll(west_of, sz.tail - LEVELS, 1), 0.0)
            gathered[s, at, :] = jnp.where(lane < sz.tail, own, 0.0)
            at = pl.ds(stack * count * f, count, stride=stack)
            after = (s + 1) % n_lon
            gathered[after, at, :] = gathered[after, at, :] + jnp.where(lane < LEVELS, east_of, 0.0)

    wide = lax.broadcasted_iota(jnp.int32, (stack, LANES), 1)
    size = PER_TILE * stack
    for row in range(count):
        starts = [stack * (count * f + row) for f in range(3)]
        circle = jnp.concatenate(
            [jnp.concatenate([gathered[s, at : at + stack] for s in range(n_lon)], axis=0) for at in starts], axis=1
        ).astype(jnp.bfloat16)
        weights = weights_ref[pl.ds(pl.multiple_of(size * (first + row), 16), size), :]
        spread = jnp.dot(weights, circle, preferred_element_type=jnp.float32)
        for f in range(3):
            same = spread[:stack, LANES * f : LANES * (f + 1)]
            carried = None
            for e in range(1, PER_TILE):
                part = spread[stack * e : stack * (e + 1), LANES * f : LANES * (f + 1)]
                part = pltpu.roll(part, LEVELS * e, 1)
                inside = wide >= LEVELS * e
                same = same + jnp.where(inside, part, 0.0)
                over = jnp.where(inside, 0.0, part)
                carried = over if carried is None else carried + over
            start = pl.multiple_of(stack * (sz.rows * f + first + row), 8)
            results[pl.ds(start, stack), :] = pltpu.roll(same, stack - 1, 0) + carried


def filter_kernel(sz, cut_ref, geo_ref, weights_ref, h_ref, w_ref, plain_w_ref, plain_h_ref, *refs):
    n_lon, rows = sz.n_lon, sz.rows
    full_refs, part_refs = refs[:n_lon], refs[n_lon : 2 * n_lon]
    new_w_ref, new_h_ref, gathered, results = refs[-4:]
    band = lax.axis_index("lat")
    from_pole = jnp.minimum(band, sz.n_lat - 1 - band)

    @pl.when(from_pole < sz.full)
    def _():
        filter_rows(sz, full_refs, gathered, geo_ref[band, 0][:rows], rows, 0, weights_ref, results)

    if sz.part:

        @pl.when(from_pole == sz.full)
        def _():
            inv_cos = geo_ref[band, 0]
            low = band < sz.n_lat // 2
            inv_cos = jnp.where(low, inv_cos[: sz.part], inv_cos[rows - sz.part : rows])
            filter_rows(sz, part_refs, gathered, inv_cos, sz.part, sz.part_first(band), weights_ref, results)

    row = lax.broadcasted_iota(jnp.int32, (rows, LANES), 0)
    cuts = jnp.zeros((rows, LANES), jnp.int32)
    for j in range(rows):
        cuts = jnp.where(row == j, cut_ref[band * rows + j], cuts)
    active = cuts < sz.nlon // 2
    for f in range(3):
        for t in range(sz.tiles):
            span = sz.span(t)
            lanes = slice(LANES * t, LANES * t + span)
            tend = results[pl.ds(sz.stack * rows * f + t, rows, stride=sz.stack), :][:, :span]
            if f == 0:
                new = h_ref[:, lanes] + TIME_STEP * tend
                new_h_ref[:, lanes] = jnp.where(active[:, :span], new, plain_h_ref[:, lanes])
            else:
                new = w_ref[f - 1, :, lanes] + TIME_STEP * tend
                new_w_ref[f - 1, :, lanes] = jnp.where(active[:, :span], new, plain_w_ref[f - 1, :, lanes])


def local(winds, thickness, tracers, cutoff):
    n_lat = lax.axis_size("lat")
    n_lon = lax.axis_size("lon")
    rows, merged = thickness.shape
    sz = Sizes(rows, merged, n_lat, n_lon)
    f32 = jnp.float32
    vmem = pl.BlockSpec(memory_space=pltpu.VMEM)
    smem = pl.BlockSpec(memory_space=pltpu.SMEM)
    hbm = pl.BlockSpec(memory_space=pl.ANY)

    def shaped(*shape):
        return jax.ShapeDtypeStruct(shape, f32)

    def call(kernel, name, in_specs, out_shape, scratch=()):
        return pl.pallas_call(
            functools.partial(kernel, sz),
            out_shape=out_shape,
            in_specs=in_specs,
            out_specs=jax.tree.map(lambda _: vmem, out_shape),
            scratch_shapes=list(scratch),
            compiler_params=pltpu.CompilerParams(vmem_limit_bytes=LIMIT),
            name=name,
        )

    def over_circles(value, bands, step):
        pairs = [(b * n_lon + (i + step) % n_lon, b * n_lon + i) for b in bands for i in range(n_lon)]
        return lax.ppermute(value, ("lat", "lon"), pairs)

    geo = jnp.asarray(geometry(sz))
    n, inverse = (jnp.asarray(table) for table in offsets(sz))

    row_pair = shaped(5 * sz.stack, LANES)
    to_near, to_far = call(
        rows_kernel,
        "rows",
        [hbm] * 3,
        (row_pair, row_pair),
        [
            pltpu.VMEM((2, 1, merged), f32),
            pltpu.VMEM((2, 2, merged), f32),
            pltpu.VMEM((2, 3, merged), jnp.bfloat16),
            pltpu.SemaphoreType.DMA((2, 3)),
        ],
    )(thickness, jnp.swapaxes(winds, 0, 1), jnp.swapaxes(tracers, 0, 1))

    near = [(band * n_lon + i, (band ^ 1) * n_lon + i) for band in range(n_lat) for i in range(n_lon)]
    far = []
    for band in range(n_lat):
        other = band - 1 if band % 2 == 0 else band + 1
        for i in range(n_lon):
            if 0 <= other < n_lat:
                far.append((band * n_lon + i, other * n_lon + i))
            else:
                far.append((band * n_lon + i, band * n_lon + (i + n_lon // 2) % n_lon))
    from_near = lax.ppermute(to_near, ("lat", "lon"), near)
    from_far = lax.ppermute(to_far, ("lat", "lon"), far)

    tend_shapes = [shaped(3 * rows * sz.stack, LANES)]
    if sz.part:
        tend_shapes.append(shaped(3 * sz.part * sz.stack, LANES))
    tends = call(
        polar_kernel, "polar", [vmem] * 5, tend_shapes, [pltpu.VMEM((3, EXT_ROWS, sz.tiles * LANES), f32)]
    )(thickness, winds, from_near, from_far, geo)
    circles = []
    for tend, bands in zip(tends, (sz.full_bands(), sz.part_bands())):
        circles += [tend] + [over_circles(tend, bands, step) for step in range(1, n_lon)]

    weights = call(
        weights_kernel,
        "weights",
        [smem, vmem, vmem, hbm],
        jax.ShapeDtypeStruct((rows * PER_TILE * sz.stack, n_lon * sz.stack), jnp.bfloat16),
    )(cutoff, n, inverse, tends[0])

    edge = shaped(rows, LANES)
    to_e, to_w = call(columns_kernel, "columns", [vmem] * 3 + [hbm], (edge, edge))(
        thickness, winds, tracers, tends[0]
    )
    everywhere = range(n_lat)
    from_w = over_circles(to_e, everywhere, n_lon - 1)
    from_e = over_circles(to_w, everywhere, 1)

    plain_w, plain_h, mass = call(
        rest_kernel,
        "rest",
        [vmem] * 8,
        (shaped(*winds.shape), shaped(rows, merged), jax.ShapeDtypeStruct(tracers.shape, jnp.bfloat16)),
        [pltpu.VMEM((6, EXT_ROWS, sz.tiles * LANES), f32)],
    )(thickness, winds, tracers, from_w, from_e, from_near, from_far, geo)

    new_w, new_h = call(
        filter_kernel,
        "filter",
        [smem] + [vmem] * (6 + len(circles)),
        (shaped(*winds.shape), shaped(rows, merged)),
        [
            pltpu.VMEM((n_lon, 3 * rows * sz.stack, LANES), f32),
            pltpu.VMEM((3 * rows * sz.stack, LANES), f32),
        ],
    )(cutoff, geo, weights, thickness, winds, plain_w, plain_h, *circles)
    return new_w, new_h, mass


def solution(mesh):
    in_specs = (P(None, "lat", "lon"), P("lat", "lon"), P(None, "lat", "lon"), P())
    out_specs = (P(None, "lat", "lon"), P("lat", "lon"), P(None, "lat", "lon"))
    return jax.shard_map(local, mesh=mesh, in_specs=in_specs, out_specs=out_specs, check_vma=False)
```

```python
import functools
import math

import jax
import jax.numpy as jnp
import numpy as np
from jax import lax
from jax.experimental import pallas as pl
from jax.experimental.pallas import tpu as pltpu
from jax.sharding import PartitionSpec as P

LEVELS = 16
TIME_STEP = 0.05
DIFFUSION = 0.5
LANES = 128
PER_TILE = LANES // LEVELS
EXT_ROWS = 16
LIMIT = 48 * 1024 * 1024
ALL_VMEM = 64 * 1024 * 1024 - 256 * 1024


class Sizes:
    def __init__(self, rows, merged, n_lat, n_lon):
        self.rows = rows
        self.merged = merged
        self.columns = merged // LEVELS
        self.n_lat = n_lat
        self.n_lon = n_lon
        self.nlat = rows * n_lat
        self.nlon = self.columns * n_lon
        self.ratio = 2.0 * self.nlat / self.nlon
        self.tiles = -(-merged // LANES)
        self.end = (self.tiles - 1) * LANES
        self.tail = merged - self.end
        self.stack = -(-(self.tiles + 1) // 8) * 8
        polar = self.nlat // 6
        self.full = polar // rows
        self.part = polar % rows
        assert self.tail <= LANES - 4 * LEVELS and rows + 2 <= EXT_ROWS and n_lat % 2 == 0
        assert n_lon & (n_lon - 1) == 0

    def span(self, tile):
        return self.tail if tile == self.tiles - 1 else LANES

    def full_bands(self):
        return [b for b in range(self.n_lat) if min(b, self.n_lat - 1 - b) < self.full]

    def part_bands(self):
        return [b for b in range(self.n_lat) if min(b, self.n_lat - 1 - b) == self.full and self.part]

    def part_first(self, band):
        return jnp.where(band < self.n_lat // 2, 0, self.rows - self.part)


def geometry(sz):
    table = np.zeros((sz.n_lat, 3, EXT_ROWS, LANES), np.float64)

    def face(j):
        return math.sin((j + 1) * math.pi / sz.nlat) if 0 <= j < sz.nlat - 1 else 0.0

    for band in range(sz.n_lat):
        for row in range(sz.rows):
            j = band * sz.rows + row
            centre = (j + 0.5) * math.pi / sz.nlat - math.pi / 2
            table[band, 0, row] = 1.0 / math.cos(centre)
            table[band, 1, row] = math.sin(centre)
            table[band, 2, row] = face(j)
        table[band, 2, EXT_ROWS - 1] = face(band * sz.rows - 1)
    return table.astype(np.float32)


def offsets(sz):
    shift, out_tile = np.divmod(np.arange(PER_TILE * sz.stack), sz.stack)
    sector, in_tile = np.divmod(np.arange(sz.n_lon * sz.stack), sz.stack)
    n = (PER_TILE * (out_tile - 1) + shift)[:, None] - (PER_TILE * in_tile + sz.columns * sector)[None, :]
    n = (n + sz.nlon // 2) % sz.nlon - sz.nlon // 2
    with np.errstate(divide="ignore"):
        inverse = np.where(n == 0, 0.0, 1.0 / (sz.nlon * np.sin(np.pi * n / sz.nlon)))
    return n.astype(np.float32), inverse.astype(np.float32)


def rows_kernel(sz, h_hbm, w_hbm, q_hbm, near_ref, far_ref, h_rows, w_rows, q_rows, sems):
    last = sz.rows - 1
    copies = []
    for k, row in enumerate((0, last)):
        copies.append(pltpu.make_async_copy(h_hbm.at[pl.ds(row, 1)], h_rows.at[k], sems.at[k, 0]))
        copies.append(pltpu.make_async_copy(w_hbm.at[row], w_rows.at[k], sems.at[k, 1]))
        copies.append(pltpu.make_async_copy(q_hbm.at[row], q_rows.at[k], sems.at[k, 2]))
    for copy in copies:
        copy.start()
    for copy in copies:
        copy.wait()
    even = lax.rem(lax.axis_index("lat"), 2) == 0
    for t in range(sz.tiles):
        wide = sz.span(t)
        lanes = slice(LANES * t, LANES * t + wide)
        q = [q_rows[k, :, lanes].astype(jnp.float32) for k in range(2)]
        for f in range(5):
            if f == 0:
                first, final = h_rows[0, :, lanes], h_rows[1, :, lanes]
            elif f == 1:
                first, final = w_rows[0, 1:2, lanes], w_rows[1, 1:2, lanes]
            else:
                first, final = q[0][f - 2 : f - 1], q[1][f - 2 : f - 1]
            at = sz.stack * f + t
            near_ref[at : at + 1, :wide] = jnp.where(even, final, first)
            far_ref[at : at + 1, :wide] = jnp.where(even, first, final)


def columns_kernel(sz, h_ref, w_ref, q_ref, after_ref, east_ref, west_ref):
    for f in range(5):
        to = slice(LEVELS * f, LEVELS * (f + 1))

        def load(lanes):
            if f < 2:
                return (h_ref[:, lanes], w_ref[0, :, lanes])[f]
            return q_ref[f - 2, :, lanes].astype(jnp.float32)

        east_ref[:, to] = load(slice(sz.merged - LEVELS, sz.merged))
        west_ref[:, to] = load(slice(0, LEVELS))


def add_rows(sz, ext, fields, near_ref, far_ref):
    band = lax.axis_index("lat")
    even = lax.rem(band, 2) == 0
    over_pole = (band == 0) | (band == sz.n_lat - 1)
    for f in range(fields):
        flip = jnp.where(over_pole, -1.0, 1.0) if f == 1 else 1.0
        for t in range(sz.tiles):
            at = slice(sz.stack * f + t, sz.stack * f + t + 1)
            near, far = near_ref[at], far_ref[at] * flip
            lanes = slice(LANES * t, LANES * (t + 1))
            ext[f, sz.rows : sz.rows + 1, lanes] = jnp.where(even, near, far)
            ext[f, EXT_ROWS - 1 : EXT_ROWS, lanes] = jnp.where(even, far, near)


class Tiles:
    def __init__(self, sz):
        self.sz = sz
        self.lane = lax.broadcasted_iota(jnp.int32, (EXT_ROWS, LANES), 1)
        self.turned = {}

    def turn(self, name, t, value, step):
        key = (name, t % self.sz.tiles, step)
        if key not in self.turned:
            self.turned[key] = pltpu.roll(value(t % self.sz.tiles), step % LANES, 1)
        return self.turned[key]

    def east(self, name, t, value):
        here = self.turn(name, t, value, -LEVELS)
        return jnp.where(self.lane < LANES - LEVELS, here, self.turn(name, t + 1, value, -LEVELS))

    def west(self, name, t, value):
        here = self.turn(name, t, value, LEVELS)
        return jnp.where(self.lane >= LEVELS, here, self.turn(name, t - 1, value, LEVELS))


def north(value):
    return pltpu.roll(value, EXT_ROWS - 1, 0)


def south(value):
    return pltpu.roll(value, 1, 0)


def polar_kernel(sz, h_ref, w_ref, near_ref, far_ref, geo_ref, *refs):
    tend_ref, ext = refs[0], refs[-1]
    band = lax.axis_index("lat")
    ring = Tiles(sz)
    lane = ring.lane
    tiles, stack, rows = sz.tiles, sz.stack, sz.rows
    for f, value in enumerate((h_ref[...], w_ref[1], w_ref[0])):
        ext[f, :rows, sz.end :] = jnp.zeros((rows, LANES), jnp.float32)
        ext[f, :rows, : sz.merged] = value
    add_rows(sz, ext, 2, near_ref, far_ref)
    inv_cos, sin_centre, cos_face = geo_ref[band, 0], geo_ref[band, 1], geo_ref[band, 2]
    ratio = sz.ratio

    def tile(f, t):
        return ext[f, :, LANES * t : LANES * (t + 1)]

    kept = {}

    def zonal(t):
        if t not in kept:
            thick_e = ring.east("h", t, functools.partial(tile, 0))
            wind_e = ring.east("u", t, functools.partial(tile, 2))
            flux = 0.25 * (tile(2, t) + wind_e) * (tile(0, t) + thick_e) * inv_cos
            if t == tiles - 1:
                flux = jnp.where(lane < sz.tail - LEVELS, flux, 0.0)
            kept[t] = (flux, thick_e)
        return kept[t]

    for t in range(tiles):
        flux, thick_e = zonal(t)
        thick, wind_v, wind_u = tile(0, t), tile(1, t), tile(2, t)
        flux_w = ring.west("f", t, lambda s: zonal(s)[0])
        thick_w = ring.west("hw", t, functools.partial(tile, 0))
        thick_n = north(thick)
        flux_n = (0.25 * ratio) * (wind_v + north(wind_v)) * (thick + thick_n) * cos_face
        thick_tend = -((flux - flux_w) + (flux_n - south(flux_n)) * inv_cos)
        wind_u_tend = sin_centre * wind_v - (thick_e - thick_w) * (0.5 * inv_cos)
        wind_v_tend = -sin_centre * wind_u - (0.5 * ratio) * (thick_n - south(thick))
        for f, tend in enumerate((thick_tend, wind_u_tend, wind_v_tend)):
            if t == tiles - 1:
                spare = 0.0
                if f == 0:
                    last = sz.tail - LEVELS
                    columns = [(tile(0, 0), 0), (thick, last), (tile(2, 0), 0), (wind_u, last)]
                    for k, (source, at) in reversed(list(enumerate(columns))):
                        to = sz.tail + LEVELS * k
                        spare = jnp.where(lane < to + LEVELS, pltpu.roll(source, (to - at) % LANES, 1), spare)
                tend = jnp.where(lane < sz.tail, tend, spare)
            tend_ref[pl.ds(stack * rows * f + t, rows, stride=stack), :] = tend[:rows]
    for f in range(3):
        for t in range(tiles, stack):
            tend_ref[pl.ds(stack * rows * f + t, rows, stride=stack), :] = jnp.zeros((rows, LANES), jnp.float32)
    if sz.part:
        size = sz.part * stack
        first = sz.part_first(band)
        for f in range(3):
            start = pl.multiple_of((rows * f + first) * stack, 8)
            refs[1][size * f : size * (f + 1)] = tend_ref[pl.ds(start, size), :]


def rest_kernel(
    sz, h_ref, w_ref, q_ref, from_w, from_e, near_ref, far_ref, geo_ref, new_w_ref, new_h_ref, mass_ref, ext
):
    band = lax.axis_index("lat")
    ring = Tiles(sz)
    lane = ring.lane
    tiles, rows = sz.tiles, sz.rows
    for f in range(6):
        if f < 2 or f == 5:
            value = (h_ref[...], w_ref[1], w_ref[0])[min(f, 2)]
        else:
            value = q_ref[f - 2].astype(jnp.float32)
        ext[f, :rows, : sz.merged] = value
    add_rows(sz, ext, 5, near_ref, far_ref)
    lane9 = lane[:rows]
    for place, f in enumerate((0, 5, 2, 3, 4)):
        after = pltpu.roll(from_e[...], (sz.tail - LEVELS * place) % LANES, 1)
        before = pltpu.roll(from_w[...], (LANES - LEVELS - LEVELS * place) % LANES, 1)
        own = ext[f, :rows, sz.end :]
        edge = jnp.where(lane9 < LANES - LEVELS, after, before)
        ext[f, :rows, sz.end :] = jnp.where(lane9 < sz.tail, own, edge)
    inv_cos, sin_centre, cos_face = geo_ref[band, 0], geo_ref[band, 1], geo_ref[band, 2]
    ratio = sz.ratio

    def tile(f, t):
        return ext[f, :, LANES * t : LANES * (t + 1)]

    kept = {}

    def zonal(t):
        if t not in kept:
            thick_e = ring.east("h", t, functools.partial(tile, 0))
            wind_e = ring.east("u", t, functools.partial(tile, 5))
            flux = 0.25 * (tile(5, t) + wind_e) * (tile(0, t) + thick_e) * inv_cos
            parts = []
            for k in range(3):
                q = tile(2 + k, t)
                q_e = ring.east(k, t, functools.partial(tile, 2 + k))
                parts.append(DIFFUSION * (q_e - q) - flux * (0.5 * (q + q_e)))
            kept[t] = (flux, thick_e, parts)
        return kept[t]

    for t in range(tiles):
        span = sz.span(t)
        lanes = slice(LANES * t, LANES * t + span)
        flux, thick_e, parts = zonal(t)
        thick, wind_u, wind_v = tile(0, t), tile(5, t), tile(1, t)
        flux_w = ring.west("f", t, lambda s: zonal(s)[0])
        thick_w = ring.west("hw", t, functools.partial(tile, 0))
        thick_n = north(thick)
        flux_n = (0.25 * ratio) * (wind_v + north(wind_v)) * (thick + thick_n) * cos_face
        thick_tend = -((flux - flux_w) + (flux_n - south(flux_n)) * inv_cos)
        wind_u_tend = sin_centre * wind_v - (thick_e - thick_w) * (0.5 * inv_cos)
        wind_v_tend = -sin_centre * wind_u - (0.5 * ratio) * (thick_n - south(thick))
        new_h_ref[:, lanes] = (thick + TIME_STEP * thick_tend)[:rows, :span]
        new_w_ref[0, :, lanes] = (wind_u + TIME_STEP * wind_u_tend)[:rows, :span]
        new_w_ref[1, :, lanes] = (wind_v + TIME_STEP * wind_v_tend)[:rows, :span]
        for k in range(3):
            q = tile(2 + k, t)
            q_n = north(q)
            zonal_part = parts[k] - ring.west(("p", k), t, lambda s: zonal(s)[2][k])
            lap = q_n + south(q) - 2.0 * q
            over = flux_n * (0.5 * (q + q_n))
            merid_part = DIFFUSION * lap - (over - south(over)) * inv_cos
            mass = thick * q + TIME_STEP * (zonal_part + merid_part)
            mass_ref[k, :, lanes] = mass[:rows, :span].astype(jnp.bfloat16)


def sin_pi(y):
    y = jnp.where(y > 0.5, 1.0 - y, jnp.where(y < -0.5, -1.0 - y, y))
    s = y * y
    series = [(-1) ** i * math.pi ** (2 * i + 1) / math.factorial(2 * i + 1) for i in range(7)]
    total = series[-1]
    for factor in reversed(series[:-1]):
        total = total * s + factor
    return total * y


def weights_kernel(sz, cut_ref, n_ref, inverse_ref, after_ref, weights_ref):
    band = lax.axis_index("lat")
    size = PER_TILE * sz.stack
    for row in range(sz.rows):
        width = (2 * cut_ref[band * sz.rows + row] + 1).astype(jnp.float32)
        n = n_ref[...]
        turns = n * width
        turns = turns - jnp.round(turns * (0.5 / sz.nlon)) * (2.0 * sz.nlon)
        weights = sin_pi(turns * (1.0 / sz.nlon)) * inverse_ref[...]
        weights = jnp.where(n == 0.0, width * (1.0 / sz.nlon), weights)
        weights_ref[size * row : size * (row + 1)] = weights.astype(jnp.bfloat16)


def filter_rows(sz, pieces, gathered, inv_cos, count, first, weights_ref, results):
    here = lax.axis_index("lon")
    stack, n_lon = sz.stack, sz.n_lon
    lane = lax.broadcasted_iota(jnp.int32, (count, LANES), 1)
    for turn, ref in enumerate(pieces):
        eastward = lax.rem(jnp.bitwise_xor(here, turn) - here + n_lon, n_lon)
        gathered[eastward, : 3 * count * stack] = ref[...]
    sides = [gathered[s, pl.ds(sz.tiles - 1, count, stride=stack), :] for s in range(n_lon)]

    def column(s, k):
        return pltpu.roll(sides[s % n_lon], (-sz.tail - LEVELS * k) % LANES, 1)

    for s in range(n_lon):
        thick_w, thick_e = column(s, 1), column(s + 1, 0)
        flux = 0.25 * (column(s, 3) + column(s + 1, 2)) * (thick_w + thick_e) * inv_cos
        slope = 0.5 * inv_cos
        for f, (west_of, east_of) in enumerate(((flux, flux), (slope * thick_e, slope * thick_w))):
            at = pl.ds(stack * count * f + sz.tiles - 1, count, stride=stack)
            own = gathered[s, at, :]
            own = own - jnp.where(lane >= sz.tail - LEVELS, pltpu.roll(west_of, sz.tail - LEVELS, 1), 0.0)
            gathered[s, at, :] = jnp.where(lane < sz.tail, own, 0.0)
            at = pl.ds(stack * count * f, count, stride=stack)
            after = (s + 1) % n_lon
            gathered[after, at, :] = gathered[after, at, :] + jnp.where(lane < LEVELS, east_of, 0.0)

    wide = lax.broadcasted_iota(jnp.int32, (stack, LANES), 1)
    size = PER_TILE * stack
    for row in range(count):
        starts = [stack * (count * f + row) for f in range(3)]
        circle = jnp.concatenate(
            [jnp.concatenate([gathered[s, at : at + stack] for s in range(n_lon)], axis=0) for at in starts], axis=1
        ).astype(jnp.bfloat16)
        weights = weights_ref[pl.ds(pl.multiple_of(size * (first + row), 16), size), :]
        spread = jnp.dot(weights, circle, preferred_element_type=jnp.float32)
        for f in range(3):
            same = spread[:stack, LANES * f : LANES * (f + 1)]
            carried = None
            for e in range(1, PER_TILE):
                part = spread[stack * e : stack * (e + 1), LANES * f : LANES * (f + 1)]
                part = pltpu.roll(part, LEVELS * e, 1)
                inside = wide >= LEVELS * e
                same = same + jnp.where(inside, part, 0.0)
                over = jnp.where(inside, 0.0, part)
                carried = over if carried is None else carried + over
            start = pl.multiple_of(stack * (sz.rows * f + first + row), 8)
            results[pl.ds(start, stack), :] = pltpu.roll(same, stack - 1, 0) + carried


def filter_kernel(sz, cut_ref, geo_ref, weights_ref, h_ref, w_ref, plain_w_ref, plain_h_ref, *refs):
    n_lon, rows = sz.n_lon, sz.rows
    full_refs, part_refs = refs[:n_lon], refs[n_lon : 2 * n_lon]
    new_w_ref, new_h_ref, gathered, results = refs[-4:]
    band = lax.axis_index("lat")
    from_pole = jnp.minimum(band, sz.n_lat - 1 - band)

    @pl.when(from_pole < sz.full)
    def _():
        filter_rows(sz, full_refs, gathered, geo_ref[band, 0][:rows], rows, 0, weights_ref, results)

    if sz.part:

        @pl.when(from_pole == sz.full)
        def _():
            inv_cos = geo_ref[band, 0]
            low = band < sz.n_lat // 2
            inv_cos = jnp.where(low, inv_cos[: sz.part], inv_cos[rows - sz.part : rows])
            filter_rows(sz, part_refs, gathered, inv_cos, sz.part, sz.part_first(band), weights_ref, results)

    row = lax.broadcasted_iota(jnp.int32, (rows, LANES), 0)
    cuts = jnp.zeros((rows, LANES), jnp.int32)
    for j in range(rows):
        cuts = jnp.where(row == j, cut_ref[band * rows + j], cuts)
    active = cuts < sz.nlon // 2
    for f in range(3):
        for t in range(sz.tiles):
            span = sz.span(t)
            lanes = slice(LANES * t, LANES * t + span)
            tend = results[pl.ds(sz.stack * rows * f + t, rows, stride=sz.stack), :][:, :span]
            if f == 0:
                new = h_ref[:, lanes] + TIME_STEP * tend
                new_h_ref[:, lanes] = jnp.where(active[:, :span], new, plain_h_ref[:, lanes])
            else:
                new = w_ref[f - 1, :, lanes] + TIME_STEP * tend
                new_w_ref[f - 1, :, lanes] = jnp.where(active[:, :span], new, plain_w_ref[f - 1, :, lanes])


def local(winds, thickness, tracers, cutoff):
    n_lat = lax.axis_size("lat")
    n_lon = lax.axis_size("lon")
    rows, merged = thickness.shape
    sz = Sizes(rows, merged, n_lat, n_lon)
    f32 = jnp.float32
    vmem = pl.BlockSpec(memory_space=pltpu.VMEM)
    smem = pl.BlockSpec(memory_space=pltpu.SMEM)
    hbm = pl.BlockSpec(memory_space=pltpu.HBM)
    anywhere = pl.BlockSpec(memory_space=pl.ANY)

    def shaped(*shape):
        return jax.ShapeDtypeStruct(shape, f32)

    def call(kernel, name, in_specs, out_shape, scratch=(), limit=LIMIT):
        return pl.pallas_call(
            functools.partial(kernel, sz),
            out_shape=out_shape,
            in_specs=in_specs,
            out_specs=jax.tree.map(lambda _: vmem, out_shape),
            scratch_shapes=list(scratch),
            compiler_params=pltpu.CompilerParams(vmem_limit_bytes=limit),
            name=name,
        )

    def swapped(value, bands, turn):
        sectors = [(b, i, i ^ turn if b in bands else i) for b in range(n_lat) for i in range(n_lon)]
        return lax.ppermute(value, ("lat", "lon"), [(b * n_lon + i, b * n_lon + k) for b, i, k in sectors])

    geo = jnp.asarray(geometry(sz))
    n, inverse = (jnp.asarray(table) for table in offsets(sz))

    row_pair = shaped(5 * sz.stack, LANES)
    to_near, to_far = call(
        rows_kernel,
        "rows",
        [hbm] * 3,
        (row_pair, row_pair),
        [
            pltpu.VMEM((2, 1, merged), f32),
            pltpu.VMEM((2, 2, merged), f32),
            pltpu.VMEM((2, 3, merged), jnp.bfloat16),
            pltpu.SemaphoreType.DMA((2, 3)),
        ],
        limit=ALL_VMEM,
    )(thickness, jnp.swapaxes(winds, 0, 1), jnp.swapaxes(tracers, 0, 1))

    near = [(band * n_lon + i, (band ^ 1) * n_lon + i) for band in range(n_lat) for i in range(n_lon)]
    far = []
    for band in range(n_lat):
        other = band - 1 if band % 2 == 0 else band + 1
        for i in range(n_lon):
            if 0 <= other < n_lat:
                far.append((band * n_lon + i, other * n_lon + i))
            else:
                far.append((band * n_lon + i, band * n_lon + (i + n_lon // 2) % n_lon))
    from_near = lax.ppermute(to_near, ("lat", "lon"), near)
    from_far = lax.ppermute(to_far, ("lat", "lon"), far)

    tend_shapes = [shaped(3 * rows * sz.stack, LANES)]
    if sz.part:
        tend_shapes.append(shaped(3 * sz.part * sz.stack, LANES))
    tends = call(
        polar_kernel, "polar", [vmem] * 5, tend_shapes, [pltpu.VMEM((3, EXT_ROWS, sz.tiles * LANES), f32)]
    )(thickness, winds, from_near, from_far, geo)
    circles = []
    for tend, bands in zip(tends, (sz.full_bands(), sz.part_bands())):
        circles += [tend] + [swapped(tend, bands, turn) for turn in range(1, n_lon)]

    weights = call(
        weights_kernel,
        "weights",
        [smem, vmem, vmem, anywhere],
        jax.ShapeDtypeStruct((rows * PER_TILE * sz.stack, n_lon * sz.stack), jnp.bfloat16),
    )(cutoff, n, inverse, tends[0])

    edge = shaped(rows, LANES)
    to_e, to_w = call(columns_kernel, "columns", [vmem] * 3 + [anywhere], (edge, edge))(
        thickness, winds, tracers, tends[0]
    )
    from_w = lax.ppermute(to_e, "lon", [(i, (i + 1) % n_lon) for i in range(n_lon)])
    from_e = lax.ppermute(to_w, "lon", [((i + 1) % n_lon, i) for i in range(n_lon)])

    plain_w, plain_h, mass = call(
        rest_kernel,
        "rest",
        [vmem] * 8,
        (shaped(*winds.shape), shaped(rows, merged), jax.ShapeDtypeStruct(tracers.shape, jnp.bfloat16)),
        [pltpu.VMEM((6, EXT_ROWS, sz.tiles * LANES), f32)],
    )(thickness, winds, tracers, from_w, from_e, from_near, from_far, geo)

    new_w, new_h = call(
        filter_kernel,
        "filter",
        [smem] + [vmem] * (6 + len(circles)),
        (shaped(*winds.shape), shaped(rows, merged)),
        [
            pltpu.VMEM((n_lon, 3 * rows * sz.stack, LANES), f32),
            pltpu.VMEM((3 * rows * sz.stack, LANES), f32),
        ],
    )(cutoff, geo, weights, thickness, winds, plain_w, plain_h, *circles)
    return new_w, new_h, mass


def solution(mesh):
    in_specs = (P(None, "lat", "lon"), P("lat", "lon"), P(None, "lat", "lon"), P())
    out_specs = (P(None, "lat", "lon"), P("lat", "lon"), P(None, "lat", "lon"))
    return jax.shard_map(local, mesh=mesh, in_specs=in_specs, out_specs=out_specs, check_vma=False)
```

```python
import functools
import math

import jax
import jax.numpy as jnp
import numpy as np
from jax import lax
from jax.experimental import pallas as pl
from jax.experimental.pallas import tpu as pltpu
from jax.sharding import PartitionSpec as P

LEVELS = 16
TIME_STEP = 0.05
DIFFUSION = 0.5
LANES = 128
PER_TILE = LANES // LEVELS
EXT_ROWS = 16
LIMIT = 48 * 1024 * 1024
ALL_VMEM = 64 * 1024 * 1024 - 256 * 1024


class Sizes:
    def __init__(self, rows, merged, n_lat, n_lon):
        self.rows = rows
        self.merged = merged
        self.columns = merged // LEVELS
        self.n_lat = n_lat
        self.n_lon = n_lon
        self.nlat = rows * n_lat
        self.nlon = self.columns * n_lon
        self.ratio = 2.0 * self.nlat / self.nlon
        self.tiles = -(-merged // LANES)
        self.end = (self.tiles - 1) * LANES
        self.tail = merged - self.end
        self.stack = -(-(self.tiles + 1) // 8) * 8
        polar = self.nlat // 6
        self.full = polar // rows
        self.part = polar % rows
        assert self.tail <= LANES - 4 * LEVELS and rows + 2 <= EXT_ROWS and n_lat % 2 == 0
        assert n_lon & (n_lon - 1) == 0

    def span(self, tile):
        return self.tail if tile == self.tiles - 1 else LANES

    def part_first(self, band):
        return jnp.where(band < self.n_lat // 2, 0, self.rows - self.part)


def geometry(sz):
    table = np.zeros((sz.n_lat, 3, EXT_ROWS, LANES), np.float64)

    def face(j):
        return math.sin((j + 1) * math.pi / sz.nlat) if 0 <= j < sz.nlat - 1 else 0.0

    for band in range(sz.n_lat):
        for row in range(sz.rows):
            j = band * sz.rows + row
            centre = (j + 0.5) * math.pi / sz.nlat - math.pi / 2
            table[band, 0, row] = 1.0 / math.cos(centre)
            table[band, 1, row] = math.sin(centre)
            table[band, 2, row] = face(j)
        table[band, 2, EXT_ROWS - 1] = face(band * sz.rows - 1)
    return table.astype(np.float32)


def offsets(sz):
    shift, out_tile = np.divmod(np.arange(PER_TILE * sz.stack), sz.stack)
    sector, in_tile = np.divmod(np.arange(sz.n_lon * sz.stack), sz.stack)
    n = (PER_TILE * (out_tile - 1) + shift)[:, None] - (PER_TILE * in_tile + sz.columns * sector)[None, :]
    n = (n + sz.nlon // 2) % sz.nlon - sz.nlon // 2
    with np.errstate(divide="ignore"):
        inverse = np.where(n == 0, 0.0, 1.0 / (sz.nlon * np.sin(np.pi * n / sz.nlon)))
    return n.astype(np.float32), inverse.astype(np.float32)


def rows_kernel(sz, h_hbm, w_hbm, q_hbm, near_ref, far_ref, h_rows, w_rows, q_rows, sems):
    last = sz.rows - 1
    copies = []
    for k, row in enumerate((0, last)):
        copies.append(pltpu.make_async_copy(h_hbm.at[pl.ds(row, 1)], h_rows.at[k], sems.at[k, 0]))
        copies.append(pltpu.make_async_copy(w_hbm.at[row], w_rows.at[k], sems.at[k, 1]))
        copies.append(pltpu.make_async_copy(q_hbm.at[row], q_rows.at[k], sems.at[k, 2]))
    for copy in copies:
        copy.start()
    for copy in copies:
        copy.wait()
    even = lax.rem(lax.axis_index("lat"), 2) == 0
    for t in range(sz.tiles):
        wide = sz.span(t)
        lanes = slice(LANES * t, LANES * t + wide)
        q = [q_rows[k, :, lanes].astype(jnp.float32) for k in range(2)]
        for f in range(5):
            if f == 0:
                first, final = h_rows[0, :, lanes], h_rows[1, :, lanes]
            elif f == 1:
                first, final = w_rows[0, 1:2, lanes], w_rows[1, 1:2, lanes]
            else:
                first, final = q[0][f - 2 : f - 1], q[1][f - 2 : f - 1]
            at = sz.stack * f + t
            near_ref[at : at + 1, :wide] = jnp.where(even, final, first)
            far_ref[at : at + 1, :wide] = jnp.where(even, first, final)


def columns_kernel(sz, h_ref, w_ref, q_ref, after_ref, east_ref, west_ref):
    for f in range(5):
        to = slice(LEVELS * f, LEVELS * (f + 1))

        def load(lanes):
            if f < 2:
                return (h_ref[:, lanes], w_ref[0, :, lanes])[f]
            return q_ref[f - 2, :, lanes].astype(jnp.float32)

        east_ref[:, to] = load(slice(sz.merged - LEVELS, sz.merged))
        west_ref[:, to] = load(slice(0, LEVELS))


def add_rows(sz, ext, fields, near_ref, far_ref):
    band = lax.axis_index("lat")
    even = lax.rem(band, 2) == 0
    over_pole = (band == 0) | (band == sz.n_lat - 1)
    for f in range(fields):
        flip = jnp.where(over_pole, -1.0, 1.0) if f == 1 else 1.0
        for t in range(sz.tiles):
            at = slice(sz.stack * f + t, sz.stack * f + t + 1)
            near, far = near_ref[at], far_ref[at] * flip
            lanes = slice(LANES * t, LANES * (t + 1))
            ext[f, sz.rows : sz.rows + 1, lanes] = jnp.where(even, near, far)
            ext[f, EXT_ROWS - 1 : EXT_ROWS, lanes] = jnp.where(even, far, near)


class Tiles:
    def __init__(self, sz):
        self.sz = sz
        self.lane = lax.broadcasted_iota(jnp.int32, (EXT_ROWS, LANES), 1)
        self.turned = {}

    def turn(self, name, t, value, step):
        key = (name, t % self.sz.tiles, step)
        if key not in self.turned:
            self.turned[key] = pltpu.roll(value(t % self.sz.tiles), step % LANES, 1)
        return self.turned[key]

    def east(self, name, t, value):
        here = self.turn(name, t, value, -LEVELS)
        return jnp.where(self.lane < LANES - LEVELS, here, self.turn(name, t + 1, value, -LEVELS))

    def west(self, name, t, value):
        here = self.turn(name, t, value, LEVELS)
        return jnp.where(self.lane >= LEVELS, here, self.turn(name, t - 1, value, LEVELS))


def north(value):
    return pltpu.roll(value, EXT_ROWS - 1, 0)


def south(value):
    return pltpu.roll(value, 1, 0)


def polar_kernel(sz, h_ref, w_ref, near_ref, far_ref, geo_ref, tend_ref, ext):
    band = lax.axis_index("lat")
    ring = Tiles(sz)
    lane = ring.lane
    tiles, stack, rows = sz.tiles, sz.stack, sz.rows
    for f, value in enumerate((h_ref[...], w_ref[1], w_ref[0])):
        ext[f, :rows, sz.end :] = jnp.zeros((rows, LANES), jnp.float32)
        ext[f, :rows, : sz.merged] = value
    add_rows(sz, ext, 2, near_ref, far_ref)
    inv_cos, sin_centre, cos_face = geo_ref[band, 0], geo_ref[band, 1], geo_ref[band, 2]
    ratio = sz.ratio

    def tile(f, t):
        return ext[f, :, LANES * t : LANES * (t + 1)]

    kept = {}

    def zonal(t):
        if t not in kept:
            thick_e = ring.east("h", t, functools.partial(tile, 0))
            wind_e = ring.east("u", t, functools.partial(tile, 2))
            flux = 0.25 * (tile(2, t) + wind_e) * (tile(0, t) + thick_e) * inv_cos
            if t == tiles - 1:
                flux = jnp.where(lane < sz.tail - LEVELS, flux, 0.0)
            kept[t] = (flux, thick_e)
        return kept[t]

    for t in range(tiles):
        flux, thick_e = zonal(t)
        thick, wind_v, wind_u = tile(0, t), tile(1, t), tile(2, t)
        flux_w = ring.west("f", t, lambda s: zonal(s)[0])
        thick_w = ring.west("hw", t, functools.partial(tile, 0))
        thick_n = north(thick)
        flux_n = (0.25 * ratio) * (wind_v + north(wind_v)) * (thick + thick_n) * cos_face
        thick_tend = -((flux - flux_w) + (flux_n - south(flux_n)) * inv_cos)
        wind_u_tend = sin_centre * wind_v - (thick_e - thick_w) * (0.5 * inv_cos)
        wind_v_tend = -sin_centre * wind_u - (0.5 * ratio) * (thick_n - south(thick))
        for f, tend in enumerate((thick_tend, wind_u_tend, wind_v_tend)):
            if t == tiles - 1:
                spare = 0.0
                if f == 0:
                    last = sz.tail - LEVELS
                    columns = [(tile(0, 0), 0), (thick, last), (tile(2, 0), 0), (wind_u, last)]
                    for k, (source, at) in reversed(list(enumerate(columns))):
                        to = sz.tail + LEVELS * k
                        spare = jnp.where(lane < to + LEVELS, pltpu.roll(source, (to - at) % LANES, 1), spare)
                tend = jnp.where(lane < sz.tail, tend, spare)
            tend_ref[pl.ds(stack * rows * f + t, rows, stride=stack), :] = tend[:rows]
    for f in range(3):
        for t in range(tiles, stack):
            tend_ref[pl.ds(stack * rows * f + t, rows, stride=stack), :] = jnp.zeros((rows, LANES), jnp.float32)


def rest_kernel(
    sz, h_ref, w_ref, q_ref, from_w, from_e, near_ref, far_ref, geo_ref, new_w_ref, new_h_ref, mass_ref, ext
):
    band = lax.axis_index("lat")
    ring = Tiles(sz)
    lane = ring.lane
    tiles, rows = sz.tiles, sz.rows
    for f in range(6):
        if f < 2 or f == 5:
            value = (h_ref[...], w_ref[1], w_ref[0])[min(f, 2)]
        else:
            value = q_ref[f - 2].astype(jnp.float32)
        ext[f, :rows, : sz.merged] = value
    add_rows(sz, ext, 5, near_ref, far_ref)
    lane9 = lane[:rows]
    for place, f in enumerate((0, 5, 2, 3, 4)):
        after = pltpu.roll(from_e[...], (sz.tail - LEVELS * place) % LANES, 1)
        before = pltpu.roll(from_w[...], (LANES - LEVELS - LEVELS * place) % LANES, 1)
        own = ext[f, :rows, sz.end :]
        edge = jnp.where(lane9 < LANES - LEVELS, after, before)
        ext[f, :rows, sz.end :] = jnp.where(lane9 < sz.tail, own, edge)
    inv_cos, sin_centre, cos_face = geo_ref[band, 0], geo_ref[band, 1], geo_ref[band, 2]
    ratio = sz.ratio

    def tile(f, t):
        return ext[f, :, LANES * t : LANES * (t + 1)]

    kept = {}

    def zonal(t):
        if t not in kept:
            thick_e = ring.east("h", t, functools.partial(tile, 0))
            wind_e = ring.east("u", t, functools.partial(tile, 5))
            flux = 0.25 * (tile(5, t) + wind_e) * (tile(0, t) + thick_e) * inv_cos
            parts = []
            for k in range(3):
                q = tile(2 + k, t)
                q_e = ring.east(k, t, functools.partial(tile, 2 + k))
                parts.append(DIFFUSION * (q_e - q) - flux * (0.5 * (q + q_e)))
            kept[t] = (flux, thick_e, parts)
        return kept[t]

    for t in range(tiles):
        span = sz.span(t)
        lanes = slice(LANES * t, LANES * t + span)
        flux, thick_e, parts = zonal(t)
        thick, wind_u, wind_v = tile(0, t), tile(5, t), tile(1, t)
        flux_w = ring.west("f", t, lambda s: zonal(s)[0])
        thick_w = ring.west("hw", t, functools.partial(tile, 0))
        thick_n = north(thick)
        flux_n = (0.25 * ratio) * (wind_v + north(wind_v)) * (thick + thick_n) * cos_face
        thick_tend = -((flux - flux_w) + (flux_n - south(flux_n)) * inv_cos)
        wind_u_tend = sin_centre * wind_v - (thick_e - thick_w) * (0.5 * inv_cos)
        wind_v_tend = -sin_centre * wind_u - (0.5 * ratio) * (thick_n - south(thick))
        new_h_ref[:, lanes] = (thick + TIME_STEP * thick_tend)[:rows, :span]
        new_w_ref[0, :, lanes] = (wind_u + TIME_STEP * wind_u_tend)[:rows, :span]
        new_w_ref[1, :, lanes] = (wind_v + TIME_STEP * wind_v_tend)[:rows, :span]
        for k in range(3):
            q = tile(2 + k, t)
            q_n = north(q)
            zonal_part = parts[k] - ring.west(("p", k), t, lambda s: zonal(s)[2][k])
            lap = q_n + south(q) - 2.0 * q
            over = flux_n * (0.5 * (q + q_n))
            merid_part = DIFFUSION * lap - (over - south(over)) * inv_cos
            mass = thick * q + TIME_STEP * (zonal_part + merid_part)
            mass_ref[k, :, lanes] = mass[:rows, :span].astype(jnp.bfloat16)


def sin_pi(y):
    y = jnp.where(y > 0.5, 1.0 - y, jnp.where(y < -0.5, -1.0 - y, y))
    s = y * y
    series = [(-1) ** i * math.pi ** (2 * i + 1) / math.factorial(2 * i + 1) for i in range(7)]
    total = series[-1]
    for factor in reversed(series[:-1]):
        total = total * s + factor
    return total * y


def weights_kernel(sz, cut_ref, n_ref, inverse_ref, after_ref, weights_ref):
    band = lax.axis_index("lat")
    size = PER_TILE * sz.stack
    for row in range(sz.rows):
        width = (2 * cut_ref[band * sz.rows + row] + 1).astype(jnp.float32)
        n = n_ref[...]
        turns = n * width
        turns = turns - jnp.round(turns * (0.5 / sz.nlon)) * (2.0 * sz.nlon)
        weights = sin_pi(turns * (1.0 / sz.nlon)) * inverse_ref[...]
        weights = jnp.where(n == 0.0, width * (1.0 / sz.nlon), weights)
        weights_ref[size * row : size * (row + 1)] = weights.astype(jnp.bfloat16)


def filter_rows(sz, circle_ref, gathered, inv_cos, count, first, weights_ref, results):
    here = lax.axis_index("lon")
    stack, n_lon = sz.stack, sz.n_lon
    lane = lax.broadcasted_iota(jnp.int32, (count, LANES), 1)
    for s in range(n_lon):
        sector = lax.rem(here + s, n_lon)
        for f in range(3):
            start = pl.multiple_of(stack * (sz.rows * f + first), 8)
            piece = circle_ref[sector, pl.ds(start, count * stack), :]
            gathered[s, stack * count * f : stack * count * (f + 1)] = piece
    sides = [gathered[s, pl.ds(sz.tiles - 1, count, stride=stack), :] for s in range(n_lon)]

    def column(s, k):
        return pltpu.roll(sides[s % n_lon], (-sz.tail - LEVELS * k) % LANES, 1)

    for s in range(n_lon):
        thick_w, thick_e = column(s, 1), column(s + 1, 0)
        flux = 0.25 * (column(s, 3) + column(s + 1, 2)) * (thick_w + thick_e) * inv_cos
        slope = 0.5 * inv_cos
        for f, (west_of, east_of) in enumerate(((flux, flux), (slope * thick_e, slope * thick_w))):
            at = pl.ds(stack * count * f + sz.tiles - 1, count, stride=stack)
            own = gathered[s, at, :]
            own = own - jnp.where(lane >= sz.tail - LEVELS, pltpu.roll(west_of, sz.tail - LEVELS, 1), 0.0)
            gathered[s, at, :] = jnp.where(lane < sz.tail, own, 0.0)
            at = pl.ds(stack * count * f, count, stride=stack)
            after = (s + 1) % n_lon
            gathered[after, at, :] = gathered[after, at, :] + jnp.where(lane < LEVELS, east_of, 0.0)

    wide = lax.broadcasted_iota(jnp.int32, (stack, LANES), 1)
    size = PER_TILE * stack
    for row in range(count):
        starts = [stack * (count * f + row) for f in range(3)]
        circle = jnp.concatenate(
            [jnp.concatenate([gathered[s, at : at + stack] for s in range(n_lon)], axis=0) for at in starts], axis=1
        ).astype(jnp.bfloat16)
        weights = weights_ref[pl.ds(pl.multiple_of(size * (first + row), 16), size), :]
        spread = jnp.dot(weights, circle, preferred_element_type=jnp.float32)
        for f in range(3):
            same = spread[:stack, LANES * f : LANES * (f + 1)]
            carried = None
            for e in range(1, PER_TILE):
                part = spread[stack * e : stack * (e + 1), LANES * f : LANES * (f + 1)]
                part = pltpu.roll(part, LEVELS * e, 1)
                inside = wide >= LEVELS * e
                same = same + jnp.where(inside, part, 0.0)
                over = jnp.where(inside, 0.0, part)
                carried = over if carried is None else carried + over
            start = pl.multiple_of(stack * (sz.rows * f + first + row), 8)
            results[pl.ds(start, stack), :] = pltpu.roll(same, stack - 1, 0) + carried


def filter_kernel(
    sz, cut_ref, geo_ref, weights_ref, h_ref, w_ref, plain_w_ref, plain_h_ref, circle_ref,
    new_w_ref, new_h_ref, gathered, results,
):
    rows = sz.rows
    band = lax.axis_index("lat")
    from_pole = jnp.minimum(band, sz.n_lat - 1 - band)

    @pl.when(from_pole < sz.full)
    def _():
        filter_rows(sz, circle_ref, gathered, geo_ref[band, 0][:rows], rows, 0, weights_ref, results)

    if sz.part:

        @pl.when(from_pole == sz.full)
        def _():
            inv_cos = geo_ref[band, 0]
            low = band < sz.n_lat // 2
            inv_cos = jnp.where(low, inv_cos[: sz.part], inv_cos[rows - sz.part : rows])
            filter_rows(sz, circle_ref, gathered, inv_cos, sz.part, sz.part_first(band), weights_ref, results)

    row = lax.broadcasted_iota(jnp.int32, (rows, LANES), 0)
    cuts = jnp.zeros((rows, LANES), jnp.int32)
    for j in range(rows):
        cuts = jnp.where(row == j, cut_ref[band * rows + j], cuts)
    active = cuts < sz.nlon // 2
    for f in range(3):
        for t in range(sz.tiles):
            span = sz.span(t)
            lanes = slice(LANES * t, LANES * t + span)
            tend = results[pl.ds(sz.stack * rows * f + t, rows, stride=sz.stack), :][:, :span]
            if f == 0:
                new = h_ref[:, lanes] + TIME_STEP * tend
                new_h_ref[:, lanes] = jnp.where(active[:, :span], new, plain_h_ref[:, lanes])
            else:
                new = w_ref[f - 1, :, lanes] + TIME_STEP * tend
                new_w_ref[f - 1, :, lanes] = jnp.where(active[:, :span], new, plain_w_ref[f - 1, :, lanes])


def local(winds, thickness, tracers, cutoff):
    n_lat = lax.axis_size("lat")
    n_lon = lax.axis_size("lon")
    rows, merged = thickness.shape
    sz = Sizes(rows, merged, n_lat, n_lon)
    f32 = jnp.float32
    vmem = pl.BlockSpec(memory_space=pltpu.VMEM)
    smem = pl.BlockSpec(memory_space=pltpu.SMEM)
    hbm = pl.BlockSpec(memory_space=pltpu.HBM)
    anywhere = pl.BlockSpec(memory_space=pl.ANY)

    def shaped(*shape):
        return jax.ShapeDtypeStruct(shape, f32)

    def call(kernel, name, in_specs, out_shape, scratch=(), limit=LIMIT):
        return pl.pallas_call(
            functools.partial(kernel, sz),
            out_shape=out_shape,
            in_specs=in_specs,
            out_specs=jax.tree.map(lambda _: vmem, out_shape),
            scratch_shapes=list(scratch),
            compiler_params=pltpu.CompilerParams(vmem_limit_bytes=limit),
            name=name,
        )

    geo = jnp.asarray(geometry(sz))
    n, inverse = (jnp.asarray(table) for table in offsets(sz))

    row_pair = shaped(5 * sz.stack, LANES)
    to_near, to_far = call(
        rows_kernel,
        "rows",
        [hbm] * 3,
        (row_pair, row_pair),
        [
            pltpu.VMEM((2, 1, merged), f32),
            pltpu.VMEM((2, 2, merged), f32),
            pltpu.VMEM((2, 3, merged), jnp.bfloat16),
            pltpu.SemaphoreType.DMA((2, 3)),
        ],
        limit=ALL_VMEM,
    )(thickness, jnp.swapaxes(winds, 0, 1), jnp.swapaxes(tracers, 0, 1))

    near = [(band * n_lon + i, (band ^ 1) * n_lon + i) for band in range(n_lat) for i in range(n_lon)]
    far = []
    for band in range(n_lat):
        other = band - 1 if band % 2 == 0 else band + 1
        for i in range(n_lon):
            if 0 <= other < n_lat:
                far.append((band * n_lon + i, other * n_lon + i))
            else:
                far.append((band * n_lon + i, band * n_lon + (i + n_lon // 2) % n_lon))
    from_near = lax.ppermute(to_near, ("lat", "lon"), near)
    from_far = lax.ppermute(to_far, ("lat", "lon"), far)

    tend = call(
        polar_kernel,
        "polar",
        [vmem] * 5,
        shaped(3 * rows * sz.stack, LANES),
        [pltpu.VMEM((3, EXT_ROWS, sz.tiles * LANES), f32)],
    )(thickness, winds, from_near, from_far, geo)
    circle = lax.all_gather(tend, "lon")

    weights = call(
        weights_kernel,
        "weights",
        [smem, vmem, vmem, anywhere],
        jax.ShapeDtypeStruct((rows * PER_TILE * sz.stack, n_lon * sz.stack), jnp.bfloat16),
    )(cutoff, n, inverse, tend)

    edge = shaped(rows, LANES)
    to_e, to_w = call(columns_kernel, "columns", [vmem] * 3 + [anywhere], (edge, edge))(
        thickness, winds, tracers, tend
    )
    from_w = lax.ppermute(to_e, "lon", [(i, (i + 1) % n_lon) for i in range(n_lon)])
    from_e = lax.ppermute(to_w, "lon", [((i + 1) % n_lon, i) for i in range(n_lon)])

    plain_w, plain_h, mass = call(
        rest_kernel,
        "rest",
        [vmem] * 8,
        (shaped(*winds.shape), shaped(rows, merged), jax.ShapeDtypeStruct(tracers.shape, jnp.bfloat16)),
        [pltpu.VMEM((6, EXT_ROWS, sz.tiles * LANES), f32)],
    )(thickness, winds, tracers, from_w, from_e, from_near, from_far, geo)

    new_w, new_h = call(
        filter_kernel,
        "filter",
        [smem] + [vmem] * 7,
        (shaped(*winds.shape), shaped(rows, merged)),
        [
            pltpu.VMEM((n_lon, 3 * rows * sz.stack, LANES), f32),
            pltpu.VMEM((3 * rows * sz.stack, LANES), f32),
        ],
    )(cutoff, geo, weights, thickness, winds, plain_w, plain_h, circle)
    return new_w, new_h, mass


def solution(mesh):
    in_specs = (P(None, "lat", "lon"), P("lat", "lon"), P(None, "lat", "lon"), P())
    out_specs = (P(None, "lat", "lon"), P("lat", "lon"), P(None, "lat", "lon"))
    return jax.shard_map(local, mesh=mesh, in_specs=in_specs, out_specs=out_specs, check_vma=False)
```

```python
import functools
import math

import jax
import jax.numpy as jnp
import numpy as np
from jax import lax
from jax.experimental import pallas as pl
from jax.experimental.pallas import tpu as pltpu
from jax.sharding import PartitionSpec as P

LEVELS = 16
TIME_STEP = 0.05
DIFFUSION = 0.5
LANES = 128
PER_TILE = LANES // LEVELS
EXT_ROWS = 16
LIMIT = 48 * 1024 * 1024
ALL_VMEM = 64 * 1024 * 1024 - 3600 * 1024


class Sizes:
    def __init__(self, rows, merged, n_lat, n_lon):
        self.rows = rows
        self.merged = merged
        self.columns = merged // LEVELS
        self.n_lat = n_lat
        self.n_lon = n_lon
        self.nlat = rows * n_lat
        self.nlon = self.columns * n_lon
        self.ratio = 2.0 * self.nlat / self.nlon
        self.tiles = -(-merged // LANES)
        self.end = (self.tiles - 1) * LANES
        self.tail = merged - self.end
        self.stack = -(-(self.tiles + 1) // 8) * 8
        self.units = 3 * rows
        self.share = -(-self.units // n_lon)
        self.size = self.share * self.stack
        assert self.tail <= LANES - 4 * LEVELS and rows + 2 <= EXT_ROWS and n_lat % 2 == 0
        assert n_lon >= 4 and n_lon & (n_lon - 1) == 0

    def span(self, tile):
        return self.tail if tile == self.tiles - 1 else LANES

    def turns(self, odd):
        middle = list(range(1, self.n_lon - 1))
        return [0, self.n_lon - 1] + (middle[::-1] if odd else middle)

    def partner(self, k):
        odd = lax.rem(lax.axis_index("lat"), 2) == 1
        turn = jnp.where(odd, self.turns(True)[k], self.turns(False)[k])
        return jnp.bitwise_xor(lax.axis_index("lon"), turn)

    def piece(self, k):
        return pl.ds(pl.multiple_of(self.partner(k) * self.size, 8), self.size)


def geometry(sz):
    table = np.zeros((sz.n_lat, 3, EXT_ROWS, LANES), np.float64)

    def face(j):
        return math.sin((j + 1) * math.pi / sz.nlat) if 0 <= j < sz.nlat - 1 else 0.0

    for band in range(sz.n_lat):
        for row in range(sz.rows):
            j = band * sz.rows + row
            centre = (j + 0.5) * math.pi / sz.nlat - math.pi / 2
            table[band, 0, row] = 1.0 / math.cos(centre)
            table[band, 1, row] = math.sin(centre)
            table[band, 2, row] = face(j)
        table[band, 2, EXT_ROWS - 1] = face(band * sz.rows - 1)
    return table.astype(np.float32)


def offsets(sz):
    shift, out_tile = np.divmod(np.arange(PER_TILE * sz.stack), sz.stack)
    sector, in_tile = np.divmod(np.arange(sz.n_lon * sz.stack), sz.stack)
    n = (PER_TILE * (out_tile - 1) + shift)[:, None] - (PER_TILE * in_tile + sz.columns * sector)[None, :]
    n = (n + sz.nlon // 2) % sz.nlon - sz.nlon // 2
    with np.errstate(divide="ignore"):
        inverse = np.where(n == 0, 0.0, 1.0 / (sz.nlon * np.sin(np.pi * n / sz.nlon)))
    return n.astype(np.float32), inverse.astype(np.float32)


def rows_kernel(sz, h_hbm, w_hbm, q_hbm, geo_hbm, near_ref, far_ref, sides_ref, block_ref, geo_ref, h_in, w_in, q_in, sems):
    band = lax.axis_index("lat")
    pairs = ((h_hbm, h_in), (w_hbm, w_in), (q_hbm, q_in), (geo_hbm.at[band], geo_ref))
    copies = [pltpu.make_async_copy(source, to, sems.at[i]) for i, (source, to) in enumerate(pairs)]
    for copy in copies:
        copy.start()
    for copy in copies:
        copy.wait()
    rows, last = sz.rows, sz.rows - 1
    fields = [h_in[...], w_in[:, 1, :]] + [q_in[:, k, :].astype(jnp.float32) for k in range(3)] + [w_in[:, 0, :]]
    for f, value in enumerate(fields):
        block_ref[f, :rows, : sz.merged] = value
    even = lax.rem(band, 2) == 0
    for t in range(sz.tiles):
        wide = sz.span(t)
        lanes = slice(LANES * t, LANES * t + wide)
        for f in range(5):
            first, final = block_ref[f, 0:1, lanes], block_ref[f, last:rows, lanes]
            at = sz.stack * f + t
            near_ref[at : at + 1, :wide] = jnp.where(even, final, first)
            far_ref[at : at + 1, :wide] = jnp.where(even, first, final)
    sides_ref[...] = jnp.zeros(sides_ref.shape, jnp.float32)
    for k, at in enumerate((0, sz.merged - LEVELS)):
        for place, f in enumerate((0, 5, 2, 3, 4)):
            to = slice(LEVELS * place, LEVELS * (place + 1))
            sides_ref[EXT_ROWS * k : EXT_ROWS * k + rows, to] = block_ref[f, :rows, at : at + LEVELS]


def add_rows(sz, ext, fields, near_ref, far_ref):
    band = lax.axis_index("lat")
    even = lax.rem(band, 2) == 0
    over_pole = (band == 0) | (band == sz.n_lat - 1)
    for f in range(fields):
        flip = jnp.where(over_pole, -1.0, 1.0) if f == 1 else 1.0
        for t in range(sz.tiles):
            at = slice(sz.stack * f + t, sz.stack * f + t + 1)
            near, far = near_ref[at], far_ref[at] * flip
            lanes = slice(LANES * t, LANES * (t + 1))
            ext[f, sz.rows : sz.rows + 1, lanes] = jnp.where(even, near, far)
            ext[f, EXT_ROWS - 1 : EXT_ROWS, lanes] = jnp.where(even, far, near)


class Tiles:
    def __init__(self, sz):
        self.sz = sz
        self.lane = lax.broadcasted_iota(jnp.int32, (EXT_ROWS, LANES), 1)
        self.turned = {}

    def turn(self, name, t, value, step):
        key = (name, t % self.sz.tiles, step)
        if key not in self.turned:
            self.turned[key] = pltpu.roll(value(t % self.sz.tiles), step % LANES, 1)
        return self.turned[key]

    def east(self, name, t, value):
        here = self.turn(name, t, value, -LEVELS)
        return jnp.where(self.lane < LANES - LEVELS, here, self.turn(name, t + 1, value, -LEVELS))

    def west(self, name, t, value):
        here = self.turn(name, t, value, LEVELS)
        return jnp.where(self.lane >= LEVELS, here, self.turn(name, t - 1, value, LEVELS))


def north(value):
    return pltpu.roll(value, EXT_ROWS - 1, 0)


def south(value):
    return pltpu.roll(value, 1, 0)


def polar_kernel(sz, block_ref, near_ref, far_ref, sides_ref, geo_ref, *refs):
    out_refs, (tend_ref, ext) = refs[:-2], refs[-2:]
    ring = Tiles(sz)
    lane = ring.lane
    tiles, stack, rows = sz.tiles, sz.stack, sz.rows
    for f, source in enumerate((0, 1, 5)):
        ext[f, :rows, sz.end :] = jnp.zeros((rows, LANES), jnp.float32)
        ext[f, :rows, : sz.merged] = block_ref[source, :rows, : sz.merged]
    add_rows(sz, ext, 2, near_ref, far_ref)
    inv_cos, sin_centre, cos_face = geo_ref[0], geo_ref[1], geo_ref[2]
    ratio = sz.ratio

    def tile(f, t):
        return ext[f, :, LANES * t : LANES * (t + 1)]

    kept = {}

    def zonal(t):
        if t not in kept:
            thick_e = ring.east("h", t, functools.partial(tile, 0))
            wind_e = ring.east("u", t, functools.partial(tile, 2))
            flux = 0.25 * (tile(2, t) + wind_e) * (tile(0, t) + thick_e) * inv_cos
            if t == tiles - 1:
                flux = jnp.where(lane < sz.tail - LEVELS, flux, 0.0)
            kept[t] = (flux, thick_e)
        return kept[t]

    for t in range(tiles):
        flux, thick_e = zonal(t)
        thick, wind_v, wind_u = tile(0, t), tile(1, t), tile(2, t)
        flux_w = ring.west("f", t, lambda s: zonal(s)[0])
        thick_w = ring.west("hw", t, functools.partial(tile, 0))
        thick_n = north(thick)
        flux_n = (0.25 * ratio) * (wind_v + north(wind_v)) * (thick + thick_n) * cos_face
        thick_tend = -((flux - flux_w) + (flux_n - south(flux_n)) * inv_cos)
        wind_u_tend = sin_centre * wind_v - (thick_e - thick_w) * (0.5 * inv_cos)
        wind_v_tend = -sin_centre * wind_u - (0.5 * ratio) * (thick_n - south(thick))
        spare = 0.0
        if t == tiles - 1:
            last = sz.tail - LEVELS
            columns = [(tile(0, 0), 0), (thick, last), (tile(2, 0), 0), (wind_u, last)]
            for k, (source, at) in reversed(list(enumerate(columns))):
                to = sz.tail + LEVELS * k
                spare = jnp.where(lane < to + LEVELS, pltpu.roll(source, (to - at) % LANES, 1), spare)
        for f, tend in enumerate((thick_tend, wind_u_tend, wind_v_tend)):
            if t == tiles - 1:
                tend = jnp.where(lane < sz.tail, tend, spare)
            tend_ref[pl.ds(stack * rows * f + t, rows, stride=stack), :] = tend[:rows]
    for f in range(3):
        for t in range(tiles, stack):
            tend_ref[pl.ds(stack * rows * f + t, rows, stride=stack), :] = jnp.zeros((rows, LANES), jnp.float32)
    used = stack * sz.units
    if used < tend_ref.shape[0]:
        tend_ref[used:, :] = jnp.zeros((tend_ref.shape[0] - used, LANES), jnp.float32)
    here = lax.axis_index("lon")
    for k, out_ref in enumerate(out_refs):
        out_ref[: sz.size] = tend_ref[sz.piece(k), :]
        if k:
            eastward = sz.partner(k) == lax.rem(here + 1, sz.n_lon)
            out_ref[sz.size :] = jnp.where(eastward, sides_ref[EXT_ROWS:], sides_ref[:EXT_ROWS])


def rest_kernel(sz, block_ref, near_ref, far_ref, geo_ref, after_ref, *refs):
    met_refs, (new_w_ref, new_h_ref, mass_ref, ext) = refs[: sz.n_lon - 1], refs[sz.n_lon - 1 :]
    ring = Tiles(sz)
    lane = ring.lane
    tiles, rows = sz.tiles, sz.rows
    ext[:, :rows, : sz.merged] = block_ref[:, :rows, : sz.merged]
    add_rows(sz, ext, 5, near_ref, far_ref)
    lane9 = lane[:rows]
    here = lax.axis_index("lon")
    from_e = from_w = met_refs[0][sz.size :]
    for k, met_ref in enumerate(met_refs[1:], 2):
        from_e = jnp.where(sz.partner(k) == lax.rem(here + 1, sz.n_lon), met_ref[sz.size :], from_e)
        from_w = jnp.where(sz.partner(k) == lax.rem(here + sz.n_lon - 1, sz.n_lon), met_ref[sz.size :], from_w)
    for place, f in enumerate((0, 5, 2, 3, 4)):
        after = pltpu.roll(from_e, (sz.tail - LEVELS * place) % LANES, 1)[:rows]
        before = pltpu.roll(from_w, (LANES - LEVELS - LEVELS * place) % LANES, 1)[:rows]
        own = ext[f, :rows, sz.end :]
        edge = jnp.where(lane9 < LANES - LEVELS, after, before)
        ext[f, :rows, sz.end :] = jnp.where(lane9 < sz.tail, own, edge)
    inv_cos, sin_centre, cos_face = geo_ref[0], geo_ref[1], geo_ref[2]
    ratio = sz.ratio

    def tile(f, t):
        return ext[f, :, LANES * t : LANES * (t + 1)]

    kept = {}

    def zonal(t):
        if t not in kept:
            thick_e = ring.east("h", t, functools.partial(tile, 0))
            wind_e = ring.east("u", t, functools.partial(tile, 5))
            flux = 0.25 * (tile(5, t) + wind_e) * (tile(0, t) + thick_e) * inv_cos
            parts = []
            for k in range(3):
                q = tile(2 + k, t)
                q_e = ring.east(k, t, functools.partial(tile, 2 + k))
                parts.append(DIFFUSION * (q_e - q) - flux * (0.5 * (q + q_e)))
            kept[t] = (flux, thick_e, parts)
        return kept[t]

    for t in range(tiles):
        span = sz.span(t)
        lanes = slice(LANES * t, LANES * t + span)
        flux, thick_e, parts = zonal(t)
        thick, wind_u, wind_v = tile(0, t), tile(5, t), tile(1, t)
        flux_w = ring.west("f", t, lambda s: zonal(s)[0])
        thick_w = ring.west("hw", t, functools.partial(tile, 0))
        thick_n = north(thick)
        flux_n = (0.25 * ratio) * (wind_v + north(wind_v)) * (thick + thick_n) * cos_face
        thick_tend = -((flux - flux_w) + (flux_n - south(flux_n)) * inv_cos)
        wind_u_tend = sin_centre * wind_v - (thick_e - thick_w) * (0.5 * inv_cos)
        wind_v_tend = -sin_centre * wind_u - (0.5 * ratio) * (thick_n - south(thick))
        new_h_ref[:, lanes] = (thick + TIME_STEP * thick_tend)[:rows, :span]
        new_w_ref[0, :, lanes] = (wind_u + TIME_STEP * wind_u_tend)[:rows, :span]
        new_w_ref[1, :, lanes] = (wind_v + TIME_STEP * wind_v_tend)[:rows, :span]
        for k in range(3):
            q = tile(2 + k, t)
            q_n = north(q)
            zonal_part = parts[k] - ring.west(("p", k), t, lambda s: zonal(s)[2][k])
            lap = q_n + south(q) - 2.0 * q
            over = flux_n * (0.5 * (q + q_n))
            merid_part = DIFFUSION * lap - (over - south(over)) * inv_cos
            mass = thick * q + TIME_STEP * (zonal_part + merid_part)
            mass_ref[:, k, lanes] = mass[:rows, :span].astype(jnp.bfloat16)


def sin_pi(y):
    y = jnp.where(y > 0.5, 1.0 - y, jnp.where(y < -0.5, -1.0 - y, y))
    s = y * y
    series = [(-1) ** i * math.pi ** (2 * i + 1) / math.factorial(2 * i + 1) for i in range(7)]
    total = series[-1]
    for factor in reversed(series[:-1]):
        total = total * s + factor
    return total * y


def share_of(sz, i):
    unit = lax.axis_index("lon") * sz.share + i
    return unit // sz.rows, lax.rem(unit, sz.rows)


def weights_kernel(sz, cut_ref, n_ref, inverse_ref, after_ref, weights_ref):
    band = lax.axis_index("lat")
    size = PER_TILE * sz.stack
    for i in range(sz.share):
        width = (2 * cut_ref[band * sz.rows + share_of(sz, i)[1]] + 1).astype(jnp.float32)
        n = n_ref[...]
        turns = n * width
        turns = turns - jnp.round(turns * (0.5 / sz.nlon)) * (2.0 * sz.nlon)
        weights = sin_pi(turns * (1.0 / sz.nlon)) * inverse_ref[...]
        weights = jnp.where(n == 0.0, width * (1.0 / sz.nlon), weights)
        weights_ref[size * i : size * (i + 1)] = weights.astype(jnp.bfloat16)


def filter_kernel(sz, weights_ref, geo_ref, *refs):
    n_lon, stack, share = sz.n_lon, sz.stack, sz.share
    in_refs, out_refs, (gathered, results) = refs[:n_lon], refs[n_lon : 2 * n_lon], refs[2 * n_lon :]
    for k, in_ref in enumerate(in_refs):
        gathered[sz.partner(k)] = in_ref[: sz.size]

    lane = lax.broadcasted_iota(jnp.int32, (share, LANES), 1)
    place = lax.broadcasted_iota(jnp.int32, (share, LANES), 0)
    by_flux = by_thick = jnp.zeros((share, LANES), jnp.float32)
    for i in range(share):
        field, row = share_of(sz, i)
        inv_cos = geo_ref[0, pl.ds(row, 1), :]
        by_flux = jnp.where((place == i) & (field == 0), inv_cos, by_flux)
        by_thick = jnp.where((place == i) & (field == 1), 0.5 * inv_cos, by_thick)
    sides = [gathered[s, pl.ds(sz.tiles - 1, share, stride=stack), :] for s in range(n_lon)]

    def column(s, k):
        return pltpu.roll(sides[s % n_lon], (-sz.tail - LEVELS * k) % LANES, 1)

    for s in range(n_lon):
        thick_w, thick_e = column(s, 1), column(s + 1, 0)
        flux = 0.25 * (column(s, 3) + column(s + 1, 2)) * (thick_w + thick_e) * by_flux
        west_of, east_of = flux + by_thick * thick_e, flux + by_thick * thick_w
        at = pl.ds(sz.tiles - 1, share, stride=stack)
        own = gathered[s, at, :]
        own = own - jnp.where(lane >= sz.tail - LEVELS, pltpu.roll(west_of, sz.tail - LEVELS, 1), 0.0)
        gathered[s, at, :] = jnp.where(lane < sz.tail, own, 0.0)
        at = pl.ds(0, share, stride=stack)
        after = (s + 1) % n_lon
        gathered[after, at, :] = gathered[after, at, :] + jnp.where(lane < LEVELS, east_of, 0.0)

    wide = lax.broadcasted_iota(jnp.int32, (stack, LANES), 1)
    rows = PER_TILE * stack
    for i in range(share):
        here = slice(stack * i, stack * (i + 1))
        pieces = [gathered[s, here].astype(jnp.bfloat16) for s in range(n_lon)]
        circle = jnp.concatenate([jnp.concatenate(pieces[s:] + pieces[:s], axis=0) for s in range(n_lon)], axis=1)
        spread = jnp.dot(weights_ref[rows * i : rows * (i + 1)], circle, preferred_element_type=jnp.float32)
        for s in range(n_lon):
            same = spread[:stack, LANES * s : LANES * (s + 1)]
            carried = None
            for e in range(1, PER_TILE):
                part = spread[stack * e : stack * (e + 1), LANES * s : LANES * (s + 1)]
                part = pltpu.roll(part, LEVELS * e, 1)
                inside = wide >= LEVELS * e
                same = same + jnp.where(inside, part, 0.0)
                over = jnp.where(inside, 0.0, part)
                carried = over if carried is None else carried + over
            results[s, here] = pltpu.roll(same, stack - 1, 0) + carried
    for k, out_ref in enumerate(out_refs):
        out_ref[...] = results[sz.partner(k)]


def finish_kernel(sz, cut_ref, block_ref, plain_w_ref, plain_h_ref, *refs):
    back_refs, (new_w_ref, new_h_ref, back_ref) = refs[: sz.n_lon], refs[sz.n_lon :]
    rows = sz.rows
    for k, ref in enumerate(back_refs):
        back_ref[sz.piece(k), :] = ref[...]
    row = lax.broadcasted_iota(jnp.int32, (rows, LANES), 0)
    cuts = jnp.zeros((rows, LANES), jnp.int32)
    for j in range(rows):
        cuts = jnp.where(row == j, cut_ref[lax.axis_index("lat") * rows + j], cuts)
    active = cuts < sz.nlon // 2
    for f in range(3):
        for t in range(sz.tiles):
            span = sz.span(t)
            lanes = slice(LANES * t, LANES * t + span)
            tend = back_ref[pl.ds(sz.stack * rows * f + t, rows, stride=sz.stack), :][:, :span]
            new = block_ref[(0, 5, 1)[f], :rows, lanes] + TIME_STEP * tend
            if f == 0:
                new_h_ref[:, lanes] = jnp.where(active[:, :span], new, plain_h_ref[:, lanes])
            else:
                new_w_ref[:, f - 1, lanes] = jnp.where(active[:, :span], new, plain_w_ref[f - 1, :, lanes])


def local(winds, thickness, tracers, cutoff):
    n_lat = lax.axis_size("lat")
    n_lon = lax.axis_size("lon")
    rows, merged = thickness.shape
    sz = Sizes(rows, merged, n_lat, n_lon)
    f32 = jnp.float32
    vmem = pl.BlockSpec(memory_space=pltpu.VMEM)
    smem = pl.BlockSpec(memory_space=pltpu.SMEM)
    hbm = pl.BlockSpec(memory_space=pltpu.HBM)
    anywhere = pl.BlockSpec(memory_space=pl.ANY)

    def shaped(*shape):
        return jax.ShapeDtypeStruct(shape, f32)

    def call(kernel, name, in_specs, out_shape, scratch=(), limit=LIMIT):
        return pl.pallas_call(
            functools.partial(kernel, sz),
            out_shape=out_shape,
            in_specs=in_specs,
            out_specs=jax.tree.map(lambda _: vmem, out_shape),
            scratch_shapes=list(scratch),
            compiler_params=pltpu.CompilerParams(vmem_limit_bytes=limit),
            name=name,
        )

    n, inverse = (jnp.asarray(table) for table in offsets(sz))

    wind_rows = jnp.swapaxes(winds, 0, 1)
    tracer_rows = jnp.swapaxes(tracers, 0, 1)
    row_pair = shaped(5 * sz.stack, LANES)
    to_near, to_far, sides, block, geo = call(
        rows_kernel,
        "rows",
        [hbm] * 4,
        (
            row_pair,
            row_pair,
            shaped(2 * EXT_ROWS, LANES),
            shaped(6, EXT_ROWS, sz.tiles * LANES),
            shaped(3, EXT_ROWS, LANES),
        ),
        [
            pltpu.VMEM((rows, merged), f32),
            pltpu.VMEM((rows, 2, merged), f32),
            pltpu.VMEM((rows, 3, merged), jnp.bfloat16),
            pltpu.SemaphoreType.DMA((4,)),
        ],
        limit=ALL_VMEM,
    )(thickness, wind_rows, tracer_rows, jnp.asarray(geometry(sz)))

    near = [(band * n_lon + i, (band ^ 1) * n_lon + i) for band in range(n_lat) for i in range(n_lon)]
    far = []
    for band in range(n_lat):
        other = band - 1 if band % 2 == 0 else band + 1
        for i in range(n_lon):
            if 0 <= other < n_lat:
                far.append((band * n_lon + i, other * n_lon + i))
            else:
                far.append((band * n_lon + i, band * n_lon + (i + n_lon // 2) % n_lon))
    from_near = lax.ppermute(to_near, ("lat", "lon"), near)
    from_far = lax.ppermute(to_far, ("lat", "lon"), far)

    order = [sz.turns(False), sz.turns(True)]

    def meetings(shares):
        got = [shares[0]]
        for k in range(1, n_lon):
            sectors = [(band, i, i ^ order[band % 2][k]) for band in range(n_lat) for i in range(n_lon)]
            got.append(lax.ppermute(shares[k], ("lat", "lon"), [(b * n_lon + i, b * n_lon + j) for b, i, j in sectors]))
        return got

    all_pieces = pltpu.VMEM((n_lon, sz.size, LANES), f32)
    tends = call(
        polar_kernel,
        "polar",
        [vmem] * 5,
        [shaped(sz.size, LANES)] + [shaped(sz.size + EXT_ROWS, LANES)] * (n_lon - 1),
        [pltpu.VMEM((n_lon * sz.size, LANES), f32), pltpu.VMEM((3, EXT_ROWS, sz.tiles * LANES), f32)],
    )(block, from_near, from_far, sides, geo)
    met = meetings(tends)
    weights = call(
        weights_kernel,
        "weights",
        [smem, vmem, vmem, anywhere],
        jax.ShapeDtypeStruct((sz.share * PER_TILE * sz.stack, n_lon * sz.stack), jnp.bfloat16),
    )(cutoff, n, inverse, tends[0])
    worked = call(
        filter_kernel,
        "filter",
        [vmem] * (2 + n_lon),
        [shaped(sz.size, LANES)] * n_lon,
        [all_pieces, all_pieces],
    )(weights, geo, *met)
    back = meetings(worked)

    plain_w, plain_h, mass = call(
        rest_kernel,
        "rest",
        [vmem] * 4 + [anywhere] + [vmem] * (n_lon - 1),
        (shaped(2, rows, merged), shaped(rows, merged), jax.ShapeDtypeStruct(tracer_rows.shape, jnp.bfloat16)),
        [pltpu.VMEM((6, EXT_ROWS, sz.tiles * LANES), f32)],
    )(block, from_near, from_far, geo, worked[0], *met[1:])

    new_w, new_h = call(
        finish_kernel,
        "finish",
        [smem] + [vmem] * (3 + n_lon),
        (shaped(*wind_rows.shape), shaped(rows, merged)),
        [pltpu.VMEM((n_lon * sz.size, LANES), f32)],
    )(cutoff, block, plain_w, plain_h, *back)
    return jnp.swapaxes(new_w, 0, 1), new_h, jnp.swapaxes(mass, 0, 1)


def solution(mesh):
    in_specs = (P(None, "lat", "lon"), P("lat", "lon"), P(None, "lat", "lon"), P())
    out_specs = (P(None, "lat", "lon"), P("lat", "lon"), P(None, "lat", "lon"))
    return jax.shard_map(local, mesh=mesh, in_specs=in_specs, out_specs=out_specs, check_vma=False)
```

```python
import functools
import math

import jax
import jax.numpy as jnp
import numpy as np
from jax import lax
from jax.experimental import pallas as pl
from jax.experimental.pallas import tpu as pltpu
from jax.sharding import PartitionSpec as P

LEVELS = 16
TIME_STEP = 0.05
DIFFUSION = 0.5
LANES = 128
PER_TILE = LANES // LEVELS
EXT_ROWS = 16
LIMIT = 48 * 1024 * 1024
ALL_VMEM = 64 * 1024 * 1024 - 256 * 1024


class Sizes:
    def __init__(self, rows, merged, n_lat, n_lon):
        self.rows = rows
        self.merged = merged
        self.columns = merged // LEVELS
        self.n_lat = n_lat
        self.n_lon = n_lon
        self.nlat = rows * n_lat
        self.nlon = self.columns * n_lon
        self.ratio = 2.0 * self.nlat / self.nlon
        self.tiles = -(-merged // LANES)
        self.end = (self.tiles - 1) * LANES
        self.tail = merged - self.end
        self.stack = -(-(self.tiles + 1) // 8) * 8
        self.units = 3 * rows
        self.share = -(-self.units // n_lon)
        self.size = self.share * self.stack
        self.pole = self.units - 1
        self.near_only = self.nlat // 6 < 2 * rows and self.units % self.share > 0
        assert self.tail <= LANES - 4 * LEVELS and rows + 2 <= EXT_ROWS and n_lat % 2 == 0
        assert n_lon >= 4 and n_lon & (n_lon - 1) == 0

    def span(self, tile):
        return self.tail if tile == self.tiles - 1 else LANES

    def turns(self, odd):
        middle = list(range(1, self.n_lon - 1))
        return [0, self.n_lon - 1] + (middle[::-1] if odd else middle)

    def partner(self, k):
        odd = lax.rem(lax.axis_index("lat"), 2) == 1
        turn = jnp.where(odd, self.turns(True)[k], self.turns(False)[k])
        return jnp.bitwise_xor(lax.axis_index("lon"), turn)

    def piece(self, k):
        return pl.ds(pl.multiple_of(self.partner(k) * self.size, 8), self.size)


def geometry(sz):
    table = np.zeros((sz.n_lat, 3, EXT_ROWS, LANES), np.float64)

    def face(j):
        return math.sin((j + 1) * math.pi / sz.nlat) if 0 <= j < sz.nlat - 1 else 0.0

    for band in range(sz.n_lat):
        for row in range(sz.rows):
            j = band * sz.rows + row
            centre = (j + 0.5) * math.pi / sz.nlat - math.pi / 2
            table[band, 0, row] = 1.0 / math.cos(centre)
            table[band, 1, row] = math.sin(centre)
            table[band, 2, row] = face(j)
        table[band, 2, EXT_ROWS - 1] = face(band * sz.rows - 1)
    return table.astype(np.float32)


def offsets(sz):
    shift, out_tile = np.divmod(np.arange(PER_TILE * sz.stack), sz.stack)
    sector, in_tile = np.divmod(np.arange(sz.n_lon * sz.stack), sz.stack)
    n = (PER_TILE * (out_tile - 1) + shift)[:, None] - (PER_TILE * in_tile + sz.columns * sector)[None, :]
    n = (n + sz.nlon // 2) % sz.nlon - sz.nlon // 2
    with np.errstate(divide="ignore"):
        inverse = np.where(n == 0, 0.0, 1.0 / (sz.nlon * np.sin(np.pi * n / sz.nlon)))
    return n.astype(np.float32), inverse.astype(np.float32)


def rows_kernel(sz, h_hbm, w_hbm, q_hbm, near_ref, far_ref, sides_ref, *scratch):
    row_refs, first_refs, last_refs, sems = scratch[:3], scratch[3:6], scratch[6:9], scratch[9]
    rows, last = sz.rows, sz.rows - 1
    copies = []
    for i, source in enumerate((h_hbm, w_hbm, q_hbm)):
        for k, row in enumerate((0, last)):
            one = source.at[pl.ds(row, 1)] if i == 0 else source.at[row]
            copies.append(pltpu.make_async_copy(one, row_refs[i].at[k], sems.at[i, k]))
        for k, (start, to) in enumerate(((0, first_refs[i]), (sz.end, last_refs[i]))):
            lanes = pl.ds(start, to.shape[-1])
            cut = source.at[:, lanes] if i == 0 else source.at[:, :, lanes]
            copies.append(pltpu.make_async_copy(cut, to, sems.at[i, 2 + k]))
    for copy in copies:
        copy.start()
    for copy in copies:
        copy.wait()
    even = lax.rem(lax.axis_index("lat"), 2) == 0
    h_rows, w_rows, q_rows = row_refs
    for t in range(sz.tiles):
        wide = sz.span(t)
        lanes = slice(LANES * t, LANES * t + wide)
        q = [q_rows[k, :, lanes].astype(jnp.float32) for k in range(2)]
        for f in range(5):
            if f == 0:
                first, final = h_rows[0, :, lanes], h_rows[1, :, lanes]
            elif f == 1:
                first, final = w_rows[0, 1:2, lanes], w_rows[1, 1:2, lanes]
            else:
                first, final = q[0][f - 2 : f - 1], q[1][f - 2 : f - 1]
            at = sz.stack * f + t
            near_ref[at : at + 1, :wide] = jnp.where(even, final, first)
            far_ref[at : at + 1, :wide] = jnp.where(even, first, final)
    sides_ref[...] = jnp.zeros(sides_ref.shape, jnp.float32)
    for k, (refs, at) in enumerate(((first_refs, 0), (last_refs, sz.tail - LEVELS))):
        columns = slice(at, at + LEVELS)
        for f in range(5):
            if f == 0:
                value = refs[0][:, columns]
            elif f == 1:
                value = refs[1][:, 0, columns]
            else:
                value = refs[2][:, f - 2, columns].astype(jnp.float32)
            sides_ref[EXT_ROWS * k : EXT_ROWS * k + rows, LEVELS * f : LEVELS * (f + 1)] = value


def add_rows(sz, ext, fields, near_ref, far_ref):
    band = lax.axis_index("lat")
    even = lax.rem(band, 2) == 0
    over_pole = (band == 0) | (band == sz.n_lat - 1)
    for f in range(fields):
        flip = jnp.where(over_pole, -1.0, 1.0) if f == 1 else 1.0
        for t in range(sz.tiles):
            at = slice(sz.stack * f + t, sz.stack * f + t + 1)
            near = near_ref[at]
            far = jnp.zeros_like(near) if far_ref is None else far_ref[at] * flip
            lanes = slice(LANES * t, LANES * (t + 1))
            ext[f, sz.rows : sz.rows + 1, lanes] = jnp.where(even, near, far)
            ext[f, EXT_ROWS - 1 : EXT_ROWS, lanes] = jnp.where(even, far, near)


class Tiles:
    def __init__(self, sz):
        self.sz = sz
        self.lane = lax.broadcasted_iota(jnp.int32, (EXT_ROWS, LANES), 1)
        self.turned = {}

    def turn(self, name, t, value, step):
        key = (name, t % self.sz.tiles, step)
        if key not in self.turned:
            self.turned[key] = pltpu.roll(value(t % self.sz.tiles), step % LANES, 1)
        return self.turned[key]

    def east(self, name, t, value):
        here = self.turn(name, t, value, -LEVELS)
        return jnp.where(self.lane < LANES - LEVELS, here, self.turn(name, t + 1, value, -LEVELS))

    def west(self, name, t, value):
        here = self.turn(name, t, value, LEVELS)
        return jnp.where(self.lane >= LEVELS, here, self.turn(name, t - 1, value, LEVELS))


def north(value):
    return pltpu.roll(value, EXT_ROWS - 1, 0)


def south(value):
    return pltpu.roll(value, 1, 0)


def polar_kernel(sz, h_ref, w_ref, near_ref, sides_ref, geo_ref, *refs):
    far_ref, refs = (None, refs) if sz.near_only else (refs[0], refs[1:])
    out_refs, (tend_ref, ext) = refs[:-2], refs[-2:]
    band = lax.axis_index("lat")
    ring = Tiles(sz)
    lane = ring.lane
    tiles, stack, rows = sz.tiles, sz.stack, sz.rows
    for f, value in enumerate((h_ref[...], w_ref[1], w_ref[0])):
        ext[f, :rows, sz.end :] = jnp.zeros((rows, LANES), jnp.float32)
        ext[f, :rows, : sz.merged] = value
    add_rows(sz, ext, 2, near_ref, far_ref)
    inv_cos, sin_centre, cos_face = geo_ref[band, 0], geo_ref[band, 1], geo_ref[band, 2]
    ratio = sz.ratio

    def tile(f, t):
        return ext[f, :, LANES * t : LANES * (t + 1)]

    kept = {}

    def zonal(t):
        if t not in kept:
            thick_e = ring.east("h", t, functools.partial(tile, 0))
            wind_e = ring.east("u", t, functools.partial(tile, 2))
            flux = 0.25 * (tile(2, t) + wind_e) * (tile(0, t) + thick_e) * inv_cos
            if t == tiles - 1:
                flux = jnp.where(lane < sz.tail - LEVELS, flux, 0.0)
            kept[t] = (flux, thick_e)
        return kept[t]

    for t in range(tiles):
        flux, thick_e = zonal(t)
        thick, wind_v, wind_u = tile(0, t), tile(1, t), tile(2, t)
        flux_w = ring.west("f", t, lambda s: zonal(s)[0])
        thick_w = ring.west("hw", t, functools.partial(tile, 0))
        thick_n = north(thick)
        flux_n = (0.25 * ratio) * (wind_v + north(wind_v)) * (thick + thick_n) * cos_face
        thick_tend = -((flux - flux_w) + (flux_n - south(flux_n)) * inv_cos)
        wind_u_tend = sin_centre * wind_v - (thick_e - thick_w) * (0.5 * inv_cos)
        wind_v_tend = -sin_centre * wind_u - (0.5 * ratio) * (thick_n - south(thick))
        spare = 0.0
        if t == tiles - 1:
            last = sz.tail - LEVELS
            columns = [(tile(0, 0), 0), (thick, last), (tile(2, 0), 0), (wind_u, last)]
            for k, (source, at) in reversed(list(enumerate(columns))):
                to = sz.tail + LEVELS * k
                spare = jnp.where(lane < to + LEVELS, pltpu.roll(source, (to - at) % LANES, 1), spare)
        for f, tend in enumerate((thick_tend, wind_u_tend, wind_v_tend)):
            if t == tiles - 1:
                tend = jnp.where(lane < sz.tail, tend, spare)
            tend_ref[pl.ds(stack * rows * f + t, rows, stride=stack), :] = tend[:rows]
    for f in range(3):
        for t in range(tiles, stack):
            tend_ref[pl.ds(stack * rows * f + t, rows, stride=stack), :] = jnp.zeros((rows, LANES), jnp.float32)
    used = stack * sz.units
    if used < tend_ref.shape[0]:
        tend_ref[used:, :] = jnp.zeros((tend_ref.shape[0] - used, LANES), jnp.float32)
    if sz.near_only:
        swap_ends(sz, tend_ref)
        for t in range(tiles):
            lanes = slice(LANES * t, LANES * (t + 1))
            row = jnp.where(band < sz.n_lat // 2, ext[0, 0:1, lanes], ext[0, rows - 1 : rows, lanes])
            tend_ref[used + t : used + t + 1, :] = row
    here = lax.axis_index("lon")
    for k, out_ref in enumerate(out_refs):
        out_ref[: sz.size] = tend_ref[sz.piece(k), :]
        if k:
            eastward = sz.partner(k) == lax.rem(here + 1, sz.n_lon)
            out_ref[sz.size :] = jnp.where(eastward, sides_ref[EXT_ROWS:], sides_ref[:EXT_ROWS])


def rest_kernel(sz, h_ref, w_ref, q_ref, near_ref, far_ref, geo_ref, after_ref, *refs):
    met_refs, (new_w_ref, new_h_ref, mass_ref, ext) = refs[: sz.n_lon - 1], refs[sz.n_lon - 1 :]
    band = lax.axis_index("lat")
    ring = Tiles(sz)
    lane = ring.lane
    tiles, rows = sz.tiles, sz.rows
    for f in range(6):
        if f < 2 or f == 5:
            value = (h_ref[...], w_ref[1], w_ref[0])[min(f, 2)]
        else:
            value = q_ref[f - 2].astype(jnp.float32)
        ext[f, :rows, : sz.merged] = value
    add_rows(sz, ext, 5, near_ref, far_ref)
    lane9 = lane[:rows]
    here = lax.axis_index("lon")
    from_e = from_w = met_refs[0][sz.size :]
    for k, met_ref in enumerate(met_refs[1:], 2):
        from_e = jnp.where(sz.partner(k) == lax.rem(here + 1, sz.n_lon), met_ref[sz.size :], from_e)
        from_w = jnp.where(sz.partner(k) == lax.rem(here + sz.n_lon - 1, sz.n_lon), met_ref[sz.size :], from_w)
    for place, f in enumerate((0, 5, 2, 3, 4)):
        after = pltpu.roll(from_e, (sz.tail - LEVELS * place) % LANES, 1)[:rows]
        before = pltpu.roll(from_w, (LANES - LEVELS - LEVELS * place) % LANES, 1)[:rows]
        own = ext[f, :rows, sz.end :]
        edge = jnp.where(lane9 < LANES - LEVELS, after, before)
        ext[f, :rows, sz.end :] = jnp.where(lane9 < sz.tail, own, edge)
    inv_cos, sin_centre, cos_face = geo_ref[band, 0], geo_ref[band, 1], geo_ref[band, 2]
    ratio = sz.ratio

    def tile(f, t):
        return ext[f, :, LANES * t : LANES * (t + 1)]

    kept = {}

    def zonal(t):
        if t not in kept:
            thick_e = ring.east("h", t, functools.partial(tile, 0))
            wind_e = ring.east("u", t, functools.partial(tile, 5))
            flux = 0.25 * (tile(5, t) + wind_e) * (tile(0, t) + thick_e) * inv_cos
            parts = []
            for k in range(3):
                q = tile(2 + k, t)
                q_e = ring.east(k, t, functools.partial(tile, 2 + k))
                parts.append(DIFFUSION * (q_e - q) - flux * (0.5 * (q + q_e)))
            kept[t] = (flux, thick_e, parts)
        return kept[t]

    for t in range(tiles):
        span = sz.span(t)
        lanes = slice(LANES * t, LANES * t + span)
        flux, thick_e, parts = zonal(t)
        thick, wind_u, wind_v = tile(0, t), tile(5, t), tile(1, t)
        flux_w = ring.west("f", t, lambda s: zonal(s)[0])
        thick_w = ring.west("hw", t, functools.partial(tile, 0))
        thick_n = north(thick)
        flux_n = (0.25 * ratio) * (wind_v + north(wind_v)) * (thick + thick_n) * cos_face
        thick_tend = -((flux - flux_w) + (flux_n - south(flux_n)) * inv_cos)
        wind_u_tend = sin_centre * wind_v - (thick_e - thick_w) * (0.5 * inv_cos)
        wind_v_tend = -sin_centre * wind_u - (0.5 * ratio) * (thick_n - south(thick))
        new_h_ref[:, lanes] = (thick + TIME_STEP * thick_tend)[:rows, :span]
        new_w_ref[0, :, lanes] = (wind_u + TIME_STEP * wind_u_tend)[:rows, :span]
        new_w_ref[1, :, lanes] = (wind_v + TIME_STEP * wind_v_tend)[:rows, :span]
        for k in range(3):
            q = tile(2 + k, t)
            q_n = north(q)
            zonal_part = parts[k] - ring.west(("p", k), t, lambda s: zonal(s)[2][k])
            lap = q_n + south(q) - 2.0 * q
            over = flux_n * (0.5 * (q + q_n))
            merid_part = DIFFUSION * lap - (over - south(over)) * inv_cos
            mass = thick * q + TIME_STEP * (zonal_part + merid_part)
            mass_ref[k, :, lanes] = mass[:rows, :span].astype(jnp.bfloat16)


def sin_pi(y):
    y = jnp.where(y > 0.5, 1.0 - y, jnp.where(y < -0.5, -1.0 - y, y))
    s = y * y
    series = [(-1) ** i * math.pi ** (2 * i + 1) / math.factorial(2 * i + 1) for i in range(7)]
    total = series[-1]
    for factor in reversed(series[:-1]):
        total = total * s + factor
    return total * y


def share_of(sz, i):
    unit = lax.axis_index("lon") * sz.share + i
    row = lax.rem(unit, sz.rows)
    if sz.near_only:
        low = lax.axis_index("lat") < sz.n_lat // 2
        row = jnp.where(low & (unit == sz.pole), 0, row)
        row = jnp.where(low & (unit == 2 * sz.rows), sz.rows - 1, row)
    return unit // sz.rows, row


def swap_ends(sz, ref):
    low = lax.axis_index("lat") < sz.n_lat // 2
    first = slice(2 * sz.rows * sz.stack, (2 * sz.rows + 1) * sz.stack)
    last = slice(sz.pole * sz.stack, sz.units * sz.stack)
    a, b = ref[first], ref[last]
    ref[first] = jnp.where(low, b, a)
    ref[last] = jnp.where(low, a, b)


def weights_kernel(sz, cut_ref, n_ref, inverse_ref, far_ref, after_ref, weights_ref, to_far_ref):
    to_far_ref[...] = far_ref[...]
    band = lax.axis_index("lat")
    size = PER_TILE * sz.stack
    for i in range(sz.share):
        width = (2 * cut_ref[band * sz.rows + share_of(sz, i)[1]] + 1).astype(jnp.float32)
        n = n_ref[...]
        turns = n * width
        turns = turns - jnp.round(turns * (0.5 / sz.nlon)) * (2.0 * sz.nlon)
        weights = sin_pi(turns * (1.0 / sz.nlon)) * inverse_ref[...]
        weights = jnp.where(n == 0.0, width * (1.0 / sz.nlon), weights)
        weights_ref[size * i : size * (i + 1)] = weights.astype(jnp.bfloat16)


def filter_kernel(sz, weights_ref, geo_ref, *refs):
    n_lon, stack, share = sz.n_lon, sz.stack, sz.share
    in_refs, out_refs, (gathered, results) = refs[:n_lon], refs[n_lon : 2 * n_lon], refs[2 * n_lon :]
    for k, in_ref in enumerate(in_refs):
        gathered[sz.partner(k)] = in_ref[: sz.size]

    band = lax.axis_index("lat")
    lane = lax.broadcasted_iota(jnp.int32, (share, LANES), 1)
    place = lax.broadcasted_iota(jnp.int32, (share, LANES), 0)
    by_flux = by_thick = jnp.zeros((share, LANES), jnp.float32)
    for i in range(share):
        field, row = share_of(sz, i)
        inv_cos = geo_ref[band, 0, pl.ds(row, 1), :]
        by_flux = jnp.where((place == i) & (field == 0), inv_cos, by_flux)
        by_thick = jnp.where((place == i) & (field == 1), 0.5 * inv_cos, by_thick)
    sides = [gathered[s, pl.ds(sz.tiles - 1, share, stride=stack), :] for s in range(n_lon)]

    def column(s, k):
        return pltpu.roll(sides[s % n_lon], (-sz.tail - LEVELS * k) % LANES, 1)

    for s in range(n_lon):
        thick_w, thick_e = column(s, 1), column(s + 1, 0)
        flux = 0.25 * (column(s, 3) + column(s + 1, 2)) * (thick_w + thick_e) * by_flux
        west_of, east_of = flux + by_thick * thick_e, flux + by_thick * thick_w
        at = pl.ds(sz.tiles - 1, share, stride=stack)
        own = gathered[s, at, :]
        own = own - jnp.where(lane >= sz.tail - LEVELS, pltpu.roll(west_of, sz.tail - LEVELS, 1), 0.0)
        gathered[s, at, :] = jnp.where(lane < sz.tail, own, 0.0)
        at = pl.ds(0, share, stride=stack)
        after = (s + 1) % n_lon
        gathered[after, at, :] = gathered[after, at, :] + jnp.where(lane < LEVELS, east_of, 0.0)

    if sz.near_only:
        sign = jnp.where(band == 0, 1.0, jnp.where(band == sz.n_lat - 1, -1.0, 0.0))
        factor = jnp.where(lax.axis_index("lon") == sz.pole // share, 0.5 * sz.ratio * sign, 0.0)
        at = sz.pole % share * stack
        for s in range(n_lon):
            over = gathered[(s + n_lon // 2) % n_lon, at + stack : at + 2 * stack]
            gathered[s, at : at + stack] = gathered[s, at : at + stack] + factor * over

    wide = lax.broadcasted_iota(jnp.int32, (stack, LANES), 1)
    rows = PER_TILE * stack
    for i in range(share):
        here = slice(stack * i, stack * (i + 1))
        pieces = [gathered[s, here].astype(jnp.bfloat16) for s in range(n_lon)]
        circle = jnp.concatenate([jnp.concatenate(pieces[s:] + pieces[:s], axis=0) for s in range(n_lon)], axis=1)
        spread = jnp.dot(weights_ref[rows * i : rows * (i + 1)], circle, preferred_element_type=jnp.float32)
        for s in range(n_lon):
            same = spread[:stack, LANES * s : LANES * (s + 1)]
            carried = None
            for e in range(1, PER_TILE):
                part = spread[stack * e : stack * (e + 1), LANES * s : LANES * (s + 1)]
                part = pltpu.roll(part, LEVELS * e, 1)
                inside = wide >= LEVELS * e
                same = same + jnp.where(inside, part, 0.0)
                over = jnp.where(inside, 0.0, part)
                carried = over if carried is None else carried + over
            results[s, here] = pltpu.roll(same, stack - 1, 0) + carried
    for k, out_ref in enumerate(out_refs):
        out_ref[...] = results[sz.partner(k)]


def finish_kernel(sz, cut_ref, h_ref, w_ref, plain_w_ref, plain_h_ref, *refs):
    back_refs, (new_w_ref, new_h_ref, back_ref) = refs[: sz.n_lon], refs[sz.n_lon :]
    rows = sz.rows
    for k, ref in enumerate(back_refs):
        back_ref[sz.piece(k), :] = ref[...]
    if sz.near_only:
        swap_ends(sz, back_ref)
    row = lax.broadcasted_iota(jnp.int32, (rows, LANES), 0)
    cuts = jnp.zeros((rows, LANES), jnp.int32)
    for j in range(rows):
        cuts = jnp.where(row == j, cut_ref[lax.axis_index("lat") * rows + j], cuts)
    active = cuts < sz.nlon // 2
    for f in range(3):
        for t in range(sz.tiles):
            span = sz.span(t)
            lanes = slice(LANES * t, LANES * t + span)
            tend = back_ref[pl.ds(sz.stack * rows * f + t, rows, stride=sz.stack), :][:, :span]
            if f == 0:
                new = h_ref[:, lanes] + TIME_STEP * tend
                new_h_ref[:, lanes] = jnp.where(active[:, :span], new, plain_h_ref[:, lanes])
            else:
                new = w_ref[f - 1, :, lanes] + TIME_STEP * tend
                new_w_ref[:, f - 1, lanes] = jnp.where(active[:, :span], new, plain_w_ref[f - 1, :, lanes])


def local(winds, thickness, tracers, cutoff):
    n_lat = lax.axis_size("lat")
    n_lon = lax.axis_size("lon")
    rows, merged = thickness.shape
    sz = Sizes(rows, merged, n_lat, n_lon)
    f32 = jnp.float32
    vmem = pl.BlockSpec(memory_space=pltpu.VMEM)
    smem = pl.BlockSpec(memory_space=pltpu.SMEM)
    hbm = pl.BlockSpec(memory_space=pltpu.HBM)
    anywhere = pl.BlockSpec(memory_space=pl.ANY)

    def shaped(*shape):
        return jax.ShapeDtypeStruct(shape, f32)

    def call(kernel, name, in_specs, out_shape, scratch=(), limit=LIMIT):
        return pl.pallas_call(
            functools.partial(kernel, sz),
            out_shape=out_shape,
            in_specs=in_specs,
            out_specs=jax.tree.map(lambda _: vmem, out_shape),
            scratch_shapes=list(scratch),
            compiler_params=pltpu.CompilerParams(vmem_limit_bytes=limit),
            name=name,
        )

    geo = jnp.asarray(geometry(sz))
    n, inverse = (jnp.asarray(table) for table in offsets(sz))

    wind_rows = jnp.swapaxes(winds, 0, 1)
    tracer_rows = jnp.swapaxes(tracers, 0, 1)
    row_pair = shaped(5 * sz.stack, LANES)
    kept = [((1,), f32), ((2,), f32), ((3,), jnp.bfloat16)]
    to_near, to_far, sides = call(
        rows_kernel,
        "rows",
        [hbm] * 3,
        (row_pair, row_pair, shaped(2 * EXT_ROWS, LANES)),
        [pltpu.VMEM((2,) + count + (merged,), dtype) for count, dtype in kept]
        + [
            pltpu.VMEM((rows,) + (count if count != (1,) else ()) + (lanes,), dtype)
            for lanes in (LANES, sz.tail)
            for count, dtype in kept
        ]
        + [pltpu.SemaphoreType.DMA((3, 4))],
        limit=ALL_VMEM,
    )(thickness, wind_rows, tracer_rows)

    near = [(band * n_lon + i, (band ^ 1) * n_lon + i) for band in range(n_lat) for i in range(n_lon)]
    far = []
    for band in range(n_lat):
        other = band - 1 if band % 2 == 0 else band + 1
        for i in range(n_lon):
            if 0 <= other < n_lat:
                far.append((band * n_lon + i, other * n_lon + i))
            else:
                far.append((band * n_lon + i, band * n_lon + (i + n_lon // 2) % n_lon))
    from_near = lax.ppermute(to_near, ("lat", "lon"), near)
    first_far = () if sz.near_only else (lax.ppermute(to_far, ("lat", "lon"), far),)

    order = [sz.turns(False), sz.turns(True)]

    def meetings(shares):
        got = [shares[0]]
        for k in range(1, n_lon):
            sectors = [(band, i, i ^ order[band % 2][k]) for band in range(n_lat) for i in range(n_lon)]
            got.append(lax.ppermute(shares[k], ("lat", "lon"), [(b * n_lon + i, b * n_lon + j) for b, i, j in sectors]))
        return got

    all_pieces = pltpu.VMEM((n_lon, sz.size, LANES), f32)
    tends = call(
        polar_kernel,
        "polar",
        [vmem] * (5 + len(first_far)),
        [shaped(sz.size, LANES)] + [shaped(sz.size + EXT_ROWS, LANES)] * (n_lon - 1),
        [pltpu.VMEM((n_lon * sz.size, LANES), f32), pltpu.VMEM((3, EXT_ROWS, sz.tiles * LANES), f32)],
    )(thickness, winds, from_near, sides, geo, *first_far)
    met = meetings(tends)
    weights, to_far = call(
        weights_kernel,
        "weights",
        [smem, vmem, vmem, vmem, anywhere],
        (jax.ShapeDtypeStruct((sz.share * PER_TILE * sz.stack, n_lon * sz.stack), jnp.bfloat16), row_pair),
    )(cutoff, n, inverse, to_far, tends[0])
    from_far = lax.ppermute(to_far, ("lat", "lon"), far) if sz.near_only else first_far[0]
    worked = call(
        filter_kernel,
        "filter",
        [vmem] * (2 + n_lon),
        [shaped(sz.size, LANES)] * n_lon,
        [all_pieces, all_pieces],
    )(weights, geo, *met)
    back = meetings(worked)

    plain_w, plain_h, mass = call(
        rest_kernel,
        "rest",
        [vmem] * 6 + [anywhere] + [vmem] * (n_lon - 1),
        (shaped(2, rows, merged), shaped(rows, merged), jax.ShapeDtypeStruct(tracers.shape, jnp.bfloat16)),
        [pltpu.VMEM((6, EXT_ROWS, sz.tiles * LANES), f32)],
    )(thickness, winds, tracers, from_near, from_far, geo, worked[0], *met[1:])

    new_w, new_h = call(
        finish_kernel,
        "finish",
        [smem] + [vmem] * (4 + n_lon),
        (shaped(*wind_rows.shape), shaped(rows, merged)),
        [pltpu.VMEM((n_lon * sz.size, LANES), f32)],
    )(cutoff, thickness, winds, plain_w, plain_h, *back)
    return jnp.swapaxes(new_w, 0, 1), new_h, mass


def solution(mesh):
    in_specs = (P(None, "lat", "lon"), P("lat", "lon"), P(None, "lat", "lon"), P())
    out_specs = (P(None, "lat", "lon"), P("lat", "lon"), P(None, "lat", "lon"))
    return jax.shard_map(local, mesh=mesh, in_specs=in_specs, out_specs=out_specs, check_vma=False)
```

```python
import functools
import math

import jax
import jax.numpy as jnp
import numpy as np
from jax import lax
from jax.experimental import pallas as pl
from jax.experimental.pallas import tpu as pltpu
from jax.sharding import PartitionSpec as P

LEVELS = 16
TIME_STEP = 0.05
DIFFUSION = 0.5
LANES = 128
PER_TILE = LANES // LEVELS
EXT_ROWS = 16
LIMIT = 48 * 1024 * 1024
ALL_VMEM = 64 * 1024 * 1024 - 256 * 1024


class Sizes:
    def __init__(self, rows, merged, n_lat, n_lon):
        self.rows = rows
        self.merged = merged
        self.columns = merged // LEVELS
        self.n_lat = n_lat
        self.n_lon = n_lon
        self.nlat = rows * n_lat
        self.nlon = self.columns * n_lon
        self.ratio = 2.0 * self.nlat / self.nlon
        self.tiles = -(-merged // LANES)
        self.end = (self.tiles - 1) * LANES
        self.tail = merged - self.end
        self.stack = -(-(self.tiles + 1) // 8) * 8
        self.units = 3 * rows
        self.share = -(-self.units // n_lon)
        self.size = self.share * self.stack
        self.pole = self.units - 1
        self.near_only = self.nlat // 6 < 2 * rows and self.units % self.share > 0
        assert self.tail <= LANES - 4 * LEVELS and rows + 2 <= EXT_ROWS and n_lat % 2 == 0
        assert n_lon >= 4 and n_lon & (n_lon - 1) == 0

    def span(self, tile):
        return self.tail if tile == self.tiles - 1 else LANES

    def turns(self, odd):
        middle = list(range(1, self.n_lon - 1))
        return [0, self.n_lon - 1] + (middle[::-1] if odd else middle)

    def partner(self, k):
        odd = lax.rem(lax.axis_index("lat"), 2) == 1
        turn = jnp.where(odd, self.turns(True)[k], self.turns(False)[k])
        return jnp.bitwise_xor(lax.axis_index("lon"), turn)

    def piece(self, k):
        return pl.ds(pl.multiple_of(self.partner(k) * self.size, 8), self.size)


def geometry(sz):
    table = np.zeros((sz.n_lat, 3, EXT_ROWS, LANES), np.float64)

    def face(j):
        return math.sin((j + 1) * math.pi / sz.nlat) if 0 <= j < sz.nlat - 1 else 0.0

    for band in range(sz.n_lat):
        for row in range(sz.rows):
            j = band * sz.rows + row
            centre = (j + 0.5) * math.pi / sz.nlat - math.pi / 2
            table[band, 0, row] = 1.0 / math.cos(centre)
            table[band, 1, row] = math.sin(centre)
            table[band, 2, row] = face(j)
        table[band, 2, EXT_ROWS - 1] = face(band * sz.rows - 1)
    return table.astype(np.float32)


def offsets(sz):
    shift, out_tile = np.divmod(np.arange(PER_TILE * sz.stack), sz.stack)
    sector, in_tile = np.divmod(np.arange(sz.n_lon * sz.stack), sz.stack)
    n = (PER_TILE * (out_tile - 1) + shift)[:, None] - (PER_TILE * in_tile + sz.columns * sector)[None, :]
    n = (n + sz.nlon // 2) % sz.nlon - sz.nlon // 2
    with np.errstate(divide="ignore"):
        inverse = np.where(n == 0, 0.0, 1.0 / (sz.nlon * np.sin(np.pi * n / sz.nlon)))
    return n.astype(np.float32), inverse.astype(np.float32)


def rows_kernel(sz, h_hbm, w_hbm, q_hbm, near_ref, far_ref, sides_ref, *scratch):
    row_refs, first_refs, last_refs, sems = scratch[:3], scratch[3:6], scratch[6:9], scratch[9]
    rows, last = sz.rows, sz.rows - 1
    copies = []
    for i, source in enumerate((h_hbm, w_hbm, q_hbm)):
        for k, row in enumerate((0, last)):
            one = source.at[pl.ds(row, 1)] if i == 0 else source.at[row]
            copies.append(pltpu.make_async_copy(one, row_refs[i].at[k], sems.at[i, k]))
        for k, (start, to) in enumerate(((0, first_refs[i]), (sz.end, last_refs[i]))):
            lanes = pl.ds(start, to.shape[-1])
            cut = source.at[:, lanes] if i == 0 else source.at[:, :, lanes]
            copies.append(pltpu.make_async_copy(cut, to, sems.at[i, 2 + k]))
    for copy in copies:
        copy.start()
    for copy in copies:
        copy.wait()
    even = lax.rem(lax.axis_index("lat"), 2) == 0
    h_rows, w_rows, q_rows = row_refs
    for t in range(sz.tiles):
        wide = sz.span(t)
        lanes = slice(LANES * t, LANES * t + wide)
        q = [q_rows[k, :, lanes].astype(jnp.float32) for k in range(2)]
        for f in range(5):
            if f == 0:
                first, final = h_rows[0, :, lanes], h_rows[1, :, lanes]
            elif f == 1:
                first, final = w_rows[0, 1:2, lanes], w_rows[1, 1:2, lanes]
            else:
                first, final = q[0][f - 2 : f - 1], q[1][f - 2 : f - 1]
            at = sz.stack * f + t
            near_ref[at : at + 1, :wide] = jnp.where(even, final, first)
            far_ref[at : at + 1, :wide] = jnp.where(even, first, final)
    sides_ref[...] = jnp.zeros(sides_ref.shape, jnp.float32)
    for k, (refs, at) in enumerate(((first_refs, 0), (last_refs, sz.tail - LEVELS))):
        columns = slice(at, at + LEVELS)
        for f in range(5):
            if f == 0:
                value = refs[0][:, columns]
            elif f == 1:
                value = refs[1][:, 0, columns]
            else:
                value = refs[2][:, f - 2, columns].astype(jnp.float32)
            sides_ref[EXT_ROWS * k : EXT_ROWS * k + rows, LEVELS * f : LEVELS * (f + 1)] = value


def add_rows(sz, ext, fields, near_ref, far_ref):
    band = lax.axis_index("lat")
    even = lax.rem(band, 2) == 0
    over_pole = (band == 0) | (band == sz.n_lat - 1)
    for f in range(fields):
        flip = jnp.where(over_pole, -1.0, 1.0) if f == 1 else 1.0
        for t in range(sz.tiles):
            at = slice(sz.stack * f + t, sz.stack * f + t + 1)
            near = near_ref[at]
            far = jnp.zeros_like(near) if far_ref is None else far_ref[at] * flip
            lanes = slice(LANES * t, LANES * (t + 1))
            ext[f, sz.rows : sz.rows + 1, lanes] = jnp.where(even, near, far)
            ext[f, EXT_ROWS - 1 : EXT_ROWS, lanes] = jnp.where(even, far, near)


class Tiles:
    def __init__(self, sz):
        self.sz = sz
        self.lane = lax.broadcasted_iota(jnp.int32, (EXT_ROWS, LANES), 1)
        self.turned = {}

    def turn(self, name, t, value, step):
        key = (name, t % self.sz.tiles, step)
        if key not in self.turned:
            self.turned[key] = pltpu.roll(value(t % self.sz.tiles), step % LANES, 1)
        return self.turned[key]

    def east(self, name, t, value):
        here = self.turn(name, t, value, -LEVELS)
        return jnp.where(self.lane < LANES - LEVELS, here, self.turn(name, t + 1, value, -LEVELS))

    def west(self, name, t, value):
        here = self.turn(name, t, value, LEVELS)
        return jnp.where(self.lane >= LEVELS, here, self.turn(name, t - 1, value, LEVELS))


def north(value):
    return pltpu.roll(value, EXT_ROWS - 1, 0)


def south(value):
    return pltpu.roll(value, 1, 0)


def polar_kernel(sz, h_ref, w_ref, near_ref, sides_ref, geo_ref, far_ref, *refs):
    out_refs, (through_ref, tend_ref, ext) = refs[:-3], refs[-3:]
    through_ref[...] = far_ref[...]
    if sz.near_only:
        far_ref = None
    band = lax.axis_index("lat")
    ring = Tiles(sz)
    lane = ring.lane
    tiles, stack, rows = sz.tiles, sz.stack, sz.rows
    for f, value in enumerate((h_ref[...], w_ref[1], w_ref[0])):
        ext[f, :rows, sz.end :] = jnp.zeros((rows, LANES), jnp.float32)
        ext[f, :rows, : sz.merged] = value
    add_rows(sz, ext, 2, near_ref, far_ref)
    inv_cos, sin_centre, cos_face = geo_ref[band, 0], geo_ref[band, 1], geo_ref[band, 2]
    ratio = sz.ratio

    def tile(f, t):
        return ext[f, :, LANES * t : LANES * (t + 1)]

    kept = {}

    def zonal(t):
        if t not in kept:
            thick_e = ring.east("h", t, functools.partial(tile, 0))
            wind_e = ring.east("u", t, functools.partial(tile, 2))
            flux = 0.25 * (tile(2, t) + wind_e) * (tile(0, t) + thick_e) * inv_cos
            if t == tiles - 1:
                flux = jnp.where(lane < sz.tail - LEVELS, flux, 0.0)
            kept[t] = (flux, thick_e)
        return kept[t]

    for t in range(tiles):
        flux, thick_e = zonal(t)
        thick, wind_v, wind_u = tile(0, t), tile(1, t), tile(2, t)
        flux_w = ring.west("f", t, lambda s: zonal(s)[0])
        thick_w = ring.west("hw", t, functools.partial(tile, 0))
        thick_n = north(thick)
        flux_n = (0.25 * ratio) * (wind_v + north(wind_v)) * (thick + thick_n) * cos_face
        thick_tend = -((flux - flux_w) + (flux_n - south(flux_n)) * inv_cos)
        wind_u_tend = sin_centre * wind_v - (thick_e - thick_w) * (0.5 * inv_cos)
        wind_v_tend = -sin_centre * wind_u - (0.5 * ratio) * (thick_n - south(thick))
        spare = 0.0
        if t == tiles - 1:
            last = sz.tail - LEVELS
            columns = [(tile(0, 0), 0), (thick, last), (tile(2, 0), 0), (wind_u, last)]
            for k, (source, at) in reversed(list(enumerate(columns))):
                to = sz.tail + LEVELS * k
                spare = jnp.where(lane < to + LEVELS, pltpu.roll(source, (to - at) % LANES, 1), spare)
        for f, tend in enumerate((thick_tend, wind_u_tend, wind_v_tend)):
            if t == tiles - 1:
                tend = jnp.where(lane < sz.tail, tend, spare)
            tend_ref[pl.ds(stack * rows * f + t, rows, stride=stack), :] = tend[:rows]
    for f in range(3):
        for t in range(tiles, stack):
            tend_ref[pl.ds(stack * rows * f + t, rows, stride=stack), :] = jnp.zeros((rows, LANES), jnp.float32)
    used = stack * sz.units
    if used < tend_ref.shape[0]:
        tend_ref[used:, :] = jnp.zeros((tend_ref.shape[0] - used, LANES), jnp.float32)
    if sz.near_only:
        swap_ends(sz, tend_ref)
        for t in range(tiles):
            lanes = slice(LANES * t, LANES * (t + 1))
            row = jnp.where(band < sz.n_lat // 2, ext[0, 0:1, lanes], ext[0, rows - 1 : rows, lanes])
            tend_ref[used + t : used + t + 1, :] = row
    here = lax.axis_index("lon")
    for k, out_ref in enumerate(out_refs):
        out_ref[: sz.size] = tend_ref[sz.piece(k), :]
        if k:
            eastward = sz.partner(k) == lax.rem(here + 1, sz.n_lon)
            out_ref[sz.size :] = jnp.where(eastward, sides_ref[EXT_ROWS:], sides_ref[:EXT_ROWS])


def rest_kernel(sz, h_ref, w_ref, q_ref, near_ref, far_ref, geo_ref, after_ref, *refs):
    met_refs, (new_w_ref, new_h_ref, mass_ref, ext) = refs[: sz.n_lon - 1], refs[sz.n_lon - 1 :]
    band = lax.axis_index("lat")
    ring = Tiles(sz)
    lane = ring.lane
    tiles, rows = sz.tiles, sz.rows
    for f in range(6):
        if f < 2 or f == 5:
            value = (h_ref[...], w_ref[1], w_ref[0])[min(f, 2)]
        else:
            value = q_ref[f - 2].astype(jnp.float32)
        ext[f, :rows, : sz.merged] = value
    add_rows(sz, ext, 5, near_ref, far_ref)
    lane9 = lane[:rows]
    here = lax.axis_index("lon")
    from_e = from_w = met_refs[0][sz.size :]
    for k, met_ref in enumerate(met_refs[1:], 2):
        from_e = jnp.where(sz.partner(k) == lax.rem(here + 1, sz.n_lon), met_ref[sz.size :], from_e)
        from_w = jnp.where(sz.partner(k) == lax.rem(here + sz.n_lon - 1, sz.n_lon), met_ref[sz.size :], from_w)
    for place, f in enumerate((0, 5, 2, 3, 4)):
        after = pltpu.roll(from_e, (sz.tail - LEVELS * place) % LANES, 1)[:rows]
        before = pltpu.roll(from_w, (LANES - LEVELS - LEVELS * place) % LANES, 1)[:rows]
        own = ext[f, :rows, sz.end :]
        edge = jnp.where(lane9 < LANES - LEVELS, after, before)
        ext[f, :rows, sz.end :] = jnp.where(lane9 < sz.tail, own, edge)
    inv_cos, sin_centre, cos_face = geo_ref[band, 0], geo_ref[band, 1], geo_ref[band, 2]
    ratio = sz.ratio

    def tile(f, t):
        return ext[f, :, LANES * t : LANES * (t + 1)]

    kept = {}

    def zonal(t):
        if t not in kept:
            thick_e = ring.east("h", t, functools.partial(tile, 0))
            wind_e = ring.east("u", t, functools.partial(tile, 5))
            flux = 0.25 * (tile(5, t) + wind_e) * (tile(0, t) + thick_e) * inv_cos
            parts = []
            for k in range(3):
                q = tile(2 + k, t)
                q_e = ring.east(k, t, functools.partial(tile, 2 + k))
                parts.append(DIFFUSION * (q_e - q) - flux * (0.5 * (q + q_e)))
            kept[t] = (flux, thick_e, parts)
        return kept[t]

    for t in range(tiles):
        span = sz.span(t)
        lanes = slice(LANES * t, LANES * t + span)
        flux, thick_e, parts = zonal(t)
        thick, wind_u, wind_v = tile(0, t), tile(5, t), tile(1, t)
        flux_w = ring.west("f", t, lambda s: zonal(s)[0])
        thick_w = ring.west("hw", t, functools.partial(tile, 0))
        thick_n = north(thick)
        flux_n = (0.25 * ratio) * (wind_v + north(wind_v)) * (thick + thick_n) * cos_face
        thick_tend = -((flux - flux_w) + (flux_n - south(flux_n)) * inv_cos)
        wind_u_tend = sin_centre * wind_v - (thick_e - thick_w) * (0.5 * inv_cos)
        wind_v_tend = -sin_centre * wind_u - (0.5 * ratio) * (thick_n - south(thick))
        new_h_ref[:, lanes] = (thick + TIME_STEP * thick_tend)[:rows, :span]
        new_w_ref[0, :, lanes] = (wind_u + TIME_STEP * wind_u_tend)[:rows, :span]
        new_w_ref[1, :, lanes] = (wind_v + TIME_STEP * wind_v_tend)[:rows, :span]
        for k in range(3):
            q = tile(2 + k, t)
            q_n = north(q)
            zonal_part = parts[k] - ring.west(("p", k), t, lambda s: zonal(s)[2][k])
            lap = q_n + south(q) - 2.0 * q
            over = flux_n * (0.5 * (q + q_n))
            merid_part = DIFFUSION * lap - (over - south(over)) * inv_cos
            mass = thick * q + TIME_STEP * (zonal_part + merid_part)
            mass_ref[k, :, lanes] = mass[:rows, :span].astype(jnp.bfloat16)


def sin_pi(y):
    y = jnp.where(y > 0.5, 1.0 - y, jnp.where(y < -0.5, -1.0 - y, y))
    s = y * y
    series = [(-1) ** i * math.pi ** (2 * i + 1) / math.factorial(2 * i + 1) for i in range(7)]
    total = series[-1]
    for factor in reversed(series[:-1]):
        total = total * s + factor
    return total * y


def share_of(sz, i):
    unit = lax.axis_index("lon") * sz.share + i
    row = lax.rem(unit, sz.rows)
    if sz.near_only:
        low = lax.axis_index("lat") < sz.n_lat // 2
        row = jnp.where(low & (unit == sz.pole), 0, row)
        row = jnp.where(low & (unit == 2 * sz.rows), sz.rows - 1, row)
    return unit // sz.rows, row


def swap_ends(sz, ref):
    low = lax.axis_index("lat") < sz.n_lat // 2
    first = slice(2 * sz.rows * sz.stack, (2 * sz.rows + 1) * sz.stack)
    last = slice(sz.pole * sz.stack, sz.units * sz.stack)
    a, b = ref[first], ref[last]
    ref[first] = jnp.where(low, b, a)
    ref[last] = jnp.where(low, a, b)


def weights_kernel(sz, cut_ref, n_ref, inverse_ref, after_ref, weights_ref):
    band = lax.axis_index("lat")
    size = PER_TILE * sz.stack
    for i in range(sz.share):
        width = (2 * cut_ref[band * sz.rows + share_of(sz, i)[1]] + 1).astype(jnp.float32)
        n = n_ref[...]
        turns = n * width
        turns = turns - jnp.round(turns * (0.5 / sz.nlon)) * (2.0 * sz.nlon)
        weights = sin_pi(turns * (1.0 / sz.nlon)) * inverse_ref[...]
        weights = jnp.where(n == 0.0, width * (1.0 / sz.nlon), weights)
        weights_ref[size * i : size * (i + 1)] = weights.astype(jnp.bfloat16)


def filter_kernel(sz, weights_ref, geo_ref, after_ref, *refs):
    n_lon, stack, share = sz.n_lon, sz.stack, sz.share
    in_refs, out_refs, (gathered, results) = refs[:n_lon], refs[n_lon : 2 * n_lon], refs[2 * n_lon :]
    for k, in_ref in enumerate(in_refs):
        gathered[sz.partner(k)] = in_ref[: sz.size]

    band = lax.axis_index("lat")
    lane = lax.broadcasted_iota(jnp.int32, (share, LANES), 1)
    place = lax.broadcasted_iota(jnp.int32, (share, LANES), 0)
    by_flux = by_thick = jnp.zeros((share, LANES), jnp.float32)
    for i in range(share):
        field, row = share_of(sz, i)
        inv_cos = geo_ref[band, 0, pl.ds(row, 1), :]
        by_flux = jnp.where((place == i) & (field == 0), inv_cos, by_flux)
        by_thick = jnp.where((place == i) & (field == 1), 0.5 * inv_cos, by_thick)
    sides = [gathered[s, pl.ds(sz.tiles - 1, share, stride=stack), :] for s in range(n_lon)]

    def column(s, k):
        return pltpu.roll(sides[s % n_lon], (-sz.tail - LEVELS * k) % LANES, 1)

    for s in range(n_lon):
        thick_w, thick_e = column(s, 1), column(s + 1, 0)
        flux = 0.25 * (column(s, 3) + column(s + 1, 2)) * (thick_w + thick_e) * by_flux
        west_of, east_of = flux + by_thick * thick_e, flux + by_thick * thick_w
        at = pl.ds(sz.tiles - 1, share, stride=stack)
        own = gathered[s, at, :]
        own = own - jnp.where(lane >= sz.tail - LEVELS, pltpu.roll(west_of, sz.tail - LEVELS, 1), 0.0)
        gathered[s, at, :] = jnp.where(lane < sz.tail, own, 0.0)
        at = pl.ds(0, share, stride=stack)
        after = (s + 1) % n_lon
        gathered[after, at, :] = gathered[after, at, :] + jnp.where(lane < LEVELS, east_of, 0.0)

    if sz.near_only:
        sign = jnp.where(band == 0, 1.0, jnp.where(band == sz.n_lat - 1, -1.0, 0.0))
        factor = jnp.where(lax.axis_index("lon") == sz.pole // share, 0.5 * sz.ratio * sign, 0.0)
        at = sz.pole % share * stack
        for s in range(n_lon):
            over = gathered[(s + n_lon // 2) % n_lon, at + stack : at + 2 * stack]
            gathered[s, at : at + stack] = gathered[s, at : at + stack] + factor * over

    wide = lax.broadcasted_iota(jnp.int32, (stack, LANES), 1)
    rows = PER_TILE * stack
    for i in range(share):
        here = slice(stack * i, stack * (i + 1))
        pieces = [gathered[s, here].astype(jnp.bfloat16) for s in range(n_lon)]
        circle = jnp.concatenate([jnp.concatenate(pieces[s:] + pieces[:s], axis=0) for s in range(n_lon)], axis=1)
        spread = jnp.dot(weights_ref[rows * i : rows * (i + 1)], circle, preferred_element_type=jnp.float32)
        for s in range(n_lon):
            same = spread[:stack, LANES * s : LANES * (s + 1)]
            carried = None
            for e in range(1, PER_TILE):
                part = spread[stack * e : stack * (e + 1), LANES * s : LANES * (s + 1)]
                part = pltpu.roll(part, LEVELS * e, 1)
                inside = wide >= LEVELS * e
                same = same + jnp.where(inside, part, 0.0)
                over = jnp.where(inside, 0.0, part)
                carried = over if carried is None else carried + over
            results[s, here] = pltpu.roll(same, stack - 1, 0) + carried
    for k, out_ref in enumerate(out_refs):
        out_ref[...] = results[sz.partner(k)]


def finish_kernel(sz, cut_ref, h_ref, w_ref, plain_w_ref, plain_h_ref, *refs):
    back_refs, (new_w_ref, new_h_ref, back_ref) = refs[: sz.n_lon], refs[sz.n_lon :]
    rows = sz.rows
    for k, ref in enumerate(back_refs):
        back_ref[sz.piece(k), :] = ref[...]
    if sz.near_only:
        swap_ends(sz, back_ref)
    row = lax.broadcasted_iota(jnp.int32, (rows, LANES), 0)
    cuts = jnp.zeros((rows, LANES), jnp.int32)
    for j in range(rows):
        cuts = jnp.where(row == j, cut_ref[lax.axis_index("lat") * rows + j], cuts)
    active = cuts < sz.nlon // 2
    for f in range(3):
        for t in range(sz.tiles):
            span = sz.span(t)
            lanes = slice(LANES * t, LANES * t + span)
            tend = back_ref[pl.ds(sz.stack * rows * f + t, rows, stride=sz.stack), :][:, :span]
            if f == 0:
                new = h_ref[:, lanes] + TIME_STEP * tend
                new_h_ref[:, lanes] = jnp.where(active[:, :span], new, plain_h_ref[:, lanes])
            else:
                new = w_ref[f - 1, :, lanes] + TIME_STEP * tend
                new_w_ref[:, f - 1, lanes] = jnp.where(active[:, :span], new, plain_w_ref[f - 1, :, lanes])


def local(winds, thickness, tracers, cutoff):
    n_lat = lax.axis_size("lat")
    n_lon = lax.axis_size("lon")
    rows, merged = thickness.shape
    sz = Sizes(rows, merged, n_lat, n_lon)
    f32 = jnp.float32
    vmem = pl.BlockSpec(memory_space=pltpu.VMEM)
    smem = pl.BlockSpec(memory_space=pltpu.SMEM)
    hbm = pl.BlockSpec(memory_space=pltpu.HBM)
    anywhere = pl.BlockSpec(memory_space=pl.ANY)

    def shaped(*shape):
        return jax.ShapeDtypeStruct(shape, f32)

    def call(kernel, name, in_specs, out_shape, scratch=(), limit=LIMIT):
        return pl.pallas_call(
            functools.partial(kernel, sz),
            out_shape=out_shape,
            in_specs=in_specs,
            out_specs=jax.tree.map(lambda _: vmem, out_shape),
            scratch_shapes=list(scratch),
            compiler_params=pltpu.CompilerParams(vmem_limit_bytes=limit),
            name=name,
        )

    geo = jnp.asarray(geometry(sz))
    n, inverse = (jnp.asarray(table) for table in offsets(sz))

    wind_rows = jnp.swapaxes(winds, 0, 1)
    tracer_rows = jnp.swapaxes(tracers, 0, 1)
    row_pair = shaped(5 * sz.stack, LANES)
    kept = [((1,), f32), ((2,), f32), ((3,), jnp.bfloat16)]
    to_near, to_far, sides = call(
        rows_kernel,
        "rows",
        [hbm] * 3,
        (row_pair, row_pair, shaped(2 * EXT_ROWS, LANES)),
        [pltpu.VMEM((2,) + count + (merged,), dtype) for count, dtype in kept]
        + [
            pltpu.VMEM((rows,) + (count if count != (1,) else ()) + (lanes,), dtype)
            for lanes in (LANES, sz.tail)
            for count, dtype in kept
        ]
        + [pltpu.SemaphoreType.DMA((3, 4))],
        limit=ALL_VMEM,
    )(thickness, wind_rows, tracer_rows)

    near = [(band * n_lon + i, (band ^ 1) * n_lon + i) for band in range(n_lat) for i in range(n_lon)]
    far = []
    for band in range(n_lat):
        other = band - 1 if band % 2 == 0 else band + 1
        for i in range(n_lon):
            if 0 <= other < n_lat:
                far.append((band * n_lon + i, other * n_lon + i))
            else:
                far.append((band * n_lon + i, band * n_lon + (i + n_lon // 2) % n_lon))
    from_near = lax.ppermute(to_near, ("lat", "lon"), near)
    far_rows = to_far if sz.near_only else lax.ppermute(to_far, ("lat", "lon"), far)

    order = [sz.turns(False), sz.turns(True)]

    def meetings(shares):
        got = [shares[0]]
        for k in range(1, n_lon):
            sectors = [(band, i, i ^ order[band % 2][k]) for band in range(n_lat) for i in range(n_lon)]
            got.append(lax.ppermute(shares[k], ("lat", "lon"), [(b * n_lon + i, b * n_lon + j) for b, i, j in sectors]))
        return got

    all_pieces = pltpu.VMEM((n_lon, sz.size, LANES), f32)
    *tends, far_rows = call(
        polar_kernel,
        "polar",
        [vmem] * 6,
        [shaped(sz.size, LANES)] + [shaped(sz.size + EXT_ROWS, LANES)] * (n_lon - 1) + [row_pair],
        [pltpu.VMEM((n_lon * sz.size, LANES), f32), pltpu.VMEM((3, EXT_ROWS, sz.tiles * LANES), f32)],
    )(thickness, winds, from_near, sides, geo, far_rows)
    met = meetings(tends)
    from_far = lax.ppermute(far_rows, ("lat", "lon"), far) if sz.near_only else far_rows
    weights = call(
        weights_kernel,
        "weights",
        [smem, vmem, vmem, anywhere],
        jax.ShapeDtypeStruct((sz.share * PER_TILE * sz.stack, n_lon * sz.stack), jnp.bfloat16),
    )(cutoff, n, inverse, tends[0])
    worked = call(
        filter_kernel,
        "filter",
        [vmem] * 2 + [anywhere] + [vmem] * n_lon,
        [shaped(sz.size, LANES)] * n_lon,
        [all_pieces, all_pieces],
    )(weights, geo, from_far, *met)
    back = meetings(worked)

    plain_w, plain_h, mass = call(
        rest_kernel,
        "rest",
        [vmem] * 6 + [anywhere] + [vmem] * (n_lon - 1),
        (shaped(2, rows, merged), shaped(rows, merged), jax.ShapeDtypeStruct(tracers.shape, jnp.bfloat16)),
        [pltpu.VMEM((6, EXT_ROWS, sz.tiles * LANES), f32)],
    )(thickness, winds, tracers, from_near, from_far, geo, worked[0], *met[1:])

    new_w, new_h = call(
        finish_kernel,
        "finish",
        [smem] + [vmem] * (4 + n_lon),
        (shaped(*wind_rows.shape), shaped(rows, merged)),
        [pltpu.VMEM((n_lon * sz.size, LANES), f32)],
    )(cutoff, thickness, winds, plain_w, plain_h, *back)
    return jnp.swapaxes(new_w, 0, 1), new_h, mass


def solution(mesh):
    in_specs = (P(None, "lat", "lon"), P("lat", "lon"), P(None, "lat", "lon"), P())
    out_specs = (P(None, "lat", "lon"), P("lat", "lon"), P(None, "lat", "lon"))
    return jax.shard_map(local, mesh=mesh, in_specs=in_specs, out_specs=out_specs, check_vma=False)
```

```python
import functools
import math

import jax
import jax.numpy as jnp
import numpy as np
from jax import lax
from jax.experimental import pallas as pl
from jax.experimental.pallas import tpu as pltpu
from jax.sharding import PartitionSpec as P

LEVELS = 16
TIME_STEP = 0.05
DIFFUSION = 0.5
LANES = 128
PER_TILE = LANES // LEVELS
EXT_ROWS = 16
LIMIT = 48 * 1024 * 1024
MOST_VMEM = 64 * 1024 * 1024 - 10500 * 1024


class Sizes:
    def __init__(self, rows, merged, n_lat, n_lon):
        self.rows = rows
        self.merged = merged
        self.columns = merged // LEVELS
        self.n_lat = n_lat
        self.n_lon = n_lon
        self.nlat = rows * n_lat
        self.nlon = self.columns * n_lon
        self.ratio = 2.0 * self.nlat / self.nlon
        self.tiles = -(-merged // LANES)
        self.end = (self.tiles - 1) * LANES
        self.tail = merged - self.end
        self.stack = -(-(self.tiles + 1) // 8) * 8
        self.units = 3 * rows
        self.share = -(-self.units // n_lon)
        self.size = self.share * self.stack
        self.pole = self.units - 1
        self.near_only = self.nlat // 6 < 2 * rows and self.units % self.share > 0
        assert self.tail <= LANES - 4 * LEVELS and rows + 2 <= EXT_ROWS and n_lat % 2 == 0
        assert n_lon >= 4 and n_lon & (n_lon - 1) == 0

    def span(self, tile):
        return self.tail if tile == self.tiles - 1 else LANES

    def turns(self, odd):
        middle = list(range(1, self.n_lon - 1))
        return [0, self.n_lon - 1] + (middle[::-1] if odd else middle)

    def partner(self, k):
        odd = lax.rem(lax.axis_index("lat"), 2) == 1
        turn = jnp.where(odd, self.turns(True)[k], self.turns(False)[k])
        return jnp.bitwise_xor(lax.axis_index("lon"), turn)

    def piece(self, k):
        return pl.ds(pl.multiple_of(self.partner(k) * self.size, 8), self.size)


def geometry(sz):
    table = np.zeros((sz.n_lat, 3, EXT_ROWS, LANES), np.float64)

    def face(j):
        return math.sin((j + 1) * math.pi / sz.nlat) if 0 <= j < sz.nlat - 1 else 0.0

    for band in range(sz.n_lat):
        for row in range(sz.rows):
            j = band * sz.rows + row
            centre = (j + 0.5) * math.pi / sz.nlat - math.pi / 2
            table[band, 0, row] = 1.0 / math.cos(centre)
            table[band, 1, row] = math.sin(centre)
            table[band, 2, row] = face(j)
        table[band, 2, EXT_ROWS - 1] = face(band * sz.rows - 1)
    return table.astype(np.float32)


def offsets(sz):
    shift, out_tile = np.divmod(np.arange(PER_TILE * sz.stack), sz.stack)
    sector, in_tile = np.divmod(np.arange(sz.n_lon * sz.stack), sz.stack)
    n = (PER_TILE * (out_tile - 1) + shift)[:, None] - (PER_TILE * in_tile + sz.columns * sector)[None, :]
    n = (n + sz.nlon // 2) % sz.nlon - sz.nlon // 2
    with np.errstate(divide="ignore"):
        inverse = np.where(n == 0, 0.0, 1.0 / (sz.nlon * np.sin(np.pi * n / sz.nlon)))
    return n.astype(np.float32), inverse.astype(np.float32)


def edges_kernel(sz, h_hbm, w_hbm, q_hbm, near_ref, far_ref, sides_ref, *scratch):
    row_refs, first_refs, last_refs, sems = scratch[:3], scratch[3:6], scratch[6:9], scratch[9]
    rows, last = sz.rows, sz.rows - 1
    even = lax.rem(lax.axis_index("lat"), 2) == 0
    copies = []
    for i, source in enumerate((h_hbm, w_hbm, q_hbm)):
        for k, row in enumerate((0, last)):
            one = source.at[pl.ds(row, 1)] if i == 0 else source.at[row]
            copies.append(pltpu.make_async_copy(one, row_refs[i].at[k], sems.at[i, k]))
        for k, (start, to) in enumerate(((0, first_refs[i]), (sz.end, last_refs[i]))):
            lanes = pl.ds(start, to.shape[-1])
            cut = source.at[:, lanes] if i == 0 else source.at[:, :, lanes]
            copies.append(pltpu.make_async_copy(cut, to, sems.at[i, 2 + k]))
    for copy in copies:
        copy.start()
    for copy in copies:
        copy.wait()
    h_rows, w_rows, q_rows = row_refs
    for t in range(sz.tiles):
        wide = sz.span(t)
        lanes = slice(LANES * t, LANES * t + wide)
        q = [q_rows[k, :, lanes].astype(jnp.float32) for k in range(2)]
        for f in range(5):
            if f == 0:
                first, final = h_rows[0, :, lanes], h_rows[1, :, lanes]
            elif f == 1:
                first, final = w_rows[0, 1:2, lanes], w_rows[1, 1:2, lanes]
            else:
                first, final = q[0][f - 2 : f - 1], q[1][f - 2 : f - 1]
                at = sz.stack * (f - 2) + t
                near_ref[at : at + 1, :wide] = jnp.where(even, final, first)
            at = sz.stack * f + t
            far_ref[at : at + 1, :wide] = jnp.where(even, first, final)
    sides_ref[...] = jnp.zeros(sides_ref.shape, jnp.float32)
    for k, (refs, at) in enumerate(((first_refs, 0), (last_refs, sz.tail - LEVELS))):
        columns = slice(at, at + LEVELS)
        for f in range(5):
            if f == 0:
                value = refs[0][:, columns]
            elif f == 1:
                value = refs[1][:, 0, columns]
            else:
                value = refs[2][:, f - 2, columns].astype(jnp.float32)
            sides_ref[EXT_ROWS * k : EXT_ROWS * k + rows, LEVELS * f : LEVELS * (f + 1)] = value


def add_rows(sz, ext, near_h_ref, near_w_ref, near_q_ref, far_ref):
    band = lax.axis_index("lat")
    even = lax.rem(band, 2) == 0
    over_pole = (band == 0) | (band == sz.n_lat - 1)
    last = sz.rows - 1
    for f in range(2 if near_q_ref is None else 5):
        flip = jnp.where(over_pole, -1.0, 1.0) if f == 1 else 1.0
        for t in range(sz.tiles):
            lanes = slice(LANES * t, LANES * t + sz.span(t))
            if f == 0:
                near = jnp.where(even, near_h_ref[0:1, lanes], near_h_ref[last : sz.rows, lanes])
            elif f == 1:
                near = jnp.where(even, near_w_ref[0, 1:2, lanes], near_w_ref[last, 1:2, lanes])
            else:
                at = sz.stack * (f - 2) + t
                near = near_q_ref[at : at + 1, : sz.span(t)]
            at = sz.stack * f + t
            far = jnp.zeros_like(near) if far_ref is None else far_ref[at : at + 1, : sz.span(t)] * flip
            ext[f, sz.rows : sz.rows + 1, lanes] = jnp.where(even, near, far)
            ext[f, EXT_ROWS - 1 : EXT_ROWS, lanes] = jnp.where(even, far, near)


class Tiles:
    def __init__(self, sz):
        self.sz = sz
        self.lane = lax.broadcasted_iota(jnp.int32, (EXT_ROWS, LANES), 1)
        self.turned = {}

    def turn(self, name, t, value, step):
        key = (name, t % self.sz.tiles, step)
        if key not in self.turned:
            self.turned[key] = pltpu.roll(value(t % self.sz.tiles), step % LANES, 1)
        return self.turned[key]

    def east(self, name, t, value):
        here = self.turn(name, t, value, -LEVELS)
        return jnp.where(self.lane < LANES - LEVELS, here, self.turn(name, t + 1, value, -LEVELS))

    def west(self, name, t, value):
        here = self.turn(name, t, value, LEVELS)
        return jnp.where(self.lane >= LEVELS, here, self.turn(name, t - 1, value, LEVELS))


def north(value):
    return pltpu.roll(value, EXT_ROWS - 1, 0)


def south(value):
    return pltpu.roll(value, 1, 0)


def polar_kernel(sz, h_ref, w_ref, near_h_ref, near_w_ref, sides_ref, geo_ref, far_ref, near_q_ref, *refs):
    out_refs, (far_out, near_out, tend_ref, ext) = refs[:-4], refs[-4:]
    far_out[...] = far_ref[...]
    near_out[...] = near_q_ref[...]
    if sz.near_only:
        far_ref = None
    band = lax.axis_index("lat")
    ring = Tiles(sz)
    lane = ring.lane
    tiles, stack, rows = sz.tiles, sz.stack, sz.rows
    for f, value in enumerate((h_ref[...], w_ref[:, 1, :], w_ref[:, 0, :])):
        ext[f, :rows, sz.end :] = jnp.zeros((rows, LANES), jnp.float32)
        ext[f, :rows, : sz.merged] = value
    add_rows(sz, ext, near_h_ref, near_w_ref, None, far_ref)
    inv_cos, sin_centre, cos_face = geo_ref[band, 0], geo_ref[band, 1], geo_ref[band, 2]
    ratio = sz.ratio

    def tile(f, t):
        return ext[f, :, LANES * t : LANES * (t + 1)]

    kept = {}

    def zonal(t):
        if t not in kept:
            thick_e = ring.east("h", t, functools.partial(tile, 0))
            wind_e = ring.east("u", t, functools.partial(tile, 2))
            flux = 0.25 * (tile(2, t) + wind_e) * (tile(0, t) + thick_e) * inv_cos
            if t == tiles - 1:
                flux = jnp.where(lane < sz.tail - LEVELS, flux, 0.0)
            kept[t] = (flux, thick_e)
        return kept[t]

    for t in range(tiles):
        flux, thick_e = zonal(t)
        thick, wind_v, wind_u = tile(0, t), tile(1, t), tile(2, t)
        flux_w = ring.west("f", t, lambda s: zonal(s)[0])
        thick_w = ring.west("hw", t, functools.partial(tile, 0))
        thick_n = north(thick)
        flux_n = (0.25 * ratio) * (wind_v + north(wind_v)) * (thick + thick_n) * cos_face
        thick_tend = -((flux - flux_w) + (flux_n - south(flux_n)) * inv_cos)
        wind_u_tend = sin_centre * wind_v - (thick_e - thick_w) * (0.5 * inv_cos)
        wind_v_tend = -sin_centre * wind_u - (0.5 * ratio) * (thick_n - south(thick))
        spare = 0.0
        if t == tiles - 1:
            last = sz.tail - LEVELS
            columns = [(tile(0, 0), 0), (thick, last), (tile(2, 0), 0), (wind_u, last)]
            for k, (source, at) in reversed(list(enumerate(columns))):
                to = sz.tail + LEVELS * k
                spare = jnp.where(lane < to + LEVELS, pltpu.roll(source, (to - at) % LANES, 1), spare)
        for f, tend in enumerate((thick_tend, wind_u_tend, wind_v_tend)):
            if t == tiles - 1:
                tend = jnp.where(lane < sz.tail, tend, spare)
            tend_ref[pl.ds(stack * rows * f + t, rows, stride=stack), :] = tend[:rows]
    for f in range(3):
        for t in range(tiles, stack):
            tend_ref[pl.ds(stack * rows * f + t, rows, stride=stack), :] = jnp.zeros((rows, LANES), jnp.float32)
    used = stack * sz.units
    if used < tend_ref.shape[0]:
        tend_ref[used:, :] = jnp.zeros((tend_ref.shape[0] - used, LANES), jnp.float32)
    if sz.near_only:
        swap_ends(sz, tend_ref)
        for t in range(tiles):
            lanes = slice(LANES * t, LANES * (t + 1))
            row = jnp.where(band < sz.n_lat // 2, ext[0, 0:1, lanes], ext[0, rows - 1 : rows, lanes])
            tend_ref[used + t : used + t + 1, :] = row
    here = lax.axis_index("lon")
    for k, out_ref in enumerate(out_refs):
        out_ref[: sz.size] = tend_ref[sz.piece(k), :]
        if k:
            eastward = sz.partner(k) == lax.rem(here + 1, sz.n_lon)
            out_ref[sz.size :] = jnp.where(eastward, sides_ref[EXT_ROWS:], sides_ref[:EXT_ROWS])


def rest_kernel(sz, h_ref, w_ref, q_ref, near_h_ref, near_w_ref, near_q_ref, far_ref, geo_ref, after_ref, *refs):
    met_refs, (new_w_ref, new_h_ref, mass_ref, ext) = refs[: sz.n_lon - 1], refs[sz.n_lon - 1 :]
    band = lax.axis_index("lat")
    ring = Tiles(sz)
    lane = ring.lane
    tiles, rows = sz.tiles, sz.rows
    for f in range(6):
        if f < 2 or f == 5:
            value = (h_ref[...], w_ref[:, 1, :], w_ref[:, 0, :])[min(f, 2)]
        else:
            value = q_ref[f - 2].astype(jnp.float32)
        ext[f, :rows, : sz.merged] = value
    add_rows(sz, ext, near_h_ref, near_w_ref, near_q_ref, far_ref)
    lane9 = lane[:rows]
    here = lax.axis_index("lon")
    from_e = from_w = met_refs[0][sz.size :]
    for k, met_ref in enumerate(met_refs[1:], 2):
        from_e = jnp.where(sz.partner(k) == lax.rem(here + 1, sz.n_lon), met_ref[sz.size :], from_e)
        from_w = jnp.where(sz.partner(k) == lax.rem(here + sz.n_lon - 1, sz.n_lon), met_ref[sz.size :], from_w)
    for place, f in enumerate((0, 5, 2, 3, 4)):
        after = pltpu.roll(from_e, (sz.tail - LEVELS * place) % LANES, 1)[:rows]
        before = pltpu.roll(from_w, (LANES - LEVELS - LEVELS * place) % LANES, 1)[:rows]
        own = ext[f, :rows, sz.end :]
        edge = jnp.where(lane9 < LANES - LEVELS, after, before)
        ext[f, :rows, sz.end :] = jnp.where(lane9 < sz.tail, own, edge)
    inv_cos, sin_centre, cos_face = geo_ref[band, 0], geo_ref[band, 1], geo_ref[band, 2]
    ratio = sz.ratio

    def tile(f, t):
        return ext[f, :, LANES * t : LANES * (t + 1)]

    kept = {}

    def zonal(t):
        if t not in kept:
            thick_e = ring.east("h", t, functools.partial(tile, 0))
            wind_e = ring.east("u", t, functools.partial(tile, 5))
            flux = 0.25 * (tile(5, t) + wind_e) * (tile(0, t) + thick_e) * inv_cos
            parts = []
            for k in range(3):
                q = tile(2 + k, t)
                q_e = ring.east(k, t, functools.partial(tile, 2 + k))
                parts.append(DIFFUSION * (q_e - q) - flux * (0.5 * (q + q_e)))
            kept[t] = (flux, thick_e, parts)
        return kept[t]

    for t in range(tiles):
        span = sz.span(t)
        lanes = slice(LANES * t, LANES * t + span)
        flux, thick_e, parts = zonal(t)
        thick, wind_u, wind_v = tile(0, t), tile(5, t), tile(1, t)
        flux_w = ring.west("f", t, lambda s: zonal(s)[0])
        thick_w = ring.west("hw", t, functools.partial(tile, 0))
        thick_n = north(thick)
        flux_n = (0.25 * ratio) * (wind_v + north(wind_v)) * (thick + thick_n) * cos_face
        thick_tend = -((flux - flux_w) + (flux_n - south(flux_n)) * inv_cos)
        wind_u_tend = sin_centre * wind_v - (thick_e - thick_w) * (0.5 * inv_cos)
        wind_v_tend = -sin_centre * wind_u - (0.5 * ratio) * (thick_n - south(thick))
        new_h_ref[:, lanes] = (thick + TIME_STEP * thick_tend)[:rows, :span]
        new_w_ref[0, :, lanes] = (wind_u + TIME_STEP * wind_u_tend)[:rows, :span]
        new_w_ref[1, :, lanes] = (wind_v + TIME_STEP * wind_v_tend)[:rows, :span]
        for k in range(3):
            q = tile(2 + k, t)
            q_n = north(q)
            zonal_part = parts[k] - ring.west(("p", k), t, lambda s: zonal(s)[2][k])
            lap = q_n + south(q) - 2.0 * q
            over = flux_n * (0.5 * (q + q_n))
            merid_part = DIFFUSION * lap - (over - south(over)) * inv_cos
            mass = thick * q + TIME_STEP * (zonal_part + merid_part)
            mass_ref[k, :, lanes] = mass[:rows, :span].astype(jnp.bfloat16)


def sin_pi(y):
    y = jnp.where(y > 0.5, 1.0 - y, jnp.where(y < -0.5, -1.0 - y, y))
    s = y * y
    series = [(-1) ** i * math.pi ** (2 * i + 1) / math.factorial(2 * i + 1) for i in range(7)]
    total = series[-1]
    for factor in reversed(series[:-1]):
        total = total * s + factor
    return total * y


def share_of(sz, i):
    unit = lax.axis_index("lon") * sz.share + i
    row = lax.rem(unit, sz.rows)
    if sz.near_only:
        low = lax.axis_index("lat") < sz.n_lat // 2
        row = jnp.where(low & (unit == sz.pole), 0, row)
        row = jnp.where(low & (unit == 2 * sz.rows), sz.rows - 1, row)
    return unit // sz.rows, row


def swap_ends(sz, ref):
    low = lax.axis_index("lat") < sz.n_lat // 2
    first = slice(2 * sz.rows * sz.stack, (2 * sz.rows + 1) * sz.stack)
    last = slice(sz.pole * sz.stack, sz.units * sz.stack)
    a, b = ref[first], ref[last]
    ref[first] = jnp.where(low, b, a)
    ref[last] = jnp.where(low, a, b)


def weights_kernel(sz, cut_ref, n_ref, inverse_ref, after_ref, weights_ref):
    band = lax.axis_index("lat")
    size = PER_TILE * sz.stack
    for i in range(sz.share):
        width = (2 * cut_ref[band * sz.rows + share_of(sz, i)[1]] + 1).astype(jnp.float32)
        n = n_ref[...]
        turns = n * width
        turns = turns - jnp.round(turns * (0.5 / sz.nlon)) * (2.0 * sz.nlon)
        weights = sin_pi(turns * (1.0 / sz.nlon)) * inverse_ref[...]
        weights = jnp.where(n == 0.0, width * (1.0 / sz.nlon), weights)
        weights_ref[size * i : size * (i + 1)] = weights.astype(jnp.bfloat16)


def filter_kernel(sz, weights_ref, geo_ref, after_ref, also_after_ref, *refs):
    n_lon, stack, share = sz.n_lon, sz.stack, sz.share
    in_refs, out_refs, (gathered, results) = refs[:n_lon], refs[n_lon : 2 * n_lon], refs[2 * n_lon :]
    for k, in_ref in enumerate(in_refs):
        gathered[sz.partner(k)] = in_ref[: sz.size]

    band = lax.axis_index("lat")
    lane = lax.broadcasted_iota(jnp.int32, (share, LANES), 1)
    place = lax.broadcasted_iota(jnp.int32, (share, LANES), 0)
    by_flux = by_thick = jnp.zeros((share, LANES), jnp.float32)
    for i in range(share):
        field, row = share_of(sz, i)
        inv_cos = geo_ref[band, 0, pl.ds(row, 1), :]
        by_flux = jnp.where((place == i) & (field == 0), inv_cos, by_flux)
        by_thick = jnp.where((place == i) & (field == 1), 0.5 * inv_cos, by_thick)
    sides = [gathered[s, pl.ds(sz.tiles - 1, share, stride=stack), :] for s in range(n_lon)]

    def column(s, k):
        return pltpu.roll(sides[s % n_lon], (-sz.tail - LEVELS * k) % LANES, 1)

    for s in range(n_lon):
        thick_w, thick_e = column(s, 1), column(s + 1, 0)
        flux = 0.25 * (column(s, 3) + column(s + 1, 2)) * (thick_w + thick_e) * by_flux
        west_of, east_of = flux + by_thick * thick_e, flux + by_thick * thick_w
        at = pl.ds(sz.tiles - 1, share, stride=stack)
        own = gathered[s, at, :]
        own = own - jnp.where(lane >= sz.tail - LEVELS, pltpu.roll(west_of, sz.tail - LEVELS, 1), 0.0)
        gathered[s, at, :] = jnp.where(lane < sz.tail, own, 0.0)
        at = pl.ds(0, share, stride=stack)
        after = (s + 1) % n_lon
        gathered[after, at, :] = gathered[after, at, :] + jnp.where(lane < LEVELS, east_of, 0.0)

    if sz.near_only:
        sign = jnp.where(band == 0, 1.0, jnp.where(band == sz.n_lat - 1, -1.0, 0.0))
        factor = jnp.where(lax.axis_index("lon") == sz.pole // share, 0.5 * sz.ratio * sign, 0.0)
        at = sz.pole % share * stack
        for s in range(n_lon):
            over = gathered[(s + n_lon // 2) % n_lon, at + stack : at + 2 * stack]
            gathered[s, at : at + stack] = gathered[s, at : at + stack] + factor * over

    wide = lax.broadcasted_iota(jnp.int32, (stack, LANES), 1)
    rows = PER_TILE * stack
    for i in range(share):
        here = slice(stack * i, stack * (i + 1))
        pieces = [gathered[s, here].astype(jnp.bfloat16) for s in range(n_lon)]
        circle = jnp.concatenate([jnp.concatenate(pieces[s:] + pieces[:s], axis=0) for s in range(n_lon)], axis=1)
        spread = jnp.dot(weights_ref[rows * i : rows * (i + 1)], circle, preferred_element_type=jnp.float32)
        for s in range(n_lon):
            same = spread[:stack, LANES * s : LANES * (s + 1)]
            carried = None
            for e in range(1, PER_TILE):
                part = spread[stack * e : stack * (e + 1), LANES * s : LANES * (s + 1)]
                part = pltpu.roll(part, LEVELS * e, 1)
                inside = wide >= LEVELS * e
                same = same + jnp.where(inside, part, 0.0)
                over = jnp.where(inside, 0.0, part)
                carried = over if carried is None else carried + over
            results[s, here] = pltpu.roll(same, stack - 1, 0) + carried
    for k, out_ref in enumerate(out_refs):
        out_ref[...] = results[sz.partner(k)]


def finish_kernel(sz, cut_ref, h_ref, w_ref, plain_w_ref, plain_h_ref, *refs):
    back_refs, (new_w_ref, new_h_ref, back_ref) = refs[: sz.n_lon], refs[sz.n_lon :]
    rows = sz.rows
    for k, ref in enumerate(back_refs):
        back_ref[sz.piece(k), :] = ref[...]
    if sz.near_only:
        swap_ends(sz, back_ref)
    row = lax.broadcasted_iota(jnp.int32, (rows, LANES), 0)
    cuts = jnp.zeros((rows, LANES), jnp.int32)
    for j in range(rows):
        cuts = jnp.where(row == j, cut_ref[lax.axis_index("lat") * rows + j], cuts)
    active = cuts < sz.nlon // 2
    for f in range(3):
        for t in range(sz.tiles):
            span = sz.span(t)
            lanes = slice(LANES * t, LANES * t + span)
            tend = back_ref[pl.ds(sz.stack * rows * f + t, rows, stride=sz.stack), :][:, :span]
            if f == 0:
                new = h_ref[:, lanes] + TIME_STEP * tend
                new_h_ref[:, lanes] = jnp.where(active[:, :span], new, plain_h_ref[:, lanes])
            else:
                new = w_ref[:, f - 1, lanes] + TIME_STEP * tend
                new_w_ref[:, f - 1, lanes] = jnp.where(active[:, :span], new, plain_w_ref[f - 1, :, lanes])


def local(winds, thickness, tracers, cutoff):
    n_lat = lax.axis_size("lat")
    n_lon = lax.axis_size("lon")
    rows, merged = thickness.shape
    sz = Sizes(rows, merged, n_lat, n_lon)
    f32 = jnp.float32
    vmem = pl.BlockSpec(memory_space=pltpu.VMEM)
    smem = pl.BlockSpec(memory_space=pltpu.SMEM)
    hbm = pl.BlockSpec(memory_space=pltpu.HBM)
    anywhere = pl.BlockSpec(memory_space=pl.ANY)

    def shaped(*shape):
        return jax.ShapeDtypeStruct(shape, f32)

    def call(kernel, name, in_specs, out_shape, scratch=(), limit=LIMIT):
        return pl.pallas_call(
            functools.partial(kernel, sz),
            out_shape=out_shape,
            in_specs=in_specs,
            out_specs=jax.tree.map(lambda _: vmem, out_shape),
            scratch_shapes=list(scratch),
            compiler_params=pltpu.CompilerParams(vmem_limit_bytes=limit),
            name=name,
        )

    geo = jnp.asarray(geometry(sz))
    n, inverse = (jnp.asarray(table) for table in offsets(sz))

    wind_rows = jnp.swapaxes(winds, 0, 1)
    tracer_rows = jnp.swapaxes(tracers, 0, 1)
    far_row, near_row = shaped(5 * sz.stack, LANES), shaped(3 * sz.stack, LANES)
    kept = [((1,), f32), ((2,), f32), ((3,), jnp.bfloat16)]
    near_q, far_rows, sides = call(
        edges_kernel,
        "edges",
        [hbm] * 3,
        (near_row, far_row, shaped(2 * EXT_ROWS, LANES)),
        [pltpu.VMEM((2,) + count + (merged,), dtype) for count, dtype in kept]
        + [
            pltpu.VMEM((rows,) + (count if count != (1,) else ()) + (lanes,), dtype)
            for lanes in (LANES, sz.tail)
            for count, dtype in kept
        ]
        + [pltpu.SemaphoreType.DMA((3, 4))],
        limit=MOST_VMEM,
    )(thickness, wind_rows, tracer_rows)

    near = [(band * n_lon + i, (band ^ 1) * n_lon + i) for band in range(n_lat) for i in range(n_lon)]
    far = []
    for band in range(n_lat):
        other = band - 1 if band % 2 == 0 else band + 1
        for i in range(n_lon):
            if 0 <= other < n_lat:
                far.append((band * n_lon + i, other * n_lon + i))
            else:
                far.append((band * n_lon + i, band * n_lon + (i + n_lon // 2) % n_lon))
    near_h = lax.ppermute(thickness, ("lat", "lon"), near)
    near_w = lax.ppermute(wind_rows, ("lat", "lon"), near)
    if not sz.near_only:
        far_rows = lax.ppermute(far_rows, ("lat", "lon"), far)

    order = [sz.turns(False), sz.turns(True)]

    def meetings(shares):
        got = [shares[0]]
        for k in range(1, n_lon):
            sectors = [(band, i, i ^ order[band % 2][k]) for band in range(n_lat) for i in range(n_lon)]
            got.append(lax.ppermute(shares[k], ("lat", "lon"), [(b * n_lon + i, b * n_lon + j) for b, i, j in sectors]))
        return got

    all_pieces = pltpu.VMEM((n_lon, sz.size, LANES), f32)
    *tends, far_rows, near_q = call(
        polar_kernel,
        "polar",
        [vmem] * 8,
        [shaped(sz.size, LANES)] + [shaped(sz.size + EXT_ROWS, LANES)] * (n_lon - 1) + [far_row, near_row],
        [pltpu.VMEM((n_lon * sz.size, LANES), f32), pltpu.VMEM((3, EXT_ROWS, sz.tiles * LANES), f32)],
    )(thickness, wind_rows, near_h, near_w, sides, geo, far_rows, near_q)
    met = meetings(tends)
    near_q = lax.ppermute(near_q, ("lat", "lon"), near)
    from_far = lax.ppermute(far_rows, ("lat", "lon"), far) if sz.near_only else far_rows
    weights = call(
        weights_kernel,
        "weights",
        [smem, vmem, vmem, anywhere],
        jax.ShapeDtypeStruct((sz.share * PER_TILE * sz.stack, n_lon * sz.stack), jnp.bfloat16),
    )(cutoff, n, inverse, tends[0])
    worked = call(
        filter_kernel,
        "filter",
        [vmem] * 2 + [anywhere] * 2 + [vmem] * n_lon,
        [shaped(sz.size, LANES)] * n_lon,
        [all_pieces, all_pieces],
    )(weights, geo, from_far, near_q, *met)
    back = meetings(worked)

    plain_w, plain_h, mass = call(
        rest_kernel,
        "rest",
        [vmem] * 8 + [anywhere] + [vmem] * (n_lon - 1),
        (shaped(2, rows, merged), shaped(rows, merged), jax.ShapeDtypeStruct(tracers.shape, jnp.bfloat16)),
        [pltpu.VMEM((6, EXT_ROWS, sz.tiles * LANES), f32)],
    )(thickness, wind_rows, tracers, near_h, near_w, near_q, from_far, geo, worked[0], *met[1:])

    new_w, new_h = call(
        finish_kernel,
        "finish",
        [smem] + [vmem] * (4 + n_lon),
        (shaped(*wind_rows.shape), shaped(rows, merged)),
        [pltpu.VMEM((n_lon * sz.size, LANES), f32)],
    )(cutoff, thickness, wind_rows, plain_w, plain_h, *back)
    return jnp.swapaxes(new_w, 0, 1), new_h, mass


def solution(mesh):
    in_specs = (P(None, "lat", "lon"), P("lat", "lon"), P(None, "lat", "lon"), P())
    out_specs = (P(None, "lat", "lon"), P("lat", "lon"), P(None, "lat", "lon"))
    return jax.shard_map(local, mesh=mesh, in_specs=in_specs, out_specs=out_specs, check_vma=False)
```

```python
import functools
import math

import jax
import jax.numpy as jnp
import numpy as np
from jax import lax
from jax.experimental import pallas as pl
from jax.experimental.pallas import tpu as pltpu
from jax.sharding import PartitionSpec as P

LEVELS = 16
TIME_STEP = 0.05
DIFFUSION = 0.5
LANES = 128
PER_TILE = LANES // LEVELS
EXT_ROWS = 16
LIMIT = 48 * 1024 * 1024
MOST_VMEM = 64 * 1024 * 1024 - 10500 * 1024


class Sizes:
    def __init__(self, rows, merged, n_lat, n_lon):
        self.rows = rows
        self.merged = merged
        self.columns = merged // LEVELS
        self.n_lat = n_lat
        self.n_lon = n_lon
        self.nlat = rows * n_lat
        self.nlon = self.columns * n_lon
        self.ratio = 2.0 * self.nlat / self.nlon
        self.tiles = -(-merged // LANES)
        self.end = (self.tiles - 1) * LANES
        self.tail = merged - self.end
        self.stack = -(-(self.tiles + 1) // 8) * 8
        self.near_only = rows <= self.nlat // 6 < 2 * rows
        self.work = rows - 1 if self.near_only else rows
        self.units = 3 * self.work
        self.share = -(-self.units // n_lon)
        self.size = self.share * self.stack
        assert self.tail <= LANES - 4 * LEVELS and rows + 2 <= EXT_ROWS and n_lat % 2 == 0
        assert n_lon >= 4 and n_lon & (n_lon - 1) == 0

    def span(self, tile):
        return self.tail if tile == self.tiles - 1 else LANES

    def first(self):
        return jnp.where(lax.rem(lax.axis_index("lat"), 2) == 0, 1, 0) if self.near_only else 0

    def at_pole(self, row):
        band = lax.axis_index("lat")
        south, north = (row == 0) & (band == 0), (row == self.rows - 1) & (band == self.n_lat - 1)
        return (south | north) & self.near_only

    def active(self, cut_ref, shape):
        row = lax.broadcasted_iota(jnp.int32, shape, 0)
        cuts = jnp.full(shape, self.nlon // 2, jnp.int32)
        for j in range(self.rows):
            cuts = jnp.where(row == j, cut_ref[lax.axis_index("lat") * self.rows + j], cuts)
        return cuts < self.nlon // 2, self.at_pole(row)

    def turns(self, odd):
        middle = list(range(1, self.n_lon - 1))
        return [0, self.n_lon - 1] + (middle[::-1] if odd else middle)

    def partner(self, k):
        odd = lax.rem(lax.axis_index("lat"), 2) == 1
        turn = jnp.where(odd, self.turns(True)[k], self.turns(False)[k])
        return jnp.bitwise_xor(lax.axis_index("lon"), turn)

    def piece(self, k):
        return pl.ds(pl.multiple_of(self.partner(k) * self.size, 8), self.size)


def geometry(sz):
    table = np.zeros((sz.n_lat, 3, EXT_ROWS, LANES), np.float64)

    def face(j):
        return math.sin((j + 1) * math.pi / sz.nlat) if 0 <= j < sz.nlat - 1 else 0.0

    for band in range(sz.n_lat):
        for row in range(sz.rows):
            j = band * sz.rows + row
            centre = (j + 0.5) * math.pi / sz.nlat - math.pi / 2
            table[band, 0, row] = 1.0 / math.cos(centre)
            table[band, 1, row] = math.sin(centre)
            table[band, 2, row] = face(j)
        table[band, 2, EXT_ROWS - 1] = face(band * sz.rows - 1)
    return table.astype(np.float32)


def offsets(sz):
    shift, out_tile = np.divmod(np.arange(PER_TILE * sz.stack), sz.stack)
    sector, in_tile = np.divmod(np.arange(sz.n_lon * sz.stack), sz.stack)
    n = (PER_TILE * (out_tile - 1) + shift)[:, None] - (PER_TILE * in_tile + sz.columns * sector)[None, :]
    n = (n + sz.nlon // 2) % sz.nlon - sz.nlon // 2
    with np.errstate(divide="ignore"):
        inverse = np.where(n == 0, 0.0, 1.0 / (sz.nlon * np.sin(np.pi * n / sz.nlon)))
    return n.astype(np.float32), inverse.astype(np.float32)


def waves(sz):
    column = PER_TILE * np.arange(sz.stack)[:, None] + np.arange(LANES)[None, :] // LEVELS
    angle = 2 * np.pi * column / sz.nlon
    return np.stack([np.cos(angle), np.sin(angle)]).astype(np.float32)


def edges_kernel(sz, h_hbm, w_hbm, q_hbm, near_ref, far_ref, sides_ref, *scratch):
    row_refs, first_refs, last_refs, sems = scratch[:3], scratch[3:6], scratch[6:9], scratch[9]
    rows, last = sz.rows, sz.rows - 1
    even = lax.rem(lax.axis_index("lat"), 2) == 0
    copies = []
    for i, source in enumerate((h_hbm, w_hbm, q_hbm)):
        for k, row in enumerate((0, last)):
            one = source.at[pl.ds(row, 1)] if i == 0 else source.at[row]
            copies.append(pltpu.make_async_copy(one, row_refs[i].at[k], sems.at[i, k]))
        for k, (start, to) in enumerate(((0, first_refs[i]), (sz.end, last_refs[i]))):
            lanes = pl.ds(start, to.shape[-1])
            cut = source.at[:, lanes] if i == 0 else source.at[:, :, lanes]
            copies.append(pltpu.make_async_copy(cut, to, sems.at[i, 2 + k]))
    for copy in copies:
        copy.start()
    for copy in copies:
        copy.wait()
    h_rows, w_rows, q_rows = row_refs
    for t in range(sz.tiles):
        wide = sz.span(t)
        lanes = slice(LANES * t, LANES * t + wide)
        q = [q_rows[k, :, lanes].astype(jnp.float32) for k in range(2)]
        for f in range(5):
            if f == 0:
                first, final = h_rows[0, :, lanes], h_rows[1, :, lanes]
            elif f == 1:
                first, final = w_rows[0, 1:2, lanes], w_rows[1, 1:2, lanes]
            else:
                first, final = q[0][f - 2 : f - 1], q[1][f - 2 : f - 1]
                at = sz.stack * (f - 2) + t
                near_ref[at : at + 1, :wide] = jnp.where(even, final, first)
            at = sz.stack * f + t
            far_ref[at : at + 1, :wide] = jnp.where(even, first, final)
    sides_ref[...] = jnp.zeros(sides_ref.shape, jnp.float32)
    for k, (refs, at) in enumerate(((first_refs, 0), (last_refs, sz.tail - LEVELS))):
        columns = slice(at, at + LEVELS)
        for f in range(5):
            if f == 0:
                value = refs[0][:, columns]
            elif f == 1:
                value = refs[1][:, 0, columns]
            else:
                value = refs[2][:, f - 2, columns].astype(jnp.float32)
            sides_ref[EXT_ROWS * k : EXT_ROWS * k + rows, LEVELS * f : LEVELS * (f + 1)] = value


def add_rows(sz, ext, near_h_ref, near_w_ref, near_q_ref, far_ref):
    band = lax.axis_index("lat")
    even = lax.rem(band, 2) == 0
    over_pole = (band == 0) | (band == sz.n_lat - 1)
    last = sz.rows - 1
    for f in range(2 if near_q_ref is None else 5):
        flip = jnp.where(over_pole, -1.0, 1.0) if f == 1 else 1.0
        for t in range(sz.tiles):
            lanes = slice(LANES * t, LANES * t + sz.span(t))
            if f == 0:
                near = jnp.where(even, near_h_ref[0:1, lanes], near_h_ref[last : sz.rows, lanes])
            elif f == 1:
                near = jnp.where(even, near_w_ref[0, 1:2, lanes], near_w_ref[last, 1:2, lanes])
            else:
                at = sz.stack * (f - 2) + t
                near = near_q_ref[at : at + 1, : sz.span(t)]
            at = sz.stack * f + t
            far = jnp.zeros_like(near) if far_ref is None else far_ref[at : at + 1, : sz.span(t)] * flip
            ext[f, sz.rows : sz.rows + 1, lanes] = jnp.where(even, near, far)
            ext[f, EXT_ROWS - 1 : EXT_ROWS, lanes] = jnp.where(even, far, near)


class Tiles:
    def __init__(self, sz):
        self.sz = sz
        self.lane = lax.broadcasted_iota(jnp.int32, (EXT_ROWS, LANES), 1)
        self.turned = {}

    def turn(self, name, t, value, step):
        key = (name, t % self.sz.tiles, step)
        if key not in self.turned:
            self.turned[key] = pltpu.roll(value(t % self.sz.tiles), step % LANES, 1)
        return self.turned[key]

    def east(self, name, t, value):
        here = self.turn(name, t, value, -LEVELS)
        return jnp.where(self.lane < LANES - LEVELS, here, self.turn(name, t + 1, value, -LEVELS))

    def west(self, name, t, value):
        here = self.turn(name, t, value, LEVELS)
        return jnp.where(self.lane >= LEVELS, here, self.turn(name, t - 1, value, LEVELS))


def north(value):
    return pltpu.roll(value, EXT_ROWS - 1, 0)


def south(value):
    return pltpu.roll(value, 1, 0)


def polar_kernel(sz, h_ref, w_ref, near_h_ref, near_w_ref, sides_ref, geo_ref, wave_ref, far_ref, near_q_ref, *refs):
    out_refs, (far_out, near_out, tend_ref, pole_ref, ext) = refs[:-5], refs[-5:]
    far_out[...] = far_ref[...]
    near_out[...] = near_q_ref[...]
    if sz.near_only:
        far_ref = None
    band = lax.axis_index("lat")
    ring = Tiles(sz)
    lane = ring.lane
    tiles, stack, rows, work = sz.tiles, sz.stack, sz.rows, sz.work
    even = lax.rem(band, 2) == 0
    for f, value in enumerate((h_ref[...], w_ref[:, 1, :], w_ref[:, 0, :])):
        ext[f, :rows, sz.end :] = jnp.zeros((rows, LANES), jnp.float32)
        ext[f, :rows, : sz.merged] = value
    add_rows(sz, ext, near_h_ref, near_w_ref, None, far_ref)
    inv_cos, sin_centre, cos_face = geo_ref[band, 0], geo_ref[band, 1], geo_ref[band, 2]
    ratio = sz.ratio

    def tile(f, t):
        return ext[f, :, LANES * t : LANES * (t + 1)]

    kept = {}

    def zonal(t):
        if t not in kept:
            thick_e = ring.east("h", t, functools.partial(tile, 0))
            wind_e = ring.east("u", t, functools.partial(tile, 2))
            flux = 0.25 * (tile(2, t) + wind_e) * (tile(0, t) + thick_e) * inv_cos
            if t == tiles - 1:
                flux = jnp.where(lane < sz.tail - LEVELS, flux, 0.0)
            kept[t] = (flux, thick_e)
        return kept[t]

    for t in range(tiles):
        flux, thick_e = zonal(t)
        thick, wind_v, wind_u = tile(0, t), tile(1, t), tile(2, t)
        flux_w = ring.west("f", t, lambda s: zonal(s)[0])
        thick_w = ring.west("hw", t, functools.partial(tile, 0))
        thick_n = north(thick)
        flux_n = (0.25 * ratio) * (wind_v + north(wind_v)) * (thick + thick_n) * cos_face
        thick_tend = -((flux - flux_w) + (flux_n - south(flux_n)) * inv_cos)
        wind_u_tend = sin_centre * wind_v - (thick_e - thick_w) * (0.5 * inv_cos)
        wind_v_tend = -sin_centre * wind_u - (0.5 * ratio) * (thick_n - south(thick))
        spare = 0.0
        if t == tiles - 1:
            last = sz.tail - LEVELS
            columns = [(tile(0, 0), 0), (thick, last), (tile(2, 0), 0), (wind_u, last)]
            for k, (source, at) in reversed(list(enumerate(columns))):
                to = sz.tail + LEVELS * k
                spare = jnp.where(lane < to + LEVELS, pltpu.roll(source, (to - at) % LANES, 1), spare)
        for f, tend in enumerate((thick_tend, wind_u_tend, wind_v_tend, thick)):
            if sz.near_only:
                alone = jnp.where(band < sz.n_lat // 2, tend[:1], tend[rows - 1 : rows])
                if t == tiles - 1:
                    alone = jnp.where(lane[:1] < sz.tail, alone, 0.0)
                pole_ref[stack * f + t : stack * f + t + 1] = alone
            if f == 3:
                continue
            if t == tiles - 1:
                tend = jnp.where(lane < sz.tail, tend, spare)
            if sz.near_only:
                tend = jnp.where(even, north(tend), tend)
            tend_ref[pl.ds(stack * work * f + t, work, stride=stack), :] = tend[:work]
    for f in range(3):
        for t in range(tiles, stack):
            tend_ref[pl.ds(stack * work * f + t, work, stride=stack), :] = jnp.zeros((work, LANES), jnp.float32)
    used = stack * sz.units
    if used < tend_ref.shape[0]:
        tend_ref[used:, :] = jnp.zeros((tend_ref.shape[0] - used, LANES), jnp.float32)
    sides = [sides_ref[:EXT_ROWS], sides_ref[EXT_ROWS:]]
    if sz.near_only:
        sums = pole_sums(sz, pole_ref, wave_ref, spare, band)
        row = lax.broadcasted_iota(jnp.int32, (EXT_ROWS, LANES), 0)
        for k, total in enumerate(sums):
            sides = [jnp.where(row == rows + k, total, side) for side in sides]
    here = lax.axis_index("lon")
    for k, out_ref in enumerate(out_refs):
        out_ref[: sz.size] = tend_ref[sz.piece(k), :]
        eastward = sz.partner(k) == lax.rem(here + 1, sz.n_lon)
        out_ref[sz.size :] = jnp.where(eastward, sides[1], sides[0])


def pole_sums(sz, pole_ref, wave_ref, spare, band):
    stack, rows = sz.stack, sz.rows
    lane = lax.broadcasted_iota(jnp.int32, (1, LANES), 1)
    sides = jnp.where(band < sz.n_lat // 2, spare[:1], spare[rows - 1 : rows])
    found = [jnp.zeros((1, LANES), jnp.float32), pltpu.roll(sides, (LANES // 2 - sz.tail) % LANES, 1)]
    for f in range(4):
        if sz.tiles < stack:
            pole_ref[stack * f + sz.tiles : stack * (f + 1)] = jnp.zeros((stack - sz.tiles, LANES), jnp.float32)
        values = pole_ref[stack * f : stack * (f + 1)]
        for k, terms in enumerate((values, values * wave_ref[0], values * wave_ref[1])):
            total = jnp.sum(terms, axis=0, keepdims=True)
            for step in (64, 32, 16):
                total = total + pltpu.roll(total, step, 1)
            row, place = divmod(3 * f + k, PER_TILE)
            inside = (lane >= LEVELS * place) & (lane < LEVELS * (place + 1))
            found[row] = jnp.where(inside, total, found[row])
    return found


def pole_waves(sz, rows_in, inv_cos, sign):
    n_lon = sz.n_lon
    lane = lax.broadcasted_iota(jnp.int32, (1, LANES), 1)

    def value(s, place):
        row, at = divmod(place, PER_TILE)
        return pltpu.roll(rows_in[s % n_lon, row : row + 1], (-LEVELS * at) % LANES, 1)

    theta = 2 * math.pi / sz.nlon
    ends = (1.0, math.cos(theta * (sz.columns - 1)), math.sin(theta * (sz.columns - 1)))
    sums = [[[value(s, 3 * f + k) for k in range(3)] for f in range(4)] for s in range(n_lon)]
    for s in range(n_lon):
        thick_w, thick_e = value(s, 13), value(s + 1, 12)
        flux = 0.25 * (value(s, 15) + value(s + 1, 14)) * (thick_w + thick_e) * inv_cos
        slope = 0.5 * inv_cos
        after = (s + 1) % n_lon
        for f, (west_of, east_of) in enumerate(((flux, flux), (slope * thick_e, slope * thick_w))):
            for k in range(3):
                sums[s][f][k] = sums[s][f][k] - west_of * ends[k]
            for k in range(2):
                sums[after][f][k] = sums[after][f][k] + east_of
    result = []
    for f in range(3):
        waves_of = [0.0, 0.0, 0.0]
        for s in range(n_lon):
            level, cosine, sine = sums[s][f]
            if f == 2:
                level = level + (0.5 * sz.ratio) * sign * sums[s][3][0]
                cosine = cosine - (0.5 * sz.ratio) * sign * sums[s][3][1]
                sine = sine - (0.5 * sz.ratio) * sign * sums[s][3][2]
            c, d = math.cos(2 * math.pi * s / n_lon), math.sin(2 * math.pi * s / n_lon)
            waves_of[0] = waves_of[0] + level
            waves_of[1] = waves_of[1] + (c * cosine - d * sine)
            waves_of[2] = waves_of[2] + (d * cosine + c * sine)
        spread = []
        for k, total in enumerate(waves_of):
            total = jnp.where(lane < LEVELS, total * ((1.0 if k == 0 else 2.0) / sz.nlon), 0.0)
            for step in (16, 32, 64):
                total = total + pltpu.roll(total, step, 1)
            spread.append(total)
        result.append(spread)
    return result


def rest_kernel(sz, cut_ref, h_ref, w_ref, q_ref, near_h_ref, near_w_ref, near_q_ref, far_ref, geo_ref, wave_ref, after_ref, *refs):
    met_refs, (new_w_ref, new_h_ref, mass_ref, ext, pole_in) = refs[: sz.n_lon], refs[sz.n_lon :]
    band = lax.axis_index("lat")
    ring = Tiles(sz)
    lane = ring.lane
    tiles, rows = sz.tiles, sz.rows
    for f in range(6):
        if f < 2 or f == 5:
            value = (h_ref[...], w_ref[:, 1, :], w_ref[:, 0, :])[min(f, 2)]
        else:
            value = q_ref[f - 2].astype(jnp.float32)
        ext[f, :rows, : sz.merged] = value
    add_rows(sz, ext, near_h_ref, near_w_ref, near_q_ref, far_ref)
    lane9 = lane[:rows]
    here = lax.axis_index("lon")
    from_e = from_w = met_refs[0][sz.size :]
    for k, met_ref in enumerate(met_refs):
        eastward = lax.rem(sz.partner(k) - here + sz.n_lon, sz.n_lon)
        pole_in[eastward] = met_ref[sz.size + 8 :]
        from_e = jnp.where(sz.partner(k) == lax.rem(here + 1, sz.n_lon), met_ref[sz.size :], from_e)
        from_w = jnp.where(sz.partner(k) == lax.rem(here + sz.n_lon - 1, sz.n_lon), met_ref[sz.size :], from_w)
    for place, f in enumerate((0, 5, 2, 3, 4)):
        after = pltpu.roll(from_e, (sz.tail - LEVELS * place) % LANES, 1)[:rows]
        before = pltpu.roll(from_w, (LANES - LEVELS - LEVELS * place) % LANES, 1)[:rows]
        own = ext[f, :rows, sz.end :]
        edge = jnp.where(lane9 < LANES - LEVELS, after, before)
        ext[f, :rows, sz.end :] = jnp.where(lane9 < sz.tail, own, edge)
    inv_cos, sin_centre, cos_face = geo_ref[band, 0], geo_ref[band, 1], geo_ref[band, 2]
    ratio = sz.ratio

    active, alone = sz.active(cut_ref, (EXT_ROWS, LANES))
    if sz.near_only:
        band = lax.axis_index("lat")
        low = band < sz.n_lat // 2
        pole_cos = jnp.where(low, inv_cos[:1], inv_cos[rows - 1 : rows])
        kept_waves = pole_waves(sz, pole_in.at[:, rows - 8 :], pole_cos, jnp.where(low, 1.0, -1.0))

    def stepped(f, t, value, tend):
        tend = jnp.where(active, 0.0, tend)
        if sz.near_only:
            level, cosine, sine = kept_waves[f]
            wave = level + cosine * wave_ref[0, t : t + 1] + sine * wave_ref[1, t : t + 1]
            tend = jnp.where(alone, wave, tend)
        return value + TIME_STEP * tend

    def tile(f, t):
        return ext[f, :, LANES * t : LANES * (t + 1)]

    kept = {}

    def zonal(t):
        if t not in kept:
            thick_e = ring.east("h", t, functools.partial(tile, 0))
            wind_e = ring.east("u", t, functools.partial(tile, 5))
            flux = 0.25 * (tile(5, t) + wind_e) * (tile(0, t) + thick_e) * inv_cos
            parts = []
            for k in range(3):
                q = tile(2 + k, t)
                q_e = ring.east(k, t, functools.partial(tile, 2 + k))
                parts.append(DIFFUSION * (q_e - q) - flux * (0.5 * (q + q_e)))
            kept[t] = (flux, thick_e, parts)
        return kept[t]

    for t in range(tiles):
        span = sz.span(t)
        lanes = slice(LANES * t, LANES * t + span)
        flux, thick_e, parts = zonal(t)
        thick, wind_u, wind_v = tile(0, t), tile(5, t), tile(1, t)
        flux_w = ring.west("f", t, lambda s: zonal(s)[0])
        thick_w = ring.west("hw", t, functools.partial(tile, 0))
        thick_n = north(thick)
        flux_n = (0.25 * ratio) * (wind_v + north(wind_v)) * (thick + thick_n) * cos_face
        thick_tend = -((flux - flux_w) + (flux_n - south(flux_n)) * inv_cos)
        wind_u_tend = sin_centre * wind_v - (thick_e - thick_w) * (0.5 * inv_cos)
        wind_v_tend = -sin_centre * wind_u - (0.5 * ratio) * (thick_n - south(thick))
        new_h_ref[:, lanes] = stepped(0, t, thick, thick_tend)[:rows, :span]
        new_w_ref[0, :, lanes] = stepped(1, t, wind_u, wind_u_tend)[:rows, :span]
        new_w_ref[1, :, lanes] = stepped(2, t, wind_v, wind_v_tend)[:rows, :span]
        for k in range(3):
            q = tile(2 + k, t)
            q_n = north(q)
            zonal_part = parts[k] - ring.west(("p", k), t, lambda s: zonal(s)[2][k])
            lap = q_n + south(q) - 2.0 * q
            over = flux_n * (0.5 * (q + q_n))
            merid_part = DIFFUSION * lap - (over - south(over)) * inv_cos
            mass = thick * q + TIME_STEP * (zonal_part + merid_part)
            mass_ref[k, :, lanes] = mass[:rows, :span].astype(jnp.bfloat16)


def sin_pi(y):
    y = jnp.where(y > 0.5, 1.0 - y, jnp.where(y < -0.5, -1.0 - y, y))
    s = y * y
    series = [(-1) ** i * math.pi ** (2 * i + 1) / math.factorial(2 * i + 1) for i in range(7)]
    total = series[-1]
    for factor in reversed(series[:-1]):
        total = total * s + factor
    return total * y


def share_of(sz, i):
    unit = lax.axis_index("lon") * sz.share + i
    return unit // sz.work, sz.first() + lax.rem(unit, sz.work)


def weights_kernel(sz, cut_ref, n_ref, inverse_ref, after_ref, weights_ref):
    band = lax.axis_index("lat")
    size = PER_TILE * sz.stack
    for i in range(sz.share):
        width = (2 * cut_ref[band * sz.rows + share_of(sz, i)[1]] + 1).astype(jnp.float32)
        n = n_ref[...]
        turns = n * width
        turns = turns - jnp.round(turns * (0.5 / sz.nlon)) * (2.0 * sz.nlon)
        weights = sin_pi(turns * (1.0 / sz.nlon)) * inverse_ref[...]
        weights = jnp.where(n == 0.0, width * (1.0 / sz.nlon), weights)
        weights_ref[size * i : size * (i + 1)] = weights.astype(jnp.bfloat16)


def filter_kernel(sz, weights_ref, geo_ref, after_ref, also_after_ref, *refs):
    n_lon, stack, share = sz.n_lon, sz.stack, sz.share
    in_refs, out_refs, (gathered, results) = refs[:n_lon], refs[n_lon : 2 * n_lon], refs[2 * n_lon :]
    for k, in_ref in enumerate(in_refs):
        gathered[sz.partner(k)] = in_ref[: sz.size]

    band = lax.axis_index("lat")
    lane = lax.broadcasted_iota(jnp.int32, (share, LANES), 1)
    place = lax.broadcasted_iota(jnp.int32, (share, LANES), 0)
    by_flux = by_thick = jnp.zeros((share, LANES), jnp.float32)
    for i in range(share):
        field, row = share_of(sz, i)
        inv_cos = geo_ref[band, 0, pl.ds(row, 1), :]
        by_flux = jnp.where((place == i) & (field == 0), inv_cos, by_flux)
        by_thick = jnp.where((place == i) & (field == 1), 0.5 * inv_cos, by_thick)
    sides = [gathered[s, pl.ds(sz.tiles - 1, share, stride=stack), :] for s in range(n_lon)]

    def column(s, k):
        return pltpu.roll(sides[s % n_lon], (-sz.tail - LEVELS * k) % LANES, 1)

    for s in range(n_lon):
        thick_w, thick_e = column(s, 1), column(s + 1, 0)
        flux = 0.25 * (column(s, 3) + column(s + 1, 2)) * (thick_w + thick_e) * by_flux
        west_of, east_of = flux + by_thick * thick_e, flux + by_thick * thick_w
        at = pl.ds(sz.tiles - 1, share, stride=stack)
        own = gathered[s, at, :]
        own = own - jnp.where(lane >= sz.tail - LEVELS, pltpu.roll(west_of, sz.tail - LEVELS, 1), 0.0)
        gathered[s, at, :] = jnp.where(lane < sz.tail, own, 0.0)
        at = pl.ds(0, share, stride=stack)
        after = (s + 1) % n_lon
        gathered[after, at, :] = gathered[after, at, :] + jnp.where(lane < LEVELS, east_of, 0.0)

    wide = lax.broadcasted_iota(jnp.int32, (stack, LANES), 1)
    rows = PER_TILE * stack
    for i in range(share):
        here = slice(stack * i, stack * (i + 1))
        pieces = [gathered[s, here].astype(jnp.bfloat16) for s in range(n_lon)]
        circle = jnp.concatenate([jnp.concatenate(pieces[s:] + pieces[:s], axis=0) for s in range(n_lon)], axis=1)
        spread = jnp.dot(weights_ref[rows * i : rows * (i + 1)], circle, preferred_element_type=jnp.float32)
        for s in range(n_lon):
            same = spread[:stack, LANES * s : LANES * (s + 1)]
            carried = None
            for e in range(1, PER_TILE):
                part = spread[stack * e : stack * (e + 1), LANES * s : LANES * (s + 1)]
                part = pltpu.roll(part, LEVELS * e, 1)
                inside = wide >= LEVELS * e
                same = same + jnp.where(inside, part, 0.0)
                over = jnp.where(inside, 0.0, part)
                carried = over if carried is None else carried + over
            results[s, here] = pltpu.roll(same, stack - 1, 0) + carried
    for k, out_ref in enumerate(out_refs):
        out_ref[...] = results[sz.partner(k)]


def finish_kernel(sz, cut_ref, base_w_ref, base_h_ref, *refs):
    back_refs, (new_w_ref, new_h_ref, back_ref) = refs[: sz.n_lon], refs[sz.n_lon :]
    rows, work = sz.rows, sz.work
    for k, ref in enumerate(back_refs):
        back_ref[sz.piece(k), :] = ref[...]
    active, alone = sz.active(cut_ref, (EXT_ROWS, LANES))
    scale = jnp.where(active & jnp.logical_not(alone), TIME_STEP, 0.0)
    even = lax.rem(lax.axis_index("lat"), 2) == 0
    for f in range(3):
        for t in range(sz.tiles):
            span = sz.span(t)
            lanes = slice(LANES * t, LANES * t + span)
            tend = back_ref[pl.ds(sz.stack * work * f + t, work, stride=sz.stack), :]
            if sz.near_only:
                tend = jnp.concatenate([tend, jnp.zeros((EXT_ROWS - work, LANES), jnp.float32)], axis=0)
                tend = jnp.where(even, south(tend), tend)
            change = (scale[:rows] * tend[:rows])[:, :span]
            if f == 0:
                new_h_ref[:, lanes] = base_h_ref[:, lanes] + change
            else:
                new_w_ref[:, f - 1, lanes] = base_w_ref[f - 1, :, lanes] + change


def local(winds, thickness, tracers, cutoff):
    n_lat = lax.axis_size("lat")
    n_lon = lax.axis_size("lon")
    rows, merged = thickness.shape
    sz = Sizes(rows, merged, n_lat, n_lon)
    f32 = jnp.float32
    vmem = pl.BlockSpec(memory_space=pltpu.VMEM)
    smem = pl.BlockSpec(memory_space=pltpu.SMEM)
    hbm = pl.BlockSpec(memory_space=pltpu.HBM)
    anywhere = pl.BlockSpec(memory_space=pl.ANY)

    def shaped(*shape):
        return jax.ShapeDtypeStruct(shape, f32)

    def call(kernel, name, in_specs, out_shape, scratch=(), limit=LIMIT):
        return pl.pallas_call(
            functools.partial(kernel, sz),
            out_shape=out_shape,
            in_specs=in_specs,
            out_specs=jax.tree.map(lambda _: vmem, out_shape),
            scratch_shapes=list(scratch),
            compiler_params=pltpu.CompilerParams(vmem_limit_bytes=limit),
            name=name,
        )

    geo = jnp.asarray(geometry(sz))
    wave = jnp.asarray(waves(sz))
    n, inverse = (jnp.asarray(table) for table in offsets(sz))

    wind_rows = jnp.swapaxes(winds, 0, 1)
    tracer_rows = jnp.swapaxes(tracers, 0, 1)
    far_row, near_row = shaped(5 * sz.stack, LANES), shaped(3 * sz.stack, LANES)
    kept = [((1,), f32), ((2,), f32), ((3,), jnp.bfloat16)]
    near_q, far_rows, sides = call(
        edges_kernel,
        "edges",
        [hbm] * 3,
        (near_row, far_row, shaped(2 * EXT_ROWS, LANES)),
        [pltpu.VMEM((2,) + count + (merged,), dtype) for count, dtype in kept]
        + [
            pltpu.VMEM((rows,) + (count if count != (1,) else ()) + (lanes,), dtype)
            for lanes in (LANES, sz.tail)
            for count, dtype in kept
        ]
        + [pltpu.SemaphoreType.DMA((3, 4))],
        limit=MOST_VMEM,
    )(thickness, wind_rows, tracer_rows)

    near = [(band * n_lon + i, (band ^ 1) * n_lon + i) for band in range(n_lat) for i in range(n_lon)]
    far = []
    for band in range(n_lat):
        other = band - 1 if band % 2 == 0 else band + 1
        for i in range(n_lon):
            if 0 <= other < n_lat:
                far.append((band * n_lon + i, other * n_lon + i))
            else:
                far.append((band * n_lon + i, band * n_lon + (i + n_lon // 2) % n_lon))
    near_h = lax.ppermute(thickness, ("lat", "lon"), near)
    near_w = lax.ppermute(wind_rows, ("lat", "lon"), near)
    if not sz.near_only:
        far_rows = lax.ppermute(far_rows, ("lat", "lon"), far)

    order = [sz.turns(False), sz.turns(True)]

    def meetings(shares):
        got = [shares[0]]
        for k in range(1, n_lon):
            sectors = [(band, i, i ^ order[band % 2][k]) for band in range(n_lat) for i in range(n_lon)]
            got.append(lax.ppermute(shares[k], ("lat", "lon"), [(b * n_lon + i, b * n_lon + j) for b, i, j in sectors]))
        return got

    all_pieces = pltpu.VMEM((n_lon, sz.size, LANES), f32)
    *tends, far_rows, near_q = call(
        polar_kernel,
        "polar",
        [vmem] * 9,
        [shaped(sz.size + EXT_ROWS, LANES)] * n_lon + [far_row, near_row],
        [
            pltpu.VMEM((n_lon * sz.size, LANES), f32),
            pltpu.VMEM((4 * sz.stack, LANES), f32),
            pltpu.VMEM((3, EXT_ROWS, sz.tiles * LANES), f32),
        ],
    )(thickness, wind_rows, near_h, near_w, sides, geo, wave, far_rows, near_q)
    met = meetings(tends)
    near_q = lax.ppermute(near_q, ("lat", "lon"), near)
    from_far = lax.ppermute(far_rows, ("lat", "lon"), far) if sz.near_only else far_rows
    weights = call(
        weights_kernel,
        "weights",
        [smem, vmem, vmem, anywhere],
        jax.ShapeDtypeStruct((sz.share * PER_TILE * sz.stack, n_lon * sz.stack), jnp.bfloat16),
    )(cutoff, n, inverse, tends[0])
    worked = call(
        filter_kernel,
        "filter",
        [vmem] * 2 + [anywhere] * 2 + [vmem] * n_lon,
        [shaped(sz.size, LANES)] * n_lon,
        [all_pieces, all_pieces],
    )(weights, geo, from_far, near_q, *met)
    back = meetings(worked)

    base_w, base_h, mass = call(
        rest_kernel,
        "rest",
        [smem] + [vmem] * 9 + [anywhere] + [vmem] * n_lon,
        (shaped(2, rows, merged), shaped(rows, merged), jax.ShapeDtypeStruct(tracers.shape, jnp.bfloat16)),
        [pltpu.VMEM((6, EXT_ROWS, sz.tiles * LANES), f32), pltpu.VMEM((n_lon, 8, LANES), f32)],
    )(cutoff, thickness, wind_rows, tracers, near_h, near_w, near_q, from_far, geo, wave, worked[0], *met)

    new_w, new_h = call(
        finish_kernel,
        "finish",
        [smem] + [vmem] * (2 + n_lon),
        (shaped(*wind_rows.shape), shaped(rows, merged)),
        [pltpu.VMEM((n_lon * sz.size, LANES), f32)],
    )(cutoff, base_w, base_h, *back)
    return jnp.swapaxes(new_w, 0, 1), new_h, mass


def solution(mesh):
    in_specs = (P(None, "lat", "lon"), P("lat", "lon"), P(None, "lat", "lon"), P())
    out_specs = (P(None, "lat", "lon"), P("lat", "lon"), P(None, "lat", "lon"))
    return jax.shard_map(local, mesh=mesh, in_specs=in_specs, out_specs=out_specs, check_vma=False)
```

```python
import functools
import math

import jax
import jax.numpy as jnp
import numpy as np
from jax import lax
from jax.experimental import pallas as pl
from jax.experimental.pallas import tpu as pltpu
from jax.sharding import PartitionSpec as P

LEVELS = 16
TIME_STEP = 0.05
DIFFUSION = 0.5
LANES = 128
PER_TILE = LANES // LEVELS
EXT_ROWS = 16
LIMIT = 48 * 1024 * 1024
MOST_VMEM = 64 * 1024 * 1024 - 10500 * 1024


class Sizes:
    def __init__(self, rows, merged, n_lat, n_lon):
        self.rows = rows
        self.merged = merged
        self.columns = merged // LEVELS
        self.n_lat = n_lat
        self.n_lon = n_lon
        self.nlat = rows * n_lat
        self.nlon = self.columns * n_lon
        self.ratio = 2.0 * self.nlat / self.nlon
        self.tiles = -(-merged // LANES)
        self.end = (self.tiles - 1) * LANES
        self.tail = merged - self.end
        self.stack = -(-(self.tiles + 1) // 8) * 8
        self.near_only = rows <= self.nlat // 6 < 2 * rows
        self.work = rows - 1 if self.near_only else rows
        self.units = 3 * self.work
        self.share = -(-self.units // n_lon)
        self.size = self.share * self.stack
        assert self.tail <= LANES - 4 * LEVELS and rows + 2 <= EXT_ROWS and n_lat % 2 == 0
        assert n_lon >= 4 and n_lon & (n_lon - 1) == 0

    def span(self, tile):
        return self.tail if tile == self.tiles - 1 else LANES

    def first(self):
        return jnp.where(lax.rem(lax.axis_index("lat"), 2) == 0, 1, 0) if self.near_only else 0

    def at_pole(self, row):
        band = lax.axis_index("lat")
        pole = jnp.where(band == 0, 0, jnp.where(band == self.n_lat - 1, self.rows - 1, -1))
        return row == (pole if self.near_only else -1)

    def turns(self, odd):
        middle = list(range(1, self.n_lon - 1))
        return [0, self.n_lon - 1] + (middle[::-1] if odd else middle)

    def partner(self, k):
        odd = lax.rem(lax.axis_index("lat"), 2) == 1
        turn = jnp.where(odd, self.turns(True)[k], self.turns(False)[k])
        return jnp.bitwise_xor(lax.axis_index("lon"), turn)

    def piece(self, k):
        return pl.ds(pl.multiple_of(self.partner(k) * self.size, 8), self.size)


def geometry(sz):
    table = np.zeros((sz.n_lat, 3, EXT_ROWS, LANES), np.float64)

    def face(j):
        return math.sin((j + 1) * math.pi / sz.nlat) if 0 <= j < sz.nlat - 1 else 0.0

    for band in range(sz.n_lat):
        for row in range(sz.rows):
            j = band * sz.rows + row
            centre = (j + 0.5) * math.pi / sz.nlat - math.pi / 2
            table[band, 0, row] = 1.0 / math.cos(centre)
            table[band, 1, row] = math.sin(centre)
            table[band, 2, row] = face(j)
        table[band, 2, EXT_ROWS - 1] = face(band * sz.rows - 1)
    return table.astype(np.float32)


def offsets(sz):
    shift, out_tile = np.divmod(np.arange(PER_TILE * sz.stack), sz.stack)
    sector, in_tile = np.divmod(np.arange(sz.n_lon * sz.stack), sz.stack)
    n = (PER_TILE * (out_tile - 1) + shift)[:, None] - (PER_TILE * in_tile + sz.columns * sector)[None, :]
    n = (n + sz.nlon // 2) % sz.nlon - sz.nlon // 2
    with np.errstate(divide="ignore"):
        inverse = np.where(n == 0, 0.0, 1.0 / (sz.nlon * np.sin(np.pi * n / sz.nlon)))
    return n.astype(np.float32), inverse.astype(np.float32)


def waves(sz):
    column = PER_TILE * np.arange(sz.stack)[:, None] + np.arange(LANES)[None, :] // LEVELS
    angle = 2 * np.pi * column / sz.nlon
    return np.stack([np.cos(angle), np.sin(angle)]).astype(np.float32)


def edges_kernel(sz, h_hbm, w_hbm, q_hbm, near_ref, far_ref, sides_ref, *scratch):
    row_refs, first_refs, last_refs, sems = scratch[:3], scratch[3:6], scratch[6:9], scratch[9]
    rows, last = sz.rows, sz.rows - 1
    even = lax.rem(lax.axis_index("lat"), 2) == 0
    copies = []
    for i, source in enumerate((h_hbm, w_hbm, q_hbm)):
        for k, row in enumerate((0, last)):
            one = source.at[pl.ds(row, 1)] if i == 0 else source.at[row]
            copies.append(pltpu.make_async_copy(one, row_refs[i].at[k], sems.at[i, k]))
        for k, (start, to) in enumerate(((0, first_refs[i]), (sz.end, last_refs[i]))):
            lanes = pl.ds(start, to.shape[-1])
            cut = source.at[:, lanes] if i == 0 else source.at[:, :, lanes]
            copies.append(pltpu.make_async_copy(cut, to, sems.at[i, 2 + k]))
    for copy in copies:
        copy.start()
    for copy in copies:
        copy.wait()
    h_rows, w_rows, q_rows = row_refs
    for t in range(sz.tiles):
        wide = sz.span(t)
        lanes = slice(LANES * t, LANES * t + wide)
        q = [q_rows[k, :, lanes].astype(jnp.float32) for k in range(2)]
        for f in range(5):
            if f == 0:
                first, final = h_rows[0, :, lanes], h_rows[1, :, lanes]
            elif f == 1:
                first, final = w_rows[0, 1:2, lanes], w_rows[1, 1:2, lanes]
            else:
                first, final = q[0][f - 2 : f - 1], q[1][f - 2 : f - 1]
                at = sz.stack * (f - 2) + t
                near_ref[at : at + 1, :wide] = jnp.where(even, final, first)
            at = sz.stack * f + t
            far_ref[at : at + 1, :wide] = jnp.where(even, first, final)
    sides_ref[...] = jnp.zeros(sides_ref.shape, jnp.float32)
    for k, (refs, at) in enumerate(((first_refs, 0), (last_refs, sz.tail - LEVELS))):
        columns = slice(at, at + LEVELS)
        for f in range(5):
            if f == 0:
                value = refs[0][:, columns]
            elif f == 1:
                value = refs[1][:, 0, columns]
            else:
                value = refs[2][:, f - 2, columns].astype(jnp.float32)
            sides_ref[EXT_ROWS * k : EXT_ROWS * k + rows, LEVELS * f : LEVELS * (f + 1)] = value


def add_rows(sz, ext, near_h_ref, near_w_ref, near_q_ref, far_ref):
    band = lax.axis_index("lat")
    even = lax.rem(band, 2) == 0
    over_pole = (band == 0) | (band == sz.n_lat - 1)
    last = sz.rows - 1
    for f in range(2 if near_q_ref is None else 5):
        flip = jnp.where(over_pole, -1.0, 1.0) if f == 1 else 1.0
        for t in range(sz.tiles):
            lanes = slice(LANES * t, LANES * t + sz.span(t))
            if f == 0:
                near = jnp.where(even, near_h_ref[0:1, lanes], near_h_ref[last : sz.rows, lanes])
            elif f == 1:
                near = jnp.where(even, near_w_ref[0, 1:2, lanes], near_w_ref[last, 1:2, lanes])
            else:
                at = sz.stack * (f - 2) + t
                near = near_q_ref[at : at + 1, : sz.span(t)]
            at = sz.stack * f + t
            far = jnp.zeros_like(near) if far_ref is None else far_ref[at : at + 1, : sz.span(t)] * flip
            ext[f, sz.rows : sz.rows + 1, lanes] = jnp.where(even, near, far)
            ext[f, EXT_ROWS - 1 : EXT_ROWS, lanes] = jnp.where(even, far, near)


class Tiles:
    def __init__(self, sz):
        self.sz = sz
        self.lane = lax.broadcasted_iota(jnp.int32, (EXT_ROWS, LANES), 1)
        self.turned = {}

    def turn(self, name, t, value, step):
        key = (name, t % self.sz.tiles, step)
        if key not in self.turned:
            self.turned[key] = pltpu.roll(value(t % self.sz.tiles), step % LANES, 1)
        return self.turned[key]

    def east(self, name, t, value):
        here = self.turn(name, t, value, -LEVELS)
        return jnp.where(self.lane < LANES - LEVELS, here, self.turn(name, t + 1, value, -LEVELS))

    def west(self, name, t, value):
        here = self.turn(name, t, value, LEVELS)
        return jnp.where(self.lane >= LEVELS, here, self.turn(name, t - 1, value, LEVELS))


def north(value):
    return pltpu.roll(value, EXT_ROWS - 1, 0)


def south(value):
    return pltpu.roll(value, 1, 0)


def polar_kernel(sz, h_ref, w_ref, near_h_ref, near_w_ref, sides_ref, geo_ref, wave_ref, far_ref, near_q_ref, *refs):
    out_refs, (far_out, near_out, tend_ref, pole_ref, ext) = refs[:-5], refs[-5:]
    far_out[...] = far_ref[...]
    near_out[...] = near_q_ref[...]
    if sz.near_only:
        far_ref = None
    band = lax.axis_index("lat")
    ring = Tiles(sz)
    lane = ring.lane
    tiles, stack, rows, work = sz.tiles, sz.stack, sz.rows, sz.work
    even = lax.rem(band, 2) == 0
    for f, value in enumerate((h_ref[...], w_ref[:, 1, :], w_ref[:, 0, :])):
        ext[f, :rows, sz.end :] = jnp.zeros((rows, LANES), jnp.float32)
        ext[f, :rows, : sz.merged] = value
    add_rows(sz, ext, near_h_ref, near_w_ref, None, far_ref)
    inv_cos, sin_centre, cos_face = geo_ref[band, 0], geo_ref[band, 1], geo_ref[band, 2]
    ratio = sz.ratio

    def tile(f, t):
        return ext[f, :, LANES * t : LANES * (t + 1)]

    kept = {}

    def zonal(t):
        if t not in kept:
            thick_e = ring.east("h", t, functools.partial(tile, 0))
            wind_e = ring.east("u", t, functools.partial(tile, 2))
            flux = 0.25 * (tile(2, t) + wind_e) * (tile(0, t) + thick_e) * inv_cos
            if t == tiles - 1:
                flux = jnp.where(lane < sz.tail - LEVELS, flux, 0.0)
            kept[t] = (flux, thick_e)
        return kept[t]

    for t in range(tiles):
        flux, thick_e = zonal(t)
        thick, wind_v, wind_u = tile(0, t), tile(1, t), tile(2, t)
        flux_w = ring.west("f", t, lambda s: zonal(s)[0])
        thick_w = ring.west("hw", t, functools.partial(tile, 0))
        thick_n = north(thick)
        flux_n = (0.25 * ratio) * (wind_v + north(wind_v)) * (thick + thick_n) * cos_face
        thick_tend = -((flux - flux_w) + (flux_n - south(flux_n)) * inv_cos)
        wind_u_tend = sin_centre * wind_v - (thick_e - thick_w) * (0.5 * inv_cos)
        wind_v_tend = -sin_centre * wind_u - (0.5 * ratio) * (thick_n - south(thick))
        spare = 0.0
        if t == tiles - 1:
            last = sz.tail - LEVELS
            columns = [(tile(0, 0), 0), (thick, last), (tile(2, 0), 0), (wind_u, last)]
            for k, (source, at) in reversed(list(enumerate(columns))):
                to = sz.tail + LEVELS * k
                spare = jnp.where(lane < to + LEVELS, pltpu.roll(source, (to - at) % LANES, 1), spare)
        for f, tend in enumerate((thick_tend, wind_u_tend, wind_v_tend, thick)):
            if sz.near_only:
                alone = jnp.where(band < sz.n_lat // 2, tend[:1], tend[rows - 1 : rows])
                if t == tiles - 1:
                    alone = jnp.where(lane[:1] < sz.tail, alone, 0.0)
                pole_ref[stack * f + t : stack * f + t + 1] = alone
            if f == 3:
                continue
            if t == tiles - 1:
                tend = jnp.where(lane < sz.tail, tend, spare)
            if sz.near_only:
                tend = jnp.where(even, north(tend), tend)
            tend_ref[pl.ds(stack * work * f + t, work, stride=stack), :] = tend[:work]
    for f in range(3):
        for t in range(tiles, stack):
            tend_ref[pl.ds(stack * work * f + t, work, stride=stack), :] = jnp.zeros((work, LANES), jnp.float32)
    used = stack * sz.units
    if used < tend_ref.shape[0]:
        tend_ref[used:, :] = jnp.zeros((tend_ref.shape[0] - used, LANES), jnp.float32)
    sides = [sides_ref[:EXT_ROWS], sides_ref[EXT_ROWS:]]
    if sz.near_only:
        sums = pole_sums(sz, pole_ref, wave_ref, spare, band)
        row = lax.broadcasted_iota(jnp.int32, (EXT_ROWS, LANES), 0)
        for k, total in enumerate(sums):
            sides = [jnp.where(row == rows + k, total, side) for side in sides]
    here = lax.axis_index("lon")
    for k, out_ref in enumerate(out_refs):
        out_ref[: sz.size] = tend_ref[sz.piece(k), :]
        eastward = sz.partner(k) == lax.rem(here + 1, sz.n_lon)
        out_ref[sz.size :] = jnp.where(eastward, sides[1], sides[0])


def pole_sums(sz, pole_ref, wave_ref, spare, band):
    stack, rows = sz.stack, sz.rows
    lane = lax.broadcasted_iota(jnp.int32, (1, LANES), 1)
    sides = jnp.where(band < sz.n_lat // 2, spare[:1], spare[rows - 1 : rows])
    found = [jnp.zeros((1, LANES), jnp.float32), pltpu.roll(sides, (LANES // 2 - sz.tail) % LANES, 1)]
    for f in range(4):
        if sz.tiles < stack:
            pole_ref[stack * f + sz.tiles : stack * (f + 1)] = jnp.zeros((stack - sz.tiles, LANES), jnp.float32)
        values = pole_ref[stack * f : stack * (f + 1)]
        for k, terms in enumerate((values, values * wave_ref[0], values * wave_ref[1])):
            total = jnp.sum(terms, axis=0, keepdims=True)
            for step in (64, 32, 16):
                total = total + pltpu.roll(total, step, 1)
            row, place = divmod(3 * f + k, PER_TILE)
            inside = (lane >= LEVELS * place) & (lane < LEVELS * (place + 1))
            found[row] = jnp.where(inside, total, found[row])
    return found


def pole_waves(sz, rows_in, inv_cos, sign):
    n_lon = sz.n_lon
    lane = lax.broadcasted_iota(jnp.int32, (1, LANES), 1)

    def value(s, place):
        row, at = divmod(place, PER_TILE)
        return pltpu.roll(rows_in[s % n_lon, row : row + 1], (-LEVELS * at) % LANES, 1)

    theta = 2 * math.pi / sz.nlon
    ends = (1.0, math.cos(theta * (sz.columns - 1)), math.sin(theta * (sz.columns - 1)))
    sums = [[[value(s, 3 * f + k) for k in range(3)] for f in range(4)] for s in range(n_lon)]
    for s in range(n_lon):
        thick_w, thick_e = value(s, 13), value(s + 1, 12)
        flux = 0.25 * (value(s, 15) + value(s + 1, 14)) * (thick_w + thick_e) * inv_cos
        slope = 0.5 * inv_cos
        after = (s + 1) % n_lon
        for f, (west_of, east_of) in enumerate(((flux, flux), (slope * thick_e, slope * thick_w))):
            for k in range(3):
                sums[s][f][k] = sums[s][f][k] - west_of * ends[k]
            for k in range(2):
                sums[after][f][k] = sums[after][f][k] + east_of
    result = []
    for f in range(3):
        waves_of = [0.0, 0.0, 0.0]
        for s in range(n_lon):
            level, cosine, sine = sums[s][f]
            if f == 2:
                level = level + (0.5 * sz.ratio) * sign * sums[s][3][0]
                cosine = cosine - (0.5 * sz.ratio) * sign * sums[s][3][1]
                sine = sine - (0.5 * sz.ratio) * sign * sums[s][3][2]
            c, d = math.cos(2 * math.pi * s / n_lon), math.sin(2 * math.pi * s / n_lon)
            waves_of[0] = waves_of[0] + level
            waves_of[1] = waves_of[1] + (c * cosine - d * sine)
            waves_of[2] = waves_of[2] + (d * cosine + c * sine)
        spread = []
        for k, total in enumerate(waves_of):
            total = jnp.where(lane < LEVELS, total * ((1.0 if k == 0 else 2.0) / sz.nlon), 0.0)
            for step in (16, 32, 64):
                total = total + pltpu.roll(total, step, 1)
            spread.append(total)
        result.append(spread)
    return result


def rest_kernel(sz, masks_ref, h_ref, w_ref, q_ref, near_h_ref, near_w_ref, near_q_ref, far_ref, geo_ref, wave_ref, after_ref, *refs):
    met_refs, (new_w_ref, new_h_ref, mass_ref, ext, pole_in) = refs[: sz.n_lon], refs[sz.n_lon :]
    band = lax.axis_index("lat")
    ring = Tiles(sz)
    lane = ring.lane
    tiles, rows = sz.tiles, sz.rows
    for f in range(6):
        if f < 2 or f == 5:
            value = (h_ref[...], w_ref[:, 1, :], w_ref[:, 0, :])[min(f, 2)]
        else:
            value = q_ref[f - 2].astype(jnp.float32)
        ext[f, :rows, : sz.merged] = value
    add_rows(sz, ext, near_h_ref, near_w_ref, near_q_ref, far_ref)
    lane9 = lane[:rows]
    here = lax.axis_index("lon")
    from_e = from_w = met_refs[0][sz.size :]
    for k, met_ref in enumerate(met_refs):
        eastward = lax.rem(sz.partner(k) - here + sz.n_lon, sz.n_lon)
        pole_in[eastward] = met_ref[sz.size + 8 :]
        from_e = jnp.where(sz.partner(k) == lax.rem(here + 1, sz.n_lon), met_ref[sz.size :], from_e)
        from_w = jnp.where(sz.partner(k) == lax.rem(here + sz.n_lon - 1, sz.n_lon), met_ref[sz.size :], from_w)
    for place, f in enumerate((0, 5, 2, 3, 4)):
        after = pltpu.roll(from_e, (sz.tail - LEVELS * place) % LANES, 1)[:rows]
        before = pltpu.roll(from_w, (LANES - LEVELS - LEVELS * place) % LANES, 1)[:rows]
        own = ext[f, :rows, sz.end :]
        edge = jnp.where(lane9 < LANES - LEVELS, after, before)
        ext[f, :rows, sz.end :] = jnp.where(lane9 < sz.tail, own, edge)
    inv_cos, sin_centre, cos_face = geo_ref[band, 0], geo_ref[band, 1], geo_ref[band, 2]
    ratio = sz.ratio

    plain, alone = masks_ref[0], masks_ref[1]
    if sz.near_only:
        band = lax.axis_index("lat")
        low = band < sz.n_lat // 2
        pole_cos = jnp.where(low, inv_cos[:1], inv_cos[rows - 1 : rows])
        kept_waves = pole_waves(sz, pole_in.at[:, rows - 8 :], pole_cos, jnp.where(low, 1.0, -1.0))

    def stepped(f, t, value, tend):
        value = value + plain * tend
        if sz.near_only:
            level, cosine, sine = kept_waves[f]
            wave = level + cosine * wave_ref[0, t : t + 1] + sine * wave_ref[1, t : t + 1]
            value = value + alone * wave
        return value

    def tile(f, t):
        return ext[f, :, LANES * t : LANES * (t + 1)]

    kept = {}

    def zonal(t):
        if t not in kept:
            thick_e = ring.east("h", t, functools.partial(tile, 0))
            wind_e = ring.east("u", t, functools.partial(tile, 5))
            flux = 0.25 * (tile(5, t) + wind_e) * (tile(0, t) + thick_e) * inv_cos
            parts = []
            for k in range(3):
                q = tile(2 + k, t)
                q_e = ring.east(k, t, functools.partial(tile, 2 + k))
                parts.append(DIFFUSION * (q_e - q) - flux * (0.5 * (q + q_e)))
            kept[t] = (flux, thick_e, parts)
        return kept[t]

    for t in range(tiles):
        span = sz.span(t)
        lanes = slice(LANES * t, LANES * t + span)
        flux, thick_e, parts = zonal(t)
        thick, wind_u, wind_v = tile(0, t), tile(5, t), tile(1, t)
        flux_w = ring.west("f", t, lambda s: zonal(s)[0])
        thick_w = ring.west("hw", t, functools.partial(tile, 0))
        thick_n = north(thick)
        flux_n = (0.25 * ratio) * (wind_v + north(wind_v)) * (thick + thick_n) * cos_face
        thick_tend = -((flux - flux_w) + (flux_n - south(flux_n)) * inv_cos)
        wind_u_tend = sin_centre * wind_v - (thick_e - thick_w) * (0.5 * inv_cos)
        wind_v_tend = -sin_centre * wind_u - (0.5 * ratio) * (thick_n - south(thick))
        new_h_ref[:, lanes] = stepped(0, t, thick, thick_tend)[:rows, :span]
        new_w_ref[0, :, lanes] = stepped(1, t, wind_u, wind_u_tend)[:rows, :span]
        new_w_ref[1, :, lanes] = stepped(2, t, wind_v, wind_v_tend)[:rows, :span]
        for k in range(3):
            q = tile(2 + k, t)
            q_n = north(q)
            zonal_part = parts[k] - ring.west(("p", k), t, lambda s: zonal(s)[2][k])
            lap = q_n + south(q) - 2.0 * q
            over = flux_n * (0.5 * (q + q_n))
            merid_part = DIFFUSION * lap - (over - south(over)) * inv_cos
            mass = thick * q + TIME_STEP * (zonal_part + merid_part)
            mass_ref[k, :, lanes] = mass[:rows, :span].astype(jnp.bfloat16)


def sin_pi(y):
    y = jnp.where(y > 0.5, 1.0 - y, jnp.where(y < -0.5, -1.0 - y, y))
    s = y * y
    series = [(-1) ** i * math.pi ** (2 * i + 1) / math.factorial(2 * i + 1) for i in range(7)]
    total = series[-1]
    for factor in reversed(series[:-1]):
        total = total * s + factor
    return total * y


def share_of(sz, i):
    unit = lax.axis_index("lon") * sz.share + i
    return unit // sz.work, sz.first() + lax.rem(unit, sz.work)


def weights_kernel(sz, cut_ref, n_ref, inverse_ref, after_ref, weights_ref, masks_ref):
    band = lax.axis_index("lat")
    row = lax.broadcasted_iota(jnp.int32, (EXT_ROWS, LANES), 0)
    cuts = jnp.full((EXT_ROWS, LANES), sz.nlon // 2, jnp.int32)
    for j in range(sz.rows):
        cuts = jnp.where(row == j, cut_ref[band * sz.rows + j], cuts)
    plain, alone = cuts >= sz.nlon // 2, sz.at_pole(row)
    masks_ref[0] = jnp.where(plain, TIME_STEP, 0.0)
    masks_ref[1] = jnp.where(alone, TIME_STEP, 0.0)
    masks_ref[2] = jnp.where(plain | alone, 0.0, TIME_STEP)
    size = PER_TILE * sz.stack
    for i in range(sz.share):
        width = (2 * cut_ref[band * sz.rows + share_of(sz, i)[1]] + 1).astype(jnp.float32)
        n = n_ref[...]
        turns = n * width
        turns = turns - jnp.round(turns * (0.5 / sz.nlon)) * (2.0 * sz.nlon)
        weights = sin_pi(turns * (1.0 / sz.nlon)) * inverse_ref[...]
        weights = jnp.where(n == 0.0, width * (1.0 / sz.nlon), weights)
        weights_ref[size * i : size * (i + 1)] = weights.astype(jnp.bfloat16)


def filter_kernel(sz, weights_ref, geo_ref, after_ref, also_after_ref, *refs):
    n_lon, stack, share = sz.n_lon, sz.stack, sz.share
    in_refs, out_refs, (gathered, results) = refs[:n_lon], refs[n_lon : 2 * n_lon], refs[2 * n_lon :]
    for k, in_ref in enumerate(in_refs):
        gathered[sz.partner(k)] = in_ref[: sz.size]

    band = lax.axis_index("lat")
    lane = lax.broadcasted_iota(jnp.int32, (share, LANES), 1)
    place = lax.broadcasted_iota(jnp.int32, (share, LANES), 0)
    by_flux = by_thick = jnp.zeros((share, LANES), jnp.float32)
    for i in range(share):
        field, row = share_of(sz, i)
        inv_cos = geo_ref[band, 0, pl.ds(row, 1), :]
        by_flux = jnp.where((place == i) & (field == 0), inv_cos, by_flux)
        by_thick = jnp.where((place == i) & (field == 1), 0.5 * inv_cos, by_thick)
    sides = [gathered[s, pl.ds(sz.tiles - 1, share, stride=stack), :] for s in range(n_lon)]

    def column(s, k):
        return pltpu.roll(sides[s % n_lon], (-sz.tail - LEVELS * k) % LANES, 1)

    for s in range(n_lon):
        thick_w, thick_e = column(s, 1), column(s + 1, 0)
        flux = 0.25 * (column(s, 3) + column(s + 1, 2)) * (thick_w + thick_e) * by_flux
        west_of, east_of = flux + by_thick * thick_e, flux + by_thick * thick_w
        at = pl.ds(sz.tiles - 1, share, stride=stack)
        own = gathered[s, at, :]
        own = own - jnp.where(lane >= sz.tail - LEVELS, pltpu.roll(west_of, sz.tail - LEVELS, 1), 0.0)
        gathered[s, at, :] = jnp.where(lane < sz.tail, own, 0.0)
        at = pl.ds(0, share, stride=stack)
        after = (s + 1) % n_lon
        gathered[after, at, :] = gathered[after, at, :] + jnp.where(lane < LEVELS, east_of, 0.0)

    wide = lax.broadcasted_iota(jnp.int32, (stack, LANES), 1)
    rows = PER_TILE * stack
    for i in range(share):
        here = slice(stack * i, stack * (i + 1))
        pieces = [gathered[s, here].astype(jnp.bfloat16) for s in range(n_lon)]
        circle = jnp.concatenate([jnp.concatenate(pieces[s:] + pieces[:s], axis=0) for s in range(n_lon)], axis=1)
        spread = jnp.dot(weights_ref[rows * i : rows * (i + 1)], circle, preferred_element_type=jnp.float32)
        for s in range(n_lon):
            same = spread[:stack, LANES * s : LANES * (s + 1)]
            carried = None
            for e in range(1, PER_TILE):
                part = spread[stack * e : stack * (e + 1), LANES * s : LANES * (s + 1)]
                part = pltpu.roll(part, LEVELS * e, 1)
                inside = wide >= LEVELS * e
                same = same + jnp.where(inside, part, 0.0)
                over = jnp.where(inside, 0.0, part)
                carried = over if carried is None else carried + over
            results[s, here] = pltpu.roll(same, stack - 1, 0) + carried
    for k, out_ref in enumerate(out_refs):
        out_ref[...] = results[sz.partner(k)]


def finish_kernel(sz, masks_ref, base_w_ref, base_h_ref, *refs):
    back_refs, (new_w_ref, new_h_ref, back_ref) = refs[: sz.n_lon], refs[sz.n_lon :]
    rows, work = sz.rows, sz.work
    for k, ref in enumerate(back_refs):
        back_ref[sz.piece(k), :] = ref[...]
    scale = masks_ref[2]
    even = lax.rem(lax.axis_index("lat"), 2) == 0
    for f in range(3):
        for t in range(sz.tiles):
            span = sz.span(t)
            lanes = slice(LANES * t, LANES * t + span)
            tend = back_ref[pl.ds(sz.stack * work * f + t, work, stride=sz.stack), :]
            if sz.near_only:
                tend = jnp.concatenate([tend, jnp.zeros((EXT_ROWS - work, LANES), jnp.float32)], axis=0)
                tend = jnp.where(even, south(tend), tend)
            change = (scale[:rows] * tend[:rows])[:, :span]
            if f == 0:
                new_h_ref[:, lanes] = base_h_ref[:, lanes] + change
            else:
                new_w_ref[:, f - 1, lanes] = base_w_ref[f - 1, :, lanes] + change


def local(winds, thickness, tracers, cutoff):
    n_lat = lax.axis_size("lat")
    n_lon = lax.axis_size("lon")
    rows, merged = thickness.shape
    sz = Sizes(rows, merged, n_lat, n_lon)
    f32 = jnp.float32
    vmem = pl.BlockSpec(memory_space=pltpu.VMEM)
    smem = pl.BlockSpec(memory_space=pltpu.SMEM)
    hbm = pl.BlockSpec(memory_space=pltpu.HBM)
    anywhere = pl.BlockSpec(memory_space=pl.ANY)

    def shaped(*shape):
        return jax.ShapeDtypeStruct(shape, f32)

    def call(kernel, name, in_specs, out_shape, scratch=(), limit=LIMIT):
        return pl.pallas_call(
            functools.partial(kernel, sz),
            out_shape=out_shape,
            in_specs=in_specs,
            out_specs=jax.tree.map(lambda _: vmem, out_shape),
            scratch_shapes=list(scratch),
            compiler_params=pltpu.CompilerParams(vmem_limit_bytes=limit),
            name=name,
        )

    geo = jnp.asarray(geometry(sz))
    wave = jnp.asarray(waves(sz))
    n, inverse = (jnp.asarray(table) for table in offsets(sz))

    wind_rows = jnp.swapaxes(winds, 0, 1)
    tracer_rows = jnp.swapaxes(tracers, 0, 1)
    far_row, near_row = shaped(5 * sz.stack, LANES), shaped(3 * sz.stack, LANES)
    kept = [((1,), f32), ((2,), f32), ((3,), jnp.bfloat16)]
    near_q, far_rows, sides = call(
        edges_kernel,
        "edges",
        [hbm] * 3,
        (near_row, far_row, shaped(2 * EXT_ROWS, LANES)),
        [pltpu.VMEM((2,) + count + (merged,), dtype) for count, dtype in kept]
        + [
            pltpu.VMEM((rows,) + (count if count != (1,) else ()) + (lanes,), dtype)
            for lanes in (LANES, sz.tail)
            for count, dtype in kept
        ]
        + [pltpu.SemaphoreType.DMA((3, 4))],
        limit=MOST_VMEM,
    )(thickness, wind_rows, tracer_rows)

    near = [(band * n_lon + i, (band ^ 1) * n_lon + i) for band in range(n_lat) for i in range(n_lon)]
    far = []
    for band in range(n_lat):
        other = band - 1 if band % 2 == 0 else band + 1
        for i in range(n_lon):
            if 0 <= other < n_lat:
                far.append((band * n_lon + i, other * n_lon + i))
            else:
                far.append((band * n_lon + i, band * n_lon + (i + n_lon // 2) % n_lon))
    near_h = lax.ppermute(thickness, ("lat", "lon"), near)
    near_w = lax.ppermute(wind_rows, ("lat", "lon"), near)
    if not sz.near_only:
        far_rows = lax.ppermute(far_rows, ("lat", "lon"), far)

    order = [sz.turns(False), sz.turns(True)]

    def meetings(shares):
        got = [shares[0]]
        for k in range(1, n_lon):
            sectors = [(band, i, i ^ order[band % 2][k]) for band in range(n_lat) for i in range(n_lon)]
            got.append(lax.ppermute(shares[k], ("lat", "lon"), [(b * n_lon + i, b * n_lon + j) for b, i, j in sectors]))
        return got

    all_pieces = pltpu.VMEM((n_lon, sz.size, LANES), f32)
    *tends, far_rows, near_q = call(
        polar_kernel,
        "polar",
        [vmem] * 9,
        [shaped(sz.size + EXT_ROWS, LANES)] * n_lon + [far_row, near_row],
        [
            pltpu.VMEM((n_lon * sz.size, LANES), f32),
            pltpu.VMEM((4 * sz.stack, LANES), f32),
            pltpu.VMEM((3, EXT_ROWS, sz.tiles * LANES), f32),
        ],
    )(thickness, wind_rows, near_h, near_w, sides, geo, wave, far_rows, near_q)
    met = meetings(tends)
    near_q = lax.ppermute(near_q, ("lat", "lon"), near)
    from_far = lax.ppermute(far_rows, ("lat", "lon"), far) if sz.near_only else far_rows
    weights, masks = call(
        weights_kernel,
        "weights",
        [smem, vmem, vmem, anywhere],
        (
            jax.ShapeDtypeStruct((sz.share * PER_TILE * sz.stack, n_lon * sz.stack), jnp.bfloat16),
            shaped(3, EXT_ROWS, LANES),
        ),
    )(cutoff, n, inverse, tends[0])
    worked = call(
        filter_kernel,
        "filter",
        [vmem] * 2 + [anywhere] * 2 + [vmem] * n_lon,
        [shaped(sz.size, LANES)] * n_lon,
        [all_pieces, all_pieces],
    )(weights, geo, from_far, near_q, *met)
    back = meetings(worked)

    base_w, base_h, mass = call(
        rest_kernel,
        "rest",
        [vmem] * 10 + [anywhere] + [vmem] * n_lon,
        (shaped(2, rows, merged), shaped(rows, merged), jax.ShapeDtypeStruct(tracers.shape, jnp.bfloat16)),
        [pltpu.VMEM((6, EXT_ROWS, sz.tiles * LANES), f32), pltpu.VMEM((n_lon, 8, LANES), f32)],
    )(masks, thickness, wind_rows, tracers, near_h, near_w, near_q, from_far, geo, wave, worked[0], *met)

    new_w, new_h = call(
        finish_kernel,
        "finish",
        [vmem] * (3 + n_lon),
        (shaped(*wind_rows.shape), shaped(rows, merged)),
        [pltpu.VMEM((n_lon * sz.size, LANES), f32)],
    )(masks, base_w, base_h, *back)
    return jnp.swapaxes(new_w, 0, 1), new_h, mass


def solution(mesh):
    in_specs = (P(None, "lat", "lon"), P("lat", "lon"), P(None, "lat", "lon"), P())
    out_specs = (P(None, "lat", "lon"), P("lat", "lon"), P(None, "lat", "lon"))
    return jax.shard_map(local, mesh=mesh, in_specs=in_specs, out_specs=out_specs, check_vma=False)
```

```python
import functools
import math

import jax
import jax.numpy as jnp
import numpy as np
from jax import lax
from jax.experimental import pallas as pl
from jax.experimental.pallas import tpu as pltpu
from jax.sharding import PartitionSpec as P

LEVELS = 16
TIME_STEP = 0.05
DIFFUSION = 0.5
LANES = 128
PER_TILE = LANES // LEVELS
EXT_ROWS = 16
LIMIT = 48 * 1024 * 1024
MOST_VMEM = 64 * 1024 * 1024 - 10500 * 1024


class Sizes:
    def __init__(self, rows, merged, n_lat, n_lon):
        self.rows = rows
        self.merged = merged
        self.columns = merged // LEVELS
        self.n_lat = n_lat
        self.n_lon = n_lon
        self.nlat = rows * n_lat
        self.nlon = self.columns * n_lon
        self.ratio = 2.0 * self.nlat / self.nlon
        self.tiles = -(-merged // LANES)
        self.end = (self.tiles - 1) * LANES
        self.tail = merged - self.end
        self.stack = -(-(self.tiles + 1) // 8) * 8
        self.near_only = rows <= self.nlat // 6 < 2 * rows
        self.work = rows - 1 if self.near_only else rows
        self.units = 3 * self.work
        self.share = -(-self.units // n_lon)
        self.size = self.share * self.stack
        assert self.tail <= LANES - 4 * LEVELS and rows + 2 <= EXT_ROWS and n_lat % 2 == 0
        assert n_lon >= 4 and n_lon & (n_lon - 1) == 0

    def span(self, tile):
        return self.tail if tile == self.tiles - 1 else LANES

    def first(self):
        return jnp.where(lax.rem(lax.axis_index("lat"), 2) == 0, 1, 0) if self.near_only else 0

    def at_pole(self, row):
        band = lax.axis_index("lat")
        pole = jnp.where(band == 0, 0, jnp.where(band == self.n_lat - 1, self.rows - 1, -1))
        return row == (pole if self.near_only else -1)

    def turns(self, odd):
        middle = list(range(1, self.n_lon - 1))
        return [0, self.n_lon - 1] + (middle[::-1] if odd else middle)

    def partner(self, k):
        odd = lax.rem(lax.axis_index("lat"), 2) == 1
        turn = jnp.where(odd, self.turns(True)[k], self.turns(False)[k])
        return jnp.bitwise_xor(lax.axis_index("lon"), turn)

    def piece(self, k):
        return pl.ds(pl.multiple_of(self.partner(k) * self.size, 8), self.size)


def geometry(sz):
    table = np.zeros((sz.n_lat, 3, EXT_ROWS, LANES), np.float64)

    def face(j):
        return math.sin((j + 1) * math.pi / sz.nlat) if 0 <= j < sz.nlat - 1 else 0.0

    for band in range(sz.n_lat):
        for row in range(sz.rows):
            j = band * sz.rows + row
            centre = (j + 0.5) * math.pi / sz.nlat - math.pi / 2
            table[band, 0, row] = 1.0 / math.cos(centre)
            table[band, 1, row] = math.sin(centre)
            table[band, 2, row] = face(j)
        table[band, 2, EXT_ROWS - 1] = face(band * sz.rows - 1)
    return table.astype(np.float32)


def offsets(sz):
    shift, out_tile = np.divmod(np.arange(PER_TILE * sz.stack), sz.stack)
    sector, in_tile = np.divmod(np.arange(sz.n_lon * sz.stack), sz.stack)
    n = (PER_TILE * (out_tile - 1) + shift)[:, None] - (PER_TILE * in_tile + sz.columns * sector)[None, :]
    n = (n + sz.nlon // 2) % sz.nlon - sz.nlon // 2
    with np.errstate(divide="ignore"):
        inverse = np.where(n == 0, 0.0, 1.0 / (sz.nlon * np.sin(np.pi * n / sz.nlon)))
    return n.astype(np.float32), inverse.astype(np.float32)


def waves(sz):
    column = PER_TILE * np.arange(sz.stack)[:, None] + np.arange(LANES)[None, :] // LEVELS
    angle = 2 * np.pi * column / sz.nlon
    return np.stack([np.cos(angle), np.sin(angle)]).astype(np.float32)


def edges_kernel(sz, h_hbm, w_hbm, q_hbm, near_ref, far_ref, sides_ref, *scratch):
    row_refs, first_refs, last_refs, sems = scratch[:3], scratch[3:6], scratch[6:9], scratch[9]
    rows, last = sz.rows, sz.rows - 1
    even = lax.rem(lax.axis_index("lat"), 2) == 0
    copies = []
    for i, source in enumerate((h_hbm, w_hbm, q_hbm)):
        for k, row in enumerate((0, last)):
            one = source.at[pl.ds(row, 1)] if i == 0 else source.at[row]
            copies.append(pltpu.make_async_copy(one, row_refs[i].at[k], sems.at[i, k]))
        for k, (start, to) in enumerate(((0, first_refs[i]), (sz.end, last_refs[i]))):
            lanes = pl.ds(start, to.shape[-1])
            cut = source.at[:, lanes] if i == 0 else source.at[:, :, lanes]
            copies.append(pltpu.make_async_copy(cut, to, sems.at[i, 2 + k]))
    for copy in copies:
        copy.start()
    for copy in copies:
        copy.wait()
    h_rows, w_rows, q_rows = row_refs
    for t in range(sz.tiles):
        wide = sz.span(t)
        lanes = slice(LANES * t, LANES * t + wide)
        q = [q_rows[k, :, lanes].astype(jnp.float32) for k in range(2)]
        for f in range(5):
            if f == 0:
                first, final = h_rows[0, :, lanes], h_rows[1, :, lanes]
            elif f == 1:
                first, final = w_rows[0, 1:2, lanes], w_rows[1, 1:2, lanes]
            else:
                first, final = q[0][f - 2 : f - 1], q[1][f - 2 : f - 1]
                at = sz.stack * (f - 2) + t
                near_ref[at : at + 1, :wide] = jnp.where(even, final, first)
            at = sz.stack * f + t
            far_ref[at : at + 1, :wide] = jnp.where(even, first, final)
    sides_ref[...] = jnp.zeros(sides_ref.shape, jnp.float32)
    for k, (refs, at) in enumerate(((first_refs, 0), (last_refs, sz.tail - LEVELS))):
        columns = slice(at, at + LEVELS)
        for f in range(5):
            if f == 0:
                value = refs[0][:, columns]
            elif f == 1:
                value = refs[1][:, 0, columns]
            else:
                value = refs[2][:, f - 2, columns].astype(jnp.float32)
            sides_ref[EXT_ROWS * k : EXT_ROWS * k + rows, LEVELS * f : LEVELS * (f + 1)] = value


def add_rows(sz, ext, near_h_ref, near_w_ref, near_q_ref, far_ref):
    band = lax.axis_index("lat")
    even = lax.rem(band, 2) == 0
    over_pole = (band == 0) | (band == sz.n_lat - 1)
    last = sz.rows - 1
    for f in range(2 if near_q_ref is None else 5):
        flip = jnp.where(over_pole, -1.0, 1.0) if f == 1 else 1.0
        for t in range(sz.tiles):
            lanes = slice(LANES * t, LANES * t + sz.span(t))
            if f == 0:
                near = jnp.where(even, near_h_ref[0:1, lanes], near_h_ref[last : sz.rows, lanes])
            elif f == 1:
                near = jnp.where(even, near_w_ref[0, 1:2, lanes], near_w_ref[last, 1:2, lanes])
            else:
                at = sz.stack * (f - 2) + t
                near = near_q_ref[at : at + 1, : sz.span(t)]
            at = sz.stack * f + t
            far = jnp.zeros_like(near) if far_ref is None else far_ref[at : at + 1, : sz.span(t)] * flip
            ext[f, sz.rows : sz.rows + 1, lanes] = jnp.where(even, near, far)
            ext[f, EXT_ROWS - 1 : EXT_ROWS, lanes] = jnp.where(even, far, near)


class Tiles:
    def __init__(self, sz):
        self.sz = sz
        self.lane = lax.broadcasted_iota(jnp.int32, (EXT_ROWS, LANES), 1)
        self.turned = {}

    def turn(self, name, t, value, step):
        key = (name, t % self.sz.tiles, step)
        if key not in self.turned:
            self.turned[key] = pltpu.roll(value(t % self.sz.tiles), step % LANES, 1)
        return self.turned[key]

    def east(self, name, t, value):
        here = self.turn(name, t, value, -LEVELS)
        return jnp.where(self.lane < LANES - LEVELS, here, self.turn(name, t + 1, value, -LEVELS))

    def west(self, name, t, value):
        here = self.turn(name, t, value, LEVELS)
        return jnp.where(self.lane >= LEVELS, here, self.turn(name, t - 1, value, LEVELS))


def north(value):
    return pltpu.roll(value, EXT_ROWS - 1, 0)


def south(value):
    return pltpu.roll(value, 1, 0)


def polar_kernel(sz, h_ref, w_ref, near_h_ref, near_w_ref, sides_ref, geo_ref, wave_ref, far_ref, near_q_ref, *refs):
    out_refs, (far_out, near_out, tend_ref, pole_ref, ext) = refs[:-5], refs[-5:]
    far_out[...] = far_ref[...]
    near_out[...] = near_q_ref[...]
    if sz.near_only:
        far_ref = None
    band = lax.axis_index("lat")
    ring = Tiles(sz)
    lane = ring.lane
    tiles, stack, rows, work = sz.tiles, sz.stack, sz.rows, sz.work
    even = lax.rem(band, 2) == 0
    for f, value in enumerate((h_ref[...], w_ref[:, 1, :], w_ref[:, 0, :])):
        ext[f, :rows, sz.end :] = jnp.zeros((rows, LANES), jnp.float32)
        ext[f, :rows, : sz.merged] = value
    add_rows(sz, ext, near_h_ref, near_w_ref, None, far_ref)
    inv_cos, sin_centre, cos_face = geo_ref[band, 0], geo_ref[band, 1], geo_ref[band, 2]
    ratio = sz.ratio

    def tile(f, t):
        return ext[f, :, LANES * t : LANES * (t + 1)]

    kept = {}

    def zonal(t):
        if t not in kept:
            thick_e = ring.east("h", t, functools.partial(tile, 0))
            wind_e = ring.east("u", t, functools.partial(tile, 2))
            flux = 0.25 * (tile(2, t) + wind_e) * (tile(0, t) + thick_e) * inv_cos
            if t == tiles - 1:
                flux = jnp.where(lane < sz.tail - LEVELS, flux, 0.0)
            kept[t] = (flux, thick_e)
        return kept[t]

    for t in range(tiles):
        flux, thick_e = zonal(t)
        thick, wind_v, wind_u = tile(0, t), tile(1, t), tile(2, t)
        flux_w = ring.west("f", t, lambda s: zonal(s)[0])
        thick_w = ring.west("hw", t, functools.partial(tile, 0))
        thick_n = north(thick)
        flux_n = (0.25 * ratio) * (wind_v + north(wind_v)) * (thick + thick_n) * cos_face
        thick_tend = -((flux - flux_w) + (flux_n - south(flux_n)) * inv_cos)
        wind_u_tend = sin_centre * wind_v - (thick_e - thick_w) * (0.5 * inv_cos)
        wind_v_tend = -sin_centre * wind_u - (0.5 * ratio) * (thick_n - south(thick))
        spare = 0.0
        if t == tiles - 1:
            last = sz.tail - LEVELS
            columns = [(tile(0, 0), 0), (thick, last), (tile(2, 0), 0), (wind_u, last)]
            for k, (source, at) in reversed(list(enumerate(columns))):
                to = sz.tail + LEVELS * k
                spare = jnp.where(lane < to + LEVELS, pltpu.roll(source, (to - at) % LANES, 1), spare)
        for f, tend in enumerate((thick_tend, wind_u_tend, wind_v_tend, thick)):
            if sz.near_only:
                alone = jnp.where(band < sz.n_lat // 2, tend[:1], tend[rows - 1 : rows])
                if t == tiles - 1:
                    alone = jnp.where(lane[:1] < sz.tail, alone, 0.0)
                pole_ref[stack * f + t : stack * f + t + 1] = alone
            if f == 3:
                continue
            if t == tiles - 1:
                tend = jnp.where(lane < sz.tail, tend, spare)
            if sz.near_only:
                tend = jnp.where(even, north(tend), tend)
            tend_ref[pl.ds(stack * work * f + t, work, stride=stack), :] = tend[:work]
    for f in range(3):
        for t in range(tiles, stack):
            tend_ref[pl.ds(stack * work * f + t, work, stride=stack), :] = jnp.zeros((work, LANES), jnp.float32)
    used = stack * sz.units
    if used < tend_ref.shape[0]:
        tend_ref[used:, :] = jnp.zeros((tend_ref.shape[0] - used, LANES), jnp.float32)
    sides = [sides_ref[:EXT_ROWS], sides_ref[EXT_ROWS:]]
    if sz.near_only:
        sums = pole_sums(sz, pole_ref, wave_ref, spare, band)
        row = lax.broadcasted_iota(jnp.int32, (EXT_ROWS, LANES), 0)
        for k, total in enumerate(sums):
            sides = [jnp.where(row == rows + k, total, side) for side in sides]
    here = lax.axis_index("lon")
    for k, out_ref in enumerate(out_refs):
        out_ref[: sz.size] = tend_ref[sz.piece(k), :]
        eastward = sz.partner(k) == lax.rem(here + 1, sz.n_lon)
        out_ref[sz.size :] = jnp.where(eastward, sides[1], sides[0])


def pole_sums(sz, pole_ref, wave_ref, spare, band):
    stack, rows = sz.stack, sz.rows
    lane = lax.broadcasted_iota(jnp.int32, (1, LANES), 1)
    sides = jnp.where(band < sz.n_lat // 2, spare[:1], spare[rows - 1 : rows])
    found = [jnp.zeros((1, LANES), jnp.float32), pltpu.roll(sides, (LANES // 2 - sz.tail) % LANES, 1)]
    for f in range(4):
        if sz.tiles < stack:
            pole_ref[stack * f + sz.tiles : stack * (f + 1)] = jnp.zeros((stack - sz.tiles, LANES), jnp.float32)
        values = pole_ref[stack * f : stack * (f + 1)]
        for k, terms in enumerate((values, values * wave_ref[0], values * wave_ref[1])):
            total = jnp.sum(terms, axis=0, keepdims=True)
            for step in (64, 32, 16):
                total = total + pltpu.roll(total, step, 1)
            row, place = divmod(3 * f + k, PER_TILE)
            inside = (lane >= LEVELS * place) & (lane < LEVELS * (place + 1))
            found[row] = jnp.where(inside, total, found[row])
    return found


def pole_waves(sz, rows_in, inv_cos, sign):
    n_lon = sz.n_lon
    lane = lax.broadcasted_iota(jnp.int32, (1, LANES), 1)

    def value(s, place):
        row, at = divmod(place, PER_TILE)
        return pltpu.roll(rows_in[s % n_lon, row : row + 1], (-LEVELS * at) % LANES, 1)

    theta = 2 * math.pi / sz.nlon
    ends = (1.0, math.cos(theta * (sz.columns - 1)), math.sin(theta * (sz.columns - 1)))
    sums = [[[value(s, 3 * f + k) for k in range(3)] for f in range(4)] for s in range(n_lon)]
    for s in range(n_lon):
        thick_w, thick_e = value(s, 13), value(s + 1, 12)
        flux = 0.25 * (value(s, 15) + value(s + 1, 14)) * (thick_w + thick_e) * inv_cos
        slope = 0.5 * inv_cos
        after = (s + 1) % n_lon
        for f, (west_of, east_of) in enumerate(((flux, flux), (slope * thick_e, slope * thick_w))):
            for k in range(3):
                sums[s][f][k] = sums[s][f][k] - west_of * ends[k]
            for k in range(2):
                sums[after][f][k] = sums[after][f][k] + east_of
    result = []
    for f in range(3):
        waves_of = [0.0, 0.0, 0.0]
        for s in range(n_lon):
            level, cosine, sine = sums[s][f]
            if f == 2:
                level = level + (0.5 * sz.ratio) * sign * sums[s][3][0]
                cosine = cosine - (0.5 * sz.ratio) * sign * sums[s][3][1]
                sine = sine - (0.5 * sz.ratio) * sign * sums[s][3][2]
            c, d = math.cos(2 * math.pi * s / n_lon), math.sin(2 * math.pi * s / n_lon)
            waves_of[0] = waves_of[0] + level
            waves_of[1] = waves_of[1] + (c * cosine - d * sine)
            waves_of[2] = waves_of[2] + (d * cosine + c * sine)
        spread = []
        for k, total in enumerate(waves_of):
            total = jnp.where(lane < LEVELS, total * ((1.0 if k == 0 else 2.0) / sz.nlon), 0.0)
            for step in (16, 32, 64):
                total = total + pltpu.roll(total, step, 1)
            spread.append(total)
        result.append(spread)
    return result


def rest_kernel(sz, masks_ref, h_ref, w_ref, q_ref, near_h_ref, near_w_ref, near_q_ref, far_ref, geo_ref, wave_ref, after_ref, *refs):
    met_refs, (new_w_ref, new_h_ref, mass_ref, ext, pole_in) = refs[: sz.n_lon], refs[sz.n_lon :]
    band = lax.axis_index("lat")
    ring = Tiles(sz)
    lane = ring.lane
    tiles, rows = sz.tiles, sz.rows
    for f in range(6):
        if f < 2 or f == 5:
            value = (h_ref[...], w_ref[:, 1, :], w_ref[:, 0, :])[min(f, 2)]
        else:
            value = q_ref[f - 2].astype(jnp.float32)
        ext[f, :rows, : sz.merged] = value
    add_rows(sz, ext, near_h_ref, near_w_ref, near_q_ref, far_ref)
    lane9 = lane[:rows]
    here = lax.axis_index("lon")
    from_e = from_w = met_refs[0][sz.size :]
    for k, met_ref in enumerate(met_refs):
        eastward = lax.rem(sz.partner(k) - here + sz.n_lon, sz.n_lon)
        pole_in[eastward] = met_ref[sz.size + 8 :]
        from_e = jnp.where(sz.partner(k) == lax.rem(here + 1, sz.n_lon), met_ref[sz.size :], from_e)
        from_w = jnp.where(sz.partner(k) == lax.rem(here + sz.n_lon - 1, sz.n_lon), met_ref[sz.size :], from_w)
    for place, f in enumerate((0, 5, 2, 3, 4)):
        after = pltpu.roll(from_e, (sz.tail - LEVELS * place) % LANES, 1)[:rows]
        before = pltpu.roll(from_w, (LANES - LEVELS - LEVELS * place) % LANES, 1)[:rows]
        own = ext[f, :rows, sz.end :]
        edge = jnp.where(lane9 < LANES - LEVELS, after, before)
        ext[f, :rows, sz.end :] = jnp.where(lane9 < sz.tail, own, edge)
    inv_cos, sin_centre, cos_face = geo_ref[band, 0], geo_ref[band, 1], geo_ref[band, 2]
    ratio = sz.ratio

    plain, alone = masks_ref[0], masks_ref[1]
    if sz.near_only:
        band = lax.axis_index("lat")
        low = band < sz.n_lat // 2
        pole_cos = jnp.where(low, inv_cos[:1], inv_cos[rows - 1 : rows])
        kept_waves = pole_waves(sz, pole_in.at[:, rows - 8 :], pole_cos, jnp.where(low, 1.0, -1.0))

    def stepped(f, t, value, tend):
        value = value + plain * tend
        if sz.near_only:
            level, cosine, sine = kept_waves[f]
            wave = level + cosine * wave_ref[0, t : t + 1] + sine * wave_ref[1, t : t + 1]
            value = value + alone * wave
        return value

    def tile(f, t):
        return ext[f, :, LANES * t : LANES * (t + 1)]

    kept = {}

    def zonal(t):
        if t not in kept:
            thick_e = ring.east("h", t, functools.partial(tile, 0))
            wind_e = ring.east("u", t, functools.partial(tile, 5))
            flux = 0.25 * (tile(5, t) + wind_e) * (tile(0, t) + thick_e) * inv_cos
            parts = []
            for k in range(3):
                q = tile(2 + k, t)
                q_e = ring.east(k, t, functools.partial(tile, 2 + k))
                parts.append(DIFFUSION * (q_e - q) - flux * (0.5 * (q + q_e)))
            kept[t] = (flux, thick_e, parts)
        return kept[t]

    for t in range(tiles):
        span = sz.span(t)
        lanes = slice(LANES * t, LANES * t + span)
        flux, thick_e, parts = zonal(t)
        thick, wind_u, wind_v = tile(0, t), tile(5, t), tile(1, t)
        flux_w = ring.west("f", t, lambda s: zonal(s)[0])
        thick_w = ring.west("hw", t, functools.partial(tile, 0))
        thick_n = north(thick)
        flux_n = (0.25 * ratio) * (wind_v + north(wind_v)) * (thick + thick_n) * cos_face
        thick_tend = -((flux - flux_w) + (flux_n - south(flux_n)) * inv_cos)
        wind_u_tend = sin_centre * wind_v - (thick_e - thick_w) * (0.5 * inv_cos)
        wind_v_tend = -sin_centre * wind_u - (0.5 * ratio) * (thick_n - south(thick))
        new_h_ref[:, lanes] = stepped(0, t, thick, thick_tend)[:rows, :span]
        new_w_ref[0, :, lanes] = stepped(1, t, wind_u, wind_u_tend)[:rows, :span]
        new_w_ref[1, :, lanes] = stepped(2, t, wind_v, wind_v_tend)[:rows, :span]
        for k in range(3):
            q = tile(2 + k, t)
            q_n = north(q)
            zonal_part = parts[k] - ring.west(("p", k), t, lambda s: zonal(s)[2][k])
            lap = q_n + south(q) - 2.0 * q
            over = flux_n * (0.5 * (q + q_n))
            merid_part = DIFFUSION * lap - (over - south(over)) * inv_cos
            mass = thick * q + TIME_STEP * (zonal_part + merid_part)
            mass_ref[k, :, lanes] = mass[:rows, :span].astype(jnp.bfloat16)


def sin_pi(y):
    y = jnp.where(y > 0.5, 1.0 - y, jnp.where(y < -0.5, -1.0 - y, y))
    s = y * y
    series = [(-1) ** i * math.pi ** (2 * i + 1) / math.factorial(2 * i + 1) for i in range(7)]
    total = series[-1]
    for factor in reversed(series[:-1]):
        total = total * s + factor
    return total * y


def share_of(sz, i):
    unit = lax.axis_index("lon") * sz.share + i
    return unit // sz.work, sz.first() + lax.rem(unit, sz.work)


def weights_kernel(sz, cut_ref, n_ref, inverse_ref, after_ref, weights_ref, masks_ref):
    band = lax.axis_index("lat")
    row = lax.broadcasted_iota(jnp.int32, (EXT_ROWS, LANES), 0)
    cuts = jnp.full((EXT_ROWS, LANES), sz.nlon // 2, jnp.int32)
    for j in range(sz.rows):
        cuts = jnp.where(row == j, cut_ref[band * sz.rows + j], cuts)
    plain, alone = cuts >= sz.nlon // 2, sz.at_pole(row)
    masks_ref[0] = jnp.where(plain, TIME_STEP, 0.0)
    masks_ref[1] = jnp.where(alone, TIME_STEP, 0.0)
    masks_ref[2] = jnp.where(plain | alone, 0.0, TIME_STEP)
    size = PER_TILE * sz.stack
    for i in range(sz.share):
        width = (2 * cut_ref[band * sz.rows + share_of(sz, i)[1]] + 1).astype(jnp.float32)
        n = n_ref[...]
        turns = n * width
        turns = turns - jnp.round(turns * (0.5 / sz.nlon)) * (2.0 * sz.nlon)
        weights = sin_pi(turns * (1.0 / sz.nlon)) * inverse_ref[...]
        weights = jnp.where(n == 0.0, width * (1.0 / sz.nlon), weights)
        weights_ref[size * i : size * (i + 1)] = weights.astype(jnp.bfloat16)


def pass_kernel(sz, piece_ref, after_ref, also_after_ref, out_ref):
    out_ref[...] = piece_ref[...]


def filter_kernel(sz, weights_ref, geo_ref, *refs):
    n_lon, stack, share = sz.n_lon, sz.stack, sz.share
    in_refs, out_refs, (gathered, results) = refs[:n_lon], refs[n_lon : 2 * n_lon], refs[2 * n_lon :]
    for k, in_ref in enumerate(in_refs):
        gathered[sz.partner(k)] = in_ref[: sz.size]

    band = lax.axis_index("lat")
    lane = lax.broadcasted_iota(jnp.int32, (share, LANES), 1)
    place = lax.broadcasted_iota(jnp.int32, (share, LANES), 0)
    by_flux = by_thick = jnp.zeros((share, LANES), jnp.float32)
    for i in range(share):
        field, row = share_of(sz, i)
        inv_cos = geo_ref[band, 0, pl.ds(row, 1), :]
        by_flux = jnp.where((place == i) & (field == 0), inv_cos, by_flux)
        by_thick = jnp.where((place == i) & (field == 1), 0.5 * inv_cos, by_thick)
    sides = [gathered[s, pl.ds(sz.tiles - 1, share, stride=stack), :] for s in range(n_lon)]

    def column(s, k):
        return pltpu.roll(sides[s % n_lon], (-sz.tail - LEVELS * k) % LANES, 1)

    for s in range(n_lon):
        thick_w, thick_e = column(s, 1), column(s + 1, 0)
        flux = 0.25 * (column(s, 3) + column(s + 1, 2)) * (thick_w + thick_e) * by_flux
        west_of, east_of = flux + by_thick * thick_e, flux + by_thick * thick_w
        at = pl.ds(sz.tiles - 1, share, stride=stack)
        own = gathered[s, at, :]
        own = own - jnp.where(lane >= sz.tail - LEVELS, pltpu.roll(west_of, sz.tail - LEVELS, 1), 0.0)
        gathered[s, at, :] = jnp.where(lane < sz.tail, own, 0.0)
        at = pl.ds(0, share, stride=stack)
        after = (s + 1) % n_lon
        gathered[after, at, :] = gathered[after, at, :] + jnp.where(lane < LEVELS, east_of, 0.0)

    wide = lax.broadcasted_iota(jnp.int32, (stack, LANES), 1)
    rows = PER_TILE * stack
    for i in range(share):
        here = slice(stack * i, stack * (i + 1))
        pieces = [gathered[s, here].astype(jnp.bfloat16) for s in range(n_lon)]
        circle = jnp.concatenate([jnp.concatenate(pieces[s:] + pieces[:s], axis=0) for s in range(n_lon)], axis=1)
        spread = jnp.dot(weights_ref[rows * i : rows * (i + 1)], circle, preferred_element_type=jnp.float32)
        for s in range(n_lon):
            same = spread[:stack, LANES * s : LANES * (s + 1)]
            carried = None
            for e in range(1, PER_TILE):
                part = spread[stack * e : stack * (e + 1), LANES * s : LANES * (s + 1)]
                part = pltpu.roll(part, LEVELS * e, 1)
                inside = wide >= LEVELS * e
                same = same + jnp.where(inside, part, 0.0)
                over = jnp.where(inside, 0.0, part)
                carried = over if carried is None else carried + over
            results[s, here] = pltpu.roll(same, stack - 1, 0) + carried
    for k, out_ref in enumerate(out_refs):
        out_ref[...] = results[sz.partner(k)]


def finish_kernel(sz, masks_ref, base_w_ref, base_h_ref, *refs):
    back_refs, (new_w_ref, new_h_ref, back_ref) = refs[: sz.n_lon], refs[sz.n_lon :]
    rows, work = sz.rows, sz.work
    for k, ref in enumerate(back_refs):
        back_ref[sz.piece(k), :] = ref[...]
    scale = masks_ref[2]
    even = lax.rem(lax.axis_index("lat"), 2) == 0
    for f in range(3):
        for t in range(sz.tiles):
            span = sz.span(t)
            lanes = slice(LANES * t, LANES * t + span)
            tend = back_ref[pl.ds(sz.stack * work * f + t, work, stride=sz.stack), :]
            if sz.near_only:
                tend = jnp.concatenate([tend, jnp.zeros((EXT_ROWS - work, LANES), jnp.float32)], axis=0)
                tend = jnp.where(even, south(tend), tend)
            change = (scale[:rows] * tend[:rows])[:, :span]
            if f == 0:
                new_h_ref[:, lanes] = base_h_ref[:, lanes] + change
            else:
                new_w_ref[:, f - 1, lanes] = base_w_ref[f - 1, :, lanes] + change


def local(winds, thickness, tracers, cutoff):
    n_lat = lax.axis_size("lat")
    n_lon = lax.axis_size("lon")
    rows, merged = thickness.shape
    sz = Sizes(rows, merged, n_lat, n_lon)
    f32 = jnp.float32
    vmem = pl.BlockSpec(memory_space=pltpu.VMEM)
    smem = pl.BlockSpec(memory_space=pltpu.SMEM)
    hbm = pl.BlockSpec(memory_space=pltpu.HBM)
    anywhere = pl.BlockSpec(memory_space=pl.ANY)

    def shaped(*shape):
        return jax.ShapeDtypeStruct(shape, f32)

    def call(kernel, name, in_specs, out_shape, scratch=(), limit=LIMIT):
        return pl.pallas_call(
            functools.partial(kernel, sz),
            out_shape=out_shape,
            in_specs=in_specs,
            out_specs=jax.tree.map(lambda _: vmem, out_shape),
            scratch_shapes=list(scratch),
            compiler_params=pltpu.CompilerParams(vmem_limit_bytes=limit),
            name=name,
        )

    geo = jnp.asarray(geometry(sz))
    wave = jnp.asarray(waves(sz))
    n, inverse = (jnp.asarray(table) for table in offsets(sz))

    wind_rows = jnp.swapaxes(winds, 0, 1)
    tracer_rows = jnp.swapaxes(tracers, 0, 1)
    far_row, near_row = shaped(5 * sz.stack, LANES), shaped(3 * sz.stack, LANES)
    kept = [((1,), f32), ((2,), f32), ((3,), jnp.bfloat16)]
    near_q, far_rows, sides = call(
        edges_kernel,
        "edges",
        [hbm] * 3,
        (near_row, far_row, shaped(2 * EXT_ROWS, LANES)),
        [pltpu.VMEM((2,) + count + (merged,), dtype) for count, dtype in kept]
        + [
            pltpu.VMEM((rows,) + (count if count != (1,) else ()) + (lanes,), dtype)
            for lanes in (LANES, sz.tail)
            for count, dtype in kept
        ]
        + [pltpu.SemaphoreType.DMA((3, 4))],
        limit=MOST_VMEM,
    )(thickness, wind_rows, tracer_rows)

    near = [(band * n_lon + i, (band ^ 1) * n_lon + i) for band in range(n_lat) for i in range(n_lon)]
    far = []
    for band in range(n_lat):
        other = band - 1 if band % 2 == 0 else band + 1
        for i in range(n_lon):
            if 0 <= other < n_lat:
                far.append((band * n_lon + i, other * n_lon + i))
            else:
                far.append((band * n_lon + i, band * n_lon + (i + n_lon // 2) % n_lon))
    near_h = lax.ppermute(thickness, ("lat", "lon"), near)
    near_w = lax.ppermute(wind_rows, ("lat", "lon"), near)
    if not sz.near_only:
        far_rows = lax.ppermute(far_rows, ("lat", "lon"), far)

    order = [sz.turns(False), sz.turns(True)]

    def meetings(shares):
        got = [shares[0]]
        for k in range(1, n_lon):
            sectors = [(band, i, i ^ order[band % 2][k]) for band in range(n_lat) for i in range(n_lon)]
            got.append(lax.ppermute(shares[k], ("lat", "lon"), [(b * n_lon + i, b * n_lon + j) for b, i, j in sectors]))
        return got

    all_pieces = pltpu.VMEM((n_lon, sz.size, LANES), f32)
    *tends, far_rows, near_q = call(
        polar_kernel,
        "polar",
        [vmem] * 9,
        [shaped(sz.size + EXT_ROWS, LANES)] * n_lon + [far_row, near_row],
        [
            pltpu.VMEM((n_lon * sz.size, LANES), f32),
            pltpu.VMEM((4 * sz.stack, LANES), f32),
            pltpu.VMEM((3, EXT_ROWS, sz.tiles * LANES), f32),
        ],
    )(thickness, wind_rows, near_h, near_w, sides, geo, wave, far_rows, near_q)
    met = meetings(tends)
    near_q = lax.ppermute(near_q, ("lat", "lon"), near)
    from_far = lax.ppermute(far_rows, ("lat", "lon"), far) if sz.near_only else far_rows
    weights, masks = call(
        weights_kernel,
        "weights",
        [smem, vmem, vmem, anywhere],
        (
            jax.ShapeDtypeStruct((sz.share * PER_TILE * sz.stack, n_lon * sz.stack), jnp.bfloat16),
            shaped(3, EXT_ROWS, LANES),
        ),
    )(cutoff, n, inverse, tends[0])
    worked = call(
        filter_kernel,
        "filter",
        [vmem] * 2 + [vmem] * n_lon,
        [shaped(sz.size, LANES)] * n_lon,
        [all_pieces, all_pieces],
    )(weights, geo, *met)
    held = call(pass_kernel, "pass", [vmem] + [anywhere] * 2, shaped(sz.size, LANES))(worked[-1], from_far, near_q)
    worked = [*worked[:-1], held]
    back = meetings(worked)

    base_w, base_h, mass = call(
        rest_kernel,
        "rest",
        [vmem] * 10 + [anywhere] + [vmem] * n_lon,
        (shaped(2, rows, merged), shaped(rows, merged), jax.ShapeDtypeStruct(tracers.shape, jnp.bfloat16)),
        [pltpu.VMEM((6, EXT_ROWS, sz.tiles * LANES), f32), pltpu.VMEM((n_lon, 8, LANES), f32)],
    )(masks, thickness, wind_rows, tracers, near_h, near_w, near_q, from_far, geo, wave, worked[0], *met)

    new_w, new_h = call(
        finish_kernel,
        "finish",
        [vmem] * (3 + n_lon),
        (shaped(*wind_rows.shape), shaped(rows, merged)),
        [pltpu.VMEM((n_lon * sz.size, LANES), f32)],
    )(masks, base_w, base_h, *back)
    return jnp.swapaxes(new_w, 0, 1), new_h, mass


def solution(mesh):
    in_specs = (P(None, "lat", "lon"), P("lat", "lon"), P(None, "lat", "lon"), P())
    out_specs = (P(None, "lat", "lon"), P("lat", "lon"), P(None, "lat", "lon"))
    return jax.shard_map(local, mesh=mesh, in_specs=in_specs, out_specs=out_specs, check_vma=False)
```

```python
import functools
import math

import jax
import jax.numpy as jnp
import numpy as np
from jax import lax
from jax.experimental import pallas as pl
from jax.experimental.pallas import tpu as pltpu
from jax.sharding import PartitionSpec as P

LEVELS = 16
TIME_STEP = 0.05
DIFFUSION = 0.5
LANES = 128
PER_TILE = LANES // LEVELS
EXT_ROWS = 16
LIMIT = 48 * 1024 * 1024
MOST_VMEM = 64 * 1024 * 1024 - 10500 * 1024


class Sizes:
    def __init__(self, rows, merged, n_lat, n_lon):
        self.rows = rows
        self.merged = merged
        self.columns = merged // LEVELS
        self.n_lat = n_lat
        self.n_lon = n_lon
        self.nlat = rows * n_lat
        self.nlon = self.columns * n_lon
        self.ratio = 2.0 * self.nlat / self.nlon
        self.tiles = -(-merged // LANES)
        self.end = (self.tiles - 1) * LANES
        self.tail = merged - self.end
        self.stack = -(-(self.tiles + 1) // 8) * 8
        self.near_only = rows <= self.nlat // 6 < 2 * rows
        self.work = rows - 1 if self.near_only else rows
        self.units = 3 * self.work
        self.share = -(-self.units // n_lon)
        self.size = self.share * self.stack
        assert self.tail <= LANES - 4 * LEVELS and rows + 2 <= EXT_ROWS and n_lat % 2 == 0
        assert n_lon >= 4 and n_lon & (n_lon - 1) == 0

    def span(self, tile):
        return self.tail if tile == self.tiles - 1 else LANES

    def first(self):
        return jnp.where(lax.rem(lax.axis_index("lat"), 2) == 0, 1, 0) if self.near_only else 0

    def at_pole(self, row):
        band = lax.axis_index("lat")
        pole = jnp.where(band == 0, 0, jnp.where(band == self.n_lat - 1, self.rows - 1, -1))
        return row == (pole if self.near_only else -1)

    def turns(self, odd):
        middle = list(range(1, self.n_lon - 1))
        return [0, self.n_lon - 1] + (middle[::-1] if odd else middle)

    def partner(self, k):
        odd = lax.rem(lax.axis_index("lat"), 2) == 1
        turn = jnp.where(odd, self.turns(True)[k], self.turns(False)[k])
        return jnp.bitwise_xor(lax.axis_index("lon"), turn)

    def piece(self, k):
        return pl.ds(pl.multiple_of(self.partner(k) * self.size, 8), self.size)


def geometry(sz):
    table = np.zeros((sz.n_lat, 3, EXT_ROWS, LANES), np.float64)

    def face(j):
        return math.sin((j + 1) * math.pi / sz.nlat) if 0 <= j < sz.nlat - 1 else 0.0

    for band in range(sz.n_lat):
        for row in range(sz.rows):
            j = band * sz.rows + row
            centre = (j + 0.5) * math.pi / sz.nlat - math.pi / 2
            table[band, 0, row] = 1.0 / math.cos(centre)
            table[band, 1, row] = math.sin(centre)
            table[band, 2, row] = face(j)
        table[band, 2, EXT_ROWS - 1] = face(band * sz.rows - 1)
    return table.astype(np.float32)


def offsets(sz):
    shift, out_tile = np.divmod(np.arange(PER_TILE * sz.stack), sz.stack)
    sector, in_tile = np.divmod(np.arange(sz.n_lon * sz.stack), sz.stack)
    n = (PER_TILE * (out_tile - 1) + shift)[:, None] - (PER_TILE * in_tile + sz.columns * sector)[None, :]
    n = (n + sz.nlon // 2) % sz.nlon - sz.nlon // 2
    with np.errstate(divide="ignore"):
        inverse = np.where(n == 0, 0.0, 1.0 / (sz.nlon * np.sin(np.pi * n / sz.nlon)))
    return n.astype(np.float32), inverse.astype(np.float32)


def waves(sz):
    column = PER_TILE * np.arange(sz.stack)[:, None] + np.arange(LANES)[None, :] // LEVELS
    angle = 2 * np.pi * column / sz.nlon
    return np.stack([np.cos(angle), np.sin(angle)]).astype(np.float32)


def edges_kernel(sz, h_hbm, w_hbm, q_hbm, near_ref, far_ref, sides_ref, *scratch):
    row_refs, first_refs, last_refs, sems = scratch[:3], scratch[3:6], scratch[6:9], scratch[9]
    rows, last = sz.rows, sz.rows - 1
    even = lax.rem(lax.axis_index("lat"), 2) == 0
    copies = []
    for i, source in enumerate((h_hbm, w_hbm, q_hbm)):
        for k, row in enumerate((0, last)):
            one = source.at[pl.ds(row, 1)] if i == 0 else source.at[row]
            copies.append(pltpu.make_async_copy(one, row_refs[i].at[k], sems.at[i, k]))
        for k, (start, to) in enumerate(((0, first_refs[i]), (sz.end, last_refs[i]))):
            lanes = pl.ds(start, to.shape[-1])
            cut = source.at[:, lanes] if i == 0 else source.at[:, :, lanes]
            copies.append(pltpu.make_async_copy(cut, to, sems.at[i, 2 + k]))
    for copy in copies:
        copy.start()
    for copy in copies:
        copy.wait()
    h_rows, w_rows, q_rows = row_refs
    for t in range(sz.tiles):
        wide = sz.span(t)
        lanes = slice(LANES * t, LANES * t + wide)
        q = [q_rows[k, :, lanes].astype(jnp.float32) for k in range(2)]
        for f in range(5):
            if f == 0:
                first, final = h_rows[0, :, lanes], h_rows[1, :, lanes]
            elif f == 1:
                first, final = w_rows[0, 1:2, lanes], w_rows[1, 1:2, lanes]
            else:
                first, final = q[0][f - 2 : f - 1], q[1][f - 2 : f - 1]
                at = sz.stack * (f - 2) + t
                near_ref[at : at + 1, :wide] = jnp.where(even, final, first)
            at = sz.stack * f + t
            far_ref[at : at + 1, :wide] = jnp.where(even, first, final)
    sides_ref[...] = jnp.zeros(sides_ref.shape, jnp.float32)
    for k, (refs, at) in enumerate(((first_refs, 0), (last_refs, sz.tail - LEVELS))):
        columns = slice(at, at + LEVELS)
        for f in range(5):
            if f == 0:
                value = refs[0][:, columns]
            elif f == 1:
                value = refs[1][:, 0, columns]
            else:
                value = refs[2][:, f - 2, columns].astype(jnp.float32)
            sides_ref[EXT_ROWS * k : EXT_ROWS * k + rows, LEVELS * f : LEVELS * (f + 1)] = value


def add_rows(sz, ext, near_h_ref, near_w_ref, near_q_ref, far_ref):
    band = lax.axis_index("lat")
    even = lax.rem(band, 2) == 0
    over_pole = (band == 0) | (band == sz.n_lat - 1)
    last = sz.rows - 1
    for f in range(2 if near_q_ref is None else 5):
        flip = jnp.where(over_pole, -1.0, 1.0) if f == 1 else 1.0
        for t in range(sz.tiles):
            lanes = slice(LANES * t, LANES * t + sz.span(t))
            if f == 0:
                near = jnp.where(even, near_h_ref[0:1, lanes], near_h_ref[last : sz.rows, lanes])
            elif f == 1:
                near = jnp.where(even, near_w_ref[0, 1:2, lanes], near_w_ref[last, 1:2, lanes])
            else:
                at = sz.stack * (f - 2) + t
                near = near_q_ref[at : at + 1, : sz.span(t)]
            at = sz.stack * f + t
            far = jnp.zeros_like(near) if far_ref is None else far_ref[at : at + 1, : sz.span(t)] * flip
            ext[f, sz.rows : sz.rows + 1, lanes] = jnp.where(even, near, far)
            ext[f, EXT_ROWS - 1 : EXT_ROWS, lanes] = jnp.where(even, far, near)


class Tiles:
    def __init__(self, sz):
        self.sz = sz
        self.lane = lax.broadcasted_iota(jnp.int32, (EXT_ROWS, LANES), 1)
        self.turned = {}

    def turn(self, name, t, value, step):
        key = (name, t % self.sz.tiles, step)
        if key not in self.turned:
            self.turned[key] = pltpu.roll(value(t % self.sz.tiles), step % LANES, 1)
        return self.turned[key]

    def east(self, name, t, value):
        here = self.turn(name, t, value, -LEVELS)
        return jnp.where(self.lane < LANES - LEVELS, here, self.turn(name, t + 1, value, -LEVELS))

    def west(self, name, t, value):
        here = self.turn(name, t, value, LEVELS)
        return jnp.where(self.lane >= LEVELS, here, self.turn(name, t - 1, value, LEVELS))


def north(value):
    return pltpu.roll(value, EXT_ROWS - 1, 0)


def south(value):
    return pltpu.roll(value, 1, 0)


def polar_kernel(sz, h_ref, w_ref, near_h_ref, near_w_ref, sides_ref, geo_ref, wave_ref, far_ref, near_q_ref, *refs):
    out_refs, (far_out, near_out, tend_ref, pole_ref, ext) = refs[:-5], refs[-5:]
    far_out[...] = far_ref[...]
    near_out[...] = near_q_ref[...]
    if sz.near_only:
        far_ref = None
    band = lax.axis_index("lat")
    ring = Tiles(sz)
    lane = ring.lane
    tiles, stack, rows, work = sz.tiles, sz.stack, sz.rows, sz.work
    even = lax.rem(band, 2) == 0
    for f, value in enumerate((h_ref[...], w_ref[:, 1, :], w_ref[:, 0, :])):
        ext[f, :rows, sz.end :] = jnp.zeros((rows, LANES), jnp.float32)
        ext[f, :rows, : sz.merged] = value
    add_rows(sz, ext, near_h_ref, near_w_ref, None, far_ref)
    inv_cos, sin_centre, cos_face = geo_ref[band, 0], geo_ref[band, 1], geo_ref[band, 2]
    ratio = sz.ratio

    def tile(f, t):
        return ext[f, :, LANES * t : LANES * (t + 1)]

    kept = {}

    def zonal(t):
        if t not in kept:
            thick_e = ring.east("h", t, functools.partial(tile, 0))
            wind_e = ring.east("u", t, functools.partial(tile, 2))
            flux = 0.25 * (tile(2, t) + wind_e) * (tile(0, t) + thick_e) * inv_cos
            if t == tiles - 1:
                flux = jnp.where(lane < sz.tail - LEVELS, flux, 0.0)
            kept[t] = (flux, thick_e)
        return kept[t]

    for t in range(tiles):
        flux, thick_e = zonal(t)
        thick, wind_v, wind_u = tile(0, t), tile(1, t), tile(2, t)
        flux_w = ring.west("f", t, lambda s: zonal(s)[0])
        thick_w = ring.west("hw", t, functools.partial(tile, 0))
        thick_n = north(thick)
        flux_n = (0.25 * ratio) * (wind_v + north(wind_v)) * (thick + thick_n) * cos_face
        thick_tend = -((flux - flux_w) + (flux_n - south(flux_n)) * inv_cos)
        wind_u_tend = sin_centre * wind_v - (thick_e - thick_w) * (0.5 * inv_cos)
        wind_v_tend = -sin_centre * wind_u - (0.5 * ratio) * (thick_n - south(thick))
        spare = 0.0
        if t == tiles - 1:
            last = sz.tail - LEVELS
            columns = [(tile(0, 0), 0), (thick, last), (tile(2, 0), 0), (wind_u, last)]
            for k, (source, at) in reversed(list(enumerate(columns))):
                to = sz.tail + LEVELS * k
                spare = jnp.where(lane < to + LEVELS, pltpu.roll(source, (to - at) % LANES, 1), spare)
        for f, tend in enumerate((thick_tend, wind_u_tend, wind_v_tend, thick)):
            if sz.near_only:
                alone = jnp.where(band < sz.n_lat // 2, tend[:1], tend[rows - 1 : rows])
                if t == tiles - 1:
                    alone = jnp.where(lane[:1] < sz.tail, alone, 0.0)
                pole_ref[stack * f + t : stack * f + t + 1] = alone
            if f == 3:
                continue
            if t == tiles - 1:
                tend = jnp.where(lane < sz.tail, tend, spare)
            if sz.near_only:
                tend = jnp.where(even, north(tend), tend)
            tend_ref[pl.ds(stack * work * f + t, work, stride=stack), :] = tend[:work]
    for f in range(3):
        for t in range(tiles, stack):
            tend_ref[pl.ds(stack * work * f + t, work, stride=stack), :] = jnp.zeros((work, LANES), jnp.float32)
    used = stack * sz.units
    if used < tend_ref.shape[0]:
        tend_ref[used:, :] = jnp.zeros((tend_ref.shape[0] - used, LANES), jnp.float32)
    sides = [sides_ref[:EXT_ROWS], sides_ref[EXT_ROWS:]]
    if sz.near_only:
        sums = pole_sums(sz, pole_ref, wave_ref, spare, band)
        row = lax.broadcasted_iota(jnp.int32, (EXT_ROWS, LANES), 0)
        for k, total in enumerate(sums):
            sides = [jnp.where(row == rows + k, total, side) for side in sides]
    here = lax.axis_index("lon")
    for k, out_ref in enumerate(out_refs):
        out_ref[: sz.size] = tend_ref[sz.piece(k), :]
        eastward = sz.partner(k) == lax.rem(here + 1, sz.n_lon)
        out_ref[sz.size :] = jnp.where(eastward, sides[1], sides[0])


def pole_sums(sz, pole_ref, wave_ref, spare, band):
    stack, rows = sz.stack, sz.rows
    lane = lax.broadcasted_iota(jnp.int32, (1, LANES), 1)
    sides = jnp.where(band < sz.n_lat // 2, spare[:1], spare[rows - 1 : rows])
    found = [jnp.zeros((1, LANES), jnp.float32), pltpu.roll(sides, (LANES // 2 - sz.tail) % LANES, 1)]
    for f in range(4):
        if sz.tiles < stack:
            pole_ref[stack * f + sz.tiles : stack * (f + 1)] = jnp.zeros((stack - sz.tiles, LANES), jnp.float32)
        values = pole_ref[stack * f : stack * (f + 1)]
        for k, terms in enumerate((values, values * wave_ref[0], values * wave_ref[1])):
            total = jnp.sum(terms, axis=0, keepdims=True)
            for step in (64, 32, 16):
                total = total + pltpu.roll(total, step, 1)
            row, place = divmod(3 * f + k, PER_TILE)
            inside = (lane >= LEVELS * place) & (lane < LEVELS * (place + 1))
            found[row] = jnp.where(inside, total, found[row])
    return found


def pole_waves(sz, rows_in, inv_cos, sign):
    n_lon = sz.n_lon
    lane = lax.broadcasted_iota(jnp.int32, (1, LANES), 1)

    def value(s, place):
        row, at = divmod(place, PER_TILE)
        return pltpu.roll(rows_in[s % n_lon, row : row + 1], (-LEVELS * at) % LANES, 1)

    theta = 2 * math.pi / sz.nlon
    ends = (1.0, math.cos(theta * (sz.columns - 1)), math.sin(theta * (sz.columns - 1)))
    sums = [[[value(s, 3 * f + k) for k in range(3)] for f in range(4)] for s in range(n_lon)]
    for s in range(n_lon):
        thick_w, thick_e = value(s, 13), value(s + 1, 12)
        flux = 0.25 * (value(s, 15) + value(s + 1, 14)) * (thick_w + thick_e) * inv_cos
        slope = 0.5 * inv_cos
        after = (s + 1) % n_lon
        for f, (west_of, east_of) in enumerate(((flux, flux), (slope * thick_e, slope * thick_w))):
            for k in range(3):
                sums[s][f][k] = sums[s][f][k] - west_of * ends[k]
            for k in range(2):
                sums[after][f][k] = sums[after][f][k] + east_of
    result = []
    for f in range(3):
        waves_of = [0.0, 0.0, 0.0]
        for s in range(n_lon):
            level, cosine, sine = sums[s][f]
            if f == 2:
                level = level + (0.5 * sz.ratio) * sign * sums[s][3][0]
                cosine = cosine - (0.5 * sz.ratio) * sign * sums[s][3][1]
                sine = sine - (0.5 * sz.ratio) * sign * sums[s][3][2]
            c, d = math.cos(2 * math.pi * s / n_lon), math.sin(2 * math.pi * s / n_lon)
            waves_of[0] = waves_of[0] + level
            waves_of[1] = waves_of[1] + (c * cosine - d * sine)
            waves_of[2] = waves_of[2] + (d * cosine + c * sine)
        spread = []
        for k, total in enumerate(waves_of):
            total = jnp.where(lane < LEVELS, total * ((1.0 if k == 0 else 2.0) / sz.nlon), 0.0)
            for step in (16, 32, 64):
                total = total + pltpu.roll(total, step, 1)
            spread.append(total)
        result.append(spread)
    return result


def rest_kernel(sz, masks_ref, h_ref, w_ref, q_ref, near_h_ref, near_w_ref, near_q_ref, far_ref, geo_ref, wave_ref, after_ref, *refs):
    met_refs, (new_w_ref, new_h_ref, mass_ref, ext, pole_in) = refs[: sz.n_lon], refs[sz.n_lon :]
    band = lax.axis_index("lat")
    ring = Tiles(sz)
    lane = ring.lane
    tiles, rows = sz.tiles, sz.rows
    for f in range(6):
        if f < 2 or f == 5:
            value = (h_ref[...], w_ref[:, 1, :], w_ref[:, 0, :])[min(f, 2)]
        else:
            value = q_ref[f - 2].astype(jnp.float32)
        ext[f, :rows, : sz.merged] = value
    add_rows(sz, ext, near_h_ref, near_w_ref, near_q_ref, far_ref)
    lane9 = lane[:rows]
    here = lax.axis_index("lon")
    from_e = from_w = met_refs[0][sz.size :]
    for k, met_ref in enumerate(met_refs):
        eastward = lax.rem(sz.partner(k) - here + sz.n_lon, sz.n_lon)
        pole_in[eastward] = met_ref[sz.size + 8 :]
        from_e = jnp.where(sz.partner(k) == lax.rem(here + 1, sz.n_lon), met_ref[sz.size :], from_e)
        from_w = jnp.where(sz.partner(k) == lax.rem(here + sz.n_lon - 1, sz.n_lon), met_ref[sz.size :], from_w)
    for place, f in enumerate((0, 5, 2, 3, 4)):
        after = pltpu.roll(from_e, (sz.tail - LEVELS * place) % LANES, 1)[:rows]
        before = pltpu.roll(from_w, (LANES - LEVELS - LEVELS * place) % LANES, 1)[:rows]
        own = ext[f, :rows, sz.end :]
        edge = jnp.where(lane9 < LANES - LEVELS, after, before)
        ext[f, :rows, sz.end :] = jnp.where(lane9 < sz.tail, own, edge)
    inv_cos, sin_centre, cos_face = geo_ref[band, 0], geo_ref[band, 1], geo_ref[band, 2]
    ratio = sz.ratio

    plain, alone = masks_ref[0], masks_ref[1]
    if sz.near_only:
        band = lax.axis_index("lat")
        low = band < sz.n_lat // 2
        pole_cos = jnp.where(low, inv_cos[:1], inv_cos[rows - 1 : rows])
        kept_waves = pole_waves(sz, pole_in.at[:, rows - 8 :], pole_cos, jnp.where(low, 1.0, -1.0))

    def stepped(f, t, value, tend):
        value = value + plain * tend
        if sz.near_only:
            level, cosine, sine = kept_waves[f]
            wave = level + cosine * wave_ref[0, t : t + 1] + sine * wave_ref[1, t : t + 1]
            value = value + alone * wave
        return value

    def tile(f, t):
        return ext[f, :, LANES * t : LANES * (t + 1)]

    kept = {}

    def zonal(t):
        if t not in kept:
            thick_e = ring.east("h", t, functools.partial(tile, 0))
            wind_e = ring.east("u", t, functools.partial(tile, 5))
            flux = 0.25 * (tile(5, t) + wind_e) * (tile(0, t) + thick_e) * inv_cos
            parts = []
            for k in range(3):
                q = tile(2 + k, t)
                q_e = ring.east(k, t, functools.partial(tile, 2 + k))
                parts.append(DIFFUSION * (q_e - q) - flux * (0.5 * (q + q_e)))
            kept[t] = (flux, thick_e, parts)
        return kept[t]

    for t in range(tiles):
        span = sz.span(t)
        lanes = slice(LANES * t, LANES * t + span)
        flux, thick_e, parts = zonal(t)
        thick, wind_u, wind_v = tile(0, t), tile(5, t), tile(1, t)
        flux_w = ring.west("f", t, lambda s: zonal(s)[0])
        thick_w = ring.west("hw", t, functools.partial(tile, 0))
        thick_n = north(thick)
        flux_n = (0.25 * ratio) * (wind_v + north(wind_v)) * (thick + thick_n) * cos_face
        thick_tend = -((flux - flux_w) + (flux_n - south(flux_n)) * inv_cos)
        wind_u_tend = sin_centre * wind_v - (thick_e - thick_w) * (0.5 * inv_cos)
        wind_v_tend = -sin_centre * wind_u - (0.5 * ratio) * (thick_n - south(thick))
        new_h_ref[:, lanes] = stepped(0, t, thick, thick_tend)[:rows, :span]
        new_w_ref[0, :, lanes] = stepped(1, t, wind_u, wind_u_tend)[:rows, :span]
        new_w_ref[1, :, lanes] = stepped(2, t, wind_v, wind_v_tend)[:rows, :span]
        for k in range(3):
            q = tile(2 + k, t)
            q_n = north(q)
            zonal_part = parts[k] - ring.west(("p", k), t, lambda s: zonal(s)[2][k])
            lap = q_n + south(q) - 2.0 * q
            over = flux_n * (0.5 * (q + q_n))
            merid_part = DIFFUSION * lap - (over - south(over)) * inv_cos
            mass = thick * q + TIME_STEP * (zonal_part + merid_part)
            mass_ref[k, :, lanes] = mass[:rows, :span].astype(jnp.bfloat16)


def sin_pi(y):
    y = jnp.where(y > 0.5, 1.0 - y, jnp.where(y < -0.5, -1.0 - y, y))
    s = y * y
    series = [(-1) ** i * math.pi ** (2 * i + 1) / math.factorial(2 * i + 1) for i in range(7)]
    total = series[-1]
    for factor in reversed(series[:-1]):
        total = total * s + factor
    return total * y


def share_of(sz, i):
    unit = lax.axis_index("lon") * sz.share + i
    return unit // sz.work, sz.first() + lax.rem(unit, sz.work)


def weights_kernel(sz, cut_ref, n_ref, inverse_ref, after_ref, weights_ref, masks_ref):
    band = lax.axis_index("lat")
    cuts = cut_ref[...].astype(jnp.float32)

    def cut_of(rows):
        column = lax.broadcasted_iota(jnp.int32, (rows.shape[0], sz.nlat), 1)
        return jnp.sum(jnp.where(column == band * sz.rows + rows, cuts, 0.0), axis=1, keepdims=True)

    row = lax.broadcasted_iota(jnp.int32, (EXT_ROWS, LANES), 0)
    cut = cut_of(lax.broadcasted_iota(jnp.int32, (EXT_ROWS, sz.nlat), 0))
    inside = row < sz.rows
    plain, alone = (cut >= sz.nlon // 2) & inside, sz.at_pole(row)
    masks_ref[0] = jnp.where(plain, TIME_STEP, 0.0)
    masks_ref[1] = jnp.where(alone, TIME_STEP, 0.0)
    masks_ref[2] = jnp.where(plain | alone, 0.0, TIME_STEP)
    size = PER_TILE * sz.stack
    for i in range(sz.share):
        width = 2.0 * cut_of(jnp.full((1, sz.nlat), share_of(sz, i)[1])) + 1.0
        n = n_ref[...]
        turns = n * width
        turns = turns - jnp.round(turns * (0.5 / sz.nlon)) * (2.0 * sz.nlon)
        weights = sin_pi(turns * (1.0 / sz.nlon)) * inverse_ref[...]
        weights = jnp.where(n == 0.0, width * (1.0 / sz.nlon), weights)
        weights_ref[size * i : size * (i + 1)] = weights.astype(jnp.bfloat16)


def pass_kernel(sz, piece_ref, after_ref, also_after_ref, out_ref):
    out_ref[...] = piece_ref[...]


def filter_kernel(sz, weights_ref, geo_ref, *refs):
    n_lon, stack, share = sz.n_lon, sz.stack, sz.share
    in_refs, out_refs, (gathered, results) = refs[:n_lon], refs[n_lon : 2 * n_lon], refs[2 * n_lon :]
    for k, in_ref in enumerate(in_refs):
        gathered[sz.partner(k)] = in_ref[: sz.size]

    band = lax.axis_index("lat")
    lane = lax.broadcasted_iota(jnp.int32, (share, LANES), 1)
    place = lax.broadcasted_iota(jnp.int32, (share, LANES), 0)
    by_flux = by_thick = jnp.zeros((share, LANES), jnp.float32)
    for i in range(share):
        field, row = share_of(sz, i)
        inv_cos = geo_ref[band, 0, pl.ds(row, 1), :]
        by_flux = jnp.where((place == i) & (field == 0), inv_cos, by_flux)
        by_thick = jnp.where((place == i) & (field == 1), 0.5 * inv_cos, by_thick)
    sides = [gathered[s, pl.ds(sz.tiles - 1, share, stride=stack), :] for s in range(n_lon)]

    def column(s, k):
        return pltpu.roll(sides[s % n_lon], (-sz.tail - LEVELS * k) % LANES, 1)

    for s in range(n_lon):
        thick_w, thick_e = column(s, 1), column(s + 1, 0)
        flux = 0.25 * (column(s, 3) + column(s + 1, 2)) * (thick_w + thick_e) * by_flux
        west_of, east_of = flux + by_thick * thick_e, flux + by_thick * thick_w
        at = pl.ds(sz.tiles - 1, share, stride=stack)
        own = gathered[s, at, :]
        own = own - jnp.where(lane >= sz.tail - LEVELS, pltpu.roll(west_of, sz.tail - LEVELS, 1), 0.0)
        gathered[s, at, :] = jnp.where(lane < sz.tail, own, 0.0)
        at = pl.ds(0, share, stride=stack)
        after = (s + 1) % n_lon
        gathered[after, at, :] = gathered[after, at, :] + jnp.where(lane < LEVELS, east_of, 0.0)

    wide = lax.broadcasted_iota(jnp.int32, (stack, LANES), 1)
    rows = PER_TILE * stack
    for i in range(share):
        here = slice(stack * i, stack * (i + 1))
        pieces = [gathered[s, here].astype(jnp.bfloat16) for s in range(n_lon)]
        circle = jnp.concatenate([jnp.concatenate(pieces[s:] + pieces[:s], axis=0) for s in range(n_lon)], axis=1)
        spread = jnp.dot(weights_ref[rows * i : rows * (i + 1)], circle, preferred_element_type=jnp.float32)
        for s in range(n_lon):
            same = spread[:stack, LANES * s : LANES * (s + 1)]
            carried = None
            for e in range(1, PER_TILE):
                part = spread[stack * e : stack * (e + 1), LANES * s : LANES * (s + 1)]
                part = pltpu.roll(part, LEVELS * e, 1)
                over = jnp.where(wide < LEVELS * e, part, 0.0)
                same = same + part
                carried = over if carried is None else carried + over
            results[s, here] = pltpu.roll(same - carried, stack - 1, 0) + carried
    for k, out_ref in enumerate(out_refs):
        out_ref[...] = results[sz.partner(k)]


def finish_kernel(sz, masks_ref, base_w_ref, base_h_ref, *refs):
    back_refs, (new_w_ref, new_h_ref, back_ref) = refs[: sz.n_lon], refs[sz.n_lon :]
    rows, work = sz.rows, sz.work
    for k, ref in enumerate(back_refs):
        back_ref[sz.piece(k), :] = ref[...]
    scale = masks_ref[2]
    even = lax.rem(lax.axis_index("lat"), 2) == 0
    for f in range(3):
        for t in range(sz.tiles):
            span = sz.span(t)
            lanes = slice(LANES * t, LANES * t + span)
            tend = back_ref[pl.ds(sz.stack * work * f + t, work, stride=sz.stack), :]
            if sz.near_only:
                tend = jnp.concatenate([tend, jnp.zeros((EXT_ROWS - work, LANES), jnp.float32)], axis=0)
                tend = jnp.where(even, south(tend), tend)
            change = (scale[:rows] * tend[:rows])[:, :span]
            if f == 0:
                new_h_ref[:, lanes] = base_h_ref[:, lanes] + change
            else:
                new_w_ref[:, f - 1, lanes] = base_w_ref[f - 1, :, lanes] + change


def local(winds, thickness, tracers, cutoff):
    n_lat = lax.axis_size("lat")
    n_lon = lax.axis_size("lon")
    rows, merged = thickness.shape
    sz = Sizes(rows, merged, n_lat, n_lon)
    f32 = jnp.float32
    vmem = pl.BlockSpec(memory_space=pltpu.VMEM)
    hbm = pl.BlockSpec(memory_space=pltpu.HBM)
    anywhere = pl.BlockSpec(memory_space=pl.ANY)

    def shaped(*shape):
        return jax.ShapeDtypeStruct(shape, f32)

    def call(kernel, name, in_specs, out_shape, scratch=(), limit=LIMIT):
        return pl.pallas_call(
            functools.partial(kernel, sz),
            out_shape=out_shape,
            in_specs=in_specs,
            out_specs=jax.tree.map(lambda _: vmem, out_shape),
            scratch_shapes=list(scratch),
            compiler_params=pltpu.CompilerParams(vmem_limit_bytes=limit),
            name=name,
        )

    geo = jnp.asarray(geometry(sz))
    wave = jnp.asarray(waves(sz))
    n, inverse = (jnp.asarray(table) for table in offsets(sz))

    wind_rows = jnp.swapaxes(winds, 0, 1)
    tracer_rows = jnp.swapaxes(tracers, 0, 1)
    far_row, near_row = shaped(5 * sz.stack, LANES), shaped(3 * sz.stack, LANES)
    kept = [((1,), f32), ((2,), f32), ((3,), jnp.bfloat16)]
    near_q, far_rows, sides = call(
        edges_kernel,
        "edges",
        [hbm] * 3,
        (near_row, far_row, shaped(2 * EXT_ROWS, LANES)),
        [pltpu.VMEM((2,) + count + (merged,), dtype) for count, dtype in kept]
        + [
            pltpu.VMEM((rows,) + (count if count != (1,) else ()) + (lanes,), dtype)
            for lanes in (LANES, sz.tail)
            for count, dtype in kept
        ]
        + [pltpu.SemaphoreType.DMA((3, 4))],
        limit=MOST_VMEM,
    )(thickness, wind_rows, tracer_rows)

    near = [(band * n_lon + i, (band ^ 1) * n_lon + i) for band in range(n_lat) for i in range(n_lon)]
    far = []
    for band in range(n_lat):
        other = band - 1 if band % 2 == 0 else band + 1
        for i in range(n_lon):
            if 0 <= other < n_lat:
                far.append((band * n_lon + i, other * n_lon + i))
            else:
                far.append((band * n_lon + i, band * n_lon + (i + n_lon // 2) % n_lon))
    near_h = lax.ppermute(thickness, ("lat", "lon"), near)
    near_w = lax.ppermute(wind_rows, ("lat", "lon"), near)
    if not sz.near_only:
        far_rows = lax.ppermute(far_rows, ("lat", "lon"), far)

    order = [sz.turns(False), sz.turns(True)]

    def meetings(shares):
        got = [shares[0]]
        for k in range(1, n_lon):
            sectors = [(band, i, i ^ order[band % 2][k]) for band in range(n_lat) for i in range(n_lon)]
            got.append(lax.ppermute(shares[k], ("lat", "lon"), [(b * n_lon + i, b * n_lon + j) for b, i, j in sectors]))
        return got

    all_pieces = pltpu.VMEM((n_lon, sz.size, LANES), f32)
    *tends, far_rows, near_q = call(
        polar_kernel,
        "polar",
        [vmem] * 9,
        [shaped(sz.size + EXT_ROWS, LANES)] * n_lon + [far_row, near_row],
        [
            pltpu.VMEM((n_lon * sz.size, LANES), f32),
            pltpu.VMEM((4 * sz.stack, LANES), f32),
            pltpu.VMEM((3, EXT_ROWS, sz.tiles * LANES), f32),
        ],
    )(thickness, wind_rows, near_h, near_w, sides, geo, wave, far_rows, near_q)
    met = meetings(tends)
    near_q = lax.ppermute(near_q, ("lat", "lon"), near)
    from_far = lax.ppermute(far_rows, ("lat", "lon"), far) if sz.near_only else far_rows
    weights, masks = call(
        weights_kernel,
        "weights",
        [vmem, vmem, vmem, anywhere],
        (
            jax.ShapeDtypeStruct((sz.share * PER_TILE * sz.stack, n_lon * sz.stack), jnp.bfloat16),
            shaped(3, EXT_ROWS, LANES),
        ),
    )(cutoff.reshape(1, -1), n, inverse, tends[0])
    worked = call(
        filter_kernel,
        "filter",
        [vmem] * 2 + [vmem] * n_lon,
        [shaped(sz.size, LANES)] * n_lon,
        [all_pieces, all_pieces],
    )(weights, geo, *met)
    held = call(pass_kernel, "pass", [vmem] + [anywhere] * 2, shaped(sz.size, LANES))(worked[-1], from_far, near_q)
    worked = [*worked[:-1], held]
    back = meetings(worked)

    base_w, base_h, mass = call(
        rest_kernel,
        "rest",
        [vmem] * 10 + [anywhere] + [vmem] * n_lon,
        (shaped(2, rows, merged), shaped(rows, merged), jax.ShapeDtypeStruct(tracers.shape, jnp.bfloat16)),
        [pltpu.VMEM((6, EXT_ROWS, sz.tiles * LANES), f32), pltpu.VMEM((n_lon, 8, LANES), f32)],
    )(masks, thickness, wind_rows, tracers, near_h, near_w, near_q, from_far, geo, wave, worked[0], *met)

    new_w, new_h = call(
        finish_kernel,
        "finish",
        [vmem] * (3 + n_lon),
        (shaped(*wind_rows.shape), shaped(rows, merged)),
        [pltpu.VMEM((n_lon * sz.size, LANES), f32)],
    )(masks, base_w, base_h, *back)
    return jnp.swapaxes(new_w, 0, 1), new_h, mass


def solution(mesh):
    in_specs = (P(None, "lat", "lon"), P("lat", "lon"), P(None, "lat", "lon"), P())
    out_specs = (P(None, "lat", "lon"), P("lat", "lon"), P(None, "lat", "lon"))
    return jax.shard_map(local, mesh=mesh, in_specs=in_specs, out_specs=out_specs, check_vma=False)
```

```python
import functools
import math

import jax
import jax.numpy as jnp
import numpy as np
from jax import lax
from jax.experimental import pallas as pl
from jax.experimental.pallas import tpu as pltpu
from jax.sharding import PartitionSpec as P

LEVELS = 16
TIME_STEP = 0.05
DIFFUSION = 0.5
LANES = 128
PER_TILE = LANES // LEVELS
EXT_ROWS = 16
LIMIT = 48 * 1024 * 1024
MOST_VMEM = 64 * 1024 * 1024 - 10500 * 1024


class Sizes:
    def __init__(self, rows, merged, n_lat, n_lon):
        self.rows = rows
        self.merged = merged
        self.columns = merged // LEVELS
        self.n_lat = n_lat
        self.n_lon = n_lon
        self.nlat = rows * n_lat
        self.nlon = self.columns * n_lon
        self.ratio = 2.0 * self.nlat / self.nlon
        self.tiles = -(-merged // LANES)
        self.end = (self.tiles - 1) * LANES
        self.tail = merged - self.end
        self.stack = -(-(self.tiles + 1) // 8) * 8
        self.near_only = rows <= self.nlat // 6 < 2 * rows
        self.work = rows - 1 if self.near_only else rows
        self.units = 3 * self.work
        self.share = -(-self.units // n_lon)
        self.size = self.share * self.stack
        assert self.tail <= LANES - 4 * LEVELS and rows + 2 <= EXT_ROWS and n_lat % 2 == 0
        assert n_lon >= 4 and n_lon & (n_lon - 1) == 0

    def span(self, tile):
        return self.tail if tile == self.tiles - 1 else LANES

    def first(self):
        return jnp.where(lax.rem(lax.axis_index("lat"), 2) == 0, 1, 0) if self.near_only else 0

    def at_pole(self, row):
        band = lax.axis_index("lat")
        pole = jnp.where(band == 0, 0, jnp.where(band == self.n_lat - 1, self.rows - 1, -1))
        return row == (pole if self.near_only else -1)

    def turns(self, odd):
        middle = list(range(1, self.n_lon - 1))
        return [0, self.n_lon - 1] + (middle[::-1] if odd else middle)

    def partner(self, k):
        odd = lax.rem(lax.axis_index("lat"), 2) == 1
        turn = jnp.where(odd, self.turns(True)[k], self.turns(False)[k])
        return jnp.bitwise_xor(lax.axis_index("lon"), turn)

    def piece(self, k):
        return pl.ds(pl.multiple_of(self.partner(k) * self.size, 8), self.size)


def geometry(sz):
    table = np.zeros((sz.n_lat, 3, EXT_ROWS, LANES), np.float64)

    def face(j):
        return math.sin((j + 1) * math.pi / sz.nlat) if 0 <= j < sz.nlat - 1 else 0.0

    for band in range(sz.n_lat):
        for row in range(sz.rows):
            j = band * sz.rows + row
            centre = (j + 0.5) * math.pi / sz.nlat - math.pi / 2
            table[band, 0, row] = 1.0 / math.cos(centre)
            table[band, 1, row] = math.sin(centre)
            table[band, 2, row] = face(j)
        table[band, 2, EXT_ROWS - 1] = face(band * sz.rows - 1)
    return table.astype(np.float32)


def offsets(sz):
    shift, out_tile = np.divmod(np.arange(PER_TILE * sz.stack), sz.stack)
    sector, in_tile = np.divmod(np.arange(sz.n_lon * sz.stack), sz.stack)
    n = (PER_TILE * (out_tile - 1) + shift)[:, None] - (PER_TILE * in_tile + sz.columns * sector)[None, :]
    n = (n + sz.nlon // 2) % sz.nlon - sz.nlon // 2
    with np.errstate(divide="ignore"):
        inverse = np.where(n == 0, 0.0, 1.0 / (sz.nlon * np.sin(np.pi * n / sz.nlon)))
    return n.astype(np.float32), inverse.astype(np.float32)


def waves(sz):
    column = PER_TILE * np.arange(sz.stack)[:, None] + np.arange(LANES)[None, :] // LEVELS
    angle = 2 * np.pi * column / sz.nlon
    return np.stack([np.cos(angle), np.sin(angle)]).astype(np.float32)


def edges_kernel(sz, h_hbm, w_hbm, q_hbm, near_ref, far_ref, sides_ref, *scratch):
    row_refs, first_refs, last_refs, sems = scratch[:3], scratch[3:6], scratch[6:9], scratch[9]
    rows, last = sz.rows, sz.rows - 1
    even = lax.rem(lax.axis_index("lat"), 2) == 0
    copies = []
    for i, source in enumerate((h_hbm, w_hbm, q_hbm)):
        for k, row in enumerate((0, last)):
            one = source.at[pl.ds(row, 1)] if i == 0 else source.at[row]
            copies.append(pltpu.make_async_copy(one, row_refs[i].at[k], sems.at[i, k]))
        for k, (start, to) in enumerate(((0, first_refs[i]), (sz.end, last_refs[i]))):
            lanes = pl.ds(start, to.shape[-1])
            cut = source.at[:, lanes] if i == 0 else source.at[:, :, lanes]
            copies.append(pltpu.make_async_copy(cut, to, sems.at[i, 2 + k]))
    for copy in copies:
        copy.start()
    for copy in copies:
        copy.wait()
    h_rows, w_rows, q_rows = row_refs
    for t in range(sz.tiles):
        wide = sz.span(t)
        lanes = slice(LANES * t, LANES * t + wide)
        q = [q_rows[k, :, lanes].astype(jnp.float32) for k in range(2)]
        for f in range(5):
            if f == 0:
                first, final = h_rows[0, :, lanes], h_rows[1, :, lanes]
            elif f == 1:
                first, final = w_rows[0, 1:2, lanes], w_rows[1, 1:2, lanes]
            else:
                first, final = q[0][f - 2 : f - 1], q[1][f - 2 : f - 1]
                at = sz.stack * (f - 2) + t
                near_ref[at : at + 1, :wide] = jnp.where(even, final, first)
            at = sz.stack * f + t
            far_ref[at : at + 1, :wide] = jnp.where(even, first, final)
    sides_ref[...] = jnp.zeros(sides_ref.shape, jnp.float32)
    for k, (refs, at) in enumerate(((first_refs, 0), (last_refs, sz.tail - LEVELS))):
        columns = slice(at, at + LEVELS)
        for f in range(5):
            if f == 0:
                value = refs[0][:, columns]
            elif f == 1:
                value = refs[1][:, 0, columns]
            else:
                value = refs[2][:, f - 2, columns].astype(jnp.float32)
            sides_ref[EXT_ROWS * k : EXT_ROWS * k + rows, LEVELS * f : LEVELS * (f + 1)] = value


def add_rows(sz, ext, near_h_ref, near_w_ref, near_q_ref, far_ref):
    band = lax.axis_index("lat")
    even = lax.rem(band, 2) == 0
    over_pole = (band == 0) | (band == sz.n_lat - 1)
    last = sz.rows - 1
    for f in range(2 if near_q_ref is None else 5):
        flip = jnp.where(over_pole, -1.0, 1.0) if f == 1 else 1.0
        for t in range(sz.tiles):
            lanes = slice(LANES * t, LANES * t + sz.span(t))
            if f == 0:
                near = jnp.where(even, near_h_ref[0:1, lanes], near_h_ref[last : sz.rows, lanes])
            elif f == 1:
                near = jnp.where(even, near_w_ref[0, 1:2, lanes], near_w_ref[last, 1:2, lanes])
            else:
                at = sz.stack * (f - 2) + t
                near = near_q_ref[at : at + 1, : sz.span(t)]
            at = sz.stack * f + t
            far = jnp.zeros_like(near) if far_ref is None else far_ref[at : at + 1, : sz.span(t)] * flip
            ext[f, sz.rows : sz.rows + 1, lanes] = jnp.where(even, near, far)
            ext[f, EXT_ROWS - 1 : EXT_ROWS, lanes] = jnp.where(even, far, near)


class Tiles:
    def __init__(self, sz):
        self.sz = sz
        self.lane = lax.broadcasted_iota(jnp.int32, (EXT_ROWS, LANES), 1)
        self.turned = {}

    def turn(self, name, t, value, step):
        key = (name, t % self.sz.tiles, step)
        if key not in self.turned:
            self.turned[key] = pltpu.roll(value(t % self.sz.tiles), step % LANES, 1)
        return self.turned[key]

    def east(self, name, t, value):
        here = self.turn(name, t, value, -LEVELS)
        return jnp.where(self.lane < LANES - LEVELS, here, self.turn(name, t + 1, value, -LEVELS))

    def west(self, name, t, value):
        here = self.turn(name, t, value, LEVELS)
        return jnp.where(self.lane >= LEVELS, here, self.turn(name, t - 1, value, LEVELS))


def north(value):
    return pltpu.roll(value, EXT_ROWS - 1, 0)


def south(value):
    return pltpu.roll(value, 1, 0)


def polar_kernel(sz, h_ref, w_ref, near_h_ref, near_w_ref, sides_ref, geo_ref, wave_ref, far_ref, near_q_ref, *refs):
    out_refs, (far_out, near_out, tend_ref, pole_ref, ext) = refs[:-5], refs[-5:]
    far_out[...] = far_ref[...]
    near_out[...] = near_q_ref[...]
    if sz.near_only:
        far_ref = None
    band = lax.axis_index("lat")
    ring = Tiles(sz)
    lane = ring.lane
    tiles, stack, rows, work = sz.tiles, sz.stack, sz.rows, sz.work
    even = lax.rem(band, 2) == 0
    for f, value in enumerate((h_ref[...], w_ref[:, 1, :], w_ref[:, 0, :])):
        ext[f, :rows, sz.end :] = jnp.zeros((rows, LANES), jnp.float32)
        ext[f, :rows, : sz.merged] = value
    add_rows(sz, ext, near_h_ref, near_w_ref, None, far_ref)
    inv_cos, sin_centre, cos_face = geo_ref[band, 0], geo_ref[band, 1], geo_ref[band, 2]
    ratio = sz.ratio

    def tile(f, t):
        return ext[f, :, LANES * t : LANES * (t + 1)]

    kept = {}

    def zonal(t):
        if t not in kept:
            thick_e = ring.east("h", t, functools.partial(tile, 0))
            wind_e = ring.east("u", t, functools.partial(tile, 2))
            flux = 0.25 * (tile(2, t) + wind_e) * (tile(0, t) + thick_e) * inv_cos
            if t == tiles - 1:
                flux = jnp.where(lane < sz.tail - LEVELS, flux, 0.0)
            kept[t] = (flux, thick_e)
        return kept[t]

    for t in range(tiles):
        flux, thick_e = zonal(t)
        thick, wind_v, wind_u = tile(0, t), tile(1, t), tile(2, t)
        flux_w = ring.west("f", t, lambda s: zonal(s)[0])
        thick_w = ring.west("hw", t, functools.partial(tile, 0))
        thick_n = north(thick)
        flux_n = (0.25 * ratio) * (wind_v + north(wind_v)) * (thick + thick_n) * cos_face
        thick_tend = -((flux - flux_w) + (flux_n - south(flux_n)) * inv_cos)
        wind_u_tend = sin_centre * wind_v - (thick_e - thick_w) * (0.5 * inv_cos)
        wind_v_tend = -sin_centre * wind_u - (0.5 * ratio) * (thick_n - south(thick))
        spare = 0.0
        if t == tiles - 1:
            last = sz.tail - LEVELS
            columns = [(tile(0, 0), 0), (thick, last), (tile(2, 0), 0), (wind_u, last)]
            for k, (source, at) in reversed(list(enumerate(columns))):
                to = sz.tail + LEVELS * k
                spare = jnp.where(lane < to + LEVELS, pltpu.roll(source, (to - at) % LANES, 1), spare)
        for f, tend in enumerate((thick_tend, wind_u_tend, wind_v_tend, thick)):
            if sz.near_only:
                alone = jnp.where(band < sz.n_lat // 2, tend[:1], tend[rows - 1 : rows])
                if t == tiles - 1:
                    alone = jnp.where(lane[:1] < sz.tail, alone, 0.0)
                pole_ref[stack * f + t : stack * f + t + 1] = alone
            if f == 3:
                continue
            if t == tiles - 1:
                tend = jnp.where(lane < sz.tail, tend, spare)
            if sz.near_only:
                tend = jnp.where(even, north(tend), tend)
            tend_ref[pl.ds(stack * work * f + t, work, stride=stack), :] = tend[:work]
    for f in range(3):
        for t in range(tiles, stack):
            tend_ref[pl.ds(stack * work * f + t, work, stride=stack), :] = jnp.zeros((work, LANES), jnp.float32)
    used = stack * sz.units
    if used < tend_ref.shape[0]:
        tend_ref[used:, :] = jnp.zeros((tend_ref.shape[0] - used, LANES), jnp.float32)
    sides = [sides_ref[:EXT_ROWS], sides_ref[EXT_ROWS:]]
    if sz.near_only:
        sums = pole_sums(sz, pole_ref, wave_ref, spare, band)
        row = lax.broadcasted_iota(jnp.int32, (EXT_ROWS, LANES), 0)
        for k, total in enumerate(sums):
            sides = [jnp.where(row == rows + k, total, side) for side in sides]
    here = lax.axis_index("lon")
    for k, out_ref in enumerate(out_refs):
        out_ref[: sz.size] = tend_ref[sz.piece(k), :]
        eastward = sz.partner(k) == lax.rem(here + 1, sz.n_lon)
        out_ref[sz.size :] = jnp.where(eastward, sides[1], sides[0])


def pole_sums(sz, pole_ref, wave_ref, spare, band):
    stack, rows = sz.stack, sz.rows
    lane = lax.broadcasted_iota(jnp.int32, (1, LANES), 1)
    sides = jnp.where(band < sz.n_lat // 2, spare[:1], spare[rows - 1 : rows])
    found = [jnp.zeros((1, LANES), jnp.float32), pltpu.roll(sides, (LANES // 2 - sz.tail) % LANES, 1)]
    for f in range(4):
        if sz.tiles < stack:
            pole_ref[stack * f + sz.tiles : stack * (f + 1)] = jnp.zeros((stack - sz.tiles, LANES), jnp.float32)
        values = pole_ref[stack * f : stack * (f + 1)]
        for k, terms in enumerate((values, values * wave_ref[0], values * wave_ref[1])):
            total = jnp.sum(terms, axis=0, keepdims=True)
            for step in (64, 32, 16):
                total = total + pltpu.roll(total, step, 1)
            row, place = divmod(3 * f + k, PER_TILE)
            inside = (lane >= LEVELS * place) & (lane < LEVELS * (place + 1))
            found[row] = jnp.where(inside, total, found[row])
    return found


def pole_waves(sz, rows_in, inv_cos, sign):
    n_lon = sz.n_lon
    lane = lax.broadcasted_iota(jnp.int32, (1, LANES), 1)

    def value(s, place):
        row, at = divmod(place, PER_TILE)
        return pltpu.roll(rows_in[s % n_lon, row : row + 1], (-LEVELS * at) % LANES, 1)

    theta = 2 * math.pi / sz.nlon
    ends = (1.0, math.cos(theta * (sz.columns - 1)), math.sin(theta * (sz.columns - 1)))
    sums = [[[value(s, 3 * f + k) for k in range(3)] for f in range(4)] for s in range(n_lon)]
    for s in range(n_lon):
        thick_w, thick_e = value(s, 13), value(s + 1, 12)
        flux = 0.25 * (value(s, 15) + value(s + 1, 14)) * (thick_w + thick_e) * inv_cos
        slope = 0.5 * inv_cos
        after = (s + 1) % n_lon
        for f, (west_of, east_of) in enumerate(((flux, flux), (slope * thick_e, slope * thick_w))):
            for k in range(3):
                sums[s][f][k] = sums[s][f][k] - west_of * ends[k]
            for k in range(2):
                sums[after][f][k] = sums[after][f][k] + east_of
    result = []
    for f in range(3):
        waves_of = [0.0, 0.0, 0.0]
        for s in range(n_lon):
            level, cosine, sine = sums[s][f]
            if f == 2:
                level = level + (0.5 * sz.ratio) * sign * sums[s][3][0]
                cosine = cosine - (0.5 * sz.ratio) * sign * sums[s][3][1]
                sine = sine - (0.5 * sz.ratio) * sign * sums[s][3][2]
            c, d = math.cos(2 * math.pi * s / n_lon), math.sin(2 * math.pi * s / n_lon)
            waves_of[0] = waves_of[0] + level
            waves_of[1] = waves_of[1] + (c * cosine - d * sine)
            waves_of[2] = waves_of[2] + (d * cosine + c * sine)
        spread = []
        for k, total in enumerate(waves_of):
            total = jnp.where(lane < LEVELS, total * ((1.0 if k == 0 else 2.0) / sz.nlon), 0.0)
            for step in (16, 32, 64):
                total = total + pltpu.roll(total, step, 1)
            spread.append(total)
        result.append(spread)
    return result


def rest_kernel(sz, masks_ref, h_ref, w_ref, q_ref, near_h_ref, near_w_ref, near_q_ref, far_ref, geo_ref, wave_ref, after_ref, *refs):
    met_refs, (new_w_ref, new_h_ref, mass_ref, ext, pole_in) = refs[: sz.n_lon], refs[sz.n_lon :]
    band = lax.axis_index("lat")
    ring = Tiles(sz)
    lane = ring.lane
    tiles, rows = sz.tiles, sz.rows
    for f in range(6):
        if f < 2 or f == 5:
            value = (h_ref[...], w_ref[:, 1, :], w_ref[:, 0, :])[min(f, 2)]
        else:
            value = q_ref[f - 2].astype(jnp.float32)
        ext[f, :rows, : sz.merged] = value
    add_rows(sz, ext, near_h_ref, near_w_ref, near_q_ref, far_ref)
    lane9 = lane[:rows]
    here = lax.axis_index("lon")
    from_e = from_w = met_refs[0][sz.size :]
    for k, met_ref in enumerate(met_refs):
        eastward = lax.rem(sz.partner(k) - here + sz.n_lon, sz.n_lon)
        pole_in[eastward] = met_ref[sz.size + 8 :]
        from_e = jnp.where(sz.partner(k) == lax.rem(here + 1, sz.n_lon), met_ref[sz.size :], from_e)
        from_w = jnp.where(sz.partner(k) == lax.rem(here + sz.n_lon - 1, sz.n_lon), met_ref[sz.size :], from_w)
    for place, f in enumerate((0, 5, 2, 3, 4)):
        after = pltpu.roll(from_e, (sz.tail - LEVELS * place) % LANES, 1)[:rows]
        before = pltpu.roll(from_w, (LANES - LEVELS - LEVELS * place) % LANES, 1)[:rows]
        own = ext[f, :rows, sz.end :]
        edge = jnp.where(lane9 < LANES - LEVELS, after, before)
        ext[f, :rows, sz.end :] = jnp.where(lane9 < sz.tail, own, edge)
    inv_cos, sin_centre, cos_face = geo_ref[band, 0], geo_ref[band, 1], geo_ref[band, 2]
    ratio = sz.ratio

    plain, alone = masks_ref[0], masks_ref[1]
    if sz.near_only:
        band = lax.axis_index("lat")
        low = band < sz.n_lat // 2
        pole_cos = jnp.where(low, inv_cos[:1], inv_cos[rows - 1 : rows])
        kept_waves = pole_waves(sz, pole_in.at[:, rows - 8 :], pole_cos, jnp.where(low, 1.0, -1.0))

    def stepped(f, t, value, tend):
        value = value + plain * tend
        if sz.near_only:
            level, cosine, sine = kept_waves[f]
            wave = level + cosine * wave_ref[0, t : t + 1] + sine * wave_ref[1, t : t + 1]
            value = value + alone * wave
        return value

    def tile(f, t):
        return ext[f, :, LANES * t : LANES * (t + 1)]

    kept = {}

    def zonal(t):
        if t not in kept:
            thick_e = ring.east("h", t, functools.partial(tile, 0))
            wind_e = ring.east("u", t, functools.partial(tile, 5))
            flux = 0.25 * (tile(5, t) + wind_e) * (tile(0, t) + thick_e) * inv_cos
            parts = []
            for k in range(3):
                q = tile(2 + k, t)
                q_e = ring.east(k, t, functools.partial(tile, 2 + k))
                parts.append(DIFFUSION * (q_e - q) - flux * (0.5 * (q + q_e)))
            kept[t] = (flux, thick_e, parts)
        return kept[t]

    for t in range(tiles):
        span = sz.span(t)
        lanes = slice(LANES * t, LANES * t + span)
        flux, thick_e, parts = zonal(t)
        thick, wind_u, wind_v = tile(0, t), tile(5, t), tile(1, t)
        flux_w = ring.west("f", t, lambda s: zonal(s)[0])
        thick_w = ring.west("hw", t, functools.partial(tile, 0))
        thick_n = north(thick)
        flux_n = (0.25 * ratio) * (wind_v + north(wind_v)) * (thick + thick_n) * cos_face
        thick_tend = -((flux - flux_w) + (flux_n - south(flux_n)) * inv_cos)
        wind_u_tend = sin_centre * wind_v - (thick_e - thick_w) * (0.5 * inv_cos)
        wind_v_tend = -sin_centre * wind_u - (0.5 * ratio) * (thick_n - south(thick))
        new_h_ref[:, lanes] = stepped(0, t, thick, thick_tend)[:rows, :span]
        new_w_ref[0, :, lanes] = stepped(1, t, wind_u, wind_u_tend)[:rows, :span]
        new_w_ref[1, :, lanes] = stepped(2, t, wind_v, wind_v_tend)[:rows, :span]
        for k in range(3):
            q = tile(2 + k, t)
            q_n = north(q)
            zonal_part = parts[k] - ring.west(("p", k), t, lambda s: zonal(s)[2][k])
            lap = q_n + south(q) - 2.0 * q
            over = flux_n * (0.5 * (q + q_n))
            merid_part = DIFFUSION * lap - (over - south(over)) * inv_cos
            mass = thick * q + TIME_STEP * (zonal_part + merid_part)
            mass_ref[k, :, lanes] = mass[:rows, :span].astype(jnp.bfloat16)


def sin_pi(y):
    y = jnp.where(y > 0.5, 1.0 - y, jnp.where(y < -0.5, -1.0 - y, y))
    s = y * y
    series = [(-1) ** i * math.pi ** (2 * i + 1) / math.factorial(2 * i + 1) for i in range(7)]
    total = series[-1]
    for factor in reversed(series[:-1]):
        total = total * s + factor
    return total * y


def share_of(sz, i):
    unit = lax.axis_index("lon") * sz.share + i
    return unit // sz.work, sz.first() + lax.rem(unit, sz.work)


def weights_kernel(sz, cut_ref, n_ref, inverse_ref, after_ref, weights_ref, masks_ref):
    band = lax.axis_index("lat")
    row = lax.broadcasted_iota(jnp.int32, (EXT_ROWS, LANES), 0)
    cuts = jnp.full((EXT_ROWS, LANES), sz.nlon // 2, jnp.int32)
    for j in range(sz.rows):
        cuts = jnp.where(row == j, cut_ref[band * sz.rows + j], cuts)
    plain, alone = cuts >= sz.nlon // 2, sz.at_pole(row)
    masks_ref[0] = jnp.where(plain, TIME_STEP, 0.0)
    masks_ref[1] = jnp.where(alone, TIME_STEP, 0.0)
    masks_ref[2] = jnp.where(plain | alone, 0.0, TIME_STEP)
    size = PER_TILE * sz.stack
    for i in range(sz.share):
        width = (2 * cut_ref[band * sz.rows + share_of(sz, i)[1]] + 1).astype(jnp.float32)
        n = n_ref[...]
        turns = n * width
        turns = turns - jnp.round(turns * (0.5 / sz.nlon)) * (2.0 * sz.nlon)
        weights = sin_pi(turns * (1.0 / sz.nlon)) * inverse_ref[...]
        weights = jnp.where(n == 0.0, width * (1.0 / sz.nlon), weights)
        weights_ref[size * i : size * (i + 1)] = weights.astype(jnp.bfloat16)


def pass_kernel(sz, piece_ref, after_ref, also_after_ref, out_ref):
    out_ref[...] = piece_ref[...]


def filter_kernel(sz, weights_ref, geo_ref, *refs):
    n_lon, stack, share = sz.n_lon, sz.stack, sz.share
    in_refs, out_refs, (gathered, results) = refs[:n_lon], refs[n_lon : 2 * n_lon], refs[2 * n_lon :]
    for k, in_ref in enumerate(in_refs):
        gathered[sz.partner(k)] = in_ref[: sz.size]

    band = lax.axis_index("lat")
    lane = lax.broadcasted_iota(jnp.int32, (share, LANES), 1)
    place = lax.broadcasted_iota(jnp.int32, (share, LANES), 0)
    by_flux = by_thick = jnp.zeros((share, LANES), jnp.float32)
    for i in range(share):
        field, row = share_of(sz, i)
        inv_cos = geo_ref[band, 0, pl.ds(row, 1), :]
        by_flux = jnp.where((place == i) & (field == 0), inv_cos, by_flux)
        by_thick = jnp.where((place == i) & (field == 1), 0.5 * inv_cos, by_thick)
    sides = [gathered[s, pl.ds(sz.tiles - 1, share, stride=stack), :] for s in range(n_lon)]

    def column(s, k):
        return pltpu.roll(sides[s % n_lon], (-sz.tail - LEVELS * k) % LANES, 1)

    for s in range(n_lon):
        thick_w, thick_e = column(s, 1), column(s + 1, 0)
        flux = 0.25 * (column(s, 3) + column(s + 1, 2)) * (thick_w + thick_e) * by_flux
        west_of, east_of = flux + by_thick * thick_e, flux + by_thick * thick_w
        at = pl.ds(sz.tiles - 1, share, stride=stack)
        own = gathered[s, at, :]
        own = own - jnp.where(lane >= sz.tail - LEVELS, pltpu.roll(west_of, sz.tail - LEVELS, 1), 0.0)
        gathered[s, at, :] = jnp.where(lane < sz.tail, own, 0.0)
        at = pl.ds(0, share, stride=stack)
        after = (s + 1) % n_lon
        gathered[after, at, :] = gathered[after, at, :] + jnp.where(lane < LEVELS, east_of, 0.0)

    wide = lax.broadcasted_iota(jnp.int32, (stack, LANES), 1)
    rows = PER_TILE * stack
    for i in range(share):
        here = slice(stack * i, stack * (i + 1))
        pieces = [gathered[s, here] for s in range(n_lon)]
        circle = jnp.concatenate([jnp.concatenate(pieces[s:] + pieces[:s], axis=0) for s in range(n_lon)], axis=1)
        circle = circle.astype(jnp.bfloat16)
        spread = jnp.dot(weights_ref[rows * i : rows * (i + 1)], circle, preferred_element_type=jnp.float32)
        for s in range(n_lon):
            same = spread[:stack, LANES * s : LANES * (s + 1)]
            carried = None
            for e in range(1, PER_TILE):
                part = spread[stack * e : stack * (e + 1), LANES * s : LANES * (s + 1)]
                part = pltpu.roll(part, LEVELS * e, 1)
                inside = wide >= LEVELS * e
                same = same + jnp.where(inside, part, 0.0)
                over = jnp.where(inside, 0.0, part)
                carried = over if carried is None else carried + over
            results[s, here] = pltpu.roll(same, stack - 1, 0) + carried
    for k, out_ref in enumerate(out_refs):
        out_ref[...] = results[sz.partner(k)]


def finish_kernel(sz, masks_ref, base_w_ref, base_h_ref, *refs):
    back_refs, (new_w_ref, new_h_ref, back_ref, placed) = refs[: sz.n_lon], refs[sz.n_lon :]
    rows, stack = sz.rows, sz.stack
    for k, ref in enumerate(back_refs):
        back_ref[sz.piece(k), :] = ref[...]
    size = sz.work * stack
    for f in range(3):
        start = rows * stack * f
        if sz.near_only:
            for row in (0, rows - 1):
                placed[start + stack * row : start + stack * (row + 1)] = jnp.zeros((stack, LANES), jnp.float32)
        to = pl.multiple_of(start + sz.first() * stack, 8)
        placed[pl.ds(to, size), :] = back_ref[size * f : size * (f + 1)]
    scale = masks_ref[2][:rows]
    for f in range(3):
        for t in range(sz.tiles):
            span = sz.span(t)
            lanes = slice(LANES * t, LANES * t + span)
            change = (scale * placed[pl.ds(rows * stack * f + t, rows, stride=stack), :])[:, :span]
            if f == 0:
                new_h_ref[:, lanes] = base_h_ref[:, lanes] + change
            else:
                new_w_ref[:, f - 1, lanes] = base_w_ref[f - 1, :, lanes] + change


def local(winds, thickness, tracers, cutoff):
    n_lat = lax.axis_size("lat")
    n_lon = lax.axis_size("lon")
    rows, merged = thickness.shape
    sz = Sizes(rows, merged, n_lat, n_lon)
    f32 = jnp.float32
    vmem = pl.BlockSpec(memory_space=pltpu.VMEM)
    smem = pl.BlockSpec(memory_space=pltpu.SMEM)
    hbm = pl.BlockSpec(memory_space=pltpu.HBM)
    anywhere = pl.BlockSpec(memory_space=pl.ANY)

    def shaped(*shape):
        return jax.ShapeDtypeStruct(shape, f32)

    def call(kernel, name, in_specs, out_shape, scratch=(), limit=LIMIT):
        return pl.pallas_call(
            functools.partial(kernel, sz),
            out_shape=out_shape,
            in_specs=in_specs,
            out_specs=jax.tree.map(lambda _: vmem, out_shape),
            scratch_shapes=list(scratch),
            compiler_params=pltpu.CompilerParams(vmem_limit_bytes=limit),
            name=name,
        )

    geo = jnp.asarray(geometry(sz))
    wave = jnp.asarray(waves(sz))
    n, inverse = (jnp.asarray(table) for table in offsets(sz))

    wind_rows = jnp.swapaxes(winds, 0, 1)
    tracer_rows = jnp.swapaxes(tracers, 0, 1)
    far_row, near_row = shaped(5 * sz.stack, LANES), shaped(3 * sz.stack, LANES)
    kept = [((1,), f32), ((2,), f32), ((3,), jnp.bfloat16)]
    near_q, far_rows, sides = call(
        edges_kernel,
        "edges",
        [hbm] * 3,
        (near_row, far_row, shaped(2 * EXT_ROWS, LANES)),
        [pltpu.VMEM((2,) + count + (merged,), dtype) for count, dtype in kept]
        + [
            pltpu.VMEM((rows,) + (count if count != (1,) else ()) + (lanes,), dtype)
            for lanes in (LANES, sz.tail)
            for count, dtype in kept
        ]
        + [pltpu.SemaphoreType.DMA((3, 4))],
        limit=MOST_VMEM,
    )(thickness, wind_rows, tracer_rows)

    near = [(band * n_lon + i, (band ^ 1) * n_lon + i) for band in range(n_lat) for i in range(n_lon)]
    far = []
    for band in range(n_lat):
        other = band - 1 if band % 2 == 0 else band + 1
        for i in range(n_lon):
            if 0 <= other < n_lat:
                far.append((band * n_lon + i, other * n_lon + i))
            else:
                far.append((band * n_lon + i, band * n_lon + (i + n_lon // 2) % n_lon))
    near_h = lax.ppermute(thickness, ("lat", "lon"), near)
    near_w = lax.ppermute(wind_rows, ("lat", "lon"), near)
    if not sz.near_only:
        far_rows = lax.ppermute(far_rows, ("lat", "lon"), far)

    order = [sz.turns(False), sz.turns(True)]

    def meetings(shares):
        got = [shares[0]]
        for k in range(1, n_lon):
            sectors = [(band, i, i ^ order[band % 2][k]) for band in range(n_lat) for i in range(n_lon)]
            got.append(lax.ppermute(shares[k], ("lat", "lon"), [(b * n_lon + i, b * n_lon + j) for b, i, j in sectors]))
        return got

    all_pieces = pltpu.VMEM((n_lon, sz.size, LANES), f32)
    *tends, far_rows, near_q = call(
        polar_kernel,
        "polar",
        [vmem] * 9,
        [shaped(sz.size + EXT_ROWS, LANES)] * n_lon + [far_row, near_row],
        [
            pltpu.VMEM((n_lon * sz.size, LANES), f32),
            pltpu.VMEM((4 * sz.stack, LANES), f32),
            pltpu.VMEM((3, EXT_ROWS, sz.tiles * LANES), f32),
        ],
    )(thickness, wind_rows, near_h, near_w, sides, geo, wave, far_rows, near_q)
    met = meetings(tends)
    near_q = lax.ppermute(near_q, ("lat", "lon"), near)
    from_far = lax.ppermute(far_rows, ("lat", "lon"), far) if sz.near_only else far_rows
    weights, masks = call(
        weights_kernel,
        "weights",
        [smem, vmem, vmem, anywhere],
        (
            jax.ShapeDtypeStruct((sz.share * PER_TILE * sz.stack, n_lon * sz.stack), jnp.bfloat16),
            shaped(3, EXT_ROWS, LANES),
        ),
    )(cutoff, n, inverse, tends[0])
    worked = call(
        filter_kernel,
        "filter",
        [vmem] * 2 + [vmem] * n_lon,
        [shaped(sz.size, LANES)] * n_lon,
        [all_pieces, all_pieces],
    )(weights, geo, *met)
    held = call(pass_kernel, "pass", [vmem] + [anywhere] * 2, shaped(sz.size, LANES))(worked[-1], from_far, near_q)
    worked = [*worked[:-1], held]
    back = meetings(worked)

    base_w, base_h, mass = call(
        rest_kernel,
        "rest",
        [vmem] * 10 + [anywhere] + [vmem] * n_lon,
        (shaped(2, rows, merged), shaped(rows, merged), jax.ShapeDtypeStruct(tracers.shape, jnp.bfloat16)),
        [pltpu.VMEM((6, EXT_ROWS, sz.tiles * LANES), f32), pltpu.VMEM((n_lon, 8, LANES), f32)],
    )(masks, thickness, wind_rows, tracers, near_h, near_w, near_q, from_far, geo, wave, worked[0], *met)

    new_w, new_h = call(
        finish_kernel,
        "finish",
        [vmem] * (3 + n_lon),
        (shaped(*wind_rows.shape), shaped(rows, merged)),
        [pltpu.VMEM((n_lon * sz.size, LANES), f32), pltpu.VMEM((3 * rows * sz.stack, LANES), f32)],
    )(masks, base_w, base_h, *back)
    return jnp.swapaxes(new_w, 0, 1), new_h, mass


def solution(mesh):
    in_specs = (P(None, "lat", "lon"), P("lat", "lon"), P(None, "lat", "lon"), P())
    out_specs = (P(None, "lat", "lon"), P("lat", "lon"), P(None, "lat", "lon"))
    return jax.shard_map(local, mesh=mesh, in_specs=in_specs, out_specs=out_specs, check_vma=False)
```

```python
import functools
import math

import jax
import jax.numpy as jnp
import numpy as np
from jax import lax
from jax.experimental import pallas as pl
from jax.experimental.pallas import tpu as pltpu
from jax.sharding import PartitionSpec as P

LEVELS = 16
TIME_STEP = 0.05
DIFFUSION = 0.5
LANES = 128
PER_TILE = LANES // LEVELS
EXT_ROWS = 16
LIMIT = 48 * 1024 * 1024
MOST_VMEM = 64 * 1024 * 1024 - 10500 * 1024


class Sizes:
    def __init__(self, rows, merged, n_lat, n_lon):
        self.rows = rows
        self.merged = merged
        self.columns = merged // LEVELS
        self.n_lat = n_lat
        self.n_lon = n_lon
        self.nlat = rows * n_lat
        self.nlon = self.columns * n_lon
        self.ratio = 2.0 * self.nlat / self.nlon
        self.tiles = -(-merged // LANES)
        self.end = (self.tiles - 1) * LANES
        self.tail = merged - self.end
        self.stack = -(-(self.tiles + 1) // 8) * 8
        self.near_only = rows <= self.nlat // 6 < 2 * rows
        self.work = rows - 1 if self.near_only else rows
        self.units = 3 * self.work
        self.share = -(-self.units // n_lon)
        self.size = self.share * self.stack
        assert self.tail <= LANES - 4 * LEVELS and rows + 2 <= EXT_ROWS and n_lat % 2 == 0
        assert n_lon >= 4 and n_lon & (n_lon - 1) == 0

    def span(self, tile):
        return self.tail if tile == self.tiles - 1 else LANES

    def first(self):
        return jnp.where(lax.rem(lax.axis_index("lat"), 2) == 0, 1, 0) if self.near_only else 0

    def at_pole(self, row):
        band = lax.axis_index("lat")
        pole = jnp.where(band == 0, 0, jnp.where(band == self.n_lat - 1, self.rows - 1, -1))
        return row == (pole if self.near_only else -1)

    def turns(self, odd):
        middle, last = list(range(1, self.n_lon - 1)), self.n_lon - 1
        return [0, middle[-1], last] + middle[-2::-1] if odd else [0, last] + middle

    def partner(self, k):
        odd = lax.rem(lax.axis_index("lat"), 2) == 1
        turn = jnp.where(odd, self.turns(True)[k], self.turns(False)[k])
        return jnp.bitwise_xor(lax.axis_index("lon"), turn)

    def piece(self, k):
        return pl.ds(pl.multiple_of(self.partner(k) * self.size, 8), self.size)


def geometry(sz):
    table = np.zeros((sz.n_lat, 3, EXT_ROWS, LANES), np.float64)

    def face(j):
        return math.sin((j + 1) * math.pi / sz.nlat) if 0 <= j < sz.nlat - 1 else 0.0

    for band in range(sz.n_lat):
        for row in range(sz.rows):
            j = band * sz.rows + row
            centre = (j + 0.5) * math.pi / sz.nlat - math.pi / 2
            table[band, 0, row] = 1.0 / math.cos(centre)
            table[band, 1, row] = math.sin(centre)
            table[band, 2, row] = face(j)
        table[band, 2, EXT_ROWS - 1] = face(band * sz.rows - 1)
    return table.astype(np.float32)


def offsets(sz):
    shift, out_tile = np.divmod(np.arange(PER_TILE * sz.stack), sz.stack)
    sector, in_tile = np.divmod(np.arange(sz.n_lon * sz.stack), sz.stack)
    n = (PER_TILE * (out_tile - 1) + shift)[:, None] - (PER_TILE * in_tile + sz.columns * sector)[None, :]
    n = (n + sz.nlon // 2) % sz.nlon - sz.nlon // 2
    with np.errstate(divide="ignore"):
        inverse = np.where(n == 0, 0.0, 1.0 / (sz.nlon * np.sin(np.pi * n / sz.nlon)))
    return n.astype(np.float32), inverse.astype(np.float32)


def waves(sz):
    column = PER_TILE * np.arange(sz.stack)[:, None] + np.arange(LANES)[None, :] // LEVELS
    angle = 2 * np.pi * column / sz.nlon
    return np.stack([np.cos(angle), np.sin(angle)]).astype(np.float32)


def edges_kernel(sz, h_hbm, w_hbm, q_hbm, near_ref, far_ref, sides_ref, *scratch):
    row_refs, first_refs, last_refs, sems = scratch[:3], scratch[3:6], scratch[6:9], scratch[9]
    rows, last = sz.rows, sz.rows - 1
    even = lax.rem(lax.axis_index("lat"), 2) == 0
    copies = []
    for i, source in enumerate((h_hbm, w_hbm, q_hbm)):
        for k, row in enumerate((0, last)):
            one = source.at[pl.ds(row, 1)] if i == 0 else source.at[row]
            copies.append(pltpu.make_async_copy(one, row_refs[i].at[k], sems.at[i, k]))
        for k, (start, to) in enumerate(((0, first_refs[i]), (sz.end, last_refs[i]))):
            lanes = pl.ds(start, to.shape[-1])
            cut = source.at[:, lanes] if i == 0 else source.at[:, :, lanes]
            copies.append(pltpu.make_async_copy(cut, to, sems.at[i, 2 + k]))
    for copy in copies:
        copy.start()
    for copy in copies:
        copy.wait()
    h_rows, w_rows, q_rows = row_refs
    for t in range(sz.tiles):
        wide = sz.span(t)
        lanes = slice(LANES * t, LANES * t + wide)
        q = [q_rows[k, :, lanes].astype(jnp.float32) for k in range(2)]
        for f in range(5):
            if f == 0:
                first, final = h_rows[0, :, lanes], h_rows[1, :, lanes]
            elif f == 1:
                first, final = w_rows[0, 1:2, lanes], w_rows[1, 1:2, lanes]
            else:
                first, final = q[0][f - 2 : f - 1], q[1][f - 2 : f - 1]
                at = sz.stack * (f - 2) + t
                near_ref[at : at + 1, :wide] = jnp.where(even, final, first)
            at = sz.stack * f + t
            far_ref[at : at + 1, :wide] = jnp.where(even, first, final)
    sides_ref[...] = jnp.zeros(sides_ref.shape, jnp.float32)
    for k, (refs, at) in enumerate(((first_refs, 0), (last_refs, sz.tail - LEVELS))):
        columns = slice(at, at + LEVELS)
        for f in range(5):
            if f == 0:
                value = refs[0][:, columns]
            elif f == 1:
                value = refs[1][:, 0, columns]
            else:
                value = refs[2][:, f - 2, columns].astype(jnp.float32)
            sides_ref[EXT_ROWS * k : EXT_ROWS * k + rows, LEVELS * f : LEVELS * (f + 1)] = value


def add_rows(sz, ext, near_h_ref, near_w_ref, near_q_ref, far_ref):
    band = lax.axis_index("lat")
    even = lax.rem(band, 2) == 0
    over_pole = (band == 0) | (band == sz.n_lat - 1)
    last = sz.rows - 1
    for f in range(2 if near_q_ref is None else 5):
        flip = jnp.where(over_pole, -1.0, 1.0) if f == 1 else 1.0
        for t in range(sz.tiles):
            lanes = slice(LANES * t, LANES * t + sz.span(t))
            if f == 0:
                near = jnp.where(even, near_h_ref[0:1, lanes], near_h_ref[last : sz.rows, lanes])
            elif f == 1:
                near = jnp.where(even, near_w_ref[0, 1:2, lanes], near_w_ref[last, 1:2, lanes])
            else:
                at = sz.stack * (f - 2) + t
                near = near_q_ref[at : at + 1, : sz.span(t)]
            at = sz.stack * f + t
            far = jnp.zeros_like(near) if far_ref is None else far_ref[at : at + 1, : sz.span(t)] * flip
            ext[f, sz.rows : sz.rows + 1, lanes] = jnp.where(even, near, far)
            ext[f, EXT_ROWS - 1 : EXT_ROWS, lanes] = jnp.where(even, far, near)


class Tiles:
    def __init__(self, sz):
        self.sz = sz
        self.lane = lax.broadcasted_iota(jnp.int32, (EXT_ROWS, LANES), 1)
        self.turned = {}

    def turn(self, name, t, value, step):
        key = (name, t % self.sz.tiles, step)
        if key not in self.turned:
            self.turned[key] = pltpu.roll(value(t % self.sz.tiles), step % LANES, 1)
        return self.turned[key]

    def east(self, name, t, value):
        here = self.turn(name, t, value, -LEVELS)
        return jnp.where(self.lane < LANES - LEVELS, here, self.turn(name, t + 1, value, -LEVELS))

    def west(self, name, t, value):
        here = self.turn(name, t, value, LEVELS)
        return jnp.where(self.lane >= LEVELS, here, self.turn(name, t - 1, value, LEVELS))


def north(value):
    return pltpu.roll(value, EXT_ROWS - 1, 0)


def south(value):
    return pltpu.roll(value, 1, 0)


def polar_kernel(sz, h_ref, w_ref, near_h_ref, near_w_ref, sides_ref, geo_ref, wave_ref, far_ref, near_q_ref, *refs):
    out_refs, (far_out, near_out, tend_ref, pole_ref, ext) = refs[:-5], refs[-5:]
    far_out[...] = far_ref[...]
    near_out[...] = near_q_ref[...]
    if sz.near_only:
        far_ref = None
    band = lax.axis_index("lat")
    ring = Tiles(sz)
    lane = ring.lane
    tiles, stack, rows, work = sz.tiles, sz.stack, sz.rows, sz.work
    even = lax.rem(band, 2) == 0
    for f, value in enumerate((h_ref[...], w_ref[:, 1, :], w_ref[:, 0, :])):
        ext[f, :rows, sz.end :] = jnp.zeros((rows, LANES), jnp.float32)
        ext[f, :rows, : sz.merged] = value
    add_rows(sz, ext, near_h_ref, near_w_ref, None, far_ref)
    inv_cos, sin_centre, cos_face = geo_ref[band, 0], geo_ref[band, 1], geo_ref[band, 2]
    ratio = sz.ratio

    def tile(f, t):
        return ext[f, :, LANES * t : LANES * (t + 1)]

    kept = {}

    def zonal(t):
        if t not in kept:
            thick_e = ring.east("h", t, functools.partial(tile, 0))
            wind_e = ring.east("u", t, functools.partial(tile, 2))
            flux = 0.25 * (tile(2, t) + wind_e) * (tile(0, t) + thick_e) * inv_cos
            if t == tiles - 1:
                flux = jnp.where(lane < sz.tail - LEVELS, flux, 0.0)
            kept[t] = (flux, thick_e)
        return kept[t]

    for t in range(tiles):
        flux, thick_e = zonal(t)
        thick, wind_v, wind_u = tile(0, t), tile(1, t), tile(2, t)
        flux_w = ring.west("f", t, lambda s: zonal(s)[0])
        thick_w = ring.west("hw", t, functools.partial(tile, 0))
        thick_n = north(thick)
        flux_n = (0.25 * ratio) * (wind_v + north(wind_v)) * (thick + thick_n) * cos_face
        thick_tend = -((flux - flux_w) + (flux_n - south(flux_n)) * inv_cos)
        wind_u_tend = sin_centre * wind_v - (thick_e - thick_w) * (0.5 * inv_cos)
        wind_v_tend = -sin_centre * wind_u - (0.5 * ratio) * (thick_n - south(thick))
        spare = 0.0
        if t == tiles - 1:
            last = sz.tail - LEVELS
            columns = [(tile(0, 0), 0), (thick, last), (tile(2, 0), 0), (wind_u, last)]
            for k, (source, at) in reversed(list(enumerate(columns))):
                to = sz.tail + LEVELS * k
                spare = jnp.where(lane < to + LEVELS, pltpu.roll(source, (to - at) % LANES, 1), spare)
        for f, tend in enumerate((thick_tend, wind_u_tend, wind_v_tend, thick)):
            if sz.near_only:
                alone = jnp.where(band < sz.n_lat // 2, tend[:1], tend[rows - 1 : rows])
                if t == tiles - 1:
                    alone = jnp.where(lane[:1] < sz.tail, alone, 0.0)
                pole_ref[stack * f + t : stack * f + t + 1] = alone
            if f == 3:
                continue
            if t == tiles - 1:
                tend = jnp.where(lane < sz.tail, tend, spare)
            if sz.near_only:
                tend = jnp.where(even, north(tend), tend)
            tend_ref[pl.ds(stack * work * f + t, work, stride=stack), :] = tend[:work]
    for f in range(3):
        for t in range(tiles, stack):
            tend_ref[pl.ds(stack * work * f + t, work, stride=stack), :] = jnp.zeros((work, LANES), jnp.float32)
    used = stack * sz.units
    if used < tend_ref.shape[0]:
        tend_ref[used:, :] = jnp.zeros((tend_ref.shape[0] - used, LANES), jnp.float32)
    sides = [sides_ref[:EXT_ROWS], sides_ref[EXT_ROWS:]]
    if sz.near_only:
        sums = pole_sums(sz, pole_ref, wave_ref, spare, band)
        row = lax.broadcasted_iota(jnp.int32, (EXT_ROWS, LANES), 0)
        for k, total in enumerate(sums):
            sides = [jnp.where(row == rows + k, total, side) for side in sides]
    here = lax.axis_index("lon")
    for k, out_ref in enumerate(out_refs):
        out_ref[: sz.size] = tend_ref[sz.piece(k), :]
        eastward = sz.partner(k) == lax.rem(here + 1, sz.n_lon)
        out_ref[sz.size :] = jnp.where(eastward, sides[1], sides[0])


def pole_sums(sz, pole_ref, wave_ref, spare, band):
    stack, rows = sz.stack, sz.rows
    lane = lax.broadcasted_iota(jnp.int32, (1, LANES), 1)
    sides = jnp.where(band < sz.n_lat // 2, spare[:1], spare[rows - 1 : rows])
    found = [jnp.zeros((1, LANES), jnp.float32), pltpu.roll(sides, (LANES // 2 - sz.tail) % LANES, 1)]
    for f in range(4):
        if sz.tiles < stack:
            pole_ref[stack * f + sz.tiles : stack * (f + 1)] = jnp.zeros((stack - sz.tiles, LANES), jnp.float32)
        values = pole_ref[stack * f : stack * (f + 1)]
        for k, terms in enumerate((values, values * wave_ref[0], values * wave_ref[1])):
            total = jnp.sum(terms, axis=0, keepdims=True)
            for step in (64, 32, 16):
                total = total + pltpu.roll(total, step, 1)
            row, place = divmod(3 * f + k, PER_TILE)
            inside = (lane >= LEVELS * place) & (lane < LEVELS * (place + 1))
            found[row] = jnp.where(inside, total, found[row])
    return found


def pole_waves(sz, rows_in, inv_cos, sign):
    n_lon = sz.n_lon
    lane = lax.broadcasted_iota(jnp.int32, (1, LANES), 1)

    def value(s, place):
        row, at = divmod(place, PER_TILE)
        return pltpu.roll(rows_in[s % n_lon, row : row + 1], (-LEVELS * at) % LANES, 1)

    theta = 2 * math.pi / sz.nlon
    ends = (1.0, math.cos(theta * (sz.columns - 1)), math.sin(theta * (sz.columns - 1)))
    sums = [[[value(s, 3 * f + k) for k in range(3)] for f in range(4)] for s in range(n_lon)]
    for s in range(n_lon):
        thick_w, thick_e = value(s, 13), value(s + 1, 12)
        flux = 0.25 * (value(s, 15) + value(s + 1, 14)) * (thick_w + thick_e) * inv_cos
        slope = 0.5 * inv_cos
        after = (s + 1) % n_lon
        for f, (west_of, east_of) in enumerate(((flux, flux), (slope * thick_e, slope * thick_w))):
            for k in range(3):
                sums[s][f][k] = sums[s][f][k] - west_of * ends[k]
            for k in range(2):
                sums[after][f][k] = sums[after][f][k] + east_of
    result = []
    for f in range(3):
        waves_of = [0.0, 0.0, 0.0]
        for s in range(n_lon):
            level, cosine, sine = sums[s][f]
            if f == 2:
                level = level + (0.5 * sz.ratio) * sign * sums[s][3][0]
                cosine = cosine - (0.5 * sz.ratio) * sign * sums[s][3][1]
                sine = sine - (0.5 * sz.ratio) * sign * sums[s][3][2]
            c, d = math.cos(2 * math.pi * s / n_lon), math.sin(2 * math.pi * s / n_lon)
            waves_of[0] = waves_of[0] + level
            waves_of[1] = waves_of[1] + (c * cosine - d * sine)
            waves_of[2] = waves_of[2] + (d * cosine + c * sine)
        spread = []
        for k, total in enumerate(waves_of):
            total = jnp.where(lane < LEVELS, total * ((1.0 if k == 0 else 2.0) / sz.nlon), 0.0)
            for step in (16, 32, 64):
                total = total + pltpu.roll(total, step, 1)
            spread.append(total)
        result.append(spread)
    return result


def rest_kernel(sz, masks_ref, h_ref, w_ref, q_ref, near_h_ref, near_w_ref, near_q_ref, far_ref, geo_ref, wave_ref, after_ref, *refs):
    met_refs, (new_w_ref, new_h_ref, mass_ref, ext, pole_in) = refs[: sz.n_lon], refs[sz.n_lon :]
    band = lax.axis_index("lat")
    ring = Tiles(sz)
    lane = ring.lane
    tiles, rows = sz.tiles, sz.rows
    for f in range(6):
        if f < 2 or f == 5:
            value = (h_ref[...], w_ref[:, 1, :], w_ref[:, 0, :])[min(f, 2)]
        else:
            value = q_ref[f - 2].astype(jnp.float32)
        ext[f, :rows, : sz.merged] = value
    add_rows(sz, ext, near_h_ref, near_w_ref, near_q_ref, far_ref)
    lane9 = lane[:rows]
    here = lax.axis_index("lon")
    from_e = from_w = met_refs[0][sz.size :]
    for k, met_ref in enumerate(met_refs):
        eastward = lax.rem(sz.partner(k) - here + sz.n_lon, sz.n_lon)
        pole_in[eastward] = met_ref[sz.size + 8 :]
        from_e = jnp.where(sz.partner(k) == lax.rem(here + 1, sz.n_lon), met_ref[sz.size :], from_e)
        from_w = jnp.where(sz.partner(k) == lax.rem(here + sz.n_lon - 1, sz.n_lon), met_ref[sz.size :], from_w)
    for place, f in enumerate((0, 5, 2, 3, 4)):
        after = pltpu.roll(from_e, (sz.tail - LEVELS * place) % LANES, 1)[:rows]
        before = pltpu.roll(from_w, (LANES - LEVELS - LEVELS * place) % LANES, 1)[:rows]
        own = ext[f, :rows, sz.end :]
        edge = jnp.where(lane9 < LANES - LEVELS, after, before)
        ext[f, :rows, sz.end :] = jnp.where(lane9 < sz.tail, own, edge)
    inv_cos, sin_centre, cos_face = geo_ref[band, 0], geo_ref[band, 1], geo_ref[band, 2]
    ratio = sz.ratio

    plain, alone = masks_ref[0], masks_ref[1]
    if sz.near_only:
        band = lax.axis_index("lat")
        low = band < sz.n_lat // 2
        pole_cos = jnp.where(low, inv_cos[:1], inv_cos[rows - 1 : rows])
        kept_waves = pole_waves(sz, pole_in.at[:, rows - 8 :], pole_cos, jnp.where(low, 1.0, -1.0))

    def stepped(f, t, value, tend):
        value = value + plain * tend
        if sz.near_only:
            level, cosine, sine = kept_waves[f]
            wave = level + cosine * wave_ref[0, t : t + 1] + sine * wave_ref[1, t : t + 1]
            value = value + alone * wave
        return value

    def tile(f, t):
        return ext[f, :, LANES * t : LANES * (t + 1)]

    kept = {}

    def zonal(t):
        if t not in kept:
            thick_e = ring.east("h", t, functools.partial(tile, 0))
            wind_e = ring.east("u", t, functools.partial(tile, 5))
            flux = 0.25 * (tile(5, t) + wind_e) * (tile(0, t) + thick_e) * inv_cos
            parts = []
            for k in range(3):
                q = tile(2 + k, t)
                q_e = ring.east(k, t, functools.partial(tile, 2 + k))
                parts.append(DIFFUSION * (q_e - q) - flux * (0.5 * (q + q_e)))
            kept[t] = (flux, thick_e, parts)
        return kept[t]

    for t in range(tiles):
        span = sz.span(t)
        lanes = slice(LANES * t, LANES * t + span)
        flux, thick_e, parts = zonal(t)
        thick, wind_u, wind_v = tile(0, t), tile(5, t), tile(1, t)
        flux_w = ring.west("f", t, lambda s: zonal(s)[0])
        thick_w = ring.west("hw", t, functools.partial(tile, 0))
        thick_n = north(thick)
        flux_n = (0.25 * ratio) * (wind_v + north(wind_v)) * (thick + thick_n) * cos_face
        thick_tend = -((flux - flux_w) + (flux_n - south(flux_n)) * inv_cos)
        wind_u_tend = sin_centre * wind_v - (thick_e - thick_w) * (0.5 * inv_cos)
        wind_v_tend = -sin_centre * wind_u - (0.5 * ratio) * (thick_n - south(thick))
        new_h_ref[:, lanes] = stepped(0, t, thick, thick_tend)[:rows, :span]
        new_w_ref[0, :, lanes] = stepped(1, t, wind_u, wind_u_tend)[:rows, :span]
        new_w_ref[1, :, lanes] = stepped(2, t, wind_v, wind_v_tend)[:rows, :span]
        for k in range(3):
            q = tile(2 + k, t)
            q_n = north(q)
            zonal_part = parts[k] - ring.west(("p", k), t, lambda s: zonal(s)[2][k])
            lap = q_n + south(q) - 2.0 * q
            over = flux_n * (0.5 * (q + q_n))
            merid_part = DIFFUSION * lap - (over - south(over)) * inv_cos
            mass = thick * q + TIME_STEP * (zonal_part + merid_part)
            mass_ref[k, :, lanes] = mass[:rows, :span].astype(jnp.bfloat16)


def sin_pi(y):
    y = jnp.where(y > 0.5, 1.0 - y, jnp.where(y < -0.5, -1.0 - y, y))
    s = y * y
    series = [(-1) ** i * math.pi ** (2 * i + 1) / math.factorial(2 * i + 1) for i in range(7)]
    total = series[-1]
    for factor in reversed(series[:-1]):
        total = total * s + factor
    return total * y


def share_of(sz, i):
    unit = lax.axis_index("lon") * sz.share + i
    return unit // sz.work, sz.first() + lax.rem(unit, sz.work)


def weights_kernel(sz, cut_ref, n_ref, inverse_ref, after_ref, weights_ref, masks_ref):
    band = lax.axis_index("lat")
    row = lax.broadcasted_iota(jnp.int32, (EXT_ROWS, LANES), 0)
    cuts = jnp.full((EXT_ROWS, LANES), sz.nlon // 2, jnp.int32)
    for j in range(sz.rows):
        cuts = jnp.where(row == j, cut_ref[band * sz.rows + j], cuts)
    plain, alone = cuts >= sz.nlon // 2, sz.at_pole(row)
    masks_ref[0] = jnp.where(plain, TIME_STEP, 0.0)
    masks_ref[1] = jnp.where(alone, TIME_STEP, 0.0)
    masks_ref[2] = jnp.where(plain | alone, 0.0, TIME_STEP)
    size = PER_TILE * sz.stack
    for i in range(sz.share):
        width = (2 * cut_ref[band * sz.rows + share_of(sz, i)[1]] + 1).astype(jnp.float32)
        n = n_ref[...]
        turns = n * width
        turns = turns - jnp.round(turns * (0.5 / sz.nlon)) * (2.0 * sz.nlon)
        weights = sin_pi(turns * (1.0 / sz.nlon)) * inverse_ref[...]
        weights = jnp.where(n == 0.0, width * (1.0 / sz.nlon), weights)
        weights_ref[size * i : size * (i + 1)] = weights.astype(jnp.bfloat16)


def pass_kernel(sz, piece_ref, after_ref, also_after_ref, out_ref):
    out_ref[...] = piece_ref[...]


def filter_kernel(sz, weights_ref, geo_ref, *refs):
    n_lon, stack, share = sz.n_lon, sz.stack, sz.share
    in_refs, out_refs, (gathered, results) = refs[:n_lon], refs[n_lon : 2 * n_lon], refs[2 * n_lon :]
    for k, in_ref in enumerate(in_refs):
        gathered[sz.partner(k)] = in_ref[: sz.size]

    band = lax.axis_index("lat")
    lane = lax.broadcasted_iota(jnp.int32, (share, LANES), 1)
    place = lax.broadcasted_iota(jnp.int32, (share, LANES), 0)
    by_flux = by_thick = jnp.zeros((share, LANES), jnp.float32)
    for i in range(share):
        field, row = share_of(sz, i)
        inv_cos = geo_ref[band, 0, pl.ds(row, 1), :]
        by_flux = jnp.where((place == i) & (field == 0), inv_cos, by_flux)
        by_thick = jnp.where((place == i) & (field == 1), 0.5 * inv_cos, by_thick)
    sides = [gathered[s, pl.ds(sz.tiles - 1, share, stride=stack), :] for s in range(n_lon)]

    def column(s, k):
        return pltpu.roll(sides[s % n_lon], (-sz.tail - LEVELS * k) % LANES, 1)

    for s in range(n_lon):
        thick_w, thick_e = column(s, 1), column(s + 1, 0)
        flux = 0.25 * (column(s, 3) + column(s + 1, 2)) * (thick_w + thick_e) * by_flux
        west_of, east_of = flux + by_thick * thick_e, flux + by_thick * thick_w
        at = pl.ds(sz.tiles - 1, share, stride=stack)
        own = gathered[s, at, :]
        own = own - jnp.where(lane >= sz.tail - LEVELS, pltpu.roll(west_of, sz.tail - LEVELS, 1), 0.0)
        gathered[s, at, :] = jnp.where(lane < sz.tail, own, 0.0)
        at = pl.ds(0, share, stride=stack)
        after = (s + 1) % n_lon
        gathered[after, at, :] = gathered[after, at, :] + jnp.where(lane < LEVELS, east_of, 0.0)

    wide = lax.broadcasted_iota(jnp.int32, (stack, LANES), 1)
    rows = PER_TILE * stack
    for i in range(share):
        here = slice(stack * i, stack * (i + 1))
        pieces = [gathered[s, here].astype(jnp.bfloat16) for s in range(n_lon)]
        circle = jnp.concatenate([jnp.concatenate(pieces[s:] + pieces[:s], axis=0) for s in range(n_lon)], axis=1)
        spread = jnp.dot(weights_ref[rows * i : rows * (i + 1)], circle, preferred_element_type=jnp.float32)
        for s in range(n_lon):
            same = spread[:stack, LANES * s : LANES * (s + 1)]
            carried = None
            for e in range(1, PER_TILE):
                part = spread[stack * e : stack * (e + 1), LANES * s : LANES * (s + 1)]
                part = pltpu.roll(part, LEVELS * e, 1)
                inside = wide >= LEVELS * e
                same = same + jnp.where(inside, part, 0.0)
                over = jnp.where(inside, 0.0, part)
                carried = over if carried is None else carried + over
            results[s, here] = pltpu.roll(same, stack - 1, 0) + carried
    for k, out_ref in enumerate(out_refs):
        out_ref[...] = results[sz.partner(k)]


def finish_kernel(sz, masks_ref, base_w_ref, base_h_ref, *refs):
    back_refs, (new_w_ref, new_h_ref, back_ref) = refs[: sz.n_lon], refs[sz.n_lon :]
    rows, work = sz.rows, sz.work
    for k, ref in enumerate(back_refs):
        back_ref[sz.piece(k), :] = ref[...]
    scale = masks_ref[2]
    even = lax.rem(lax.axis_index("lat"), 2) == 0
    for f in range(3):
        for t in range(sz.tiles):
            span = sz.span(t)
            lanes = slice(LANES * t, LANES * t + span)
            tend = back_ref[pl.ds(sz.stack * work * f + t, work, stride=sz.stack), :]
            if sz.near_only:
                tend = jnp.concatenate([tend, jnp.zeros((EXT_ROWS - work, LANES), jnp.float32)], axis=0)
                tend = jnp.where(even, south(tend), tend)
            change = (scale[:rows] * tend[:rows])[:, :span]
            if f == 0:
                new_h_ref[:, lanes] = base_h_ref[:, lanes] + change
            else:
                new_w_ref[:, f - 1, lanes] = base_w_ref[f - 1, :, lanes] + change


def local(winds, thickness, tracers, cutoff):
    n_lat = lax.axis_size("lat")
    n_lon = lax.axis_size("lon")
    rows, merged = thickness.shape
    sz = Sizes(rows, merged, n_lat, n_lon)
    f32 = jnp.float32
    vmem = pl.BlockSpec(memory_space=pltpu.VMEM)
    smem = pl.BlockSpec(memory_space=pltpu.SMEM)
    hbm = pl.BlockSpec(memory_space=pltpu.HBM)
    anywhere = pl.BlockSpec(memory_space=pl.ANY)

    def shaped(*shape):
        return jax.ShapeDtypeStruct(shape, f32)

    def call(kernel, name, in_specs, out_shape, scratch=(), limit=LIMIT):
        return pl.pallas_call(
            functools.partial(kernel, sz),
            out_shape=out_shape,
            in_specs=in_specs,
            out_specs=jax.tree.map(lambda _: vmem, out_shape),
            scratch_shapes=list(scratch),
            compiler_params=pltpu.CompilerParams(vmem_limit_bytes=limit),
            name=name,
        )

    geo = jnp.asarray(geometry(sz))
    wave = jnp.asarray(waves(sz))
    n, inverse = (jnp.asarray(table) for table in offsets(sz))

    wind_rows = jnp.swapaxes(winds, 0, 1)
    tracer_rows = jnp.swapaxes(tracers, 0, 1)
    far_row, near_row = shaped(5 * sz.stack, LANES), shaped(3 * sz.stack, LANES)
    kept = [((1,), f32), ((2,), f32), ((3,), jnp.bfloat16)]
    near_q, far_rows, sides = call(
        edges_kernel,
        "edges",
        [hbm] * 3,
        (near_row, far_row, shaped(2 * EXT_ROWS, LANES)),
        [pltpu.VMEM((2,) + count + (merged,), dtype) for count, dtype in kept]
        + [
            pltpu.VMEM((rows,) + (count if count != (1,) else ()) + (lanes,), dtype)
            for lanes in (LANES, sz.tail)
            for count, dtype in kept
        ]
        + [pltpu.SemaphoreType.DMA((3, 4))],
        limit=MOST_VMEM,
    )(thickness, wind_rows, tracer_rows)

    near = [(band * n_lon + i, (band ^ 1) * n_lon + i) for band in range(n_lat) for i in range(n_lon)]
    far = []
    for band in range(n_lat):
        other = band - 1 if band % 2 == 0 else band + 1
        for i in range(n_lon):
            if 0 <= other < n_lat:
                far.append((band * n_lon + i, other * n_lon + i))
            else:
                far.append((band * n_lon + i, band * n_lon + (i + n_lon // 2) % n_lon))
    near_h = lax.ppermute(thickness, ("lat", "lon"), near)
    near_w = lax.ppermute(wind_rows, ("lat", "lon"), near)
    if not sz.near_only:
        far_rows = lax.ppermute(far_rows, ("lat", "lon"), far)

    order = [sz.turns(False), sz.turns(True)]

    def meetings(shares):
        got = [shares[0]]
        for k in range(1, n_lon):
            sectors = [(band, i, i ^ order[band % 2][k]) for band in range(n_lat) for i in range(n_lon)]
            got.append(lax.ppermute(shares[k], ("lat", "lon"), [(b * n_lon + i, b * n_lon + j) for b, i, j in sectors]))
        return got

    all_pieces = pltpu.VMEM((n_lon, sz.size, LANES), f32)
    *tends, far_rows, near_q = call(
        polar_kernel,
        "polar",
        [vmem] * 9,
        [shaped(sz.size + EXT_ROWS, LANES)] * n_lon + [far_row, near_row],
        [
            pltpu.VMEM((n_lon * sz.size, LANES), f32),
            pltpu.VMEM((4 * sz.stack, LANES), f32),
            pltpu.VMEM((3, EXT_ROWS, sz.tiles * LANES), f32),
        ],
    )(thickness, wind_rows, near_h, near_w, sides, geo, wave, far_rows, near_q)
    met = meetings(tends)
    near_q = lax.ppermute(near_q, ("lat", "lon"), near)
    from_far = lax.ppermute(far_rows, ("lat", "lon"), far) if sz.near_only else far_rows
    weights, masks = call(
        weights_kernel,
        "weights",
        [smem, vmem, vmem, anywhere],
        (
            jax.ShapeDtypeStruct((sz.share * PER_TILE * sz.stack, n_lon * sz.stack), jnp.bfloat16),
            shaped(3, EXT_ROWS, LANES),
        ),
    )(cutoff, n, inverse, tends[0])
    worked = call(
        filter_kernel,
        "filter",
        [vmem] * 2 + [vmem] * n_lon,
        [shaped(sz.size, LANES)] * n_lon,
        [all_pieces, all_pieces],
    )(weights, geo, *met)
    held = call(pass_kernel, "pass", [vmem] + [anywhere] * 2, shaped(sz.size, LANES))(worked[-1], from_far, near_q)
    worked = [*worked[:-1], held]
    back = meetings(worked)

    base_w, base_h, mass = call(
        rest_kernel,
        "rest",
        [vmem] * 10 + [anywhere] + [vmem] * n_lon,
        (shaped(2, rows, merged), shaped(rows, merged), jax.ShapeDtypeStruct(tracers.shape, jnp.bfloat16)),
        [pltpu.VMEM((6, EXT_ROWS, sz.tiles * LANES), f32), pltpu.VMEM((n_lon, 8, LANES), f32)],
    )(masks, thickness, wind_rows, tracers, near_h, near_w, near_q, from_far, geo, wave, worked[0], *met)

    new_w, new_h = call(
        finish_kernel,
        "finish",
        [vmem] * (3 + n_lon),
        (shaped(*wind_rows.shape), shaped(rows, merged)),
        [pltpu.VMEM((n_lon * sz.size, LANES), f32)],
    )(masks, base_w, base_h, *back)
    return jnp.swapaxes(new_w, 0, 1), new_h, mass


def solution(mesh):
    in_specs = (P(None, "lat", "lon"), P("lat", "lon"), P(None, "lat", "lon"), P())
    out_specs = (P(None, "lat", "lon"), P("lat", "lon"), P(None, "lat", "lon"))
    return jax.shard_map(local, mesh=mesh, in_specs=in_specs, out_specs=out_specs, check_vma=False)
```

```python
import functools
import math

import jax
import jax.numpy as jnp
import numpy as np
from jax import lax
from jax.experimental import pallas as pl
from jax.experimental.pallas import tpu as pltpu
from jax.sharding import PartitionSpec as P

LEVELS = 16
TIME_STEP = 0.05
DIFFUSION = 0.5
LANES = 128
PER_TILE = LANES // LEVELS
EXT_ROWS = 16
LIMIT = 48 * 1024 * 1024
MOST_VMEM = 64 * 1024 * 1024 - 10500 * 1024


class Sizes:
    def __init__(self, rows, merged, n_lat, n_lon):
        self.rows = rows
        self.merged = merged
        self.columns = merged // LEVELS
        self.n_lat = n_lat
        self.n_lon = n_lon
        self.nlat = rows * n_lat
        self.nlon = self.columns * n_lon
        self.ratio = 2.0 * self.nlat / self.nlon
        self.tiles = -(-merged // LANES)
        self.end = (self.tiles - 1) * LANES
        self.tail = merged - self.end
        self.stack = -(-(self.tiles + 1) // 8) * 8
        self.near_only = rows <= self.nlat // 6 < 2 * rows
        self.work = rows - 1 if self.near_only else rows
        self.units = 3 * self.work
        self.share = -(-self.units // n_lon)
        self.size = self.share * self.stack
        assert self.tail <= LANES - 4 * LEVELS and rows + 2 <= EXT_ROWS and n_lat % 2 == 0
        assert n_lon >= 4 and n_lon & (n_lon - 1) == 0

    def span(self, tile):
        return self.tail if tile == self.tiles - 1 else LANES

    def first(self):
        return jnp.where(lax.rem(lax.axis_index("lat"), 2) == 0, 1, 0) if self.near_only else 0

    def at_pole(self, row):
        band = lax.axis_index("lat")
        pole = jnp.where(band == 0, 0, jnp.where(band == self.n_lat - 1, self.rows - 1, -1))
        return row == (pole if self.near_only else -1)

    def turns(self, odd, back):
        middle, last = list(range(1, self.n_lon - 1)), self.n_lon - 1
        if odd and back:
            return [0, middle[-1], last] + middle[-2::-1]
        return [0, last] + (middle[::-1] if odd else middle)

    def partner(self, k, back=False):
        odd = lax.rem(lax.axis_index("lat"), 2) == 1
        turn = jnp.where(odd, self.turns(True, back)[k], self.turns(False, back)[k])
        return jnp.bitwise_xor(lax.axis_index("lon"), turn)

    def piece(self, k, back=False):
        return pl.ds(pl.multiple_of(self.partner(k, back) * self.size, 8), self.size)


def geometry(sz):
    table = np.zeros((sz.n_lat, 3, EXT_ROWS, LANES), np.float64)

    def face(j):
        return math.sin((j + 1) * math.pi / sz.nlat) if 0 <= j < sz.nlat - 1 else 0.0

    for band in range(sz.n_lat):
        for row in range(sz.rows):
            j = band * sz.rows + row
            centre = (j + 0.5) * math.pi / sz.nlat - math.pi / 2
            table[band, 0, row] = 1.0 / math.cos(centre)
            table[band, 1, row] = math.sin(centre)
            table[band, 2, row] = face(j)
        table[band, 2, EXT_ROWS - 1] = face(band * sz.rows - 1)
    return table.astype(np.float32)


def offsets(sz):
    shift, out_tile = np.divmod(np.arange(PER_TILE * sz.stack), sz.stack)
    sector, in_tile = np.divmod(np.arange(sz.n_lon * sz.stack), sz.stack)
    n = (PER_TILE * (out_tile - 1) + shift)[:, None] - (PER_TILE * in_tile + sz.columns * sector)[None, :]
    n = (n + sz.nlon // 2) % sz.nlon - sz.nlon // 2
    with np.errstate(divide="ignore"):
        inverse = np.where(n == 0, 0.0, 1.0 / (sz.nlon * np.sin(np.pi * n / sz.nlon)))
    return n.astype(np.float32), inverse.astype(np.float32)


def waves(sz):
    column = PER_TILE * np.arange(sz.stack)[:, None] + np.arange(LANES)[None, :] // LEVELS
    angle = 2 * np.pi * column / sz.nlon
    return np.stack([np.cos(angle), np.sin(angle)]).astype(np.float32)


def edges_kernel(sz, h_hbm, w_hbm, q_hbm, near_ref, far_ref, sides_ref, *scratch):
    row_refs, first_refs, last_refs, sems = scratch[:3], scratch[3:6], scratch[6:9], scratch[9]
    rows, last = sz.rows, sz.rows - 1
    even = lax.rem(lax.axis_index("lat"), 2) == 0
    copies = []
    for i, source in enumerate((h_hbm, w_hbm, q_hbm)):
        for k, row in enumerate((0, last)):
            one = source.at[pl.ds(row, 1)] if i == 0 else source.at[row]
            copies.append(pltpu.make_async_copy(one, row_refs[i].at[k], sems.at[i, k]))
        for k, (start, to) in enumerate(((0, first_refs[i]), (sz.end, last_refs[i]))):
            lanes = pl.ds(start, to.shape[-1])
            cut = source.at[:, lanes] if i == 0 else source.at[:, :, lanes]
            copies.append(pltpu.make_async_copy(cut, to, sems.at[i, 2 + k]))
    for copy in copies:
        copy.start()
    for copy in copies:
        copy.wait()
    h_rows, w_rows, q_rows = row_refs
    for t in range(sz.tiles):
        wide = sz.span(t)
        lanes = slice(LANES * t, LANES * t + wide)
        q = [q_rows[k, :, lanes].astype(jnp.float32) for k in range(2)]
        for f in range(5):
            if f == 0:
                first, final = h_rows[0, :, lanes], h_rows[1, :, lanes]
            elif f == 1:
                first, final = w_rows[0, 1:2, lanes], w_rows[1, 1:2, lanes]
            else:
                first, final = q[0][f - 2 : f - 1], q[1][f - 2 : f - 1]
                at = sz.stack * (f - 2) + t
                near_ref[at : at + 1, :wide] = jnp.where(even, final, first)
            at = sz.stack * f + t
            far_ref[at : at + 1, :wide] = jnp.where(even, first, final)
    sides_ref[...] = jnp.zeros(sides_ref.shape, jnp.float32)
    for k, (refs, at) in enumerate(((first_refs, 0), (last_refs, sz.tail - LEVELS))):
        columns = slice(at, at + LEVELS)
        for f in range(5):
            if f == 0:
                value = refs[0][:, columns]
            elif f == 1:
                value = refs[1][:, 0, columns]
            else:
                value = refs[2][:, f - 2, columns].astype(jnp.float32)
            sides_ref[EXT_ROWS * k : EXT_ROWS * k + rows, LEVELS * f : LEVELS * (f + 1)] = value


def add_rows(sz, ext, near_h_ref, near_w_ref, near_q_ref, far_ref):
    band = lax.axis_index("lat")
    even = lax.rem(band, 2) == 0
    over_pole = (band == 0) | (band == sz.n_lat - 1)
    last = sz.rows - 1
    for f in range(2 if near_q_ref is None else 5):
        flip = jnp.where(over_pole, -1.0, 1.0) if f == 1 else 1.0
        for t in range(sz.tiles):
            lanes = slice(LANES * t, LANES * t + sz.span(t))
            if f == 0:
                near = jnp.where(even, near_h_ref[0:1, lanes], near_h_ref[last : sz.rows, lanes])
            elif f == 1:
                near = jnp.where(even, near_w_ref[0, 1:2, lanes], near_w_ref[last, 1:2, lanes])
            else:
                at = sz.stack * (f - 2) + t
                near = near_q_ref[at : at + 1, : sz.span(t)]
            at = sz.stack * f + t
            far = jnp.zeros_like(near) if far_ref is None else far_ref[at : at + 1, : sz.span(t)] * flip
            ext[f, sz.rows : sz.rows + 1, lanes] = jnp.where(even, near, far)
            ext[f, EXT_ROWS - 1 : EXT_ROWS, lanes] = jnp.where(even, far, near)


class Tiles:
    def __init__(self, sz):
        self.sz = sz
        self.lane = lax.broadcasted_iota(jnp.int32, (EXT_ROWS, LANES), 1)
        self.turned = {}

    def turn(self, name, t, value, step):
        key = (name, t % self.sz.tiles, step)
        if key not in self.turned:
            self.turned[key] = pltpu.roll(value(t % self.sz.tiles), step % LANES, 1)
        return self.turned[key]

    def east(self, name, t, value):
        here = self.turn(name, t, value, -LEVELS)
        return jnp.where(self.lane < LANES - LEVELS, here, self.turn(name, t + 1, value, -LEVELS))

    def west(self, name, t, value):
        here = self.turn(name, t, value, LEVELS)
        return jnp.where(self.lane >= LEVELS, here, self.turn(name, t - 1, value, LEVELS))


def north(value):
    return pltpu.roll(value, EXT_ROWS - 1, 0)


def south(value):
    return pltpu.roll(value, 1, 0)


def polar_kernel(sz, h_ref, w_ref, near_h_ref, near_w_ref, sides_ref, geo_ref, wave_ref, far_ref, near_q_ref, *refs):
    out_refs, (far_out, near_out, tend_ref, pole_ref, ext) = refs[:-5], refs[-5:]
    far_out[...] = far_ref[...]
    near_out[...] = near_q_ref[...]
    if sz.near_only:
        far_ref = None
    band = lax.axis_index("lat")
    ring = Tiles(sz)
    lane = ring.lane
    tiles, stack, rows, work = sz.tiles, sz.stack, sz.rows, sz.work
    even = lax.rem(band, 2) == 0
    for f, value in enumerate((h_ref[...], w_ref[:, 1, :], w_ref[:, 0, :])):
        ext[f, :rows, sz.end :] = jnp.zeros((rows, LANES), jnp.float32)
        ext[f, :rows, : sz.merged] = value
    add_rows(sz, ext, near_h_ref, near_w_ref, None, far_ref)
    inv_cos, sin_centre, cos_face = geo_ref[band, 0], geo_ref[band, 1], geo_ref[band, 2]
    ratio = sz.ratio

    def tile(f, t):
        return ext[f, :, LANES * t : LANES * (t + 1)]

    kept = {}

    def zonal(t):
        if t not in kept:
            thick_e = ring.east("h", t, functools.partial(tile, 0))
            wind_e = ring.east("u", t, functools.partial(tile, 2))
            flux = 0.25 * (tile(2, t) + wind_e) * (tile(0, t) + thick_e) * inv_cos
            if t == tiles - 1:
                flux = jnp.where(lane < sz.tail - LEVELS, flux, 0.0)
            kept[t] = (flux, thick_e)
        return kept[t]

    for t in range(tiles):
        flux, thick_e = zonal(t)
        thick, wind_v, wind_u = tile(0, t), tile(1, t), tile(2, t)
        flux_w = ring.west("f", t, lambda s: zonal(s)[0])
        thick_w = ring.west("hw", t, functools.partial(tile, 0))
        thick_n = north(thick)
        flux_n = (0.25 * ratio) * (wind_v + north(wind_v)) * (thick + thick_n) * cos_face
        thick_tend = -((flux - flux_w) + (flux_n - south(flux_n)) * inv_cos)
        wind_u_tend = sin_centre * wind_v - (thick_e - thick_w) * (0.5 * inv_cos)
        wind_v_tend = -sin_centre * wind_u - (0.5 * ratio) * (thick_n - south(thick))
        spare = 0.0
        if t == tiles - 1:
            last = sz.tail - LEVELS
            columns = [(tile(0, 0), 0), (thick, last), (tile(2, 0), 0), (wind_u, last)]
            for k, (source, at) in reversed(list(enumerate(columns))):
                to = sz.tail + LEVELS * k
                spare = jnp.where(lane < to + LEVELS, pltpu.roll(source, (to - at) % LANES, 1), spare)
        for f, tend in enumerate((thick_tend, wind_u_tend, wind_v_tend, thick)):
            if sz.near_only:
                alone = jnp.where(band < sz.n_lat // 2, tend[:1], tend[rows - 1 : rows])
                if t == tiles - 1:
                    alone = jnp.where(lane[:1] < sz.tail, alone, 0.0)
                pole_ref[stack * f + t : stack * f + t + 1] = alone
            if f == 3:
                continue
            if t == tiles - 1:
                tend = jnp.where(lane < sz.tail, tend, spare)
            if sz.near_only:
                tend = jnp.where(even, north(tend), tend)
            tend_ref[pl.ds(stack * work * f + t, work, stride=stack), :] = tend[:work]
    for f in range(3):
        for t in range(tiles, stack):
            tend_ref[pl.ds(stack * work * f + t, work, stride=stack), :] = jnp.zeros((work, LANES), jnp.float32)
    used = stack * sz.units
    if used < tend_ref.shape[0]:
        tend_ref[used:, :] = jnp.zeros((tend_ref.shape[0] - used, LANES), jnp.float32)
    sides = [sides_ref[:EXT_ROWS], sides_ref[EXT_ROWS:]]
    if sz.near_only:
        sums = pole_sums(sz, pole_ref, wave_ref, spare, band)
        row = lax.broadcasted_iota(jnp.int32, (EXT_ROWS, LANES), 0)
        for k, total in enumerate(sums):
            sides = [jnp.where(row == rows + k, total, side) for side in sides]
    here = lax.axis_index("lon")
    for k, out_ref in enumerate(out_refs):
        out_ref[: sz.size] = tend_ref[sz.piece(k), :]
        eastward = sz.partner(k) == lax.rem(here + 1, sz.n_lon)
        out_ref[sz.size :] = jnp.where(eastward, sides[1], sides[0])


def pole_sums(sz, pole_ref, wave_ref, spare, band):
    stack, rows = sz.stack, sz.rows
    lane = lax.broadcasted_iota(jnp.int32, (1, LANES), 1)
    sides = jnp.where(band < sz.n_lat // 2, spare[:1], spare[rows - 1 : rows])
    found = [jnp.zeros((1, LANES), jnp.float32), pltpu.roll(sides, (LANES // 2 - sz.tail) % LANES, 1)]
    for f in range(4):
        if sz.tiles < stack:
            pole_ref[stack * f + sz.tiles : stack * (f + 1)] = jnp.zeros((stack - sz.tiles, LANES), jnp.float32)
        values = pole_ref[stack * f : stack * (f + 1)]
        for k, terms in enumerate((values, values * wave_ref[0], values * wave_ref[1])):
            total = jnp.sum(terms, axis=0, keepdims=True)
            for step in (64, 32, 16):
                total = total + pltpu.roll(total, step, 1)
            row, place = divmod(3 * f + k, PER_TILE)
            inside = (lane >= LEVELS * place) & (lane < LEVELS * (place + 1))
            found[row] = jnp.where(inside, total, found[row])
    return found


def pole_waves(sz, rows_in, inv_cos, sign):
    n_lon = sz.n_lon
    lane = lax.broadcasted_iota(jnp.int32, (1, LANES), 1)

    def value(s, place):
        row, at = divmod(place, PER_TILE)
        return pltpu.roll(rows_in[s % n_lon, row : row + 1], (-LEVELS * at) % LANES, 1)

    theta = 2 * math.pi / sz.nlon
    ends = (1.0, math.cos(theta * (sz.columns - 1)), math.sin(theta * (sz.columns - 1)))
    sums = [[[value(s, 3 * f + k) for k in range(3)] for f in range(4)] for s in range(n_lon)]
    for s in range(n_lon):
        thick_w, thick_e = value(s, 13), value(s + 1, 12)
        flux = 0.25 * (value(s, 15) + value(s + 1, 14)) * (thick_w + thick_e) * inv_cos
        slope = 0.5 * inv_cos
        after = (s + 1) % n_lon
        for f, (west_of, east_of) in enumerate(((flux, flux), (slope * thick_e, slope * thick_w))):
            for k in range(3):
                sums[s][f][k] = sums[s][f][k] - west_of * ends[k]
            for k in range(2):
                sums[after][f][k] = sums[after][f][k] + east_of
    result = []
    for f in range(3):
        waves_of = [0.0, 0.0, 0.0]
        for s in range(n_lon):
            level, cosine, sine = sums[s][f]
            if f == 2:
                level = level + (0.5 * sz.ratio) * sign * sums[s][3][0]
                cosine = cosine - (0.5 * sz.ratio) * sign * sums[s][3][1]
                sine = sine - (0.5 * sz.ratio) * sign * sums[s][3][2]
            c, d = math.cos(2 * math.pi * s / n_lon), math.sin(2 * math.pi * s / n_lon)
            waves_of[0] = waves_of[0] + level
            waves_of[1] = waves_of[1] + (c * cosine - d * sine)
            waves_of[2] = waves_of[2] + (d * cosine + c * sine)
        spread = []
        for k, total in enumerate(waves_of):
            total = jnp.where(lane < LEVELS, total * ((1.0 if k == 0 else 2.0) / sz.nlon), 0.0)
            for step in (16, 32, 64):
                total = total + pltpu.roll(total, step, 1)
            spread.append(total)
        result.append(spread)
    return result


def rest_kernel(sz, masks_ref, h_ref, w_ref, q_ref, near_h_ref, near_w_ref, near_q_ref, far_ref, geo_ref, wave_ref, after_ref, *refs):
    met_refs, (new_w_ref, new_h_ref, mass_ref, ext, pole_in) = refs[: sz.n_lon], refs[sz.n_lon :]
    band = lax.axis_index("lat")
    ring = Tiles(sz)
    lane = ring.lane
    tiles, rows = sz.tiles, sz.rows
    for f in range(6):
        if f < 2 or f == 5:
            value = (h_ref[...], w_ref[:, 1, :], w_ref[:, 0, :])[min(f, 2)]
        else:
            value = q_ref[f - 2].astype(jnp.float32)
        ext[f, :rows, : sz.merged] = value
    add_rows(sz, ext, near_h_ref, near_w_ref, near_q_ref, far_ref)
    lane9 = lane[:rows]
    here = lax.axis_index("lon")
    from_e = from_w = met_refs[0][sz.size :]
    for k, met_ref in enumerate(met_refs):
        eastward = lax.rem(sz.partner(k) - here + sz.n_lon, sz.n_lon)
        pole_in[eastward] = met_ref[sz.size + 8 :]
        from_e = jnp.where(sz.partner(k) == lax.rem(here + 1, sz.n_lon), met_ref[sz.size :], from_e)
        from_w = jnp.where(sz.partner(k) == lax.rem(here + sz.n_lon - 1, sz.n_lon), met_ref[sz.size :], from_w)
    for place, f in enumerate((0, 5, 2, 3, 4)):
        after = pltpu.roll(from_e, (sz.tail - LEVELS * place) % LANES, 1)[:rows]
        before = pltpu.roll(from_w, (LANES - LEVELS - LEVELS * place) % LANES, 1)[:rows]
        own = ext[f, :rows, sz.end :]
        edge = jnp.where(lane9 < LANES - LEVELS, after, before)
        ext[f, :rows, sz.end :] = jnp.where(lane9 < sz.tail, own, edge)
    inv_cos, sin_centre, cos_face = geo_ref[band, 0], geo_ref[band, 1], geo_ref[band, 2]
    ratio = sz.ratio

    plain, alone = masks_ref[0], masks_ref[1]
    if sz.near_only:
        band = lax.axis_index("lat")
        low = band < sz.n_lat // 2
        pole_cos = jnp.where(low, inv_cos[:1], inv_cos[rows - 1 : rows])
        kept_waves = pole_waves(sz, pole_in.at[:, rows - 8 :], pole_cos, jnp.where(low, 1.0, -1.0))

    def stepped(f, t, value, tend):
        value = value + plain * tend
        if sz.near_only:
            level, cosine, sine = kept_waves[f]
            wave = level + cosine * wave_ref[0, t : t + 1] + sine * wave_ref[1, t : t + 1]
            value = value + alone * wave
        return value

    def tile(f, t):
        return ext[f, :, LANES * t : LANES * (t + 1)]

    kept = {}

    def zonal(t):
        if t not in kept:
            thick_e = ring.east("h", t, functools.partial(tile, 0))
            wind_e = ring.east("u", t, functools.partial(tile, 5))
            flux = 0.25 * (tile(5, t) + wind_e) * (tile(0, t) + thick_e) * inv_cos
            parts = []
            for k in range(3):
                q = tile(2 + k, t)
                q_e = ring.east(k, t, functools.partial(tile, 2 + k))
                parts.append(DIFFUSION * (q_e - q) - flux * (0.5 * (q + q_e)))
            kept[t] = (flux, thick_e, parts)
        return kept[t]

    for t in range(tiles):
        span = sz.span(t)
        lanes = slice(LANES * t, LANES * t + span)
        flux, thick_e, parts = zonal(t)
        thick, wind_u, wind_v = tile(0, t), tile(5, t), tile(1, t)
        flux_w = ring.west("f", t, lambda s: zonal(s)[0])
        thick_w = ring.west("hw", t, functools.partial(tile, 0))
        thick_n = north(thick)
        flux_n = (0.25 * ratio) * (wind_v + north(wind_v)) * (thick + thick_n) * cos_face
        thick_tend = -((flux - flux_w) + (flux_n - south(flux_n)) * inv_cos)
        wind_u_tend = sin_centre * wind_v - (thick_e - thick_w) * (0.5 * inv_cos)
        wind_v_tend = -sin_centre * wind_u - (0.5 * ratio) * (thick_n - south(thick))
        new_h_ref[:, lanes] = stepped(0, t, thick, thick_tend)[:rows, :span]
        new_w_ref[0, :, lanes] = stepped(1, t, wind_u, wind_u_tend)[:rows, :span]
        new_w_ref[1, :, lanes] = stepped(2, t, wind_v, wind_v_tend)[:rows, :span]
        for k in range(3):
            q = tile(2 + k, t)
            q_n = north(q)
            zonal_part = parts[k] - ring.west(("p", k), t, lambda s: zonal(s)[2][k])
            lap = q_n + south(q) - 2.0 * q
            over = flux_n * (0.5 * (q + q_n))
            merid_part = DIFFUSION * lap - (over - south(over)) * inv_cos
            mass = thick * q + TIME_STEP * (zonal_part + merid_part)
            mass_ref[k, :, lanes] = mass[:rows, :span].astype(jnp.bfloat16)


def sin_pi(y):
    y = jnp.where(y > 0.5, 1.0 - y, jnp.where(y < -0.5, -1.0 - y, y))
    s = y * y
    series = [(-1) ** i * math.pi ** (2 * i + 1) / math.factorial(2 * i + 1) for i in range(7)]
    total = series[-1]
    for factor in reversed(series[:-1]):
        total = total * s + factor
    return total * y


def share_of(sz, i):
    unit = lax.axis_index("lon") * sz.share + i
    return unit // sz.work, sz.first() + lax.rem(unit, sz.work)


def weights_kernel(sz, cut_ref, n_ref, inverse_ref, after_ref, weights_ref, masks_ref):
    band = lax.axis_index("lat")
    row = lax.broadcasted_iota(jnp.int32, (EXT_ROWS, LANES), 0)
    cuts = jnp.full((EXT_ROWS, LANES), sz.nlon // 2, jnp.int32)
    for j in range(sz.rows):
        cuts = jnp.where(row == j, cut_ref[band * sz.rows + j], cuts)
    plain, alone = cuts >= sz.nlon // 2, sz.at_pole(row)
    masks_ref[0] = jnp.where(plain, TIME_STEP, 0.0)
    masks_ref[1] = jnp.where(alone, TIME_STEP, 0.0)
    masks_ref[2] = jnp.where(plain | alone, 0.0, TIME_STEP)
    size = PER_TILE * sz.stack
    for i in range(sz.share):
        width = (2 * cut_ref[band * sz.rows + share_of(sz, i)[1]] + 1).astype(jnp.float32)
        n = n_ref[...]
        turns = n * width
        turns = turns - jnp.round(turns * (0.5 / sz.nlon)) * (2.0 * sz.nlon)
        weights = sin_pi(turns * (1.0 / sz.nlon)) * inverse_ref[...]
        weights = jnp.where(n == 0.0, width * (1.0 / sz.nlon), weights)
        weights_ref[size * i : size * (i + 1)] = weights.astype(jnp.bfloat16)


def pass_kernel(sz, piece_ref, after_ref, also_after_ref, out_ref):
    out_ref[...] = piece_ref[...]


def filter_kernel(sz, weights_ref, geo_ref, *refs):
    n_lon, stack, share = sz.n_lon, sz.stack, sz.share
    in_refs, out_refs, (gathered, results) = refs[:n_lon], refs[n_lon : 2 * n_lon], refs[2 * n_lon :]
    for k, in_ref in enumerate(in_refs):
        gathered[sz.partner(k)] = in_ref[: sz.size]

    band = lax.axis_index("lat")
    lane = lax.broadcasted_iota(jnp.int32, (share, LANES), 1)
    place = lax.broadcasted_iota(jnp.int32, (share, LANES), 0)
    by_flux = by_thick = jnp.zeros((share, LANES), jnp.float32)
    for i in range(share):
        field, row = share_of(sz, i)
        inv_cos = geo_ref[band, 0, pl.ds(row, 1), :]
        by_flux = jnp.where((place == i) & (field == 0), inv_cos, by_flux)
        by_thick = jnp.where((place == i) & (field == 1), 0.5 * inv_cos, by_thick)
    sides = [gathered[s, pl.ds(sz.tiles - 1, share, stride=stack), :] for s in range(n_lon)]

    def column(s, k):
        return pltpu.roll(sides[s % n_lon], (-sz.tail - LEVELS * k) % LANES, 1)

    for s in range(n_lon):
        thick_w, thick_e = column(s, 1), column(s + 1, 0)
        flux = 0.25 * (column(s, 3) + column(s + 1, 2)) * (thick_w + thick_e) * by_flux
        west_of, east_of = flux + by_thick * thick_e, flux + by_thick * thick_w
        at = pl.ds(sz.tiles - 1, share, stride=stack)
        own = gathered[s, at, :]
        own = own - jnp.where(lane >= sz.tail - LEVELS, pltpu.roll(west_of, sz.tail - LEVELS, 1), 0.0)
        gathered[s, at, :] = jnp.where(lane < sz.tail, own, 0.0)
        at = pl.ds(0, share, stride=stack)
        after = (s + 1) % n_lon
        gathered[after, at, :] = gathered[after, at, :] + jnp.where(lane < LEVELS, east_of, 0.0)

    wide = lax.broadcasted_iota(jnp.int32, (stack, LANES), 1)
    rows = PER_TILE * stack
    for i in range(share):
        here = slice(stack * i, stack * (i + 1))
        pieces = [gathered[s, here].astype(jnp.bfloat16) for s in range(n_lon)]
        circle = jnp.concatenate([jnp.concatenate(pieces[s:] + pieces[:s], axis=0) for s in range(n_lon)], axis=1)
        spread = jnp.dot(weights_ref[rows * i : rows * (i + 1)], circle, preferred_element_type=jnp.float32)
        for s in range(n_lon):
            same = spread[:stack, LANES * s : LANES * (s + 1)]
            carried = None
            for e in range(1, PER_TILE):
                part = spread[stack * e : stack * (e + 1), LANES * s : LANES * (s + 1)]
                part = pltpu.roll(part, LEVELS * e, 1)
                inside = wide >= LEVELS * e
                same = same + jnp.where(inside, part, 0.0)
                over = jnp.where(inside, 0.0, part)
                carried = over if carried is None else carried + over
            results[s, here] = pltpu.roll(same, stack - 1, 0) + carried
    for k, out_ref in enumerate(out_refs):
        out_ref[...] = results[sz.partner(k, True)]


def finish_kernel(sz, masks_ref, base_w_ref, base_h_ref, *refs):
    back_refs, (new_w_ref, new_h_ref, back_ref) = refs[: sz.n_lon], refs[sz.n_lon :]
    rows, work = sz.rows, sz.work
    for k, ref in enumerate(back_refs):
        back_ref[sz.piece(k, True), :] = ref[...]
    scale = masks_ref[2]
    even = lax.rem(lax.axis_index("lat"), 2) == 0
    for f in range(3):
        for t in range(sz.tiles):
            span = sz.span(t)
            lanes = slice(LANES * t, LANES * t + span)
            tend = back_ref[pl.ds(sz.stack * work * f + t, work, stride=sz.stack), :]
            if sz.near_only:
                tend = jnp.concatenate([tend, jnp.zeros((EXT_ROWS - work, LANES), jnp.float32)], axis=0)
                tend = jnp.where(even, south(tend), tend)
            change = (scale[:rows] * tend[:rows])[:, :span]
            if f == 0:
                new_h_ref[:, lanes] = base_h_ref[:, lanes] + change
            else:
                new_w_ref[:, f - 1, lanes] = base_w_ref[f - 1, :, lanes] + change


def local(winds, thickness, tracers, cutoff):
    n_lat = lax.axis_size("lat")
    n_lon = lax.axis_size("lon")
    rows, merged = thickness.shape
    sz = Sizes(rows, merged, n_lat, n_lon)
    f32 = jnp.float32
    vmem = pl.BlockSpec(memory_space=pltpu.VMEM)
    smem = pl.BlockSpec(memory_space=pltpu.SMEM)
    hbm = pl.BlockSpec(memory_space=pltpu.HBM)
    anywhere = pl.BlockSpec(memory_space=pl.ANY)

    def shaped(*shape):
        return jax.ShapeDtypeStruct(shape, f32)

    def call(kernel, name, in_specs, out_shape, scratch=(), limit=LIMIT):
        return pl.pallas_call(
            functools.partial(kernel, sz),
            out_shape=out_shape,
            in_specs=in_specs,
            out_specs=jax.tree.map(lambda _: vmem, out_shape),
            scratch_shapes=list(scratch),
            compiler_params=pltpu.CompilerParams(vmem_limit_bytes=limit),
            name=name,
        )

    geo = jnp.asarray(geometry(sz))
    wave = jnp.asarray(waves(sz))
    n, inverse = (jnp.asarray(table) for table in offsets(sz))

    wind_rows = jnp.swapaxes(winds, 0, 1)
    tracer_rows = jnp.swapaxes(tracers, 0, 1)
    far_row, near_row = shaped(5 * sz.stack, LANES), shaped(3 * sz.stack, LANES)
    kept = [((1,), f32), ((2,), f32), ((3,), jnp.bfloat16)]
    near_q, far_rows, sides = call(
        edges_kernel,
        "edges",
        [hbm] * 3,
        (near_row, far_row, shaped(2 * EXT_ROWS, LANES)),
        [pltpu.VMEM((2,) + count + (merged,), dtype) for count, dtype in kept]
        + [
            pltpu.VMEM((rows,) + (count if count != (1,) else ()) + (lanes,), dtype)
            for lanes in (LANES, sz.tail)
            for count, dtype in kept
        ]
        + [pltpu.SemaphoreType.DMA((3, 4))],
        limit=MOST_VMEM,
    )(thickness, wind_rows, tracer_rows)

    near = [(band * n_lon + i, (band ^ 1) * n_lon + i) for band in range(n_lat) for i in range(n_lon)]
    far = []
    for band in range(n_lat):
        other = band - 1 if band % 2 == 0 else band + 1
        for i in range(n_lon):
            if 0 <= other < n_lat:
                far.append((band * n_lon + i, other * n_lon + i))
            else:
                far.append((band * n_lon + i, band * n_lon + (i + n_lon // 2) % n_lon))
    near_h = lax.ppermute(thickness, ("lat", "lon"), near)
    near_w = lax.ppermute(wind_rows, ("lat", "lon"), near)
    if not sz.near_only:
        far_rows = lax.ppermute(far_rows, ("lat", "lon"), far)

    def meetings(shares, back):
        order = [sz.turns(False, back), sz.turns(True, back)]
        got = [shares[0]]
        for k in range(1, n_lon):
            sectors = [(band, i, i ^ order[band % 2][k]) for band in range(n_lat) for i in range(n_lon)]
            got.append(lax.ppermute(shares[k], ("lat", "lon"), [(b * n_lon + i, b * n_lon + j) for b, i, j in sectors]))
        return got

    all_pieces = pltpu.VMEM((n_lon, sz.size, LANES), f32)
    *tends, far_rows, near_q = call(
        polar_kernel,
        "polar",
        [vmem] * 9,
        [shaped(sz.size + EXT_ROWS, LANES)] * n_lon + [far_row, near_row],
        [
            pltpu.VMEM((n_lon * sz.size, LANES), f32),
            pltpu.VMEM((4 * sz.stack, LANES), f32),
            pltpu.VMEM((3, EXT_ROWS, sz.tiles * LANES), f32),
        ],
    )(thickness, wind_rows, near_h, near_w, sides, geo, wave, far_rows, near_q)
    met = meetings(tends, False)
    near_q = lax.ppermute(near_q, ("lat", "lon"), near)
    from_far = lax.ppermute(far_rows, ("lat", "lon"), far) if sz.near_only else far_rows
    weights, masks = call(
        weights_kernel,
        "weights",
        [smem, vmem, vmem, anywhere],
        (
            jax.ShapeDtypeStruct((sz.share * PER_TILE * sz.stack, n_lon * sz.stack), jnp.bfloat16),
            shaped(3, EXT_ROWS, LANES),
        ),
    )(cutoff, n, inverse, tends[0])
    worked = call(
        filter_kernel,
        "filter",
        [vmem] * 2 + [vmem] * n_lon,
        [shaped(sz.size, LANES)] * n_lon,
        [all_pieces, all_pieces],
    )(weights, geo, *met)
    held = call(pass_kernel, "pass", [vmem] + [anywhere] * 2, shaped(sz.size, LANES))(worked[-1], from_far, near_q)
    worked = [*worked[:-1], held]
    back = meetings(worked, True)

    base_w, base_h, mass = call(
        rest_kernel,
        "rest",
        [vmem] * 10 + [anywhere] + [vmem] * n_lon,
        (shaped(2, rows, merged), shaped(rows, merged), jax.ShapeDtypeStruct(tracers.shape, jnp.bfloat16)),
        [pltpu.VMEM((6, EXT_ROWS, sz.tiles * LANES), f32), pltpu.VMEM((n_lon, 8, LANES), f32)],
    )(masks, thickness, wind_rows, tracers, near_h, near_w, near_q, from_far, geo, wave, worked[0], *met)

    new_w, new_h = call(
        finish_kernel,
        "finish",
        [vmem] * (3 + n_lon),
        (shaped(*wind_rows.shape), shaped(rows, merged)),
        [pltpu.VMEM((n_lon * sz.size, LANES), f32)],
    )(masks, base_w, base_h, *back)
    return jnp.swapaxes(new_w, 0, 1), new_h, mass


def solution(mesh):
    in_specs = (P(None, "lat", "lon"), P("lat", "lon"), P(None, "lat", "lon"), P())
    out_specs = (P(None, "lat", "lon"), P("lat", "lon"), P(None, "lat", "lon"))
    return jax.shard_map(local, mesh=mesh, in_specs=in_specs, out_specs=out_specs, check_vma=False)
```

```python
import functools
import math

import jax
import jax.numpy as jnp
import numpy as np
from jax import lax
from jax.experimental import pallas as pl
from jax.experimental.pallas import tpu as pltpu
from jax.sharding import PartitionSpec as P

LEVELS = 16
TIME_STEP = 0.05
DIFFUSION = 0.5
LANES = 128
PER_TILE = LANES // LEVELS
EXT_ROWS = 16
LIMIT = 48 * 1024 * 1024
MOST_VMEM = 64 * 1024 * 1024 - 10500 * 1024


class Sizes:
    def __init__(self, rows, merged, n_lat, n_lon):
        self.rows = rows
        self.merged = merged
        self.columns = merged // LEVELS
        self.n_lat = n_lat
        self.n_lon = n_lon
        self.nlat = rows * n_lat
        self.nlon = self.columns * n_lon
        self.ratio = 2.0 * self.nlat / self.nlon
        self.tiles = -(-merged // LANES)
        self.end = (self.tiles - 1) * LANES
        self.tail = merged - self.end
        self.stack = -(-(self.tiles + 1) // 8) * 8
        self.near_only = rows <= self.nlat // 6 < 2 * rows
        self.work = rows - 1 if self.near_only else rows
        self.units = 3 * self.work
        self.share = -(-self.units // n_lon)
        self.size = self.share * self.stack
        assert self.tail <= LANES - 4 * LEVELS and rows + 2 <= EXT_ROWS and n_lat % 2 == 0
        assert n_lon >= 4 and n_lon & (n_lon - 1) == 0

    def span(self, tile):
        return self.tail if tile == self.tiles - 1 else LANES

    def first(self):
        return jnp.where(lax.rem(lax.axis_index("lat"), 2) == 0, 1, 0) if self.near_only else 0

    def at_pole(self, row):
        band = lax.axis_index("lat")
        pole = jnp.where(band == 0, 0, jnp.where(band == self.n_lat - 1, self.rows - 1, -1))
        return row == (pole if self.near_only else -1)

    def turns(self, odd, back):
        middle, last = list(range(1, self.n_lon - 1)), self.n_lon - 1
        if odd and not back:
            return [0, middle[-1], last] + middle[-2::-1]
        return [0, last] + (middle[::-1] if odd else middle)

    def partner(self, k, back=False):
        odd = lax.rem(lax.axis_index("lat"), 2) == 1
        turn = jnp.where(odd, self.turns(True, back)[k], self.turns(False, back)[k])
        return jnp.bitwise_xor(lax.axis_index("lon"), turn)

    def piece(self, k, back=False):
        return pl.ds(pl.multiple_of(self.partner(k, back) * self.size, 8), self.size)


def geometry(sz):
    table = np.zeros((sz.n_lat, 3, EXT_ROWS, LANES), np.float64)

    def face(j):
        return math.sin((j + 1) * math.pi / sz.nlat) if 0 <= j < sz.nlat - 1 else 0.0

    for band in range(sz.n_lat):
        for row in range(sz.rows):
            j = band * sz.rows + row
            centre = (j + 0.5) * math.pi / sz.nlat - math.pi / 2
            table[band, 0, row] = 1.0 / math.cos(centre)
            table[band, 1, row] = math.sin(centre)
            table[band, 2, row] = face(j)
        table[band, 2, EXT_ROWS - 1] = face(band * sz.rows - 1)
    return table.astype(np.float32)


def offsets(sz):
    shift, out_tile = np.divmod(np.arange(PER_TILE * sz.stack), sz.stack)
    sector, in_tile = np.divmod(np.arange(sz.n_lon * sz.stack), sz.stack)
    n = (PER_TILE * (out_tile - 1) + shift)[:, None] - (PER_TILE * in_tile + sz.columns * sector)[None, :]
    n = (n + sz.nlon // 2) % sz.nlon - sz.nlon // 2
    with np.errstate(divide="ignore"):
        inverse = np.where(n == 0, 0.0, 1.0 / (sz.nlon * np.sin(np.pi * n / sz.nlon)))
    return n.astype(np.float32), inverse.astype(np.float32)


def waves(sz):
    column = PER_TILE * np.arange(sz.stack)[:, None] + np.arange(LANES)[None, :] // LEVELS
    angle = 2 * np.pi * column / sz.nlon
    return np.stack([np.cos(angle), np.sin(angle)]).astype(np.float32)


def edges_kernel(sz, h_hbm, w_hbm, q_hbm, near_ref, far_ref, sides_ref, *scratch):
    row_refs, first_refs, last_refs, sems = scratch[:3], scratch[3:6], scratch[6:9], scratch[9]
    rows, last = sz.rows, sz.rows - 1
    even = lax.rem(lax.axis_index("lat"), 2) == 0
    copies = []
    for i, source in enumerate((h_hbm, w_hbm, q_hbm)):
        for k, row in enumerate((0, last)):
            one = source.at[pl.ds(row, 1)] if i == 0 else source.at[row]
            copies.append(pltpu.make_async_copy(one, row_refs[i].at[k], sems.at[i, k]))
        for k, (start, to) in enumerate(((0, first_refs[i]), (sz.end, last_refs[i]))):
            lanes = pl.ds(start, to.shape[-1])
            cut = source.at[:, lanes] if i == 0 else source.at[:, :, lanes]
            copies.append(pltpu.make_async_copy(cut, to, sems.at[i, 2 + k]))
    for copy in copies:
        copy.start()
    for copy in copies:
        copy.wait()
    h_rows, w_rows, q_rows = row_refs
    for t in range(sz.tiles):
        wide = sz.span(t)
        lanes = slice(LANES * t, LANES * t + wide)
        q = [q_rows[k, :, lanes].astype(jnp.float32) for k in range(2)]
        for f in range(5):
            if f == 0:
                first, final = h_rows[0, :, lanes], h_rows[1, :, lanes]
            elif f == 1:
                first, final = w_rows[0, 1:2, lanes], w_rows[1, 1:2, lanes]
            else:
                first, final = q[0][f - 2 : f - 1], q[1][f - 2 : f - 1]
                at = sz.stack * (f - 2) + t
                near_ref[at : at + 1, :wide] = jnp.where(even, final, first)
            at = sz.stack * f + t
            far_ref[at : at + 1, :wide] = jnp.where(even, first, final)
    sides_ref[...] = jnp.zeros(sides_ref.shape, jnp.float32)
    for k, (refs, at) in enumerate(((first_refs, 0), (last_refs, sz.tail - LEVELS))):
        columns = slice(at, at + LEVELS)
        for f in range(5):
            if f == 0:
                value = refs[0][:, columns]
            elif f == 1:
                value = refs[1][:, 0, columns]
            else:
                value = refs[2][:, f - 2, columns].astype(jnp.float32)
            sides_ref[EXT_ROWS * k : EXT_ROWS * k + rows, LEVELS * f : LEVELS * (f + 1)] = value


def add_rows(sz, ext, near_h_ref, near_w_ref, near_q_ref, far_ref):
    band = lax.axis_index("lat")
    even = lax.rem(band, 2) == 0
    over_pole = (band == 0) | (band == sz.n_lat - 1)
    last = sz.rows - 1
    for f in range(2 if near_q_ref is None else 5):
        flip = jnp.where(over_pole, -1.0, 1.0) if f == 1 else 1.0
        for t in range(sz.tiles):
            lanes = slice(LANES * t, LANES * t + sz.span(t))
            if f == 0:
                near = jnp.where(even, near_h_ref[0:1, lanes], near_h_ref[last : sz.rows, lanes])
            elif f == 1:
                near = jnp.where(even, near_w_ref[0, 1:2, lanes], near_w_ref[last, 1:2, lanes])
            else:
                at = sz.stack * (f - 2) + t
                near = near_q_ref[at : at + 1, : sz.span(t)]
            at = sz.stack * f + t
            far = jnp.zeros_like(near) if far_ref is None else far_ref[at : at + 1, : sz.span(t)] * flip
            ext[f, sz.rows : sz.rows + 1, lanes] = jnp.where(even, near, far)
            ext[f, EXT_ROWS - 1 : EXT_ROWS, lanes] = jnp.where(even, far, near)


class Tiles:
    def __init__(self, sz):
        self.sz = sz
        self.lane = lax.broadcasted_iota(jnp.int32, (EXT_ROWS, LANES), 1)
        self.turned = {}

    def turn(self, name, t, value, step):
        key = (name, t % self.sz.tiles, step)
        if key not in self.turned:
            self.turned[key] = pltpu.roll(value(t % self.sz.tiles), step % LANES, 1)
        return self.turned[key]

    def east(self, name, t, value):
        here = self.turn(name, t, value, -LEVELS)
        return jnp.where(self.lane < LANES - LEVELS, here, self.turn(name, t + 1, value, -LEVELS))

    def west(self, name, t, value):
        here = self.turn(name, t, value, LEVELS)
        return jnp.where(self.lane >= LEVELS, here, self.turn(name, t - 1, value, LEVELS))


def north(value):
    return pltpu.roll(value, EXT_ROWS - 1, 0)


def south(value):
    return pltpu.roll(value, 1, 0)


def polar_kernel(sz, h_ref, w_ref, near_h_ref, near_w_ref, sides_ref, geo_ref, wave_ref, far_ref, near_q_ref, *refs):
    out_refs, (far_out, near_out, tend_ref, pole_ref, ext) = refs[:-5], refs[-5:]
    far_out[...] = far_ref[...]
    near_out[...] = near_q_ref[...]
    if sz.near_only:
        far_ref = None
    band = lax.axis_index("lat")
    ring = Tiles(sz)
    lane = ring.lane
    tiles, stack, rows, work = sz.tiles, sz.stack, sz.rows, sz.work
    even = lax.rem(band, 2) == 0
    for f, value in enumerate((h_ref[...], w_ref[:, 1, :], w_ref[:, 0, :])):
        ext[f, :rows, sz.end :] = jnp.zeros((rows, LANES), jnp.float32)
        ext[f, :rows, : sz.merged] = value
    add_rows(sz, ext, near_h_ref, near_w_ref, None, far_ref)
    inv_cos, sin_centre, cos_face = geo_ref[band, 0], geo_ref[band, 1], geo_ref[band, 2]
    ratio = sz.ratio

    def tile(f, t):
        return ext[f, :, LANES * t : LANES * (t + 1)]

    kept = {}

    def zonal(t):
        if t not in kept:
            thick_e = ring.east("h", t, functools.partial(tile, 0))
            wind_e = ring.east("u", t, functools.partial(tile, 2))
            flux = 0.25 * (tile(2, t) + wind_e) * (tile(0, t) + thick_e) * inv_cos
            if t == tiles - 1:
                flux = jnp.where(lane < sz.tail - LEVELS, flux, 0.0)
            kept[t] = (flux, thick_e)
        return kept[t]

    for t in range(tiles):
        flux, thick_e = zonal(t)
        thick, wind_v, wind_u = tile(0, t), tile(1, t), tile(2, t)
        flux_w = ring.west("f", t, lambda s: zonal(s)[0])
        thick_w = ring.west("hw", t, functools.partial(tile, 0))
        thick_n = north(thick)
        flux_n = (0.25 * ratio) * (wind_v + north(wind_v)) * (thick + thick_n) * cos_face
        thick_tend = -((flux - flux_w) + (flux_n - south(flux_n)) * inv_cos)
        wind_u_tend = sin_centre * wind_v - (thick_e - thick_w) * (0.5 * inv_cos)
        wind_v_tend = -sin_centre * wind_u - (0.5 * ratio) * (thick_n - south(thick))
        spare = 0.0
        if t == tiles - 1:
            last = sz.tail - LEVELS
            columns = [(tile(0, 0), 0), (thick, last), (tile(2, 0), 0), (wind_u, last)]
            for k, (source, at) in reversed(list(enumerate(columns))):
                to = sz.tail + LEVELS * k
                spare = jnp.where(lane < to + LEVELS, pltpu.roll(source, (to - at) % LANES, 1), spare)
        for f, tend in enumerate((thick_tend, wind_u_tend, wind_v_tend, thick)):
            if sz.near_only:
                alone = jnp.where(band < sz.n_lat // 2, tend[:1], tend[rows - 1 : rows])
                if t == tiles - 1:
                    alone = jnp.where(lane[:1] < sz.tail, alone, 0.0)
                pole_ref[stack * f + t : stack * f + t + 1] = alone
            if f == 3:
                continue
            if t == tiles - 1:
                tend = jnp.where(lane < sz.tail, tend, spare)
            if sz.near_only:
                tend = jnp.where(even, north(tend), tend)
            tend_ref[pl.ds(stack * work * f + t, work, stride=stack), :] = tend[:work]
    for f in range(3):
        for t in range(tiles, stack):
            tend_ref[pl.ds(stack * work * f + t, work, stride=stack), :] = jnp.zeros((work, LANES), jnp.float32)
    used = stack * sz.units
    if used < tend_ref.shape[0]:
        tend_ref[used:, :] = jnp.zeros((tend_ref.shape[0] - used, LANES), jnp.float32)
    sides = [sides_ref[:EXT_ROWS], sides_ref[EXT_ROWS:]]
    if sz.near_only:
        sums = pole_sums(sz, pole_ref, wave_ref, spare, band)
        row = lax.broadcasted_iota(jnp.int32, (EXT_ROWS, LANES), 0)
        for k, total in enumerate(sums):
            sides = [jnp.where(row == rows + k, total, side) for side in sides]
    here = lax.axis_index("lon")
    for k, out_ref in enumerate(out_refs):
        out_ref[: sz.size] = tend_ref[sz.piece(k), :]
        eastward = sz.partner(k) == lax.rem(here + 1, sz.n_lon)
        out_ref[sz.size :] = jnp.where(eastward, sides[1], sides[0])


def pole_sums(sz, pole_ref, wave_ref, spare, band):
    stack, rows = sz.stack, sz.rows
    lane = lax.broadcasted_iota(jnp.int32, (1, LANES), 1)
    sides = jnp.where(band < sz.n_lat // 2, spare[:1], spare[rows - 1 : rows])
    found = [jnp.zeros((1, LANES), jnp.float32), pltpu.roll(sides, (LANES // 2 - sz.tail) % LANES, 1)]
    for f in range(4):
        if sz.tiles < stack:
            pole_ref[stack * f + sz.tiles : stack * (f + 1)] = jnp.zeros((stack - sz.tiles, LANES), jnp.float32)
        values = pole_ref[stack * f : stack * (f + 1)]
        for k, terms in enumerate((values, values * wave_ref[0], values * wave_ref[1])):
            total = jnp.sum(terms, axis=0, keepdims=True)
            for step in (64, 32, 16):
                total = total + pltpu.roll(total, step, 1)
            row, place = divmod(3 * f + k, PER_TILE)
            inside = (lane >= LEVELS * place) & (lane < LEVELS * (place + 1))
            found[row] = jnp.where(inside, total, found[row])
    return found


def pole_waves(sz, rows_in, inv_cos, sign):
    n_lon = sz.n_lon
    lane = lax.broadcasted_iota(jnp.int32, (1, LANES), 1)

    def value(s, place):
        row, at = divmod(place, PER_TILE)
        return pltpu.roll(rows_in[s % n_lon, row : row + 1], (-LEVELS * at) % LANES, 1)

    theta = 2 * math.pi / sz.nlon
    ends = (1.0, math.cos(theta * (sz.columns - 1)), math.sin(theta * (sz.columns - 1)))
    sums = [[[value(s, 3 * f + k) for k in range(3)] for f in range(4)] for s in range(n_lon)]
    for s in range(n_lon):
        thick_w, thick_e = value(s, 13), value(s + 1, 12)
        flux = 0.25 * (value(s, 15) + value(s + 1, 14)) * (thick_w + thick_e) * inv_cos
        slope = 0.5 * inv_cos
        after = (s + 1) % n_lon
        for f, (west_of, east_of) in enumerate(((flux, flux), (slope * thick_e, slope * thick_w))):
            for k in range(3):
                sums[s][f][k] = sums[s][f][k] - west_of * ends[k]
            for k in range(2):
                sums[after][f][k] = sums[after][f][k] + east_of
    result = []
    for f in range(3):
        waves_of = [0.0, 0.0, 0.0]
        for s in range(n_lon):
            level, cosine, sine = sums[s][f]
            if f == 2:
                level = level + (0.5 * sz.ratio) * sign * sums[s][3][0]
                cosine = cosine - (0.5 * sz.ratio) * sign * sums[s][3][1]
                sine = sine - (0.5 * sz.ratio) * sign * sums[s][3][2]
            c, d = math.cos(2 * math.pi * s / n_lon), math.sin(2 * math.pi * s / n_lon)
            waves_of[0] = waves_of[0] + level
            waves_of[1] = waves_of[1] + (c * cosine - d * sine)
            waves_of[2] = waves_of[2] + (d * cosine + c * sine)
        spread = []
        for k, total in enumerate(waves_of):
            total = jnp.where(lane < LEVELS, total * ((1.0 if k == 0 else 2.0) / sz.nlon), 0.0)
            for step in (16, 32, 64):
                total = total + pltpu.roll(total, step, 1)
            spread.append(total)
        result.append(spread)
    return result


def rest_kernel(sz, masks_ref, h_ref, w_ref, q_ref, near_h_ref, near_w_ref, near_q_ref, far_ref, geo_ref, wave_ref, after_ref, *refs):
    met_refs, (new_w_ref, new_h_ref, mass_ref, ext, pole_in) = refs[: sz.n_lon], refs[sz.n_lon :]
    band = lax.axis_index("lat")
    ring = Tiles(sz)
    lane = ring.lane
    tiles, rows = sz.tiles, sz.rows
    for f in range(6):
        if f < 2 or f == 5:
            value = (h_ref[...], w_ref[:, 1, :], w_ref[:, 0, :])[min(f, 2)]
        else:
            value = q_ref[f - 2].astype(jnp.float32)
        ext[f, :rows, : sz.merged] = value
    add_rows(sz, ext, near_h_ref, near_w_ref, near_q_ref, far_ref)
    lane9 = lane[:rows]
    here = lax.axis_index("lon")
    from_e = from_w = met_refs[0][sz.size :]
    for k, met_ref in enumerate(met_refs):
        eastward = lax.rem(sz.partner(k) - here + sz.n_lon, sz.n_lon)
        pole_in[eastward] = met_ref[sz.size + 8 :]
        from_e = jnp.where(sz.partner(k) == lax.rem(here + 1, sz.n_lon), met_ref[sz.size :], from_e)
        from_w = jnp.where(sz.partner(k) == lax.rem(here + sz.n_lon - 1, sz.n_lon), met_ref[sz.size :], from_w)
    for place, f in enumerate((0, 5, 2, 3, 4)):
        after = pltpu.roll(from_e, (sz.tail - LEVELS * place) % LANES, 1)[:rows]
        before = pltpu.roll(from_w, (LANES - LEVELS - LEVELS * place) % LANES, 1)[:rows]
        own = ext[f, :rows, sz.end :]
        edge = jnp.where(lane9 < LANES - LEVELS, after, before)
        ext[f, :rows, sz.end :] = jnp.where(lane9 < sz.tail, own, edge)
    inv_cos, sin_centre, cos_face = geo_ref[band, 0], geo_ref[band, 1], geo_ref[band, 2]
    ratio = sz.ratio

    plain, alone = masks_ref[0], masks_ref[1]
    if sz.near_only:
        band = lax.axis_index("lat")
        low = band < sz.n_lat // 2
        pole_cos = jnp.where(low, inv_cos[:1], inv_cos[rows - 1 : rows])
        kept_waves = pole_waves(sz, pole_in.at[:, rows - 8 :], pole_cos, jnp.where(low, 1.0, -1.0))

    def stepped(f, t, value, tend):
        value = value + plain * tend
        if sz.near_only:
            level, cosine, sine = kept_waves[f]
            wave = level + cosine * wave_ref[0, t : t + 1] + sine * wave_ref[1, t : t + 1]
            value = value + alone * wave
        return value

    def tile(f, t):
        return ext[f, :, LANES * t : LANES * (t + 1)]

    kept = {}

    def zonal(t):
        if t not in kept:
            thick_e = ring.east("h", t, functools.partial(tile, 0))
            wind_e = ring.east("u", t, functools.partial(tile, 5))
            flux = 0.25 * (tile(5, t) + wind_e) * (tile(0, t) + thick_e) * inv_cos
            parts = []
            for k in range(3):
                q = tile(2 + k, t)
                q_e = ring.east(k, t, functools.partial(tile, 2 + k))
                parts.append(DIFFUSION * (q_e - q) - flux * (0.5 * (q + q_e)))
            kept[t] = (flux, thick_e, parts)
        return kept[t]

    for t in range(tiles):
        span = sz.span(t)
        lanes = slice(LANES * t, LANES * t + span)
        flux, thick_e, parts = zonal(t)
        thick, wind_u, wind_v = tile(0, t), tile(5, t), tile(1, t)
        flux_w = ring.west("f", t, lambda s: zonal(s)[0])
        thick_w = ring.west("hw", t, functools.partial(tile, 0))
        thick_n = north(thick)
        flux_n = (0.25 * ratio) * (wind_v + north(wind_v)) * (thick + thick_n) * cos_face
        thick_tend = -((flux - flux_w) + (flux_n - south(flux_n)) * inv_cos)
        wind_u_tend = sin_centre * wind_v - (thick_e - thick_w) * (0.5 * inv_cos)
        wind_v_tend = -sin_centre * wind_u - (0.5 * ratio) * (thick_n - south(thick))
        new_h_ref[:, lanes] = stepped(0, t, thick, thick_tend)[:rows, :span]
        new_w_ref[0, :, lanes] = stepped(1, t, wind_u, wind_u_tend)[:rows, :span]
        new_w_ref[1, :, lanes] = stepped(2, t, wind_v, wind_v_tend)[:rows, :span]
        for k in range(3):
            q = tile(2 + k, t)
            q_n = north(q)
            zonal_part = parts[k] - ring.west(("p", k), t, lambda s: zonal(s)[2][k])
            lap = q_n + south(q) - 2.0 * q
            over = flux_n * (0.5 * (q + q_n))
            merid_part = DIFFUSION * lap - (over - south(over)) * inv_cos
            mass = thick * q + TIME_STEP * (zonal_part + merid_part)
            mass_ref[k, :, lanes] = mass[:rows, :span].astype(jnp.bfloat16)


def sin_pi(y):
    y = jnp.where(y > 0.5, 1.0 - y, jnp.where(y < -0.5, -1.0 - y, y))
    s = y * y
    series = [(-1) ** i * math.pi ** (2 * i + 1) / math.factorial(2 * i + 1) for i in range(7)]
    total = series[-1]
    for factor in reversed(series[:-1]):
        total = total * s + factor
    return total * y


def share_of(sz, i):
    unit = lax.axis_index("lon") * sz.share + i
    return unit // sz.work, sz.first() + lax.rem(unit, sz.work)


def weights_kernel(sz, cut_ref, n_ref, inverse_ref, after_ref, weights_ref, masks_ref):
    band = lax.axis_index("lat")
    row = lax.broadcasted_iota(jnp.int32, (EXT_ROWS, LANES), 0)
    cuts = jnp.full((EXT_ROWS, LANES), sz.nlon // 2, jnp.int32)
    for j in range(sz.rows):
        cuts = jnp.where(row == j, cut_ref[band * sz.rows + j], cuts)
    plain, alone = cuts >= sz.nlon // 2, sz.at_pole(row)
    masks_ref[0] = jnp.where(plain, TIME_STEP, 0.0)
    masks_ref[1] = jnp.where(alone, TIME_STEP, 0.0)
    masks_ref[2] = jnp.where(plain | alone, 0.0, TIME_STEP)
    size = PER_TILE * sz.stack
    for i in range(sz.share):
        width = (2 * cut_ref[band * sz.rows + share_of(sz, i)[1]] + 1).astype(jnp.float32)
        n = n_ref[...]
        turns = n * width
        turns = turns - jnp.round(turns * (0.5 / sz.nlon)) * (2.0 * sz.nlon)
        weights = sin_pi(turns * (1.0 / sz.nlon)) * inverse_ref[...]
        weights = jnp.where(n == 0.0, width * (1.0 / sz.nlon), weights)
        weights_ref[size * i : size * (i + 1)] = weights.astype(jnp.bfloat16)


def pass_kernel(sz, piece_ref, after_ref, also_after_ref, out_ref):
    out_ref[...] = piece_ref[...]


def filter_kernel(sz, weights_ref, geo_ref, *refs):
    n_lon, stack, share = sz.n_lon, sz.stack, sz.share
    in_refs, out_refs, (gathered, results) = refs[:n_lon], refs[n_lon : 2 * n_lon], refs[2 * n_lon :]
    for k, in_ref in enumerate(in_refs):
        gathered[sz.partner(k)] = in_ref[: sz.size]

    band = lax.axis_index("lat")
    lane = lax.broadcasted_iota(jnp.int32, (share, LANES), 1)
    place = lax.broadcasted_iota(jnp.int32, (share, LANES), 0)
    by_flux = by_thick = jnp.zeros((share, LANES), jnp.float32)
    for i in range(share):
        field, row = share_of(sz, i)
        inv_cos = geo_ref[band, 0, pl.ds(row, 1), :]
        by_flux = jnp.where((place == i) & (field == 0), inv_cos, by_flux)
        by_thick = jnp.where((place == i) & (field == 1), 0.5 * inv_cos, by_thick)
    sides = [gathered[s, pl.ds(sz.tiles - 1, share, stride=stack), :] for s in range(n_lon)]

    def column(s, k):
        return pltpu.roll(sides[s % n_lon], (-sz.tail - LEVELS * k) % LANES, 1)

    for s in range(n_lon):
        thick_w, thick_e = column(s, 1), column(s + 1, 0)
        flux = 0.25 * (column(s, 3) + column(s + 1, 2)) * (thick_w + thick_e) * by_flux
        west_of, east_of = flux + by_thick * thick_e, flux + by_thick * thick_w
        at = pl.ds(sz.tiles - 1, share, stride=stack)
        own = gathered[s, at, :]
        own = own - jnp.where(lane >= sz.tail - LEVELS, pltpu.roll(west_of, sz.tail - LEVELS, 1), 0.0)
        gathered[s, at, :] = jnp.where(lane < sz.tail, own, 0.0)
        at = pl.ds(0, share, stride=stack)
        after = (s + 1) % n_lon
        gathered[after, at, :] = gathered[after, at, :] + jnp.where(lane < LEVELS, east_of, 0.0)

    wide = lax.broadcasted_iota(jnp.int32, (stack, LANES), 1)
    rows = PER_TILE * stack
    for i in range(share):
        here = slice(stack * i, stack * (i + 1))
        pieces = [gathered[s, here].astype(jnp.bfloat16) for s in range(n_lon)]
        circle = jnp.concatenate([jnp.concatenate(pieces[s:] + pieces[:s], axis=0) for s in range(n_lon)], axis=1)
        spread = jnp.dot(weights_ref[rows * i : rows * (i + 1)], circle, preferred_element_type=jnp.float32)
        for s in range(n_lon):
            same = spread[:stack, LANES * s : LANES * (s + 1)]
            carried = None
            for e in range(1, PER_TILE):
                part = spread[stack * e : stack * (e + 1), LANES * s : LANES * (s + 1)]
                part = pltpu.roll(part, LEVELS * e, 1)
                inside = wide >= LEVELS * e
                same = same + jnp.where(inside, part, 0.0)
                over = jnp.where(inside, 0.0, part)
                carried = over if carried is None else carried + over
            results[s, here] = pltpu.roll(same, stack - 1, 0) + carried
    for k, out_ref in enumerate(out_refs):
        out_ref[...] = results[sz.partner(k, True)]


def finish_kernel(sz, masks_ref, base_w_ref, base_h_ref, *refs):
    back_refs, (new_w_ref, new_h_ref, back_ref) = refs[: sz.n_lon], refs[sz.n_lon :]
    rows, work = sz.rows, sz.work
    for k, ref in enumerate(back_refs):
        back_ref[sz.piece(k, True), :] = ref[...]
    scale = masks_ref[2]
    even = lax.rem(lax.axis_index("lat"), 2) == 0
    for f in range(3):
        for t in range(sz.tiles):
            span = sz.span(t)
            lanes = slice(LANES * t, LANES * t + span)
            tend = back_ref[pl.ds(sz.stack * work * f + t, work, stride=sz.stack), :]
            if sz.near_only:
                tend = jnp.concatenate([tend, jnp.zeros((EXT_ROWS - work, LANES), jnp.float32)], axis=0)
                tend = jnp.where(even, south(tend), tend)
            change = (scale[:rows] * tend[:rows])[:, :span]
            if f == 0:
                new_h_ref[:, lanes] = base_h_ref[:, lanes] + change
            else:
                new_w_ref[:, f - 1, lanes] = base_w_ref[f - 1, :, lanes] + change


def local(winds, thickness, tracers, cutoff):
    n_lat = lax.axis_size("lat")
    n_lon = lax.axis_size("lon")
    rows, merged = thickness.shape
    sz = Sizes(rows, merged, n_lat, n_lon)
    f32 = jnp.float32
    vmem = pl.BlockSpec(memory_space=pltpu.VMEM)
    smem = pl.BlockSpec(memory_space=pltpu.SMEM)
    hbm = pl.BlockSpec(memory_space=pltpu.HBM)
    anywhere = pl.BlockSpec(memory_space=pl.ANY)

    def shaped(*shape):
        return jax.ShapeDtypeStruct(shape, f32)

    def call(kernel, name, in_specs, out_shape, scratch=(), limit=LIMIT):
        return pl.pallas_call(
            functools.partial(kernel, sz),
            out_shape=out_shape,
            in_specs=in_specs,
            out_specs=jax.tree.map(lambda _: vmem, out_shape),
            scratch_shapes=list(scratch),
            compiler_params=pltpu.CompilerParams(vmem_limit_bytes=limit),
            name=name,
        )

    geo = jnp.asarray(geometry(sz))
    wave = jnp.asarray(waves(sz))
    n, inverse = (jnp.asarray(table) for table in offsets(sz))

    wind_rows = jnp.swapaxes(winds, 0, 1)
    tracer_rows = jnp.swapaxes(tracers, 0, 1)
    far_row, near_row = shaped(5 * sz.stack, LANES), shaped(3 * sz.stack, LANES)
    kept = [((1,), f32), ((2,), f32), ((3,), jnp.bfloat16)]
    near_q, far_rows, sides = call(
        edges_kernel,
        "edges",
        [hbm] * 3,
        (near_row, far_row, shaped(2 * EXT_ROWS, LANES)),
        [pltpu.VMEM((2,) + count + (merged,), dtype) for count, dtype in kept]
        + [
            pltpu.VMEM((rows,) + (count if count != (1,) else ()) + (lanes,), dtype)
            for lanes in (LANES, sz.tail)
            for count, dtype in kept
        ]
        + [pltpu.SemaphoreType.DMA((3, 4))],
        limit=MOST_VMEM,
    )(thickness, wind_rows, tracer_rows)

    near = [(band * n_lon + i, (band ^ 1) * n_lon + i) for band in range(n_lat) for i in range(n_lon)]
    far = []
    for band in range(n_lat):
        other = band - 1 if band % 2 == 0 else band + 1
        for i in range(n_lon):
            if 0 <= other < n_lat:
                far.append((band * n_lon + i, other * n_lon + i))
            else:
                far.append((band * n_lon + i, band * n_lon + (i + n_lon // 2) % n_lon))
    near_h = lax.ppermute(thickness, ("lat", "lon"), near)
    near_w = lax.ppermute(wind_rows, ("lat", "lon"), near)
    if not sz.near_only:
        far_rows = lax.ppermute(far_rows, ("lat", "lon"), far)

    def meetings(shares, back):
        order = [sz.turns(False, back), sz.turns(True, back)]
        got = [shares[0]]
        for k in range(1, n_lon):
            sectors = [(band, i, i ^ order[band % 2][k]) for band in range(n_lat) for i in range(n_lon)]
            got.append(lax.ppermute(shares[k], ("lat", "lon"), [(b * n_lon + i, b * n_lon + j) for b, i, j in sectors]))
        return got

    all_pieces = pltpu.VMEM((n_lon, sz.size, LANES), f32)
    *tends, far_rows, near_q = call(
        polar_kernel,
        "polar",
        [vmem] * 9,
        [shaped(sz.size + EXT_ROWS, LANES)] * n_lon + [far_row, near_row],
        [
            pltpu.VMEM((n_lon * sz.size, LANES), f32),
            pltpu.VMEM((4 * sz.stack, LANES), f32),
            pltpu.VMEM((3, EXT_ROWS, sz.tiles * LANES), f32),
        ],
    )(thickness, wind_rows, near_h, near_w, sides, geo, wave, far_rows, near_q)
    met = meetings(tends, False)
    near_q = lax.ppermute(near_q, ("lat", "lon"), near)
    from_far = lax.ppermute(far_rows, ("lat", "lon"), far) if sz.near_only else far_rows
    weights, masks = call(
        weights_kernel,
        "weights",
        [smem, vmem, vmem, anywhere],
        (
            jax.ShapeDtypeStruct((sz.share * PER_TILE * sz.stack, n_lon * sz.stack), jnp.bfloat16),
            shaped(3, EXT_ROWS, LANES),
        ),
    )(cutoff, n, inverse, tends[0])
    worked = call(
        filter_kernel,
        "filter",
        [vmem] * 2 + [vmem] * n_lon,
        [shaped(sz.size, LANES)] * n_lon,
        [all_pieces, all_pieces],
    )(weights, geo, *met)
    held = call(pass_kernel, "pass", [vmem] + [anywhere] * 2, shaped(sz.size, LANES))(worked[-1], from_far, near_q)
    worked = [*worked[:-1], held]
    back = meetings(worked, True)

    base_w, base_h, mass = call(
        rest_kernel,
        "rest",
        [vmem] * 10 + [anywhere] + [vmem] * n_lon,
        (shaped(2, rows, merged), shaped(rows, merged), jax.ShapeDtypeStruct(tracers.shape, jnp.bfloat16)),
        [pltpu.VMEM((6, EXT_ROWS, sz.tiles * LANES), f32), pltpu.VMEM((n_lon, 8, LANES), f32)],
    )(masks, thickness, wind_rows, tracers, near_h, near_w, near_q, from_far, geo, wave, worked[0], *met)

    new_w, new_h = call(
        finish_kernel,
        "finish",
        [vmem] * (3 + n_lon),
        (shaped(*wind_rows.shape), shaped(rows, merged)),
        [pltpu.VMEM((n_lon * sz.size, LANES), f32)],
    )(masks, base_w, base_h, *back)
    return jnp.swapaxes(new_w, 0, 1), new_h, mass


def solution(mesh):
    in_specs = (P(None, "lat", "lon"), P("lat", "lon"), P(None, "lat", "lon"), P())
    out_specs = (P(None, "lat", "lon"), P("lat", "lon"), P(None, "lat", "lon"))
    return jax.shard_map(local, mesh=mesh, in_specs=in_specs, out_specs=out_specs, check_vma=False)
```

```python
import functools
import math

import jax
import jax.numpy as jnp
import numpy as np
from jax import lax
from jax.experimental import pallas as pl
from jax.experimental.pallas import tpu as pltpu
from jax.sharding import PartitionSpec as P

LEVELS = 16
TIME_STEP = 0.05
DIFFUSION = 0.5
LANES = 128
PER_TILE = LANES // LEVELS
EXT_ROWS = 16
LIMIT = 48 * 1024 * 1024
MOST_VMEM = 64 * 1024 * 1024 - 10500 * 1024


class Sizes:
    def __init__(self, rows, merged, n_lat, n_lon):
        self.rows = rows
        self.merged = merged
        self.columns = merged // LEVELS
        self.n_lat = n_lat
        self.n_lon = n_lon
        self.nlat = rows * n_lat
        self.nlon = self.columns * n_lon
        self.ratio = 2.0 * self.nlat / self.nlon
        self.tiles = -(-merged // LANES)
        self.end = (self.tiles - 1) * LANES
        self.tail = merged - self.end
        self.stack = -(-(self.tiles + 1) // 8) * 8
        self.near_only = rows <= self.nlat // 6 < 2 * rows
        self.work = rows - 1 if self.near_only else rows
        self.units = 3 * self.work
        self.share = -(-self.units // n_lon)
        self.size = self.share * self.stack
        assert self.tail <= LANES - 4 * LEVELS and rows + 2 <= EXT_ROWS and n_lat % 2 == 0
        assert n_lon >= 4 and n_lon & (n_lon - 1) == 0

    def span(self, tile):
        return self.tail if tile == self.tiles - 1 else LANES

    def first(self):
        return jnp.where(lax.rem(lax.axis_index("lat"), 2) == 0, 1, 0) if self.near_only else 0

    def at_pole(self, row):
        band = lax.axis_index("lat")
        pole = jnp.where(band == 0, 0, jnp.where(band == self.n_lat - 1, self.rows - 1, -1))
        return row == (pole if self.near_only else -1)

    def turns(self, odd):
        middle, last = list(range(1, self.n_lon - 1)), self.n_lon - 1
        return [0, last] + middle if odd else [0, middle[-1], last] + middle[-2::-1]

    def partner(self, k):
        odd = lax.rem(lax.axis_index("lat"), 2) == 1
        turn = jnp.where(odd, self.turns(True)[k], self.turns(False)[k])
        return jnp.bitwise_xor(lax.axis_index("lon"), turn)

    def piece(self, k):
        return pl.ds(pl.multiple_of(self.partner(k) * self.size, 8), self.size)


def geometry(sz):
    table = np.zeros((sz.n_lat, 3, EXT_ROWS, LANES), np.float64)

    def face(j):
        return math.sin((j + 1) * math.pi / sz.nlat) if 0 <= j < sz.nlat - 1 else 0.0

    for band in range(sz.n_lat):
        for row in range(sz.rows):
            j = band * sz.rows + row
            centre = (j + 0.5) * math.pi / sz.nlat - math.pi / 2
            table[band, 0, row] = 1.0 / math.cos(centre)
            table[band, 1, row] = math.sin(centre)
            table[band, 2, row] = face(j)
        table[band, 2, EXT_ROWS - 1] = face(band * sz.rows - 1)
    return table.astype(np.float32)


def offsets(sz):
    shift, out_tile = np.divmod(np.arange(PER_TILE * sz.stack), sz.stack)
    sector, in_tile = np.divmod(np.arange(sz.n_lon * sz.stack), sz.stack)
    n = (PER_TILE * (out_tile - 1) + shift)[:, None] - (PER_TILE * in_tile + sz.columns * sector)[None, :]
    n = (n + sz.nlon // 2) % sz.nlon - sz.nlon // 2
    with np.errstate(divide="ignore"):
        inverse = np.where(n == 0, 0.0, 1.0 / (sz.nlon * np.sin(np.pi * n / sz.nlon)))
    return n.astype(np.float32), inverse.astype(np.float32)


def waves(sz):
    column = PER_TILE * np.arange(sz.stack)[:, None] + np.arange(LANES)[None, :] // LEVELS
    angle = 2 * np.pi * column / sz.nlon
    return np.stack([np.cos(angle), np.sin(angle)]).astype(np.float32)


def edges_kernel(sz, h_hbm, w_hbm, q_hbm, near_ref, far_ref, sides_ref, *scratch):
    row_refs, first_refs, last_refs, sems = scratch[:3], scratch[3:6], scratch[6:9], scratch[9]
    rows, last = sz.rows, sz.rows - 1
    even = lax.rem(lax.axis_index("lat"), 2) == 0
    copies = []
    for i, source in enumerate((h_hbm, w_hbm, q_hbm)):
        for k, row in enumerate((0, last)):
            one = source.at[pl.ds(row, 1)] if i == 0 else source.at[row]
            copies.append(pltpu.make_async_copy(one, row_refs[i].at[k], sems.at[i, k]))
        for k, (start, to) in enumerate(((0, first_refs[i]), (sz.end, last_refs[i]))):
            lanes = pl.ds(start, to.shape[-1])
            cut = source.at[:, lanes] if i == 0 else source.at[:, :, lanes]
            copies.append(pltpu.make_async_copy(cut, to, sems.at[i, 2 + k]))
    for copy in copies:
        copy.start()
    for copy in copies:
        copy.wait()
    h_rows, w_rows, q_rows = row_refs
    for t in range(sz.tiles):
        wide = sz.span(t)
        lanes = slice(LANES * t, LANES * t + wide)
        q = [q_rows[k, :, lanes].astype(jnp.float32) for k in range(2)]
        for f in range(5):
            if f == 0:
                first, final = h_rows[0, :, lanes], h_rows[1, :, lanes]
            elif f == 1:
                first, final = w_rows[0, 1:2, lanes], w_rows[1, 1:2, lanes]
            else:
                first, final = q[0][f - 2 : f - 1], q[1][f - 2 : f - 1]
                at = sz.stack * (f - 2) + t
                near_ref[at : at + 1, :wide] = jnp.where(even, final, first)
            at = sz.stack * f + t
            far_ref[at : at + 1, :wide] = jnp.where(even, first, final)
    sides_ref[...] = jnp.zeros(sides_ref.shape, jnp.float32)
    for k, (refs, at) in enumerate(((first_refs, 0), (last_refs, sz.tail - LEVELS))):
        columns = slice(at, at + LEVELS)
        for f in range(5):
            if f == 0:
                value = refs[0][:, columns]
            elif f == 1:
                value = refs[1][:, 0, columns]
            else:
                value = refs[2][:, f - 2, columns].astype(jnp.float32)
            sides_ref[EXT_ROWS * k : EXT_ROWS * k + rows, LEVELS * f : LEVELS * (f + 1)] = value


def add_rows(sz, ext, near_h_ref, near_w_ref, near_q_ref, far_ref):
    band = lax.axis_index("lat")
    even = lax.rem(band, 2) == 0
    over_pole = (band == 0) | (band == sz.n_lat - 1)
    last = sz.rows - 1
    for f in range(2 if near_q_ref is None else 5):
        flip = jnp.where(over_pole, -1.0, 1.0) if f == 1 else 1.0
        for t in range(sz.tiles):
            lanes = slice(LANES * t, LANES * t + sz.span(t))
            if f == 0:
                near = jnp.where(even, near_h_ref[0:1, lanes], near_h_ref[last : sz.rows, lanes])
            elif f == 1:
                near = jnp.where(even, near_w_ref[0, 1:2, lanes], near_w_ref[last, 1:2, lanes])
            else:
                at = sz.stack * (f - 2) + t
                near = near_q_ref[at : at + 1, : sz.span(t)]
            at = sz.stack * f + t
            far = jnp.zeros_like(near) if far_ref is None else far_ref[at : at + 1, : sz.span(t)] * flip
            ext[f, sz.rows : sz.rows + 1, lanes] = jnp.where(even, near, far)
            ext[f, EXT_ROWS - 1 : EXT_ROWS, lanes] = jnp.where(even, far, near)


class Tiles:
    def __init__(self, sz):
        self.sz = sz
        self.lane = lax.broadcasted_iota(jnp.int32, (EXT_ROWS, LANES), 1)
        self.turned = {}

    def turn(self, name, t, value, step):
        key = (name, t % self.sz.tiles, step)
        if key not in self.turned:
            self.turned[key] = pltpu.roll(value(t % self.sz.tiles), step % LANES, 1)
        return self.turned[key]

    def east(self, name, t, value):
        here = self.turn(name, t, value, -LEVELS)
        return jnp.where(self.lane < LANES - LEVELS, here, self.turn(name, t + 1, value, -LEVELS))

    def west(self, name, t, value):
        here = self.turn(name, t, value, LEVELS)
        return jnp.where(self.lane >= LEVELS, here, self.turn(name, t - 1, value, LEVELS))


def north(value):
    return pltpu.roll(value, EXT_ROWS - 1, 0)


def south(value):
    return pltpu.roll(value, 1, 0)


def polar_kernel(sz, h_ref, w_ref, near_h_ref, near_w_ref, sides_ref, geo_ref, wave_ref, far_ref, near_q_ref, *refs):
    out_refs, (far_out, near_out, tend_ref, pole_ref, ext) = refs[:-5], refs[-5:]
    far_out[...] = far_ref[...]
    near_out[...] = near_q_ref[...]
    if sz.near_only:
        far_ref = None
    band = lax.axis_index("lat")
    ring = Tiles(sz)
    lane = ring.lane
    tiles, stack, rows, work = sz.tiles, sz.stack, sz.rows, sz.work
    even = lax.rem(band, 2) == 0
    for f, value in enumerate((h_ref[...], w_ref[:, 1, :], w_ref[:, 0, :])):
        ext[f, :rows, sz.end :] = jnp.zeros((rows, LANES), jnp.float32)
        ext[f, :rows, : sz.merged] = value
    add_rows(sz, ext, near_h_ref, near_w_ref, None, far_ref)
    inv_cos, sin_centre, cos_face = geo_ref[band, 0], geo_ref[band, 1], geo_ref[band, 2]
    ratio = sz.ratio

    def tile(f, t):
        return ext[f, :, LANES * t : LANES * (t + 1)]

    kept = {}

    def zonal(t):
        if t not in kept:
            thick_e = ring.east("h", t, functools.partial(tile, 0))
            wind_e = ring.east("u", t, functools.partial(tile, 2))
            flux = 0.25 * (tile(2, t) + wind_e) * (tile(0, t) + thick_e) * inv_cos
            if t == tiles - 1:
                flux = jnp.where(lane < sz.tail - LEVELS, flux, 0.0)
            kept[t] = (flux, thick_e)
        return kept[t]

    for t in range(tiles):
        flux, thick_e = zonal(t)
        thick, wind_v, wind_u = tile(0, t), tile(1, t), tile(2, t)
        flux_w = ring.west("f", t, lambda s: zonal(s)[0])
        thick_w = ring.west("hw", t, functools.partial(tile, 0))
        thick_n = north(thick)
        flux_n = (0.25 * ratio) * (wind_v + north(wind_v)) * (thick + thick_n) * cos_face
        thick_tend = -((flux - flux_w) + (flux_n - south(flux_n)) * inv_cos)
        wind_u_tend = sin_centre * wind_v - (thick_e - thick_w) * (0.5 * inv_cos)
        wind_v_tend = -sin_centre * wind_u - (0.5 * ratio) * (thick_n - south(thick))
        spare = 0.0
        if t == tiles - 1:
            last = sz.tail - LEVELS
            columns = [(tile(0, 0), 0), (thick, last), (tile(2, 0), 0), (wind_u, last)]
            for k, (source, at) in reversed(list(enumerate(columns))):
                to = sz.tail + LEVELS * k
                spare = jnp.where(lane < to + LEVELS, pltpu.roll(source, (to - at) % LANES, 1), spare)
        for f, tend in enumerate((thick_tend, wind_u_tend, wind_v_tend, thick)):
            if sz.near_only:
                alone = jnp.where(band < sz.n_lat // 2, tend[:1], tend[rows - 1 : rows])
                if t == tiles - 1:
                    alone = jnp.where(lane[:1] < sz.tail, alone, 0.0)
                pole_ref[stack * f + t : stack * f + t + 1] = alone
            if f == 3:
                continue
            if t == tiles - 1:
                tend = jnp.where(lane < sz.tail, tend, spare)
            if sz.near_only:
                tend = jnp.where(even, north(tend), tend)
            tend_ref[pl.ds(stack * work * f + t, work, stride=stack), :] = tend[:work]
    for f in range(3):
        for t in range(tiles, stack):
            tend_ref[pl.ds(stack * work * f + t, work, stride=stack), :] = jnp.zeros((work, LANES), jnp.float32)
    used, sent = stack * sz.units, sz.n_lon * sz.size
    if used < sent:
        tend_ref[used:sent, :] = jnp.zeros((sent - used, LANES), jnp.float32)
    sides = [sides_ref[:EXT_ROWS], sides_ref[EXT_ROWS:]]
    if sz.near_only:
        sums = pole_sums(sz, pole_ref, wave_ref, spare, band)
        row = lax.broadcasted_iota(jnp.int32, (EXT_ROWS, LANES), 0)
        for k, total in enumerate(sums):
            sides = [jnp.where(row == rows + k, total, side) for side in sides]
    here = lax.axis_index("lon")
    for k, out_ref in enumerate(out_refs):
        out_ref[: sz.size] = tend_ref[sz.piece(k), :]
        eastward = sz.partner(k) == lax.rem(here + 1, sz.n_lon)
        out_ref[sz.size :] = jnp.where(eastward, sides[1], sides[0])


def pole_sums(sz, pole_ref, wave_ref, spare, band):
    stack, rows = sz.stack, sz.rows
    lane = lax.broadcasted_iota(jnp.int32, (1, LANES), 1)
    sides = jnp.where(band < sz.n_lat // 2, spare[:1], spare[rows - 1 : rows])
    found = [jnp.zeros((1, LANES), jnp.float32), pltpu.roll(sides, (LANES // 2 - sz.tail) % LANES, 1)]
    for f in range(4):
        if sz.tiles < stack:
            pole_ref[stack * f + sz.tiles : stack * (f + 1)] = jnp.zeros((stack - sz.tiles, LANES), jnp.float32)
        values = pole_ref[stack * f : stack * (f + 1)]
        for k, terms in enumerate((values, values * wave_ref[0], values * wave_ref[1])):
            total = jnp.sum(terms, axis=0, keepdims=True)
            for step in (64, 32, 16):
                total = total + pltpu.roll(total, step, 1)
            row, place = divmod(3 * f + k, PER_TILE)
            inside = (lane >= LEVELS * place) & (lane < LEVELS * (place + 1))
            found[row] = jnp.where(inside, total, found[row])
    return found


def pole_waves(sz, rows_in, inv_cos, sign):
    n_lon = sz.n_lon
    lane = lax.broadcasted_iota(jnp.int32, (1, LANES), 1)

    def value(s, place):
        row, at = divmod(place, PER_TILE)
        return pltpu.roll(rows_in[s % n_lon, row : row + 1], (-LEVELS * at) % LANES, 1)

    theta = 2 * math.pi / sz.nlon
    ends = (1.0, math.cos(theta * (sz.columns - 1)), math.sin(theta * (sz.columns - 1)))
    sums = [[[value(s, 3 * f + k) for k in range(3)] for f in range(4)] for s in range(n_lon)]
    for s in range(n_lon):
        thick_w, thick_e = value(s, 13), value(s + 1, 12)
        flux = 0.25 * (value(s, 15) + value(s + 1, 14)) * (thick_w + thick_e) * inv_cos
        slope = 0.5 * inv_cos
        after = (s + 1) % n_lon
        for f, (west_of, east_of) in enumerate(((flux, flux), (slope * thick_e, slope * thick_w))):
            for k in range(3):
                sums[s][f][k] = sums[s][f][k] - west_of * ends[k]
            for k in range(2):
                sums[after][f][k] = sums[after][f][k] + east_of
    result = []
    for f in range(3):
        waves_of = [0.0, 0.0, 0.0]
        for s in range(n_lon):
            level, cosine, sine = sums[s][f]
            if f == 2:
                level = level + (0.5 * sz.ratio) * sign * sums[s][3][0]
                cosine = cosine - (0.5 * sz.ratio) * sign * sums[s][3][1]
                sine = sine - (0.5 * sz.ratio) * sign * sums[s][3][2]
            c, d = math.cos(2 * math.pi * s / n_lon), math.sin(2 * math.pi * s / n_lon)
            waves_of[0] = waves_of[0] + level
            waves_of[1] = waves_of[1] + (c * cosine - d * sine)
            waves_of[2] = waves_of[2] + (d * cosine + c * sine)
        spread = []
        for k, total in enumerate(waves_of):
            total = jnp.where(lane < LEVELS, total * ((1.0 if k == 0 else 2.0) / sz.nlon), 0.0)
            for step in (16, 32, 64):
                total = total + pltpu.roll(total, step, 1)
            spread.append(total)
        result.append(spread)
    return result


def rest_kernel(sz, masks_ref, h_ref, w_ref, q_ref, near_h_ref, near_w_ref, near_q_ref, far_ref, geo_ref, wave_ref, after_ref, *refs):
    met_refs, (new_w_ref, new_h_ref, mass_ref, ext, pole_in) = refs[: sz.n_lon], refs[sz.n_lon :]
    band = lax.axis_index("lat")
    ring = Tiles(sz)
    lane = ring.lane
    tiles, rows = sz.tiles, sz.rows
    for f in range(6):
        if f < 2 or f == 5:
            value = (h_ref[...], w_ref[:, 1, :], w_ref[:, 0, :])[min(f, 2)]
        else:
            value = q_ref[f - 2].astype(jnp.float32)
        ext[f, :rows, : sz.merged] = value
    add_rows(sz, ext, near_h_ref, near_w_ref, near_q_ref, far_ref)
    lane9 = lane[:rows]
    here = lax.axis_index("lon")
    from_e = from_w = met_refs[0][sz.size :]
    for k, met_ref in enumerate(met_refs):
        eastward = lax.rem(sz.partner(k) - here + sz.n_lon, sz.n_lon)
        pole_in[eastward] = met_ref[sz.size + 8 :]
        from_e = jnp.where(sz.partner(k) == lax.rem(here + 1, sz.n_lon), met_ref[sz.size :], from_e)
        from_w = jnp.where(sz.partner(k) == lax.rem(here + sz.n_lon - 1, sz.n_lon), met_ref[sz.size :], from_w)
    for place, f in enumerate((0, 5, 2, 3, 4)):
        after = pltpu.roll(from_e, (sz.tail - LEVELS * place) % LANES, 1)[:rows]
        before = pltpu.roll(from_w, (LANES - LEVELS - LEVELS * place) % LANES, 1)[:rows]
        own = ext[f, :rows, sz.end :]
        edge = jnp.where(lane9 < LANES - LEVELS, after, before)
        ext[f, :rows, sz.end :] = jnp.where(lane9 < sz.tail, own, edge)
    inv_cos, sin_centre, cos_face = geo_ref[band, 0], geo_ref[band, 1], geo_ref[band, 2]
    ratio = sz.ratio

    plain, alone = masks_ref[0], masks_ref[1]
    if sz.near_only:
        band = lax.axis_index("lat")
        low = band < sz.n_lat // 2
        pole_cos = jnp.where(low, inv_cos[:1], inv_cos[rows - 1 : rows])
        kept_waves = pole_waves(sz, pole_in.at[:, rows - 8 :], pole_cos, jnp.where(low, 1.0, -1.0))

    def stepped(f, t, value, tend):
        value = value + plain * tend
        if sz.near_only:
            level, cosine, sine = kept_waves[f]
            wave = level + cosine * wave_ref[0, t : t + 1] + sine * wave_ref[1, t : t + 1]
            value = value + alone * wave
        return value

    def tile(f, t):
        return ext[f, :, LANES * t : LANES * (t + 1)]

    kept = {}

    def zonal(t):
        if t not in kept:
            thick_e = ring.east("h", t, functools.partial(tile, 0))
            wind_e = ring.east("u", t, functools.partial(tile, 5))
            flux = 0.25 * (tile(5, t) + wind_e) * (tile(0, t) + thick_e) * inv_cos
            parts = []
            for k in range(3):
                q = tile(2 + k, t)
                q_e = ring.east(k, t, functools.partial(tile, 2 + k))
                parts.append(DIFFUSION * (q_e - q) - flux * (0.5 * (q + q_e)))
            kept[t] = (flux, thick_e, parts)
        return kept[t]

    for t in range(tiles):
        span = sz.span(t)
        lanes = slice(LANES * t, LANES * t + span)
        flux, thick_e, parts = zonal(t)
        thick, wind_u, wind_v = tile(0, t), tile(5, t), tile(1, t)
        flux_w = ring.west("f", t, lambda s: zonal(s)[0])
        thick_w = ring.west("hw", t, functools.partial(tile, 0))
        thick_n = north(thick)
        flux_n = (0.25 * ratio) * (wind_v + north(wind_v)) * (thick + thick_n) * cos_face
        thick_tend = -((flux - flux_w) + (flux_n - south(flux_n)) * inv_cos)
        wind_u_tend = sin_centre * wind_v - (thick_e - thick_w) * (0.5 * inv_cos)
        wind_v_tend = -sin_centre * wind_u - (0.5 * ratio) * (thick_n - south(thick))
        new_h_ref[:, lanes] = stepped(0, t, thick, thick_tend)[:rows, :span]
        new_w_ref[0, :, lanes] = stepped(1, t, wind_u, wind_u_tend)[:rows, :span]
        new_w_ref[1, :, lanes] = stepped(2, t, wind_v, wind_v_tend)[:rows, :span]
        for k in range(3):
            q = tile(2 + k, t)
            q_n = north(q)
            zonal_part = parts[k] - ring.west(("p", k), t, lambda s: zonal(s)[2][k])
            lap = q_n + south(q) - 2.0 * q
            over = flux_n * (0.5 * (q + q_n))
            merid_part = DIFFUSION * lap - (over - south(over)) * inv_cos
            mass = thick * q + TIME_STEP * (zonal_part + merid_part)
            mass_ref[k, :, lanes] = mass[:rows, :span].astype(jnp.bfloat16)


def sin_pi(y):
    y = jnp.where(y > 0.5, 1.0 - y, jnp.where(y < -0.5, -1.0 - y, y))
    s = y * y
    series = [(-1) ** i * math.pi ** (2 * i + 1) / math.factorial(2 * i + 1) for i in range(7)]
    total = series[-1]
    for factor in reversed(series[:-1]):
        total = total * s + factor
    return total * y


def share_of(sz, i):
    unit = lax.axis_index("lon") * sz.share + i
    return unit // sz.work, sz.first() + lax.rem(unit, sz.work)


def weights_kernel(sz, cut_ref, n_ref, inverse_ref, after_ref, weights_ref, masks_ref):
    band = lax.axis_index("lat")
    row = lax.broadcasted_iota(jnp.int32, (EXT_ROWS, LANES), 0)
    cuts = jnp.full((EXT_ROWS, LANES), sz.nlon // 2, jnp.int32)
    for j in range(sz.rows):
        cuts = jnp.where(row == j, cut_ref[band * sz.rows + j], cuts)
    plain, alone = cuts >= sz.nlon // 2, sz.at_pole(row)
    masks_ref[0] = jnp.where(plain, TIME_STEP, 0.0)
    masks_ref[1] = jnp.where(alone, TIME_STEP, 0.0)
    masks_ref[2] = jnp.where(plain | alone, 0.0, TIME_STEP)
    size = PER_TILE * sz.stack
    for i in range(sz.share):
        width = (2 * cut_ref[band * sz.rows + share_of(sz, i)[1]] + 1).astype(jnp.float32)
        n = n_ref[...]
        turns = n * width
        turns = turns - jnp.round(turns * (0.5 / sz.nlon)) * (2.0 * sz.nlon)
        weights = sin_pi(turns * (1.0 / sz.nlon)) * inverse_ref[...]
        weights = jnp.where(n == 0.0, width * (1.0 / sz.nlon), weights)
        weights_ref[size * i : size * (i + 1)] = weights.astype(jnp.bfloat16)


def pass_kernel(sz, piece_ref, after_ref, also_after_ref, out_ref):
    out_ref[...] = piece_ref[...]


def filter_kernel(sz, weights_ref, geo_ref, *refs):
    n_lon, stack, share = sz.n_lon, sz.stack, sz.share
    in_refs, out_refs, (gathered, results) = refs[:n_lon], refs[n_lon : 2 * n_lon], refs[2 * n_lon :]
    for k, in_ref in enumerate(in_refs):
        gathered[sz.partner(k), : sz.size] = in_ref[: sz.size]

    band = lax.axis_index("lat")
    lane = lax.broadcasted_iota(jnp.int32, (share, LANES), 1)
    place = lax.broadcasted_iota(jnp.int32, (share, LANES), 0)
    by_flux = by_thick = jnp.zeros((share, LANES), jnp.float32)
    for i in range(share):
        field, row = share_of(sz, i)
        inv_cos = geo_ref[band, 0, pl.ds(row, 1), :]
        by_flux = jnp.where((place == i) & (field == 0), inv_cos, by_flux)
        by_thick = jnp.where((place == i) & (field == 1), 0.5 * inv_cos, by_thick)
    sides = [gathered[s, pl.ds(sz.tiles - 1, share, stride=stack), :] for s in range(n_lon)]

    def column(s, k):
        return pltpu.roll(sides[s % n_lon], (-sz.tail - LEVELS * k) % LANES, 1)

    for s in range(n_lon):
        thick_w, thick_e = column(s, 1), column(s + 1, 0)
        flux = 0.25 * (column(s, 3) + column(s + 1, 2)) * (thick_w + thick_e) * by_flux
        west_of, east_of = flux + by_thick * thick_e, flux + by_thick * thick_w
        at = pl.ds(sz.tiles - 1, share, stride=stack)
        own = gathered[s, at, :]
        own = own - jnp.where(lane >= sz.tail - LEVELS, pltpu.roll(west_of, sz.tail - LEVELS, 1), 0.0)
        gathered[s, at, :] = jnp.where(lane < sz.tail, own, 0.0)
        at = pl.ds(0, share, stride=stack)
        after = (s + 1) % n_lon
        gathered[after, at, :] = gathered[after, at, :] + jnp.where(lane < LEVELS, east_of, 0.0)

    wide = lax.broadcasted_iota(jnp.int32, (stack, LANES), 1)
    rows = PER_TILE * stack
    for i in range(share):
        here = slice(stack * i, stack * (i + 1))
        pieces = [gathered[s, here].astype(jnp.bfloat16) for s in range(n_lon)]
        circle = jnp.concatenate([jnp.concatenate(pieces[s:] + pieces[:s], axis=0) for s in range(n_lon)], axis=1)
        spread = jnp.dot(weights_ref[rows * i : rows * (i + 1)], circle, preferred_element_type=jnp.float32)
        for s in range(n_lon):
            same = spread[:stack, LANES * s : LANES * (s + 1)]
            carried = None
            for e in range(1, PER_TILE):
                part = spread[stack * e : stack * (e + 1), LANES * s : LANES * (s + 1)]
                part = pltpu.roll(part, LEVELS * e, 1)
                inside = wide >= LEVELS * e
                same = same + jnp.where(inside, part, 0.0)
                over = jnp.where(inside, 0.0, part)
                carried = over if carried is None else carried + over
            results[s, here] = pltpu.roll(same, stack - 1, 0) + carried
    for k, out_ref in enumerate(out_refs):
        out_ref[...] = results[sz.partner(k), : sz.size]


def finish_kernel(sz, masks_ref, base_w_ref, base_h_ref, *refs):
    back_refs, (new_w_ref, new_h_ref, back_ref) = refs[: sz.n_lon], refs[sz.n_lon :]
    rows, work = sz.rows, sz.work
    for k, ref in enumerate(back_refs):
        back_ref[sz.piece(k), :] = ref[...]
    scale = masks_ref[2]
    even = lax.rem(lax.axis_index("lat"), 2) == 0
    for f in range(3):
        for t in range(sz.tiles):
            span = sz.span(t)
            lanes = slice(LANES * t, LANES * t + span)
            tend = back_ref[pl.ds(sz.stack * work * f + t, work, stride=sz.stack), :]
            if sz.near_only:
                tend = jnp.concatenate([tend, jnp.zeros((EXT_ROWS - work, LANES), jnp.float32)], axis=0)
                tend = jnp.where(even, south(tend), tend)
            change = (scale[:rows] * tend[:rows])[:, :span]
            if f == 0:
                new_h_ref[:, lanes] = base_h_ref[:, lanes] + change
            else:
                new_w_ref[:, f - 1, lanes] = base_w_ref[f - 1, :, lanes] + change


def local(winds, thickness, tracers, cutoff):
    n_lat = lax.axis_size("lat")
    n_lon = lax.axis_size("lon")
    rows, merged = thickness.shape
    sz = Sizes(rows, merged, n_lat, n_lon)
    f32 = jnp.float32
    vmem = pl.BlockSpec(memory_space=pltpu.VMEM)
    smem = pl.BlockSpec(memory_space=pltpu.SMEM)
    hbm = pl.BlockSpec(memory_space=pltpu.HBM)
    anywhere = pl.BlockSpec(memory_space=pl.ANY)

    def shaped(*shape):
        return jax.ShapeDtypeStruct(shape, f32)

    def call(kernel, name, in_specs, out_shape, scratch=(), limit=LIMIT):
        return pl.pallas_call(
            functools.partial(kernel, sz),
            out_shape=out_shape,
            in_specs=in_specs,
            out_specs=jax.tree.map(lambda _: vmem, out_shape),
            scratch_shapes=list(scratch),
            compiler_params=pltpu.CompilerParams(vmem_limit_bytes=limit),
            name=name,
        )

    geo = jnp.asarray(geometry(sz))
    wave = jnp.asarray(waves(sz))
    n, inverse = (jnp.asarray(table) for table in offsets(sz))

    wind_rows = jnp.swapaxes(winds, 0, 1)
    tracer_rows = jnp.swapaxes(tracers, 0, 1)
    far_row, near_row = shaped(5 * sz.stack, LANES), shaped(3 * sz.stack, LANES)
    kept = [((1,), f32), ((2,), f32), ((3,), jnp.bfloat16)]
    near_q, far_rows, sides = call(
        edges_kernel,
        "edges",
        [hbm] * 3,
        (near_row, far_row, shaped(2 * EXT_ROWS, LANES)),
        [pltpu.VMEM((2,) + count + (merged,), dtype) for count, dtype in kept]
        + [
            pltpu.VMEM((rows,) + (count if count != (1,) else ()) + (lanes,), dtype)
            for lanes in (LANES, sz.tail)
            for count, dtype in kept
        ]
        + [pltpu.SemaphoreType.DMA((3, 4))],
        limit=MOST_VMEM,
    )(thickness, wind_rows, tracer_rows)

    near = [(band * n_lon + i, (band ^ 1) * n_lon + i) for band in range(n_lat) for i in range(n_lon)]
    far = []
    for band in range(n_lat):
        other = band - 1 if band % 2 == 0 else band + 1
        for i in range(n_lon):
            if 0 <= other < n_lat:
                far.append((band * n_lon + i, other * n_lon + i))
            else:
                far.append((band * n_lon + i, band * n_lon + (i + n_lon // 2) % n_lon))
    near_h = lax.ppermute(thickness, ("lat", "lon"), near)
    near_w = lax.ppermute(wind_rows, ("lat", "lon"), near)
    if not sz.near_only:
        far_rows = lax.ppermute(far_rows, ("lat", "lon"), far)

    order = [sz.turns(False), sz.turns(True)]

    def meetings(shares):
        got = [shares[0]]
        for k in range(1, n_lon):
            sectors = [(band, i, i ^ order[band % 2][k]) for band in range(n_lat) for i in range(n_lon)]
            got.append(lax.ppermute(shares[k], ("lat", "lon"), [(b * n_lon + i, b * n_lon + j) for b, i, j in sectors]))
        return got

    all_pieces = pltpu.VMEM((n_lon, sz.size + 8 * sz.stack, LANES), f32)
    all_units = pltpu.VMEM((n_lon * sz.size + 8 * sz.stack, LANES), f32)
    *tends, far_rows, near_q = call(
        polar_kernel,
        "polar",
        [vmem] * 9,
        [shaped(sz.size + EXT_ROWS, LANES)] * n_lon + [far_row, near_row],
        [
            all_units,
            pltpu.VMEM((4 * sz.stack, LANES), f32),
            pltpu.VMEM((3, EXT_ROWS, sz.tiles * LANES), f32),
        ],
    )(thickness, wind_rows, near_h, near_w, sides, geo, wave, far_rows, near_q)
    met = meetings(tends)
    near_q = lax.ppermute(near_q, ("lat", "lon"), near)
    from_far = lax.ppermute(far_rows, ("lat", "lon"), far) if sz.near_only else far_rows
    weights, masks = call(
        weights_kernel,
        "weights",
        [smem, vmem, vmem, anywhere],
        (
            jax.ShapeDtypeStruct((sz.share * PER_TILE * sz.stack, n_lon * sz.stack), jnp.bfloat16),
            shaped(3, EXT_ROWS, LANES),
        ),
    )(cutoff, n, inverse, tends[0])
    worked = call(
        filter_kernel,
        "filter",
        [vmem] * 2 + [vmem] * n_lon,
        [shaped(sz.size, LANES)] * n_lon,
        [all_pieces, all_pieces],
    )(weights, geo, *met)
    held = call(pass_kernel, "pass", [vmem] + [anywhere] * 2, shaped(sz.size, LANES))(worked[-1], from_far, near_q)
    worked = [*worked[:-1], held]
    back = meetings(worked)

    base_w, base_h, mass = call(
        rest_kernel,
        "rest",
        [vmem] * 10 + [anywhere] + [vmem] * n_lon,
        (shaped(2, rows, merged), shaped(rows, merged), jax.ShapeDtypeStruct(tracers.shape, jnp.bfloat16)),
        [pltpu.VMEM((6, EXT_ROWS, sz.tiles * LANES), f32), pltpu.VMEM((n_lon, 8, LANES), f32)],
    )(masks, thickness, wind_rows, tracers, near_h, near_w, near_q, from_far, geo, wave, worked[0], *met)

    new_w, new_h = call(
        finish_kernel,
        "finish",
        [vmem] * (3 + n_lon),
        (shaped(*wind_rows.shape), shaped(rows, merged)),
        [all_units],
    )(masks, base_w, base_h, *back)
    return jnp.swapaxes(new_w, 0, 1), new_h, mass


def solution(mesh):
    in_specs = (P(None, "lat", "lon"), P("lat", "lon"), P(None, "lat", "lon"), P())
    out_specs = (P(None, "lat", "lon"), P("lat", "lon"), P(None, "lat", "lon"))
    return jax.shard_map(local, mesh=mesh, in_specs=in_specs, out_specs=out_specs, check_vma=False)
```

```python
import functools
import math

import jax
import jax.numpy as jnp
import numpy as np
from jax import lax
from jax.experimental import pallas as pl
from jax.experimental.pallas import tpu as pltpu
from jax.sharding import PartitionSpec as P

LEVELS = 16
TIME_STEP = 0.05
DIFFUSION = 0.5
LANES = 128
PER_TILE = LANES // LEVELS
EXT_ROWS = 16
LIMIT = 48 * 1024 * 1024
MOST_VMEM = 64 * 1024 * 1024 - 10500 * 1024


class Sizes:
    def __init__(self, rows, merged, n_lat, n_lon):
        self.rows = rows
        self.merged = merged
        self.columns = merged // LEVELS
        self.n_lat = n_lat
        self.n_lon = n_lon
        self.nlat = rows * n_lat
        self.nlon = self.columns * n_lon
        self.ratio = 2.0 * self.nlat / self.nlon
        self.tiles = -(-merged // LANES)
        self.end = (self.tiles - 1) * LANES
        self.tail = merged - self.end
        self.stack = -(-(self.tiles + 1) // 8) * 8
        self.near_only = rows <= self.nlat // 6 < 2 * rows
        self.work = rows - 1 if self.near_only else rows
        self.units = 3 * self.work
        self.share = -(-self.units // n_lon)
        self.size = self.share * self.stack
        assert self.tail <= LANES - 4 * LEVELS and rows + 2 <= EXT_ROWS and n_lat % 2 == 0
        assert n_lon >= 4 and n_lon & (n_lon - 1) == 0

    def span(self, tile):
        return self.tail if tile == self.tiles - 1 else LANES

    def first(self):
        return jnp.where(lax.rem(lax.axis_index("lat"), 2) == 0, 1, 0) if self.near_only else 0

    def at_pole(self, row):
        band = lax.axis_index("lat")
        pole = jnp.where(band == 0, 0, jnp.where(band == self.n_lat - 1, self.rows - 1, -1))
        return row == (pole if self.near_only else -1)

    def turns(self, odd):
        middle, last = list(range(1, self.n_lon - 1)), self.n_lon - 1
        return [0, middle[0], last] + middle[1:] if odd else [0, last] + middle[::-1]

    def partner(self, k):
        odd = lax.rem(lax.axis_index("lat"), 2) == 1
        turn = jnp.where(odd, self.turns(True)[k], self.turns(False)[k])
        return jnp.bitwise_xor(lax.axis_index("lon"), turn)

    def piece(self, k):
        return pl.ds(pl.multiple_of(self.partner(k) * self.size, 8), self.size)


def geometry(sz):
    table = np.zeros((sz.n_lat, 3, EXT_ROWS, LANES), np.float64)

    def face(j):
        return math.sin((j + 1) * math.pi / sz.nlat) if 0 <= j < sz.nlat - 1 else 0.0

    for band in range(sz.n_lat):
        for row in range(sz.rows):
            j = band * sz.rows + row
            centre = (j + 0.5) * math.pi / sz.nlat - math.pi / 2
            table[band, 0, row] = 1.0 / math.cos(centre)
            table[band, 1, row] = math.sin(centre)
            table[band, 2, row] = face(j)
        table[band, 2, EXT_ROWS - 1] = face(band * sz.rows - 1)
    return table.astype(np.float32)


def offsets(sz):
    shift, out_tile = np.divmod(np.arange(PER_TILE * sz.stack), sz.stack)
    sector, in_tile = np.divmod(np.arange(sz.n_lon * sz.stack), sz.stack)
    n = (PER_TILE * (out_tile - 1) + shift)[:, None] - (PER_TILE * in_tile + sz.columns * sector)[None, :]
    n = (n + sz.nlon // 2) % sz.nlon - sz.nlon // 2
    with np.errstate(divide="ignore"):
        inverse = np.where(n == 0, 0.0, 1.0 / (sz.nlon * np.sin(np.pi * n / sz.nlon)))
    return n.astype(np.float32), inverse.astype(np.float32)


def waves(sz):
    column = PER_TILE * np.arange(sz.stack)[:, None] + np.arange(LANES)[None, :] // LEVELS
    angle = 2 * np.pi * column / sz.nlon
    return np.stack([np.cos(angle), np.sin(angle)]).astype(np.float32)


def edges_kernel(sz, h_hbm, w_hbm, q_hbm, near_ref, far_ref, sides_ref, *scratch):
    row_refs, first_refs, last_refs, sems = scratch[:3], scratch[3:6], scratch[6:9], scratch[9]
    rows, last = sz.rows, sz.rows - 1
    even = lax.rem(lax.axis_index("lat"), 2) == 0
    copies = []
    for i, source in enumerate((h_hbm, w_hbm, q_hbm)):
        for k, row in enumerate((0, last)):
            one = source.at[pl.ds(row, 1)] if i == 0 else source.at[row]
            copies.append(pltpu.make_async_copy(one, row_refs[i].at[k], sems.at[i, k]))
        for k, (start, to) in enumerate(((0, first_refs[i]), (sz.end, last_refs[i]))):
            lanes = pl.ds(start, to.shape[-1])
            cut = source.at[:, lanes] if i == 0 else source.at[:, :, lanes]
            copies.append(pltpu.make_async_copy(cut, to, sems.at[i, 2 + k]))
    for copy in copies:
        copy.start()
    for copy in copies:
        copy.wait()
    h_rows, w_rows, q_rows = row_refs
    for t in range(sz.tiles):
        wide = sz.span(t)
        lanes = slice(LANES * t, LANES * t + wide)
        q = [q_rows[k, :, lanes].astype(jnp.float32) for k in range(2)]
        for f in range(5):
            if f == 0:
                first, final = h_rows[0, :, lanes], h_rows[1, :, lanes]
            elif f == 1:
                first, final = w_rows[0, 1:2, lanes], w_rows[1, 1:2, lanes]
            else:
                first, final = q[0][f - 2 : f - 1], q[1][f - 2 : f - 1]
                at = sz.stack * (f - 2) + t
                near_ref[at : at + 1, :wide] = jnp.where(even, final, first)
            at = sz.stack * f + t
            far_ref[at : at + 1, :wide] = jnp.where(even, first, final)
    sides_ref[...] = jnp.zeros(sides_ref.shape, jnp.float32)
    for k, (refs, at) in enumerate(((first_refs, 0), (last_refs, sz.tail - LEVELS))):
        columns = slice(at, at + LEVELS)
        for f in range(5):
            if f == 0:
                value = refs[0][:, columns]
            elif f == 1:
                value = refs[1][:, 0, columns]
            else:
                value = refs[2][:, f - 2, columns].astype(jnp.float32)
            sides_ref[EXT_ROWS * k : EXT_ROWS * k + rows, LEVELS * f : LEVELS * (f + 1)] = value


def add_rows(sz, ext, near_h_ref, near_w_ref, near_q_ref, far_ref):
    band = lax.axis_index("lat")
    even = lax.rem(band, 2) == 0
    over_pole = (band == 0) | (band == sz.n_lat - 1)
    last = sz.rows - 1
    for f in range(2 if near_q_ref is None else 5):
        flip = jnp.where(over_pole, -1.0, 1.0) if f == 1 else 1.0
        for t in range(sz.tiles):
            lanes = slice(LANES * t, LANES * t + sz.span(t))
            if f == 0:
                near = jnp.where(even, near_h_ref[0:1, lanes], near_h_ref[last : sz.rows, lanes])
            elif f == 1:
                near = jnp.where(even, near_w_ref[0, 1:2, lanes], near_w_ref[last, 1:2, lanes])
            else:
                at = sz.stack * (f - 2) + t
                near = near_q_ref[at : at + 1, : sz.span(t)]
            at = sz.stack * f + t
            far = jnp.zeros_like(near) if far_ref is None else far_ref[at : at + 1, : sz.span(t)] * flip
            ext[f, sz.rows : sz.rows + 1, lanes] = jnp.where(even, near, far)
            ext[f, EXT_ROWS - 1 : EXT_ROWS, lanes] = jnp.where(even, far, near)


class Tiles:
    def __init__(self, sz):
        self.sz = sz
        self.lane = lax.broadcasted_iota(jnp.int32, (EXT_ROWS, LANES), 1)
        self.turned = {}

    def turn(self, name, t, value, step):
        key = (name, t % self.sz.tiles, step)
        if key not in self.turned:
            self.turned[key] = pltpu.roll(value(t % self.sz.tiles), step % LANES, 1)
        return self.turned[key]

    def east(self, name, t, value):
        here = self.turn(name, t, value, -LEVELS)
        return jnp.where(self.lane < LANES - LEVELS, here, self.turn(name, t + 1, value, -LEVELS))

    def west(self, name, t, value):
        here = self.turn(name, t, value, LEVELS)
        return jnp.where(self.lane >= LEVELS, here, self.turn(name, t - 1, value, LEVELS))


def north(value):
    return pltpu.roll(value, EXT_ROWS - 1, 0)


def south(value):
    return pltpu.roll(value, 1, 0)


def polar_kernel(sz, h_ref, w_ref, near_h_ref, near_w_ref, sides_ref, geo_ref, wave_ref, far_ref, near_q_ref, *refs):
    out_refs, (far_out, near_out, tend_ref, pole_ref, ext) = refs[:-5], refs[-5:]
    far_out[...] = far_ref[...]
    near_out[...] = near_q_ref[...]
    if sz.near_only:
        far_ref = None
    band = lax.axis_index("lat")
    ring = Tiles(sz)
    lane = ring.lane
    tiles, stack, rows, work = sz.tiles, sz.stack, sz.rows, sz.work
    even = lax.rem(band, 2) == 0
    for f, value in enumerate((h_ref[...], w_ref[:, 1, :], w_ref[:, 0, :])):
        ext[f, :rows, sz.end :] = jnp.zeros((rows, LANES), jnp.float32)
        ext[f, :rows, : sz.merged] = value
    add_rows(sz, ext, near_h_ref, near_w_ref, None, far_ref)
    inv_cos, sin_centre, cos_face = geo_ref[band, 0], geo_ref[band, 1], geo_ref[band, 2]
    ratio = sz.ratio

    def tile(f, t):
        return ext[f, :, LANES * t : LANES * (t + 1)]

    kept = {}

    def zonal(t):
        if t not in kept:
            thick_e = ring.east("h", t, functools.partial(tile, 0))
            wind_e = ring.east("u", t, functools.partial(tile, 2))
            flux = 0.25 * (tile(2, t) + wind_e) * (tile(0, t) + thick_e) * inv_cos
            if t == tiles - 1:
                flux = jnp.where(lane < sz.tail - LEVELS, flux, 0.0)
            kept[t] = (flux, thick_e)
        return kept[t]

    for t in range(tiles):
        flux, thick_e = zonal(t)
        thick, wind_v, wind_u = tile(0, t), tile(1, t), tile(2, t)
        flux_w = ring.west("f", t, lambda s: zonal(s)[0])
        thick_w = ring.west("hw", t, functools.partial(tile, 0))
        thick_n = north(thick)
        flux_n = (0.25 * ratio) * (wind_v + north(wind_v)) * (thick + thick_n) * cos_face
        thick_tend = -((flux - flux_w) + (flux_n - south(flux_n)) * inv_cos)
        wind_u_tend = sin_centre * wind_v - (thick_e - thick_w) * (0.5 * inv_cos)
        wind_v_tend = -sin_centre * wind_u - (0.5 * ratio) * (thick_n - south(thick))
        spare = 0.0
        if t == tiles - 1:
            last = sz.tail - LEVELS
            columns = [(tile(0, 0), 0), (thick, last), (tile(2, 0), 0), (wind_u, last)]
            for k, (source, at) in reversed(list(enumerate(columns))):
                to = sz.tail + LEVELS * k
                spare = jnp.where(lane < to + LEVELS, pltpu.roll(source, (to - at) % LANES, 1), spare)
        for f, tend in enumerate((thick_tend, wind_u_tend, wind_v_tend, thick)):
            if sz.near_only:
                alone = jnp.where(band < sz.n_lat // 2, tend[:1], tend[rows - 1 : rows])
                if t == tiles - 1:
                    alone = jnp.where(lane[:1] < sz.tail, alone, 0.0)
                pole_ref[stack * f + t : stack * f + t + 1] = alone
            if f == 3:
                continue
            if t == tiles - 1:
                tend = jnp.where(lane < sz.tail, tend, spare)
            if sz.near_only:
                tend = jnp.where(even, north(tend), tend)
            tend_ref[pl.ds(stack * work * f + t, work, stride=stack), :] = tend[:work]
    for f in range(3):
        for t in range(tiles, stack):
            tend_ref[pl.ds(stack * work * f + t, work, stride=stack), :] = jnp.zeros((work, LANES), jnp.float32)
    used, sent = stack * sz.units, sz.n_lon * sz.size
    if used < sent:
        tend_ref[used:sent, :] = jnp.zeros((sent - used, LANES), jnp.float32)
    sides = [sides_ref[:EXT_ROWS], sides_ref[EXT_ROWS:]]
    if sz.near_only:
        sums = pole_sums(sz, pole_ref, wave_ref, spare, band)
        row = lax.broadcasted_iota(jnp.int32, (EXT_ROWS, LANES), 0)
        for k, total in enumerate(sums):
            sides = [jnp.where(row == rows + k, total, side) for side in sides]
    here = lax.axis_index("lon")
    for k, out_ref in enumerate(out_refs):
        out_ref[: sz.size] = tend_ref[sz.piece(k), :]
        eastward = sz.partner(k) == lax.rem(here + 1, sz.n_lon)
        out_ref[sz.size :] = jnp.where(eastward, sides[1], sides[0])


def pole_sums(sz, pole_ref, wave_ref, spare, band):
    stack, rows = sz.stack, sz.rows
    lane = lax.broadcasted_iota(jnp.int32, (1, LANES), 1)
    sides = jnp.where(band < sz.n_lat // 2, spare[:1], spare[rows - 1 : rows])
    found = [jnp.zeros((1, LANES), jnp.float32), pltpu.roll(sides, (LANES // 2 - sz.tail) % LANES, 1)]
    for f in range(4):
        if sz.tiles < stack:
            pole_ref[stack * f + sz.tiles : stack * (f + 1)] = jnp.zeros((stack - sz.tiles, LANES), jnp.float32)
        values = pole_ref[stack * f : stack * (f + 1)]
        for k, terms in enumerate((values, values * wave_ref[0], values * wave_ref[1])):
            total = jnp.sum(terms, axis=0, keepdims=True)
            for step in (64, 32, 16):
                total = total + pltpu.roll(total, step, 1)
            row, place = divmod(3 * f + k, PER_TILE)
            inside = (lane >= LEVELS * place) & (lane < LEVELS * (place + 1))
            found[row] = jnp.where(inside, total, found[row])
    return found


def pole_waves(sz, rows_in, inv_cos, sign):
    n_lon = sz.n_lon
    lane = lax.broadcasted_iota(jnp.int32, (1, LANES), 1)

    def value(s, place):
        row, at = divmod(place, PER_TILE)
        return pltpu.roll(rows_in[s % n_lon, row : row + 1], (-LEVELS * at) % LANES, 1)

    theta = 2 * math.pi / sz.nlon
    ends = (1.0, math.cos(theta * (sz.columns - 1)), math.sin(theta * (sz.columns - 1)))
    sums = [[[value(s, 3 * f + k) for k in range(3)] for f in range(4)] for s in range(n_lon)]
    for s in range(n_lon):
        thick_w, thick_e = value(s, 13), value(s + 1, 12)
        flux = 0.25 * (value(s, 15) + value(s + 1, 14)) * (thick_w + thick_e) * inv_cos
        slope = 0.5 * inv_cos
        after = (s + 1) % n_lon
        for f, (west_of, east_of) in enumerate(((flux, flux), (slope * thick_e, slope * thick_w))):
            for k in range(3):
                sums[s][f][k] = sums[s][f][k] - west_of * ends[k]
            for k in range(2):
                sums[after][f][k] = sums[after][f][k] + east_of
    result = []
    for f in range(3):
        waves_of = [0.0, 0.0, 0.0]
        for s in range(n_lon):
            level, cosine, sine = sums[s][f]
            if f == 2:
                level = level + (0.5 * sz.ratio) * sign * sums[s][3][0]
                cosine = cosine - (0.5 * sz.ratio) * sign * sums[s][3][1]
                sine = sine - (0.5 * sz.ratio) * sign * sums[s][3][2]
            c, d = math.cos(2 * math.pi * s / n_lon), math.sin(2 * math.pi * s / n_lon)
            waves_of[0] = waves_of[0] + level
            waves_of[1] = waves_of[1] + (c * cosine - d * sine)
            waves_of[2] = waves_of[2] + (d * cosine + c * sine)
        spread = []
        for k, total in enumerate(waves_of):
            total = jnp.where(lane < LEVELS, total * ((1.0 if k == 0 else 2.0) / sz.nlon), 0.0)
            for step in (16, 32, 64):
                total = total + pltpu.roll(total, step, 1)
            spread.append(total)
        result.append(spread)
    return result


def rest_kernel(sz, masks_ref, h_ref, w_ref, q_ref, near_h_ref, near_w_ref, near_q_ref, far_ref, geo_ref, wave_ref, after_ref, *refs):
    met_refs, (new_w_ref, new_h_ref, mass_ref, ext, pole_in) = refs[: sz.n_lon], refs[sz.n_lon :]
    band = lax.axis_index("lat")
    ring = Tiles(sz)
    lane = ring.lane
    tiles, rows = sz.tiles, sz.rows
    for f in range(6):
        if f < 2 or f == 5:
            value = (h_ref[...], w_ref[:, 1, :], w_ref[:, 0, :])[min(f, 2)]
        else:
            value = q_ref[f - 2].astype(jnp.float32)
        ext[f, :rows, : sz.merged] = value
    add_rows(sz, ext, near_h_ref, near_w_ref, near_q_ref, far_ref)
    lane9 = lane[:rows]
    here = lax.axis_index("lon")
    from_e = from_w = met_refs[0][sz.size :]
    for k, met_ref in enumerate(met_refs):
        eastward = lax.rem(sz.partner(k) - here + sz.n_lon, sz.n_lon)
        pole_in[eastward] = met_ref[sz.size + 8 :]
        from_e = jnp.where(sz.partner(k) == lax.rem(here + 1, sz.n_lon), met_ref[sz.size :], from_e)
        from_w = jnp.where(sz.partner(k) == lax.rem(here + sz.n_lon - 1, sz.n_lon), met_ref[sz.size :], from_w)
    for place, f in enumerate((0, 5, 2, 3, 4)):
        after = pltpu.roll(from_e, (sz.tail - LEVELS * place) % LANES, 1)[:rows]
        before = pltpu.roll(from_w, (LANES - LEVELS - LEVELS * place) % LANES, 1)[:rows]
        own = ext[f, :rows, sz.end :]
        edge = jnp.where(lane9 < LANES - LEVELS, after, before)
        ext[f, :rows, sz.end :] = jnp.where(lane9 < sz.tail, own, edge)
    inv_cos, sin_centre, cos_face = geo_ref[band, 0], geo_ref[band, 1], geo_ref[band, 2]
    ratio = sz.ratio

    plain, alone = masks_ref[0], masks_ref[1]
    if sz.near_only:
        band = lax.axis_index("lat")
        low = band < sz.n_lat // 2
        pole_cos = jnp.where(low, inv_cos[:1], inv_cos[rows - 1 : rows])
        kept_waves = pole_waves(sz, pole_in.at[:, rows - 8 :], pole_cos, jnp.where(low, 1.0, -1.0))

    def stepped(f, t, value, tend):
        value = value + plain * tend
        if sz.near_only:
            level, cosine, sine = kept_waves[f]
            wave = level + cosine * wave_ref[0, t : t + 1] + sine * wave_ref[1, t : t + 1]
            value = value + alone * wave
        return value

    def tile(f, t):
        return ext[f, :, LANES * t : LANES * (t + 1)]

    kept = {}

    def zonal(t):
        if t not in kept:
            thick_e = ring.east("h", t, functools.partial(tile, 0))
            wind_e = ring.east("u", t, functools.partial(tile, 5))
            flux = 0.25 * (tile(5, t) + wind_e) * (tile(0, t) + thick_e) * inv_cos
            parts = []
            for k in range(3):
                q = tile(2 + k, t)
                q_e = ring.east(k, t, functools.partial(tile, 2 + k))
                parts.append(DIFFUSION * (q_e - q) - flux * (0.5 * (q + q_e)))
            kept[t] = (flux, thick_e, parts)
        return kept[t]

    for t in range(tiles):
        span = sz.span(t)
        lanes = slice(LANES * t, LANES * t + span)
        flux, thick_e, parts = zonal(t)
        thick, wind_u, wind_v = tile(0, t), tile(5, t), tile(1, t)
        flux_w = ring.west("f", t, lambda s: zonal(s)[0])
        thick_w = ring.west("hw", t, functools.partial(tile, 0))
        thick_n = north(thick)
        flux_n = (0.25 * ratio) * (wind_v + north(wind_v)) * (thick + thick_n) * cos_face
        thick_tend = -((flux - flux_w) + (flux_n - south(flux_n)) * inv_cos)
        wind_u_tend = sin_centre * wind_v - (thick_e - thick_w) * (0.5 * inv_cos)
        wind_v_tend = -sin_centre * wind_u - (0.5 * ratio) * (thick_n - south(thick))
        new_h_ref[:, lanes] = stepped(0, t, thick, thick_tend)[:rows, :span]
        new_w_ref[0, :, lanes] = stepped(1, t, wind_u, wind_u_tend)[:rows, :span]
        new_w_ref[1, :, lanes] = stepped(2, t, wind_v, wind_v_tend)[:rows, :span]
        for k in range(3):
            q = tile(2 + k, t)
            q_n = north(q)
            zonal_part = parts[k] - ring.west(("p", k), t, lambda s: zonal(s)[2][k])
            lap = q_n + south(q) - 2.0 * q
            over = flux_n * (0.5 * (q + q_n))
            merid_part = DIFFUSION * lap - (over - south(over)) * inv_cos
            mass = thick * q + TIME_STEP * (zonal_part + merid_part)
            mass_ref[k, :, lanes] = mass[:rows, :span].astype(jnp.bfloat16)


def sin_pi(y):
    y = jnp.where(y > 0.5, 1.0 - y, jnp.where(y < -0.5, -1.0 - y, y))
    s = y * y
    series = [(-1) ** i * math.pi ** (2 * i + 1) / math.factorial(2 * i + 1) for i in range(7)]
    total = series[-1]
    for factor in reversed(series[:-1]):
        total = total * s + factor
    return total * y


def share_of(sz, i):
    unit = lax.axis_index("lon") * sz.share + i
    return unit // sz.work, sz.first() + lax.rem(unit, sz.work)


def weights_kernel(sz, cut_ref, n_ref, inverse_ref, after_ref, weights_ref, masks_ref):
    band = lax.axis_index("lat")
    row = lax.broadcasted_iota(jnp.int32, (EXT_ROWS, LANES), 0)
    cuts = jnp.full((EXT_ROWS, LANES), sz.nlon // 2, jnp.int32)
    for j in range(sz.rows):
        cuts = jnp.where(row == j, cut_ref[band * sz.rows + j], cuts)
    plain, alone = cuts >= sz.nlon // 2, sz.at_pole(row)
    masks_ref[0] = jnp.where(plain, TIME_STEP, 0.0)
    masks_ref[1] = jnp.where(alone, TIME_STEP, 0.0)
    masks_ref[2] = jnp.where(plain | alone, 0.0, TIME_STEP)
    size = PER_TILE * sz.stack
    for i in range(sz.share):
        width = (2 * cut_ref[band * sz.rows + share_of(sz, i)[1]] + 1).astype(jnp.float32)
        n = n_ref[...]
        turns = n * width
        turns = turns - jnp.round(turns * (0.5 / sz.nlon)) * (2.0 * sz.nlon)
        weights = sin_pi(turns * (1.0 / sz.nlon)) * inverse_ref[...]
        weights = jnp.where(n == 0.0, width * (1.0 / sz.nlon), weights)
        weights_ref[size * i : size * (i + 1)] = weights.astype(jnp.bfloat16)


def pass_kernel(sz, piece_ref, after_ref, also_after_ref, out_ref):
    out_ref[...] = piece_ref[...]


def filter_kernel(sz, weights_ref, geo_ref, *refs):
    n_lon, stack, share = sz.n_lon, sz.stack, sz.share
    in_refs, out_refs, (gathered, results) = refs[:n_lon], refs[n_lon : 2 * n_lon], refs[2 * n_lon :]
    for k, in_ref in enumerate(in_refs):
        gathered[sz.partner(k), : sz.size] = in_ref[: sz.size]

    band = lax.axis_index("lat")
    lane = lax.broadcasted_iota(jnp.int32, (share, LANES), 1)
    place = lax.broadcasted_iota(jnp.int32, (share, LANES), 0)
    by_flux = by_thick = jnp.zeros((share, LANES), jnp.float32)
    for i in range(share):
        field, row = share_of(sz, i)
        inv_cos = geo_ref[band, 0, pl.ds(row, 1), :]
        by_flux = jnp.where((place == i) & (field == 0), inv_cos, by_flux)
        by_thick = jnp.where((place == i) & (field == 1), 0.5 * inv_cos, by_thick)
    sides = [gathered[s, pl.ds(sz.tiles - 1, share, stride=stack), :] for s in range(n_lon)]

    def column(s, k):
        return pltpu.roll(sides[s % n_lon], (-sz.tail - LEVELS * k) % LANES, 1)

    for s in range(n_lon):
        thick_w, thick_e = column(s, 1), column(s + 1, 0)
        flux = 0.25 * (column(s, 3) + column(s + 1, 2)) * (thick_w + thick_e) * by_flux
        west_of, east_of = flux + by_thick * thick_e, flux + by_thick * thick_w
        at = pl.ds(sz.tiles - 1, share, stride=stack)
        own = gathered[s, at, :]
        own = own - jnp.where(lane >= sz.tail - LEVELS, pltpu.roll(west_of, sz.tail - LEVELS, 1), 0.0)
        gathered[s, at, :] = jnp.where(lane < sz.tail, own, 0.0)
        at = pl.ds(0, share, stride=stack)
        after = (s + 1) % n_lon
        gathered[after, at, :] = gathered[after, at, :] + jnp.where(lane < LEVELS, east_of, 0.0)

    wide = lax.broadcasted_iota(jnp.int32, (stack, LANES), 1)
    rows = PER_TILE * stack
    for i in range(share):
        here = slice(stack * i, stack * (i + 1))
        pieces = [gathered[s, here].astype(jnp.bfloat16) for s in range(n_lon)]
        circle = jnp.concatenate([jnp.concatenate(pieces[s:] + pieces[:s], axis=0) for s in range(n_lon)], axis=1)
        spread = jnp.dot(weights_ref[rows * i : rows * (i + 1)], circle, preferred_element_type=jnp.float32)
        for s in range(n_lon):
            same = spread[:stack, LANES * s : LANES * (s + 1)]
            carried = None
            for e in range(1, PER_TILE):
                part = spread[stack * e : stack * (e + 1), LANES * s : LANES * (s + 1)]
                part = pltpu.roll(part, LEVELS * e, 1)
                inside = wide >= LEVELS * e
                same = same + jnp.where(inside, part, 0.0)
                over = jnp.where(inside, 0.0, part)
                carried = over if carried is None else carried + over
            results[s, here] = pltpu.roll(same, stack - 1, 0) + carried
    for k, out_ref in enumerate(out_refs):
        out_ref[...] = results[sz.partner(k), : sz.size]


def finish_kernel(sz, masks_ref, base_w_ref, base_h_ref, *refs):
    back_refs, (new_w_ref, new_h_ref, back_ref) = refs[: sz.n_lon], refs[sz.n_lon :]
    rows, work = sz.rows, sz.work
    for k, ref in enumerate(back_refs):
        back_ref[sz.piece(k), :] = ref[...]
    scale = masks_ref[2]
    even = lax.rem(lax.axis_index("lat"), 2) == 0
    for f in range(3):
        for t in range(sz.tiles):
            span = sz.span(t)
            lanes = slice(LANES * t, LANES * t + span)
            tend = back_ref[pl.ds(sz.stack * work * f + t, work, stride=sz.stack), :]
            if sz.near_only:
                tend = jnp.concatenate([tend, jnp.zeros((EXT_ROWS - work, LANES), jnp.float32)], axis=0)
                tend = jnp.where(even, south(tend), tend)
            change = (scale[:rows] * tend[:rows])[:, :span]
            if f == 0:
                new_h_ref[:, lanes] = base_h_ref[:, lanes] + change
            else:
                new_w_ref[:, f - 1, lanes] = base_w_ref[f - 1, :, lanes] + change


def local(winds, thickness, tracers, cutoff):
    n_lat = lax.axis_size("lat")
    n_lon = lax.axis_size("lon")
    rows, merged = thickness.shape
    sz = Sizes(rows, merged, n_lat, n_lon)
    f32 = jnp.float32
    vmem = pl.BlockSpec(memory_space=pltpu.VMEM)
    smem = pl.BlockSpec(memory_space=pltpu.SMEM)
    hbm = pl.BlockSpec(memory_space=pltpu.HBM)
    anywhere = pl.BlockSpec(memory_space=pl.ANY)

    def shaped(*shape):
        return jax.ShapeDtypeStruct(shape, f32)

    def call(kernel, name, in_specs, out_shape, scratch=(), limit=LIMIT):
        return pl.pallas_call(
            functools.partial(kernel, sz),
            out_shape=out_shape,
            in_specs=in_specs,
            out_specs=jax.tree.map(lambda _: vmem, out_shape),
            scratch_shapes=list(scratch),
            compiler_params=pltpu.CompilerParams(vmem_limit_bytes=limit),
            name=name,
        )

    geo = jnp.asarray(geometry(sz))
    wave = jnp.asarray(waves(sz))
    n, inverse = (jnp.asarray(table) for table in offsets(sz))

    wind_rows = jnp.swapaxes(winds, 0, 1)
    tracer_rows = jnp.swapaxes(tracers, 0, 1)
    far_row, near_row = shaped(5 * sz.stack, LANES), shaped(3 * sz.stack, LANES)
    kept = [((1,), f32), ((2,), f32), ((3,), jnp.bfloat16)]
    near_q, far_rows, sides = call(
        edges_kernel,
        "edges",
        [hbm] * 3,
        (near_row, far_row, shaped(2 * EXT_ROWS, LANES)),
        [pltpu.VMEM((2,) + count + (merged,), dtype) for count, dtype in kept]
        + [
            pltpu.VMEM((rows,) + (count if count != (1,) else ()) + (lanes,), dtype)
            for lanes in (LANES, sz.tail)
            for count, dtype in kept
        ]
        + [pltpu.SemaphoreType.DMA((3, 4))],
        limit=MOST_VMEM,
    )(thickness, wind_rows, tracer_rows)

    near = [(band * n_lon + i, (band ^ 1) * n_lon + i) for band in range(n_lat) for i in range(n_lon)]
    far = []
    for band in range(n_lat):
        other = band - 1 if band % 2 == 0 else band + 1
        for i in range(n_lon):
            if 0 <= other < n_lat:
                far.append((band * n_lon + i, other * n_lon + i))
            else:
                far.append((band * n_lon + i, band * n_lon + (i + n_lon // 2) % n_lon))
    near_h = lax.ppermute(thickness, ("lat", "lon"), near)
    near_w = lax.ppermute(wind_rows, ("lat", "lon"), near)
    if not sz.near_only:
        far_rows = lax.ppermute(far_rows, ("lat", "lon"), far)

    order = [sz.turns(False), sz.turns(True)]

    def meetings(shares):
        got = [shares[0]]
        for k in range(1, n_lon):
            sectors = [(band, i, i ^ order[band % 2][k]) for band in range(n_lat) for i in range(n_lon)]
            got.append(lax.ppermute(shares[k], ("lat", "lon"), [(b * n_lon + i, b * n_lon + j) for b, i, j in sectors]))
        return got

    all_pieces = pltpu.VMEM((n_lon, sz.size + 8 * sz.stack, LANES), f32)
    all_units = pltpu.VMEM((n_lon * sz.size + 8 * sz.stack, LANES), f32)
    *tends, far_rows, near_q = call(
        polar_kernel,
        "polar",
        [vmem] * 9,
        [shaped(sz.size + EXT_ROWS, LANES)] * n_lon + [far_row, near_row],
        [
            all_units,
            pltpu.VMEM((4 * sz.stack, LANES), f32),
            pltpu.VMEM((3, EXT_ROWS, sz.tiles * LANES), f32),
        ],
    )(thickness, wind_rows, near_h, near_w, sides, geo, wave, far_rows, near_q)
    met = meetings(tends)
    near_q = lax.ppermute(near_q, ("lat", "lon"), near)
    from_far = lax.ppermute(far_rows, ("lat", "lon"), far) if sz.near_only else far_rows
    weights, masks = call(
        weights_kernel,
        "weights",
        [smem, vmem, vmem, anywhere],
        (
            jax.ShapeDtypeStruct((sz.share * PER_TILE * sz.stack, n_lon * sz.stack), jnp.bfloat16),
            shaped(3, EXT_ROWS, LANES),
        ),
    )(cutoff, n, inverse, tends[0])
    worked = call(
        filter_kernel,
        "filter",
        [vmem] * 2 + [vmem] * n_lon,
        [shaped(sz.size, LANES)] * n_lon,
        [all_pieces, all_pieces],
    )(weights, geo, *met)
    held = call(pass_kernel, "pass", [vmem] + [anywhere] * 2, shaped(sz.size, LANES))(worked[-1], from_far, near_q)
    worked = [*worked[:-1], held]
    back = meetings(worked)

    base_w, base_h, mass = call(
        rest_kernel,
        "rest",
        [vmem] * 10 + [anywhere] + [vmem] * n_lon,
        (shaped(2, rows, merged), shaped(rows, merged), jax.ShapeDtypeStruct(tracers.shape, jnp.bfloat16)),
        [pltpu.VMEM((6, EXT_ROWS, sz.tiles * LANES), f32), pltpu.VMEM((n_lon, 8, LANES), f32)],
    )(masks, thickness, wind_rows, tracers, near_h, near_w, near_q, from_far, geo, wave, worked[0], *met)

    new_w, new_h = call(
        finish_kernel,
        "finish",
        [vmem] * (3 + n_lon),
        (shaped(*wind_rows.shape), shaped(rows, merged)),
        [all_units],
    )(masks, base_w, base_h, *back)
    return jnp.swapaxes(new_w, 0, 1), new_h, mass


def solution(mesh):
    in_specs = (P(None, "lat", "lon"), P("lat", "lon"), P(None, "lat", "lon"), P())
    out_specs = (P(None, "lat", "lon"), P("lat", "lon"), P(None, "lat", "lon"))
    return jax.shard_map(local, mesh=mesh, in_specs=in_specs, out_specs=out_specs, check_vma=False)
```

```python
import functools
import math

import jax
import jax.numpy as jnp
import numpy as np
from jax import lax
from jax.experimental import pallas as pl
from jax.experimental.pallas import tpu as pltpu
from jax.sharding import PartitionSpec as P

LEVELS = 16
TIME_STEP = 0.05
DIFFUSION = 0.5
LANES = 128
PER_TILE = LANES // LEVELS
EXT_ROWS = 16
LIMIT = 48 * 1024 * 1024
MOST_VMEM = 64 * 1024 * 1024 - 10500 * 1024


class Sizes:
    def __init__(self, rows, merged, n_lat, n_lon):
        self.rows = rows
        self.merged = merged
        self.columns = merged // LEVELS
        self.n_lat = n_lat
        self.n_lon = n_lon
        self.nlat = rows * n_lat
        self.nlon = self.columns * n_lon
        self.ratio = 2.0 * self.nlat / self.nlon
        self.tiles = -(-merged // LANES)
        self.end = (self.tiles - 1) * LANES
        self.tail = merged - self.end
        self.stack = -(-(self.tiles + 1) // 8) * 8
        self.near_only = rows <= self.nlat // 6 < 2 * rows
        self.work = rows - 1 if self.near_only else rows
        self.units = 3 * self.work
        self.share = -(-self.units // n_lon)
        self.size = self.share * self.stack
        assert self.tail <= LANES - 4 * LEVELS and rows + 2 <= EXT_ROWS and n_lat % 2 == 0
        assert n_lon >= 4 and n_lon & (n_lon - 1) == 0

    def span(self, tile):
        return self.tail if tile == self.tiles - 1 else LANES

    def first(self):
        return jnp.where(lax.rem(lax.axis_index("lat"), 2) == 0, 1, 0) if self.near_only else 0

    def at_pole(self, row):
        band = lax.axis_index("lat")
        pole = jnp.where(band == 0, 0, jnp.where(band == self.n_lat - 1, self.rows - 1, -1))
        return row == (pole if self.near_only else -1)

    def turns(self, odd):
        middle, last = list(range(1, self.n_lon - 1)), self.n_lon - 1
        return [0, middle[-1], last] + middle[-2::-1] if odd else [0, last] + middle[::-1]

    def partner(self, k):
        odd = lax.rem(lax.axis_index("lat"), 2) == 1
        turn = jnp.where(odd, self.turns(True)[k], self.turns(False)[k])
        return jnp.bitwise_xor(lax.axis_index("lon"), turn)

    def piece(self, k):
        return pl.ds(pl.multiple_of(self.partner(k) * self.size, 8), self.size)


def geometry(sz):
    table = np.zeros((sz.n_lat, 3, EXT_ROWS, LANES), np.float64)

    def face(j):
        return math.sin((j + 1) * math.pi / sz.nlat) if 0 <= j < sz.nlat - 1 else 0.0

    for band in range(sz.n_lat):
        for row in range(sz.rows):
            j = band * sz.rows + row
            centre = (j + 0.5) * math.pi / sz.nlat - math.pi / 2
            table[band, 0, row] = 1.0 / math.cos(centre)
            table[band, 1, row] = math.sin(centre)
            table[band, 2, row] = face(j)
        table[band, 2, EXT_ROWS - 1] = face(band * sz.rows - 1)
    return table.astype(np.float32)


def offsets(sz):
    shift, out_tile = np.divmod(np.arange(PER_TILE * sz.stack), sz.stack)
    sector, in_tile = np.divmod(np.arange(sz.n_lon * sz.stack), sz.stack)
    n = (PER_TILE * (out_tile - 1) + shift)[:, None] - (PER_TILE * in_tile + sz.columns * sector)[None, :]
    n = (n + sz.nlon // 2) % sz.nlon - sz.nlon // 2
    with np.errstate(divide="ignore"):
        inverse = np.where(n == 0, 0.0, 1.0 / (sz.nlon * np.sin(np.pi * n / sz.nlon)))
    return n.astype(np.float32), inverse.astype(np.float32)


def waves(sz):
    column = PER_TILE * np.arange(sz.stack)[:, None] + np.arange(LANES)[None, :] // LEVELS
    angle = 2 * np.pi * column / sz.nlon
    return np.stack([np.cos(angle), np.sin(angle)]).astype(np.float32)


def edges_kernel(sz, h_hbm, w_hbm, q_hbm, near_ref, far_ref, sides_ref, *scratch):
    row_refs, first_refs, last_refs, sems = scratch[:3], scratch[3:6], scratch[6:9], scratch[9]
    rows, last = sz.rows, sz.rows - 1
    even = lax.rem(lax.axis_index("lat"), 2) == 0
    copies = []
    for i, source in enumerate((h_hbm, w_hbm, q_hbm)):
        for k, row in enumerate((0, last)):
            one = source.at[pl.ds(row, 1)] if i == 0 else source.at[row]
            copies.append(pltpu.make_async_copy(one, row_refs[i].at[k], sems.at[i, k]))
        for k, (start, to) in enumerate(((0, first_refs[i]), (sz.end, last_refs[i]))):
            lanes = pl.ds(start, to.shape[-1])
            cut = source.at[:, lanes] if i == 0 else source.at[:, :, lanes]
            copies.append(pltpu.make_async_copy(cut, to, sems.at[i, 2 + k]))
    for copy in copies:
        copy.start()
    for copy in copies:
        copy.wait()
    h_rows, w_rows, q_rows = row_refs
    for t in range(sz.tiles):
        wide = sz.span(t)
        lanes = slice(LANES * t, LANES * t + wide)
        q = [q_rows[k, :, lanes].astype(jnp.float32) for k in range(2)]
        for f in range(5):
            if f == 0:
                first, final = h_rows[0, :, lanes], h_rows[1, :, lanes]
            elif f == 1:
                first, final = w_rows[0, 1:2, lanes], w_rows[1, 1:2, lanes]
            else:
                first, final = q[0][f - 2 : f - 1], q[1][f - 2 : f - 1]
                at = sz.stack * (f - 2) + t
                near_ref[at : at + 1, :wide] = jnp.where(even, final, first)
            at = sz.stack * f + t
            far_ref[at : at + 1, :wide] = jnp.where(even, first, final)
    sides_ref[...] = jnp.zeros(sides_ref.shape, jnp.float32)
    for k, (refs, at) in enumerate(((first_refs, 0), (last_refs, sz.tail - LEVELS))):
        columns = slice(at, at + LEVELS)
        for f in range(5):
            if f == 0:
                value = refs[0][:, columns]
            elif f == 1:
                value = refs[1][:, 0, columns]
            else:
                value = refs[2][:, f - 2, columns].astype(jnp.float32)
            sides_ref[EXT_ROWS * k : EXT_ROWS * k + rows, LEVELS * f : LEVELS * (f + 1)] = value


def add_rows(sz, ext, near_h_ref, near_w_ref, near_q_ref, far_ref):
    band = lax.axis_index("lat")
    even = lax.rem(band, 2) == 0
    over_pole = (band == 0) | (band == sz.n_lat - 1)
    last = sz.rows - 1
    for f in range(2 if near_q_ref is None else 5):
        flip = jnp.where(over_pole, -1.0, 1.0) if f == 1 else 1.0
        for t in range(sz.tiles):
            lanes = slice(LANES * t, LANES * t + sz.span(t))
            if f == 0:
                near = jnp.where(even, near_h_ref[0:1, lanes], near_h_ref[last : sz.rows, lanes])
            elif f == 1:
                near = jnp.where(even, near_w_ref[0, 1:2, lanes], near_w_ref[last, 1:2, lanes])
            else:
                at = sz.stack * (f - 2) + t
                near = near_q_ref[at : at + 1, : sz.span(t)]
            at = sz.stack * f + t
            far = jnp.zeros_like(near) if far_ref is None else far_ref[at : at + 1, : sz.span(t)] * flip
            ext[f, sz.rows : sz.rows + 1, lanes] = jnp.where(even, near, far)
            ext[f, EXT_ROWS - 1 : EXT_ROWS, lanes] = jnp.where(even, far, near)


class Tiles:
    def __init__(self, sz):
        self.sz = sz
        self.lane = lax.broadcasted_iota(jnp.int32, (EXT_ROWS, LANES), 1)
        self.turned = {}

    def turn(self, name, t, value, step):
        key = (name, t % self.sz.tiles, step)
        if key not in self.turned:
            self.turned[key] = pltpu.roll(value(t % self.sz.tiles), step % LANES, 1)
        return self.turned[key]

    def east(self, name, t, value):
        here = self.turn(name, t, value, -LEVELS)
        return jnp.where(self.lane < LANES - LEVELS, here, self.turn(name, t + 1, value, -LEVELS))

    def west(self, name, t, value):
        here = self.turn(name, t, value, LEVELS)
        return jnp.where(self.lane >= LEVELS, here, self.turn(name, t - 1, value, LEVELS))


def north(value):
    return pltpu.roll(value, EXT_ROWS - 1, 0)


def south(value):
    return pltpu.roll(value, 1, 0)


def polar_kernel(sz, h_ref, w_ref, near_h_ref, near_w_ref, sides_ref, geo_ref, wave_ref, far_ref, near_q_ref, *refs):
    out_refs, (far_out, near_out, tend_ref, pole_ref, ext) = refs[:-5], refs[-5:]
    far_out[...] = far_ref[...]
    near_out[...] = near_q_ref[...]
    if sz.near_only:
        far_ref = None
    band = lax.axis_index("lat")
    ring = Tiles(sz)
    lane = ring.lane
    tiles, stack, rows, work = sz.tiles, sz.stack, sz.rows, sz.work
    even = lax.rem(band, 2) == 0
    for f, value in enumerate((h_ref[...], w_ref[:, 1, :], w_ref[:, 0, :])):
        ext[f, :rows, sz.end :] = jnp.zeros((rows, LANES), jnp.float32)
        ext[f, :rows, : sz.merged] = value
    add_rows(sz, ext, near_h_ref, near_w_ref, None, far_ref)
    inv_cos, sin_centre, cos_face = geo_ref[band, 0], geo_ref[band, 1], geo_ref[band, 2]
    ratio = sz.ratio

    def tile(f, t):
        return ext[f, :, LANES * t : LANES * (t + 1)]

    kept = {}

    def zonal(t):
        if t not in kept:
            thick_e = ring.east("h", t, functools.partial(tile, 0))
            wind_e = ring.east("u", t, functools.partial(tile, 2))
            flux = 0.25 * (tile(2, t) + wind_e) * (tile(0, t) + thick_e) * inv_cos
            if t == tiles - 1:
                flux = jnp.where(lane < sz.tail - LEVELS, flux, 0.0)
            kept[t] = (flux, thick_e)
        return kept[t]

    for t in range(tiles):
        flux, thick_e = zonal(t)
        thick, wind_v, wind_u = tile(0, t), tile(1, t), tile(2, t)
        flux_w = ring.west("f", t, lambda s: zonal(s)[0])
        thick_w = ring.west("hw", t, functools.partial(tile, 0))
        thick_n = north(thick)
        flux_n = (0.25 * ratio) * (wind_v + north(wind_v)) * (thick + thick_n) * cos_face
        thick_tend = -((flux - flux_w) + (flux_n - south(flux_n)) * inv_cos)
        wind_u_tend = sin_centre * wind_v - (thick_e - thick_w) * (0.5 * inv_cos)
        wind_v_tend = -sin_centre * wind_u - (0.5 * ratio) * (thick_n - south(thick))
        spare = 0.0
        if t == tiles - 1:
            last = sz.tail - LEVELS
            columns = [(tile(0, 0), 0), (thick, last), (tile(2, 0), 0), (wind_u, last)]
            for k, (source, at) in reversed(list(enumerate(columns))):
                to = sz.tail + LEVELS * k
                spare = jnp.where(lane < to + LEVELS, pltpu.roll(source, (to - at) % LANES, 1), spare)
        for f, tend in enumerate((thick_tend, wind_u_tend, wind_v_tend, thick)):
            if sz.near_only:
                alone = jnp.where(band < sz.n_lat // 2, tend[:1], tend[rows - 1 : rows])
                if t == tiles - 1:
                    alone = jnp.where(lane[:1] < sz.tail, alone, 0.0)
                pole_ref[stack * f + t : stack * f + t + 1] = alone
            if f == 3:
                continue
            if t == tiles - 1:
                tend = jnp.where(lane < sz.tail, tend, spare)
            if sz.near_only:
                tend = jnp.where(even, north(tend), tend)
            tend_ref[pl.ds(stack * work * f + t, work, stride=stack), :] = tend[:work]
    for f in range(3):
        for t in range(tiles, stack):
            tend_ref[pl.ds(stack * work * f + t, work, stride=stack), :] = jnp.zeros((work, LANES), jnp.float32)
    used, sent = stack * sz.units, sz.n_lon * sz.size
    if used < sent:
        tend_ref[used:sent, :] = jnp.zeros((sent - used, LANES), jnp.float32)
    sides = [sides_ref[:EXT_ROWS], sides_ref[EXT_ROWS:]]
    if sz.near_only:
        sums = pole_sums(sz, pole_ref, wave_ref, spare, band)
        row = lax.broadcasted_iota(jnp.int32, (EXT_ROWS, LANES), 0)
        for k, total in enumerate(sums):
            sides = [jnp.where(row == rows + k, total, side) for side in sides]
    here = lax.axis_index("lon")
    for k, out_ref in enumerate(out_refs):
        out_ref[: sz.size] = tend_ref[sz.piece(k), :]
        eastward = sz.partner(k) == lax.rem(here + 1, sz.n_lon)
        out_ref[sz.size :] = jnp.where(eastward, sides[1], sides[0])


def pole_sums(sz, pole_ref, wave_ref, spare, band):
    stack, rows = sz.stack, sz.rows
    lane = lax.broadcasted_iota(jnp.int32, (1, LANES), 1)
    sides = jnp.where(band < sz.n_lat // 2, spare[:1], spare[rows - 1 : rows])
    found = [jnp.zeros((1, LANES), jnp.float32), pltpu.roll(sides, (LANES // 2 - sz.tail) % LANES, 1)]
    for f in range(4):
        if sz.tiles < stack:
            pole_ref[stack * f + sz.tiles : stack * (f + 1)] = jnp.zeros((stack - sz.tiles, LANES), jnp.float32)
        values = pole_ref[stack * f : stack * (f + 1)]
        for k, terms in enumerate((values, values * wave_ref[0], values * wave_ref[1])):
            total = jnp.sum(terms, axis=0, keepdims=True)
            for step in (64, 32, 16):
                total = total + pltpu.roll(total, step, 1)
            row, place = divmod(3 * f + k, PER_TILE)
            inside = (lane >= LEVELS * place) & (lane < LEVELS * (place + 1))
            found[row] = jnp.where(inside, total, found[row])
    return found


def pole_waves(sz, rows_in, inv_cos, sign):
    n_lon = sz.n_lon
    lane = lax.broadcasted_iota(jnp.int32, (1, LANES), 1)

    def value(s, place):
        row, at = divmod(place, PER_TILE)
        return pltpu.roll(rows_in[s % n_lon, row : row + 1], (-LEVELS * at) % LANES, 1)

    theta = 2 * math.pi / sz.nlon
    ends = (1.0, math.cos(theta * (sz.columns - 1)), math.sin(theta * (sz.columns - 1)))
    sums = [[[value(s, 3 * f + k) for k in range(3)] for f in range(4)] for s in range(n_lon)]
    for s in range(n_lon):
        thick_w, thick_e = value(s, 13), value(s + 1, 12)
        flux = 0.25 * (value(s, 15) + value(s + 1, 14)) * (thick_w + thick_e) * inv_cos
        slope = 0.5 * inv_cos
        after = (s + 1) % n_lon
        for f, (west_of, east_of) in enumerate(((flux, flux), (slope * thick_e, slope * thick_w))):
            for k in range(3):
                sums[s][f][k] = sums[s][f][k] - west_of * ends[k]
            for k in range(2):
                sums[after][f][k] = sums[after][f][k] + east_of
    result = []
    for f in range(3):
        waves_of = [0.0, 0.0, 0.0]
        for s in range(n_lon):
            level, cosine, sine = sums[s][f]
            if f == 2:
                level = level + (0.5 * sz.ratio) * sign * sums[s][3][0]
                cosine = cosine - (0.5 * sz.ratio) * sign * sums[s][3][1]
                sine = sine - (0.5 * sz.ratio) * sign * sums[s][3][2]
            c, d = math.cos(2 * math.pi * s / n_lon), math.sin(2 * math.pi * s / n_lon)
            waves_of[0] = waves_of[0] + level
            waves_of[1] = waves_of[1] + (c * cosine - d * sine)
            waves_of[2] = waves_of[2] + (d * cosine + c * sine)
        spread = []
        for k, total in enumerate(waves_of):
            total = jnp.where(lane < LEVELS, total * ((1.0 if k == 0 else 2.0) / sz.nlon), 0.0)
            for step in (16, 32, 64):
                total = total + pltpu.roll(total, step, 1)
            spread.append(total)
        result.append(spread)
    return result


def rest_kernel(sz, masks_ref, h_ref, w_ref, q_ref, near_h_ref, near_w_ref, near_q_ref, far_ref, geo_ref, wave_ref, after_ref, *refs):
    met_refs, (new_w_ref, new_h_ref, mass_ref, ext, pole_in) = refs[: sz.n_lon], refs[sz.n_lon :]
    band = lax.axis_index("lat")
    ring = Tiles(sz)
    lane = ring.lane
    tiles, rows = sz.tiles, sz.rows
    for f in range(6):
        if f < 2 or f == 5:
            value = (h_ref[...], w_ref[:, 1, :], w_ref[:, 0, :])[min(f, 2)]
        else:
            value = q_ref[f - 2].astype(jnp.float32)
        ext[f, :rows, : sz.merged] = value
    add_rows(sz, ext, near_h_ref, near_w_ref, near_q_ref, far_ref)
    lane9 = lane[:rows]
    here = lax.axis_index("lon")
    from_e = from_w = met_refs[0][sz.size :]
    for k, met_ref in enumerate(met_refs):
        eastward = lax.rem(sz.partner(k) - here + sz.n_lon, sz.n_lon)
        pole_in[eastward] = met_ref[sz.size + 8 :]
        from_e = jnp.where(sz.partner(k) == lax.rem(here + 1, sz.n_lon), met_ref[sz.size :], from_e)
        from_w = jnp.where(sz.partner(k) == lax.rem(here + sz.n_lon - 1, sz.n_lon), met_ref[sz.size :], from_w)
    for place, f in enumerate((0, 5, 2, 3, 4)):
        after = pltpu.roll(from_e, (sz.tail - LEVELS * place) % LANES, 1)[:rows]
        before = pltpu.roll(from_w, (LANES - LEVELS - LEVELS * place) % LANES, 1)[:rows]
        own = ext[f, :rows, sz.end :]
        edge = jnp.where(lane9 < LANES - LEVELS, after, before)
        ext[f, :rows, sz.end :] = jnp.where(lane9 < sz.tail, own, edge)
    inv_cos, sin_centre, cos_face = geo_ref[band, 0], geo_ref[band, 1], geo_ref[band, 2]
    ratio = sz.ratio

    plain, alone = masks_ref[0], masks_ref[1]
    if sz.near_only:
        band = lax.axis_index("lat")
        low = band < sz.n_lat // 2
        pole_cos = jnp.where(low, inv_cos[:1], inv_cos[rows - 1 : rows])
        kept_waves = pole_waves(sz, pole_in.at[:, rows - 8 :], pole_cos, jnp.where(low, 1.0, -1.0))

    def stepped(f, t, value, tend):
        value = value + plain * tend
        if sz.near_only:
            level, cosine, sine = kept_waves[f]
            wave = level + cosine * wave_ref[0, t : t + 1] + sine * wave_ref[1, t : t + 1]
            value = value + alone * wave
        return value

    def tile(f, t):
        return ext[f, :, LANES * t : LANES * (t + 1)]

    kept = {}

    def zonal(t):
        if t not in kept:
            thick_e = ring.east("h", t, functools.partial(tile, 0))
            wind_e = ring.east("u", t, functools.partial(tile, 5))
            flux = 0.25 * (tile(5, t) + wind_e) * (tile(0, t) + thick_e) * inv_cos
            parts = []
            for k in range(3):
                q = tile(2 + k, t)
                q_e = ring.east(k, t, functools.partial(tile, 2 + k))
                parts.append(DIFFUSION * (q_e - q) - flux * (0.5 * (q + q_e)))
            kept[t] = (flux, thick_e, parts)
        return kept[t]

    for t in range(tiles):
        span = sz.span(t)
        lanes = slice(LANES * t, LANES * t + span)
        flux, thick_e, parts = zonal(t)
        thick, wind_u, wind_v = tile(0, t), tile(5, t), tile(1, t)
        flux_w = ring.west("f", t, lambda s: zonal(s)[0])
        thick_w = ring.west("hw", t, functools.partial(tile, 0))
        thick_n = north(thick)
        flux_n = (0.25 * ratio) * (wind_v + north(wind_v)) * (thick + thick_n) * cos_face
        thick_tend = -((flux - flux_w) + (flux_n - south(flux_n)) * inv_cos)
        wind_u_tend = sin_centre * wind_v - (thick_e - thick_w) * (0.5 * inv_cos)
        wind_v_tend = -sin_centre * wind_u - (0.5 * ratio) * (thick_n - south(thick))
        new_h_ref[:, lanes] = stepped(0, t, thick, thick_tend)[:rows, :span]
        new_w_ref[0, :, lanes] = stepped(1, t, wind_u, wind_u_tend)[:rows, :span]
        new_w_ref[1, :, lanes] = stepped(2, t, wind_v, wind_v_tend)[:rows, :span]
        for k in range(3):
            q = tile(2 + k, t)
            q_n = north(q)
            zonal_part = parts[k] - ring.west(("p", k), t, lambda s: zonal(s)[2][k])
            lap = q_n + south(q) - 2.0 * q
            over = flux_n * (0.5 * (q + q_n))
            merid_part = DIFFUSION * lap - (over - south(over)) * inv_cos
            mass = thick * q + TIME_STEP * (zonal_part + merid_part)
            mass_ref[k, :, lanes] = mass[:rows, :span].astype(jnp.bfloat16)


def sin_pi(y):
    y = jnp.where(y > 0.5, 1.0 - y, jnp.where(y < -0.5, -1.0 - y, y))
    s = y * y
    series = [(-1) ** i * math.pi ** (2 * i + 1) / math.factorial(2 * i + 1) for i in range(7)]
    total = series[-1]
    for factor in reversed(series[:-1]):
        total = total * s + factor
    return total * y


def share_of(sz, i):
    unit = lax.axis_index("lon") * sz.share + i
    return unit // sz.work, sz.first() + lax.rem(unit, sz.work)


def weights_kernel(sz, cut_ref, n_ref, inverse_ref, after_ref, weights_ref, masks_ref):
    band = lax.axis_index("lat")
    row = lax.broadcasted_iota(jnp.int32, (EXT_ROWS, LANES), 0)
    cuts = jnp.full((EXT_ROWS, LANES), sz.nlon // 2, jnp.int32)
    for j in range(sz.rows):
        cuts = jnp.where(row == j, cut_ref[band * sz.rows + j], cuts)
    plain, alone = cuts >= sz.nlon // 2, sz.at_pole(row)
    masks_ref[0] = jnp.where(plain, TIME_STEP, 0.0)
    masks_ref[1] = jnp.where(alone, TIME_STEP, 0.0)
    masks_ref[2] = jnp.where(plain | alone, 0.0, TIME_STEP)
    size = PER_TILE * sz.stack
    for i in range(sz.share):
        width = (2 * cut_ref[band * sz.rows + share_of(sz, i)[1]] + 1).astype(jnp.float32)
        n = n_ref[...]
        turns = n * width
        turns = turns - jnp.round(turns * (0.5 / sz.nlon)) * (2.0 * sz.nlon)
        weights = sin_pi(turns * (1.0 / sz.nlon)) * inverse_ref[...]
        weights = jnp.where(n == 0.0, width * (1.0 / sz.nlon), weights)
        weights_ref[size * i : size * (i + 1)] = weights.astype(jnp.bfloat16)


def pass_kernel(sz, piece_ref, after_ref, also_after_ref, out_ref):
    out_ref[...] = piece_ref[...]


def filter_kernel(sz, weights_ref, geo_ref, *refs):
    n_lon, stack, share = sz.n_lon, sz.stack, sz.share
    in_refs, out_refs, (gathered, results) = refs[:n_lon], refs[n_lon : 2 * n_lon], refs[2 * n_lon :]
    for k, in_ref in enumerate(in_refs):
        gathered[sz.partner(k), : sz.size] = in_ref[: sz.size]

    band = lax.axis_index("lat")
    lane = lax.broadcasted_iota(jnp.int32, (share, LANES), 1)
    place = lax.broadcasted_iota(jnp.int32, (share, LANES), 0)
    by_flux = by_thick = jnp.zeros((share, LANES), jnp.float32)
    for i in range(share):
        field, row = share_of(sz, i)
        inv_cos = geo_ref[band, 0, pl.ds(row, 1), :]
        by_flux = jnp.where((place == i) & (field == 0), inv_cos, by_flux)
        by_thick = jnp.where((place == i) & (field == 1), 0.5 * inv_cos, by_thick)
    sides = [gathered[s, pl.ds(sz.tiles - 1, share, stride=stack), :] for s in range(n_lon)]

    def column(s, k):
        return pltpu.roll(sides[s % n_lon], (-sz.tail - LEVELS * k) % LANES, 1)

    for s in range(n_lon):
        thick_w, thick_e = column(s, 1), column(s + 1, 0)
        flux = 0.25 * (column(s, 3) + column(s + 1, 2)) * (thick_w + thick_e) * by_flux
        west_of, east_of = flux + by_thick * thick_e, flux + by_thick * thick_w
        at = pl.ds(sz.tiles - 1, share, stride=stack)
        own = gathered[s, at, :]
        own = own - jnp.where(lane >= sz.tail - LEVELS, pltpu.roll(west_of, sz.tail - LEVELS, 1), 0.0)
        gathered[s, at, :] = jnp.where(lane < sz.tail, own, 0.0)
        at = pl.ds(0, share, stride=stack)
        after = (s + 1) % n_lon
        gathered[after, at, :] = gathered[after, at, :] + jnp.where(lane < LEVELS, east_of, 0.0)

    wide = lax.broadcasted_iota(jnp.int32, (stack, LANES), 1)
    rows = PER_TILE * stack
    for i in range(share):
        here = slice(stack * i, stack * (i + 1))
        pieces = [gathered[s, here].astype(jnp.bfloat16) for s in range(n_lon)]
        circle = jnp.concatenate([jnp.concatenate(pieces[s:] + pieces[:s], axis=0) for s in range(n_lon)], axis=1)
        spread = jnp.dot(weights_ref[rows * i : rows * (i + 1)], circle, preferred_element_type=jnp.float32)
        for s in range(n_lon):
            same = spread[:stack, LANES * s : LANES * (s + 1)]
            carried = None
            for e in range(1, PER_TILE):
                part = spread[stack * e : stack * (e + 1), LANES * s : LANES * (s + 1)]
                part = pltpu.roll(part, LEVELS * e, 1)
                inside = wide >= LEVELS * e
                same = same + jnp.where(inside, part, 0.0)
                over = jnp.where(inside, 0.0, part)
                carried = over if carried is None else carried + over
            results[s, here] = pltpu.roll(same, stack - 1, 0) + carried
    for k, out_ref in enumerate(out_refs):
        out_ref[...] = results[sz.partner(k), : sz.size]


def finish_kernel(sz, masks_ref, base_w_ref, base_h_ref, *refs):
    back_refs, (new_w_ref, new_h_ref, back_ref) = refs[: sz.n_lon], refs[sz.n_lon :]
    rows, work = sz.rows, sz.work
    for k, ref in enumerate(back_refs):
        back_ref[sz.piece(k), :] = ref[...]
    scale = masks_ref[2]
    even = lax.rem(lax.axis_index("lat"), 2) == 0
    for f in range(3):
        for t in range(sz.tiles):
            span = sz.span(t)
            lanes = slice(LANES * t, LANES * t + span)
            tend = back_ref[pl.ds(sz.stack * work * f + t, work, stride=sz.stack), :]
            if sz.near_only:
                tend = jnp.concatenate([tend, jnp.zeros((EXT_ROWS - work, LANES), jnp.float32)], axis=0)
                tend = jnp.where(even, south(tend), tend)
            change = (scale[:rows] * tend[:rows])[:, :span]
            if f == 0:
                new_h_ref[:, lanes] = base_h_ref[:, lanes] + change
            else:
                new_w_ref[:, f - 1, lanes] = base_w_ref[f - 1, :, lanes] + change


def local(winds, thickness, tracers, cutoff):
    n_lat = lax.axis_size("lat")
    n_lon = lax.axis_size("lon")
    rows, merged = thickness.shape
    sz = Sizes(rows, merged, n_lat, n_lon)
    f32 = jnp.float32
    vmem = pl.BlockSpec(memory_space=pltpu.VMEM)
    smem = pl.BlockSpec(memory_space=pltpu.SMEM)
    hbm = pl.BlockSpec(memory_space=pltpu.HBM)
    anywhere = pl.BlockSpec(memory_space=pl.ANY)

    def shaped(*shape):
        return jax.ShapeDtypeStruct(shape, f32)

    def call(kernel, name, in_specs, out_shape, scratch=(), limit=LIMIT):
        return pl.pallas_call(
            functools.partial(kernel, sz),
            out_shape=out_shape,
            in_specs=in_specs,
            out_specs=jax.tree.map(lambda _: vmem, out_shape),
            scratch_shapes=list(scratch),
            compiler_params=pltpu.CompilerParams(vmem_limit_bytes=limit),
            name=name,
        )

    geo = jnp.asarray(geometry(sz))
    wave = jnp.asarray(waves(sz))
    n, inverse = (jnp.asarray(table) for table in offsets(sz))

    wind_rows = jnp.swapaxes(winds, 0, 1)
    tracer_rows = jnp.swapaxes(tracers, 0, 1)
    far_row, near_row = shaped(5 * sz.stack, LANES), shaped(3 * sz.stack, LANES)
    kept = [((1,), f32), ((2,), f32), ((3,), jnp.bfloat16)]
    near_q, far_rows, sides = call(
        edges_kernel,
        "edges",
        [hbm] * 3,
        (near_row, far_row, shaped(2 * EXT_ROWS, LANES)),
        [pltpu.VMEM((2,) + count + (merged,), dtype) for count, dtype in kept]
        + [
            pltpu.VMEM((rows,) + (count if count != (1,) else ()) + (lanes,), dtype)
            for lanes in (LANES, sz.tail)
            for count, dtype in kept
        ]
        + [pltpu.SemaphoreType.DMA((3, 4))],
        limit=MOST_VMEM,
    )(thickness, wind_rows, tracer_rows)

    near = [(band * n_lon + i, (band ^ 1) * n_lon + i) for band in range(n_lat) for i in range(n_lon)]
    far = []
    for band in range(n_lat):
        other = band - 1 if band % 2 == 0 else band + 1
        for i in range(n_lon):
            if 0 <= other < n_lat:
                far.append((band * n_lon + i, other * n_lon + i))
            else:
                far.append((band * n_lon + i, band * n_lon + (i + n_lon // 2) % n_lon))
    near_h = lax.ppermute(thickness, ("lat", "lon"), near)
    near_w = lax.ppermute(wind_rows, ("lat", "lon"), near)
    if not sz.near_only:
        far_rows = lax.ppermute(far_rows, ("lat", "lon"), far)

    order = [sz.turns(False), sz.turns(True)]

    def meetings(shares):
        got = [shares[0]]
        for k in range(1, n_lon):
            sectors = [(band, i, i ^ order[band % 2][k]) for band in range(n_lat) for i in range(n_lon)]
            got.append(lax.ppermute(shares[k], ("lat", "lon"), [(b * n_lon + i, b * n_lon + j) for b, i, j in sectors]))
        return got

    all_pieces = pltpu.VMEM((n_lon, sz.size + 8 * sz.stack, LANES), f32)
    all_units = pltpu.VMEM((n_lon * sz.size + 8 * sz.stack, LANES), f32)
    *tends, far_rows, near_q = call(
        polar_kernel,
        "polar",
        [vmem] * 9,
        [shaped(sz.size + EXT_ROWS, LANES)] * n_lon + [far_row, near_row],
        [
            all_units,
            pltpu.VMEM((4 * sz.stack, LANES), f32),
            pltpu.VMEM((3, EXT_ROWS, sz.tiles * LANES), f32),
        ],
    )(thickness, wind_rows, near_h, near_w, sides, geo, wave, far_rows, near_q)
    met = meetings(tends)
    near_q = lax.ppermute(near_q, ("lat", "lon"), near)
    from_far = lax.ppermute(far_rows, ("lat", "lon"), far) if sz.near_only else far_rows
    weights, masks = call(
        weights_kernel,
        "weights",
        [smem, vmem, vmem, anywhere],
        (
            jax.ShapeDtypeStruct((sz.share * PER_TILE * sz.stack, n_lon * sz.stack), jnp.bfloat16),
            shaped(3, EXT_ROWS, LANES),
        ),
    )(cutoff, n, inverse, tends[0])
    worked = call(
        filter_kernel,
        "filter",
        [vmem] * 2 + [vmem] * n_lon,
        [shaped(sz.size, LANES)] * n_lon,
        [all_pieces, all_pieces],
    )(weights, geo, *met)
    held = call(pass_kernel, "pass", [vmem] + [anywhere] * 2, shaped(sz.size, LANES))(worked[-1], from_far, near_q)
    worked = [*worked[:-1], held]
    back = meetings(worked)

    base_w, base_h, mass = call(
        rest_kernel,
        "rest",
        [vmem] * 10 + [anywhere] + [vmem] * n_lon,
        (shaped(2, rows, merged), shaped(rows, merged), jax.ShapeDtypeStruct(tracers.shape, jnp.bfloat16)),
        [pltpu.VMEM((6, EXT_ROWS, sz.tiles * LANES), f32), pltpu.VMEM((n_lon, 8, LANES), f32)],
    )(masks, thickness, wind_rows, tracers, near_h, near_w, near_q, from_far, geo, wave, worked[0], *met)

    new_w, new_h = call(
        finish_kernel,
        "finish",
        [vmem] * (3 + n_lon),
        (shaped(*wind_rows.shape), shaped(rows, merged)),
        [all_units],
    )(masks, base_w, base_h, *back)
    return jnp.swapaxes(new_w, 0, 1), new_h, mass


def solution(mesh):
    in_specs = (P(None, "lat", "lon"), P("lat", "lon"), P(None, "lat", "lon"), P())
    out_specs = (P(None, "lat", "lon"), P("lat", "lon"), P(None, "lat", "lon"))
    return jax.shard_map(local, mesh=mesh, in_specs=in_specs, out_specs=out_specs, check_vma=False)
```

```python
import functools
import math

import jax
import jax.numpy as jnp
import numpy as np
from jax import lax
from jax.experimental import pallas as pl
from jax.experimental.pallas import tpu as pltpu
from jax.sharding import PartitionSpec as P

LEVELS = 16
TIME_STEP = 0.05
DIFFUSION = 0.5
LANES = 128
PER_TILE = LANES // LEVELS
EXT_ROWS = 16
LIMIT = 48 * 1024 * 1024
MOST_VMEM = 64 * 1024 * 1024 - 10500 * 1024


class Sizes:
    def __init__(self, rows, merged, n_lat, n_lon):
        self.rows = rows
        self.merged = merged
        self.columns = merged // LEVELS
        self.n_lat = n_lat
        self.n_lon = n_lon
        self.nlat = rows * n_lat
        self.nlon = self.columns * n_lon
        self.ratio = 2.0 * self.nlat / self.nlon
        self.tiles = -(-merged // LANES)
        self.end = (self.tiles - 1) * LANES
        self.tail = merged - self.end
        self.stack = -(-(self.tiles + 1) // 8) * 8
        self.near_only = rows <= self.nlat // 6 < 2 * rows
        self.work = rows - 1 if self.near_only else rows
        self.units = 3 * self.work
        self.share = -(-self.units // n_lon)
        self.size = self.share * self.stack
        assert self.tail <= LANES - 4 * LEVELS and rows + 2 <= EXT_ROWS and n_lat % 2 == 0
        assert n_lon >= 4 and n_lon & (n_lon - 1) == 0

    def span(self, tile):
        return self.tail if tile == self.tiles - 1 else LANES

    def first(self):
        return jnp.where(lax.rem(lax.axis_index("lat"), 2) == 0, 1, 0) if self.near_only else 0

    def at_pole(self, row):
        band = lax.axis_index("lat")
        pole = jnp.where(band == 0, 0, jnp.where(band == self.n_lat - 1, self.rows - 1, -1))
        return row == (pole if self.near_only else -1)

    def turns(self, odd):
        middle, last = list(range(1, self.n_lon - 1)), self.n_lon - 1
        return [0, middle[-1], last] + middle[-2::-1] if odd else [0, last] + middle

    def partner(self, k):
        odd = lax.rem(lax.axis_index("lat"), 2) == 1
        turn = jnp.where(odd, self.turns(True)[k], self.turns(False)[k])
        return jnp.bitwise_xor(lax.axis_index("lon"), turn)

    def piece(self, k):
        return pl.ds(pl.multiple_of(self.partner(k) * self.size, 8), self.size)


def geometry(sz):
    table = np.zeros((sz.n_lat, 3, EXT_ROWS, LANES), np.float64)

    def face(j):
        return math.sin((j + 1) * math.pi / sz.nlat) if 0 <= j < sz.nlat - 1 else 0.0

    for band in range(sz.n_lat):
        for row in range(sz.rows):
            j = band * sz.rows + row
            centre = (j + 0.5) * math.pi / sz.nlat - math.pi / 2
            table[band, 0, row] = 1.0 / math.cos(centre)
            table[band, 1, row] = math.sin(centre)
            table[band, 2, row] = face(j)
        table[band, 2, EXT_ROWS - 1] = face(band * sz.rows - 1)
    return table.astype(np.float32)


def offsets(sz):
    shift, out_tile = np.divmod(np.arange(PER_TILE * sz.stack), sz.stack)
    sector, in_tile = np.divmod(np.arange(sz.n_lon * sz.stack), sz.stack)
    n = (PER_TILE * (out_tile - 1) + shift)[:, None] - (PER_TILE * in_tile + sz.columns * sector)[None, :]
    n = (n + sz.nlon // 2) % sz.nlon - sz.nlon // 2
    with np.errstate(divide="ignore"):
        inverse = np.where(n == 0, 0.0, 1.0 / (sz.nlon * np.sin(np.pi * n / sz.nlon)))
    return n.astype(np.float32), inverse.astype(np.float32)


def waves(sz):
    column = PER_TILE * np.arange(sz.stack)[:, None] + np.arange(LANES)[None, :] // LEVELS
    angle = 2 * np.pi * column / sz.nlon
    return np.stack([np.cos(angle), np.sin(angle)]).astype(np.float32)


def edges_kernel(sz, h_hbm, w_hbm, q_hbm, near_ref, far_ref, sides_ref, *scratch):
    row_refs, first_refs, last_refs, sems = scratch[:3], scratch[3:6], scratch[6:9], scratch[9]
    rows, last = sz.rows, sz.rows - 1
    even = lax.rem(lax.axis_index("lat"), 2) == 0
    copies = []
    for i, source in enumerate((h_hbm, w_hbm, q_hbm)):
        for k, row in enumerate((0, last)):
            one = source.at[pl.ds(row, 1)] if i == 0 else source.at[row]
            copies.append(pltpu.make_async_copy(one, row_refs[i].at[k], sems.at[i, k]))
        for k, (start, to) in enumerate(((0, first_refs[i]), (sz.end, last_refs[i]))):
            lanes = pl.ds(start, to.shape[-1])
            cut = source.at[:, lanes] if i == 0 else source.at[:, :, lanes]
            copies.append(pltpu.make_async_copy(cut, to, sems.at[i, 2 + k]))
    for copy in copies:
        copy.start()
    for copy in copies:
        copy.wait()
    h_rows, w_rows, q_rows = row_refs
    for t in range(sz.tiles):
        wide = sz.span(t)
        lanes = slice(LANES * t, LANES * t + wide)
        q = [q_rows[k, :, lanes].astype(jnp.float32) for k in range(2)]
        for f in range(5):
            if f == 0:
                first, final = h_rows[0, :, lanes], h_rows[1, :, lanes]
            elif f == 1:
                first, final = w_rows[0, 1:2, lanes], w_rows[1, 1:2, lanes]
            else:
                first, final = q[0][f - 2 : f - 1], q[1][f - 2 : f - 1]
                at = sz.stack * (f - 2) + t
                near_ref[at : at + 1, :wide] = jnp.where(even, final, first)
            at = sz.stack * f + t
            far_ref[at : at + 1, :wide] = jnp.where(even, first, final)
    sides_ref[...] = jnp.zeros(sides_ref.shape, jnp.float32)
    for k, (refs, at) in enumerate(((first_refs, 0), (last_refs, sz.tail - LEVELS))):
        columns = slice(at, at + LEVELS)
        for f in range(5):
            if f == 0:
                value = refs[0][:, columns]
            elif f == 1:
                value = refs[1][:, 0, columns]
            else:
                value = refs[2][:, f - 2, columns].astype(jnp.float32)
            sides_ref[EXT_ROWS * k : EXT_ROWS * k + rows, LEVELS * f : LEVELS * (f + 1)] = value


def add_rows(sz, ext, near_h_ref, near_w_ref, near_q_ref, far_ref):
    band = lax.axis_index("lat")
    even = lax.rem(band, 2) == 0
    over_pole = (band == 0) | (band == sz.n_lat - 1)
    last = sz.rows - 1
    for f in range(2 if near_q_ref is None else 5):
        flip = jnp.where(over_pole, -1.0, 1.0) if f == 1 else 1.0
        for t in range(sz.tiles):
            lanes = slice(LANES * t, LANES * t + sz.span(t))
            if f == 0:
                near = jnp.where(even, near_h_ref[0:1, lanes], near_h_ref[last : sz.rows, lanes])
            elif f == 1:
                near = jnp.where(even, near_w_ref[0, 1:2, lanes], near_w_ref[last, 1:2, lanes])
            else:
                at = sz.stack * (f - 2) + t
                near = near_q_ref[at : at + 1, : sz.span(t)]
            at = sz.stack * f + t
            far = jnp.zeros_like(near) if far_ref is None else far_ref[at : at + 1, : sz.span(t)] * flip
            ext[f, sz.rows : sz.rows + 1, lanes] = jnp.where(even, near, far)
            ext[f, EXT_ROWS - 1 : EXT_ROWS, lanes] = jnp.where(even, far, near)


class Tiles:
    def __init__(self, sz):
        self.sz = sz
        self.lane = lax.broadcasted_iota(jnp.int32, (EXT_ROWS, LANES), 1)
        self.turned = {}

    def turn(self, name, t, value, step):
        key = (name, t % self.sz.tiles, step)
        if key not in self.turned:
            self.turned[key] = pltpu.roll(value(t % self.sz.tiles), step % LANES, 1)
        return self.turned[key]

    def east(self, name, t, value):
        here = self.turn(name, t, value, -LEVELS)
        return jnp.where(self.lane < LANES - LEVELS, here, self.turn(name, t + 1, value, -LEVELS))

    def west(self, name, t, value):
        here = self.turn(name, t, value, LEVELS)
        return jnp.where(self.lane >= LEVELS, here, self.turn(name, t - 1, value, LEVELS))


def north(value):
    return pltpu.roll(value, EXT_ROWS - 1, 0)


def south(value):
    return pltpu.roll(value, 1, 0)


def polar_kernel(sz, h_ref, w_ref, near_h_ref, near_w_ref, sides_ref, geo_ref, wave_ref, far_ref, near_q_ref, *refs):
    out_refs, (far_out, near_out, tend_ref, pole_ref, ext) = refs[:-5], refs[-5:]
    far_out[...] = far_ref[...]
    near_out[...] = near_q_ref[...]
    if sz.near_only:
        far_ref = None
    band = lax.axis_index("lat")
    ring = Tiles(sz)
    lane = ring.lane
    tiles, stack, rows, work = sz.tiles, sz.stack, sz.rows, sz.work
    even = lax.rem(band, 2) == 0
    for f, value in enumerate((h_ref[...], w_ref[:, 1, :], w_ref[:, 0, :])):
        ext[f, :rows, sz.end :] = jnp.zeros((rows, LANES), jnp.float32)
        ext[f, :rows, : sz.merged] = value
    add_rows(sz, ext, near_h_ref, near_w_ref, None, far_ref)
    inv_cos, sin_centre, cos_face = geo_ref[band, 0], geo_ref[band, 1], geo_ref[band, 2]
    ratio = sz.ratio

    def tile(f, t):
        return ext[f, :, LANES * t : LANES * (t + 1)]

    kept = {}

    def zonal(t):
        if t not in kept:
            thick_e = ring.east("h", t, functools.partial(tile, 0))
            wind_e = ring.east("u", t, functools.partial(tile, 2))
            flux = 0.25 * (tile(2, t) + wind_e) * (tile(0, t) + thick_e) * inv_cos
            if t == tiles - 1:
                flux = jnp.where(lane < sz.tail - LEVELS, flux, 0.0)
            kept[t] = (flux, thick_e)
        return kept[t]

    for t in range(tiles):
        flux, thick_e = zonal(t)
        thick, wind_v, wind_u = tile(0, t), tile(1, t), tile(2, t)
        flux_w = ring.west("f", t, lambda s: zonal(s)[0])
        thick_w = ring.west("hw", t, functools.partial(tile, 0))
        thick_n = north(thick)
        flux_n = (0.25 * ratio) * (wind_v + north(wind_v)) * (thick + thick_n) * cos_face
        thick_tend = -((flux - flux_w) + (flux_n - south(flux_n)) * inv_cos)
        wind_u_tend = sin_centre * wind_v - (thick_e - thick_w) * (0.5 * inv_cos)
        wind_v_tend = -sin_centre * wind_u - (0.5 * ratio) * (thick_n - south(thick))
        spare = 0.0
        if t == tiles - 1:
            last = sz.tail - LEVELS
            columns = [(tile(0, 0), 0), (thick, last), (tile(2, 0), 0), (wind_u, last)]
            for k, (source, at) in reversed(list(enumerate(columns))):
                to = sz.tail + LEVELS * k
                spare = jnp.where(lane < to + LEVELS, pltpu.roll(source, (to - at) % LANES, 1), spare)
        for f, tend in enumerate((thick_tend, wind_u_tend, wind_v_tend, thick)):
            if sz.near_only:
                alone = jnp.where(band < sz.n_lat // 2, tend[:1], tend[rows - 1 : rows])
                if t == tiles - 1:
                    alone = jnp.where(lane[:1] < sz.tail, alone, 0.0)
                pole_ref[stack * f + t : stack * f + t + 1] = alone
            if f == 3:
                continue
            if t == tiles - 1:
                tend = jnp.where(lane < sz.tail, tend, spare)
            if sz.near_only:
                tend = jnp.where(even, north(tend), tend)
            tend_ref[pl.ds(stack * work * f + t, work, stride=stack), :] = tend[:work]
    for f in range(3):
        for t in range(tiles, stack):
            tend_ref[pl.ds(stack * work * f + t, work, stride=stack), :] = jnp.zeros((work, LANES), jnp.float32)
    used, sent = stack * sz.units, sz.n_lon * sz.size
    if used < sent:
        tend_ref[used:sent, :] = jnp.zeros((sent - used, LANES), jnp.float32)
    sides = [sides_ref[:EXT_ROWS], sides_ref[EXT_ROWS:]]
    if sz.near_only:
        sums = pole_sums(sz, pole_ref, wave_ref, spare, band)
        row = lax.broadcasted_iota(jnp.int32, (EXT_ROWS, LANES), 0)
        for k, total in enumerate(sums):
            sides = [jnp.where(row == rows + k, total, side) for side in sides]
    here = lax.axis_index("lon")
    for k, out_ref in enumerate(out_refs):
        out_ref[: sz.size] = tend_ref[sz.piece(k), :]
        eastward = sz.partner(k) == lax.rem(here + 1, sz.n_lon)
        out_ref[sz.size :] = jnp.where(eastward, sides[1], sides[0])


def pole_sums(sz, pole_ref, wave_ref, spare, band):
    stack, rows = sz.stack, sz.rows
    lane = lax.broadcasted_iota(jnp.int32, (1, LANES), 1)
    sides = jnp.where(band < sz.n_lat // 2, spare[:1], spare[rows - 1 : rows])
    found = [jnp.zeros((1, LANES), jnp.float32), pltpu.roll(sides, (LANES // 2 - sz.tail) % LANES, 1)]
    for f in range(4):
        if sz.tiles < stack:
            pole_ref[stack * f + sz.tiles : stack * (f + 1)] = jnp.zeros((stack - sz.tiles, LANES), jnp.float32)
        values = pole_ref[stack * f : stack * (f + 1)]
        for k, terms in enumerate((values, values * wave_ref[0], values * wave_ref[1])):
            total = jnp.sum(terms, axis=0, keepdims=True)
            for step in (64, 32, 16):
                total = total + pltpu.roll(total, step, 1)
            row, place = divmod(3 * f + k, PER_TILE)
            inside = (lane >= LEVELS * place) & (lane < LEVELS * (place + 1))
            found[row] = jnp.where(inside, total, found[row])
    return found


def pole_waves(sz, rows_in, inv_cos, sign):
    n_lon = sz.n_lon
    lane = lax.broadcasted_iota(jnp.int32, (1, LANES), 1)

    def value(s, place):
        row, at = divmod(place, PER_TILE)
        return pltpu.roll(rows_in[s % n_lon, row : row + 1], (-LEVELS * at) % LANES, 1)

    theta = 2 * math.pi / sz.nlon
    ends = (1.0, math.cos(theta * (sz.columns - 1)), math.sin(theta * (sz.columns - 1)))
    sums = [[[value(s, 3 * f + k) for k in range(3)] for f in range(4)] for s in range(n_lon)]
    for s in range(n_lon):
        thick_w, thick_e = value(s, 13), value(s + 1, 12)
        flux = 0.25 * (value(s, 15) + value(s + 1, 14)) * (thick_w + thick_e) * inv_cos
        slope = 0.5 * inv_cos
        after = (s + 1) % n_lon
        for f, (west_of, east_of) in enumerate(((flux, flux), (slope * thick_e, slope * thick_w))):
            for k in range(3):
                sums[s][f][k] = sums[s][f][k] - west_of * ends[k]
            for k in range(2):
                sums[after][f][k] = sums[after][f][k] + east_of
    result = []
    for f in range(3):
        waves_of = [0.0, 0.0, 0.0]
        for s in range(n_lon):
            level, cosine, sine = sums[s][f]
            if f == 2:
                level = level + (0.5 * sz.ratio) * sign * sums[s][3][0]
                cosine = cosine - (0.5 * sz.ratio) * sign * sums[s][3][1]
                sine = sine - (0.5 * sz.ratio) * sign * sums[s][3][2]
            c, d = math.cos(2 * math.pi * s / n_lon), math.sin(2 * math.pi * s / n_lon)
            waves_of[0] = waves_of[0] + level
            waves_of[1] = waves_of[1] + (c * cosine - d * sine)
            waves_of[2] = waves_of[2] + (d * cosine + c * sine)
        spread = []
        for k, total in enumerate(waves_of):
            total = jnp.where(lane < LEVELS, total * ((1.0 if k == 0 else 2.0) / sz.nlon), 0.0)
            for step in (16, 32, 64):
                total = total + pltpu.roll(total, step, 1)
            spread.append(total)
        result.append(spread)
    return result


def rest_kernel(sz, masks_ref, h_ref, w_ref, q_ref, near_h_ref, near_w_ref, near_q_ref, far_ref, geo_ref, wave_ref, after_ref, *refs):
    met_refs, (new_w_ref, new_h_ref, mass_ref, ext, pole_in) = refs[: sz.n_lon], refs[sz.n_lon :]
    band = lax.axis_index("lat")
    ring = Tiles(sz)
    lane = ring.lane
    tiles, rows = sz.tiles, sz.rows
    for f in range(6):
        if f < 2 or f == 5:
            value = (h_ref[...], w_ref[:, 1, :], w_ref[:, 0, :])[min(f, 2)]
        else:
            value = q_ref[f - 2].astype(jnp.float32)
        ext[f, :rows, : sz.merged] = value
    add_rows(sz, ext, near_h_ref, near_w_ref, near_q_ref, far_ref)
    lane9 = lane[:rows]
    here = lax.axis_index("lon")
    from_e = from_w = met_refs[0][sz.size :]
    for k, met_ref in enumerate(met_refs):
        eastward = lax.rem(sz.partner(k) - here + sz.n_lon, sz.n_lon)
        pole_in[eastward] = met_ref[sz.size + 8 :]
        from_e = jnp.where(sz.partner(k) == lax.rem(here + 1, sz.n_lon), met_ref[sz.size :], from_e)
        from_w = jnp.where(sz.partner(k) == lax.rem(here + sz.n_lon - 1, sz.n_lon), met_ref[sz.size :], from_w)
    for place, f in enumerate((0, 5, 2, 3, 4)):
        after = pltpu.roll(from_e, (sz.tail - LEVELS * place) % LANES, 1)[:rows]
        before = pltpu.roll(from_w, (LANES - LEVELS - LEVELS * place) % LANES, 1)[:rows]
        own = ext[f, :rows, sz.end :]
        edge = jnp.where(lane9 < LANES - LEVELS, after, before)
        ext[f, :rows, sz.end :] = jnp.where(lane9 < sz.tail, own, edge)
    inv_cos, sin_centre, cos_face = geo_ref[band, 0], geo_ref[band, 1], geo_ref[band, 2]
    ratio = sz.ratio

    plain, alone = masks_ref[0], masks_ref[1]
    if sz.near_only:
        band = lax.axis_index("lat")
        low = band < sz.n_lat // 2
        pole_cos = jnp.where(low, inv_cos[:1], inv_cos[rows - 1 : rows])
        kept_waves = pole_waves(sz, pole_in.at[:, rows - 8 :], pole_cos, jnp.where(low, 1.0, -1.0))

    def stepped(f, t, value, tend):
        value = value + plain * tend
        if sz.near_only:
            level, cosine, sine = kept_waves[f]
            wave = level + cosine * wave_ref[0, t : t + 1] + sine * wave_ref[1, t : t + 1]
            value = value + alone * wave
        return value

    def tile(f, t):
        return ext[f, :, LANES * t : LANES * (t + 1)]

    kept = {}

    def zonal(t):
        if t not in kept:
            thick_e = ring.east("h", t, functools.partial(tile, 0))
            wind_e = ring.east("u", t, functools.partial(tile, 5))
            flux = 0.25 * (tile(5, t) + wind_e) * (tile(0, t) + thick_e) * inv_cos
            parts = []
            for k in range(3):
                q = tile(2 + k, t)
                q_e = ring.east(k, t, functools.partial(tile, 2 + k))
                parts.append(DIFFUSION * (q_e - q) - flux * (0.5 * (q + q_e)))
            kept[t] = (flux, thick_e, parts)
        return kept[t]

    for t in range(tiles):
        span = sz.span(t)
        lanes = slice(LANES * t, LANES * t + span)
        flux, thick_e, parts = zonal(t)
        thick, wind_u, wind_v = tile(0, t), tile(5, t), tile(1, t)
        flux_w = ring.west("f", t, lambda s: zonal(s)[0])
        thick_w = ring.west("hw", t, functools.partial(tile, 0))
        thick_n = north(thick)
        flux_n = (0.25 * ratio) * (wind_v + north(wind_v)) * (thick + thick_n) * cos_face
        thick_tend = -((flux - flux_w) + (flux_n - south(flux_n)) * inv_cos)
        wind_u_tend = sin_centre * wind_v - (thick_e - thick_w) * (0.5 * inv_cos)
        wind_v_tend = -sin_centre * wind_u - (0.5 * ratio) * (thick_n - south(thick))
        new_h_ref[:, lanes] = stepped(0, t, thick, thick_tend)[:rows, :span]
        new_w_ref[0, :, lanes] = stepped(1, t, wind_u, wind_u_tend)[:rows, :span]
        new_w_ref[1, :, lanes] = stepped(2, t, wind_v, wind_v_tend)[:rows, :span]
        for k in range(3):
            q = tile(2 + k, t)
            q_n = north(q)
            zonal_part = parts[k] - ring.west(("p", k), t, lambda s: zonal(s)[2][k])
            lap = q_n + south(q) - 2.0 * q
            over = flux_n * (0.5 * (q + q_n))
            merid_part = DIFFUSION * lap - (over - south(over)) * inv_cos
            mass = thick * q + TIME_STEP * (zonal_part + merid_part)
            mass_ref[k, :, lanes] = mass[:rows, :span].astype(jnp.bfloat16)


def sin_pi(y):
    y = jnp.where(y > 0.5, 1.0 - y, jnp.where(y < -0.5, -1.0 - y, y))
    s = y * y
    series = [(-1) ** i * math.pi ** (2 * i + 1) / math.factorial(2 * i + 1) for i in range(7)]
    total = series[-1]
    for factor in reversed(series[:-1]):
        total = total * s + factor
    return total * y


def share_of(sz, i):
    unit = lax.axis_index("lon") * sz.share + i
    return unit // sz.work, sz.first() + lax.rem(unit, sz.work)


def weights_kernel(sz, cut_ref, n_ref, inverse_ref, after_ref, weights_ref, masks_ref):
    band = lax.axis_index("lat")
    row = lax.broadcasted_iota(jnp.int32, (EXT_ROWS, LANES), 0)
    cuts = jnp.full((EXT_ROWS, LANES), sz.nlon // 2, jnp.int32)
    for j in range(sz.rows):
        cuts = jnp.where(row == j, cut_ref[band * sz.rows + j], cuts)
    plain, alone = cuts >= sz.nlon // 2, sz.at_pole(row)
    masks_ref[0] = jnp.where(plain, TIME_STEP, 0.0)
    masks_ref[1] = jnp.where(alone, TIME_STEP, 0.0)
    masks_ref[2] = jnp.where(plain | alone, 0.0, TIME_STEP)
    size = PER_TILE * sz.stack
    for i in range(sz.share):
        width = (2 * cut_ref[band * sz.rows + share_of(sz, i)[1]] + 1).astype(jnp.float32)
        n = n_ref[...]
        turns = n * width
        turns = turns - jnp.round(turns * (0.5 / sz.nlon)) * (2.0 * sz.nlon)
        weights = sin_pi(turns * (1.0 / sz.nlon)) * inverse_ref[...]
        weights = jnp.where(n == 0.0, width * (1.0 / sz.nlon), weights)
        weights_ref[size * i : size * (i + 1)] = weights.astype(jnp.bfloat16)


def pass_kernel(sz, piece_ref, after_ref, also_after_ref, out_ref):
    out_ref[...] = piece_ref[...]


def filter_kernel(sz, weights_ref, geo_ref, *refs):
    n_lon, stack, share = sz.n_lon, sz.stack, sz.share
    in_refs, out_refs, (gathered, results) = refs[:n_lon], refs[n_lon : 2 * n_lon], refs[2 * n_lon :]
    for k, in_ref in enumerate(in_refs):
        gathered[sz.partner(k), : sz.size] = in_ref[: sz.size]

    band = lax.axis_index("lat")
    lane = lax.broadcasted_iota(jnp.int32, (share, LANES), 1)
    place = lax.broadcasted_iota(jnp.int32, (share, LANES), 0)
    by_flux = by_thick = jnp.zeros((share, LANES), jnp.float32)
    for i in range(share):
        field, row = share_of(sz, i)
        inv_cos = geo_ref[band, 0, pl.ds(row, 1), :]
        by_flux = jnp.where((place == i) & (field == 0), inv_cos, by_flux)
        by_thick = jnp.where((place == i) & (field == 1), 0.5 * inv_cos, by_thick)
    sides = [gathered[s, pl.ds(sz.tiles - 1, share, stride=stack), :] for s in range(n_lon)]

    def column(s, k):
        return pltpu.roll(sides[s % n_lon], (-sz.tail - LEVELS * k) % LANES, 1)

    for s in range(n_lon):
        thick_w, thick_e = column(s, 1), column(s + 1, 0)
        flux = 0.25 * (column(s, 3) + column(s + 1, 2)) * (thick_w + thick_e) * by_flux
        west_of, east_of = flux + by_thick * thick_e, flux + by_thick * thick_w
        at = pl.ds(sz.tiles - 1, share, stride=stack)
        own = gathered[s, at, :]
        own = own - jnp.where(lane >= sz.tail - LEVELS, pltpu.roll(west_of, sz.tail - LEVELS, 1), 0.0)
        gathered[s, at, :] = jnp.where(lane < sz.tail, own, 0.0)
        at = pl.ds(0, share, stride=stack)
        after = (s + 1) % n_lon
        gathered[after, at, :] = gathered[after, at, :] + jnp.where(lane < LEVELS, east_of, 0.0)

    wide = lax.broadcasted_iota(jnp.int32, (stack, LANES), 1)
    rows = PER_TILE * stack
    for i in range(share):
        here = slice(stack * i, stack * (i + 1))
        pieces = [gathered[s, here].astype(jnp.bfloat16) for s in range(n_lon)]
        circle = jnp.concatenate([jnp.concatenate(pieces[s:] + pieces[:s], axis=0) for s in range(n_lon)], axis=1)
        spread = jnp.dot(weights_ref[rows * i : rows * (i + 1)], circle, preferred_element_type=jnp.float32)
        for s in range(n_lon):
            same = spread[:stack, LANES * s : LANES * (s + 1)]
            carried = None
            for e in range(1, PER_TILE):
                part = spread[stack * e : stack * (e + 1), LANES * s : LANES * (s + 1)]
                part = pltpu.roll(part, LEVELS * e, 1)
                inside = wide >= LEVELS * e
                same = same + jnp.where(inside, part, 0.0)
                over = jnp.where(inside, 0.0, part)
                carried = over if carried is None else carried + over
            results[s, here] = pltpu.roll(same, stack - 1, 0) + carried
    for k, out_ref in enumerate(out_refs):
        out_ref[...] = results[sz.partner(k), : sz.size]


def finish_kernel(sz, masks_ref, base_w_ref, base_h_ref, *refs):
    back_refs, (new_w_ref, new_h_ref, back_ref) = refs[: sz.n_lon], refs[sz.n_lon :]
    rows, work = sz.rows, sz.work
    for k, ref in enumerate(back_refs):
        back_ref[sz.piece(k), :] = ref[...]
    scale = masks_ref[2]
    even = lax.rem(lax.axis_index("lat"), 2) == 0
    for f in range(3):
        for t in range(sz.tiles):
            span = sz.span(t)
            lanes = slice(LANES * t, LANES * t + span)
            tend = back_ref[pl.ds(sz.stack * work * f + t, work, stride=sz.stack), :]
            if sz.near_only:
                tend = jnp.concatenate([tend, jnp.zeros((EXT_ROWS - work, LANES), jnp.float32)], axis=0)
                tend = jnp.where(even, south(tend), tend)
            change = (scale[:rows] * tend[:rows])[:, :span]
            if f == 0:
                new_h_ref[:, lanes] = base_h_ref[:, lanes] + change
            else:
                new_w_ref[:, f - 1, lanes] = base_w_ref[f - 1, :, lanes] + change


def local(winds, thickness, tracers, cutoff):
    n_lat = lax.axis_size("lat")
    n_lon = lax.axis_size("lon")
    rows, merged = thickness.shape
    sz = Sizes(rows, merged, n_lat, n_lon)
    f32 = jnp.float32
    vmem = pl.BlockSpec(memory_space=pltpu.VMEM)
    smem = pl.BlockSpec(memory_space=pltpu.SMEM)
    hbm = pl.BlockSpec(memory_space=pltpu.HBM)
    anywhere = pl.BlockSpec(memory_space=pl.ANY)

    def shaped(*shape):
        return jax.ShapeDtypeStruct(shape, f32)

    def call(kernel, name, in_specs, out_shape, scratch=(), limit=LIMIT):
        return pl.pallas_call(
            functools.partial(kernel, sz),
            out_shape=out_shape,
            in_specs=in_specs,
            out_specs=jax.tree.map(lambda _: vmem, out_shape),
            scratch_shapes=list(scratch),
            compiler_params=pltpu.CompilerParams(vmem_limit_bytes=limit),
            name=name,
        )

    geo = jnp.asarray(geometry(sz))
    wave = jnp.asarray(waves(sz))
    n, inverse = (jnp.asarray(table) for table in offsets(sz))

    wind_rows = jnp.swapaxes(winds, 0, 1)
    tracer_rows = jnp.swapaxes(tracers, 0, 1)
    far_row, near_row = shaped(5 * sz.stack, LANES), shaped(3 * sz.stack, LANES)
    kept = [((1,), f32), ((2,), f32), ((3,), jnp.bfloat16)]
    near_q, far_rows, sides = call(
        edges_kernel,
        "edges",
        [hbm] * 3,
        (near_row, far_row, shaped(2 * EXT_ROWS, LANES)),
        [pltpu.VMEM((2,) + count + (merged,), dtype) for count, dtype in kept]
        + [
            pltpu.VMEM((rows,) + (count if count != (1,) else ()) + (lanes,), dtype)
            for lanes in (LANES, sz.tail)
            for count, dtype in kept
        ]
        + [pltpu.SemaphoreType.DMA((3, 4))],
        limit=MOST_VMEM,
    )(thickness, wind_rows, tracer_rows)

    near = [(band * n_lon + i, (band ^ 1) * n_lon + i) for band in range(n_lat) for i in range(n_lon)]
    far = []
    for band in range(n_lat):
        other = band - 1 if band % 2 == 0 else band + 1
        for i in range(n_lon):
            if 0 <= other < n_lat:
                far.append((band * n_lon + i, other * n_lon + i))
            else:
                far.append((band * n_lon + i, band * n_lon + (i + n_lon // 2) % n_lon))
    near_h = lax.ppermute(thickness, ("lat", "lon"), near)
    near_w = lax.ppermute(wind_rows, ("lat", "lon"), near)
    if not sz.near_only:
        far_rows = lax.ppermute(far_rows, ("lat", "lon"), far)

    order = [sz.turns(False), sz.turns(True)]

    def meetings(shares):
        got = [shares[0]]
        for k in range(1, n_lon):
            sectors = [(band, i, i ^ order[band % 2][k]) for band in range(n_lat) for i in range(n_lon)]
            got.append(lax.ppermute(shares[k], ("lat", "lon"), [(b * n_lon + i, b * n_lon + j) for b, i, j in sectors]))
        return got

    all_pieces = pltpu.VMEM((n_lon, sz.size + 8 * sz.stack, LANES), f32)
    all_units = pltpu.VMEM((n_lon * sz.size + 8 * sz.stack, LANES), f32)
    *tends, far_rows, near_q = call(
        polar_kernel,
        "polar",
        [vmem] * 9,
        [shaped(sz.size + EXT_ROWS, LANES)] * n_lon + [far_row, near_row],
        [
            all_units,
            pltpu.VMEM((4 * sz.stack, LANES), f32),
            pltpu.VMEM((3, EXT_ROWS, sz.tiles * LANES), f32),
        ],
    )(thickness, wind_rows, near_h, near_w, sides, geo, wave, far_rows, near_q)
    met = meetings(tends)
    near_q = lax.ppermute(near_q, ("lat", "lon"), near)
    from_far = lax.ppermute(far_rows, ("lat", "lon"), far) if sz.near_only else far_rows
    weights, masks = call(
        weights_kernel,
        "weights",
        [smem, vmem, vmem, anywhere],
        (
            jax.ShapeDtypeStruct((sz.share * PER_TILE * sz.stack, n_lon * sz.stack), jnp.bfloat16),
            shaped(3, EXT_ROWS, LANES),
        ),
    )(cutoff, n, inverse, tends[0])
    worked = call(
        filter_kernel,
        "filter",
        [vmem] * 2 + [vmem] * n_lon,
        [shaped(sz.size, LANES)] * n_lon,
        [all_pieces, all_pieces],
    )(weights, geo, *met)
    held = call(pass_kernel, "pass", [vmem] + [anywhere] * 2, shaped(sz.size, LANES))(worked[-1], from_far, near_q)
    worked = [*worked[:-1], held]
    back = meetings(worked)

    base_w, base_h, mass = call(
        rest_kernel,
        "rest",
        [vmem] * 10 + [anywhere] + [vmem] * n_lon,
        (shaped(2, rows, merged), shaped(rows, merged), jax.ShapeDtypeStruct(tracers.shape, jnp.bfloat16)),
        [pltpu.VMEM((6, EXT_ROWS, sz.tiles * LANES), f32), pltpu.VMEM((n_lon, 8, LANES), f32)],
    )(masks, thickness, wind_rows, tracers, near_h, near_w, near_q, from_far, geo, wave, worked[0], *met)

    new_w, new_h = call(
        finish_kernel,
        "finish",
        [vmem] * (3 + n_lon),
        (shaped(*wind_rows.shape), shaped(rows, merged)),
        [all_units],
    )(masks, base_w, base_h, *back)
    return jnp.swapaxes(new_w, 0, 1), new_h, mass


def solution(mesh):
    in_specs = (P(None, "lat", "lon"), P("lat", "lon"), P(None, "lat", "lon"), P())
    out_specs = (P(None, "lat", "lon"), P("lat", "lon"), P(None, "lat", "lon"))
    return jax.shard_map(local, mesh=mesh, in_specs=in_specs, out_specs=out_specs, check_vma=False)
```

```python
import functools
import math

import jax
import jax.numpy as jnp
import numpy as np
from jax import lax
from jax.experimental import pallas as pl
from jax.experimental.pallas import tpu as pltpu
from jax.sharding import PartitionSpec as P

LEVELS = 16
TIME_STEP = 0.05
DIFFUSION = 0.5
LANES = 128
PER_TILE = LANES // LEVELS
SIDE_ROWS = 8
EXT_ROWS = 16
LIMIT = 48 * 1024 * 1024
MOST_VMEM = 64 * 1024 * 1024 - 10500 * 1024


class Sizes:
    def __init__(self, rows, merged, n_lat, n_lon):
        self.rows = rows
        self.merged = merged
        self.columns = merged // LEVELS
        self.n_lat = n_lat
        self.n_lon = n_lon
        self.nlat = rows * n_lat
        self.nlon = self.columns * n_lon
        self.ratio = 2.0 * self.nlat / self.nlon
        self.tiles = -(-merged // LANES)
        self.end = (self.tiles - 1) * LANES
        self.tail = merged - self.end
        self.stack = -(-(self.tiles + 1) // 8) * 8
        self.near_only = rows <= self.nlat // 6 < 2 * rows
        self.work = rows - 1 if self.near_only else rows
        self.units = 3 * self.work
        self.share = -(-self.units // n_lon)
        self.size = self.share * self.stack
        assert self.tail <= LANES - 4 * LEVELS and rows + 2 <= EXT_ROWS and n_lat % 2 == 0
        assert n_lon >= 4 and n_lon & (n_lon - 1) == 0 and rows == SIDE_ROWS + 1

    def span(self, tile):
        return self.tail if tile == self.tiles - 1 else LANES

    def first(self):
        return jnp.where(lax.rem(lax.axis_index("lat"), 2) == 0, 1, 0) if self.near_only else 0

    def at_pole(self, row):
        band = lax.axis_index("lat")
        pole = jnp.where(band == 0, 0, jnp.where(band == self.n_lat - 1, self.rows - 1, -1))
        return row == (pole if self.near_only else -1)

    def turns(self, odd):
        middle, last = list(range(1, self.n_lon - 1)), self.n_lon - 1
        return [0, middle[-1], last] + middle[-2::-1] if odd else [0, last] + middle

    def partner(self, k):
        odd = lax.rem(lax.axis_index("lat"), 2) == 1
        turn = jnp.where(odd, self.turns(True)[k], self.turns(False)[k])
        return jnp.bitwise_xor(lax.axis_index("lon"), turn)

    def piece(self, k):
        return pl.ds(pl.multiple_of(self.partner(k) * self.size, 8), self.size)


def geometry(sz):
    table = np.zeros((sz.n_lat, 3, EXT_ROWS, LANES), np.float64)

    def face(j):
        return math.sin((j + 1) * math.pi / sz.nlat) if 0 <= j < sz.nlat - 1 else 0.0

    for band in range(sz.n_lat):
        for row in range(sz.rows):
            j = band * sz.rows + row
            centre = (j + 0.5) * math.pi / sz.nlat - math.pi / 2
            table[band, 0, row] = 1.0 / math.cos(centre)
            table[band, 1, row] = math.sin(centre)
            table[band, 2, row] = face(j)
        table[band, 2, EXT_ROWS - 1] = face(band * sz.rows - 1)
    return table.astype(np.float32)


def offsets(sz):
    shift, out_tile = np.divmod(np.arange(PER_TILE * sz.stack), sz.stack)
    sector, in_tile = np.divmod(np.arange(sz.n_lon * sz.stack), sz.stack)
    n = (PER_TILE * (out_tile - 1) + shift)[:, None] - (PER_TILE * in_tile + sz.columns * sector)[None, :]
    n = (n + sz.nlon // 2) % sz.nlon - sz.nlon // 2
    with np.errstate(divide="ignore"):
        inverse = np.where(n == 0, 0.0, 1.0 / (sz.nlon * np.sin(np.pi * n / sz.nlon)))
    return n.astype(np.float32), inverse.astype(np.float32)


def waves(sz):
    column = PER_TILE * np.arange(sz.stack)[:, None] + np.arange(LANES)[None, :] // LEVELS
    angle = 2 * np.pi * column / sz.nlon
    return np.stack([np.cos(angle), np.sin(angle)]).astype(np.float32)


def spare(place):
    row, group = divmod(place, 3)
    return row, LEVELS * (5 + group)


def edges_kernel(sz, h_hbm, w_hbm, q_hbm, near_ref, far_ref, sides_ref, *scratch):
    row_refs, first_refs, last_refs, sems = scratch[:3], scratch[3:6], scratch[6:9], scratch[9]
    rows, last = sz.rows, sz.rows - 1
    even = lax.rem(lax.axis_index("lat"), 2) == 0
    copies = []
    for i, source in enumerate((h_hbm, w_hbm, q_hbm)):
        for k, row in enumerate((0, last)):
            one = source.at[pl.ds(row, 1)] if i == 0 else source.at[row]
            copies.append(pltpu.make_async_copy(one, row_refs[i].at[k], sems.at[i, k]))
        for k, (start, to) in enumerate(((0, first_refs[i]), (sz.end, last_refs[i]))):
            lanes = pl.ds(start, to.shape[-1])
            cut = source.at[:, lanes] if i == 0 else source.at[:, :, lanes]
            copies.append(pltpu.make_async_copy(cut, to, sems.at[i, 2 + k]))
    for copy in copies:
        copy.start()
    for copy in copies:
        copy.wait()
    h_rows, w_rows, q_rows = row_refs
    for t in range(sz.tiles):
        wide = sz.span(t)
        lanes = slice(LANES * t, LANES * t + wide)
        q = [q_rows[k, :, lanes].astype(jnp.float32) for k in range(2)]
        for f in range(5):
            if f == 0:
                first, final = h_rows[0, :, lanes], h_rows[1, :, lanes]
            elif f == 1:
                first, final = w_rows[0, 1:2, lanes], w_rows[1, 1:2, lanes]
            else:
                first, final = q[0][f - 2 : f - 1], q[1][f - 2 : f - 1]
                at = sz.stack * (f - 2) + t
                near_ref[at : at + 1, :wide] = jnp.where(even, final, first)
            at = sz.stack * f + t
            far_ref[at : at + 1, :wide] = jnp.where(even, first, final)
    sides_ref[...] = jnp.zeros(sides_ref.shape, jnp.float32)
    for k, (refs, at) in enumerate(((first_refs, 0), (last_refs, sz.tail - LEVELS))):
        columns = slice(at, at + LEVELS)
        for f in range(5):
            if f == 0:
                value = refs[0][:, columns]
            elif f == 1:
                value = refs[1][:, 0, columns]
            else:
                value = refs[2][:, f - 2, columns].astype(jnp.float32)
            start = SIDE_ROWS * k
            sides_ref[start : start + SIDE_ROWS, LEVELS * f : LEVELS * (f + 1)] = value[:SIDE_ROWS]
            row, lane = spare(f)
            sides_ref[start + row : start + row + 1, lane : lane + LEVELS] = value[SIDE_ROWS:]


def add_rows(sz, ext, near_h_ref, near_w_ref, near_q_ref, far_ref):
    band = lax.axis_index("lat")
    even = lax.rem(band, 2) == 0
    over_pole = (band == 0) | (band == sz.n_lat - 1)
    last = sz.rows - 1
    for f in range(2 if near_q_ref is None else 5):
        flip = jnp.where(over_pole, -1.0, 1.0) if f == 1 else 1.0
        for t in range(sz.tiles):
            lanes = slice(LANES * t, LANES * t + sz.span(t))
            if f == 0:
                near = jnp.where(even, near_h_ref[0:1, lanes], near_h_ref[last : sz.rows, lanes])
            elif f == 1:
                near = jnp.where(even, near_w_ref[0, 1:2, lanes], near_w_ref[last, 1:2, lanes])
            else:
                at = sz.stack * (f - 2) + t
                near = near_q_ref[at : at + 1, : sz.span(t)]
            at = sz.stack * f + t
            far = jnp.zeros_like(near) if far_ref is None else far_ref[at : at + 1, : sz.span(t)] * flip
            ext[f, sz.rows : sz.rows + 1, lanes] = jnp.where(even, near, far)
            ext[f, EXT_ROWS - 1 : EXT_ROWS, lanes] = jnp.where(even, far, near)


class Tiles:
    def __init__(self, sz):
        self.sz = sz
        self.lane = lax.broadcasted_iota(jnp.int32, (EXT_ROWS, LANES), 1)
        self.turned = {}

    def turn(self, name, t, value, step):
        key = (name, t % self.sz.tiles, step)
        if key not in self.turned:
            self.turned[key] = pltpu.roll(value(t % self.sz.tiles), step % LANES, 1)
        return self.turned[key]

    def east(self, name, t, value):
        here = self.turn(name, t, value, -LEVELS)
        return jnp.where(self.lane < LANES - LEVELS, here, self.turn(name, t + 1, value, -LEVELS))

    def west(self, name, t, value):
        here = self.turn(name, t, value, LEVELS)
        return jnp.where(self.lane >= LEVELS, here, self.turn(name, t - 1, value, LEVELS))


def north(value):
    return pltpu.roll(value, EXT_ROWS - 1, 0)


def south(value):
    return pltpu.roll(value, 1, 0)


def polar_kernel(sz, h_ref, w_ref, near_h_ref, near_w_ref, sides_ref, geo_ref, wave_ref, far_ref, near_q_ref, *refs):
    out_refs, (far_out, near_out, tend_ref, pole_ref, ext) = refs[:-5], refs[-5:]
    far_out[...] = far_ref[...]
    near_out[...] = near_q_ref[...]
    if sz.near_only:
        far_ref = None
    band = lax.axis_index("lat")
    ring = Tiles(sz)
    lane = ring.lane
    tiles, stack, rows, work = sz.tiles, sz.stack, sz.rows, sz.work
    even = lax.rem(band, 2) == 0
    for f, value in enumerate((h_ref[...], w_ref[:, 1, :], w_ref[:, 0, :])):
        ext[f, :rows, sz.end :] = jnp.zeros((rows, LANES), jnp.float32)
        ext[f, :rows, : sz.merged] = value
    add_rows(sz, ext, near_h_ref, near_w_ref, None, far_ref)
    inv_cos, sin_centre, cos_face = geo_ref[band, 0], geo_ref[band, 1], geo_ref[band, 2]
    ratio = sz.ratio

    def tile(f, t):
        return ext[f, :, LANES * t : LANES * (t + 1)]

    kept = {}

    def zonal(t):
        if t not in kept:
            thick_e = ring.east("h", t, functools.partial(tile, 0))
            wind_e = ring.east("u", t, functools.partial(tile, 2))
            flux = 0.25 * (tile(2, t) + wind_e) * (tile(0, t) + thick_e) * inv_cos
            if t == tiles - 1:
                flux = jnp.where(lane < sz.tail - LEVELS, flux, 0.0)
            kept[t] = (flux, thick_e)
        return kept[t]

    for t in range(tiles):
        flux, thick_e = zonal(t)
        thick, wind_v, wind_u = tile(0, t), tile(1, t), tile(2, t)
        flux_w = ring.west("f", t, lambda s: zonal(s)[0])
        thick_w = ring.west("hw", t, functools.partial(tile, 0))
        thick_n = north(thick)
        flux_n = (0.25 * ratio) * (wind_v + north(wind_v)) * (thick + thick_n) * cos_face
        thick_tend = -((flux - flux_w) + (flux_n - south(flux_n)) * inv_cos)
        wind_u_tend = sin_centre * wind_v - (thick_e - thick_w) * (0.5 * inv_cos)
        wind_v_tend = -sin_centre * wind_u - (0.5 * ratio) * (thick_n - south(thick))
        extra = 0.0
        if t == tiles - 1:
            last = sz.tail - LEVELS
            columns = [(tile(0, 0), 0), (thick, last), (tile(2, 0), 0), (wind_u, last)]
            for k, (source, at) in reversed(list(enumerate(columns))):
                to = sz.tail + LEVELS * k
                extra = jnp.where(lane < to + LEVELS, pltpu.roll(source, (to - at) % LANES, 1), extra)
        for f, tend in enumerate((thick_tend, wind_u_tend, wind_v_tend, thick)):
            if sz.near_only:
                alone = jnp.where(band < sz.n_lat // 2, tend[:1], tend[rows - 1 : rows])
                if t == tiles - 1:
                    alone = jnp.where(lane[:1] < sz.tail, alone, 0.0)
                pole_ref[stack * f + t : stack * f + t + 1] = alone
            if f == 3:
                continue
            if t == tiles - 1:
                tend = jnp.where(lane < sz.tail, tend, extra)
            if sz.near_only:
                tend = jnp.where(even, north(tend), tend)
            tend_ref[pl.ds(stack * work * f + t, work, stride=stack), :] = tend[:work]
    for f in range(3):
        for t in range(tiles, stack):
            tend_ref[pl.ds(stack * work * f + t, work, stride=stack), :] = jnp.zeros((work, LANES), jnp.float32)
    used, sent = stack * sz.units, sz.n_lon * sz.size
    if used < sent:
        tend_ref[used:sent, :] = jnp.zeros((sent - used, LANES), jnp.float32)
    sides = [sides_ref[:SIDE_ROWS], sides_ref[SIDE_ROWS:]]
    if sz.near_only:
        sums = pole_sums(sz, pole_ref, wave_ref, extra, band)
        sides = [side + sums for side in sides]
    here = lax.axis_index("lon")
    for k, out_ref in enumerate(out_refs):
        out_ref[: sz.size] = tend_ref[sz.piece(k), :]
        eastward = sz.partner(k) == lax.rem(here + 1, sz.n_lon)
        out_ref[sz.size :] = jnp.where(eastward, sides[1], sides[0])


def pole_sums(sz, pole_ref, wave_ref, extra, band):
    stack, rows = sz.stack, sz.rows
    lane = lax.broadcasted_iota(jnp.int32, (SIDE_ROWS, LANES), 1)
    row = lax.broadcasted_iota(jnp.int32, (SIDE_ROWS, LANES), 0)
    found = jnp.zeros((SIDE_ROWS, LANES), jnp.float32)

    def put(place, value):
        at_row, at = spare(6 + place)
        return jnp.where((row == at_row) & (lane >= at) & (lane < at + LEVELS), value, found)

    for f in range(4):
        if sz.tiles < stack:
            pole_ref[stack * f + sz.tiles : stack * (f + 1)] = jnp.zeros((stack - sz.tiles, LANES), jnp.float32)
        values = pole_ref[stack * f : stack * (f + 1)]
        for k, terms in enumerate((values, values * wave_ref[0], values * wave_ref[1])):
            total = jnp.sum(terms, axis=0, keepdims=True)
            for step in (64, 32, 16):
                total = total + pltpu.roll(total, step, 1)
            found = put(3 * f + k, total)
    beside = jnp.where(band < sz.n_lat // 2, extra[:1], extra[rows - 1 : rows])
    for k in range(4):
        found = put(12 + k, pltpu.roll(beside, (spare(18 + k)[1] - sz.tail - LEVELS * k) % LANES, 1))
    return found


def pole_waves(sz, rows_in, inv_cos, sign):
    n_lon = sz.n_lon
    lane = lax.broadcasted_iota(jnp.int32, (1, LANES), 1)

    def value(s, place):
        row, at = spare(6 + place)
        return pltpu.roll(rows_in[s % n_lon, row : row + 1], -at % LANES, 1)

    theta = 2 * math.pi / sz.nlon
    ends = (1.0, math.cos(theta * (sz.columns - 1)), math.sin(theta * (sz.columns - 1)))
    sums = [[[value(s, 3 * f + k) for k in range(3)] for f in range(4)] for s in range(n_lon)]
    for s in range(n_lon):
        thick_w, thick_e = value(s, 13), value(s + 1, 12)
        flux = 0.25 * (value(s, 15) + value(s + 1, 14)) * (thick_w + thick_e) * inv_cos
        slope = 0.5 * inv_cos
        after = (s + 1) % n_lon
        for f, (west_of, east_of) in enumerate(((flux, flux), (slope * thick_e, slope * thick_w))):
            for k in range(3):
                sums[s][f][k] = sums[s][f][k] - west_of * ends[k]
            for k in range(2):
                sums[after][f][k] = sums[after][f][k] + east_of
    result = []
    for f in range(3):
        waves_of = [0.0, 0.0, 0.0]
        for s in range(n_lon):
            level, cosine, sine = sums[s][f]
            if f == 2:
                level = level + (0.5 * sz.ratio) * sign * sums[s][3][0]
                cosine = cosine - (0.5 * sz.ratio) * sign * sums[s][3][1]
                sine = sine - (0.5 * sz.ratio) * sign * sums[s][3][2]
            c, d = math.cos(2 * math.pi * s / n_lon), math.sin(2 * math.pi * s / n_lon)
            waves_of[0] = waves_of[0] + level
            waves_of[1] = waves_of[1] + (c * cosine - d * sine)
            waves_of[2] = waves_of[2] + (d * cosine + c * sine)
        spread = []
        for k, total in enumerate(waves_of):
            total = jnp.where(lane < LEVELS, total * ((1.0 if k == 0 else 2.0) / sz.nlon), 0.0)
            for step in (16, 32, 64):
                total = total + pltpu.roll(total, step, 1)
            spread.append(total)
        result.append(spread)
    return result


def unfolded(sides):
    lane = lax.broadcasted_iota(jnp.int32, (1, LANES), 1)
    start, width = spare(0)[1], 3 * LEVELS
    ninth = jnp.where(
        lane < width,
        pltpu.roll(sides[0:1], -start % LANES, 1),
        pltpu.roll(sides[1:2], (width - start) % LANES, 1),
    )
    return jnp.concatenate([sides, jnp.broadcast_to(ninth, sides.shape)], axis=0)


def rest_kernel(sz, masks_ref, h_ref, w_ref, q_ref, near_h_ref, near_w_ref, near_q_ref, far_ref, geo_ref, wave_ref, after_ref, *refs):
    met_refs, (new_w_ref, new_h_ref, mass_ref, ext, pole_in) = refs[: sz.n_lon], refs[sz.n_lon :]
    band = lax.axis_index("lat")
    ring = Tiles(sz)
    lane = ring.lane
    tiles, rows = sz.tiles, sz.rows
    for f in range(6):
        if f < 2 or f == 5:
            value = (h_ref[...], w_ref[:, 1, :], w_ref[:, 0, :])[min(f, 2)]
        else:
            value = q_ref[f - 2].astype(jnp.float32)
        ext[f, :rows, : sz.merged] = value
    add_rows(sz, ext, near_h_ref, near_w_ref, near_q_ref, far_ref)
    lane9 = lane[:rows]
    here = lax.axis_index("lon")
    from_e = from_w = met_refs[0][sz.size :]
    for k, met_ref in enumerate(met_refs):
        eastward = lax.rem(sz.partner(k) - here + sz.n_lon, sz.n_lon)
        pole_in[eastward] = met_ref[sz.size :]
        from_e = jnp.where(sz.partner(k) == lax.rem(here + 1, sz.n_lon), met_ref[sz.size :], from_e)
        from_w = jnp.where(sz.partner(k) == lax.rem(here + sz.n_lon - 1, sz.n_lon), met_ref[sz.size :], from_w)
    from_e, from_w = unfolded(from_e), unfolded(from_w)
    for place, f in enumerate((0, 5, 2, 3, 4)):
        after = pltpu.roll(from_e, (sz.tail - LEVELS * place) % LANES, 1)[:rows]
        before = pltpu.roll(from_w, (LANES - LEVELS - LEVELS * place) % LANES, 1)[:rows]
        own = ext[f, :rows, sz.end :]
        edge = jnp.where(lane9 < LANES - LEVELS, after, before)
        ext[f, :rows, sz.end :] = jnp.where(lane9 < sz.tail, own, edge)
    inv_cos, sin_centre, cos_face = geo_ref[band, 0], geo_ref[band, 1], geo_ref[band, 2]
    ratio = sz.ratio

    plain, alone = masks_ref[0], masks_ref[1]
    if sz.near_only:
        band = lax.axis_index("lat")
        low = band < sz.n_lat // 2
        pole_cos = jnp.where(low, inv_cos[:1], inv_cos[rows - 1 : rows])
        kept_waves = pole_waves(sz, pole_in, pole_cos, jnp.where(low, 1.0, -1.0))

    def stepped(f, t, value, tend):
        value = value + plain * tend
        if sz.near_only:
            level, cosine, sine = kept_waves[f]
            wave = level + cosine * wave_ref[0, t : t + 1] + sine * wave_ref[1, t : t + 1]
            value = value + alone * wave
        return value

    def tile(f, t):
        return ext[f, :, LANES * t : LANES * (t + 1)]

    kept = {}

    def zonal(t):
        if t not in kept:
            thick_e = ring.east("h", t, functools.partial(tile, 0))
            wind_e = ring.east("u", t, functools.partial(tile, 5))
            flux = 0.25 * (tile(5, t) + wind_e) * (tile(0, t) + thick_e) * inv_cos
            parts = []
            for k in range(3):
                q = tile(2 + k, t)
                q_e = ring.east(k, t, functools.partial(tile, 2 + k))
                parts.append(DIFFUSION * (q_e - q) - flux * (0.5 * (q + q_e)))
            kept[t] = (flux, thick_e, parts)
        return kept[t]

    for t in range(tiles):
        span = sz.span(t)
        lanes = slice(LANES * t, LANES * t + span)
        flux, thick_e, parts = zonal(t)
        thick, wind_u, wind_v = tile(0, t), tile(5, t), tile(1, t)
        flux_w = ring.west("f", t, lambda s: zonal(s)[0])
        thick_w = ring.west("hw", t, functools.partial(tile, 0))
        thick_n = north(thick)
        flux_n = (0.25 * ratio) * (wind_v + north(wind_v)) * (thick + thick_n) * cos_face
        thick_tend = -((flux - flux_w) + (flux_n - south(flux_n)) * inv_cos)
        wind_u_tend = sin_centre * wind_v - (thick_e - thick_w) * (0.5 * inv_cos)
        wind_v_tend = -sin_centre * wind_u - (0.5 * ratio) * (thick_n - south(thick))
        new_h_ref[:, lanes] = stepped(0, t, thick, thick_tend)[:rows, :span]
        new_w_ref[0, :, lanes] = stepped(1, t, wind_u, wind_u_tend)[:rows, :span]
        new_w_ref[1, :, lanes] = stepped(2, t, wind_v, wind_v_tend)[:rows, :span]
        for k in range(3):
            q = tile(2 + k, t)
            q_n = north(q)
            zonal_part = parts[k] - ring.west(("p", k), t, lambda s: zonal(s)[2][k])
            lap = q_n + south(q) - 2.0 * q
            over = flux_n * (0.5 * (q + q_n))
            merid_part = DIFFUSION * lap - (over - south(over)) * inv_cos
            mass = thick * q + TIME_STEP * (zonal_part + merid_part)
            mass_ref[k, :, lanes] = mass[:rows, :span].astype(jnp.bfloat16)


def sin_pi(y):
    y = jnp.where(y > 0.5, 1.0 - y, jnp.where(y < -0.5, -1.0 - y, y))
    s = y * y
    series = [(-1) ** i * math.pi ** (2 * i + 1) / math.factorial(2 * i + 1) for i in range(7)]
    total = series[-1]
    for factor in reversed(series[:-1]):
        total = total * s + factor
    return total * y


def share_of(sz, i):
    unit = lax.axis_index("lon") * sz.share + i
    return unit // sz.work, sz.first() + lax.rem(unit, sz.work)


def weights_kernel(sz, cut_ref, n_ref, inverse_ref, after_ref, weights_ref, masks_ref):
    band = lax.axis_index("lat")
    row = lax.broadcasted_iota(jnp.int32, (EXT_ROWS, LANES), 0)
    cuts = jnp.full((EXT_ROWS, LANES), sz.nlon // 2, jnp.int32)
    for j in range(sz.rows):
        cuts = jnp.where(row == j, cut_ref[band * sz.rows + j], cuts)
    plain, alone = cuts >= sz.nlon // 2, sz.at_pole(row)
    masks_ref[0] = jnp.where(plain, TIME_STEP, 0.0)
    masks_ref[1] = jnp.where(alone, TIME_STEP, 0.0)
    masks_ref[2] = jnp.where(plain | alone, 0.0, TIME_STEP)
    size = PER_TILE * sz.stack
    for i in range(sz.share):
        width = (2 * cut_ref[band * sz.rows + share_of(sz, i)[1]] + 1).astype(jnp.float32)
        n = n_ref[...]
        turns = n * width
        turns = turns - jnp.round(turns * (0.5 / sz.nlon)) * (2.0 * sz.nlon)
        weights = sin_pi(turns * (1.0 / sz.nlon)) * inverse_ref[...]
        weights = jnp.where(n == 0.0, width * (1.0 / sz.nlon), weights)
        weights_ref[size * i : size * (i + 1)] = weights.astype(jnp.bfloat16)


def pass_kernel(sz, piece_ref, after_ref, also_after_ref, out_ref):
    out_ref[...] = piece_ref[...]


def filter_kernel(sz, weights_ref, geo_ref, *refs):
    n_lon, stack, share = sz.n_lon, sz.stack, sz.share
    in_refs, out_refs, (gathered, results) = refs[:n_lon], refs[n_lon : 2 * n_lon], refs[2 * n_lon :]
    for k, in_ref in enumerate(in_refs):
        gathered[sz.partner(k), : sz.size] = in_ref[: sz.size]

    band = lax.axis_index("lat")
    lane = lax.broadcasted_iota(jnp.int32, (share, LANES), 1)
    place = lax.broadcasted_iota(jnp.int32, (share, LANES), 0)
    by_flux = by_thick = jnp.zeros((share, LANES), jnp.float32)
    for i in range(share):
        field, row = share_of(sz, i)
        inv_cos = geo_ref[band, 0, pl.ds(row, 1), :]
        by_flux = jnp.where((place == i) & (field == 0), inv_cos, by_flux)
        by_thick = jnp.where((place == i) & (field == 1), 0.5 * inv_cos, by_thick)
    sides = [gathered[s, pl.ds(sz.tiles - 1, share, stride=stack), :] for s in range(n_lon)]

    def column(s, k):
        return pltpu.roll(sides[s % n_lon], (-sz.tail - LEVELS * k) % LANES, 1)

    for s in range(n_lon):
        thick_w, thick_e = column(s, 1), column(s + 1, 0)
        flux = 0.25 * (column(s, 3) + column(s + 1, 2)) * (thick_w + thick_e) * by_flux
        west_of, east_of = flux + by_thick * thick_e, flux + by_thick * thick_w
        at = pl.ds(sz.tiles - 1, share, stride=stack)
        own = gathered[s, at, :]
        own = own - jnp.where(lane >= sz.tail - LEVELS, pltpu.roll(west_of, sz.tail - LEVELS, 1), 0.0)
        gathered[s, at, :] = jnp.where(lane < sz.tail, own, 0.0)
        at = pl.ds(0, share, stride=stack)
        after = (s + 1) % n_lon
        gathered[after, at, :] = gathered[after, at, :] + jnp.where(lane < LEVELS, east_of, 0.0)

    wide = lax.broadcasted_iota(jnp.int32, (stack, LANES), 1)
    rows = PER_TILE * stack
    for i in range(share):
        here = slice(stack * i, stack * (i + 1))
        pieces = [gathered[s, here].astype(jnp.bfloat16) for s in range(n_lon)]
        circle = jnp.concatenate([jnp.concatenate(pieces[s:] + pieces[:s], axis=0) for s in range(n_lon)], axis=1)
        spread = jnp.dot(weights_ref[rows * i : rows * (i + 1)], circle, preferred_element_type=jnp.float32)
        for s in range(n_lon):
            same = spread[:stack, LANES * s : LANES * (s + 1)]
            carried = None
            for e in range(1, PER_TILE):
                part = spread[stack * e : stack * (e + 1), LANES * s : LANES * (s + 1)]
                part = pltpu.roll(part, LEVELS * e, 1)
                inside = wide >= LEVELS * e
                same = same + jnp.where(inside, part, 0.0)
                over = jnp.where(inside, 0.0, part)
                carried = over if carried is None else carried + over
            results[s, here] = pltpu.roll(same, stack - 1, 0) + carried
    for k, out_ref in enumerate(out_refs):
        out_ref[...] = results[sz.partner(k), : sz.size]


def finish_kernel(sz, masks_ref, base_w_ref, base_h_ref, *refs):
    back_refs, (new_w_ref, new_h_ref, back_ref) = refs[: sz.n_lon], refs[sz.n_lon :]
    rows, work = sz.rows, sz.work
    for k, ref in enumerate(back_refs):
        back_ref[sz.piece(k), :] = ref[...]
    scale = masks_ref[2]
    even = lax.rem(lax.axis_index("lat"), 2) == 0
    for f in range(3):
        for t in range(sz.tiles):
            span = sz.span(t)
            lanes = slice(LANES * t, LANES * t + span)
            tend = back_ref[pl.ds(sz.stack * work * f + t, work, stride=sz.stack), :]
            if sz.near_only:
                tend = jnp.concatenate([tend, jnp.zeros((EXT_ROWS - work, LANES), jnp.float32)], axis=0)
                tend = jnp.where(even, south(tend), tend)
            change = (scale[:rows] * tend[:rows])[:, :span]
            if f == 0:
                new_h_ref[:, lanes] = base_h_ref[:, lanes] + change
            else:
                new_w_ref[:, f - 1, lanes] = base_w_ref[f - 1, :, lanes] + change


def local(winds, thickness, tracers, cutoff):
    n_lat = lax.axis_size("lat")
    n_lon = lax.axis_size("lon")
    rows, merged = thickness.shape
    sz = Sizes(rows, merged, n_lat, n_lon)
    f32 = jnp.float32
    vmem = pl.BlockSpec(memory_space=pltpu.VMEM)
    smem = pl.BlockSpec(memory_space=pltpu.SMEM)
    hbm = pl.BlockSpec(memory_space=pltpu.HBM)
    anywhere = pl.BlockSpec(memory_space=pl.ANY)

    def shaped(*shape):
        return jax.ShapeDtypeStruct(shape, f32)

    def call(kernel, name, in_specs, out_shape, scratch=(), limit=LIMIT):
        return pl.pallas_call(
            functools.partial(kernel, sz),
            out_shape=out_shape,
            in_specs=in_specs,
            out_specs=jax.tree.map(lambda _: vmem, out_shape),
            scratch_shapes=list(scratch),
            compiler_params=pltpu.CompilerParams(vmem_limit_bytes=limit),
            name=name,
        )

    geo = jnp.asarray(geometry(sz))
    wave = jnp.asarray(waves(sz))
    n, inverse = (jnp.asarray(table) for table in offsets(sz))

    wind_rows = jnp.swapaxes(winds, 0, 1)
    tracer_rows = jnp.swapaxes(tracers, 0, 1)
    far_row, near_row = shaped(5 * sz.stack, LANES), shaped(3 * sz.stack, LANES)
    kept = [((1,), f32), ((2,), f32), ((3,), jnp.bfloat16)]
    near_q, far_rows, sides = call(
        edges_kernel,
        "edges",
        [hbm] * 3,
        (near_row, far_row, shaped(2 * SIDE_ROWS, LANES)),
        [pltpu.VMEM((2,) + count + (merged,), dtype) for count, dtype in kept]
        + [
            pltpu.VMEM((rows,) + (count if count != (1,) else ()) + (lanes,), dtype)
            for lanes in (LANES, sz.tail)
            for count, dtype in kept
        ]
        + [pltpu.SemaphoreType.DMA((3, 4))],
        limit=MOST_VMEM,
    )(thickness, wind_rows, tracer_rows)

    near = [(band * n_lon + i, (band ^ 1) * n_lon + i) for band in range(n_lat) for i in range(n_lon)]
    far = []
    for band in range(n_lat):
        other = band - 1 if band % 2 == 0 else band + 1
        for i in range(n_lon):
            if 0 <= other < n_lat:
                far.append((band * n_lon + i, other * n_lon + i))
            else:
                far.append((band * n_lon + i, band * n_lon + (i + n_lon // 2) % n_lon))
    near_h = lax.ppermute(thickness, ("lat", "lon"), near)
    near_w = lax.ppermute(wind_rows, ("lat", "lon"), near)
    if not sz.near_only:
        far_rows = lax.ppermute(far_rows, ("lat", "lon"), far)

    order = [sz.turns(False), sz.turns(True)]

    def meetings(shares):
        got = [shares[0]]
        for k in range(1, n_lon):
            sectors = [(band, i, i ^ order[band % 2][k]) for band in range(n_lat) for i in range(n_lon)]
            got.append(lax.ppermute(shares[k], ("lat", "lon"), [(b * n_lon + i, b * n_lon + j) for b, i, j in sectors]))
        return got

    all_pieces = pltpu.VMEM((n_lon, sz.size + 8 * sz.stack, LANES), f32)
    all_units = pltpu.VMEM((n_lon * sz.size + 8 * sz.stack, LANES), f32)
    *tends, far_rows, near_q = call(
        polar_kernel,
        "polar",
        [vmem] * 9,
        [shaped(sz.size + SIDE_ROWS, LANES)] * n_lon + [far_row, near_row],
        [
            all_units,
            pltpu.VMEM((4 * sz.stack, LANES), f32),
            pltpu.VMEM((3, EXT_ROWS, sz.tiles * LANES), f32),
        ],
    )(thickness, wind_rows, near_h, near_w, sides, geo, wave, far_rows, near_q)
    met = meetings(tends)
    near_q = lax.ppermute(near_q, ("lat", "lon"), near)
    from_far = lax.ppermute(far_rows, ("lat", "lon"), far) if sz.near_only else far_rows
    weights, masks = call(
        weights_kernel,
        "weights",
        [smem, vmem, vmem, anywhere],
        (
            jax.ShapeDtypeStruct((sz.share * PER_TILE * sz.stack, n_lon * sz.stack), jnp.bfloat16),
            shaped(3, EXT_ROWS, LANES),
        ),
    )(cutoff, n, inverse, tends[0])
    worked = call(
        filter_kernel,
        "filter",
        [vmem] * 2 + [vmem] * n_lon,
        [shaped(sz.size, LANES)] * n_lon,
        [all_pieces, all_pieces],
    )(weights, geo, *met)
    held = call(pass_kernel, "pass", [vmem] + [anywhere] * 2, shaped(sz.size, LANES))(worked[-1], from_far, near_q)
    worked = [*worked[:-1], held]
    back = meetings(worked)

    base_w, base_h, mass = call(
        rest_kernel,
        "rest",
        [vmem] * 10 + [anywhere] + [vmem] * n_lon,
        (shaped(2, rows, merged), shaped(rows, merged), jax.ShapeDtypeStruct(tracers.shape, jnp.bfloat16)),
        [pltpu.VMEM((6, EXT_ROWS, sz.tiles * LANES), f32), pltpu.VMEM((n_lon, 8, LANES), f32)],
    )(masks, thickness, wind_rows, tracers, near_h, near_w, near_q, from_far, geo, wave, worked[0], *met)

    new_w, new_h = call(
        finish_kernel,
        "finish",
        [vmem] * (3 + n_lon),
        (shaped(*wind_rows.shape), shaped(rows, merged)),
        [all_units],
    )(masks, base_w, base_h, *back)
    return jnp.swapaxes(new_w, 0, 1), new_h, mass


def solution(mesh):
    in_specs = (P(None, "lat", "lon"), P("lat", "lon"), P(None, "lat", "lon"), P())
    out_specs = (P(None, "lat", "lon"), P("lat", "lon"), P(None, "lat", "lon"))
    return jax.shard_map(local, mesh=mesh, in_specs=in_specs, out_specs=out_specs, check_vma=False)
```

```python
import functools
import math

import jax
import jax.numpy as jnp
import numpy as np
from jax import lax
from jax.experimental import pallas as pl
from jax.experimental.pallas import tpu as pltpu
from jax.sharding import PartitionSpec as P

LEVELS = 16
TIME_STEP = 0.05
DIFFUSION = 0.5
LANES = 128
PER_TILE = LANES // LEVELS
SIDE_ROWS = 8
EXT_ROWS = 16
LIMIT = 48 * 1024 * 1024
MOST_VMEM = 64 * 1024 * 1024 - 10500 * 1024


class Sizes:
    def __init__(self, rows, merged, n_lat, n_lon):
        self.rows = rows
        self.merged = merged
        self.columns = merged // LEVELS
        self.n_lat = n_lat
        self.n_lon = n_lon
        self.nlat = rows * n_lat
        self.nlon = self.columns * n_lon
        self.ratio = 2.0 * self.nlat / self.nlon
        self.tiles = -(-merged // LANES)
        self.end = (self.tiles - 1) * LANES
        self.tail = merged - self.end
        self.stack = -(-(self.tiles + 1) // 8) * 8
        self.near_only = rows <= self.nlat // 6 < 2 * rows
        self.work = rows - 1 if self.near_only else rows
        self.units = 3 * self.work
        self.share = -(-self.units // n_lon)
        self.size = self.share * self.stack
        assert self.tail <= LANES - 4 * LEVELS and rows + 2 <= EXT_ROWS and n_lat % 2 == 0
        assert n_lon >= 4 and n_lon & (n_lon - 1) == 0 and rows == SIDE_ROWS + 1

    def span(self, tile):
        return self.tail if tile == self.tiles - 1 else LANES

    def first(self):
        return jnp.where(lax.rem(lax.axis_index("lat"), 2) == 0, 1, 0) if self.near_only else 0

    def at_pole(self, row):
        band = lax.axis_index("lat")
        pole = jnp.where(band == 0, 0, jnp.where(band == self.n_lat - 1, self.rows - 1, -1))
        return row == (pole if self.near_only else -1)

    def turns(self, odd, back):
        middle, last = list(range(1, self.n_lon - 1)), self.n_lon - 1
        if odd and not back:
            return [0, middle[-1], last] + middle[-2::-1]
        return [0, last] + (middle[::-1] if odd else middle)

    def partner(self, k, back=False):
        odd = lax.rem(lax.axis_index("lat"), 2) == 1
        turn = jnp.where(odd, self.turns(True, back)[k], self.turns(False, back)[k])
        return jnp.bitwise_xor(lax.axis_index("lon"), turn)

    def piece(self, k, back=False):
        return pl.ds(pl.multiple_of(self.partner(k, back) * self.size, 8), self.size)


def geometry(sz):
    table = np.zeros((sz.n_lat, 3, EXT_ROWS, LANES), np.float64)

    def face(j):
        return math.sin((j + 1) * math.pi / sz.nlat) if 0 <= j < sz.nlat - 1 else 0.0

    for band in range(sz.n_lat):
        for row in range(sz.rows):
            j = band * sz.rows + row
            centre = (j + 0.5) * math.pi / sz.nlat - math.pi / 2
            table[band, 0, row] = 1.0 / math.cos(centre)
            table[band, 1, row] = math.sin(centre)
            table[band, 2, row] = face(j)
        table[band, 2, EXT_ROWS - 1] = face(band * sz.rows - 1)
    return table.astype(np.float32)


def offsets(sz):
    shift, out_tile = np.divmod(np.arange(PER_TILE * sz.stack), sz.stack)
    sector, in_tile = np.divmod(np.arange(sz.n_lon * sz.stack), sz.stack)
    n = (PER_TILE * (out_tile - 1) + shift)[:, None] - (PER_TILE * in_tile + sz.columns * sector)[None, :]
    n = (n + sz.nlon // 2) % sz.nlon - sz.nlon // 2
    with np.errstate(divide="ignore"):
        inverse = np.where(n == 0, 0.0, 1.0 / (sz.nlon * np.sin(np.pi * n / sz.nlon)))
    return n.astype(np.float32), inverse.astype(np.float32)


def waves(sz):
    column = PER_TILE * np.arange(sz.stack)[:, None] + np.arange(LANES)[None, :] // LEVELS
    angle = 2 * np.pi * column / sz.nlon
    return np.stack([np.cos(angle), np.sin(angle)]).astype(np.float32)


def spare(place):
    row, group = divmod(place, 3)
    return row, LEVELS * (5 + group)


def edges_kernel(sz, h_hbm, w_hbm, q_hbm, near_ref, far_ref, sides_ref, *scratch):
    row_refs, first_refs, last_refs, sems = scratch[:3], scratch[3:6], scratch[6:9], scratch[9]
    rows, last = sz.rows, sz.rows - 1
    even = lax.rem(lax.axis_index("lat"), 2) == 0
    copies = []
    for i, source in enumerate((h_hbm, w_hbm, q_hbm)):
        for k, row in enumerate((0, last)):
            one = source.at[pl.ds(row, 1)] if i == 0 else source.at[row]
            copies.append(pltpu.make_async_copy(one, row_refs[i].at[k], sems.at[i, k]))
        for k, (start, to) in enumerate(((0, first_refs[i]), (sz.end, last_refs[i]))):
            lanes = pl.ds(start, to.shape[-1])
            cut = source.at[:, lanes] if i == 0 else source.at[:, :, lanes]
            copies.append(pltpu.make_async_copy(cut, to, sems.at[i, 2 + k]))
    for copy in copies:
        copy.start()
    for copy in copies:
        copy.wait()
    h_rows, w_rows, q_rows = row_refs
    for t in range(sz.tiles):
        wide = sz.span(t)
        lanes = slice(LANES * t, LANES * t + wide)
        q = [q_rows[k, :, lanes].astype(jnp.float32) for k in range(2)]
        for f in range(5):
            if f == 0:
                first, final = h_rows[0, :, lanes], h_rows[1, :, lanes]
            elif f == 1:
                first, final = w_rows[0, 1:2, lanes], w_rows[1, 1:2, lanes]
            else:
                first, final = q[0][f - 2 : f - 1], q[1][f - 2 : f - 1]
                at = sz.stack * (f - 2) + t
                near_ref[at : at + 1, :wide] = jnp.where(even, final, first)
            at = sz.stack * f + t
            far_ref[at : at + 1, :wide] = jnp.where(even, first, final)
    sides_ref[...] = jnp.zeros(sides_ref.shape, jnp.float32)
    for k, (refs, at) in enumerate(((first_refs, 0), (last_refs, sz.tail - LEVELS))):
        columns = slice(at, at + LEVELS)
        for f in range(5):
            if f == 0:
                value = refs[0][:, columns]
            elif f == 1:
                value = refs[1][:, 0, columns]
            else:
                value = refs[2][:, f - 2, columns].astype(jnp.float32)
            start = SIDE_ROWS * k
            sides_ref[start : start + SIDE_ROWS, LEVELS * f : LEVELS * (f + 1)] = value[:SIDE_ROWS]
            row, lane = spare(f)
            sides_ref[start + row : start + row + 1, lane : lane + LEVELS] = value[SIDE_ROWS:]


def add_rows(sz, ext, near_h_ref, near_w_ref, near_q_ref, far_ref):
    band = lax.axis_index("lat")
    even = lax.rem(band, 2) == 0
    over_pole = (band == 0) | (band == sz.n_lat - 1)
    last = sz.rows - 1
    for f in range(2 if near_q_ref is None else 5):
        flip = jnp.where(over_pole, -1.0, 1.0) if f == 1 else 1.0
        for t in range(sz.tiles):
            lanes = slice(LANES * t, LANES * t + sz.span(t))
            if f == 0:
                near = jnp.where(even, near_h_ref[0:1, lanes], near_h_ref[last : sz.rows, lanes])
            elif f == 1:
                near = jnp.where(even, near_w_ref[0, 1:2, lanes], near_w_ref[last, 1:2, lanes])
            else:
                at = sz.stack * (f - 2) + t
                near = near_q_ref[at : at + 1, : sz.span(t)]
            at = sz.stack * f + t
            far = jnp.zeros_like(near) if far_ref is None else far_ref[at : at + 1, : sz.span(t)] * flip
            ext[f, sz.rows : sz.rows + 1, lanes] = jnp.where(even, near, far)
            ext[f, EXT_ROWS - 1 : EXT_ROWS, lanes] = jnp.where(even, far, near)


class Tiles:
    def __init__(self, sz):
        self.sz = sz
        self.lane = lax.broadcasted_iota(jnp.int32, (EXT_ROWS, LANES), 1)
        self.turned = {}

    def turn(self, name, t, value, step):
        key = (name, t % self.sz.tiles, step)
        if key not in self.turned:
            self.turned[key] = pltpu.roll(value(t % self.sz.tiles), step % LANES, 1)
        return self.turned[key]

    def east(self, name, t, value):
        here = self.turn(name, t, value, -LEVELS)
        return jnp.where(self.lane < LANES - LEVELS, here, self.turn(name, t + 1, value, -LEVELS))

    def west(self, name, t, value):
        here = self.turn(name, t, value, LEVELS)
        return jnp.where(self.lane >= LEVELS, here, self.turn(name, t - 1, value, LEVELS))


def north(value):
    return pltpu.roll(value, EXT_ROWS - 1, 0)


def south(value):
    return pltpu.roll(value, 1, 0)


def polar_kernel(sz, h_ref, w_ref, near_h_ref, near_w_ref, sides_ref, geo_ref, wave_ref, far_ref, near_q_ref, *refs):
    out_refs, (far_out, near_out, tend_ref, pole_ref, ext) = refs[:-5], refs[-5:]
    far_out[...] = far_ref[...]
    near_out[...] = near_q_ref[...]
    if sz.near_only:
        far_ref = None
    band = lax.axis_index("lat")
    ring = Tiles(sz)
    lane = ring.lane
    tiles, stack, rows, work = sz.tiles, sz.stack, sz.rows, sz.work
    even = lax.rem(band, 2) == 0
    for f, value in enumerate((h_ref[...], w_ref[:, 1, :], w_ref[:, 0, :])):
        ext[f, :rows, sz.end :] = jnp.zeros((rows, LANES), jnp.float32)
        ext[f, :rows, : sz.merged] = value
    add_rows(sz, ext, near_h_ref, near_w_ref, None, far_ref)
    inv_cos, sin_centre, cos_face = geo_ref[band, 0], geo_ref[band, 1], geo_ref[band, 2]
    ratio = sz.ratio

    def tile(f, t):
        return ext[f, :, LANES * t : LANES * (t + 1)]

    kept = {}

    def zonal(t):
        if t not in kept:
            thick_e = ring.east("h", t, functools.partial(tile, 0))
            wind_e = ring.east("u", t, functools.partial(tile, 2))
            flux = 0.25 * (tile(2, t) + wind_e) * (tile(0, t) + thick_e) * inv_cos
            if t == tiles - 1:
                flux = jnp.where(lane < sz.tail - LEVELS, flux, 0.0)
            kept[t] = (flux, thick_e)
        return kept[t]

    for t in range(tiles):
        flux, thick_e = zonal(t)
        thick, wind_v, wind_u = tile(0, t), tile(1, t), tile(2, t)
        flux_w = ring.west("f", t, lambda s: zonal(s)[0])
        thick_w = ring.west("hw", t, functools.partial(tile, 0))
        thick_n = north(thick)
        flux_n = (0.25 * ratio) * (wind_v + north(wind_v)) * (thick + thick_n) * cos_face
        thick_tend = -((flux - flux_w) + (flux_n - south(flux_n)) * inv_cos)
        wind_u_tend = sin_centre * wind_v - (thick_e - thick_w) * (0.5 * inv_cos)
        wind_v_tend = -sin_centre * wind_u - (0.5 * ratio) * (thick_n - south(thick))
        extra = 0.0
        if t == tiles - 1:
            last = sz.tail - LEVELS
            columns = [(tile(0, 0), 0), (thick, last), (tile(2, 0), 0), (wind_u, last)]
            for k, (source, at) in reversed(list(enumerate(columns))):
                to = sz.tail + LEVELS * k
                extra = jnp.where(lane < to + LEVELS, pltpu.roll(source, (to - at) % LANES, 1), extra)
        for f, tend in enumerate((thick_tend, wind_u_tend, wind_v_tend, thick)):
            if sz.near_only:
                alone = jnp.where(band < sz.n_lat // 2, tend[:1], tend[rows - 1 : rows])
                if t == tiles - 1:
                    alone = jnp.where(lane[:1] < sz.tail, alone, 0.0)
                pole_ref[stack * f + t : stack * f + t + 1] = alone
            if f == 3:
                continue
            if t == tiles - 1:
                tend = jnp.where(lane < sz.tail, tend, extra)
            if sz.near_only:
                tend = jnp.where(even, north(tend), tend)
            tend_ref[pl.ds(stack * work * f + t, work, stride=stack), :] = tend[:work]
    for f in range(3):
        for t in range(tiles, stack):
            tend_ref[pl.ds(stack * work * f + t, work, stride=stack), :] = jnp.zeros((work, LANES), jnp.float32)
    used, sent = stack * sz.units, sz.n_lon * sz.size
    if used < sent:
        tend_ref[used:sent, :] = jnp.zeros((sent - used, LANES), jnp.float32)
    sides = [sides_ref[:SIDE_ROWS], sides_ref[SIDE_ROWS:]]
    if sz.near_only:
        sums = pole_sums(sz, pole_ref, wave_ref, extra, band)
        sides = [side + sums for side in sides]
    here = lax.axis_index("lon")
    for k, out_ref in enumerate(out_refs):
        out_ref[: sz.size] = tend_ref[sz.piece(k), :]
        eastward = sz.partner(k) == lax.rem(here + 1, sz.n_lon)
        out_ref[sz.size :] = jnp.where(eastward, sides[1], sides[0])


def pole_sums(sz, pole_ref, wave_ref, extra, band):
    stack, rows = sz.stack, sz.rows
    lane = lax.broadcasted_iota(jnp.int32, (SIDE_ROWS, LANES), 1)
    row = lax.broadcasted_iota(jnp.int32, (SIDE_ROWS, LANES), 0)
    found = jnp.zeros((SIDE_ROWS, LANES), jnp.float32)

    def put(place, value):
        at_row, at = spare(6 + place)
        return jnp.where((row == at_row) & (lane >= at) & (lane < at + LEVELS), value, found)

    for f in range(4):
        if sz.tiles < stack:
            pole_ref[stack * f + sz.tiles : stack * (f + 1)] = jnp.zeros((stack - sz.tiles, LANES), jnp.float32)
        values = pole_ref[stack * f : stack * (f + 1)]
        for k, terms in enumerate((values, values * wave_ref[0], values * wave_ref[1])):
            total = jnp.sum(terms, axis=0, keepdims=True)
            for step in (64, 32, 16):
                total = total + pltpu.roll(total, step, 1)
            found = put(3 * f + k, total)
    beside = jnp.where(band < sz.n_lat // 2, extra[:1], extra[rows - 1 : rows])
    for k in range(4):
        found = put(12 + k, pltpu.roll(beside, (spare(18 + k)[1] - sz.tail - LEVELS * k) % LANES, 1))
    return found


def pole_waves(sz, rows_in, inv_cos, sign):
    n_lon = sz.n_lon
    lane = lax.broadcasted_iota(jnp.int32, (1, LANES), 1)

    def value(s, place):
        row, at = spare(6 + place)
        return pltpu.roll(rows_in[s % n_lon, row : row + 1], -at % LANES, 1)

    theta = 2 * math.pi / sz.nlon
    ends = (1.0, math.cos(theta * (sz.columns - 1)), math.sin(theta * (sz.columns - 1)))
    sums = [[[value(s, 3 * f + k) for k in range(3)] for f in range(4)] for s in range(n_lon)]
    for s in range(n_lon):
        thick_w, thick_e = value(s, 13), value(s + 1, 12)
        flux = 0.25 * (value(s, 15) + value(s + 1, 14)) * (thick_w + thick_e) * inv_cos
        slope = 0.5 * inv_cos
        after = (s + 1) % n_lon
        for f, (west_of, east_of) in enumerate(((flux, flux), (slope * thick_e, slope * thick_w))):
            for k in range(3):
                sums[s][f][k] = sums[s][f][k] - west_of * ends[k]
            for k in range(2):
                sums[after][f][k] = sums[after][f][k] + east_of
    result = []
    for f in range(3):
        waves_of = [0.0, 0.0, 0.0]
        for s in range(n_lon):
            level, cosine, sine = sums[s][f]
            if f == 2:
                level = level + (0.5 * sz.ratio) * sign * sums[s][3][0]
                cosine = cosine - (0.5 * sz.ratio) * sign * sums[s][3][1]
                sine = sine - (0.5 * sz.ratio) * sign * sums[s][3][2]
            c, d = math.cos(2 * math.pi * s / n_lon), math.sin(2 * math.pi * s / n_lon)
            waves_of[0] = waves_of[0] + level
            waves_of[1] = waves_of[1] + (c * cosine - d * sine)
            waves_of[2] = waves_of[2] + (d * cosine + c * sine)
        spread = []
        for k, total in enumerate(waves_of):
            total = jnp.where(lane < LEVELS, total * ((1.0 if k == 0 else 2.0) / sz.nlon), 0.0)
            for step in (16, 32, 64):
                total = total + pltpu.roll(total, step, 1)
            spread.append(total)
        result.append(spread)
    return result


def unfolded(sides):
    lane = lax.broadcasted_iota(jnp.int32, (1, LANES), 1)
    start, width = spare(0)[1], 3 * LEVELS
    ninth = jnp.where(
        lane < width,
        pltpu.roll(sides[0:1], -start % LANES, 1),
        pltpu.roll(sides[1:2], (width - start) % LANES, 1),
    )
    return jnp.concatenate([sides, jnp.broadcast_to(ninth, sides.shape)], axis=0)


def rest_kernel(sz, masks_ref, h_ref, w_ref, q_ref, near_h_ref, near_w_ref, near_q_ref, far_ref, geo_ref, wave_ref, after_ref, *refs):
    met_refs, (new_w_ref, new_h_ref, mass_ref, ext, pole_in) = refs[: sz.n_lon], refs[sz.n_lon :]
    band = lax.axis_index("lat")
    ring = Tiles(sz)
    lane = ring.lane
    tiles, rows = sz.tiles, sz.rows
    for f in range(6):
        if f < 2 or f == 5:
            value = (h_ref[...], w_ref[:, 1, :], w_ref[:, 0, :])[min(f, 2)]
        else:
            value = q_ref[f - 2].astype(jnp.float32)
        ext[f, :rows, : sz.merged] = value
    add_rows(sz, ext, near_h_ref, near_w_ref, near_q_ref, far_ref)
    lane9 = lane[:rows]
    here = lax.axis_index("lon")
    from_e = from_w = met_refs[0][sz.size :]
    for k, met_ref in enumerate(met_refs):
        eastward = lax.rem(sz.partner(k) - here + sz.n_lon, sz.n_lon)
        pole_in[eastward] = met_ref[sz.size :]
        from_e = jnp.where(sz.partner(k) == lax.rem(here + 1, sz.n_lon), met_ref[sz.size :], from_e)
        from_w = jnp.where(sz.partner(k) == lax.rem(here + sz.n_lon - 1, sz.n_lon), met_ref[sz.size :], from_w)
    from_e, from_w = unfolded(from_e), unfolded(from_w)
    for place, f in enumerate((0, 5, 2, 3, 4)):
        after = pltpu.roll(from_e, (sz.tail - LEVELS * place) % LANES, 1)[:rows]
        before = pltpu.roll(from_w, (LANES - LEVELS - LEVELS * place) % LANES, 1)[:rows]
        own = ext[f, :rows, sz.end :]
        edge = jnp.where(lane9 < LANES - LEVELS, after, before)
        ext[f, :rows, sz.end :] = jnp.where(lane9 < sz.tail, own, edge)
    inv_cos, sin_centre, cos_face = geo_ref[band, 0], geo_ref[band, 1], geo_ref[band, 2]
    ratio = sz.ratio

    plain, alone = masks_ref[0], masks_ref[1]
    if sz.near_only:
        band = lax.axis_index("lat")
        low = band < sz.n_lat // 2
        pole_cos = jnp.where(low, inv_cos[:1], inv_cos[rows - 1 : rows])
        kept_waves = pole_waves(sz, pole_in, pole_cos, jnp.where(low, 1.0, -1.0))

    def stepped(f, t, value, tend):
        value = value + plain * tend
        if sz.near_only:
            level, cosine, sine = kept_waves[f]
            wave = level + cosine * wave_ref[0, t : t + 1] + sine * wave_ref[1, t : t + 1]
            value = value + alone * wave
        return value

    def tile(f, t):
        return ext[f, :, LANES * t : LANES * (t + 1)]

    kept = {}

    def zonal(t):
        if t not in kept:
            thick_e = ring.east("h", t, functools.partial(tile, 0))
            wind_e = ring.east("u", t, functools.partial(tile, 5))
            flux = 0.25 * (tile(5, t) + wind_e) * (tile(0, t) + thick_e) * inv_cos
            parts = []
            for k in range(3):
                q = tile(2 + k, t)
                q_e = ring.east(k, t, functools.partial(tile, 2 + k))
                parts.append(DIFFUSION * (q_e - q) - flux * (0.5 * (q + q_e)))
            kept[t] = (flux, thick_e, parts)
        return kept[t]

    for t in range(tiles):
        span = sz.span(t)
        lanes = slice(LANES * t, LANES * t + span)
        flux, thick_e, parts = zonal(t)
        thick, wind_u, wind_v = tile(0, t), tile(5, t), tile(1, t)
        flux_w = ring.west("f", t, lambda s: zonal(s)[0])
        thick_w = ring.west("hw", t, functools.partial(tile, 0))
        thick_n = north(thick)
        flux_n = (0.25 * ratio) * (wind_v + north(wind_v)) * (thick + thick_n) * cos_face
        thick_tend = -((flux - flux_w) + (flux_n - south(flux_n)) * inv_cos)
        wind_u_tend = sin_centre * wind_v - (thick_e - thick_w) * (0.5 * inv_cos)
        wind_v_tend = -sin_centre * wind_u - (0.5 * ratio) * (thick_n - south(thick))
        new_h_ref[:, lanes] = stepped(0, t, thick, thick_tend)[:rows, :span]
        new_w_ref[0, :, lanes] = stepped(1, t, wind_u, wind_u_tend)[:rows, :span]
        new_w_ref[1, :, lanes] = stepped(2, t, wind_v, wind_v_tend)[:rows, :span]
        for k in range(3):
            q = tile(2 + k, t)
            q_n = north(q)
            zonal_part = parts[k] - ring.west(("p", k), t, lambda s: zonal(s)[2][k])
            lap = q_n + south(q) - 2.0 * q
            over = flux_n * (0.5 * (q + q_n))
            merid_part = DIFFUSION * lap - (over - south(over)) * inv_cos
            mass = thick * q + TIME_STEP * (zonal_part + merid_part)
            mass_ref[k, :, lanes] = mass[:rows, :span].astype(jnp.bfloat16)


def sin_pi(y):
    y = jnp.maximum(jnp.minimum(y, 1.0 - y), -1.0 - y)
    s = y * y
    series = [(-1) ** i * math.pi ** (2 * i + 1) / math.factorial(2 * i + 1) for i in range(6)]
    total = series[-1]
    for factor in reversed(series[:-1]):
        total = total * s + factor
    return total * y


def share_of(sz, i):
    unit = lax.axis_index("lon") * sz.share + i
    return unit // sz.work, sz.first() + lax.rem(unit, sz.work)


def weights_kernel(sz, cut_ref, n_ref, inverse_ref, after_ref, weights_ref, masks_ref):
    band = lax.axis_index("lat")
    row = lax.broadcasted_iota(jnp.int32, (EXT_ROWS, LANES), 0)
    cuts = jnp.full((EXT_ROWS, LANES), sz.nlon // 2, jnp.int32)
    for j in range(sz.rows):
        cuts = jnp.where(row == j, cut_ref[band * sz.rows + j], cuts)
    plain, alone = cuts >= sz.nlon // 2, sz.at_pole(row)
    masks_ref[0] = jnp.where(plain, TIME_STEP, 0.0)
    masks_ref[1] = jnp.where(alone, TIME_STEP, 0.0)
    masks_ref[2] = jnp.where(plain | alone, 0.0, TIME_STEP)
    size = PER_TILE * sz.stack
    for i in range(sz.share):
        width = (2 * cut_ref[band * sz.rows + share_of(sz, i)[1]] + 1).astype(jnp.float32)
        n = n_ref[...]
        turns = n * width
        turns = turns - jnp.round(turns * (0.5 / sz.nlon)) * (2.0 * sz.nlon)
        weights = sin_pi(turns * (1.0 / sz.nlon)) * inverse_ref[...]
        weights = jnp.where(n == 0.0, width * (1.0 / sz.nlon), weights)
        weights_ref[size * i : size * (i + 1)] = weights.astype(jnp.bfloat16)


def pass_kernel(sz, piece_ref, after_ref, also_after_ref, out_ref):
    out_ref[...] = piece_ref[...]


def filter_kernel(sz, weights_ref, geo_ref, *refs):
    n_lon, stack, share = sz.n_lon, sz.stack, sz.share
    in_refs, out_refs, (gathered, results) = refs[:n_lon], refs[n_lon : 2 * n_lon], refs[2 * n_lon :]
    for k, in_ref in enumerate(in_refs):
        gathered[sz.partner(k), : sz.size] = in_ref[: sz.size]

    band = lax.axis_index("lat")
    lane = lax.broadcasted_iota(jnp.int32, (share, LANES), 1)
    place = lax.broadcasted_iota(jnp.int32, (share, LANES), 0)
    by_flux = by_thick = jnp.zeros((share, LANES), jnp.float32)
    for i in range(share):
        field, row = share_of(sz, i)
        inv_cos = geo_ref[band, 0, pl.ds(row, 1), :]
        by_flux = jnp.where((place == i) & (field == 0), inv_cos, by_flux)
        by_thick = jnp.where((place == i) & (field == 1), 0.5 * inv_cos, by_thick)
    sides = [gathered[s, pl.ds(sz.tiles - 1, share, stride=stack), :] for s in range(n_lon)]

    def column(s, k):
        return pltpu.roll(sides[s % n_lon], (-sz.tail - LEVELS * k) % LANES, 1)

    for s in range(n_lon):
        thick_w, thick_e = column(s, 1), column(s + 1, 0)
        flux = 0.25 * (column(s, 3) + column(s + 1, 2)) * (thick_w + thick_e) * by_flux
        west_of, east_of = flux + by_thick * thick_e, flux + by_thick * thick_w
        at = pl.ds(sz.tiles - 1, share, stride=stack)
        own = gathered[s, at, :]
        own = own - jnp.where(lane >= sz.tail - LEVELS, pltpu.roll(west_of, sz.tail - LEVELS, 1), 0.0)
        gathered[s, at, :] = jnp.where(lane < sz.tail, own, 0.0)
        at = pl.ds(0, share, stride=stack)
        after = (s + 1) % n_lon
        gathered[after, at, :] = gathered[after, at, :] + jnp.where(lane < LEVELS, east_of, 0.0)

    wide = lax.broadcasted_iota(jnp.int32, (stack, LANES), 1)
    rows = PER_TILE * stack
    for i in range(share):
        here = slice(stack * i, stack * (i + 1))
        pieces = [gathered[s, here].astype(jnp.bfloat16) for s in range(n_lon)]
        circle = jnp.concatenate([jnp.concatenate(pieces[s:] + pieces[:s], axis=0) for s in range(n_lon)], axis=1)
        spread = jnp.dot(weights_ref[rows * i : rows * (i + 1)], circle, preferred_element_type=jnp.float32)
        for s in range(n_lon):
            same = spread[:stack, LANES * s : LANES * (s + 1)]
            carried = None
            for e in range(1, PER_TILE):
                part = spread[stack * e : stack * (e + 1), LANES * s : LANES * (s + 1)]
                part = pltpu.roll(part, LEVELS * e, 1)
                inside = wide >= LEVELS * e
                same = same + jnp.where(inside, part, 0.0)
                over = jnp.where(inside, 0.0, part)
                carried = over if carried is None else carried + over
            results[s, here] = pltpu.roll(same, stack - 1, 0) + carried
    for k, out_ref in enumerate(out_refs):
        out_ref[...] = results[sz.partner(k, True), : sz.size]


def finish_kernel(sz, masks_ref, base_w_ref, base_h_ref, *refs):
    back_refs, (new_w_ref, new_h_ref, back_ref) = refs[: sz.n_lon], refs[sz.n_lon :]
    rows, work = sz.rows, sz.work
    for k, ref in enumerate(back_refs):
        back_ref[sz.piece(k, True), :] = ref[...]
    scale = masks_ref[2]
    even = lax.rem(lax.axis_index("lat"), 2) == 0
    for f in range(3):
        for t in range(sz.tiles):
            span = sz.span(t)
            lanes = slice(LANES * t, LANES * t + span)
            tend = back_ref[pl.ds(sz.stack * work * f + t, work, stride=sz.stack), :]
            if sz.near_only:
                tend = jnp.concatenate([tend, jnp.zeros((EXT_ROWS - work, LANES), jnp.float32)], axis=0)
                tend = jnp.where(even, south(tend), tend)
            change = (scale[:rows] * tend[:rows])[:, :span]
            if f == 0:
                new_h_ref[:, lanes] = base_h_ref[:, lanes] + change
            else:
                new_w_ref[:, f - 1, lanes] = base_w_ref[f - 1, :, lanes] + change


def local(winds, thickness, tracers, cutoff):
    n_lat = lax.axis_size("lat")
    n_lon = lax.axis_size("lon")
    rows, merged = thickness.shape
    sz = Sizes(rows, merged, n_lat, n_lon)
    f32 = jnp.float32
    vmem = pl.BlockSpec(memory_space=pltpu.VMEM)
    smem = pl.BlockSpec(memory_space=pltpu.SMEM)
    hbm = pl.BlockSpec(memory_space=pltpu.HBM)
    anywhere = pl.BlockSpec(memory_space=pl.ANY)

    def shaped(*shape):
        return jax.ShapeDtypeStruct(shape, f32)

    def call(kernel, name, in_specs, out_shape, scratch=(), limit=LIMIT):
        return pl.pallas_call(
            functools.partial(kernel, sz),
            out_shape=out_shape,
            in_specs=in_specs,
            out_specs=jax.tree.map(lambda _: vmem, out_shape),
            scratch_shapes=list(scratch),
            compiler_params=pltpu.CompilerParams(vmem_limit_bytes=limit),
            name=name,
        )

    geo = jnp.asarray(geometry(sz))
    wave = jnp.asarray(waves(sz))
    n, inverse = (jnp.asarray(table) for table in offsets(sz))

    wind_rows = jnp.swapaxes(winds, 0, 1)
    tracer_rows = jnp.swapaxes(tracers, 0, 1)
    far_row, near_row = shaped(5 * sz.stack, LANES), shaped(3 * sz.stack, LANES)
    kept = [((1,), f32), ((2,), f32), ((3,), jnp.bfloat16)]
    near_q, far_rows, sides = call(
        edges_kernel,
        "edges",
        [hbm] * 3,
        (near_row, far_row, shaped(2 * SIDE_ROWS, LANES)),
        [pltpu.VMEM((2,) + count + (merged,), dtype) for count, dtype in kept]
        + [
            pltpu.VMEM((rows,) + (count if count != (1,) else ()) + (lanes,), dtype)
            for lanes in (LANES, sz.tail)
            for count, dtype in kept
        ]
        + [pltpu.SemaphoreType.DMA((3, 4))],
        limit=MOST_VMEM,
    )(thickness, wind_rows, tracer_rows)

    near = [(band * n_lon + i, (band ^ 1) * n_lon + i) for band in range(n_lat) for i in range(n_lon)]
    far = []
    for band in range(n_lat):
        other = band - 1 if band % 2 == 0 else band + 1
        for i in range(n_lon):
            if 0 <= other < n_lat:
                far.append((band * n_lon + i, other * n_lon + i))
            else:
                far.append((band * n_lon + i, band * n_lon + (i + n_lon // 2) % n_lon))
    near_h = lax.ppermute(thickness, ("lat", "lon"), near)
    near_w = lax.ppermute(wind_rows, ("lat", "lon"), near)
    if not sz.near_only:
        far_rows = lax.ppermute(far_rows, ("lat", "lon"), far)

    def meetings(shares, back):
        order = [sz.turns(False, back), sz.turns(True, back)]
        got = [shares[0]]
        for k in range(1, n_lon):
            sectors = [(band, i, i ^ order[band % 2][k]) for band in range(n_lat) for i in range(n_lon)]
            got.append(lax.ppermute(shares[k], ("lat", "lon"), [(b * n_lon + i, b * n_lon + j) for b, i, j in sectors]))
        return got

    all_pieces = pltpu.VMEM((n_lon, sz.size + 8 * sz.stack, LANES), f32)
    all_units = pltpu.VMEM((n_lon * sz.size + 8 * sz.stack, LANES), f32)
    *tends, far_rows, near_q = call(
        polar_kernel,
        "polar",
        [vmem] * 9,
        [shaped(sz.size + SIDE_ROWS, LANES)] * n_lon + [far_row, near_row],
        [
            all_units,
            pltpu.VMEM((4 * sz.stack, LANES), f32),
            pltpu.VMEM((3, EXT_ROWS, sz.tiles * LANES), f32),
        ],
    )(thickness, wind_rows, near_h, near_w, sides, geo, wave, far_rows, near_q)
    met = meetings(tends, False)
    near_q = lax.ppermute(near_q, ("lat", "lon"), near)
    from_far = lax.ppermute(far_rows, ("lat", "lon"), far) if sz.near_only else far_rows
    weights, masks = call(
        weights_kernel,
        "weights",
        [smem, vmem, vmem, anywhere],
        (
            jax.ShapeDtypeStruct((sz.share * PER_TILE * sz.stack, n_lon * sz.stack), jnp.bfloat16),
            shaped(3, EXT_ROWS, LANES),
        ),
    )(cutoff, n, inverse, tends[0])
    worked = call(
        filter_kernel,
        "filter",
        [vmem] * 2 + [vmem] * n_lon,
        [shaped(sz.size, LANES)] * n_lon,
        [all_pieces, all_pieces],
    )(weights, geo, *met)
    held = call(pass_kernel, "pass", [vmem] + [anywhere] * 2, shaped(sz.size, LANES))(worked[-1], from_far, near_q)
    worked = [*worked[:-1], held]
    back = meetings(worked, True)

    base_w, base_h, mass = call(
        rest_kernel,
        "rest",
        [vmem] * 10 + [anywhere] + [vmem] * n_lon,
        (shaped(2, rows, merged), shaped(rows, merged), jax.ShapeDtypeStruct(tracers.shape, jnp.bfloat16)),
        [pltpu.VMEM((6, EXT_ROWS, sz.tiles * LANES), f32), pltpu.VMEM((n_lon, 8, LANES), f32)],
    )(masks, thickness, wind_rows, tracers, near_h, near_w, near_q, from_far, geo, wave, worked[0], *met)

    new_w, new_h = call(
        finish_kernel,
        "finish",
        [vmem] * (3 + n_lon),
        (shaped(*wind_rows.shape), shaped(rows, merged)),
        [all_units],
    )(masks, base_w, base_h, *back)
    return jnp.swapaxes(new_w, 0, 1), new_h, mass


def solution(mesh):
    in_specs = (P(None, "lat", "lon"), P("lat", "lon"), P(None, "lat", "lon"), P())
    out_specs = (P(None, "lat", "lon"), P("lat", "lon"), P(None, "lat", "lon"))
    return jax.shard_map(local, mesh=mesh, in_specs=in_specs, out_specs=out_specs, check_vma=False)
```

```python
import functools
import math

import jax
import jax.numpy as jnp
import numpy as np
from jax import lax
from jax.experimental import pallas as pl
from jax.experimental.pallas import tpu as pltpu
from jax.sharding import PartitionSpec as P

LEVELS = 16
TIME_STEP = 0.05
DIFFUSION = 0.5
LANES = 128
PER_TILE = LANES // LEVELS
SIDE_ROWS = 8
EXT_ROWS = 16
LIMIT = 48 * 1024 * 1024
MOST_VMEM = 64 * 1024 * 1024 - 10500 * 1024


class Sizes:
    def __init__(self, rows, merged, n_lat, n_lon):
        self.rows = rows
        self.merged = merged
        self.columns = merged // LEVELS
        self.n_lat = n_lat
        self.n_lon = n_lon
        self.nlat = rows * n_lat
        self.nlon = self.columns * n_lon
        self.ratio = 2.0 * self.nlat / self.nlon
        self.tiles = -(-merged // LANES)
        self.end = (self.tiles - 1) * LANES
        self.tail = merged - self.end
        self.stack = -(-(self.tiles + 1) // 8) * 8
        self.near_only = rows <= self.nlat // 6 < 2 * rows
        self.work = rows - 1 if self.near_only else rows
        self.units = 3 * self.work
        self.share = -(-self.units // n_lon)
        self.size = self.share * self.stack
        assert self.tail <= LANES - 4 * LEVELS and rows + 2 <= EXT_ROWS and n_lat % 2 == 0
        assert n_lon >= 4 and n_lon & (n_lon - 1) == 0 and rows == SIDE_ROWS + 1

    def span(self, tile):
        return self.tail if tile == self.tiles - 1 else LANES

    def first(self):
        return jnp.where(lax.rem(lax.axis_index("lat"), 2) == 0, 1, 0) if self.near_only else 0

    def at_pole(self, row):
        band = lax.axis_index("lat")
        pole = jnp.where(band == 0, 0, jnp.where(band == self.n_lat - 1, self.rows - 1, -1))
        return row == (pole if self.near_only else -1)

    def turns(self, odd):
        middle, last = list(range(1, self.n_lon - 1)), self.n_lon - 1
        return [0, middle[-1], last] + middle[-2::-1] if odd else [0, last] + middle

    def partner(self, k):
        odd = lax.rem(lax.axis_index("lat"), 2) == 1
        turn = jnp.where(odd, self.turns(True)[k], self.turns(False)[k])
        return jnp.bitwise_xor(lax.axis_index("lon"), turn)

    def piece(self, k):
        return pl.ds(pl.multiple_of(self.partner(k) * self.size, 8), self.size)


def geometry(sz):
    table = np.zeros((sz.n_lat, 3, EXT_ROWS, LANES), np.float64)

    def face(j):
        return math.sin((j + 1) * math.pi / sz.nlat) if 0 <= j < sz.nlat - 1 else 0.0

    for band in range(sz.n_lat):
        for row in range(sz.rows):
            j = band * sz.rows + row
            centre = (j + 0.5) * math.pi / sz.nlat - math.pi / 2
            table[band, 0, row] = 1.0 / math.cos(centre)
            table[band, 1, row] = math.sin(centre)
            table[band, 2, row] = face(j)
        table[band, 2, EXT_ROWS - 1] = face(band * sz.rows - 1)
    return table.astype(np.float32)


def offsets(sz):
    shift, out_tile = np.divmod(np.arange(PER_TILE * sz.stack), sz.stack)
    sector, in_tile = np.divmod(np.arange(sz.n_lon * sz.stack), sz.stack)
    n = (PER_TILE * (out_tile - 1) + shift)[:, None] - (PER_TILE * in_tile + sz.columns * sector)[None, :]
    n = (n + sz.nlon // 2) % sz.nlon - sz.nlon // 2
    with np.errstate(divide="ignore"):
        inverse = np.where(n == 0, 0.0, 1.0 / (sz.nlon * np.sin(np.pi * n / sz.nlon)))
    return n.astype(np.float32), inverse.astype(np.float32)


def waves(sz):
    column = PER_TILE * np.arange(sz.stack)[:, None] + np.arange(LANES)[None, :] // LEVELS
    angle = 2 * np.pi * column / sz.nlon
    return np.stack([np.cos(angle), np.sin(angle)]).astype(np.float32)


def spare(place):
    row, group = divmod(place, 3)
    return row, LEVELS * (5 + group)


def edges_kernel(sz, h_hbm, w_hbm, q_hbm, near_ref, far_ref, sides_ref, *scratch):
    row_refs, first_refs, last_refs, sems = scratch[:3], scratch[3:6], scratch[6:9], scratch[9]
    rows, last = sz.rows, sz.rows - 1
    even = lax.rem(lax.axis_index("lat"), 2) == 0
    copies = []
    for i, source in enumerate((h_hbm, w_hbm, q_hbm)):
        for k, row in enumerate((0, last)):
            one = source.at[pl.ds(row, 1)] if i == 0 else source.at[row]
            copies.append(pltpu.make_async_copy(one, row_refs[i].at[k], sems.at[i, k]))
        for k, (start, to) in enumerate(((0, first_refs[i]), (sz.end, last_refs[i]))):
            lanes = pl.ds(start, to.shape[-1])
            cut = source.at[:, lanes] if i == 0 else source.at[:, :, lanes]
            copies.append(pltpu.make_async_copy(cut, to, sems.at[i, 2 + k]))
    for copy in copies:
        copy.start()
    for copy in copies:
        copy.wait()
    h_rows, w_rows, q_rows = row_refs
    for t in range(sz.tiles):
        wide = sz.span(t)
        lanes = slice(LANES * t, LANES * t + wide)
        q = [q_rows[k, :, lanes].astype(jnp.float32) for k in range(2)]
        for f in range(5):
            if f == 0:
                first, final = h_rows[0, :, lanes], h_rows[1, :, lanes]
            elif f == 1:
                first, final = w_rows[0, 1:2, lanes], w_rows[1, 1:2, lanes]
            else:
                first, final = q[0][f - 2 : f - 1], q[1][f - 2 : f - 1]
                at = sz.stack * (f - 2) + t
                near_ref[at : at + 1, :wide] = jnp.where(even, final, first)
            at = sz.stack * f + t
            far_ref[at : at + 1, :wide] = jnp.where(even, first, final)
    sides_ref[...] = jnp.zeros(sides_ref.shape, jnp.float32)
    for k, (refs, at) in enumerate(((first_refs, 0), (last_refs, sz.tail - LEVELS))):
        columns = slice(at, at + LEVELS)
        for f in range(5):
            if f == 0:
                value = refs[0][:, columns]
            elif f == 1:
                value = refs[1][:, 0, columns]
            else:
                value = refs[2][:, f - 2, columns].astype(jnp.float32)
            start = SIDE_ROWS * k
            sides_ref[start : start + SIDE_ROWS, LEVELS * f : LEVELS * (f + 1)] = value[:SIDE_ROWS]
            row, lane = spare(f)
            sides_ref[start + row : start + row + 1, lane : lane + LEVELS] = value[SIDE_ROWS:]


def add_rows(sz, ext, near_h_ref, near_w_ref, near_q_ref, far_ref):
    band = lax.axis_index("lat")
    even = lax.rem(band, 2) == 0
    over_pole = (band == 0) | (band == sz.n_lat - 1)
    last = sz.rows - 1
    for f in range(2 if near_q_ref is None else 5):
        flip = jnp.where(over_pole, -1.0, 1.0) if f == 1 else 1.0
        for t in range(sz.tiles):
            lanes = slice(LANES * t, LANES * t + sz.span(t))
            if f == 0:
                near = jnp.where(even, near_h_ref[0:1, lanes], near_h_ref[last : sz.rows, lanes])
            elif f == 1:
                near = jnp.where(even, near_w_ref[0, 1:2, lanes], near_w_ref[last, 1:2, lanes])
            else:
                at = sz.stack * (f - 2) + t
                near = near_q_ref[at : at + 1, : sz.span(t)]
            at = sz.stack * f + t
            far = jnp.zeros_like(near) if far_ref is None else far_ref[at : at + 1, : sz.span(t)] * flip
            ext[f, sz.rows : sz.rows + 1, lanes] = jnp.where(even, near, far)
            ext[f, EXT_ROWS - 1 : EXT_ROWS, lanes] = jnp.where(even, far, near)


class Tiles:
    def __init__(self, sz):
        self.sz = sz
        self.lane = lax.broadcasted_iota(jnp.int32, (EXT_ROWS, LANES), 1)
        self.turned = {}

    def turn(self, name, t, value, step):
        key = (name, t % self.sz.tiles, step)
        if key not in self.turned:
            self.turned[key] = pltpu.roll(value(t % self.sz.tiles), step % LANES, 1)
        return self.turned[key]

    def east(self, name, t, value):
        here = self.turn(name, t, value, -LEVELS)
        return jnp.where(self.lane < LANES - LEVELS, here, self.turn(name, t + 1, value, -LEVELS))

    def west(self, name, t, value):
        here = self.turn(name, t, value, LEVELS)
        return jnp.where(self.lane >= LEVELS, here, self.turn(name, t - 1, value, LEVELS))


def north(value):
    return pltpu.roll(value, EXT_ROWS - 1, 0)


def south(value):
    return pltpu.roll(value, 1, 0)


def polar_kernel(sz, h_ref, w_ref, near_h_ref, near_w_ref, sides_ref, geo_ref, wave_ref, *refs):
    far_ref, refs = (None, refs) if sz.near_only else (refs[0], refs[1:])
    out_refs, (tend_ref, pole_ref, ext) = refs[:-3], refs[-3:]
    band = lax.axis_index("lat")
    ring = Tiles(sz)
    lane = ring.lane
    tiles, stack, rows, work = sz.tiles, sz.stack, sz.rows, sz.work
    even = lax.rem(band, 2) == 0
    for f, value in enumerate((h_ref[...], w_ref[:, 1, :], w_ref[:, 0, :])):
        ext[f, :rows, sz.end :] = jnp.zeros((rows, LANES), jnp.float32)
        ext[f, :rows, : sz.merged] = value
    add_rows(sz, ext, near_h_ref, near_w_ref, None, far_ref)
    inv_cos, sin_centre, cos_face = geo_ref[band, 0], geo_ref[band, 1], geo_ref[band, 2]
    ratio = sz.ratio

    def tile(f, t):
        return ext[f, :, LANES * t : LANES * (t + 1)]

    kept = {}

    def zonal(t):
        if t not in kept:
            thick_e = ring.east("h", t, functools.partial(tile, 0))
            wind_e = ring.east("u", t, functools.partial(tile, 2))
            flux = 0.25 * (tile(2, t) + wind_e) * (tile(0, t) + thick_e) * inv_cos
            if t == tiles - 1:
                flux = jnp.where(lane < sz.tail - LEVELS, flux, 0.0)
            kept[t] = (flux, thick_e)
        return kept[t]

    for t in range(tiles):
        flux, thick_e = zonal(t)
        thick, wind_v, wind_u = tile(0, t), tile(1, t), tile(2, t)
        flux_w = ring.west("f", t, lambda s: zonal(s)[0])
        thick_w = ring.west("hw", t, functools.partial(tile, 0))
        thick_n = north(thick)
        flux_n = (0.25 * ratio) * (wind_v + north(wind_v)) * (thick + thick_n) * cos_face
        thick_tend = -((flux - flux_w) + (flux_n - south(flux_n)) * inv_cos)
        wind_u_tend = sin_centre * wind_v - (thick_e - thick_w) * (0.5 * inv_cos)
        wind_v_tend = -sin_centre * wind_u - (0.5 * ratio) * (thick_n - south(thick))
        extra = 0.0
        if t == tiles - 1:
            last = sz.tail - LEVELS
            columns = [(tile(0, 0), 0), (thick, last), (tile(2, 0), 0), (wind_u, last)]
            for k, (source, at) in reversed(list(enumerate(columns))):
                to = sz.tail + LEVELS * k
                extra = jnp.where(lane < to + LEVELS, pltpu.roll(source, (to - at) % LANES, 1), extra)
        for f, tend in enumerate((thick_tend, wind_u_tend, wind_v_tend, thick)):
            if sz.near_only:
                alone = jnp.where(band < sz.n_lat // 2, tend[:1], tend[rows - 1 : rows])
                if t == tiles - 1:
                    alone = jnp.where(lane[:1] < sz.tail, alone, 0.0)
                pole_ref[stack * f + t : stack * f + t + 1] = alone
            if f == 3:
                continue
            if t == tiles - 1:
                tend = jnp.where(lane < sz.tail, tend, extra)
            if sz.near_only:
                tend = jnp.where(even, north(tend), tend)
            tend_ref[pl.ds(stack * work * f + t, work, stride=stack), :] = tend[:work]
    for f in range(3):
        for t in range(tiles, stack):
            tend_ref[pl.ds(stack * work * f + t, work, stride=stack), :] = jnp.zeros((work, LANES), jnp.float32)
    used, sent = stack * sz.units, sz.n_lon * sz.size
    if used < sent:
        tend_ref[used:sent, :] = jnp.zeros((sent - used, LANES), jnp.float32)
    sides = [sides_ref[:SIDE_ROWS], sides_ref[SIDE_ROWS:]]
    if sz.near_only:
        sums = pole_sums(sz, pole_ref, wave_ref, extra, band)
        sides = [side + sums for side in sides]
    here = lax.axis_index("lon")
    for k, out_ref in enumerate(out_refs):
        out_ref[: sz.size] = tend_ref[sz.piece(k), :]
        eastward = sz.partner(k) == lax.rem(here + 1, sz.n_lon)
        out_ref[sz.size :] = jnp.where(eastward, sides[1], sides[0])


def pole_sums(sz, pole_ref, wave_ref, extra, band):
    stack, rows = sz.stack, sz.rows
    lane = lax.broadcasted_iota(jnp.int32, (SIDE_ROWS, LANES), 1)
    row = lax.broadcasted_iota(jnp.int32, (SIDE_ROWS, LANES), 0)
    found = jnp.zeros((SIDE_ROWS, LANES), jnp.float32)

    def put(place, value):
        at_row, at = spare(6 + place)
        return jnp.where((row == at_row) & (lane >= at) & (lane < at + LEVELS), value, found)

    for f in range(4):
        if sz.tiles < stack:
            pole_ref[stack * f + sz.tiles : stack * (f + 1)] = jnp.zeros((stack - sz.tiles, LANES), jnp.float32)
        values = pole_ref[stack * f : stack * (f + 1)]
        for k, terms in enumerate((values, values * wave_ref[0], values * wave_ref[1])):
            total = jnp.sum(terms, axis=0, keepdims=True)
            for step in (64, 32, 16):
                total = total + pltpu.roll(total, step, 1)
            found = put(3 * f + k, total)
    beside = jnp.where(band < sz.n_lat // 2, extra[:1], extra[rows - 1 : rows])
    for k in range(4):
        found = put(12 + k, pltpu.roll(beside, (spare(18 + k)[1] - sz.tail - LEVELS * k) % LANES, 1))
    return found


def pole_waves(sz, rows_in, inv_cos, sign):
    n_lon = sz.n_lon
    lane = lax.broadcasted_iota(jnp.int32, (1, LANES), 1)

    def value(s, place):
        row, at = spare(6 + place)
        return pltpu.roll(rows_in[s % n_lon, row : row + 1], -at % LANES, 1)

    theta = 2 * math.pi / sz.nlon
    ends = (1.0, math.cos(theta * (sz.columns - 1)), math.sin(theta * (sz.columns - 1)))
    sums = [[[value(s, 3 * f + k) for k in range(3)] for f in range(4)] for s in range(n_lon)]
    for s in range(n_lon):
        thick_w, thick_e = value(s, 13), value(s + 1, 12)
        flux = 0.25 * (value(s, 15) + value(s + 1, 14)) * (thick_w + thick_e) * inv_cos
        slope = 0.5 * inv_cos
        after = (s + 1) % n_lon
        for f, (west_of, east_of) in enumerate(((flux, flux), (slope * thick_e, slope * thick_w))):
            for k in range(3):
                sums[s][f][k] = sums[s][f][k] - west_of * ends[k]
            for k in range(2):
                sums[after][f][k] = sums[after][f][k] + east_of
    result = []
    for f in range(3):
        waves_of = [0.0, 0.0, 0.0]
        for s in range(n_lon):
            level, cosine, sine = sums[s][f]
            if f == 2:
                level = level + (0.5 * sz.ratio) * sign * sums[s][3][0]
                cosine = cosine - (0.5 * sz.ratio) * sign * sums[s][3][1]
                sine = sine - (0.5 * sz.ratio) * sign * sums[s][3][2]
            c, d = math.cos(2 * math.pi * s / n_lon), math.sin(2 * math.pi * s / n_lon)
            waves_of[0] = waves_of[0] + level
            waves_of[1] = waves_of[1] + (c * cosine - d * sine)
            waves_of[2] = waves_of[2] + (d * cosine + c * sine)
        spread = []
        for k, total in enumerate(waves_of):
            total = jnp.where(lane < LEVELS, total * ((1.0 if k == 0 else 2.0) / sz.nlon), 0.0)
            for step in (16, 32, 64):
                total = total + pltpu.roll(total, step, 1)
            spread.append(total)
        result.append(spread)
    return result


def unfolded(sides):
    lane = lax.broadcasted_iota(jnp.int32, (1, LANES), 1)
    start, width = spare(0)[1], 3 * LEVELS
    ninth = jnp.where(
        lane < width,
        pltpu.roll(sides[0:1], -start % LANES, 1),
        pltpu.roll(sides[1:2], (width - start) % LANES, 1),
    )
    return jnp.concatenate([sides, jnp.broadcast_to(ninth, sides.shape)], axis=0)


def rest_kernel(sz, masks_ref, h_ref, w_ref, q_ref, near_h_ref, near_w_ref, near_q_ref, far_ref, geo_ref, wave_ref, after_ref, *refs):
    met_refs, (new_w_ref, new_h_ref, mass_ref, ext, pole_in) = refs[: sz.n_lon], refs[sz.n_lon :]
    band = lax.axis_index("lat")
    ring = Tiles(sz)
    lane = ring.lane
    tiles, rows = sz.tiles, sz.rows
    for f in range(6):
        if f < 2 or f == 5:
            value = (h_ref[...], w_ref[:, 1, :], w_ref[:, 0, :])[min(f, 2)]
        else:
            value = q_ref[f - 2].astype(jnp.float32)
        ext[f, :rows, : sz.merged] = value
    add_rows(sz, ext, near_h_ref, near_w_ref, near_q_ref, far_ref)
    lane9 = lane[:rows]
    here = lax.axis_index("lon")
    from_e = from_w = met_refs[0][sz.size :]
    for k, met_ref in enumerate(met_refs):
        eastward = lax.rem(sz.partner(k) - here + sz.n_lon, sz.n_lon)
        pole_in[eastward] = met_ref[sz.size :]
        from_e = jnp.where(sz.partner(k) == lax.rem(here + 1, sz.n_lon), met_ref[sz.size :], from_e)
        from_w = jnp.where(sz.partner(k) == lax.rem(here + sz.n_lon - 1, sz.n_lon), met_ref[sz.size :], from_w)
    from_e, from_w = unfolded(from_e), unfolded(from_w)
    for place, f in enumerate((0, 5, 2, 3, 4)):
        after = pltpu.roll(from_e, (sz.tail - LEVELS * place) % LANES, 1)[:rows]
        before = pltpu.roll(from_w, (LANES - LEVELS - LEVELS * place) % LANES, 1)[:rows]
        own = ext[f, :rows, sz.end :]
        edge = jnp.where(lane9 < LANES - LEVELS, after, before)
        ext[f, :rows, sz.end :] = jnp.where(lane9 < sz.tail, own, edge)
    inv_cos, sin_centre, cos_face = geo_ref[band, 0], geo_ref[band, 1], geo_ref[band, 2]
    ratio = sz.ratio

    plain, alone = masks_ref[0], masks_ref[1]
    if sz.near_only:
        band = lax.axis_index("lat")
        low = band < sz.n_lat // 2
        pole_cos = jnp.where(low, inv_cos[:1], inv_cos[rows - 1 : rows])
        kept_waves = pole_waves(sz, pole_in, pole_cos, jnp.where(low, 1.0, -1.0))

    def stepped(f, t, value, tend):
        value = value + plain * tend
        if sz.near_only:
            level, cosine, sine = kept_waves[f]
            wave = level + cosine * wave_ref[0, t : t + 1] + sine * wave_ref[1, t : t + 1]
            value = value + alone * wave
        return value

    def tile(f, t):
        return ext[f, :, LANES * t : LANES * (t + 1)]

    kept = {}

    def zonal(t):
        if t not in kept:
            thick_e = ring.east("h", t, functools.partial(tile, 0))
            wind_e = ring.east("u", t, functools.partial(tile, 5))
            flux = 0.25 * (tile(5, t) + wind_e) * (tile(0, t) + thick_e) * inv_cos
            parts = []
            for k in range(3):
                q = tile(2 + k, t)
                q_e = ring.east(k, t, functools.partial(tile, 2 + k))
                parts.append(DIFFUSION * (q_e - q) - flux * (0.5 * (q + q_e)))
            kept[t] = (flux, thick_e, parts)
        return kept[t]

    for t in range(tiles):
        span = sz.span(t)
        lanes = slice(LANES * t, LANES * t + span)
        flux, thick_e, parts = zonal(t)
        thick, wind_u, wind_v = tile(0, t), tile(5, t), tile(1, t)
        flux_w = ring.west("f", t, lambda s: zonal(s)[0])
        thick_w = ring.west("hw", t, functools.partial(tile, 0))
        thick_n = north(thick)
        flux_n = (0.25 * ratio) * (wind_v + north(wind_v)) * (thick + thick_n) * cos_face
        thick_tend = -((flux - flux_w) + (flux_n - south(flux_n)) * inv_cos)
        wind_u_tend = sin_centre * wind_v - (thick_e - thick_w) * (0.5 * inv_cos)
        wind_v_tend = -sin_centre * wind_u - (0.5 * ratio) * (thick_n - south(thick))
        new_h_ref[:, lanes] = stepped(0, t, thick, thick_tend)[:rows, :span]
        new_w_ref[0, :, lanes] = stepped(1, t, wind_u, wind_u_tend)[:rows, :span]
        new_w_ref[1, :, lanes] = stepped(2, t, wind_v, wind_v_tend)[:rows, :span]
        for k in range(3):
            q = tile(2 + k, t)
            q_n = north(q)
            zonal_part = parts[k] - ring.west(("p", k), t, lambda s: zonal(s)[2][k])
            lap = q_n + south(q) - 2.0 * q
            over = flux_n * (0.5 * (q + q_n))
            merid_part = DIFFUSION * lap - (over - south(over)) * inv_cos
            mass = thick * q + TIME_STEP * (zonal_part + merid_part)
            mass_ref[k, :, lanes] = mass[:rows, :span].astype(jnp.bfloat16)


def sin_pi(y):
    y = jnp.where(y > 0.5, 1.0 - y, jnp.where(y < -0.5, -1.0 - y, y))
    s = y * y
    series = [(-1) ** i * math.pi ** (2 * i + 1) / math.factorial(2 * i + 1) for i in range(7)]
    total = series[-1]
    for factor in reversed(series[:-1]):
        total = total * s + factor
    return total * y


def share_of(sz, i):
    unit = lax.axis_index("lon") * sz.share + i
    return unit // sz.work, sz.first() + lax.rem(unit, sz.work)


def weights_kernel(sz, cut_ref, n_ref, inverse_ref, after_ref, weights_ref, masks_ref):
    band = lax.axis_index("lat")
    row = lax.broadcasted_iota(jnp.int32, (EXT_ROWS, LANES), 0)
    cuts = jnp.full((EXT_ROWS, LANES), sz.nlon // 2, jnp.int32)
    for j in range(sz.rows):
        cuts = jnp.where(row == j, cut_ref[band * sz.rows + j], cuts)
    plain, alone = cuts >= sz.nlon // 2, sz.at_pole(row)
    masks_ref[0] = jnp.where(plain, TIME_STEP, 0.0)
    masks_ref[1] = jnp.where(alone, TIME_STEP, 0.0)
    masks_ref[2] = jnp.where(plain | alone, 0.0, TIME_STEP)
    size = PER_TILE * sz.stack
    for i in range(sz.share):
        width = (2 * cut_ref[band * sz.rows + share_of(sz, i)[1]] + 1).astype(jnp.float32)
        n = n_ref[...]
        turns = n * width
        turns = turns - jnp.round(turns * (0.5 / sz.nlon)) * (2.0 * sz.nlon)
        weights = sin_pi(turns * (1.0 / sz.nlon)) * inverse_ref[...]
        weights = jnp.where(n == 0.0, width * (1.0 / sz.nlon), weights)
        weights_ref[size * i : size * (i + 1)] = weights.astype(jnp.bfloat16)


def pass_kernel(sz, piece_ref, after_ref, also_after_ref, out_ref):
    out_ref[...] = piece_ref[...]


def filter_kernel(sz, weights_ref, geo_ref, *refs):
    n_lon, stack, share = sz.n_lon, sz.stack, sz.share
    in_refs, out_refs, (gathered, results) = refs[:n_lon], refs[n_lon : 2 * n_lon], refs[2 * n_lon :]
    for k, in_ref in enumerate(in_refs):
        gathered[sz.partner(k), : sz.size] = in_ref[: sz.size]

    band = lax.axis_index("lat")
    lane = lax.broadcasted_iota(jnp.int32, (share, LANES), 1)
    place = lax.broadcasted_iota(jnp.int32, (share, LANES), 0)
    by_flux = by_thick = jnp.zeros((share, LANES), jnp.float32)
    for i in range(share):
        field, row = share_of(sz, i)
        inv_cos = geo_ref[band, 0, pl.ds(row, 1), :]
        by_flux = jnp.where((place == i) & (field == 0), inv_cos, by_flux)
        by_thick = jnp.where((place == i) & (field == 1), 0.5 * inv_cos, by_thick)
    sides = [gathered[s, pl.ds(sz.tiles - 1, share, stride=stack), :] for s in range(n_lon)]

    def column(s, k):
        return pltpu.roll(sides[s % n_lon], (-sz.tail - LEVELS * k) % LANES, 1)

    for s in range(n_lon):
        thick_w, thick_e = column(s, 1), column(s + 1, 0)
        flux = 0.25 * (column(s, 3) + column(s + 1, 2)) * (thick_w + thick_e) * by_flux
        west_of, east_of = flux + by_thick * thick_e, flux + by_thick * thick_w
        at = pl.ds(sz.tiles - 1, share, stride=stack)
        own = gathered[s, at, :]
        own = own - jnp.where(lane >= sz.tail - LEVELS, pltpu.roll(west_of, sz.tail - LEVELS, 1), 0.0)
        gathered[s, at, :] = jnp.where(lane < sz.tail, own, 0.0)
        at = pl.ds(0, share, stride=stack)
        after = (s + 1) % n_lon
        gathered[after, at, :] = gathered[after, at, :] + jnp.where(lane < LEVELS, east_of, 0.0)

    wide = lax.broadcasted_iota(jnp.int32, (stack, LANES), 1)
    rows = PER_TILE * stack
    for i in range(share):
        here = slice(stack * i, stack * (i + 1))
        pieces = [gathered[s, here].astype(jnp.bfloat16) for s in range(n_lon)]
        circle = jnp.concatenate([jnp.concatenate(pieces[s:] + pieces[:s], axis=0) for s in range(n_lon)], axis=1)
        spread = jnp.dot(weights_ref[rows * i : rows * (i + 1)], circle, preferred_element_type=jnp.float32)
        for s in range(n_lon):
            same = spread[:stack, LANES * s : LANES * (s + 1)]
            carried = None
            for e in range(1, PER_TILE):
                part = spread[stack * e : stack * (e + 1), LANES * s : LANES * (s + 1)]
                part = pltpu.roll(part, LEVELS * e, 1)
                inside = wide >= LEVELS * e
                same = same + jnp.where(inside, part, 0.0)
                over = jnp.where(inside, 0.0, part)
                carried = over if carried is None else carried + over
            results[s, here] = pltpu.roll(same, stack - 1, 0) + carried
    for k, out_ref in enumerate(out_refs):
        out_ref[...] = results[sz.partner(k), : sz.size]


def finish_kernel(sz, masks_ref, base_w_ref, base_h_ref, *refs):
    back_refs, (new_w_ref, new_h_ref, back_ref) = refs[: sz.n_lon], refs[sz.n_lon :]
    rows, work = sz.rows, sz.work
    for k, ref in enumerate(back_refs):
        back_ref[sz.piece(k), :] = ref[...]
    scale = masks_ref[2]
    even = lax.rem(lax.axis_index("lat"), 2) == 0
    for f in range(3):
        for t in range(sz.tiles):
            span = sz.span(t)
            lanes = slice(LANES * t, LANES * t + span)
            tend = back_ref[pl.ds(sz.stack * work * f + t, work, stride=sz.stack), :]
            if sz.near_only:
                tend = jnp.concatenate([tend, jnp.zeros((EXT_ROWS - work, LANES), jnp.float32)], axis=0)
                tend = jnp.where(even, south(tend), tend)
            change = (scale[:rows] * tend[:rows])[:, :span]
            if f == 0:
                new_h_ref[:, lanes] = base_h_ref[:, lanes] + change
            else:
                new_w_ref[:, f - 1, lanes] = base_w_ref[f - 1, :, lanes] + change


def local(winds, thickness, tracers, cutoff):
    n_lat = lax.axis_size("lat")
    n_lon = lax.axis_size("lon")
    rows, merged = thickness.shape
    sz = Sizes(rows, merged, n_lat, n_lon)
    f32 = jnp.float32
    vmem = pl.BlockSpec(memory_space=pltpu.VMEM)
    smem = pl.BlockSpec(memory_space=pltpu.SMEM)
    hbm = pl.BlockSpec(memory_space=pltpu.HBM)
    anywhere = pl.BlockSpec(memory_space=pl.ANY)

    def shaped(*shape):
        return jax.ShapeDtypeStruct(shape, f32)

    def call(kernel, name, in_specs, out_shape, scratch=(), limit=LIMIT):
        return pl.pallas_call(
            functools.partial(kernel, sz),
            out_shape=out_shape,
            in_specs=in_specs,
            out_specs=jax.tree.map(lambda _: vmem, out_shape),
            scratch_shapes=list(scratch),
            compiler_params=pltpu.CompilerParams(vmem_limit_bytes=limit),
            name=name,
        )

    geo = jnp.asarray(geometry(sz))
    wave = jnp.asarray(waves(sz))
    n, inverse = (jnp.asarray(table) for table in offsets(sz))

    wind_rows = jnp.swapaxes(winds, 0, 1)
    tracer_rows = jnp.swapaxes(tracers, 0, 1)
    far_row, near_row = shaped(5 * sz.stack, LANES), shaped(3 * sz.stack, LANES)
    kept = [((1,), f32), ((2,), f32), ((3,), jnp.bfloat16)]
    near_q, far_rows, sides = call(
        edges_kernel,
        "edges",
        [hbm] * 3,
        (near_row, far_row, shaped(2 * SIDE_ROWS, LANES)),
        [pltpu.VMEM((2,) + count + (merged,), dtype) for count, dtype in kept]
        + [
            pltpu.VMEM((rows,) + (count if count != (1,) else ()) + (lanes,), dtype)
            for lanes in (LANES, sz.tail)
            for count, dtype in kept
        ]
        + [pltpu.SemaphoreType.DMA((3, 4))],
        limit=MOST_VMEM,
    )(thickness, wind_rows, tracer_rows)

    near = [(band * n_lon + i, (band ^ 1) * n_lon + i) for band in range(n_lat) for i in range(n_lon)]
    far = []
    for band in range(n_lat):
        other = band - 1 if band % 2 == 0 else band + 1
        for i in range(n_lon):
            if 0 <= other < n_lat:
                far.append((band * n_lon + i, other * n_lon + i))
            else:
                far.append((band * n_lon + i, band * n_lon + (i + n_lon // 2) % n_lon))
    near_h = lax.ppermute(thickness, ("lat", "lon"), near)
    near_w = lax.ppermute(wind_rows, ("lat", "lon"), near)
    if not sz.near_only:
        far_rows = lax.ppermute(far_rows, ("lat", "lon"), far)

    order = [sz.turns(False), sz.turns(True)]

    def meetings(shares):
        got = [shares[0]]
        for k in range(1, n_lon):
            sectors = [(band, i, i ^ order[band % 2][k]) for band in range(n_lat) for i in range(n_lon)]
            got.append(lax.ppermute(shares[k], ("lat", "lon"), [(b * n_lon + i, b * n_lon + j) for b, i, j in sectors]))
        return got

    all_pieces = pltpu.VMEM((n_lon, sz.size + 8 * sz.stack, LANES), f32)
    all_units = pltpu.VMEM((n_lon * sz.size + 8 * sz.stack, LANES), f32)
    tends = call(
        polar_kernel,
        "polar",
        [vmem] * (7 if sz.near_only else 8),
        [shaped(sz.size + SIDE_ROWS, LANES)] * n_lon,
        [
            all_units,
            pltpu.VMEM((4 * sz.stack, LANES), f32),
            pltpu.VMEM((3, EXT_ROWS, sz.tiles * LANES), f32),
        ],
    )(thickness, wind_rows, near_h, near_w, sides, geo, wave, *(() if sz.near_only else (far_rows,)))
    met = meetings(tends)
    near_q = lax.ppermute(near_q, ("lat", "lon"), near)
    from_far = lax.ppermute(far_rows, ("lat", "lon"), far) if sz.near_only else far_rows
    weights, masks = call(
        weights_kernel,
        "weights",
        [smem, vmem, vmem, anywhere],
        (
            jax.ShapeDtypeStruct((sz.share * PER_TILE * sz.stack, n_lon * sz.stack), jnp.bfloat16),
            shaped(3, EXT_ROWS, LANES),
        ),
    )(cutoff, n, inverse, tends[0])
    worked = call(
        filter_kernel,
        "filter",
        [vmem] * 2 + [vmem] * n_lon,
        [shaped(sz.size, LANES)] * n_lon,
        [all_pieces, all_pieces],
    )(weights, geo, *met)
    held = call(pass_kernel, "pass", [vmem] + [anywhere] * 2, shaped(sz.size, LANES))(worked[-1], from_far, near_q)
    worked = [*worked[:-1], held]
    back = meetings(worked)

    base_w, base_h, mass = call(
        rest_kernel,
        "rest",
        [vmem] * 10 + [anywhere] + [vmem] * n_lon,
        (shaped(2, rows, merged), shaped(rows, merged), jax.ShapeDtypeStruct(tracers.shape, jnp.bfloat16)),
        [pltpu.VMEM((6, EXT_ROWS, sz.tiles * LANES), f32), pltpu.VMEM((n_lon, 8, LANES), f32)],
    )(masks, thickness, wind_rows, tracers, near_h, near_w, near_q, from_far, geo, wave, worked[0], *met)

    new_w, new_h = call(
        finish_kernel,
        "finish",
        [vmem] * (3 + n_lon),
        (shaped(*wind_rows.shape), shaped(rows, merged)),
        [all_units],
    )(masks, base_w, base_h, *back)
    return jnp.swapaxes(new_w, 0, 1), new_h, mass


def solution(mesh):
    in_specs = (P(None, "lat", "lon"), P("lat", "lon"), P(None, "lat", "lon"), P())
    out_specs = (P(None, "lat", "lon"), P("lat", "lon"), P(None, "lat", "lon"))
    return jax.shard_map(local, mesh=mesh, in_specs=in_specs, out_specs=out_specs, check_vma=False)
```

```python
import functools
import math

import jax
import jax.numpy as jnp
import numpy as np
from jax import lax
from jax.experimental import pallas as pl
from jax.experimental.pallas import tpu as pltpu
from jax.sharding import PartitionSpec as P

LEVELS = 16
TIME_STEP = 0.05
DIFFUSION = 0.5
LANES = 128
PER_TILE = LANES // LEVELS
SIDE_ROWS = 8
EXT_ROWS = 16
LIMIT = 48 * 1024 * 1024
MOST_VMEM = 64 * 1024 * 1024 - 10500 * 1024


class Sizes:
    def __init__(self, rows, merged, n_lat, n_lon):
        self.rows = rows
        self.merged = merged
        self.columns = merged // LEVELS
        self.n_lat = n_lat
        self.n_lon = n_lon
        self.nlat = rows * n_lat
        self.nlon = self.columns * n_lon
        self.ratio = 2.0 * self.nlat / self.nlon
        self.tiles = -(-merged // LANES)
        self.end = (self.tiles - 1) * LANES
        self.tail = merged - self.end
        self.stack = -(-(self.tiles + 1) // 8) * 8
        self.near_only = rows <= self.nlat // 6 < 2 * rows
        self.work = rows - 1 if self.near_only else rows
        self.units = 3 * self.work
        self.share = -(-self.units // n_lon)
        self.size = self.share * self.stack
        assert self.tail <= LANES - 4 * LEVELS and rows + 2 <= EXT_ROWS and n_lat % 2 == 0
        assert n_lon >= 4 and n_lon & (n_lon - 1) == 0 and rows == SIDE_ROWS + 1

    def span(self, tile):
        return self.tail if tile == self.tiles - 1 else LANES

    def first(self):
        return jnp.where(lax.rem(lax.axis_index("lat"), 2) == 0, 1, 0) if self.near_only else 0

    def at_pole(self, row):
        band = lax.axis_index("lat")
        pole = jnp.where(band == 0, 0, jnp.where(band == self.n_lat - 1, self.rows - 1, -1))
        return row == (pole if self.near_only else -1)

    def turns(self, odd):
        middle, last = list(range(1, self.n_lon - 1)), self.n_lon - 1
        return [0, middle[-1], last] + middle[-2::-1] if odd else [0, last] + middle

    def partner(self, k):
        odd = lax.rem(lax.axis_index("lat"), 2) == 1
        turn = jnp.where(odd, self.turns(True)[k], self.turns(False)[k])
        return jnp.bitwise_xor(lax.axis_index("lon"), turn)

    def piece(self, k):
        return pl.ds(pl.multiple_of(self.partner(k) * self.size, 8), self.size)


def geometry(sz):
    table = np.zeros((sz.n_lat, 3, EXT_ROWS, LANES), np.float64)

    def face(j):
        return math.sin((j + 1) * math.pi / sz.nlat) if 0 <= j < sz.nlat - 1 else 0.0

    for band in range(sz.n_lat):
        for row in range(sz.rows):
            j = band * sz.rows + row
            centre = (j + 0.5) * math.pi / sz.nlat - math.pi / 2
            table[band, 0, row] = 1.0 / math.cos(centre)
            table[band, 1, row] = math.sin(centre)
            table[band, 2, row] = face(j)
        table[band, 2, EXT_ROWS - 1] = face(band * sz.rows - 1)
    return table.astype(np.float32)


def offsets(sz):
    shift, out_tile = np.divmod(np.arange(PER_TILE * sz.stack), sz.stack)
    sector, in_tile = np.divmod(np.arange(sz.n_lon * sz.stack), sz.stack)
    n = (PER_TILE * (out_tile - 1) + shift)[:, None] - (PER_TILE * in_tile + sz.columns * sector)[None, :]
    n = (n + sz.nlon // 2) % sz.nlon - sz.nlon // 2
    with np.errstate(divide="ignore"):
        inverse = np.where(n == 0, 0.0, 1.0 / (sz.nlon * np.sin(np.pi * n / sz.nlon)))
    return n.astype(np.float32), inverse.astype(np.float32)


def waves(sz):
    column = PER_TILE * np.arange(sz.stack)[:, None] + np.arange(LANES)[None, :] // LEVELS
    angle = 2 * np.pi * column / sz.nlon
    return np.stack([np.cos(angle), np.sin(angle)]).astype(np.float32)


def spare(place):
    row, group = divmod(place, 3)
    return row, LEVELS * (5 + group)


def edges_kernel(sz, h_hbm, w_hbm, q_hbm, near_ref, far_ref, sides_ref, *scratch):
    row_refs, first_refs, last_refs, sems = scratch[:3], scratch[3:6], scratch[6:9], scratch[9]
    rows, last = sz.rows, sz.rows - 1
    even = lax.rem(lax.axis_index("lat"), 2) == 0
    copies = []
    for i, source in enumerate((h_hbm, w_hbm, q_hbm)):
        for k, row in enumerate((0, last)):
            one = source.at[pl.ds(row, 1)] if i == 0 else source.at[row]
            copies.append(pltpu.make_async_copy(one, row_refs[i].at[k], sems.at[i, k]))
        for k, (start, to) in enumerate(((0, first_refs[i]), (sz.end, last_refs[i]))):
            lanes = pl.ds(start, to.shape[-1])
            cut = source.at[:, lanes] if i == 0 else source.at[:, :, lanes]
            copies.append(pltpu.make_async_copy(cut, to, sems.at[i, 2 + k]))
    for copy in copies:
        copy.start()
    for copy in copies:
        copy.wait()
    h_rows, w_rows, q_rows = row_refs
    for t in range(sz.tiles):
        wide = sz.span(t)
        lanes = slice(LANES * t, LANES * t + wide)
        q = [q_rows[k, :, lanes].astype(jnp.float32) for k in range(2)]
        for f in range(5):
            if f == 0:
                first, final = h_rows[0, :, lanes], h_rows[1, :, lanes]
            elif f == 1:
                first, final = w_rows[0, 1:2, lanes], w_rows[1, 1:2, lanes]
            else:
                first, final = q[0][f - 2 : f - 1], q[1][f - 2 : f - 1]
                at = sz.stack * (f - 2) + t
                near_ref[at : at + 1, :wide] = jnp.where(even, final, first)
            at = sz.stack * f + t
            far_ref[at : at + 1, :wide] = jnp.where(even, first, final)
    sides_ref[...] = jnp.zeros(sides_ref.shape, jnp.float32)
    for k, (refs, at) in enumerate(((first_refs, 0), (last_refs, sz.tail - LEVELS))):
        columns = slice(at, at + LEVELS)
        for f in range(5):
            if f == 0:
                value = refs[0][:, columns]
            elif f == 1:
                value = refs[1][:, 0, columns]
            else:
                value = refs[2][:, f - 2, columns].astype(jnp.float32)
            start = SIDE_ROWS * k
            sides_ref[start : start + SIDE_ROWS, LEVELS * f : LEVELS * (f + 1)] = value[:SIDE_ROWS]
            row, lane = spare(f)
            sides_ref[start + row : start + row + 1, lane : lane + LEVELS] = value[SIDE_ROWS:]


def add_rows(sz, ext, near_h_ref, near_w_ref, near_q_ref, far_ref):
    band = lax.axis_index("lat")
    even = lax.rem(band, 2) == 0
    over_pole = (band == 0) | (band == sz.n_lat - 1)
    last = sz.rows - 1
    for f in range(2 if near_q_ref is None else 5):
        flip = jnp.where(over_pole, -1.0, 1.0) if f == 1 else 1.0
        for t in range(sz.tiles):
            lanes = slice(LANES * t, LANES * t + sz.span(t))
            if f == 0:
                near = jnp.where(even, near_h_ref[0:1, lanes], near_h_ref[last : sz.rows, lanes])
            elif f == 1:
                near = jnp.where(even, near_w_ref[0, 1:2, lanes], near_w_ref[last, 1:2, lanes])
            else:
                at = sz.stack * (f - 2) + t
                near = near_q_ref[at : at + 1, : sz.span(t)]
            at = sz.stack * f + t
            far = jnp.zeros_like(near) if far_ref is None else far_ref[at : at + 1, : sz.span(t)] * flip
            ext[f, sz.rows : sz.rows + 1, lanes] = jnp.where(even, near, far)
            ext[f, EXT_ROWS - 1 : EXT_ROWS, lanes] = jnp.where(even, far, near)


class Tiles:
    def __init__(self, sz):
        self.sz = sz
        self.lane = lax.broadcasted_iota(jnp.int32, (EXT_ROWS, LANES), 1)
        self.turned = {}

    def turn(self, name, t, value, step):
        key = (name, t % self.sz.tiles, step)
        if key not in self.turned:
            self.turned[key] = pltpu.roll(value(t % self.sz.tiles), step % LANES, 1)
        return self.turned[key]

    def east(self, name, t, value):
        here = self.turn(name, t, value, -LEVELS)
        return jnp.where(self.lane < LANES - LEVELS, here, self.turn(name, t + 1, value, -LEVELS))

    def west(self, name, t, value):
        here = self.turn(name, t, value, LEVELS)
        return jnp.where(self.lane >= LEVELS, here, self.turn(name, t - 1, value, LEVELS))


def north(value):
    return pltpu.roll(value, EXT_ROWS - 1, 0)


def south(value):
    return pltpu.roll(value, 1, 0)


def polar_kernel(sz, h_ref, w_ref, near_h_ref, near_w_ref, sides_ref, geo_ref, wave_ref, far_ref, near_q_ref, *refs):
    out_refs, (far_out, near_out, tend_ref, pole_ref, ext) = refs[:-5], refs[-5:]
    far_out[...] = far_ref[...]
    near_out[...] = near_q_ref[...]
    if sz.near_only:
        far_ref = None
    band = lax.axis_index("lat")
    ring = Tiles(sz)
    lane = ring.lane
    tiles, stack, rows, work = sz.tiles, sz.stack, sz.rows, sz.work
    even = lax.rem(band, 2) == 0
    for f, value in enumerate((h_ref[...], w_ref[:, 1, :], w_ref[:, 0, :])):
        ext[f, :rows, sz.end :] = jnp.zeros((rows, LANES), jnp.float32)
        ext[f, :rows, : sz.merged] = value
    add_rows(sz, ext, near_h_ref, near_w_ref, None, far_ref)
    inv_cos, sin_centre, cos_face = geo_ref[band, 0], geo_ref[band, 1], geo_ref[band, 2]
    ratio = sz.ratio

    def tile(f, t):
        return ext[f, :, LANES * t : LANES * (t + 1)]

    kept = {}

    def zonal(t):
        if t not in kept:
            thick_e = ring.east("h", t, functools.partial(tile, 0))
            wind_e = ring.east("u", t, functools.partial(tile, 2))
            flux = 0.25 * (tile(2, t) + wind_e) * (tile(0, t) + thick_e) * inv_cos
            if t == tiles - 1:
                flux = jnp.where(lane < sz.tail - LEVELS, flux, 0.0)
            kept[t] = (flux, thick_e)
        return kept[t]

    for t in range(tiles):
        flux, thick_e = zonal(t)
        thick, wind_v, wind_u = tile(0, t), tile(1, t), tile(2, t)
        flux_w = ring.west("f", t, lambda s: zonal(s)[0])
        thick_w = ring.west("hw", t, functools.partial(tile, 0))
        thick_n = north(thick)
        flux_n = (0.25 * ratio) * (wind_v + north(wind_v)) * (thick + thick_n) * cos_face
        thick_tend = -((flux - flux_w) + (flux_n - south(flux_n)) * inv_cos)
        wind_u_tend = sin_centre * wind_v - (thick_e - thick_w) * (0.5 * inv_cos)
        wind_v_tend = -sin_centre * wind_u - (0.5 * ratio) * (thick_n - south(thick))
        extra = 0.0
        if t == tiles - 1:
            last = sz.tail - LEVELS
            columns = [(tile(0, 0), 0), (thick, last), (tile(2, 0), 0), (wind_u, last)]
            for k, (source, at) in reversed(list(enumerate(columns))):
                to = sz.tail + LEVELS * k
                extra = jnp.where(lane < to + LEVELS, pltpu.roll(source, (to - at) % LANES, 1), extra)
        for f, tend in enumerate((thick_tend, wind_u_tend, wind_v_tend, thick)):
            if sz.near_only:
                alone = jnp.where(band < sz.n_lat // 2, tend[:1], tend[rows - 1 : rows])
                if t == tiles - 1:
                    alone = jnp.where(lane[:1] < sz.tail, alone, 0.0)
                pole_ref[stack * f + t : stack * f + t + 1] = alone
            if f == 3:
                continue
            if t == tiles - 1:
                tend = jnp.where(lane < sz.tail, tend, extra)
            if sz.near_only:
                tend = jnp.where(even, north(tend), tend)
            tend_ref[pl.ds(stack * work * f + t, work, stride=stack), :] = tend[:work]
    for f in range(3):
        for t in range(tiles, stack):
            tend_ref[pl.ds(stack * work * f + t, work, stride=stack), :] = jnp.zeros((work, LANES), jnp.float32)
    used, sent = stack * sz.units, sz.n_lon * sz.size
    if used < sent:
        tend_ref[used:sent, :] = jnp.zeros((sent - used, LANES), jnp.float32)
    sides = [sides_ref[:SIDE_ROWS], sides_ref[SIDE_ROWS:]]
    if sz.near_only:
        sums = pole_sums(sz, pole_ref, wave_ref, extra, band)
        sides = [side + sums for side in sides]
    here = lax.axis_index("lon")
    for k, out_ref in enumerate(out_refs):
        out_ref[: sz.size] = tend_ref[sz.piece(k), :]
        eastward = sz.partner(k) == lax.rem(here + 1, sz.n_lon)
        out_ref[sz.size :] = jnp.where(eastward, sides[1], sides[0])


def pole_sums(sz, pole_ref, wave_ref, extra, band):
    stack, rows = sz.stack, sz.rows
    lane = lax.broadcasted_iota(jnp.int32, (SIDE_ROWS, LANES), 1)
    row = lax.broadcasted_iota(jnp.int32, (SIDE_ROWS, LANES), 0)
    found = jnp.zeros((SIDE_ROWS, LANES), jnp.float32)

    def put(place, value):
        at_row, at = spare(6 + place)
        return jnp.where((row == at_row) & (lane >= at) & (lane < at + LEVELS), value, found)

    for f in range(4):
        if sz.tiles < stack:
            pole_ref[stack * f + sz.tiles : stack * (f + 1)] = jnp.zeros((stack - sz.tiles, LANES), jnp.float32)
        values = pole_ref[stack * f : stack * (f + 1)]
        for k, terms in enumerate((values, values * wave_ref[0], values * wave_ref[1])):
            total = jnp.sum(terms, axis=0, keepdims=True)
            for step in (64, 32, 16):
                total = total + pltpu.roll(total, step, 1)
            found = put(3 * f + k, total)
    beside = jnp.where(band < sz.n_lat // 2, extra[:1], extra[rows - 1 : rows])
    for k in range(4):
        found = put(12 + k, pltpu.roll(beside, (spare(18 + k)[1] - sz.tail - LEVELS * k) % LANES, 1))
    return found


def pole_waves(sz, rows_in, inv_cos, sign):
    n_lon = sz.n_lon
    lane = lax.broadcasted_iota(jnp.int32, (1, LANES), 1)

    def value(s, place):
        row, at = spare(6 + place)
        return pltpu.roll(rows_in[s % n_lon, row : row + 1], -at % LANES, 1)

    theta = 2 * math.pi / sz.nlon
    ends = (1.0, math.cos(theta * (sz.columns - 1)), math.sin(theta * (sz.columns - 1)))
    sums = [[[value(s, 3 * f + k) for k in range(3)] for f in range(4)] for s in range(n_lon)]
    for s in range(n_lon):
        thick_w, thick_e = value(s, 13), value(s + 1, 12)
        flux = 0.25 * (value(s, 15) + value(s + 1, 14)) * (thick_w + thick_e) * inv_cos
        slope = 0.5 * inv_cos
        after = (s + 1) % n_lon
        for f, (west_of, east_of) in enumerate(((flux, flux), (slope * thick_e, slope * thick_w))):
            for k in range(3):
                sums[s][f][k] = sums[s][f][k] - west_of * ends[k]
            for k in range(2):
                sums[after][f][k] = sums[after][f][k] + east_of
    result = []
    for f in range(3):
        waves_of = [0.0, 0.0, 0.0]
        for s in range(n_lon):
            level, cosine, sine = sums[s][f]
            if f == 2:
                level = level + (0.5 * sz.ratio) * sign * sums[s][3][0]
                cosine = cosine - (0.5 * sz.ratio) * sign * sums[s][3][1]
                sine = sine - (0.5 * sz.ratio) * sign * sums[s][3][2]
            c, d = math.cos(2 * math.pi * s / n_lon), math.sin(2 * math.pi * s / n_lon)
            waves_of[0] = waves_of[0] + level
            waves_of[1] = waves_of[1] + (c * cosine - d * sine)
            waves_of[2] = waves_of[2] + (d * cosine + c * sine)
        spread = []
        for k, total in enumerate(waves_of):
            total = jnp.where(lane < LEVELS, total * ((1.0 if k == 0 else 2.0) / sz.nlon), 0.0)
            for step in (16, 32, 64):
                total = total + pltpu.roll(total, step, 1)
            spread.append(total)
        result.append(spread)
    return result


def unfolded(sides):
    lane = lax.broadcasted_iota(jnp.int32, (1, LANES), 1)
    start, width = spare(0)[1], 3 * LEVELS
    ninth = jnp.where(
        lane < width,
        pltpu.roll(sides[0:1], -start % LANES, 1),
        pltpu.roll(sides[1:2], (width - start) % LANES, 1),
    )
    return jnp.concatenate([sides, jnp.broadcast_to(ninth, sides.shape)], axis=0)


def rest_kernel(sz, masks_ref, h_ref, w_ref, q_ref, near_h_ref, near_w_ref, near_q_ref, far_ref, geo_ref, wave_ref, after_ref, *refs):
    met_refs, (new_w_ref, new_h_ref, mass_ref, ext, pole_in) = refs[: sz.n_lon], refs[sz.n_lon :]
    band = lax.axis_index("lat")
    ring = Tiles(sz)
    lane = ring.lane
    tiles, rows = sz.tiles, sz.rows
    for f in range(6):
        if f < 2 or f == 5:
            value = (h_ref[...], w_ref[:, 1, :], w_ref[:, 0, :])[min(f, 2)]
        else:
            value = q_ref[f - 2].astype(jnp.float32)
        ext[f, :rows, : sz.merged] = value
    add_rows(sz, ext, near_h_ref, near_w_ref, near_q_ref, far_ref)
    lane9 = lane[:rows]
    here = lax.axis_index("lon")
    from_e = from_w = met_refs[0][sz.size :]
    for k, met_ref in enumerate(met_refs):
        eastward = lax.rem(sz.partner(k) - here + sz.n_lon, sz.n_lon)
        pole_in[eastward] = met_ref[sz.size :]
        from_e = jnp.where(sz.partner(k) == lax.rem(here + 1, sz.n_lon), met_ref[sz.size :], from_e)
        from_w = jnp.where(sz.partner(k) == lax.rem(here + sz.n_lon - 1, sz.n_lon), met_ref[sz.size :], from_w)
    from_e, from_w = unfolded(from_e), unfolded(from_w)
    for place, f in enumerate((0, 5, 2, 3, 4)):
        after = pltpu.roll(from_e, (sz.tail - LEVELS * place) % LANES, 1)[:rows]
        before = pltpu.roll(from_w, (LANES - LEVELS - LEVELS * place) % LANES, 1)[:rows]
        own = ext[f, :rows, sz.end :]
        edge = jnp.where(lane9 < LANES - LEVELS, after, before)
        ext[f, :rows, sz.end :] = jnp.where(lane9 < sz.tail, own, edge)
    inv_cos, sin_centre, cos_face = geo_ref[band, 0], geo_ref[band, 1], geo_ref[band, 2]
    ratio = sz.ratio

    plain, alone = masks_ref[0], masks_ref[1]
    if sz.near_only:
        band = lax.axis_index("lat")
        low = band < sz.n_lat // 2
        pole_cos = jnp.where(low, inv_cos[:1], inv_cos[rows - 1 : rows])
        kept_waves = pole_waves(sz, pole_in, pole_cos, jnp.where(low, 1.0, -1.0))

    def stepped(f, t, value, tend):
        value = value + plain * tend
        if sz.near_only:
            level, cosine, sine = kept_waves[f]
            wave = level + cosine * wave_ref[0, t : t + 1] + sine * wave_ref[1, t : t + 1]
            value = value + alone * wave
        return value

    def tile(f, t):
        return ext[f, :, LANES * t : LANES * (t + 1)]

    kept = {}

    def zonal(t):
        if t not in kept:
            thick_e = ring.east("h", t, functools.partial(tile, 0))
            wind_e = ring.east("u", t, functools.partial(tile, 5))
            flux = 0.25 * (tile(5, t) + wind_e) * (tile(0, t) + thick_e) * inv_cos
            parts = []
            for k in range(3):
                q = tile(2 + k, t)
                q_e = ring.east(k, t, functools.partial(tile, 2 + k))
                parts.append(DIFFUSION * (q_e - q) - flux * (0.5 * (q + q_e)))
            kept[t] = (flux, thick_e, parts)
        return kept[t]

    for t in range(tiles):
        span = sz.span(t)
        lanes = slice(LANES * t, LANES * t + span)
        flux, thick_e, parts = zonal(t)
        thick, wind_u, wind_v = tile(0, t), tile(5, t), tile(1, t)
        flux_w = ring.west("f", t, lambda s: zonal(s)[0])
        thick_w = ring.west("hw", t, functools.partial(tile, 0))
        thick_n = north(thick)
        flux_n = (0.25 * ratio) * (wind_v + north(wind_v)) * (thick + thick_n) * cos_face
        thick_tend = -((flux - flux_w) + (flux_n - south(flux_n)) * inv_cos)
        wind_u_tend = sin_centre * wind_v - (thick_e - thick_w) * (0.5 * inv_cos)
        wind_v_tend = -sin_centre * wind_u - (0.5 * ratio) * (thick_n - south(thick))
        new_h_ref[:, lanes] = stepped(0, t, thick, thick_tend)[:rows, :span]
        new_w_ref[0, :, lanes] = stepped(1, t, wind_u, wind_u_tend)[:rows, :span]
        new_w_ref[1, :, lanes] = stepped(2, t, wind_v, wind_v_tend)[:rows, :span]
        for k in range(3):
            q = tile(2 + k, t)
            q_n = north(q)
            zonal_part = parts[k] - ring.west(("p", k), t, lambda s: zonal(s)[2][k])
            lap = q_n + south(q) - 2.0 * q
            over = flux_n * (0.5 * (q + q_n))
            merid_part = DIFFUSION * lap - (over - south(over)) * inv_cos
            mass = thick * q + TIME_STEP * (zonal_part + merid_part)
            mass_ref[k, :, lanes] = mass[:rows, :span].astype(jnp.bfloat16)


def sin_pi(y):
    y = jnp.maximum(jnp.minimum(y, 1.0 - y), -1.0 - y)
    s = y * y
    series = [(-1) ** i * math.pi ** (2 * i + 1) / math.factorial(2 * i + 1) for i in range(6)]
    total = series[-1]
    for factor in reversed(series[:-1]):
        total = total * s + factor
    return total * y


def share_of(sz, i):
    unit = lax.axis_index("lon") * sz.share + i
    return unit // sz.work, sz.first() + lax.rem(unit, sz.work)


def weights_kernel(sz, cut_ref, n_ref, inverse_ref, after_ref, weights_ref, masks_ref):
    band = lax.axis_index("lat")
    row = lax.broadcasted_iota(jnp.int32, (EXT_ROWS, LANES), 0)
    cuts = jnp.full((EXT_ROWS, LANES), sz.nlon // 2, jnp.int32)
    for j in range(sz.rows):
        cuts = jnp.where(row == j, cut_ref[band * sz.rows + j], cuts)
    plain, alone = cuts >= sz.nlon // 2, sz.at_pole(row)
    masks_ref[0] = jnp.where(plain, TIME_STEP, 0.0)
    masks_ref[1] = jnp.where(alone, TIME_STEP, 0.0)
    masks_ref[2] = jnp.where(plain | alone, 0.0, TIME_STEP)
    size = PER_TILE * sz.stack
    for i in range(sz.share):
        width = (2 * cut_ref[band * sz.rows + share_of(sz, i)[1]] + 1).astype(jnp.float32)
        n = n_ref[...]
        turns = n * width
        turns = turns - jnp.round(turns * (0.5 / sz.nlon)) * (2.0 * sz.nlon)
        weights = sin_pi(turns * (1.0 / sz.nlon)) * inverse_ref[...]
        weights = jnp.where(n == 0.0, width * (1.0 / sz.nlon), weights)
        weights_ref[size * i : size * (i + 1)] = weights.astype(jnp.bfloat16)


def pass_kernel(sz, piece_ref, after_ref, also_after_ref, out_ref):
    out_ref[...] = piece_ref[...]


def filter_kernel(sz, weights_ref, geo_ref, *refs):
    n_lon, stack, share = sz.n_lon, sz.stack, sz.share
    in_refs, out_refs, (gathered, results) = refs[:n_lon], refs[n_lon : 2 * n_lon], refs[2 * n_lon :]
    for k, in_ref in enumerate(in_refs):
        gathered[sz.partner(k), : sz.size] = in_ref[: sz.size]

    band = lax.axis_index("lat")
    lane = lax.broadcasted_iota(jnp.int32, (share, LANES), 1)
    place = lax.broadcasted_iota(jnp.int32, (share, LANES), 0)
    by_flux = by_thick = jnp.zeros((share, LANES), jnp.float32)
    for i in range(share):
        field, row = share_of(sz, i)
        inv_cos = geo_ref[band, 0, pl.ds(row, 1), :]
        by_flux = jnp.where((place == i) & (field == 0), inv_cos, by_flux)
        by_thick = jnp.where((place == i) & (field == 1), 0.5 * inv_cos, by_thick)
    sides = [gathered[s, pl.ds(sz.tiles - 1, share, stride=stack), :] for s in range(n_lon)]

    def column(s, k):
        return pltpu.roll(sides[s % n_lon], (-sz.tail - LEVELS * k) % LANES, 1)

    for s in range(n_lon):
        thick_w, thick_e = column(s, 1), column(s + 1, 0)
        flux = 0.25 * (column(s, 3) + column(s + 1, 2)) * (thick_w + thick_e) * by_flux
        west_of, east_of = flux + by_thick * thick_e, flux + by_thick * thick_w
        at = pl.ds(sz.tiles - 1, share, stride=stack)
        own = gathered[s, at, :]
        own = own - jnp.where(lane >= sz.tail - LEVELS, pltpu.roll(west_of, sz.tail - LEVELS, 1), 0.0)
        gathered[s, at, :] = jnp.where(lane < sz.tail, own, 0.0)
        at = pl.ds(0, share, stride=stack)
        after = (s + 1) % n_lon
        gathered[after, at, :] = gathered[after, at, :] + jnp.where(lane < LEVELS, east_of, 0.0)

    wide = lax.broadcasted_iota(jnp.int32, (stack, LANES), 1)
    rows = PER_TILE * stack
    for i in range(share):
        here = slice(stack * i, stack * (i + 1))
        pieces = [gathered[s, here].astype(jnp.bfloat16) for s in range(n_lon)]
        circle = jnp.concatenate([jnp.concatenate(pieces[s:] + pieces[:s], axis=0) for s in range(n_lon)], axis=1)
        spread = jnp.dot(weights_ref[rows * i : rows * (i + 1)], circle, preferred_element_type=jnp.float32)
        for s in range(n_lon):
            same = spread[:stack, LANES * s : LANES * (s + 1)]
            carried = None
            for e in range(1, PER_TILE):
                part = spread[stack * e : stack * (e + 1), LANES * s : LANES * (s + 1)]
                part = pltpu.roll(part, LEVELS * e, 1)
                inside = wide >= LEVELS * e
                same = same + jnp.where(inside, part, 0.0)
                over = jnp.where(inside, 0.0, part)
                carried = over if carried is None else carried + over
            results[s, here] = pltpu.roll(same, stack - 1, 0) + carried
    for k, out_ref in enumerate(out_refs):
        out_ref[...] = results[sz.partner(k), : sz.size]


def finish_kernel(sz, masks_ref, base_w_ref, base_h_ref, *refs):
    back_refs, (new_w_ref, new_h_ref, back_ref) = refs[: sz.n_lon], refs[sz.n_lon :]
    rows, work = sz.rows, sz.work
    for k, ref in enumerate(back_refs):
        back_ref[sz.piece(k), :] = ref[...]
    scale = masks_ref[2]
    even = lax.rem(lax.axis_index("lat"), 2) == 0
    for f in range(3):
        for t in range(sz.tiles):
            span = sz.span(t)
            lanes = slice(LANES * t, LANES * t + span)
            tend = back_ref[pl.ds(sz.stack * work * f + t, work, stride=sz.stack), :]
            if sz.near_only:
                tend = jnp.concatenate([tend, jnp.zeros((EXT_ROWS - work, LANES), jnp.float32)], axis=0)
                tend = jnp.where(even, south(tend), tend)
            change = (scale[:rows] * tend[:rows])[:, :span]
            if f == 0:
                new_h_ref[:, lanes] = base_h_ref[:, lanes] + change
            else:
                new_w_ref[:, f - 1, lanes] = base_w_ref[f - 1, :, lanes] + change


def local(winds, thickness, tracers, cutoff):
    n_lat = lax.axis_size("lat")
    n_lon = lax.axis_size("lon")
    rows, merged = thickness.shape
    sz = Sizes(rows, merged, n_lat, n_lon)
    f32 = jnp.float32
    vmem = pl.BlockSpec(memory_space=pltpu.VMEM)
    smem = pl.BlockSpec(memory_space=pltpu.SMEM)
    hbm = pl.BlockSpec(memory_space=pltpu.HBM)
    anywhere = pl.BlockSpec(memory_space=pl.ANY)

    def shaped(*shape):
        return jax.ShapeDtypeStruct(shape, f32)

    def call(kernel, name, in_specs, out_shape, scratch=(), limit=LIMIT):
        return pl.pallas_call(
            functools.partial(kernel, sz),
            out_shape=out_shape,
            in_specs=in_specs,
            out_specs=jax.tree.map(lambda _: vmem, out_shape),
            scratch_shapes=list(scratch),
            compiler_params=pltpu.CompilerParams(vmem_limit_bytes=limit),
            name=name,
        )

    geo = jnp.asarray(geometry(sz))
    wave = jnp.asarray(waves(sz))
    n, inverse = (jnp.asarray(table) for table in offsets(sz))

    wind_rows = jnp.swapaxes(winds, 0, 1)
    tracer_rows = jnp.swapaxes(tracers, 0, 1)
    far_row, near_row = shaped(5 * sz.stack, LANES), shaped(3 * sz.stack, LANES)
    kept = [((1,), f32), ((2,), f32), ((3,), jnp.bfloat16)]
    near_q, far_rows, sides = call(
        edges_kernel,
        "edges",
        [hbm] * 3,
        (near_row, far_row, shaped(2 * SIDE_ROWS, LANES)),
        [pltpu.VMEM((2,) + count + (merged,), dtype) for count, dtype in kept]
        + [
            pltpu.VMEM((rows,) + (count if count != (1,) else ()) + (lanes,), dtype)
            for lanes in (LANES, sz.tail)
            for count, dtype in kept
        ]
        + [pltpu.SemaphoreType.DMA((3, 4))],
        limit=MOST_VMEM,
    )(thickness, wind_rows, tracer_rows)

    near = [(band * n_lon + i, (band ^ 1) * n_lon + i) for band in range(n_lat) for i in range(n_lon)]
    far = []
    for band in range(n_lat):
        other = band - 1 if band % 2 == 0 else band + 1
        for i in range(n_lon):
            if 0 <= other < n_lat:
                far.append((band * n_lon + i, other * n_lon + i))
            else:
                far.append((band * n_lon + i, band * n_lon + (i + n_lon // 2) % n_lon))
    near_h = lax.ppermute(thickness, ("lat", "lon"), near)
    near_w = lax.ppermute(wind_rows, ("lat", "lon"), near)
    if not sz.near_only:
        far_rows = lax.ppermute(far_rows, ("lat", "lon"), far)

    order = [sz.turns(False), sz.turns(True)]

    def meetings(shares):
        got = [shares[0]]
        for k in range(1, n_lon):
            sectors = [(band, i, i ^ order[band % 2][k]) for band in range(n_lat) for i in range(n_lon)]
            got.append(lax.ppermute(shares[k], ("lat", "lon"), [(b * n_lon + i, b * n_lon + j) for b, i, j in sectors]))
        return got

    all_pieces = pltpu.VMEM((n_lon, sz.size + 8 * sz.stack, LANES), f32)
    all_units = pltpu.VMEM((n_lon * sz.size + 8 * sz.stack, LANES), f32)
    *tends, far_rows, near_q = call(
        polar_kernel,
        "polar",
        [vmem] * 9,
        [shaped(sz.size + SIDE_ROWS, LANES)] * n_lon + [far_row, near_row],
        [
            all_units,
            pltpu.VMEM((4 * sz.stack, LANES), f32),
            pltpu.VMEM((3, EXT_ROWS, sz.tiles * LANES), f32),
        ],
    )(thickness, wind_rows, near_h, near_w, sides, geo, wave, far_rows, near_q)
    met = meetings(tends)
    near_q = lax.ppermute(near_q, ("lat", "lon"), near)
    from_far = lax.ppermute(far_rows, ("lat", "lon"), far) if sz.near_only else far_rows
    weights, masks = call(
        weights_kernel,
        "weights",
        [smem, vmem, vmem, anywhere],
        (
            jax.ShapeDtypeStruct((sz.share * PER_TILE * sz.stack, n_lon * sz.stack), jnp.bfloat16),
            shaped(3, EXT_ROWS, LANES),
        ),
    )(cutoff, n, inverse, tends[0])
    worked = call(
        filter_kernel,
        "filter",
        [vmem] * 2 + [vmem] * n_lon,
        [shaped(sz.size, LANES)] * n_lon,
        [all_pieces, all_pieces],
    )(weights, geo, *met)
    held = call(pass_kernel, "pass", [vmem] + [anywhere] * 2, shaped(sz.size, LANES))(worked[-1], from_far, near_q)
    worked = [*worked[:-1], held]
    back = meetings(worked)

    base_w, base_h, mass = call(
        rest_kernel,
        "rest",
        [vmem] * 10 + [anywhere] + [vmem] * n_lon,
        (shaped(2, rows, merged), shaped(rows, merged), jax.ShapeDtypeStruct(tracers.shape, jnp.bfloat16)),
        [pltpu.VMEM((6, EXT_ROWS, sz.tiles * LANES), f32), pltpu.VMEM((n_lon, 8, LANES), f32)],
    )(masks, thickness, wind_rows, tracers, near_h, near_w, near_q, from_far, geo, wave, worked[0], *met)

    new_w, new_h = call(
        finish_kernel,
        "finish",
        [vmem] * (3 + n_lon),
        (shaped(*wind_rows.shape), shaped(rows, merged)),
        [all_units],
    )(masks, base_w, base_h, *back)
    return jnp.swapaxes(new_w, 0, 1), new_h, mass


def solution(mesh):
    in_specs = (P(None, "lat", "lon"), P("lat", "lon"), P(None, "lat", "lon"), P())
    out_specs = (P(None, "lat", "lon"), P("lat", "lon"), P(None, "lat", "lon"))
    return jax.shard_map(local, mesh=mesh, in_specs=in_specs, out_specs=out_specs, check_vma=False)
```

```python
import functools
import math

import jax
import jax.numpy as jnp
import numpy as np
from jax import lax
from jax.experimental import pallas as pl
from jax.experimental.pallas import tpu as pltpu
from jax.sharding import PartitionSpec as P

LEVELS = 16
TIME_STEP = 0.05
DIFFUSION = 0.5
LANES = 128
PER_TILE = LANES // LEVELS
SIDE_ROWS = 8
EXT_ROWS = 16
LIMIT = 48 * 1024 * 1024
MOST_VMEM = 64 * 1024 * 1024 - 10500 * 1024


class Sizes:
    def __init__(self, rows, merged, n_lat, n_lon):
        self.rows = rows
        self.merged = merged
        self.columns = merged // LEVELS
        self.n_lat = n_lat
        self.n_lon = n_lon
        self.nlat = rows * n_lat
        self.nlon = self.columns * n_lon
        self.ratio = 2.0 * self.nlat / self.nlon
        self.tiles = -(-merged // LANES)
        self.end = (self.tiles - 1) * LANES
        self.tail = merged - self.end
        self.stack = -(-(self.tiles + 1) // 8) * 8
        self.near_only = rows <= self.nlat // 6 < 2 * rows
        self.work = rows - 1 if self.near_only else rows
        self.units = 3 * self.work
        self.share = -(-self.units // n_lon)
        self.size = self.share * self.stack
        assert self.tail <= LANES - 4 * LEVELS and rows + 2 <= EXT_ROWS and n_lat % 2 == 0
        assert n_lon >= 4 and n_lon & (n_lon - 1) == 0 and rows == SIDE_ROWS + 1

    def span(self, tile):
        return self.tail if tile == self.tiles - 1 else LANES

    def first(self):
        return jnp.where(lax.rem(lax.axis_index("lat"), 2) == 0, 1, 0) if self.near_only else 0

    def at_pole(self, row):
        band = lax.axis_index("lat")
        pole = jnp.where(band == 0, 0, jnp.where(band == self.n_lat - 1, self.rows - 1, -1))
        return row == (pole if self.near_only else -1)

    def turns(self, odd, back):
        middle, last = list(range(1, self.n_lon - 1)), self.n_lon - 1
        return [0, middle[-1], last] + middle[-2::-1] if odd != back else [0, last] + middle

    def partner(self, k, back=False):
        odd = lax.rem(lax.axis_index("lat"), 2) == 1
        turn = jnp.where(odd, self.turns(True, back)[k], self.turns(False, back)[k])
        return jnp.bitwise_xor(lax.axis_index("lon"), turn)

    def piece(self, k, back=False):
        return pl.ds(pl.multiple_of(self.partner(k, back) * self.size, 8), self.size)


def geometry(sz):
    table = np.zeros((sz.n_lat, 3, EXT_ROWS, LANES), np.float64)

    def face(j):
        return math.sin((j + 1) * math.pi / sz.nlat) if 0 <= j < sz.nlat - 1 else 0.0

    for band in range(sz.n_lat):
        for row in range(sz.rows):
            j = band * sz.rows + row
            centre = (j + 0.5) * math.pi / sz.nlat - math.pi / 2
            table[band, 0, row] = 1.0 / math.cos(centre)
            table[band, 1, row] = math.sin(centre)
            table[band, 2, row] = face(j)
        table[band, 2, EXT_ROWS - 1] = face(band * sz.rows - 1)
    return table.astype(np.float32)


def offsets(sz):
    shift, out_tile = np.divmod(np.arange(PER_TILE * sz.stack), sz.stack)
    sector, in_tile = np.divmod(np.arange(sz.n_lon * sz.stack), sz.stack)
    n = (PER_TILE * (out_tile - 1) + shift)[:, None] - (PER_TILE * in_tile + sz.columns * sector)[None, :]
    n = (n + sz.nlon // 2) % sz.nlon - sz.nlon // 2
    with np.errstate(divide="ignore"):
        inverse = np.where(n == 0, 0.0, 1.0 / (sz.nlon * np.sin(np.pi * n / sz.nlon)))
    return n.astype(np.float32), inverse.astype(np.float32)


def waves(sz):
    column = PER_TILE * np.arange(sz.stack)[:, None] + np.arange(LANES)[None, :] // LEVELS
    angle = 2 * np.pi * column / sz.nlon
    return np.stack([np.cos(angle), np.sin(angle)]).astype(np.float32)


def spare(place):
    row, group = divmod(place, 3)
    return row, LEVELS * (5 + group)


def edges_kernel(sz, h_hbm, w_hbm, q_hbm, near_ref, far_ref, sides_ref, *scratch):
    row_refs, first_refs, last_refs, sems = scratch[:3], scratch[3:6], scratch[6:9], scratch[9]
    rows, last = sz.rows, sz.rows - 1
    even = lax.rem(lax.axis_index("lat"), 2) == 0
    copies = []
    for i, source in enumerate((h_hbm, w_hbm, q_hbm)):
        for k, row in enumerate((0, last)):
            one = source.at[pl.ds(row, 1)] if i == 0 else source.at[row]
            copies.append(pltpu.make_async_copy(one, row_refs[i].at[k], sems.at[i, k]))
        for k, (start, to) in enumerate(((0, first_refs[i]), (sz.end, last_refs[i]))):
            lanes = pl.ds(start, to.shape[-1])
            cut = source.at[:, lanes] if i == 0 else source.at[:, :, lanes]
            copies.append(pltpu.make_async_copy(cut, to, sems.at[i, 2 + k]))
    for copy in copies:
        copy.start()
    for copy in copies:
        copy.wait()
    h_rows, w_rows, q_rows = row_refs
    for t in range(sz.tiles):
        wide = sz.span(t)
        lanes = slice(LANES * t, LANES * t + wide)
        q = [q_rows[k, :, lanes].astype(jnp.float32) for k in range(2)]
        for f in range(5):
            if f == 0:
                first, final = h_rows[0, :, lanes], h_rows[1, :, lanes]
            elif f == 1:
                first, final = w_rows[0, 1:2, lanes], w_rows[1, 1:2, lanes]
            else:
                first, final = q[0][f - 2 : f - 1], q[1][f - 2 : f - 1]
                at = sz.stack * (f - 2) + t
                near_ref[at : at + 1, :wide] = jnp.where(even, final, first)
            at = sz.stack * f + t
            far_ref[at : at + 1, :wide] = jnp.where(even, first, final)
    sides_ref[...] = jnp.zeros(sides_ref.shape, jnp.float32)
    for k, (refs, at) in enumerate(((first_refs, 0), (last_refs, sz.tail - LEVELS))):
        columns = slice(at, at + LEVELS)
        for f in range(5):
            if f == 0:
                value = refs[0][:, columns]
            elif f == 1:
                value = refs[1][:, 0, columns]
            else:
                value = refs[2][:, f - 2, columns].astype(jnp.float32)
            start = SIDE_ROWS * k
            sides_ref[start : start + SIDE_ROWS, LEVELS * f : LEVELS * (f + 1)] = value[:SIDE_ROWS]
            row, lane = spare(f)
            sides_ref[start + row : start + row + 1, lane : lane + LEVELS] = value[SIDE_ROWS:]


def add_rows(sz, ext, near_h_ref, near_w_ref, near_q_ref, far_ref):
    band = lax.axis_index("lat")
    even = lax.rem(band, 2) == 0
    over_pole = (band == 0) | (band == sz.n_lat - 1)
    last = sz.rows - 1
    for f in range(2 if near_q_ref is None else 5):
        flip = jnp.where(over_pole, -1.0, 1.0) if f == 1 else 1.0
        for t in range(sz.tiles):
            lanes = slice(LANES * t, LANES * t + sz.span(t))
            if f == 0:
                near = jnp.where(even, near_h_ref[0:1, lanes], near_h_ref[last : sz.rows, lanes])
            elif f == 1:
                near = jnp.where(even, near_w_ref[0, 1:2, lanes], near_w_ref[last, 1:2, lanes])
            else:
                at = sz.stack * (f - 2) + t
                near = near_q_ref[at : at + 1, : sz.span(t)]
            at = sz.stack * f + t
            far = jnp.zeros_like(near) if far_ref is None else far_ref[at : at + 1, : sz.span(t)] * flip
            ext[f, sz.rows : sz.rows + 1, lanes] = jnp.where(even, near, far)
            ext[f, EXT_ROWS - 1 : EXT_ROWS, lanes] = jnp.where(even, far, near)


class Tiles:
    def __init__(self, sz):
        self.sz = sz
        self.lane = lax.broadcasted_iota(jnp.int32, (EXT_ROWS, LANES), 1)
        self.turned = {}

    def turn(self, name, t, value, step):
        key = (name, t % self.sz.tiles, step)
        if key not in self.turned:
            self.turned[key] = pltpu.roll(value(t % self.sz.tiles), step % LANES, 1)
        return self.turned[key]

    def east(self, name, t, value):
        here = self.turn(name, t, value, -LEVELS)
        return jnp.where(self.lane < LANES - LEVELS, here, self.turn(name, t + 1, value, -LEVELS))

    def west(self, name, t, value):
        here = self.turn(name, t, value, LEVELS)
        return jnp.where(self.lane >= LEVELS, here, self.turn(name, t - 1, value, LEVELS))


def north(value):
    return pltpu.roll(value, EXT_ROWS - 1, 0)


def south(value):
    return pltpu.roll(value, 1, 0)


def polar_kernel(sz, h_ref, w_ref, near_h_ref, near_w_ref, sides_ref, geo_ref, wave_ref, far_ref, near_q_ref, *refs):
    out_refs, (far_out, near_out, tend_ref, pole_ref, ext) = refs[:-5], refs[-5:]
    far_out[...] = far_ref[...]
    near_out[...] = near_q_ref[...]
    if sz.near_only:
        far_ref = None
    band = lax.axis_index("lat")
    ring = Tiles(sz)
    lane = ring.lane
    tiles, stack, rows, work = sz.tiles, sz.stack, sz.rows, sz.work
    even = lax.rem(band, 2) == 0
    for f, value in enumerate((h_ref[...], w_ref[:, 1, :], w_ref[:, 0, :])):
        ext[f, :rows, sz.end :] = jnp.zeros((rows, LANES), jnp.float32)
        ext[f, :rows, : sz.merged] = value
    add_rows(sz, ext, near_h_ref, near_w_ref, None, far_ref)
    inv_cos, sin_centre, cos_face = geo_ref[band, 0], geo_ref[band, 1], geo_ref[band, 2]
    ratio = sz.ratio

    def tile(f, t):
        return ext[f, :, LANES * t : LANES * (t + 1)]

    kept = {}

    def zonal(t):
        if t not in kept:
            thick_e = ring.east("h", t, functools.partial(tile, 0))
            wind_e = ring.east("u", t, functools.partial(tile, 2))
            flux = 0.25 * (tile(2, t) + wind_e) * (tile(0, t) + thick_e) * inv_cos
            if t == tiles - 1:
                flux = jnp.where(lane < sz.tail - LEVELS, flux, 0.0)
            kept[t] = (flux, thick_e)
        return kept[t]

    for t in range(tiles):
        flux, thick_e = zonal(t)
        thick, wind_v, wind_u = tile(0, t), tile(1, t), tile(2, t)
        flux_w = ring.west("f", t, lambda s: zonal(s)[0])
        thick_w = ring.west("hw", t, functools.partial(tile, 0))
        thick_n = north(thick)
        flux_n = (0.25 * ratio) * (wind_v + north(wind_v)) * (thick + thick_n) * cos_face
        thick_tend = -((flux - flux_w) + (flux_n - south(flux_n)) * inv_cos)
        wind_u_tend = sin_centre * wind_v - (thick_e - thick_w) * (0.5 * inv_cos)
        wind_v_tend = -sin_centre * wind_u - (0.5 * ratio) * (thick_n - south(thick))
        extra = 0.0
        if t == tiles - 1:
            last = sz.tail - LEVELS
            columns = [(tile(0, 0), 0), (thick, last), (tile(2, 0), 0), (wind_u, last)]
            for k, (source, at) in reversed(list(enumerate(columns))):
                to = sz.tail + LEVELS * k
                extra = jnp.where(lane < to + LEVELS, pltpu.roll(source, (to - at) % LANES, 1), extra)
        for f, tend in enumerate((thick_tend, wind_u_tend, wind_v_tend, thick)):
            if sz.near_only:
                alone = jnp.where(band < sz.n_lat // 2, tend[:1], tend[rows - 1 : rows])
                if t == tiles - 1:
                    alone = jnp.where(lane[:1] < sz.tail, alone, 0.0)
                pole_ref[stack * f + t : stack * f + t + 1] = alone
            if f == 3:
                continue
            if t == tiles - 1:
                tend = jnp.where(lane < sz.tail, tend, extra)
            if sz.near_only:
                tend = jnp.where(even, north(tend), tend)
            tend_ref[pl.ds(stack * work * f + t, work, stride=stack), :] = tend[:work]
    for f in range(3):
        for t in range(tiles, stack):
            tend_ref[pl.ds(stack * work * f + t, work, stride=stack), :] = jnp.zeros((work, LANES), jnp.float32)
    used, sent = stack * sz.units, sz.n_lon * sz.size
    if used < sent:
        tend_ref[used:sent, :] = jnp.zeros((sent - used, LANES), jnp.float32)
    sides = [sides_ref[:SIDE_ROWS], sides_ref[SIDE_ROWS:]]
    if sz.near_only:
        sums = pole_sums(sz, pole_ref, wave_ref, extra, band)
        sides = [side + sums for side in sides]
    here = lax.axis_index("lon")
    for k, out_ref in enumerate(out_refs):
        out_ref[: sz.size] = tend_ref[sz.piece(k), :]
        eastward = sz.partner(k) == lax.rem(here + 1, sz.n_lon)
        out_ref[sz.size :] = jnp.where(eastward, sides[1], sides[0])


def pole_sums(sz, pole_ref, wave_ref, extra, band):
    stack, rows = sz.stack, sz.rows
    lane = lax.broadcasted_iota(jnp.int32, (SIDE_ROWS, LANES), 1)
    row = lax.broadcasted_iota(jnp.int32, (SIDE_ROWS, LANES), 0)
    found = jnp.zeros((SIDE_ROWS, LANES), jnp.float32)

    def put(place, value):
        at_row, at = spare(6 + place)
        return jnp.where((row == at_row) & (lane >= at) & (lane < at + LEVELS), value, found)

    for f in range(4):
        if sz.tiles < stack:
            pole_ref[stack * f + sz.tiles : stack * (f + 1)] = jnp.zeros((stack - sz.tiles, LANES), jnp.float32)
        values = pole_ref[stack * f : stack * (f + 1)]
        for k, terms in enumerate((values, values * wave_ref[0], values * wave_ref[1])):
            total = jnp.sum(terms, axis=0, keepdims=True)
            for step in (64, 32, 16):
                total = total + pltpu.roll(total, step, 1)
            found = put(3 * f + k, total)
    beside = jnp.where(band < sz.n_lat // 2, extra[:1], extra[rows - 1 : rows])
    for k in range(4):
        found = put(12 + k, pltpu.roll(beside, (spare(18 + k)[1] - sz.tail - LEVELS * k) % LANES, 1))
    return found


def pole_waves(sz, rows_in, inv_cos, sign):
    n_lon = sz.n_lon
    lane = lax.broadcasted_iota(jnp.int32, (1, LANES), 1)

    def value(s, place):
        row, at = spare(6 + place)
        return pltpu.roll(rows_in[s % n_lon, row : row + 1], -at % LANES, 1)

    theta = 2 * math.pi / sz.nlon
    ends = (1.0, math.cos(theta * (sz.columns - 1)), math.sin(theta * (sz.columns - 1)))
    sums = [[[value(s, 3 * f + k) for k in range(3)] for f in range(4)] for s in range(n_lon)]
    for s in range(n_lon):
        thick_w, thick_e = value(s, 13), value(s + 1, 12)
        flux = 0.25 * (value(s, 15) + value(s + 1, 14)) * (thick_w + thick_e) * inv_cos
        slope = 0.5 * inv_cos
        after = (s + 1) % n_lon
        for f, (west_of, east_of) in enumerate(((flux, flux), (slope * thick_e, slope * thick_w))):
            for k in range(3):
                sums[s][f][k] = sums[s][f][k] - west_of * ends[k]
            for k in range(2):
                sums[after][f][k] = sums[after][f][k] + east_of
    result = []
    for f in range(3):
        waves_of = [0.0, 0.0, 0.0]
        for s in range(n_lon):
            level, cosine, sine = sums[s][f]
            if f == 2:
                level = level + (0.5 * sz.ratio) * sign * sums[s][3][0]
                cosine = cosine - (0.5 * sz.ratio) * sign * sums[s][3][1]
                sine = sine - (0.5 * sz.ratio) * sign * sums[s][3][2]
            c, d = math.cos(2 * math.pi * s / n_lon), math.sin(2 * math.pi * s / n_lon)
            waves_of[0] = waves_of[0] + level
            waves_of[1] = waves_of[1] + (c * cosine - d * sine)
            waves_of[2] = waves_of[2] + (d * cosine + c * sine)
        spread = []
        for k, total in enumerate(waves_of):
            total = jnp.where(lane < LEVELS, total * ((1.0 if k == 0 else 2.0) / sz.nlon), 0.0)
            for step in (16, 32, 64):
                total = total + pltpu.roll(total, step, 1)
            spread.append(total)
        result.append(spread)
    return result


def unfolded(sides):
    lane = lax.broadcasted_iota(jnp.int32, (1, LANES), 1)
    start, width = spare(0)[1], 3 * LEVELS
    ninth = jnp.where(
        lane < width,
        pltpu.roll(sides[0:1], -start % LANES, 1),
        pltpu.roll(sides[1:2], (width - start) % LANES, 1),
    )
    return jnp.concatenate([sides, jnp.broadcast_to(ninth, sides.shape)], axis=0)


def rest_kernel(sz, masks_ref, h_ref, w_ref, q_ref, near_h_ref, near_w_ref, near_q_ref, far_ref, geo_ref, wave_ref, after_ref, *refs):
    met_refs, (new_w_ref, new_h_ref, mass_ref, ext, pole_in) = refs[: sz.n_lon], refs[sz.n_lon :]
    band = lax.axis_index("lat")
    ring = Tiles(sz)
    lane = ring.lane
    tiles, rows = sz.tiles, sz.rows
    for f in range(6):
        if f < 2 or f == 5:
            value = (h_ref[...], w_ref[:, 1, :], w_ref[:, 0, :])[min(f, 2)]
        else:
            value = q_ref[f - 2].astype(jnp.float32)
        ext[f, :rows, : sz.merged] = value
    add_rows(sz, ext, near_h_ref, near_w_ref, near_q_ref, far_ref)
    lane9 = lane[:rows]
    here = lax.axis_index("lon")
    from_e = from_w = met_refs[0][sz.size :]
    for k, met_ref in enumerate(met_refs):
        eastward = lax.rem(sz.partner(k) - here + sz.n_lon, sz.n_lon)
        pole_in[eastward] = met_ref[sz.size :]
        from_e = jnp.where(sz.partner(k) == lax.rem(here + 1, sz.n_lon), met_ref[sz.size :], from_e)
        from_w = jnp.where(sz.partner(k) == lax.rem(here + sz.n_lon - 1, sz.n_lon), met_ref[sz.size :], from_w)
    from_e, from_w = unfolded(from_e), unfolded(from_w)
    for place, f in enumerate((0, 5, 2, 3, 4)):
        after = pltpu.roll(from_e, (sz.tail - LEVELS * place) % LANES, 1)[:rows]
        before = pltpu.roll(from_w, (LANES - LEVELS - LEVELS * place) % LANES, 1)[:rows]
        own = ext[f, :rows, sz.end :]
        edge = jnp.where(lane9 < LANES - LEVELS, after, before)
        ext[f, :rows, sz.end :] = jnp.where(lane9 < sz.tail, own, edge)
    inv_cos, sin_centre, cos_face = geo_ref[band, 0], geo_ref[band, 1], geo_ref[band, 2]
    ratio = sz.ratio

    plain, alone = masks_ref[0], masks_ref[1]
    if sz.near_only:
        band = lax.axis_index("lat")
        low = band < sz.n_lat // 2
        pole_cos = jnp.where(low, inv_cos[:1], inv_cos[rows - 1 : rows])
        kept_waves = pole_waves(sz, pole_in, pole_cos, jnp.where(low, 1.0, -1.0))

    def stepped(f, t, value, tend):
        value = value + plain * tend
        if sz.near_only:
            level, cosine, sine = kept_waves[f]
            wave = level + cosine * wave_ref[0, t : t + 1] + sine * wave_ref[1, t : t + 1]
            value = value + alone * wave
        return value

    def tile(f, t):
        return ext[f, :, LANES * t : LANES * (t + 1)]

    kept = {}

    def zonal(t):
        if t not in kept:
            thick_e = ring.east("h", t, functools.partial(tile, 0))
            wind_e = ring.east("u", t, functools.partial(tile, 5))
            flux = 0.25 * (tile(5, t) + wind_e) * (tile(0, t) + thick_e) * inv_cos
            parts = []
            for k in range(3):
                q = tile(2 + k, t)
                q_e = ring.east(k, t, functools.partial(tile, 2 + k))
                parts.append(DIFFUSION * (q_e - q) - flux * (0.5 * (q + q_e)))
            kept[t] = (flux, thick_e, parts)
        return kept[t]

    for t in range(tiles):
        span = sz.span(t)
        lanes = slice(LANES * t, LANES * t + span)
        flux, thick_e, parts = zonal(t)
        thick, wind_u, wind_v = tile(0, t), tile(5, t), tile(1, t)
        flux_w = ring.west("f", t, lambda s: zonal(s)[0])
        thick_w = ring.west("hw", t, functools.partial(tile, 0))
        thick_n = north(thick)
        flux_n = (0.25 * ratio) * (wind_v + north(wind_v)) * (thick + thick_n) * cos_face
        thick_tend = -((flux - flux_w) + (flux_n - south(flux_n)) * inv_cos)
        wind_u_tend = sin_centre * wind_v - (thick_e - thick_w) * (0.5 * inv_cos)
        wind_v_tend = -sin_centre * wind_u - (0.5 * ratio) * (thick_n - south(thick))
        new_h_ref[:, lanes] = stepped(0, t, thick, thick_tend)[:rows, :span]
        new_w_ref[0, :, lanes] = stepped(1, t, wind_u, wind_u_tend)[:rows, :span]
        new_w_ref[1, :, lanes] = stepped(2, t, wind_v, wind_v_tend)[:rows, :span]
        for k in range(3):
            q = tile(2 + k, t)
            q_n = north(q)
            zonal_part = parts[k] - ring.west(("p", k), t, lambda s: zonal(s)[2][k])
            lap = q_n + south(q) - 2.0 * q
            over = flux_n * (0.5 * (q + q_n))
            merid_part = DIFFUSION * lap - (over - south(over)) * inv_cos
            mass = thick * q + TIME_STEP * (zonal_part + merid_part)
            mass_ref[k, :, lanes] = mass[:rows, :span].astype(jnp.bfloat16)


def sin_pi(y):
    y = jnp.where(y > 0.5, 1.0 - y, jnp.where(y < -0.5, -1.0 - y, y))
    s = y * y
    series = [(-1) ** i * math.pi ** (2 * i + 1) / math.factorial(2 * i + 1) for i in range(7)]
    total = series[-1]
    for factor in reversed(series[:-1]):
        total = total * s + factor
    return total * y


def share_of(sz, i):
    unit = lax.axis_index("lon") * sz.share + i
    return unit // sz.work, sz.first() + lax.rem(unit, sz.work)


def weights_kernel(sz, cut_ref, n_ref, inverse_ref, after_ref, weights_ref, masks_ref):
    band = lax.axis_index("lat")
    row = lax.broadcasted_iota(jnp.int32, (EXT_ROWS, LANES), 0)
    cuts = jnp.full((EXT_ROWS, LANES), sz.nlon // 2, jnp.int32)
    for j in range(sz.rows):
        cuts = jnp.where(row == j, cut_ref[band * sz.rows + j], cuts)
    plain, alone = cuts >= sz.nlon // 2, sz.at_pole(row)
    masks_ref[0] = jnp.where(plain, TIME_STEP, 0.0)
    masks_ref[1] = jnp.where(alone, TIME_STEP, 0.0)
    masks_ref[2] = jnp.where(plain | alone, 0.0, TIME_STEP)
    size = PER_TILE * sz.stack
    for i in range(sz.share):
        width = (2 * cut_ref[band * sz.rows + share_of(sz, i)[1]] + 1).astype(jnp.float32)
        n = n_ref[...]
        turns = n * width
        turns = turns - jnp.round(turns * (0.5 / sz.nlon)) * (2.0 * sz.nlon)
        weights = sin_pi(turns * (1.0 / sz.nlon)) * inverse_ref[...]
        weights = jnp.where(n == 0.0, width * (1.0 / sz.nlon), weights)
        weights_ref[size * i : size * (i + 1)] = weights.astype(jnp.bfloat16)


def pass_kernel(sz, piece_ref, after_ref, also_after_ref, out_ref):
    out_ref[...] = piece_ref[...]


def filter_kernel(sz, weights_ref, geo_ref, *refs):
    n_lon, stack, share = sz.n_lon, sz.stack, sz.share
    in_refs, out_refs, (gathered, results) = refs[:n_lon], refs[n_lon : 2 * n_lon], refs[2 * n_lon :]
    for k, in_ref in enumerate(in_refs):
        gathered[sz.partner(k), : sz.size] = in_ref[: sz.size]

    band = lax.axis_index("lat")
    lane = lax.broadcasted_iota(jnp.int32, (share, LANES), 1)
    place = lax.broadcasted_iota(jnp.int32, (share, LANES), 0)
    by_flux = by_thick = jnp.zeros((share, LANES), jnp.float32)
    for i in range(share):
        field, row = share_of(sz, i)
        inv_cos = geo_ref[band, 0, pl.ds(row, 1), :]
        by_flux = jnp.where((place == i) & (field == 0), inv_cos, by_flux)
        by_thick = jnp.where((place == i) & (field == 1), 0.5 * inv_cos, by_thick)
    sides = [gathered[s, pl.ds(sz.tiles - 1, share, stride=stack), :] for s in range(n_lon)]

    def column(s, k):
        return pltpu.roll(sides[s % n_lon], (-sz.tail - LEVELS * k) % LANES, 1)

    for s in range(n_lon):
        thick_w, thick_e = column(s, 1), column(s + 1, 0)
        flux = 0.25 * (column(s, 3) + column(s + 1, 2)) * (thick_w + thick_e) * by_flux
        west_of, east_of = flux + by_thick * thick_e, flux + by_thick * thick_w
        at = pl.ds(sz.tiles - 1, share, stride=stack)
        own = gathered[s, at, :]
        own = own - jnp.where(lane >= sz.tail - LEVELS, pltpu.roll(west_of, sz.tail - LEVELS, 1), 0.0)
        gathered[s, at, :] = jnp.where(lane < sz.tail, own, 0.0)
        at = pl.ds(0, share, stride=stack)
        after = (s + 1) % n_lon
        gathered[after, at, :] = gathered[after, at, :] + jnp.where(lane < LEVELS, east_of, 0.0)

    wide = lax.broadcasted_iota(jnp.int32, (stack, LANES), 1)
    rows = PER_TILE * stack
    for i in range(share):
        here = slice(stack * i, stack * (i + 1))
        pieces = [gathered[s, here].astype(jnp.bfloat16) for s in range(n_lon)]
        circle = jnp.concatenate([jnp.concatenate(pieces[s:] + pieces[:s], axis=0) for s in range(n_lon)], axis=1)
        spread = jnp.dot(weights_ref[rows * i : rows * (i + 1)], circle, preferred_element_type=jnp.float32)
        for s in range(n_lon):
            same = spread[:stack, LANES * s : LANES * (s + 1)]
            carried = None
            for e in range(1, PER_TILE):
                part = spread[stack * e : stack * (e + 1), LANES * s : LANES * (s + 1)]
                part = pltpu.roll(part, LEVELS * e, 1)
                inside = wide >= LEVELS * e
                same = same + jnp.where(inside, part, 0.0)
                over = jnp.where(inside, 0.0, part)
                carried = over if carried is None else carried + over
            results[s, here] = pltpu.roll(same, stack - 1, 0) + carried
    for k, out_ref in enumerate(out_refs):
        out_ref[...] = results[sz.partner(k, True), : sz.size]


def finish_kernel(sz, masks_ref, base_w_ref, base_h_ref, *refs):
    back_refs, (new_w_ref, new_h_ref, back_ref) = refs[: sz.n_lon], refs[sz.n_lon :]
    rows, work = sz.rows, sz.work
    for k, ref in enumerate(back_refs):
        back_ref[sz.piece(k, True), :] = ref[...]
    scale = masks_ref[2]
    even = lax.rem(lax.axis_index("lat"), 2) == 0
    for f in range(3):
        for t in range(sz.tiles):
            span = sz.span(t)
            lanes = slice(LANES * t, LANES * t + span)
            tend = back_ref[pl.ds(sz.stack * work * f + t, work, stride=sz.stack), :]
            if sz.near_only:
                tend = jnp.concatenate([tend, jnp.zeros((EXT_ROWS - work, LANES), jnp.float32)], axis=0)
                tend = jnp.where(even, south(tend), tend)
            change = (scale[:rows] * tend[:rows])[:, :span]
            if f == 0:
                new_h_ref[:, lanes] = base_h_ref[:, lanes] + change
            else:
                new_w_ref[:, f - 1, lanes] = base_w_ref[f - 1, :, lanes] + change


def local(winds, thickness, tracers, cutoff):
    n_lat = lax.axis_size("lat")
    n_lon = lax.axis_size("lon")
    rows, merged = thickness.shape
    sz = Sizes(rows, merged, n_lat, n_lon)
    f32 = jnp.float32
    vmem = pl.BlockSpec(memory_space=pltpu.VMEM)
    smem = pl.BlockSpec(memory_space=pltpu.SMEM)
    hbm = pl.BlockSpec(memory_space=pltpu.HBM)
    anywhere = pl.BlockSpec(memory_space=pl.ANY)

    def shaped(*shape):
        return jax.ShapeDtypeStruct(shape, f32)

    def call(kernel, name, in_specs, out_shape, scratch=(), limit=LIMIT):
        return pl.pallas_call(
            functools.partial(kernel, sz),
            out_shape=out_shape,
            in_specs=in_specs,
            out_specs=jax.tree.map(lambda _: vmem, out_shape),
            scratch_shapes=list(scratch),
            compiler_params=pltpu.CompilerParams(vmem_limit_bytes=limit),
            name=name,
        )

    geo = jnp.asarray(geometry(sz))
    wave = jnp.asarray(waves(sz))
    n, inverse = (jnp.asarray(table) for table in offsets(sz))

    wind_rows = jnp.swapaxes(winds, 0, 1)
    tracer_rows = jnp.swapaxes(tracers, 0, 1)
    far_row, near_row = shaped(5 * sz.stack, LANES), shaped(3 * sz.stack, LANES)
    kept = [((1,), f32), ((2,), f32), ((3,), jnp.bfloat16)]
    near_q, far_rows, sides = call(
        edges_kernel,
        "edges",
        [hbm] * 3,
        (near_row, far_row, shaped(2 * SIDE_ROWS, LANES)),
        [pltpu.VMEM((2,) + count + (merged,), dtype) for count, dtype in kept]
        + [
            pltpu.VMEM((rows,) + (count if count != (1,) else ()) + (lanes,), dtype)
            for lanes in (LANES, sz.tail)
            for count, dtype in kept
        ]
        + [pltpu.SemaphoreType.DMA((3, 4))],
        limit=MOST_VMEM,
    )(thickness, wind_rows, tracer_rows)

    near = [(band * n_lon + i, (band ^ 1) * n_lon + i) for band in range(n_lat) for i in range(n_lon)]
    far = []
    for band in range(n_lat):
        other = band - 1 if band % 2 == 0 else band + 1
        for i in range(n_lon):
            if 0 <= other < n_lat:
                far.append((band * n_lon + i, other * n_lon + i))
            else:
                far.append((band * n_lon + i, band * n_lon + (i + n_lon // 2) % n_lon))
    near_h = lax.ppermute(thickness, ("lat", "lon"), near)
    near_w = lax.ppermute(wind_rows, ("lat", "lon"), near)
    if not sz.near_only:
        far_rows = lax.ppermute(far_rows, ("lat", "lon"), far)

    def meetings(shares, back):
        order = [sz.turns(False, back), sz.turns(True, back)]
        got = [shares[0]]
        for k in range(1, n_lon):
            sectors = [(band, i, i ^ order[band % 2][k]) for band in range(n_lat) for i in range(n_lon)]
            got.append(lax.ppermute(shares[k], ("lat", "lon"), [(b * n_lon + i, b * n_lon + j) for b, i, j in sectors]))
        return got

    all_pieces = pltpu.VMEM((n_lon, sz.size + 8 * sz.stack, LANES), f32)
    all_units = pltpu.VMEM((n_lon * sz.size + 8 * sz.stack, LANES), f32)
    *tends, far_rows, near_q = call(
        polar_kernel,
        "polar",
        [vmem] * 9,
        [shaped(sz.size + SIDE_ROWS, LANES)] * n_lon + [far_row, near_row],
        [
            all_units,
            pltpu.VMEM((4 * sz.stack, LANES), f32),
            pltpu.VMEM((3, EXT_ROWS, sz.tiles * LANES), f32),
        ],
    )(thickness, wind_rows, near_h, near_w, sides, geo, wave, far_rows, near_q)
    met = meetings(tends, False)
    near_q = lax.ppermute(near_q, ("lat", "lon"), near)
    from_far = lax.ppermute(far_rows, ("lat", "lon"), far) if sz.near_only else far_rows
    weights, masks = call(
        weights_kernel,
        "weights",
        [smem, vmem, vmem, anywhere],
        (
            jax.ShapeDtypeStruct((sz.share * PER_TILE * sz.stack, n_lon * sz.stack), jnp.bfloat16),
            shaped(3, EXT_ROWS, LANES),
        ),
    )(cutoff, n, inverse, tends[0])
    worked = call(
        filter_kernel,
        "filter",
        [vmem] * 2 + [vmem] * n_lon,
        [shaped(sz.size, LANES)] * n_lon,
        [all_pieces, all_pieces],
    )(weights, geo, *met)
    held = call(pass_kernel, "pass", [vmem] + [anywhere] * 2, shaped(sz.size, LANES))(worked[-1], from_far, near_q)
    worked = [*worked[:-1], held]
    back = meetings(worked, True)

    base_w, base_h, mass = call(
        rest_kernel,
        "rest",
        [vmem] * 10 + [anywhere] + [vmem] * n_lon,
        (shaped(2, rows, merged), shaped(rows, merged), jax.ShapeDtypeStruct(tracers.shape, jnp.bfloat16)),
        [pltpu.VMEM((6, EXT_ROWS, sz.tiles * LANES), f32), pltpu.VMEM((n_lon, 8, LANES), f32)],
    )(masks, thickness, wind_rows, tracers, near_h, near_w, near_q, from_far, geo, wave, worked[0], *met)

    new_w, new_h = call(
        finish_kernel,
        "finish",
        [vmem] * (3 + n_lon),
        (shaped(*wind_rows.shape), shaped(rows, merged)),
        [all_units],
    )(masks, base_w, base_h, *back)
    return jnp.swapaxes(new_w, 0, 1), new_h, mass


def solution(mesh):
    in_specs = (P(None, "lat", "lon"), P("lat", "lon"), P(None, "lat", "lon"), P())
    out_specs = (P(None, "lat", "lon"), P("lat", "lon"), P(None, "lat", "lon"))
    return jax.shard_map(local, mesh=mesh, in_specs=in_specs, out_specs=out_specs, check_vma=False)
```
